32 devices in a mesh: grp: 4 (over y, x), shard: 8 (over z, core).
Axes of the slice: x: 2, y: 2, z: 4, core: 2. Of those that a mesh axis runs over, the one named last changes fastest.
Arguments:
- tokens: bfloat16 [32, 1024, 1024], P(('grp', 'shard')), may hold values from -6 to 6
- segment_ids: int32 [32, 1024], P(('grp', 'shard')), may hold values from 0 to 17, as said below
- keep_flag: int32 [32, 1024], P(('grp', 'shard')), may hold values from 0 to 1, as said below
- cotangent: bfloat16 [32, 1024, 1024], P(('grp', 'shard')), may hold values from -6 to 6
- w_qkv: bfloat16 [1024, 3072], P('shard', 'grp'), may hold values from -0.25 to 0.25
- b_query: bfloat16 [1024], P('shard'), may hold values from -3 to 3
- b_value: bfloat16 [1024], P('shard'), may hold values from -3 to 3
- w_attn_out: bfloat16 [1024, 1024], P('shard', 'grp'), may hold values from -0.75 to 0.75
- b_attn_out: bfloat16 [1024], P('shard'), may hold values from -3 to 3
- norm1_gain: bfloat16 [1024], P('shard'), may hold values from 0.5 to 1.5
- norm1_bias: bfloat16 [1024], P('shard'), may hold values from -3 to 3
- w_in: bfloat16 [1024, 4096], P('shard', 'grp'), may hold values from -0.1875 to 0.1875
- b_in: bfloat16 [4096], P('shard'), may hold values from -3 to 3
- w_out: bfloat16 [4096, 1024], P('shard', 'grp'), may hold values from -0.09375 to 0.09375
- b_out: bfloat16 [1024], P('shard'), may hold values from -3 to 3
- norm2_gain: bfloat16 [1024], P('shard'), may hold values from 0.5 to 1.5
- norm2_bias: bfloat16 [1024], P('shard'), may hold values from -3 to 3
Outputs:
- layer_out: bfloat16 [32, 1024, 1024], P(('grp', 'shard'))
- input_grad: float32 [32, 1024, 1024], P(('grp', 'shard'))
- grad_w_qkv: float32 [1024, 3072], P('shard')
- grad_b_query: float32 [1024], P('shard')
- grad_b_value: float32 [1024], P('shard')
- grad_w_attn_out: float32 [1024, 1024], P('shard')
- grad_b_attn_out: float32 [1024], P('shard')
- grad_norm1_gain: float32 [1024], P('shard')
- grad_norm1_bias: float32 [1024], P('shard')
- grad_w_in: float32 [1024, 4096], P('shard')
- grad_b_in: float32 [4096], P('shard')
- grad_w_out: float32 [4096, 1024], P('shard')
- grad_b_out: float32 [1024], P('shard')
- grad_norm2_gain: float32 [1024], P('shard')
- grad_norm2_bias: float32 [1024], P('shard')
The draws below stay inside these ranges and needn't reach their ends.
Inputs may be any that keep to these rules, and one draw needn't show every extreme that they name: `segment_ids`: along each sequence the ids start at 0 and rise by one at the first token of each document; every document but the last of its sequence has 60 to 800 tokens, the last one is cut by the sequence's end. `keep_flag`: 0 exactly on the tokens of the last document of each sequence.
All inputs are finite; a program needn't handle non-finite values.
Results may differ from the reference program's by a relative error of at most 0.02.
Values may be sent and summed in bfloat16 or wider, within the bound.
No kernel may reach another device: no remote copies, remote signals or barrier semaphores. Data moves between devices by JAX's collectives and lax.ppermute only.
A program may use at most 256 MiB of HBM per device.

```python
import math
import jax
import jax.numpy as jnp
from jax import lax

D = 1024
H = 16
HD = 64
FF = 4096
SEQ_LEN = 1024
DOC_MIN = 60
DOC_MAX = 800
SEQS = 32


def document_layout(key):
    doc_slots = SEQ_LEN // DOC_MIN + 1
    lengths = jax.random.randint(jax.random.fold_in(key, 11), (SEQS, doc_slots), DOC_MIN, DOC_MAX + 1)
    forced = jax.random.randint(jax.random.fold_in(key, 12), (SEQS,), 0, 2)
    chosen = jax.random.randint(jax.random.fold_in(key, 13), (), 0, SEQS)
    forced = jnp.where(jnp.arange(SEQS) == chosen, 1, forced)
    lengths = lengths.at[:, 0].set(jnp.where(forced == 1, DOC_MAX, lengths[:, 0]))
    lengths = lengths.at[:, 1].set(jnp.where(forced == 1, DOC_MIN, lengths[:, 1]))
    shortest = (chosen + 1) % SEQS
    lengths = jnp.where((jnp.arange(SEQS) == shortest)[:, None], DOC_MIN, lengths)
    doc_ends = jnp.cumsum(lengths, axis=1)
    positions = jnp.arange(SEQ_LEN)
    doc_ids = jnp.sum((doc_ends[:, None, :] <= positions[None, :, None]).astype(jnp.int32), axis=2).astype(jnp.int32)
    keep_mask = (doc_ids != doc_ids[:, -1:]).astype(jnp.int32)
    return (doc_ids, keep_mask)


def draw_segment_ids(key, part):
    return document_layout(key)[0]


def draw_keep_flag(key, part):
    return document_layout(key)[1]


def levels(key, shape, shards, low, top_value):
    def one(dim, shards_of):
        steps = jax.random.uniform(jax.random.fold_in(jax.random.fold_in(key, 6), dim), (shards_of,), jnp.float32, low / len(shards), top_value / len(shards))
        return jnp.repeat(jnp.exp(steps), shape[dim] // shards_of).reshape((-1,) + (1,) * (len(shape) - dim - 1))

    factor_of = one(*shards[0])
    for cut in shards[1:]:
        factor_of = factor_of * one(*cut)
    return factor_of


def normal_values(key, dims, width, reach, cuts=(), kind=jnp.bfloat16):
    gain = levels(key, dims, cuts, -0.22, 0.18) if cuts else 1.0
    array = jax.random.normal(key, dims, jnp.float32) * width * gain
    return jnp.minimum(jnp.maximum(array, -reach), reach).astype(kind)


def setup_inputs(seed: int = 0) -> dict:
    seeds = jax.random.split(jax.random.key(seed), 18)
    tokens = normal_values(seeds[0], (SEQS, SEQ_LEN, D), 1.0, 6.0, ((0, 32),))
    segment_ids = draw_segment_ids(jax.random.fold_in(seeds[17], 71), 0)
    keep_flag = draw_keep_flag(jax.random.fold_in(seeds[17], 71), 0)
    cotangent = normal_values(seeds[3], (SEQS, SEQ_LEN, D), 1.0, 6.0, ((0, 32),))
    w_qkv = normal_values(seeds[4], (D, 3 * D), (D // 2) ** -0.5, 0.25, ((0, 8), (1, 4)))
    b_query = normal_values(seeds[5], (D,), 0.5, 3.0, ((0, 8),))
    b_value = normal_values(seeds[6], (D,), 0.5, 3.0, ((0, 8),))
    w_attn_out = normal_values(seeds[7], (D, D), (D // 16) ** -0.5, 0.75, ((0, 8), (1, 4)))
    b_attn_out = normal_values(seeds[8], (D,), 0.5, 3.0, ((0, 8),))
    norm1_gain = jnp.clip(1.0 + 0.1 * jax.random.normal(seeds[9], (D,), jnp.float32), 0.5, 1.5).astype(jnp.bfloat16)
    norm1_bias = normal_values(seeds[10], (D,), 0.5, 3.0, ((0, 8),))
    w_in = normal_values(seeds[11], (D, FF), D ** -0.5, 0.1875, ((0, 8), (1, 4)))
    b_in = normal_values(seeds[12], (FF,), 0.5, 3.0, ((0, 8),))
    w_out = normal_values(seeds[13], (FF, D), FF ** -0.5, 0.09375, ((0, 8), (1, 4)))
    b_out = normal_values(seeds[14], (D,), 0.5, 3.0, ((0, 8),))
    norm2_gain = jnp.clip(1.0 + 0.1 * jax.random.normal(seeds[15], (D,), jnp.float32), 0.5, 1.5).astype(jnp.bfloat16)
    norm2_bias = normal_values(seeds[16], (D,), 0.5, 3.0, ((0, 8),))
    return dict(tokens=tokens, segment_ids=segment_ids, keep_flag=keep_flag, cotangent=cotangent, w_qkv=w_qkv, b_query=b_query, b_value=b_value, w_attn_out=w_attn_out, b_attn_out=b_attn_out, norm1_gain=norm1_gain, norm1_bias=norm1_bias, w_in=w_in, b_in=b_in, w_out=w_out, b_out=b_out, norm2_gain=norm2_gain, norm2_bias=norm2_bias)


highest = lax.Precision.HIGHEST
masked_score = -1e+30
epsilon = 1e-05

@jax.custom_vjp
def low(v):
    return lax.optimization_barrier(v.astype(jnp.bfloat16)).astype(jnp.float32)

@jax.custom_vjp
def low_back(v):
    return v

def low_keep(v):
    return (low(v), None)

def low_pass(kept, grad):
    return (grad,)

def back_keep(v):
    return (v, None)

def back_low(kept, grad):
    return (low(grad),)
low.defvjp(low_keep, low_pass)
low_back.defvjp(back_keep, back_low)

def norm_layer(rows, gain_row, shift_row):
    row_mean = lax.optimization_barrier(jnp.mean(rows, -1, keepdims=True))
    centered = rows - row_mean
    row_var = lax.optimization_barrier(jnp.mean(centered * centered, -1, keepdims=True))
    return centered * lax.rsqrt(row_var + epsilon) * gain_row + shift_row

def gelu_exact(values):
    return 0.5 * values * (1.0 + lax.erf(values * (1.0 / math.sqrt(2.0))))

def attend_pack(pieces):
    queries, key_rows, value_rows, segment_row = pieces
    length = queries.shape[0]
    query_heads = queries.reshape(length, H, HD)
    key_heads = key_rows.reshape(length, H, HD)
    value_heads = value_rows.reshape(length, H, HD)
    scaling = 1.0 / math.sqrt(HD)
    scores = low_back(jnp.einsum('qhd,khd->hqk', query_heads, key_heads, precision=highest) * scaling)
    allowed = segment_row[:, None] == segment_row[None, :]
    scores = jnp.where(allowed[None], scores, masked_score)
    powers = jnp.exp(scores - lax.optimization_barrier(jnp.max(scores, -1, keepdims=True)))
    attn_probs = low(powers / lax.optimization_barrier(jnp.sum(powers, -1, keepdims=True)))
    context = jnp.einsum('hqk,khd->qhd', attn_probs, value_heads, precision=highest)
    return context.reshape(length, H * HD)

def layer_forward(inputs, segment_rows, params):
    w_qkv, b_query, b_value, w_attn_out, b_attn_out, norm1_gain, norm1_bias, w_in, b_in, w_out, b_out, norm2_gain, norm2_bias = params
    group_size, length = segment_rows.shape
    flat_rows = inputs.reshape(group_size * length, D)
    mixed_qkv = low_back(jnp.dot(flat_rows, w_qkv, precision=highest))
    queries = low(mixed_qkv[:, :D] + b_query)
    key_rows = low(mixed_qkv[:, D:2 * D])
    value_rows = low(mixed_qkv[:, 2 * D:] + b_value)
    contexts = lax.map(jax.checkpoint(attend_pack), (queries.reshape(group_size, length, D), key_rows.reshape(group_size, length, D), value_rows.reshape(group_size, length, D), segment_rows))
    contexts = low(low_back(contexts.reshape(group_size * length, D)))
    first_sum = flat_rows + low_back(jnp.dot(contexts, w_attn_out, precision=highest)) + b_attn_out
    normed_one = norm_layer(first_sum, norm1_gain, norm1_bias)
    hidden_pre = low_back(jnp.dot(low(normed_one), w_in, precision=highest)) + b_in
    hidden = low(gelu_exact(hidden_pre))
    second_sum = normed_one + low_back(jnp.dot(hidden, w_out, precision=highest)) + b_out
    return norm_layer(second_sum, norm2_gain, norm2_bias).reshape(group_size, length, D)

def reference(tokens, segment_ids, keep_flag, cotangent, w_qkv, b_query, b_value, w_attn_out, b_attn_out, norm1_gain, norm1_bias, w_in, b_in, w_out, b_out, norm2_gain, norm2_bias):
    params = tuple((item.astype(jnp.float32) for item in (w_qkv, b_query, b_value, w_attn_out, b_attn_out, norm1_gain, norm1_bias, w_in, b_in, w_out, b_out, norm2_gain, norm2_bias)))
    group_size = math.gcd(SEQS, max(1, 4096 // SEQ_LEN))
    group_count = SEQS // group_size
    inputs = tokens.astype(jnp.float32).reshape(group_count, group_size, SEQ_LEN, D)
    segment_rows = segment_ids.astype(jnp.int32).reshape(group_count, group_size, SEQ_LEN)
    masked_cot = (cotangent.astype(jnp.float32) * keep_flag.astype(jnp.float32)[:, :, None]).reshape(group_count, group_size, SEQ_LEN, D)

    def accumulate(running, pieces):
        group_in, group_segments, group_cot = pieces

        def apply_layer(values, weights):
            return layer_forward(values, group_segments, weights)
        outputs, pullback = jax.vjp(apply_layer, group_in, params)
        group_grad, param_grads = pullback(group_cot)
        running = jax.tree.map(jnp.add, running, param_grads)
        return (running, (outputs.astype(jnp.bfloat16), group_grad))
    start = jax.tree.map(jnp.zeros_like, params)
    running, (outputs, input_grads) = lax.scan(accumulate, start, (inputs, segment_rows, masked_cot))
    return (outputs.reshape(SEQS, SEQ_LEN, D), input_grads.reshape(SEQS, SEQ_LEN, D), running[0], running[1], running[2], running[3], running[4], running[5], running[6], running[7], running[8], running[9], running[10], running[11], running[12])
```

```python
import functools
import math

import jax
import jax.numpy as jnp
from jax import lax
from jax.experimental import pallas as pl
from jax.experimental.pallas import tpu as pltpu
from jax.sharding import PartitionSpec as P

H = 16
HD = 64


masked_score = -1e30
epsilon = 1e-05


def norm_layer(rows, gain_row, shift_row):
    row_mean = jnp.mean(rows, -1, keepdims=True)
    centered = rows - row_mean
    row_var = jnp.mean(centered * centered, -1, keepdims=True)
    return centered * lax.rsqrt(row_var + epsilon) * gain_row + shift_row


def gelu_exact(values):
    return 0.5 * values * (1.0 + lax.erf(values * (1.0 / math.sqrt(2.0))))


def contract_rows(left, right):
    return lax.dot_general(
        left, right, (((0,), (0,)), ((), ())), preferred_element_type=jnp.float32
    )


def contract_cols(left, right):
    return lax.dot_general(
        left, right, (((1,), (1,)), ((), ())), preferred_element_type=jnp.float32
    )


def attend_forward(queries, key_rows, value_rows, segment_row, block_rows):
    length, model_width = queries.shape
    scaling = 1.0 / math.sqrt(HD)
    key_heads = key_rows.reshape(length, H, HD)
    value_heads = value_rows.reshape(length, H, HD)
    query_blocks = queries.reshape(length // block_rows, block_rows, H, HD)
    segment_blocks = segment_row.reshape(length // block_rows, block_rows)

    def one_block(pieces):
        query_part, segment_part = pieces
        scores = (
            jnp.einsum("qhd,khd->hqk", query_part, key_heads, preferred_element_type=jnp.float32)
            * scaling
        )
        allowed = segment_part[:, None] == segment_row[None, :]
        scores = jnp.where(allowed[None], scores, masked_score)
        row_max = jnp.max(scores, -1, keepdims=True)
        powers = jnp.exp(scores - row_max)
        totals = jnp.sum(powers, -1, keepdims=True)
        attn_probs = (powers / totals).astype(jnp.bfloat16)
        context = jnp.einsum(
            "hqk,khd->qhd", attn_probs, value_heads, preferred_element_type=jnp.float32
        )
        return (
            context.reshape(block_rows, model_width).astype(jnp.bfloat16),
            (row_max + jnp.log(totals))[:, :, 0],
        )

    contexts, log_sums = lax.map(one_block, (query_blocks, segment_blocks))
    return (contexts.reshape(length, model_width), log_sums)


def attend_backward(queries, key_rows, value_rows, segment_row, log_sums, context_grad, block_rows):
    length, model_width = queries.shape
    scaling = 1.0 / math.sqrt(HD)
    key_heads = key_rows.reshape(length, H, HD)
    value_heads = value_rows.reshape(length, H, HD)
    query_blocks = queries.reshape(length // block_rows, block_rows, H, HD)
    segment_blocks = segment_row.reshape(length // block_rows, block_rows)
    grad_blocks = context_grad.reshape(length // block_rows, block_rows, H, HD)

    def one_block(running, pieces):
        key_acc, value_acc = running
        query_part, segment_part, lse_part, grad_part = pieces
        scores = (
            jnp.einsum("qhd,khd->hqk", query_part, key_heads, preferred_element_type=jnp.float32)
            * scaling
        )
        allowed = segment_part[:, None] == segment_row[None, :]
        scores = jnp.where(allowed[None], scores, masked_score)
        probs = jnp.exp(scores - lse_part[:, :, None])
        prob_low = probs.astype(jnp.bfloat16)
        prob_grad = jnp.einsum(
            "qhd,khd->hqk", grad_part, value_heads, preferred_element_type=jnp.float32
        )
        row_dot = jnp.sum(prob_grad * probs, -1, keepdims=True)
        score_grad = (probs * (prob_grad - row_dot)).astype(jnp.bfloat16)
        query_grad = (
            jnp.einsum("hqk,khd->qhd", score_grad, key_heads, preferred_element_type=jnp.float32)
            * scaling
        )
        key_acc = (
            key_acc
            + jnp.einsum("hqk,qhd->khd", score_grad, query_part, preferred_element_type=jnp.float32)
            * scaling
        )
        value_acc = value_acc + jnp.einsum(
            "hqk,qhd->khd", prob_low, grad_part, preferred_element_type=jnp.float32
        )
        return ((key_acc, value_acc), query_grad.reshape(block_rows, model_width))

    empty_acc = jnp.zeros((length, H, HD), jnp.float32)
    (key_grad, value_grad), query_grads = lax.scan(
        one_block, (empty_acc, empty_acc), (query_blocks, segment_blocks, log_sums, grad_blocks)
    )
    return (
        query_grads.reshape(length, model_width),
        key_grad.reshape(length, model_width),
        value_grad.reshape(length, model_width),
    )


def on_device(
    tokens,
    segment_ids,
    keep_flag,
    cotangent,
    w_qkv,
    b_query,
    b_value,
    w_attn_out,
    b_attn_out,
    norm1_gain,
    norm1_bias,
    w_in,
    b_in,
    w_out,
    b_out,
    norm2_gain,
    norm2_bias,
):
    seq_count, length, model_width = tokens.shape
    block_rows = min(512, length)
    within = (
        lax.all_gather(w_qkv, "shard", axis=0, tiled=True),
        lax.all_gather(w_attn_out, "shard", axis=0, tiled=True),
        lax.all_gather(w_in, "shard", axis=0, tiled=True),
        lax.all_gather(w_out, "shard", axis=0, tiled=True),
        lax.all_gather(b_query, "shard", axis=0, tiled=True),
        lax.all_gather(b_value, "shard", axis=0, tiled=True),
        lax.all_gather(b_attn_out, "shard", axis=0, tiled=True),
        lax.all_gather(norm1_gain, "shard", axis=0, tiled=True),
        lax.all_gather(norm1_bias, "shard", axis=0, tiled=True),
        lax.all_gather(b_in, "shard", axis=0, tiled=True),
        lax.all_gather(b_out, "shard", axis=0, tiled=True),
        lax.all_gather(norm2_gain, "shard", axis=0, tiled=True),
        lax.all_gather(norm2_bias, "shard", axis=0, tiled=True),
    )
    full_qkv, full_attn, full_in, full_out = (
        lax.all_gather(within[0], "grp", axis=1, tiled=True),
        lax.all_gather(within[1], "grp", axis=1, tiled=True),
        lax.all_gather(within[2], "grp", axis=1, tiled=True),
        lax.all_gather(within[3], "grp", axis=1, tiled=True),
    )
    (
        bias_query,
        bias_value,
        bias_attn,
        gain_one,
        shift_one,
        bias_in,
        bias_out,
        gain_two,
        shift_two,
    ) = [piece.astype(jnp.float32) for piece in within[4:]]
    flat_rows = tokens.reshape(seq_count * length, model_width)
    mixed_qkv = jnp.dot(flat_rows, full_qkv, preferred_element_type=jnp.float32)
    queries = (mixed_qkv[:, :model_width] + bias_query).astype(jnp.bfloat16)
    key_rows = mixed_qkv[:, model_width : 2 * model_width].astype(jnp.bfloat16)
    value_rows = (mixed_qkv[:, 2 * model_width :] + bias_value).astype(jnp.bfloat16)
    query_seqs = queries.reshape(seq_count, length, model_width)
    key_seqs = key_rows.reshape(seq_count, length, model_width)
    value_seqs = value_rows.reshape(seq_count, length, model_width)

    def forward_sequence(pieces):
        return attend_forward(pieces[0], pieces[1], pieces[2], pieces[3], block_rows)

    contexts, log_sums = lax.map(forward_sequence, (query_seqs, key_seqs, value_seqs, segment_ids))
    contexts = contexts.reshape(seq_count * length, model_width)
    attended = jnp.dot(contexts, full_attn, preferred_element_type=jnp.float32) + bias_attn
    first_sum = flat_rows.astype(jnp.float32) + attended
    normed_one, norm_one_back = jax.vjp(norm_layer, first_sum, gain_one, shift_one)
    normed_low = normed_one.astype(jnp.bfloat16)
    hidden_pre = jnp.dot(normed_low, full_in, preferred_element_type=jnp.float32) + bias_in
    hidden, gelu_back = jax.vjp(gelu_exact, hidden_pre)
    hidden_low = hidden.astype(jnp.bfloat16)
    second_sum = normed_one + (
        jnp.dot(hidden_low, full_out, preferred_element_type=jnp.float32) + bias_out
    )
    result, norm_two_back = jax.vjp(norm_layer, second_sum, gain_two, shift_two)
    layer_out = result.astype(jnp.bfloat16).reshape(seq_count, length, model_width)
    again = (
        lax.all_gather(w_qkv, "shard", axis=0, tiled=True),
        lax.all_gather(w_attn_out, "shard", axis=0, tiled=True),
        lax.all_gather(w_in, "shard", axis=0, tiled=True),
        lax.all_gather(w_out, "shard", axis=0, tiled=True),
    )
    back_qkv, back_attn, back_in, back_out = (
        lax.all_gather(again[0], "grp", axis=1, tiled=True),
        lax.all_gather(again[1], "grp", axis=1, tiled=True),
        lax.all_gather(again[2], "grp", axis=1, tiled=True),
        lax.all_gather(again[3], "grp", axis=1, tiled=True),
    )
    masked_cot = cotangent.astype(jnp.float32).reshape(
        seq_count * length, model_width
    ) * keep_flag.reshape(seq_count * length, 1).astype(jnp.float32)
    second_grad, gain_two_grad, shift_two_grad = norm_two_back(masked_cot)
    bias_out_grad = jnp.sum(second_grad, 0)
    out_low = second_grad.astype(jnp.bfloat16)
    w_out_grad = contract_rows(hidden_low, out_low)
    hidden_grad = contract_cols(out_low, back_out)
    (pre_grad,) = gelu_back(hidden_grad)
    bias_in_grad = jnp.sum(pre_grad, 0)
    pre_low = pre_grad.astype(jnp.bfloat16)
    w_in_grad = contract_rows(normed_low, pre_low)
    normed_grad = second_grad + contract_cols(pre_low, back_in)
    first_grad, gain_one_grad, shift_one_grad = norm_one_back(normed_grad)
    bias_attn_grad = jnp.sum(first_grad, 0)
    attn_low = first_grad.astype(jnp.bfloat16)
    w_attn_grad = contract_rows(contexts, attn_low)
    context_grad = contract_cols(attn_low, back_attn).astype(jnp.bfloat16)

    def backward_sequence(pieces):
        return attend_backward(
            pieces[0], pieces[1], pieces[2], pieces[3], pieces[4], pieces[5], block_rows
        )

    query_grad, key_grad, value_grad = lax.map(
        backward_sequence,
        (
            query_seqs,
            key_seqs,
            value_seqs,
            segment_ids,
            log_sums,
            context_grad.reshape(seq_count, length, model_width),
        ),
    )
    query_grad = query_grad.reshape(seq_count * length, model_width)
    key_grad = key_grad.reshape(seq_count * length, model_width)
    value_grad = value_grad.reshape(seq_count * length, model_width)
    bias_query_grad = jnp.sum(query_grad, 0)
    bias_value_grad = jnp.sum(value_grad, 0)
    qkv_low = jnp.concatenate([query_grad, key_grad, value_grad], 1).astype(jnp.bfloat16)
    w_qkv_grad = contract_rows(flat_rows, qkv_low)
    input_grad = first_grad + contract_cols(qkv_low, back_qkv)
    reduced = (
        lax.psum_scatter(
            w_qkv_grad.astype(jnp.bfloat16), "shard", scatter_dimension=0, tiled=True
        ).astype(jnp.float32),
        lax.psum_scatter(
            bias_query_grad.astype(jnp.bfloat16), "shard", scatter_dimension=0, tiled=True
        ).astype(jnp.float32),
        lax.psum_scatter(
            bias_value_grad.astype(jnp.bfloat16), "shard", scatter_dimension=0, tiled=True
        ).astype(jnp.float32),
        lax.psum_scatter(
            w_attn_grad.astype(jnp.bfloat16), "shard", scatter_dimension=0, tiled=True
        ).astype(jnp.float32),
        lax.psum_scatter(
            bias_attn_grad.astype(jnp.bfloat16), "shard", scatter_dimension=0, tiled=True
        ).astype(jnp.float32),
        lax.psum_scatter(
            gain_one_grad.astype(jnp.bfloat16), "shard", scatter_dimension=0, tiled=True
        ).astype(jnp.float32),
        lax.psum_scatter(
            shift_one_grad.astype(jnp.bfloat16), "shard", scatter_dimension=0, tiled=True
        ).astype(jnp.float32),
        lax.psum_scatter(
            w_in_grad.astype(jnp.bfloat16), "shard", scatter_dimension=0, tiled=True
        ).astype(jnp.float32),
        lax.psum_scatter(
            bias_in_grad.astype(jnp.bfloat16), "shard", scatter_dimension=0, tiled=True
        ).astype(jnp.float32),
        lax.psum_scatter(
            w_out_grad.astype(jnp.bfloat16), "shard", scatter_dimension=0, tiled=True
        ).astype(jnp.float32),
        lax.psum_scatter(
            bias_out_grad.astype(jnp.bfloat16), "shard", scatter_dimension=0, tiled=True
        ).astype(jnp.float32),
        lax.psum_scatter(
            gain_two_grad.astype(jnp.bfloat16), "shard", scatter_dimension=0, tiled=True
        ).astype(jnp.float32),
        lax.psum_scatter(
            shift_two_grad.astype(jnp.bfloat16), "shard", scatter_dimension=0, tiled=True
        ).astype(jnp.float32),
    )
    summed = (
        lax.psum(reduced[0].astype(jnp.bfloat16), "grp").astype(jnp.float32),
        lax.psum(reduced[1].astype(jnp.bfloat16), "grp").astype(jnp.float32),
        lax.psum(reduced[2].astype(jnp.bfloat16), "grp").astype(jnp.float32),
        lax.psum(reduced[3].astype(jnp.bfloat16), "grp").astype(jnp.float32),
        lax.psum(reduced[4].astype(jnp.bfloat16), "grp").astype(jnp.float32),
        lax.psum(reduced[5].astype(jnp.bfloat16), "grp").astype(jnp.float32),
        lax.psum(reduced[6].astype(jnp.bfloat16), "grp").astype(jnp.float32),
        lax.psum(reduced[7].astype(jnp.bfloat16), "grp").astype(jnp.float32),
        lax.psum(reduced[8].astype(jnp.bfloat16), "grp").astype(jnp.float32),
        lax.psum(reduced[9].astype(jnp.bfloat16), "grp").astype(jnp.float32),
        lax.psum(reduced[10].astype(jnp.bfloat16), "grp").astype(jnp.float32),
        lax.psum(reduced[11].astype(jnp.bfloat16), "grp").astype(jnp.float32),
        lax.psum(reduced[12].astype(jnp.bfloat16), "grp").astype(jnp.float32),
    )
    return (
        layer_out,
        input_grad.reshape(seq_count, length, model_width),
        summed[0],
        summed[1],
        summed[2],
        summed[3],
        summed[4],
        summed[5],
        summed[6],
        summed[7],
        summed[8],
        summed[9],
        summed[10],
        summed[11],
        summed[12],
    )


NT = (((1,), (1,)), ((), ()))
NN = (((1,), (0,)), ((), ()))
TN = (((0,), (0,)), ((), ()))
LANES = 128
AXES = ("grp", "shard")


def mxu(left, right, dims):
    return lax.dot_general(left, right, dims, preferred_element_type=jnp.float32)


def params(megabytes=60):
    return pltpu.CompilerParams(vmem_limit_bytes=megabytes << 20)


def attention_forward_kernel(q_ref, k_ref, v_ref, seg_col, seg_row, out_ref, lse_ref, *, rows):
    length = q_ref.shape[0]
    first = lax.broadcasted_iota(jnp.int32, (1, LANES), 1) < HD
    keys = k_ref[...]
    values = v_ref[...]
    zero = jnp.zeros_like(keys)
    head_keys = (jnp.where(first, keys, zero), jnp.where(first, zero, keys))
    key_segments = seg_col[...]
    for block in range(length // rows):
        here = pl.ds(block * rows, rows)
        q = q_ref[here, :]
        allowed = key_segments == seg_row[:, here]
        outs = []
        for head in range(2):
            scores = mxu(head_keys[head], q, NT)
            scores = jnp.where(allowed, scores, masked_score)
            top = jnp.max(scores, 0, keepdims=True)
            powers = jnp.exp(scores - top)
            total = jnp.sum(powers, 0, keepdims=True)
            part = mxu(powers.astype(jnp.bfloat16), values, TN)
            outs.append(part * jnp.transpose(jnp.broadcast_to(1.0 / total, (LANES, rows))))
            lse_ref[0, head : head + 1, here] = top + jnp.log(total)
        out_ref[here, :] = jnp.where(first, outs[0], outs[1]).astype(jnp.bfloat16)


def attention_forward(q, k, v, seg_col, seg_row):
    length, width = q.shape
    pairs = width // LANES
    rows = min(512, length)
    pair = pl.BlockSpec((length, LANES), lambda j: (0, j))
    return pl.pallas_call(
        functools.partial(attention_forward_kernel, rows=rows),
        grid=(pairs,),
        in_specs=[
            pair,
            pair,
            pair,
            pl.BlockSpec((length, 1), lambda j: (0, 0)),
            pl.BlockSpec((1, length), lambda j: (0, 0)),
        ],
        out_specs=[pair, pl.BlockSpec((1, 2, length), lambda j: (j, 0, 0))],
        out_shape=[
            jax.ShapeDtypeStruct((length, width), jnp.bfloat16),
            jax.ShapeDtypeStruct((pairs, 2, length), jnp.float32),
        ],
        compiler_params=params(),
        cost_estimate=pl.CostEstimate(
            flops=16 * length * length * width, bytes_accessed=8 * length * width, transcendentals=0
        ),
        name="attn_fwd",
    )(q, k, v, seg_col, seg_row)


def attention_backward_kernel(
    q_ref, k_ref, v_ref, o_ref, do_ref, seg_col, seg_row, lse_ref, grad_ref, sum_ref, *, rows
):
    length = q_ref.shape[0]
    lane = lax.broadcasted_iota(jnp.int32, (1, LANES), 1)
    first = lane < HD
    pick = (
        lax.broadcasted_iota(jnp.int32, (8, LANES), 0)
        == lax.broadcasted_iota(jnp.int32, (8, LANES), 1) // HD
    ).astype(jnp.float32)
    keys = k_ref[...]
    values = v_ref[...]
    zero = jnp.zeros_like(keys)
    head_keys = (jnp.where(first, keys, zero), jnp.where(first, zero, keys))
    head_values = (jnp.where(first, values, zero), jnp.where(first, zero, values))
    key_segments = seg_col[...]
    key_sum = [None, None]
    value_sum = [None, None]
    query_total = jnp.zeros((1, LANES), jnp.float32)
    for block in range(length // rows):
        here = pl.ds(block * rows, rows)
        q = q_ref[here, :]
        do = do_ref[here, :]
        allowed = key_segments == seg_row[:, here]
        dots = lax.dot_general(
            pick,
            do.astype(jnp.float32) * o_ref[here, :].astype(jnp.float32),
            NT,
            precision=lax.Precision.HIGHEST,
            preferred_element_type=jnp.float32,
        )
        parts = []
        for head in range(2):
            scores = mxu(head_keys[head], q, NT)
            scores = jnp.where(allowed, scores, masked_score)
            probs = jnp.exp(scores - lse_ref[0, head : head + 1, here])
            prob_grad = mxu(head_values[head], do, NT)
            score_grad = (probs * (prob_grad - dots[head : head + 1, :])).astype(jnp.bfloat16)
            value_part = mxu(probs.astype(jnp.bfloat16), do, NN)
            key_part = mxu(score_grad, q, NN)
            value_sum[head] = value_part if block == 0 else value_sum[head] + value_part
            key_sum[head] = key_part if block == 0 else key_sum[head] + key_part
            parts.append(mxu(score_grad, keys, TN))
        query_grad = jnp.where(first, parts[0], parts[1]) * (1.0 / math.sqrt(HD))
        query_total = query_total + jnp.sum(query_grad, 0, keepdims=True)
        grad_ref[0, here, :] = query_grad.astype(jnp.bfloat16)
    grad_ref[1, :, :] = jnp.where(first, key_sum[0], key_sum[1]).astype(jnp.bfloat16)
    value_grad = jnp.where(first, value_sum[0], value_sum[1])
    grad_ref[2, :, :] = value_grad.astype(jnp.bfloat16)
    sum_ref[0:1, :] = query_total
    sum_ref[1:2, :] = jnp.sum(value_grad, 0, keepdims=True)


def attention_backward(q, k, v, out, out_grad, seg_col, seg_row, lse, start, pairs):
    length, width = q.shape
    rows = min(256, length)
    pair = pl.BlockSpec((length, LANES), lambda j: (0, j + start))
    return pl.pallas_call(
        functools.partial(attention_backward_kernel, rows=rows),
        grid=(pairs,),
        in_specs=[
            pair,
            pair,
            pair,
            pair,
            pair,
            pl.BlockSpec((length, 1), lambda j: (0, 0)),
            pl.BlockSpec((1, length), lambda j: (0, 0)),
            pl.BlockSpec((1, 2, length), lambda j: (j + start, 0, 0)),
        ],
        out_specs=[
            pl.BlockSpec((3, length, LANES), lambda j: (0, 0, j)),
            pl.BlockSpec((2, LANES), lambda j: (0, j)),
        ],
        out_shape=[
            jax.ShapeDtypeStruct((3, length, pairs * LANES), jnp.bfloat16),
            jax.ShapeDtypeStruct((2, pairs * LANES), jnp.float32),
        ],
        compiler_params=params(),
        cost_estimate=pl.CostEstimate(
            flops=40 * length * length * pairs * LANES,
            bytes_accessed=16 * length * pairs * LANES,
            transcendentals=0,
        ),
        name="attn_bwd",
    )(q, k, v, out, out_grad, seg_col, seg_row, lse)


class Place:
    def __init__(self, groups, shards):
        self.groups = groups
        self.shards = shards
        self.chips = shards // 2
        grp = lax.axis_index("grp")
        shard = lax.axis_index("shard")
        self.grp = grp
        self.shard = shard
        self.core = shard % 2
        self.chip = shard // 2
        self.scalars = jnp.stack([self.core, self.chip, grp]).astype(jnp.int32)

    def swap(self, array, grp=0, chip=0, core=0):
        mask = grp * self.shards + chip * 2 + core
        pairs = [(i, i ^ mask) for i in range(self.groups * self.shards)]
        return lax.ppermute(array, AXES, pairs)


def gather_pieces(place, piece):
    rows = piece.shape[0]
    half = rows // 2
    along = [piece] + [place.swap(piece, chip=k) for k in range(1, place.chips)]
    upper = [jnp.stack([p[:half] for p in along]), None, None, None]
    lower = [jnp.stack([p[half:] for p in along]), None, None, None]
    upper[1] = place.swap(upper[0], grp=1)
    lower[2] = place.swap(lower[0], grp=2)
    upper[2] = place.swap(upper[0], grp=2)
    lower[1] = place.swap(lower[0], grp=1)
    upper[3] = place.swap(upper[1], grp=2)
    lower[3] = place.swap(lower[2], grp=1)
    mine = upper + lower
    return mine + [place.swap(p, core=1) for p in mine]


def assemble_kernel(where, *refs, groups):
    *pieces, whole = refs
    _, half, cols = pieces[0].shape
    core, grp = where[0], where[2]
    for n, piece in enumerate(pieces):
        other_core, lower, other_grp = n // (2 * groups), (n // groups) % 2, n % groups
        col = pl.multiple_of((grp ^ other_grp) * cols, LANES)
        row = pl.multiple_of(((core ^ other_core) * 2 + lower) * half, half)
        whole[pl.ds(row, half), pl.ds(col, cols)] = piece[0]


def assemble(place, pieces, name):
    chips, half, cols = pieces[0].shape
    shape = (chips * 4 * half, place.groups * cols)
    return pl.pallas_call(
        functools.partial(assemble_kernel, groups=place.groups),
        grid_spec=pltpu.PrefetchScalarGridSpec(
            num_scalar_prefetch=1,
            grid=(chips,),
            in_specs=[pl.BlockSpec((1, half, cols), lambda i, s: (i ^ s[1], 0, 0))] * len(pieces),
            out_specs=pl.BlockSpec((4 * half, shape[1]), lambda i, s: (i, 0)),
        ),
        out_shape=jax.ShapeDtypeStruct(shape, jnp.bfloat16),
        compiler_params=params(),
        cost_estimate=pl.CostEstimate(
            flops=0, bytes_accessed=4 * shape[0] * shape[1], transcendentals=0
        ),
        name="assemble_" + name,
    )(place.scalars, *pieces)


def weight_grad_kernel(where, left_ref, right_ref, *refs, own, rows, groups, split):
    received = None
    if own:
        received, *outs = refs
    else:
        outs = refs
    core, grp = where[0], where[2]
    keep = core if own else 1 - core
    chips = left_ref.shape[1] // (2 * rows)
    lefts = []
    for k in range(chips):
        even = left_ref[:, 2 * k * rows : (2 * k + 1) * rows]
        odd = left_ref[:, (2 * k + 1) * rows : (2 * k + 2) * rows]
        lefts.append(jnp.where(keep == 0, even, odd))
    left = lefts[0] if chips == 1 else jnp.concatenate(lefts, 1)
    left = left.T
    half = rows // 2

    def emit(slot, result):
        result = result.reshape(chips, 2, half, result.shape[-1])
        if own:
            pos = 0 if split else slot
            result = result + received[pos].astype(jnp.float32)
            result = result.astype(jnp.bfloat16)
            for lower in range(2):
                outs[slot + lower * groups][...] = result[:, lower]
        else:
            outs[0][0 if split else slot] = result.astype(jnp.bfloat16)

    if split:
        if len(right_ref.shape) == 3:
            result = jnp.concatenate(
                [mxu(left, right_ref[n], NN) for n in range(right_ref.shape[0])], 1
            )
        else:
            result = mxu(left, right_ref[...], NN)
        if own:
            for slot in range(groups):
                pl.when(pl.program_id(1) == slot)(functools.partial(emit, slot, result))
        else:
            emit(0, result)
    else:
        cols = right_ref.shape[1] // groups
        for slot in range(groups):
            at = pl.multiple_of((grp ^ slot) * cols, LANES)
            emit(slot, mxu(left, right_ref[:, pl.ds(at, cols)], NN))


def weight_grad(place, left, right, received, split, name):
    tokens, height = left.shape
    groups, chips = place.groups, place.chips
    rows = height // place.shards
    half = rows // 2
    parts = right.shape[0] if right.ndim == 3 else 1
    width = right.shape[-1] * parts
    cols = width // groups
    own = received is not None
    step_chips = chips if split else max(1, 1024 // (2 * rows))
    steps = chips // step_chips
    if split:
        grid = (steps, groups)
        if parts > 1:
            right_spec = pl.BlockSpec(
                (parts, tokens, cols // parts), lambda i, j, s: (0, 0, j ^ s[2])
            )
        else:
            right_spec = pl.BlockSpec((tokens, cols), lambda i, j, s: (0, j ^ s[2]))
        passed = pl.BlockSpec((1, step_chips, 2, half, cols), lambda i, j, s: (j, i, 0, 0, 0))
    else:
        grid = (steps, 1)
        right_spec = pl.BlockSpec((tokens, width), lambda i, j, s: (0, 0))
        passed = pl.BlockSpec((groups, step_chips, 2, half, cols), lambda i, j, s: (0, i, 0, 0, 0))
    in_specs = [pl.BlockSpec((tokens, step_chips * 2 * rows), lambda i, j, s: (0, i)), right_spec]
    inputs = [left, right]
    if own:
        in_specs.append(passed)
        inputs.append(received)
        out_specs = [pl.BlockSpec((step_chips, half, cols), lambda i, j, s: (i, 0, 0))] * (2 * groups)
        out_shape = [jax.ShapeDtypeStruct((chips, half, cols), jnp.bfloat16)] * (2 * groups)
    else:
        out_specs = passed
        out_shape = jax.ShapeDtypeStruct((groups, chips, 2, half, cols), jnp.bfloat16)
    return pl.pallas_call(
        functools.partial(
            weight_grad_kernel, own=own, rows=rows, groups=groups, split=split
        ),
        grid_spec=pltpu.PrefetchScalarGridSpec(
            num_scalar_prefetch=1, grid=grid, in_specs=in_specs, out_specs=out_specs
        ),
        out_shape=out_shape,
        compiler_params=params(),
        cost_estimate=pl.CostEstimate(
            flops=tokens * height * width,
            bytes_accessed=2 * (tokens * (height + width) + height * width),
            transcendentals=0,
        ),
        name="wgrad_" + name + ("_own" if own else "_sent"),
    )(place.scalars, *inputs)


def add(*terms):
    total = terms[0].astype(jnp.float32)
    for term in terms[1:]:
        total = total + term.astype(jnp.float32)
    return total.astype(jnp.bfloat16)


def reduce_weight(place, left, right, split, name):
    groups, chips = place.groups, place.chips
    sent = weight_grad(place, left, right, None, split, name)
    received = place.swap(sent, core=1)
    own = weight_grad(place, left, right, received, split, name)
    upper, lower = own[:groups], own[groups:]
    upper_1, upper_3 = place.swap(upper[1], grp=1), place.swap(upper[3], grp=1)
    lower_2, lower_3 = place.swap(lower[2], grp=2), place.swap(lower[3], grp=2)
    upper_2 = place.swap(add(upper[2], upper_3), grp=2)
    lower_1 = place.swap(add(lower[1], lower_3), grp=1)
    mine = jnp.concatenate([add(upper[0], upper_1, upper_2), add(lower[0], lower_2, lower_1)], 1)
    terms = [lax.dynamic_index_in_dim(mine, place.chip, 0, False)]
    for k in range(1, chips):
        outgoing = lax.dynamic_index_in_dim(mine, place.chip ^ k, 0, False)
        terms.append(place.swap(outgoing, chip=k))
    share = add(*terms)
    return replicate(place, share)


def replicate(place, share):
    blocks = [share] + [place.swap(share, grp=k) for k in range(1, place.groups)]
    blocks = [b.astype(jnp.float32) for b in blocks]
    ordered = []
    for g in range(place.groups):
        block = blocks[0]
        for k in range(1, place.groups):
            block = jnp.where((place.grp ^ k) == g, blocks[k], block)
        ordered.append(block)
    return ordered


def sum_everywhere(place, vector):
    for how in ({"core": 1}, {"grp": 1}, {"grp": 2}):
        vector = vector + place.swap(vector, **how)
    step = 1
    while step < place.chips:
        vector = vector + place.swap(vector, chip=step)
        step *= 2
    return vector


def own_part(place, vector):
    size = vector.shape[0] // place.shards
    return lax.dynamic_slice_in_dim(vector, place.shard * size, size)


def on_device_permutes(
    tokens,
    segment_ids,
    keep_flag,
    cotangent,
    w_qkv,
    b_query,
    b_value,
    w_attn_out,
    b_attn_out,
    norm1_gain,
    norm1_bias,
    w_in,
    b_in,
    w_out,
    b_out,
    norm2_gain,
    norm2_bias,
    *,
    groups,
    shards,
):
    place = Place(groups, shards)
    _, length, width = tokens.shape
    vectors = (
        b_query,
        b_value,
        b_attn_out,
        norm1_gain,
        norm1_bias,
        b_in,
        b_out,
        norm2_gain,
        norm2_bias,
    )
    packed = lax.all_gather(jnp.concatenate(vectors), "shard", axis=0)
    unpacked = []
    at = 0
    for vector in vectors:
        size = vector.shape[0]
        unpacked.append(packed[:, at : at + size].reshape(1, -1).astype(jnp.float32))
        at += size
    (
        bias_query,
        bias_value,
        bias_attn,
        gain_one,
        shift_one,
        bias_in,
        bias_out,
        gain_two,
        shift_two,
    ) = unpacked
    full_qkv = assemble(place, gather_pieces(place, w_qkv), "qkv")
    full_attn = assemble(place, gather_pieces(place, w_attn_out), "attn")
    full_in = assemble(place, gather_pieces(place, w_in), "in")
    full_out = assemble(place, gather_pieces(place, w_out), "out")

    rows = tokens[0]
    seg_row = segment_ids.reshape(1, length)
    seg_col = segment_ids.reshape(length, 1)
    scaling = 1.0 / math.sqrt(HD)
    mixed_qkv = jnp.dot(rows, full_qkv, preferred_element_type=jnp.float32)
    queries = ((mixed_qkv[:, :width] + bias_query).astype(jnp.bfloat16) * scaling).astype(
        jnp.bfloat16
    )
    key_rows = mixed_qkv[:, width : 2 * width].astype(jnp.bfloat16)
    value_rows = (mixed_qkv[:, 2 * width :] + bias_value).astype(jnp.bfloat16)
    contexts, lse = attention_forward(queries, key_rows, value_rows, seg_col, seg_row)
    attended = jnp.dot(contexts, full_attn, preferred_element_type=jnp.float32) + bias_attn
    first_sum = rows.astype(jnp.float32) + attended
    normed_one, norm_one_back = jax.vjp(norm_layer, first_sum, gain_one, shift_one)
    normed_low = normed_one.astype(jnp.bfloat16)
    hidden_pre = jnp.dot(normed_low, full_in, preferred_element_type=jnp.float32) + bias_in
    hidden, gelu_back = jax.vjp(gelu_exact, hidden_pre)
    hidden_low = hidden.astype(jnp.bfloat16)
    second_sum = normed_one + (
        jnp.dot(hidden_low, full_out, preferred_element_type=jnp.float32) + bias_out
    )
    result, norm_two_back = jax.vjp(norm_layer, second_sum, gain_two, shift_two)
    layer_out = result.astype(jnp.bfloat16)[None]

    masked_cot = cotangent[0].astype(jnp.float32) * keep_flag.reshape(length, 1).astype(jnp.float32)
    second_grad, gain_two_grad, shift_two_grad = norm_two_back(masked_cot)
    bias_out_grad = jnp.sum(second_grad, 0)
    out_low = second_grad.astype(jnp.bfloat16)
    w_out_grad = reduce_weight(place, hidden_low, out_low, False, "out")
    hidden_grad = contract_cols(out_low, full_out)
    (pre_grad,) = gelu_back(hidden_grad)
    bias_in_grad = jnp.sum(pre_grad, 0)
    pre_low = pre_grad.astype(jnp.bfloat16)
    w_in_grad = reduce_weight(place, normed_low, pre_low, True, "in")
    normed_grad = second_grad + contract_cols(pre_low, full_in)
    first_grad, gain_one_grad, shift_one_grad = norm_one_back(normed_grad)
    bias_attn_grad = jnp.sum(first_grad, 0)
    attn_low = first_grad.astype(jnp.bfloat16)
    w_attn_grad = reduce_weight(place, contexts, attn_low, False, "attn")
    context_grad = contract_cols(attn_low, full_attn).astype(jnp.bfloat16)
    early = (
        bias_attn_grad,
        gain_one_grad[0],
        shift_one_grad[0],
        bias_in_grad,
        bias_out_grad,
        gain_two_grad[0],
        shift_two_grad[0],
    )
    early_sum = sum_everywhere(place, jnp.concatenate(early).reshape(-1, LANES)).reshape(-1)
    early_parts = []
    at = 0
    for vector in early:
        early_parts.append(own_part(place, early_sum[at : at + vector.shape[0]]))
        at += vector.shape[0]

    qkv_low, late = attention_backward(
        queries,
        key_rows,
        value_rows,
        contexts,
        context_grad,
        seg_col,
        seg_row,
        lse,
        0,
        width // LANES,
    )
    late_sum = sum_everywhere(place, late)
    w_qkv_grad = reduce_weight(place, rows, qkv_low, True, "qkv")
    input_grad = first_grad
    for n in range(3):
        input_grad = input_grad + contract_cols(
            qkv_low[n], full_qkv[:, n * width : (n + 1) * width]
        )
    heads = width // groups
    w_qkv_grad = jnp.concatenate(
        [block[:, n * heads : (n + 1) * heads] for n in range(3) for block in w_qkv_grad], 1
    )
    return (
        layer_out,
        input_grad[None],
        w_qkv_grad,
        own_part(place, late_sum[0]),
        own_part(place, late_sum[1]),
        jnp.concatenate(w_attn_grad, 1),
        early_parts[0],
        early_parts[1],
        early_parts[2],
        jnp.concatenate(w_in_grad, 1),
        early_parts[3],
        jnp.concatenate(w_out_grad, 1),
        early_parts[4],
        early_parts[5],
        early_parts[6],
    )


def solution(mesh):
    groups, shards = mesh.shape["grp"], mesh.shape["shard"]
    if groups == 4 and shards == 8:
        body = functools.partial(on_device_permutes, groups=groups, shards=shards)
    else:
        body = on_device
    return jax.shard_map(
        body,
        mesh=mesh,
        in_specs=(
            P(("grp", "shard"), None, None),
            P(("grp", "shard"), None),
            P(("grp", "shard"), None),
            P(("grp", "shard"), None, None),
            P("shard", "grp"),
            P("shard"),
            P("shard"),
            P("shard", "grp"),
            P("shard"),
            P("shard"),
            P("shard"),
            P("shard", "grp"),
            P("shard"),
            P("shard", "grp"),
            P("shard"),
            P("shard"),
            P("shard"),
        ),
        out_specs=(
            P(("grp", "shard"), None, None),
            P(("grp", "shard"), None, None),
            P("shard", None),
            P("shard"),
            P("shard"),
            P("shard", None),
            P("shard"),
            P("shard"),
            P("shard"),
            P("shard", None),
            P("shard"),
            P("shard", None),
            P("shard"),
            P("shard"),
            P("shard"),
        ),
        check_vma=False,
    )
```

```python
import functools
import math

import jax
import jax.numpy as jnp
from jax import lax
from jax.experimental import pallas as pl
from jax.experimental.pallas import tpu as pltpu
from jax.sharding import PartitionSpec as P

H = 16
HD = 64


masked_score = -1e30
epsilon = 1e-05


def norm_layer(rows, gain_row, shift_row):
    row_mean = jnp.mean(rows, -1, keepdims=True)
    centered = rows - row_mean
    row_var = jnp.mean(centered * centered, -1, keepdims=True)
    return centered * lax.rsqrt(row_var + epsilon) * gain_row + shift_row


def gelu_exact(values):
    return 0.5 * values * (1.0 + lax.erf(values * (1.0 / math.sqrt(2.0))))


def contract_rows(left, right):
    return lax.dot_general(
        left, right, (((0,), (0,)), ((), ())), preferred_element_type=jnp.float32
    )


def contract_cols(left, right):
    return lax.dot_general(
        left, right, (((1,), (1,)), ((), ())), preferred_element_type=jnp.float32
    )


def attend_forward(queries, key_rows, value_rows, segment_row, block_rows):
    length, model_width = queries.shape
    scaling = 1.0 / math.sqrt(HD)
    key_heads = key_rows.reshape(length, H, HD)
    value_heads = value_rows.reshape(length, H, HD)
    query_blocks = queries.reshape(length // block_rows, block_rows, H, HD)
    segment_blocks = segment_row.reshape(length // block_rows, block_rows)

    def one_block(pieces):
        query_part, segment_part = pieces
        scores = (
            jnp.einsum("qhd,khd->hqk", query_part, key_heads, preferred_element_type=jnp.float32)
            * scaling
        )
        allowed = segment_part[:, None] == segment_row[None, :]
        scores = jnp.where(allowed[None], scores, masked_score)
        row_max = jnp.max(scores, -1, keepdims=True)
        powers = jnp.exp(scores - row_max)
        totals = jnp.sum(powers, -1, keepdims=True)
        attn_probs = (powers / totals).astype(jnp.bfloat16)
        context = jnp.einsum(
            "hqk,khd->qhd", attn_probs, value_heads, preferred_element_type=jnp.float32
        )
        return (
            context.reshape(block_rows, model_width).astype(jnp.bfloat16),
            (row_max + jnp.log(totals))[:, :, 0],
        )

    contexts, log_sums = lax.map(one_block, (query_blocks, segment_blocks))
    return (contexts.reshape(length, model_width), log_sums)


def attend_backward(queries, key_rows, value_rows, segment_row, log_sums, context_grad, block_rows):
    length, model_width = queries.shape
    scaling = 1.0 / math.sqrt(HD)
    key_heads = key_rows.reshape(length, H, HD)
    value_heads = value_rows.reshape(length, H, HD)
    query_blocks = queries.reshape(length // block_rows, block_rows, H, HD)
    segment_blocks = segment_row.reshape(length // block_rows, block_rows)
    grad_blocks = context_grad.reshape(length // block_rows, block_rows, H, HD)

    def one_block(running, pieces):
        key_acc, value_acc = running
        query_part, segment_part, lse_part, grad_part = pieces
        scores = (
            jnp.einsum("qhd,khd->hqk", query_part, key_heads, preferred_element_type=jnp.float32)
            * scaling
        )
        allowed = segment_part[:, None] == segment_row[None, :]
        scores = jnp.where(allowed[None], scores, masked_score)
        probs = jnp.exp(scores - lse_part[:, :, None])
        prob_low = probs.astype(jnp.bfloat16)
        prob_grad = jnp.einsum(
            "qhd,khd->hqk", grad_part, value_heads, preferred_element_type=jnp.float32
        )
        row_dot = jnp.sum(prob_grad * probs, -1, keepdims=True)
        score_grad = (probs * (prob_grad - row_dot)).astype(jnp.bfloat16)
        query_grad = (
            jnp.einsum("hqk,khd->qhd", score_grad, key_heads, preferred_element_type=jnp.float32)
            * scaling
        )
        key_acc = (
            key_acc
            + jnp.einsum("hqk,qhd->khd", score_grad, query_part, preferred_element_type=jnp.float32)
            * scaling
        )
        value_acc = value_acc + jnp.einsum(
            "hqk,qhd->khd", prob_low, grad_part, preferred_element_type=jnp.float32
        )
        return ((key_acc, value_acc), query_grad.reshape(block_rows, model_width))

    empty_acc = jnp.zeros((length, H, HD), jnp.float32)
    (key_grad, value_grad), query_grads = lax.scan(
        one_block, (empty_acc, empty_acc), (query_blocks, segment_blocks, log_sums, grad_blocks)
    )
    return (
        query_grads.reshape(length, model_width),
        key_grad.reshape(length, model_width),
        value_grad.reshape(length, model_width),
    )


def on_device(
    tokens,
    segment_ids,
    keep_flag,
    cotangent,
    w_qkv,
    b_query,
    b_value,
    w_attn_out,
    b_attn_out,
    norm1_gain,
    norm1_bias,
    w_in,
    b_in,
    w_out,
    b_out,
    norm2_gain,
    norm2_bias,
):
    seq_count, length, model_width = tokens.shape
    block_rows = min(512, length)
    within = (
        lax.all_gather(w_qkv, "shard", axis=0, tiled=True),
        lax.all_gather(w_attn_out, "shard", axis=0, tiled=True),
        lax.all_gather(w_in, "shard", axis=0, tiled=True),
        lax.all_gather(w_out, "shard", axis=0, tiled=True),
        lax.all_gather(b_query, "shard", axis=0, tiled=True),
        lax.all_gather(b_value, "shard", axis=0, tiled=True),
        lax.all_gather(b_attn_out, "shard", axis=0, tiled=True),
        lax.all_gather(norm1_gain, "shard", axis=0, tiled=True),
        lax.all_gather(norm1_bias, "shard", axis=0, tiled=True),
        lax.all_gather(b_in, "shard", axis=0, tiled=True),
        lax.all_gather(b_out, "shard", axis=0, tiled=True),
        lax.all_gather(norm2_gain, "shard", axis=0, tiled=True),
        lax.all_gather(norm2_bias, "shard", axis=0, tiled=True),
    )
    full_qkv, full_attn, full_in, full_out = (
        lax.all_gather(within[0], "grp", axis=1, tiled=True),
        lax.all_gather(within[1], "grp", axis=1, tiled=True),
        lax.all_gather(within[2], "grp", axis=1, tiled=True),
        lax.all_gather(within[3], "grp", axis=1, tiled=True),
    )
    (
        bias_query,
        bias_value,
        bias_attn,
        gain_one,
        shift_one,
        bias_in,
        bias_out,
        gain_two,
        shift_two,
    ) = [piece.astype(jnp.float32) for piece in within[4:]]
    flat_rows = tokens.reshape(seq_count * length, model_width)
    mixed_qkv = jnp.dot(flat_rows, full_qkv, preferred_element_type=jnp.float32)
    queries = (mixed_qkv[:, :model_width] + bias_query).astype(jnp.bfloat16)
    key_rows = mixed_qkv[:, model_width : 2 * model_width].astype(jnp.bfloat16)
    value_rows = (mixed_qkv[:, 2 * model_width :] + bias_value).astype(jnp.bfloat16)
    query_seqs = queries.reshape(seq_count, length, model_width)
    key_seqs = key_rows.reshape(seq_count, length, model_width)
    value_seqs = value_rows.reshape(seq_count, length, model_width)

    def forward_sequence(pieces):
        return attend_forward(pieces[0], pieces[1], pieces[2], pieces[3], block_rows)

    contexts, log_sums = lax.map(forward_sequence, (query_seqs, key_seqs, value_seqs, segment_ids))
    contexts = contexts.reshape(seq_count * length, model_width)
    attended = jnp.dot(contexts, full_attn, preferred_element_type=jnp.float32) + bias_attn
    first_sum = flat_rows.astype(jnp.float32) + attended
    normed_one, norm_one_back = jax.vjp(norm_layer, first_sum, gain_one, shift_one)
    normed_low = normed_one.astype(jnp.bfloat16)
    hidden_pre = jnp.dot(normed_low, full_in, preferred_element_type=jnp.float32) + bias_in
    hidden, gelu_back = jax.vjp(gelu_exact, hidden_pre)
    hidden_low = hidden.astype(jnp.bfloat16)
    second_sum = normed_one + (
        jnp.dot(hidden_low, full_out, preferred_element_type=jnp.float32) + bias_out
    )
    result, norm_two_back = jax.vjp(norm_layer, second_sum, gain_two, shift_two)
    layer_out = result.astype(jnp.bfloat16).reshape(seq_count, length, model_width)
    again = (
        lax.all_gather(w_qkv, "shard", axis=0, tiled=True),
        lax.all_gather(w_attn_out, "shard", axis=0, tiled=True),
        lax.all_gather(w_in, "shard", axis=0, tiled=True),
        lax.all_gather(w_out, "shard", axis=0, tiled=True),
    )
    back_qkv, back_attn, back_in, back_out = (
        lax.all_gather(again[0], "grp", axis=1, tiled=True),
        lax.all_gather(again[1], "grp", axis=1, tiled=True),
        lax.all_gather(again[2], "grp", axis=1, tiled=True),
        lax.all_gather(again[3], "grp", axis=1, tiled=True),
    )
    masked_cot = cotangent.astype(jnp.float32).reshape(
        seq_count * length, model_width
    ) * keep_flag.reshape(seq_count * length, 1).astype(jnp.float32)
    second_grad, gain_two_grad, shift_two_grad = norm_two_back(masked_cot)
    bias_out_grad = jnp.sum(second_grad, 0)
    out_low = second_grad.astype(jnp.bfloat16)
    w_out_grad = contract_rows(hidden_low, out_low)
    hidden_grad = contract_cols(out_low, back_out)
    (pre_grad,) = gelu_back(hidden_grad)
    bias_in_grad = jnp.sum(pre_grad, 0)
    pre_low = pre_grad.astype(jnp.bfloat16)
    w_in_grad = contract_rows(normed_low, pre_low)
    normed_grad = second_grad + contract_cols(pre_low, back_in)
    first_grad, gain_one_grad, shift_one_grad = norm_one_back(normed_grad)
    bias_attn_grad = jnp.sum(first_grad, 0)
    attn_low = first_grad.astype(jnp.bfloat16)
    w_attn_grad = contract_rows(contexts, attn_low)
    context_grad = contract_cols(attn_low, back_attn).astype(jnp.bfloat16)

    def backward_sequence(pieces):
        return attend_backward(
            pieces[0], pieces[1], pieces[2], pieces[3], pieces[4], pieces[5], block_rows
        )

    query_grad, key_grad, value_grad = lax.map(
        backward_sequence,
        (
            query_seqs,
            key_seqs,
            value_seqs,
            segment_ids,
            log_sums,
            context_grad.reshape(seq_count, length, model_width),
        ),
    )
    query_grad = query_grad.reshape(seq_count * length, model_width)
    key_grad = key_grad.reshape(seq_count * length, model_width)
    value_grad = value_grad.reshape(seq_count * length, model_width)
    bias_query_grad = jnp.sum(query_grad, 0)
    bias_value_grad = jnp.sum(value_grad, 0)
    qkv_low = jnp.concatenate([query_grad, key_grad, value_grad], 1).astype(jnp.bfloat16)
    w_qkv_grad = contract_rows(flat_rows, qkv_low)
    input_grad = first_grad + contract_cols(qkv_low, back_qkv)
    reduced = (
        lax.psum_scatter(
            w_qkv_grad.astype(jnp.bfloat16), "shard", scatter_dimension=0, tiled=True
        ).astype(jnp.float32),
        lax.psum_scatter(
            bias_query_grad.astype(jnp.bfloat16), "shard", scatter_dimension=0, tiled=True
        ).astype(jnp.float32),
        lax.psum_scatter(
            bias_value_grad.astype(jnp.bfloat16), "shard", scatter_dimension=0, tiled=True
        ).astype(jnp.float32),
        lax.psum_scatter(
            w_attn_grad.astype(jnp.bfloat16), "shard", scatter_dimension=0, tiled=True
        ).astype(jnp.float32),
        lax.psum_scatter(
            bias_attn_grad.astype(jnp.bfloat16), "shard", scatter_dimension=0, tiled=True
        ).astype(jnp.float32),
        lax.psum_scatter(
            gain_one_grad.astype(jnp.bfloat16), "shard", scatter_dimension=0, tiled=True
        ).astype(jnp.float32),
        lax.psum_scatter(
            shift_one_grad.astype(jnp.bfloat16), "shard", scatter_dimension=0, tiled=True
        ).astype(jnp.float32),
        lax.psum_scatter(
            w_in_grad.astype(jnp.bfloat16), "shard", scatter_dimension=0, tiled=True
        ).astype(jnp.float32),
        lax.psum_scatter(
            bias_in_grad.astype(jnp.bfloat16), "shard", scatter_dimension=0, tiled=True
        ).astype(jnp.float32),
        lax.psum_scatter(
            w_out_grad.astype(jnp.bfloat16), "shard", scatter_dimension=0, tiled=True
        ).astype(jnp.float32),
        lax.psum_scatter(
            bias_out_grad.astype(jnp.bfloat16), "shard", scatter_dimension=0, tiled=True
        ).astype(jnp.float32),
        lax.psum_scatter(
            gain_two_grad.astype(jnp.bfloat16), "shard", scatter_dimension=0, tiled=True
        ).astype(jnp.float32),
        lax.psum_scatter(
            shift_two_grad.astype(jnp.bfloat16), "shard", scatter_dimension=0, tiled=True
        ).astype(jnp.float32),
    )
    summed = (
        lax.psum(reduced[0].astype(jnp.bfloat16), "grp").astype(jnp.float32),
        lax.psum(reduced[1].astype(jnp.bfloat16), "grp").astype(jnp.float32),
        lax.psum(reduced[2].astype(jnp.bfloat16), "grp").astype(jnp.float32),
        lax.psum(reduced[3].astype(jnp.bfloat16), "grp").astype(jnp.float32),
        lax.psum(reduced[4].astype(jnp.bfloat16), "grp").astype(jnp.float32),
        lax.psum(reduced[5].astype(jnp.bfloat16), "grp").astype(jnp.float32),
        lax.psum(reduced[6].astype(jnp.bfloat16), "grp").astype(jnp.float32),
        lax.psum(reduced[7].astype(jnp.bfloat16), "grp").astype(jnp.float32),
        lax.psum(reduced[8].astype(jnp.bfloat16), "grp").astype(jnp.float32),
        lax.psum(reduced[9].astype(jnp.bfloat16), "grp").astype(jnp.float32),
        lax.psum(reduced[10].astype(jnp.bfloat16), "grp").astype(jnp.float32),
        lax.psum(reduced[11].astype(jnp.bfloat16), "grp").astype(jnp.float32),
        lax.psum(reduced[12].astype(jnp.bfloat16), "grp").astype(jnp.float32),
    )
    return (
        layer_out,
        input_grad.reshape(seq_count, length, model_width),
        summed[0],
        summed[1],
        summed[2],
        summed[3],
        summed[4],
        summed[5],
        summed[6],
        summed[7],
        summed[8],
        summed[9],
        summed[10],
        summed[11],
        summed[12],
    )


NT = (((1,), (1,)), ((), ()))
NN = (((1,), (0,)), ((), ()))
TN = (((0,), (0,)), ((), ()))
LANES = 128
AXES = ("grp", "shard")


def mxu(left, right, dims):
    return lax.dot_general(left, right, dims, preferred_element_type=jnp.float32)


def params(megabytes=60):
    return pltpu.CompilerParams(vmem_limit_bytes=megabytes << 20)


def attention_forward_kernel(q_ref, k_ref, v_ref, seg_col, seg_row, out_ref, lse_ref, *, rows):
    length = q_ref.shape[0]
    first = lax.broadcasted_iota(jnp.int32, (1, LANES), 1) < HD
    keys = k_ref[...]
    values = v_ref[...]
    zero = jnp.zeros_like(keys)
    head_keys = (jnp.where(first, keys, zero), jnp.where(first, zero, keys))
    key_segments = seg_col[...]
    for block in range(length // rows):
        here = pl.ds(block * rows, rows)
        q = q_ref[here, :]
        allowed = key_segments == seg_row[:, here]
        outs = []
        for head in range(2):
            scores = mxu(head_keys[head], q, NT)
            scores = jnp.where(allowed, scores, masked_score)
            top = jnp.max(scores, 0, keepdims=True)
            powers = jnp.exp(scores - top)
            total = jnp.sum(powers, 0, keepdims=True)
            part = mxu(powers.astype(jnp.bfloat16), values, TN)
            outs.append(part * jnp.transpose(jnp.broadcast_to(1.0 / total, (LANES, rows))))
            lse_ref[0, head : head + 1, here] = top + jnp.log(total)
        out_ref[here, :] = jnp.where(first, outs[0], outs[1]).astype(jnp.bfloat16)


def attention_forward(qkv, seg_col, seg_row, start, pairs, before=None):
    length, width = qkv.shape[0], qkv.shape[1] // 3
    total = width // LANES
    rows = min(512, length)
    anywhere = pl.BlockSpec(memory_space=pl.ANY)

    def pair(part):
        return pl.BlockSpec((length, LANES), lambda j: (0, part * total + start + j))

    def body(q_ref, k_ref, v_ref, seg_c, seg_r, *refs):
        attention_forward_kernel(q_ref, k_ref, v_ref, seg_c, seg_r, *refs[-2:], rows=rows)

    return pl.pallas_call(
        body,
        grid=(pairs,),
        in_specs=[
            pair(0),
            pair(1),
            pair(2),
            pl.BlockSpec((length, 1), lambda j: (0, 0)),
            pl.BlockSpec((1, length), lambda j: (0, 0)),
        ]
        + [anywhere] * (0 if before is None else 2),
        out_specs=[
            pl.BlockSpec((length, LANES), lambda j: (0, start + j)),
            pl.BlockSpec((1, 2, length), lambda j: (start + j, 0, 0)),
        ],
        out_shape=[
            jax.ShapeDtypeStruct((length, width), jnp.bfloat16),
            jax.ShapeDtypeStruct((total, 2, length), jnp.float32),
        ],
        input_output_aliases={} if before is None else {5: 0, 6: 1},
        compiler_params=params(40),
        cost_estimate=pl.CostEstimate(
            flops=16 * length * length * pairs * LANES,
            bytes_accessed=8 * length * pairs * LANES,
            transcendentals=0,
        ),
        name="attn_fwd",
    )(qkv, qkv, qkv, seg_col, seg_row, *(() if before is None else before))


def attention_backward_kernel(
    q_ref, k_ref, v_ref, o_ref, do_ref, seg_col, seg_row, lse_ref, grad_ref, sum_ref, *, rows
):
    length = q_ref.shape[0]
    lane = lax.broadcasted_iota(jnp.int32, (1, LANES), 1)
    first = lane < HD
    pick = (
        lax.broadcasted_iota(jnp.int32, (8, LANES), 0)
        == lax.broadcasted_iota(jnp.int32, (8, LANES), 1) // HD
    ).astype(jnp.float32)
    keys = k_ref[...]
    values = v_ref[...]
    zero = jnp.zeros_like(keys)
    head_keys = (jnp.where(first, keys, zero), jnp.where(first, zero, keys))
    head_values = (jnp.where(first, values, zero), jnp.where(first, zero, values))
    key_segments = seg_col[...]
    key_sum = [None, None]
    value_sum = [None, None]
    query_total = jnp.zeros((1, LANES), jnp.float32)
    for block in range(length // rows):
        here = pl.ds(block * rows, rows)
        q = q_ref[here, :]
        do = do_ref[here, :]
        allowed = key_segments == seg_row[:, here]
        dots = lax.dot_general(
            pick,
            do.astype(jnp.float32) * o_ref[here, :].astype(jnp.float32),
            NT,
            precision=lax.Precision.HIGHEST,
            preferred_element_type=jnp.float32,
        )
        parts = []
        for head in range(2):
            scores = mxu(head_keys[head], q, NT)
            scores = jnp.where(allowed, scores, masked_score)
            probs = jnp.exp(scores - lse_ref[0, head : head + 1, here])
            prob_grad = mxu(head_values[head], do, NT)
            score_grad = (probs * (prob_grad - dots[head : head + 1, :])).astype(jnp.bfloat16)
            value_part = mxu(probs.astype(jnp.bfloat16), do, NN)
            key_part = mxu(score_grad, q, NN)
            value_sum[head] = value_part if block == 0 else value_sum[head] + value_part
            key_sum[head] = key_part if block == 0 else key_sum[head] + key_part
            parts.append(mxu(score_grad, keys, TN))
        query_grad = jnp.where(first, parts[0], parts[1]) * (1.0 / math.sqrt(HD))
        query_total = query_total + jnp.sum(query_grad, 0, keepdims=True)
        grad_ref[0, here, :] = query_grad.astype(jnp.bfloat16)
    grad_ref[1, :, :] = jnp.where(first, key_sum[0], key_sum[1]).astype(jnp.bfloat16)
    value_grad = jnp.where(first, value_sum[0], value_sum[1])
    grad_ref[2, :, :] = value_grad.astype(jnp.bfloat16)
    sum_ref[0:1, :] = query_total
    sum_ref[1:2, :] = jnp.sum(value_grad, 0, keepdims=True)


def attention_backward(qkv, out, out_grad, seg_col, seg_row, lse, start, pairs, at, size, before=None):
    length, width = out.shape
    total = width // LANES
    rows = min(256, length)
    anywhere = pl.BlockSpec(memory_space=pl.ANY)

    def pair(part):
        return pl.BlockSpec((length, LANES), lambda j: (0, part * total + start + j))

    def body(*refs):
        attention_backward_kernel(*refs[:8], *refs[-2:], rows=rows)

    return pl.pallas_call(
        body,
        grid=(pairs,),
        in_specs=[
            pair(0),
            pair(1),
            pair(2),
            pair(0),
            pair(0),
            pl.BlockSpec((length, 1), lambda j: (0, 0)),
            pl.BlockSpec((1, length), lambda j: (0, 0)),
            pl.BlockSpec((1, 2, length), lambda j: (j + start, 0, 0)),
        ]
        + [anywhere] * (0 if before is None else 2),
        out_specs=[
            pl.BlockSpec((3, length, LANES), lambda j: (0, 0, j + at)),
            pl.BlockSpec((2, LANES), lambda j: (0, j + at)),
        ],
        out_shape=[
            jax.ShapeDtypeStruct((3, length, size * LANES), jnp.bfloat16),
            jax.ShapeDtypeStruct((2, size * LANES), jnp.float32),
        ],
        input_output_aliases={} if before is None else {8: 0, 9: 1},
        compiler_params=params(40),
        cost_estimate=pl.CostEstimate(
            flops=40 * length * length * pairs * LANES,
            bytes_accessed=16 * length * pairs * LANES,
            transcendentals=0,
        ),
        name="attn_bwd",
    )(qkv, qkv, qkv, out, out_grad, seg_col, seg_row, lse, *(() if before is None else before))


class Place:
    def __init__(self, groups, shards):
        self.groups = groups
        self.shards = shards
        self.chips = shards // 2
        grp = lax.axis_index("grp")
        shard = lax.axis_index("shard")
        self.grp = grp
        self.shard = shard
        self.core = shard % 2
        self.chip = shard // 2
        self.scalars = jnp.stack([self.core, self.chip, grp]).astype(jnp.int32)

    def swap(self, array, grp=0, chip=0, core=0):
        mask = grp * self.shards + chip * 2 + core
        pairs = [(i, i ^ mask) for i in range(self.groups * self.shards)]
        return lax.ppermute(array, AXES, pairs)


def after(value, *others):
    return lax.optimization_barrier((value, *others))[0]


class Gather:
    def __init__(self, place, piece):
        self.place = place
        half = piece.shape[0] // 2
        self.halves = [piece[:half], piece[half:]]
        self.mine = [[None] * place.groups for _ in range(2)]
        self.theirs = [[None] * place.groups for _ in range(2)]

    def chips(self, half, *wait):
        piece = after(self.halves[half], *wait) if wait else self.halves[half]
        place = self.place
        along = [piece] + [place.swap(piece, chip=k) for k in range(1, place.chips)]
        self.mine[half][0] = jnp.stack(along)
        return self.mine[half][0]

    def near(self, half, *wait):
        slots = self.mine[half]
        piece = after(slots[0], *wait) if wait else slots[0]
        order = (1, 2) if half == 0 else (2, 1)
        for k in order:
            slots[k] = self.place.swap(piece, grp=k)
        return slots[order[0]]

    def far(self, half, *wait):
        slots = self.mine[half]
        first, second = (1, 2) if half == 0 else (2, 1)
        piece = after(slots[first], *wait) if wait else slots[first]
        slots[3] = self.place.swap(piece, grp=second)
        return slots[3]

    def cross(self, half, slot, *wait):
        piece = self.mine[half][slot]
        piece = after(piece, *wait) if wait else piece
        self.theirs[half][slot] = self.place.swap(piece, core=1)

    def pieces(self):
        return [p for side in (self.mine, self.theirs) for half in side for p in half]


def fetch(where, pieces, whole, sem, groups, by):
    chips, half, cols = pieces[0].shape
    core, chip, grp = where[0], where[1], where[2]
    for k in range(chips):
        for n, piece in enumerate(pieces):
            other_core, lower, other_grp = n // (2 * groups), (n // groups) % 2, n % groups
            col = pl.multiple_of((grp ^ other_grp) * cols, LANES)
            row = pl.multiple_of((((chip ^ k) * 2 + (core ^ other_core)) * 2 + lower) * half, half)
            slot = {"grp": other_grp, "chip": k, "all": 0}[by]
            pltpu.make_async_copy(
                piece.at[k], whole.at[pl.ds(row, half), pl.ds(col, cols)], sem.at[slot]
            ).start()


def fetched(view, sem):
    pltpu.make_async_copy(view, view, sem).wait()


def weight_call(place, kernel, pieces, inputs, in_specs, outs, out_specs, steps, by, name, flops, mb=40):
    chips, half, cols = pieces[0].shape
    groups = place.groups
    shape = (chips * 4 * half, groups * cols)
    slots = {"grp": groups, "chip": chips, "all": 1}[by]
    anywhere = pl.BlockSpec(memory_space=pl.ANY)

    def body(where, *refs):
        taken, refs = refs[: len(pieces)], refs[len(pieces) :]
        *refs, weight, sem = refs
        step = pl.program_id(0)

        @pl.when(step == 0)
        def _():
            fetch(where, taken, weight, sem, groups, by)

        def ready():
            if by == "all":

                @pl.when(step == 0)
                def _():
                    fetched(weight, sem.at[0])

            elif by == "grp":
                at = pl.multiple_of((where[2] ^ step) * cols, LANES)
                fetched(weight.at[:, pl.ds(at, cols)], sem.at[step])
            else:
                at = pl.multiple_of((where[1] ^ step) * 4 * half, 4 * half)
                fetched(weight.at[pl.ds(at, 4 * half), :], sem.at[step])

        kernel(where, ready, weight, *refs)

    total = sum(math.prod(x.shape) * x.dtype.itemsize for x in list(inputs) + list(outs))
    return pl.pallas_call(
        body,
        grid_spec=pltpu.PrefetchScalarGridSpec(
            num_scalar_prefetch=1,
            grid=(steps,),
            in_specs=[anywhere] * len(pieces) + in_specs,
            out_specs=out_specs,
            scratch_shapes=[pltpu.VMEM(shape, jnp.bfloat16), pltpu.SemaphoreType.DMA((slots,))],
        ),
        out_shape=outs,
        compiler_params=params(mb),
        cost_estimate=pl.CostEstimate(
            flops=flops, bytes_accessed=2 * shape[0] * shape[1] + total, transcendentals=0
        ),
        name=name,
    )(place.scalars, *pieces, *inputs)


TILE = 256


def row_tiles(width):
    return pl.BlockSpec((TILE, width), lambda i, s: (i, 0))


def fixed(*shape):
    return pl.BlockSpec(shape, lambda i, s: (0,) * len(shape))


def shaped(shape, dtype):
    return jax.ShapeDtypeStruct(shape, dtype)


def project_qkv(place, rows, pieces, bias, scale):
    length, width = rows.shape
    cols = pieces[0].shape[2]

    def kernel(where, ready, weight, x_ref, bias_ref, scale_ref, out_ref):
        ready()
        at = pl.ds(pl.multiple_of((where[2] ^ pl.program_id(0)) * cols, LANES), cols)
        for tile in range(length // TILE):
            here = pl.ds(tile * TILE, TILE)
            mixed = mxu(x_ref[here, :], weight[:, at], NN) + bias_ref[:, at]
            mixed = mixed.astype(jnp.bfloat16).astype(jnp.float32) * scale_ref[:, at]
            out_ref[here, :] = mixed.astype(jnp.bfloat16)

    total = cols * place.groups
    return weight_call(
        place,
        kernel,
        pieces,
        (rows, bias, scale),
        [fixed(length, width), fixed(1, total), fixed(1, total)],
        [shaped((length, total), jnp.bfloat16)],
        [pl.BlockSpec((length, cols), lambda i, s: (0, i ^ s[2]))],
        place.groups,
        "grp",
        "qkv",
        2 * length * width * total,
    )[0]


def norm_parts(rows):
    centered = rows - jnp.mean(rows, -1, keepdims=True)
    scale = lax.rsqrt(jnp.mean(centered * centered, -1, keepdims=True) + epsilon)
    return centered * scale, scale


def norm_back(grad, normed, scale):
    return scale * (
        grad
        - jnp.mean(grad, -1, keepdims=True)
        - normed * jnp.mean(grad * normed, -1, keepdims=True)
    )


def add_rows(sum_ref, *terms):
    @pl.when(pl.program_id(0) == 0)
    def _():
        sum_ref[...] = jnp.zeros_like(sum_ref)

    for n, term in enumerate(terms):
        sum_ref[n : n + 1, :] += jnp.sum(term, 0, keepdims=True)


def project_out(place, contexts, pieces, rows, bias, gain, shift):
    length, width = rows.shape

    def kernel(where, ready, weight, c_ref, x_ref, b_ref, g_ref, s_ref, n_ref, r_ref, low_ref):
        ready()
        first_sum = mxu(c_ref[...], weight[...], NN) + b_ref[...] + x_ref[...].astype(jnp.float32)
        normed, scale = norm_parts(first_sum)
        n_ref[...] = normed
        r_ref[...] = jnp.broadcast_to(scale, r_ref.shape)
        low_ref[...] = (normed * g_ref[...] + s_ref[...]).astype(jnp.bfloat16)

    return weight_call(
        place,
        kernel,
        pieces,
        (contexts, rows, bias, gain, shift),
        [row_tiles(width), row_tiles(width)] + [fixed(1, width)] * 3,
        [
            shaped((length, width), jnp.float32),
            shaped((length, LANES), jnp.float32),
            shaped((length, width), jnp.bfloat16),
        ],
        [row_tiles(width), row_tiles(LANES), row_tiles(width)],
        length // TILE,
        "all",
        "attn_out",
        2 * length * width * width,
    )


def feed_in(place, normed_low, pieces, bias):
    length, width = normed_low.shape
    cols = pieces[0].shape[2]

    def kernel(where, ready, weight, x_ref, bias_ref, hid_ref, slope_ref):
        ready()
        at = pl.ds(pl.multiple_of((where[2] ^ pl.program_id(0)) * cols, LANES), cols)
        for tile in range(length // TILE):
            here = pl.ds(tile * TILE, TILE)
            pre = mxu(x_ref[here, :], weight[:, at], NN) + bias_ref[:, at]
            share = 0.5 + 0.5 * lax.erf(pre * (1.0 / math.sqrt(2.0)))
            bell = jnp.exp(-0.5 * pre * pre) * (1.0 / math.sqrt(2.0 * math.pi))
            hid_ref[here, :] = (pre * share).astype(jnp.bfloat16)
            slope_ref[here, :] = (share + pre * bell).astype(jnp.bfloat16)

    total = cols * place.groups
    block = pl.BlockSpec((length, cols), lambda i, s: (0, i ^ s[2]))
    return weight_call(
        place,
        kernel,
        pieces,
        (normed_low, bias),
        [fixed(length, width), fixed(1, total)],
        [shaped((length, total), jnp.bfloat16)] * 2,
        [block, block],
        place.groups,
        "grp",
        "feed_in",
        2 * length * width * total,
    )


def feed_out(place, hidden, pieces, normed, cot, keep, vectors):
    length, inner = hidden.shape
    width = normed.shape[1]

    def kernel(where, ready, weight, h_ref, n_ref, cot_ref, keep_ref, g1, s1, b2, g2, s2, *outs):
        out_ref, grad_ref, low_ref, sum_ref = outs
        ready()
        fed = mxu(h_ref[...], weight[...], NN)
        second_sum = n_ref[...] * g1[...] + s1[...] + (fed + b2[...])
        second, scale = norm_parts(second_sum)
        out_ref[...] = (second * g2[...] + s2[...]).astype(jnp.bfloat16)
        masked = cot_ref[...].astype(jnp.float32) * keep_ref[...]
        grad = norm_back(masked * g2[...], second, scale)
        grad_ref[...] = grad
        low_ref[...] = grad.astype(jnp.bfloat16)
        add_rows(sum_ref, masked * second, masked, grad)

    return weight_call(
        place,
        kernel,
        pieces,
        (hidden, normed, cot, keep, *vectors),
        [row_tiles(inner), row_tiles(width), row_tiles(width), row_tiles(1)] + [fixed(1, width)] * 5,
        [
            shaped((length, width), jnp.bfloat16),
            shaped((length, width), jnp.float32),
            shaped((length, width), jnp.bfloat16),
            shaped((8, width), jnp.float32),
        ],
        [row_tiles(width), row_tiles(width), row_tiles(width), fixed(8, width)],
        length // TILE,
        "all",
        "feed_out",
        2 * length * width * inner,
    )


def feed_out_back(place, out_low, pieces, slope):
    length, width = out_low.shape
    inner = slope.shape[1]
    cols = inner // place.chips

    def kernel(where, ready, weight, g_ref, slope_ref, pre_ref, sum_ref):
        ready_rows = pl.ds(pl.multiple_of((where[1] ^ pl.program_id(0)) * cols, cols), cols)
        ready()
        total = jnp.zeros((1, cols), jnp.float32)
        for tile in range(length // TILE):
            here = pl.ds(tile * TILE, TILE)
            grad = mxu(g_ref[here, :], weight[ready_rows, :], NT) * slope_ref[here, :].astype(jnp.float32)
            pre_ref[here, :] = grad.astype(jnp.bfloat16)
            total = total + jnp.sum(grad, 0, keepdims=True)
        sum_ref[...] = total

    block = pl.BlockSpec((length, cols), lambda i, s: (0, i ^ s[1]))
    return weight_call(
        place,
        kernel,
        pieces,
        (out_low, slope),
        [fixed(length, width), block],
        [shaped((length, inner), jnp.bfloat16), shaped((1, inner), jnp.float32)],
        [block, pl.BlockSpec((1, cols), lambda i, s: (0, i ^ s[1]))],
        place.chips,
        "chip",
        "feed_out_back",
        2 * length * width * inner,
    )


def feed_in_back(place, pre_low, pieces, second_grad, normed, scale, gain):
    length, inner = pre_low.shape
    width = normed.shape[1]

    def kernel(where, ready, weight, p_ref, g_ref, n_ref, r_ref, gain_ref, first_ref, low_ref, sum_ref):
        ready()
        grad = g_ref[...] + mxu(p_ref[...], weight[...], NT)
        first = norm_back(grad * gain_ref[...], n_ref[...], r_ref[:, :1])
        first_ref[...] = first
        low_ref[...] = first.astype(jnp.bfloat16)
        add_rows(sum_ref, grad * n_ref[...], grad, first)

    return weight_call(
        place,
        kernel,
        pieces,
        (pre_low, second_grad, normed, scale, gain),
        [row_tiles(inner), row_tiles(width), row_tiles(width), row_tiles(LANES), fixed(1, width)],
        [
            shaped((length, width), jnp.float32),
            shaped((length, width), jnp.bfloat16),
            shaped((8, width), jnp.float32),
        ],
        [row_tiles(width), row_tiles(width), fixed(8, width)],
        length // TILE,
        "all",
        "feed_in_back",
        2 * length * width * inner,
    )


def project_out_back(place, attn_low, pieces):
    length, width = attn_low.shape

    def kernel(where, ready, weight, g_ref, out_ref):
        ready()
        out_ref[...] = mxu(g_ref[...], weight[...], NT).astype(jnp.bfloat16)

    return weight_call(
        place,
        kernel,
        pieces,
        (attn_low,),
        [row_tiles(width)],
        [shaped((length, width), jnp.bfloat16)],
        [row_tiles(width)],
        length // TILE,
        "all",
        "attn_out_back",
        2 * length * width * width,
    )[0]


def project_qkv_back(place, grads, pieces, first_grad):
    length, width = first_grad.shape
    part = width // len(grads)

    def kernel(where, ready, weight, *refs):
        *grad_refs, first_ref, out_ref = refs
        ready()
        total = first_ref[...]
        for n in range(3):
            for m, grad_ref in enumerate(grad_refs):
                at = n * width + m * part
                total = total + mxu(grad_ref[n], weight[:, at : at + part], NT)
        out_ref[...] = total

    return weight_call(
        place,
        kernel,
        pieces,
        (*grads, first_grad),
        [pl.BlockSpec((3, TILE, part), lambda i, s: (0, i, 0))] * len(grads) + [row_tiles(width)],
        [shaped((length, width), jnp.float32)],
        [row_tiles(width)],
        length // TILE,
        "all",
        "qkv_back",
        6 * length * width * width,
    )[0]


def weight_grad_kernel(where, left_ref, right_ref, *refs, own, rows, groups, split):
    *refs, kept = refs
    received = None
    if own:
        received, *outs = refs
    else:
        outs = refs
    core, grp = where[0], where[2]
    keep = core if own else 1 - core
    chips = left_ref.shape[1] // (2 * rows)
    half = rows // 2

    @pl.when(pl.program_id(1) == 0)
    def _():
        lefts = []
        for k in range(chips):
            even = left_ref[:, 2 * k * rows : (2 * k + 1) * rows]
            odd = left_ref[:, (2 * k + 1) * rows : (2 * k + 2) * rows]
            lefts.append(jnp.where(keep == 0, even, odd))
        left = lefts[0] if chips == 1 else jnp.concatenate(lefts, 1)
        kept[...] = left.T

    def emit(slot, part, at):
        part = part.reshape(chips, 2, half, part.shape[-1])
        pos = 0 if split else slot
        if own:
            part = part + received[pos, :, :, :, at].astype(jnp.float32)
            part = part.astype(jnp.bfloat16)

            def store(slot):
                for lower in range(2):
                    outs[slot + lower * groups][:, :, at] = part[:, lower]

            if split:
                for n in range(groups):
                    pl.when(pl.program_id(1) == n)(functools.partial(store, n))
            else:
                store(slot)
        else:
            outs[0][pos, :, :, :, at] = part.astype(jnp.bfloat16)

    if split and len(right_ref.shape) == 3:
        size = right_ref.shape[2]
        for n in range(right_ref.shape[0]):
            emit(0, mxu(kept[...], right_ref[n], NN), slice(n * size, (n + 1) * size))
    elif split:
        size = min(512, right_ref.shape[1])
        for n in range(right_ref.shape[1] // size):
            at = slice(n * size, (n + 1) * size)
            emit(0, mxu(kept[...], right_ref[:, at], NN), at)
    else:
        cols = right_ref.shape[1] // groups
        for slot in range(groups):
            at = pl.multiple_of((grp ^ slot) * cols, LANES)
            emit(slot, mxu(kept[...], right_ref[:, pl.ds(at, cols)], NN), slice(0, cols))


def weight_grad(place, left, right, received, split, name):
    tokens, height = left.shape
    groups, chips = place.groups, place.chips
    rows = height // place.shards
    half = rows // 2
    parts = right.shape[0] if right.ndim == 3 else 1
    width = right.shape[-1] * parts
    cols = width // groups
    own = received is not None
    step_chips = chips if split else max(1, 1024 // (2 * rows))
    steps = chips // step_chips
    if split:
        grid = (steps, groups)
        if parts > 1:
            right_spec = pl.BlockSpec(
                (parts, tokens, cols // parts), lambda i, j, s: (0, 0, j ^ s[2])
            )
        else:
            right_spec = pl.BlockSpec((tokens, cols), lambda i, j, s: (0, j ^ s[2]))
        passed = pl.BlockSpec((1, step_chips, 2, half, cols), lambda i, j, s: (j, i, 0, 0, 0))
    else:
        grid = (steps, 1)
        right_spec = pl.BlockSpec((tokens, width), lambda i, j, s: (0, 0))
        passed = pl.BlockSpec((groups, step_chips, 2, half, cols), lambda i, j, s: (0, i, 0, 0, 0))
    in_specs = [pl.BlockSpec((tokens, step_chips * 2 * rows), lambda i, j, s: (0, i)), right_spec]
    inputs = [left, right]
    if own:
        in_specs.append(passed)
        inputs.append(received)
        out_specs = [pl.BlockSpec((step_chips, half, cols), lambda i, j, s: (i, 0, 0))] * (2 * groups)
        out_shape = [shaped((chips, half, cols), jnp.bfloat16)] * (2 * groups)
    else:
        out_specs = passed
        out_shape = shaped((groups, chips, 2, half, cols), jnp.bfloat16)
    return pl.pallas_call(
        functools.partial(weight_grad_kernel, own=own, rows=rows, groups=groups, split=split),
        grid_spec=pltpu.PrefetchScalarGridSpec(
            num_scalar_prefetch=1,
            grid=grid,
            in_specs=in_specs,
            out_specs=out_specs,
            scratch_shapes=[pltpu.VMEM((step_chips * rows, tokens), jnp.bfloat16)],
        ),
        out_shape=out_shape,
        compiler_params=params(40),
        cost_estimate=pl.CostEstimate(
            flops=tokens * height * width,
            bytes_accessed=2 * (tokens * (height + width) + height * width),
            transcendentals=0,
        ),
        name="wgrad_" + name + ("_own" if own else "_sent"),
    )(place.scalars, *inputs)


def add(*terms):
    total = terms[0].astype(jnp.float32)
    for term in terms[1:]:
        total = total + term.astype(jnp.float32)
    return total.astype(jnp.bfloat16)


class Reduction:
    def __init__(self, place, left, right, split, name, *wait):
        self.place = place
        left = after(left, *wait) if wait else left
        self.call = (left, right, split, name)
        self.sent = weight_grad(place, left, right, None, split, name)
        self.received = place.swap(self.sent, core=1)

    def own(self, *wait):
        left, right, split, name = self.call
        received = after(self.received, *wait) if wait else self.received
        out = weight_grad(self.place, left, right, received, split, name)
        swap, groups = self.place.swap, self.place.groups
        self.upper, self.lower = out[:groups], out[groups:]
        self.near = [
            swap(self.upper[3], grp=1),
            swap(self.lower[3], grp=2),
            swap(self.upper[1], grp=1),
            swap(self.lower[2], grp=2),
        ]
        return out[0]

    def middle(self, *wait):
        near = after(self.near[0], *wait) if wait else self.near[0]
        upper = add(self.upper[2], near)
        lower = add(self.lower[1], self.near[1])
        self.far = [self.place.swap(upper, grp=2), self.place.swap(lower, grp=1)]
        return upper

    def along(self, *wait):
        place = self.place
        far = after(self.far[0], *wait) if wait else self.far[0]
        mine = jnp.concatenate(
            [add(self.upper[0], self.near[2], far), add(self.lower[0], self.near[3], self.far[1])], 1
        )
        self.terms = [lax.dynamic_index_in_dim(mine, place.chip, 0, False)]
        for k in range(1, place.chips):
            outgoing = lax.dynamic_index_in_dim(mine, place.chip ^ k, 0, False)
            self.terms.append(place.swap(outgoing, chip=k))
        return self.terms[0]

    def share(self, *wait):
        last = after(self.terms[-1], *wait) if wait else self.terms[-1]
        share = add(*self.terms[:-1], last)
        self.blocks = [share] + [self.place.swap(share, grp=k) for k in range(1, self.place.groups)]
        return share

    def result(self):
        return in_order(self.place, self.blocks)


def in_order(place, blocks):
    blocks = [b.astype(jnp.float32) for b in blocks]
    ordered = []
    for g in range(place.groups):
        block = blocks[0]
        for k in range(1, place.groups):
            block = jnp.where((place.grp ^ k) == g, blocks[k], block)
        ordered.append(block)
    return ordered


def sum_everywhere(place, vector):
    for how in ({"core": 1}, {"grp": 1}, {"grp": 2}):
        vector = vector + place.swap(vector, **how)
    step = 1
    while step < place.chips:
        vector = vector + place.swap(vector, chip=step)
        step *= 2
    return vector


def own_part(place, vector):
    size = vector.shape[0] // place.shards
    return lax.dynamic_slice_in_dim(vector, place.shard * size, size)


def on_device_permutes(
    tokens,
    segment_ids,
    keep_flag,
    cotangent,
    w_qkv,
    b_query,
    b_value,
    w_attn_out,
    b_attn_out,
    norm1_gain,
    norm1_bias,
    w_in,
    b_in,
    w_out,
    b_out,
    norm2_gain,
    norm2_bias,
    *,
    groups,
    shards,
):
    place = Place(groups, shards)
    _, length, width = tokens.shape
    vectors = (
        b_query,
        b_value,
        b_attn_out,
        norm1_gain,
        norm1_bias,
        b_in,
        b_out,
        norm2_gain,
        norm2_bias,
    )
    packed = lax.all_gather(jnp.concatenate(vectors), "shard", axis=0)
    unpacked = []
    at = 0
    for vector in vectors:
        size = vector.shape[0]
        unpacked.append(packed[:, at : at + size].reshape(1, -1).astype(jnp.float32))
        at += size
    (
        bias_query,
        bias_value,
        bias_attn,
        gain_one,
        shift_one,
        bias_in,
        bias_out,
        gain_two,
        shift_two,
    ) = unpacked
    rows = tokens[0]
    seg_row = segment_ids.reshape(1, length)
    seg_col = segment_ids.reshape(length, 1)
    keep = keep_flag.reshape(length, 1).astype(jnp.float32)
    pairs = width // LANES
    blank = jnp.zeros_like(bias_query)
    qkv_bias = jnp.concatenate([bias_query, blank, bias_value], 1)
    qkv_scale = jnp.concatenate([blank + 1.0 / math.sqrt(HD), blank + 1.0, blank + 1.0], 1)

    qkv, attn = Gather(place, w_qkv), Gather(place, w_attn_out)
    fin, fout = Gather(place, w_in), Gather(place, w_out)
    t0 = qkv.chips(0)
    t1 = qkv.chips(1, t0)
    qkv.near(0)
    qkv.near(1, qkv.mine[0][1], qkv.mine[0][2])
    qkv.far(0)
    qkv.far(1)
    tz = [g.chips(half, t1) for g in (attn, fin) for half in range(2)]
    for half, slot in ((0, 0), (0, 1), (0, 2), (1, 0), (1, 1), (1, 2), (0, 3), (1, 3)):
        qkv.cross(half, slot)
    last = (qkv.mine[0][1], qkv.mine[1][2], qkv.mine[1][1])
    for g in (attn, fin):
        for half in range(2):
            g.near(half, *last)
    for half in range(2):
        fout.chips(half, *tz)
    mixed = project_qkv(place, rows, qkv.pieces(), qkv_bias, qkv_scale)

    forward = attention_forward(mixed, seg_col, seg_row, 0, pairs // 2)
    forward_gate = forward[1]
    for g in (attn, fin):
        for half in range(2):
            g.far(half, mixed)
    for half in range(2):
        fout.near(half, attn.mine[0][2], attn.mine[1][1], fin.mine[0][2], fin.mine[1][1])
    for g in (attn, fin):
        for half in range(2):
            for slot in range(3):
                g.cross(half, slot)
    contexts, lse = attention_forward(
        after(mixed, fin.mine[0][1], fin.mine[1][2]), seg_col, seg_row, pairs // 2, pairs // 2, forward
    )
    for g in (attn, fin):
        for half in range(2):
            g.cross(half, 3)
    for half in range(2):
        fout.far(half, forward_gate)
    normed, scale_one, normed_low = project_out(
        place, contexts, attn.pieces(), rows, bias_attn, gain_one, shift_one
    )
    for half in range(2):
        for slot in range(4):
            fout.cross(half, slot)
    hidden, slope = feed_in(place, normed_low, fin.pieces(), bias_in)
    layer_out, second_grad, out_low, second_sums = feed_out(
        place,
        hidden,
        fout.pieces(),
        normed,
        cotangent[0],
        keep,
        (gain_one, shift_one, bias_out, gain_two, shift_two),
    )

    r_out = Reduction(place, hidden, out_low, False, "out")
    pre_low, bias_in_grad = feed_out_back(place, after(out_low, r_out.sent), fout.pieces(), slope)
    own_out = r_out.own(pre_low)
    r_in = Reduction(place, normed_low, pre_low, True, "in", own_out)
    first_grad, attn_low, first_sums = feed_in_back(
        place, after(pre_low, r_in.sent), fin.pieces(), second_grad, normed, scale_one, gain_one
    )
    own_in = r_in.own(first_grad)
    r_attn = Reduction(place, contexts, attn_low, False, "attn", own_in)
    context_grad = project_out_back(place, after(attn_low, r_attn.sent), attn.pieces())
    own_attn = r_attn.own(context_grad)
    quarter = pairs // 4

    def back(start, at, before=None, *wait):
        return attention_backward(
            mixed,
            contexts,
            after(context_grad, *wait),
            seg_col,
            seg_row,
            lse,
            start,
            quarter,
            at,
            2 * quarter,
            before,
        )

    mid_out = r_out.middle(own_attn)
    part = back(0, 0, None, mid_out)
    mid_in = r_in.middle(part[1])
    low_a, late_a = back(quarter, quarter, part, mid_in)
    along_out = r_out.along(late_a)
    mid_attn = r_attn.middle(late_a)
    r_qkv_a = Reduction(place, rows, low_a, True, "qkv_a", along_out, mid_attn)
    part = back(2 * quarter, 0, None, r_qkv_a.sent)
    along_in = r_in.along(part[1])
    along_attn = r_attn.along(part[1])
    share_out = r_out.share(part[1])
    own_a = r_qkv_a.own(part[1], along_in, along_attn, share_out)
    low_b, late_b = back(3 * quarter, quarter, part, own_a)
    mid_a = r_qkv_a.middle(late_b)
    share_in = r_in.share(late_b)
    share_attn = r_attn.share(late_b)
    r_qkv_b = Reduction(place, rows, low_b, True, "qkv_b", mid_a, share_in, share_attn)
    input_grad = project_qkv_back(place, (low_a, after(low_b, r_qkv_b.sent)), qkv.pieces(), first_grad)
    own_b = r_qkv_b.own(input_grad)
    r_qkv_a.along(own_b)
    r_qkv_b.middle()
    r_qkv_a.share()
    r_qkv_b.along()
    r_qkv_b.share()

    sums = (
        jnp.concatenate([late_a[0], late_b[0]]),
        jnp.concatenate([late_a[1], late_b[1]]),
        first_sums[2],
        first_sums[0],
        first_sums[1],
        bias_in_grad[0],
        second_sums[2],
        second_sums[0],
        second_sums[1],
    )
    summed = sum_everywhere(place, jnp.concatenate(sums).reshape(-1, LANES)).reshape(-1)
    vectors = []
    at = 0
    for vector in sums:
        vectors.append(own_part(place, summed[at : at + vector.shape[0]]))
        at += vector.shape[0]

    parts_a, parts_b = r_qkv_a.result(), r_qkv_b.result()
    heads = parts_a[0].shape[1] // 3
    w_qkv_grad = jnp.concatenate(
        [
            block[:, n * heads : (n + 1) * heads]
            for n in range(3)
            for half in (parts_a, parts_b)
            for block in half
        ],
        1,
    )
    return (
        layer_out[None],
        input_grad[None],
        w_qkv_grad,
        vectors[0],
        vectors[1],
        jnp.concatenate(r_attn.result(), 1),
        vectors[2],
        vectors[3],
        vectors[4],
        jnp.concatenate(r_in.result(), 1),
        vectors[5],
        jnp.concatenate(r_out.result(), 1),
        vectors[6],
        vectors[7],
        vectors[8],
    )


def solution(mesh):
    groups, shards = mesh.shape["grp"], mesh.shape["shard"]
    if groups == 4 and shards == 8:
        body = functools.partial(on_device_permutes, groups=groups, shards=shards)
    else:
        body = on_device
    return jax.shard_map(
        body,
        mesh=mesh,
        in_specs=(
            P(("grp", "shard"), None, None),
            P(("grp", "shard"), None),
            P(("grp", "shard"), None),
            P(("grp", "shard"), None, None),
            P("shard", "grp"),
            P("shard"),
            P("shard"),
            P("shard", "grp"),
            P("shard"),
            P("shard"),
            P("shard"),
            P("shard", "grp"),
            P("shard"),
            P("shard", "grp"),
            P("shard"),
            P("shard"),
            P("shard"),
        ),
        out_specs=(
            P(("grp", "shard"), None, None),
            P(("grp", "shard"), None, None),
            P("shard", None),
            P("shard"),
            P("shard"),
            P("shard", None),
            P("shard"),
            P("shard"),
            P("shard"),
            P("shard", None),
            P("shard"),
            P("shard", None),
            P("shard"),
            P("shard"),
            P("shard"),
        ),
        check_vma=False,
    )
```

```python
import functools
import math

import jax
import jax.numpy as jnp
from jax import lax
from jax.experimental import pallas as pl
from jax.experimental.pallas import tpu as pltpu
from jax.sharding import PartitionSpec as P

H = 16
HD = 64


masked_score = -1e30
epsilon = 1e-05


def norm_layer(rows, gain_row, shift_row):
    row_mean = jnp.mean(rows, -1, keepdims=True)
    centered = rows - row_mean
    row_var = jnp.mean(centered * centered, -1, keepdims=True)
    return centered * lax.rsqrt(row_var + epsilon) * gain_row + shift_row


def gelu_exact(values):
    return 0.5 * values * (1.0 + lax.erf(values * (1.0 / math.sqrt(2.0))))


def contract_rows(left, right):
    return lax.dot_general(
        left, right, (((0,), (0,)), ((), ())), preferred_element_type=jnp.float32
    )


def contract_cols(left, right):
    return lax.dot_general(
        left, right, (((1,), (1,)), ((), ())), preferred_element_type=jnp.float32
    )


def attend_forward(queries, key_rows, value_rows, segment_row, block_rows):
    length, model_width = queries.shape
    scaling = 1.0 / math.sqrt(HD)
    key_heads = key_rows.reshape(length, H, HD)
    value_heads = value_rows.reshape(length, H, HD)
    query_blocks = queries.reshape(length // block_rows, block_rows, H, HD)
    segment_blocks = segment_row.reshape(length // block_rows, block_rows)

    def one_block(pieces):
        query_part, segment_part = pieces
        scores = (
            jnp.einsum("qhd,khd->hqk", query_part, key_heads, preferred_element_type=jnp.float32)
            * scaling
        )
        allowed = segment_part[:, None] == segment_row[None, :]
        scores = jnp.where(allowed[None], scores, masked_score)
        row_max = jnp.max(scores, -1, keepdims=True)
        powers = jnp.exp(scores - row_max)
        totals = jnp.sum(powers, -1, keepdims=True)
        attn_probs = (powers / totals).astype(jnp.bfloat16)
        context = jnp.einsum(
            "hqk,khd->qhd", attn_probs, value_heads, preferred_element_type=jnp.float32
        )
        return (
            context.reshape(block_rows, model_width).astype(jnp.bfloat16),
            (row_max + jnp.log(totals))[:, :, 0],
        )

    contexts, log_sums = lax.map(one_block, (query_blocks, segment_blocks))
    return (contexts.reshape(length, model_width), log_sums)


def attend_backward(queries, key_rows, value_rows, segment_row, log_sums, context_grad, block_rows):
    length, model_width = queries.shape
    scaling = 1.0 / math.sqrt(HD)
    key_heads = key_rows.reshape(length, H, HD)
    value_heads = value_rows.reshape(length, H, HD)
    query_blocks = queries.reshape(length // block_rows, block_rows, H, HD)
    segment_blocks = segment_row.reshape(length // block_rows, block_rows)
    grad_blocks = context_grad.reshape(length // block_rows, block_rows, H, HD)

    def one_block(running, pieces):
        key_acc, value_acc = running
        query_part, segment_part, lse_part, grad_part = pieces
        scores = (
            jnp.einsum("qhd,khd->hqk", query_part, key_heads, preferred_element_type=jnp.float32)
            * scaling
        )
        allowed = segment_part[:, None] == segment_row[None, :]
        scores = jnp.where(allowed[None], scores, masked_score)
        probs = jnp.exp(scores - lse_part[:, :, None])
        prob_low = probs.astype(jnp.bfloat16)
        prob_grad = jnp.einsum(
            "qhd,khd->hqk", grad_part, value_heads, preferred_element_type=jnp.float32
        )
        row_dot = jnp.sum(prob_grad * probs, -1, keepdims=True)
        score_grad = (probs * (prob_grad - row_dot)).astype(jnp.bfloat16)
        query_grad = (
            jnp.einsum("hqk,khd->qhd", score_grad, key_heads, preferred_element_type=jnp.float32)
            * scaling
        )
        key_acc = (
            key_acc
            + jnp.einsum("hqk,qhd->khd", score_grad, query_part, preferred_element_type=jnp.float32)
            * scaling
        )
        value_acc = value_acc + jnp.einsum(
            "hqk,qhd->khd", prob_low, grad_part, preferred_element_type=jnp.float32
        )
        return ((key_acc, value_acc), query_grad.reshape(block_rows, model_width))

    empty_acc = jnp.zeros((length, H, HD), jnp.float32)
    (key_grad, value_grad), query_grads = lax.scan(
        one_block, (empty_acc, empty_acc), (query_blocks, segment_blocks, log_sums, grad_blocks)
    )
    return (
        query_grads.reshape(length, model_width),
        key_grad.reshape(length, model_width),
        value_grad.reshape(length, model_width),
    )


def on_device(
    tokens,
    segment_ids,
    keep_flag,
    cotangent,
    w_qkv,
    b_query,
    b_value,
    w_attn_out,
    b_attn_out,
    norm1_gain,
    norm1_bias,
    w_in,
    b_in,
    w_out,
    b_out,
    norm2_gain,
    norm2_bias,
):
    seq_count, length, model_width = tokens.shape
    block_rows = min(512, length)
    within = (
        lax.all_gather(w_qkv, "shard", axis=0, tiled=True),
        lax.all_gather(w_attn_out, "shard", axis=0, tiled=True),
        lax.all_gather(w_in, "shard", axis=0, tiled=True),
        lax.all_gather(w_out, "shard", axis=0, tiled=True),
        lax.all_gather(b_query, "shard", axis=0, tiled=True),
        lax.all_gather(b_value, "shard", axis=0, tiled=True),
        lax.all_gather(b_attn_out, "shard", axis=0, tiled=True),
        lax.all_gather(norm1_gain, "shard", axis=0, tiled=True),
        lax.all_gather(norm1_bias, "shard", axis=0, tiled=True),
        lax.all_gather(b_in, "shard", axis=0, tiled=True),
        lax.all_gather(b_out, "shard", axis=0, tiled=True),
        lax.all_gather(norm2_gain, "shard", axis=0, tiled=True),
        lax.all_gather(norm2_bias, "shard", axis=0, tiled=True),
    )
    full_qkv, full_attn, full_in, full_out = (
        lax.all_gather(within[0], "grp", axis=1, tiled=True),
        lax.all_gather(within[1], "grp", axis=1, tiled=True),
        lax.all_gather(within[2], "grp", axis=1, tiled=True),
        lax.all_gather(within[3], "grp", axis=1, tiled=True),
    )
    (
        bias_query,
        bias_value,
        bias_attn,
        gain_one,
        shift_one,
        bias_in,
        bias_out,
        gain_two,
        shift_two,
    ) = [piece.astype(jnp.float32) for piece in within[4:]]
    flat_rows = tokens.reshape(seq_count * length, model_width)
    mixed_qkv = jnp.dot(flat_rows, full_qkv, preferred_element_type=jnp.float32)
    queries = (mixed_qkv[:, :model_width] + bias_query).astype(jnp.bfloat16)
    key_rows = mixed_qkv[:, model_width : 2 * model_width].astype(jnp.bfloat16)
    value_rows = (mixed_qkv[:, 2 * model_width :] + bias_value).astype(jnp.bfloat16)
    query_seqs = queries.reshape(seq_count, length, model_width)
    key_seqs = key_rows.reshape(seq_count, length, model_width)
    value_seqs = value_rows.reshape(seq_count, length, model_width)

    def forward_sequence(pieces):
        return attend_forward(pieces[0], pieces[1], pieces[2], pieces[3], block_rows)

    contexts, log_sums = lax.map(forward_sequence, (query_seqs, key_seqs, value_seqs, segment_ids))
    contexts = contexts.reshape(seq_count * length, model_width)
    attended = jnp.dot(contexts, full_attn, preferred_element_type=jnp.float32) + bias_attn
    first_sum = flat_rows.astype(jnp.float32) + attended
    normed_one, norm_one_back = jax.vjp(norm_layer, first_sum, gain_one, shift_one)
    normed_low = normed_one.astype(jnp.bfloat16)
    hidden_pre = jnp.dot(normed_low, full_in, preferred_element_type=jnp.float32) + bias_in
    hidden, gelu_back = jax.vjp(gelu_exact, hidden_pre)
    hidden_low = hidden.astype(jnp.bfloat16)
    second_sum = normed_one + (
        jnp.dot(hidden_low, full_out, preferred_element_type=jnp.float32) + bias_out
    )
    result, norm_two_back = jax.vjp(norm_layer, second_sum, gain_two, shift_two)
    layer_out = result.astype(jnp.bfloat16).reshape(seq_count, length, model_width)
    again = (
        lax.all_gather(w_qkv, "shard", axis=0, tiled=True),
        lax.all_gather(w_attn_out, "shard", axis=0, tiled=True),
        lax.all_gather(w_in, "shard", axis=0, tiled=True),
        lax.all_gather(w_out, "shard", axis=0, tiled=True),
    )
    back_qkv, back_attn, back_in, back_out = (
        lax.all_gather(again[0], "grp", axis=1, tiled=True),
        lax.all_gather(again[1], "grp", axis=1, tiled=True),
        lax.all_gather(again[2], "grp", axis=1, tiled=True),
        lax.all_gather(again[3], "grp", axis=1, tiled=True),
    )
    masked_cot = cotangent.astype(jnp.float32).reshape(
        seq_count * length, model_width
    ) * keep_flag.reshape(seq_count * length, 1).astype(jnp.float32)
    second_grad, gain_two_grad, shift_two_grad = norm_two_back(masked_cot)
    bias_out_grad = jnp.sum(second_grad, 0)
    out_low = second_grad.astype(jnp.bfloat16)
    w_out_grad = contract_rows(hidden_low, out_low)
    hidden_grad = contract_cols(out_low, back_out)
    (pre_grad,) = gelu_back(hidden_grad)
    bias_in_grad = jnp.sum(pre_grad, 0)
    pre_low = pre_grad.astype(jnp.bfloat16)
    w_in_grad = contract_rows(normed_low, pre_low)
    normed_grad = second_grad + contract_cols(pre_low, back_in)
    first_grad, gain_one_grad, shift_one_grad = norm_one_back(normed_grad)
    bias_attn_grad = jnp.sum(first_grad, 0)
    attn_low = first_grad.astype(jnp.bfloat16)
    w_attn_grad = contract_rows(contexts, attn_low)
    context_grad = contract_cols(attn_low, back_attn).astype(jnp.bfloat16)

    def backward_sequence(pieces):
        return attend_backward(
            pieces[0], pieces[1], pieces[2], pieces[3], pieces[4], pieces[5], block_rows
        )

    query_grad, key_grad, value_grad = lax.map(
        backward_sequence,
        (
            query_seqs,
            key_seqs,
            value_seqs,
            segment_ids,
            log_sums,
            context_grad.reshape(seq_count, length, model_width),
        ),
    )
    query_grad = query_grad.reshape(seq_count * length, model_width)
    key_grad = key_grad.reshape(seq_count * length, model_width)
    value_grad = value_grad.reshape(seq_count * length, model_width)
    bias_query_grad = jnp.sum(query_grad, 0)
    bias_value_grad = jnp.sum(value_grad, 0)
    qkv_low = jnp.concatenate([query_grad, key_grad, value_grad], 1).astype(jnp.bfloat16)
    w_qkv_grad = contract_rows(flat_rows, qkv_low)
    input_grad = first_grad + contract_cols(qkv_low, back_qkv)
    reduced = (
        lax.psum_scatter(
            w_qkv_grad.astype(jnp.bfloat16), "shard", scatter_dimension=0, tiled=True
        ).astype(jnp.float32),
        lax.psum_scatter(
            bias_query_grad.astype(jnp.bfloat16), "shard", scatter_dimension=0, tiled=True
        ).astype(jnp.float32),
        lax.psum_scatter(
            bias_value_grad.astype(jnp.bfloat16), "shard", scatter_dimension=0, tiled=True
        ).astype(jnp.float32),
        lax.psum_scatter(
            w_attn_grad.astype(jnp.bfloat16), "shard", scatter_dimension=0, tiled=True
        ).astype(jnp.float32),
        lax.psum_scatter(
            bias_attn_grad.astype(jnp.bfloat16), "shard", scatter_dimension=0, tiled=True
        ).astype(jnp.float32),
        lax.psum_scatter(
            gain_one_grad.astype(jnp.bfloat16), "shard", scatter_dimension=0, tiled=True
        ).astype(jnp.float32),
        lax.psum_scatter(
            shift_one_grad.astype(jnp.bfloat16), "shard", scatter_dimension=0, tiled=True
        ).astype(jnp.float32),
        lax.psum_scatter(
            w_in_grad.astype(jnp.bfloat16), "shard", scatter_dimension=0, tiled=True
        ).astype(jnp.float32),
        lax.psum_scatter(
            bias_in_grad.astype(jnp.bfloat16), "shard", scatter_dimension=0, tiled=True
        ).astype(jnp.float32),
        lax.psum_scatter(
            w_out_grad.astype(jnp.bfloat16), "shard", scatter_dimension=0, tiled=True
        ).astype(jnp.float32),
        lax.psum_scatter(
            bias_out_grad.astype(jnp.bfloat16), "shard", scatter_dimension=0, tiled=True
        ).astype(jnp.float32),
        lax.psum_scatter(
            gain_two_grad.astype(jnp.bfloat16), "shard", scatter_dimension=0, tiled=True
        ).astype(jnp.float32),
        lax.psum_scatter(
            shift_two_grad.astype(jnp.bfloat16), "shard", scatter_dimension=0, tiled=True
        ).astype(jnp.float32),
    )
    summed = (
        lax.psum(reduced[0].astype(jnp.bfloat16), "grp").astype(jnp.float32),
        lax.psum(reduced[1].astype(jnp.bfloat16), "grp").astype(jnp.float32),
        lax.psum(reduced[2].astype(jnp.bfloat16), "grp").astype(jnp.float32),
        lax.psum(reduced[3].astype(jnp.bfloat16), "grp").astype(jnp.float32),
        lax.psum(reduced[4].astype(jnp.bfloat16), "grp").astype(jnp.float32),
        lax.psum(reduced[5].astype(jnp.bfloat16), "grp").astype(jnp.float32),
        lax.psum(reduced[6].astype(jnp.bfloat16), "grp").astype(jnp.float32),
        lax.psum(reduced[7].astype(jnp.bfloat16), "grp").astype(jnp.float32),
        lax.psum(reduced[8].astype(jnp.bfloat16), "grp").astype(jnp.float32),
        lax.psum(reduced[9].astype(jnp.bfloat16), "grp").astype(jnp.float32),
        lax.psum(reduced[10].astype(jnp.bfloat16), "grp").astype(jnp.float32),
        lax.psum(reduced[11].astype(jnp.bfloat16), "grp").astype(jnp.float32),
        lax.psum(reduced[12].astype(jnp.bfloat16), "grp").astype(jnp.float32),
    )
    return (
        layer_out,
        input_grad.reshape(seq_count, length, model_width),
        summed[0],
        summed[1],
        summed[2],
        summed[3],
        summed[4],
        summed[5],
        summed[6],
        summed[7],
        summed[8],
        summed[9],
        summed[10],
        summed[11],
        summed[12],
    )


NT = (((1,), (1,)), ((), ()))
NN = (((1,), (0,)), ((), ()))
TN = (((0,), (0,)), ((), ()))
LANES = 128
AXES = ("grp", "shard")


def mxu(left, right, dims):
    return lax.dot_general(left, right, dims, preferred_element_type=jnp.float32)


def params(megabytes=60):
    return pltpu.CompilerParams(vmem_limit_bytes=megabytes << 20)


def attention_forward_kernel(q_ref, k_ref, v_ref, seg_col, seg_row, out_ref, lse_ref, *, rows):
    length = q_ref.shape[0]
    first = lax.broadcasted_iota(jnp.int32, (1, LANES), 1) < HD
    keys = k_ref[...]
    values = v_ref[...]
    zero = jnp.zeros_like(keys)
    head_keys = (jnp.where(first, keys, zero), jnp.where(first, zero, keys))
    key_segments = seg_col[...]
    for block in range(length // rows):
        here = pl.ds(block * rows, rows)
        q = q_ref[here, :]
        allowed = key_segments == seg_row[:, here]
        outs = []
        for head in range(2):
            scores = mxu(head_keys[head], q, NT)
            scores = jnp.where(allowed, scores, masked_score)
            top = jnp.max(scores, 0, keepdims=True)
            powers = jnp.exp(scores - top)
            total = jnp.sum(powers, 0, keepdims=True)
            part = mxu(powers.astype(jnp.bfloat16), values, TN)
            outs.append(part * jnp.transpose(jnp.broadcast_to(1.0 / total, (LANES, rows))))
            lse_ref[0, head : head + 1, here] = top + jnp.log(total)
        out_ref[here, :] = jnp.where(first, outs[0], outs[1]).astype(jnp.bfloat16)


def attention_forward(qkv, seg_col, seg_row, start, pairs, before=None):
    length, width = qkv.shape[0], qkv.shape[1] // 3
    total = width // LANES
    rows = min(512, length)
    anywhere = pl.BlockSpec(memory_space=pl.ANY)

    def pair(part):
        return pl.BlockSpec((length, LANES), lambda j: (0, part * total + start + j))

    def body(q_ref, k_ref, v_ref, seg_c, seg_r, *refs):
        attention_forward_kernel(q_ref, k_ref, v_ref, seg_c, seg_r, *refs[-2:], rows=rows)

    return pl.pallas_call(
        body,
        grid=(pairs,),
        in_specs=[
            pair(0),
            pair(1),
            pair(2),
            pl.BlockSpec((length, 1), lambda j: (0, 0)),
            pl.BlockSpec((1, length), lambda j: (0, 0)),
        ]
        + [anywhere] * (0 if before is None else 2),
        out_specs=[
            pl.BlockSpec((length, LANES), lambda j: (0, start + j)),
            pl.BlockSpec((1, 2, length), lambda j: (start + j, 0, 0)),
        ],
        out_shape=[
            jax.ShapeDtypeStruct((length, width), jnp.bfloat16),
            jax.ShapeDtypeStruct((total, 2, length), jnp.float32),
        ],
        input_output_aliases={} if before is None else {5: 0, 6: 1},
        compiler_params=params(40),
        cost_estimate=pl.CostEstimate(
            flops=16 * length * length * pairs * LANES,
            bytes_accessed=8 * length * pairs * LANES,
            transcendentals=0,
        ),
        name="attn_fwd",
    )(qkv, qkv, qkv, seg_col, seg_row, *(() if before is None else before))


def attention_backward_kernel(
    q_ref, k_ref, v_ref, o_ref, do_ref, seg_col, seg_row, lse_ref, grad_ref, sum_ref, *, rows
):
    length = q_ref.shape[0]
    lane = lax.broadcasted_iota(jnp.int32, (1, LANES), 1)
    first = lane < HD
    pick = (
        lax.broadcasted_iota(jnp.int32, (8, LANES), 0)
        == lax.broadcasted_iota(jnp.int32, (8, LANES), 1) // HD
    ).astype(jnp.float32)
    keys = k_ref[...]
    values = v_ref[...]
    zero = jnp.zeros_like(keys)
    head_keys = (jnp.where(first, keys, zero), jnp.where(first, zero, keys))
    head_values = (jnp.where(first, values, zero), jnp.where(first, zero, values))
    key_segments = seg_col[...]
    key_sum = [None, None]
    value_sum = [None, None]
    query_total = jnp.zeros((1, LANES), jnp.float32)
    for block in range(length // rows):
        here = pl.ds(block * rows, rows)
        q = q_ref[here, :]
        do = do_ref[here, :]
        allowed = key_segments == seg_row[:, here]
        dots = lax.dot_general(
            pick,
            do.astype(jnp.float32) * o_ref[here, :].astype(jnp.float32),
            NT,
            precision=lax.Precision.HIGHEST,
            preferred_element_type=jnp.float32,
        )
        parts = []
        for head in range(2):
            scores = mxu(head_keys[head], q, NT)
            scores = jnp.where(allowed, scores, masked_score)
            probs = jnp.exp(scores - lse_ref[0, head : head + 1, here])
            prob_grad = mxu(head_values[head], do, NT)
            score_grad = (probs * (prob_grad - dots[head : head + 1, :])).astype(jnp.bfloat16)
            value_part = mxu(probs.astype(jnp.bfloat16), do, NN)
            key_part = mxu(score_grad, q, NN)
            value_sum[head] = value_part if block == 0 else value_sum[head] + value_part
            key_sum[head] = key_part if block == 0 else key_sum[head] + key_part
            parts.append(mxu(score_grad, keys, TN))
        query_grad = jnp.where(first, parts[0], parts[1]) * (1.0 / math.sqrt(HD))
        query_total = query_total + jnp.sum(query_grad, 0, keepdims=True)
        grad_ref[0, here, :] = query_grad.astype(jnp.bfloat16)
    grad_ref[1, :, :] = jnp.where(first, key_sum[0], key_sum[1]).astype(jnp.bfloat16)
    value_grad = jnp.where(first, value_sum[0], value_sum[1])
    grad_ref[2, :, :] = value_grad.astype(jnp.bfloat16)
    sum_ref[0:1, :] = query_total
    sum_ref[1:2, :] = jnp.sum(value_grad, 0, keepdims=True)


def attention_backward(qkv, out, out_grad, seg_col, seg_row, lse, start, pairs, at, size, before=None):
    length, width = out.shape
    total = width // LANES
    rows = min(256, length)
    anywhere = pl.BlockSpec(memory_space=pl.ANY)

    def pair(part):
        return pl.BlockSpec((length, LANES), lambda j: (0, part * total + start + j))

    def body(*refs):
        attention_backward_kernel(*refs[:8], *refs[-2:], rows=rows)

    return pl.pallas_call(
        body,
        grid=(pairs,),
        in_specs=[
            pair(0),
            pair(1),
            pair(2),
            pair(0),
            pair(0),
            pl.BlockSpec((length, 1), lambda j: (0, 0)),
            pl.BlockSpec((1, length), lambda j: (0, 0)),
            pl.BlockSpec((1, 2, length), lambda j: (j + start, 0, 0)),
        ]
        + [anywhere] * (0 if before is None else 2),
        out_specs=[
            pl.BlockSpec((3, length, LANES), lambda j: (0, 0, j + at)),
            pl.BlockSpec((2, LANES), lambda j: (0, j + at)),
        ],
        out_shape=[
            jax.ShapeDtypeStruct((3, length, size * LANES), jnp.bfloat16),
            jax.ShapeDtypeStruct((2, size * LANES), jnp.float32),
        ],
        input_output_aliases={} if before is None else {8: 0, 9: 1},
        compiler_params=params(40),
        cost_estimate=pl.CostEstimate(
            flops=40 * length * length * pairs * LANES,
            bytes_accessed=16 * length * pairs * LANES,
            transcendentals=0,
        ),
        name="attn_bwd",
    )(qkv, qkv, qkv, out, out_grad, seg_col, seg_row, lse, *(() if before is None else before))


class Place:
    def __init__(self, groups, shards):
        self.groups = groups
        self.shards = shards
        self.chips = shards // 2
        grp = lax.axis_index("grp")
        shard = lax.axis_index("shard")
        self.grp = grp
        self.shard = shard
        self.core = shard % 2
        self.chip = shard // 2
        self.scalars = jnp.stack([self.core, self.chip, grp]).astype(jnp.int32)

    def swap(self, array, grp=0, chip=0, core=0):
        mask = grp * self.shards + chip * 2 + core
        pairs = [(i, i ^ mask) for i in range(self.groups * self.shards)]
        return lax.ppermute(array, AXES, pairs)


def after(value, *others):
    return lax.optimization_barrier((value, *others))[0]


class Gather:
    def __init__(self, place, piece):
        self.place = place
        self.piece = piece
        self.held = [None] * 5
        self.crossed = [None] * 5

    def chips(self, *wait):
        place = self.place
        piece = after(self.piece, *wait) if wait else self.piece
        along = [piece] + [place.swap(piece, chip=k) for k in range(1, place.chips)]
        self.along = along
        self.held[0] = jnp.stack(along)
        return along[-1]

    def near(self, *wait):
        piece = after(self.held[0], *wait) if wait else self.held[0]
        self.held[1] = self.place.swap(piece, grp=1)
        self.held[2] = self.place.swap(piece, grp=2)
        return self.held[2]

    def far(self, *wait):
        half = self.held[0].shape[1] // 2
        first = after(self.held[1], *wait) if wait else self.held[1]
        second = after(self.held[2], *wait) if wait else self.held[2]
        self.held[3] = self.place.swap(first[:, :half], grp=2)
        self.held[4] = self.place.swap(second[:, half:], grp=1)
        return self.held[4]

    def cross(self, *which, wait=()):
        for n in which:
            piece = after(self.held[n], *wait) if wait else self.held[n]
            self.crossed[n] = self.place.swap(piece, core=1)

    def pieces(self):
        return self.held + self.crossed


class Window:
    def __init__(self, gather, start, cols):
        self.arrays = gather.pieces()
        self.start, self.cols = start, cols
        chips, rows, _ = self.arrays[0].shape
        self.chips, self.rows = chips, rows


def fetch(where, window, refs, whole, sem, groups, by):
    rows, cols = window.rows, window.cols
    core, chip, grp = where[0], where[1], where[2]
    for other_grp in range(groups):
        for k in range(window.chips):
            for n, ref in enumerate(refs):
                other_core, kind = n // 5, n % 5
                if min(kind, 3) != other_grp:
                    continue
                size = rows if kind < 3 else rows // 2
                col = pl.multiple_of((grp ^ other_grp) * cols, LANES)
                row = ((chip ^ k) * 2 + (core ^ other_core)) * rows + max(kind - 3, 0) * size
                slot = {"grp": other_grp, "all": 0}[by]
                pltpu.make_async_copy(
                    ref.at[k, :, pl.ds(window.start, cols)],
                    whole.at[pl.ds(pl.multiple_of(row, size), size), pl.ds(col, cols)],
                    sem.at[slot],
                ).start()


def weight_call(place, kernel, window, inputs, in_specs, outs, out_specs, steps, by, name, flops, mb=40):
    cols, groups = window.cols, place.groups
    pieces = window.arrays
    shape = (window.chips * 2 * window.rows, groups * cols)
    slots = {"grp": groups, "all": 1}[by]
    anywhere = pl.BlockSpec(memory_space=pl.ANY)

    def body(where, *refs):
        taken, refs = refs[: len(pieces)], refs[len(pieces) :]
        *refs, written, weight, sem, out_sem = refs
        step = pl.program_id(0)

        @pl.when(step == 0)
        def _():
            fetch(where, window, taken, weight, sem, groups, by)

        def ready():
            if by == "all":

                @pl.when(step == 0)
                def _():
                    pltpu.make_async_copy(weight, weight, sem.at[0]).wait()
                    pltpu.make_async_copy(weight, written, out_sem.at[0]).start()

            else:
                at = pl.ds(pl.multiple_of((where[2] ^ step) * cols, LANES), cols)
                view = weight.at[:, at]
                pltpu.make_async_copy(view, view, sem.at[step]).wait()
                pltpu.make_async_copy(view, written.at[:, at], out_sem.at[step]).start()

        kernel(where, ready, weight, *refs)

        @pl.when(step == steps - 1)
        def _():
            for slot in range(slots):
                width = shape[1] // slots
                view = weight.at[:, pl.ds(slot * width, width)]
                pltpu.make_async_copy(view, view, out_sem.at[slot]).wait()

    total = sum(math.prod(x.shape) * x.dtype.itemsize for x in list(inputs) + list(outs))
    return pl.pallas_call(
        body,
        grid_spec=pltpu.PrefetchScalarGridSpec(
            num_scalar_prefetch=1,
            grid=(steps,),
            in_specs=[anywhere] * len(pieces) + in_specs,
            out_specs=out_specs + [anywhere],
            scratch_shapes=[
                pltpu.VMEM(shape, jnp.bfloat16),
                pltpu.SemaphoreType.DMA((slots,)),
                pltpu.SemaphoreType.DMA((slots,)),
            ],
        ),
        out_shape=outs + [shaped(shape, jnp.bfloat16)],
        compiler_params=params(mb),
        cost_estimate=pl.CostEstimate(
            flops=flops, bytes_accessed=4 * shape[0] * shape[1] + total, transcendentals=0
        ),
        name=name,
    )(place.scalars, *pieces, *inputs)


def plain_call(kernel, inputs, in_specs, outs, out_specs, steps, name, flops, mb=40):
    total = sum(math.prod(x.shape) * x.dtype.itemsize for x in list(inputs) + list(outs))
    return pl.pallas_call(
        kernel,
        grid=(steps,),
        in_specs=in_specs,
        out_specs=out_specs,
        out_shape=outs,
        compiler_params=params(mb),
        cost_estimate=pl.CostEstimate(flops=flops, bytes_accessed=total, transcendentals=0),
        name=name,
    )(*inputs)


TILE = 256


def row_tiles(width):
    return pl.BlockSpec((TILE, width), lambda i, *s: (i, 0))


def fixed(*shape):
    return pl.BlockSpec(shape, lambda i, *s: (0,) * len(shape))


def whole_once(shape):
    return pl.BlockSpec(shape, lambda i: (0,) * len(shape), pipeline_mode=pl.Buffered(1))


def shaped(shape, dtype):
    return jax.ShapeDtypeStruct(shape, dtype)


def project_qkv(place, rows, window, bias, scale):
    length, width = rows.shape
    cols = window.cols

    def kernel(where, ready, weight, x_ref, bias_ref, scale_ref, out_ref):
        ready()
        at = pl.ds(pl.multiple_of((where[2] ^ pl.program_id(0)) * cols, LANES), cols)
        for tile in range(length // TILE):
            here = pl.ds(tile * TILE, TILE)
            mixed = mxu(x_ref[here, :], weight[:, at], NN) + bias_ref[:, at]
            mixed = mixed.astype(jnp.bfloat16).astype(jnp.float32) * scale_ref[:, at]
            out_ref[here, :] = mixed.astype(jnp.bfloat16)

    total = cols * place.groups
    return weight_call(
        place,
        kernel,
        window,
        (rows, bias, scale),
        [fixed(length, width), fixed(1, total), fixed(1, total)],
        [shaped((length, total), jnp.bfloat16)],
        [pl.BlockSpec((length, cols), lambda i, s: (0, i ^ s[2]))],
        place.groups,
        "grp",
        "qkv",
        2 * length * width * total,
    )


def norm_parts(rows):
    centered = rows - jnp.mean(rows, -1, keepdims=True)
    scale = lax.rsqrt(jnp.mean(centered * centered, -1, keepdims=True) + epsilon)
    return centered * scale, scale


def norm_back(grad, normed, scale):
    return scale * (
        grad
        - jnp.mean(grad, -1, keepdims=True)
        - normed * jnp.mean(grad * normed, -1, keepdims=True)
    )


def add_rows(sum_ref, *terms):
    @pl.when(pl.program_id(0) == 0)
    def _():
        sum_ref[...] = jnp.zeros_like(sum_ref)

    for n, term in enumerate(terms):
        sum_ref[n : n + 1, :] += jnp.sum(term, 0, keepdims=True)


def project_out(place, contexts, window, rows, bias, gain, shift):
    length, width = rows.shape

    def kernel(where, ready, weight, c_ref, x_ref, b_ref, g_ref, s_ref, n_ref, r_ref, low_ref):
        ready()
        first_sum = mxu(c_ref[...], weight[...], NN) + b_ref[...] + x_ref[...].astype(jnp.float32)
        normed, scale = norm_parts(first_sum)
        n_ref[...] = normed
        r_ref[...] = jnp.broadcast_to(scale, r_ref.shape)
        low_ref[...] = (normed * g_ref[...] + s_ref[...]).astype(jnp.bfloat16)

    return weight_call(
        place,
        kernel,
        window,
        (contexts, rows, bias, gain, shift),
        [row_tiles(width), row_tiles(width)] + [fixed(1, width)] * 3,
        [
            shaped((length, width), jnp.float32),
            shaped((length, LANES), jnp.float32),
            shaped((length, width), jnp.bfloat16),
        ],
        [row_tiles(width), row_tiles(LANES), row_tiles(width)],
        length // TILE,
        "all",
        "attn_out",
        2 * length * width * width,
    )


def feed_in(place, normed_low, window, bias):
    length, width = normed_low.shape
    cols = window.cols

    def kernel(where, ready, weight, x_ref, bias_ref, hid_ref, slope_ref):
        ready()
        at = pl.ds(pl.multiple_of((where[2] ^ pl.program_id(0)) * cols, LANES), cols)
        for tile in range(length // TILE):
            here = pl.ds(tile * TILE, TILE)
            pre = mxu(x_ref[here, :], weight[:, at], NN) + bias_ref[:, at]
            share = 0.5 + 0.5 * lax.erf(pre * (1.0 / math.sqrt(2.0)))
            bell = jnp.exp(-0.5 * pre * pre) * (1.0 / math.sqrt(2.0 * math.pi))
            hid_ref[here, :] = (pre * share).astype(jnp.bfloat16)
            slope_ref[here, :] = (share + pre * bell).astype(jnp.bfloat16)

    total = cols * place.groups
    block = pl.BlockSpec((length, cols), lambda i, s: (0, i ^ s[2]))
    return weight_call(
        place,
        kernel,
        window,
        (normed_low, bias),
        [fixed(length, width), fixed(1, total)],
        [shaped((length, total), jnp.bfloat16)] * 2,
        [block, block],
        place.groups,
        "grp",
        "feed_in",
        2 * length * width * total,
    )


def feed_out(place, hidden, window, normed, cot, keep, vectors):
    length, inner = hidden.shape
    width = normed.shape[1]

    def kernel(where, ready, weight, h_ref, n_ref, cot_ref, keep_ref, g1, s1, b2, g2, s2, *outs):
        out_ref, grad_ref, low_ref, sum_ref = outs
        ready()
        fed = mxu(h_ref[...], weight[...], NN)
        second_sum = n_ref[...] * g1[...] + s1[...] + (fed + b2[...])
        second, scale = norm_parts(second_sum)
        out_ref[...] = (second * g2[...] + s2[...]).astype(jnp.bfloat16)
        masked = cot_ref[...].astype(jnp.float32) * keep_ref[...]
        grad = norm_back(masked * g2[...], second, scale)
        grad_ref[...] = grad
        low_ref[...] = grad.astype(jnp.bfloat16)
        add_rows(sum_ref, masked * second, masked, grad)

    return weight_call(
        place,
        kernel,
        window,
        (hidden, normed, cot, keep, *vectors),
        [row_tiles(inner), row_tiles(width), row_tiles(width), row_tiles(1)] + [fixed(1, width)] * 5,
        [
            shaped((length, width), jnp.bfloat16),
            shaped((length, width), jnp.float32),
            shaped((length, width), jnp.bfloat16),
            shaped((8, width), jnp.float32),
        ],
        [row_tiles(width), row_tiles(width), row_tiles(width), fixed(8, width)],
        length // TILE,
        "all",
        "feed_out",
        2 * length * width * inner,
    )


def feed_out_back(out_low, weight, slope):
    length, width = out_low.shape
    inner = slope.shape[1]
    cols = min(1024, inner)

    def kernel(g_ref, w_ref, slope_ref, pre_ref, sum_ref):
        total = jnp.zeros((1, cols), jnp.float32)
        for tile in range(length // TILE):
            here = pl.ds(tile * TILE, TILE)
            grad = mxu(g_ref[here, :], w_ref[...], NT) * slope_ref[here, :].astype(jnp.float32)
            pre_ref[here, :] = grad.astype(jnp.bfloat16)
            total = total + jnp.sum(grad, 0, keepdims=True)
        sum_ref[...] = total

    block = pl.BlockSpec((length, cols), lambda i: (0, i))
    return plain_call(
        kernel,
        (out_low, weight, slope),
        [fixed(length, width), pl.BlockSpec((cols, width), lambda i: (i, 0)), block],
        [shaped((length, inner), jnp.bfloat16), shaped((1, inner), jnp.float32)],
        [block, pl.BlockSpec((1, cols), lambda i: (0, i))],
        inner // cols,
        "feed_out_back",
        2 * length * width * inner,
    )


def feed_in_back(pre_low, weight, second_grad, normed, scale, gain):
    length, inner = pre_low.shape
    width = normed.shape[1]

    def kernel(p_ref, w_ref, g_ref, n_ref, r_ref, gain_ref, first_ref, low_ref, sum_ref):
        grad = g_ref[...] + mxu(p_ref[...], w_ref[...], NT)
        first = norm_back(grad * gain_ref[...], n_ref[...], r_ref[:, :1])
        first_ref[...] = first
        low_ref[...] = first.astype(jnp.bfloat16)
        add_rows(sum_ref, grad * n_ref[...], grad, first)

    return plain_call(
        kernel,
        (pre_low, weight, second_grad, normed, scale, gain),
        [
            row_tiles(inner),
            whole_once(weight.shape),
            row_tiles(width),
            row_tiles(width),
            row_tiles(LANES),
            fixed(1, width),
        ],
        [
            shaped((length, width), jnp.float32),
            shaped((length, width), jnp.bfloat16),
            shaped((8, width), jnp.float32),
        ],
        [row_tiles(width), row_tiles(width), fixed(8, width)],
        length // TILE,
        "feed_in_back",
        2 * length * width * inner,
    )


def project_out_back(attn_low, weight):
    length, width = attn_low.shape

    def kernel(g_ref, w_ref, out_ref):
        out_ref[...] = mxu(g_ref[...], w_ref[...], NT).astype(jnp.bfloat16)

    return plain_call(
        kernel,
        (attn_low, weight),
        [row_tiles(width), whole_once(weight.shape)],
        [shaped((length, width), jnp.bfloat16)],
        [row_tiles(width)],
        length // TILE,
        "attn_out_back",
        2 * length * width * width,
    )[0]


def project_qkv_back(grads, weight, first_grad):
    length, width = first_grad.shape
    part = width // len(grads)

    def kernel(w_ref, *refs):
        *grad_refs, first_ref, out_ref = refs
        total = first_ref[...]
        for n in range(3):
            for m, grad_ref in enumerate(grad_refs):
                at = n * width + m * part
                total = total + mxu(grad_ref[n], w_ref[:, at : at + part], NT)
        out_ref[...] = total

    return plain_call(
        kernel,
        (weight, *grads, first_grad),
        [whole_once(weight.shape)]
        + [pl.BlockSpec((3, TILE, part), lambda i: (0, i, 0))] * len(grads)
        + [row_tiles(width)],
        [shaped((length, width), jnp.float32)],
        [row_tiles(width)],
        length // TILE,
        "qkv_back",
        6 * length * width * width,
    )[0]


def weight_grad_kernel(where, left_ref, right_ref, *refs, own, rows, groups, split):
    *refs, kept = refs
    received = None
    if own:
        received, *outs = refs
    else:
        outs = refs
    core, grp = where[0], where[2]
    keep = core if own else 1 - core
    chips = left_ref.shape[1] // (2 * rows)
    half = rows // 2

    @pl.when(pl.program_id(1) == 0)
    def _():
        lefts = []
        for k in range(chips):
            even = left_ref[:, 2 * k * rows : (2 * k + 1) * rows]
            odd = left_ref[:, (2 * k + 1) * rows : (2 * k + 2) * rows]
            lefts.append(jnp.where(keep == 0, even, odd))
        left = lefts[0] if chips == 1 else jnp.concatenate(lefts, 1)
        kept[...] = left.T

    def emit(slot, part, at):
        part = part.reshape(chips, 2, half, part.shape[-1])
        pos = 0 if split else slot
        if own:
            part = part + received[pos, :, :, :, at].astype(jnp.float32)
            part = part.astype(jnp.bfloat16)

            def store(slot):
                for lower in range(2):
                    near, far = ((1, 2), (2, 1))[lower]
                    block = part[:, lower]
                    if slot in (near, 3):
                        outs[3 * lower + 2][0 if slot == near else 1, :, :, at] = block
                    else:
                        outs[3 * lower + (1 if slot == far else 0)][:, :, at] = block

            if split:
                for n in range(groups):
                    pl.when(pl.program_id(1) == n)(functools.partial(store, n))
            else:
                store(slot)
        else:
            outs[0][pos, :, :, :, at] = part.astype(jnp.bfloat16)

    if split and len(right_ref.shape) == 3:
        size = right_ref.shape[2]
        for n in range(right_ref.shape[0]):
            emit(0, mxu(kept[...], right_ref[n], NN), slice(n * size, (n + 1) * size))
    elif split:
        size = min(512, right_ref.shape[1])
        for n in range(right_ref.shape[1] // size):
            at = slice(n * size, (n + 1) * size)
            emit(0, mxu(kept[...], right_ref[:, at], NN), at)
    else:
        cols = right_ref.shape[1] // groups
        for slot in range(groups):
            at = pl.multiple_of((grp ^ slot) * cols, LANES)
            emit(slot, mxu(kept[...], right_ref[:, pl.ds(at, cols)], NN), slice(0, cols))


def weight_grad(place, left, right, received, split, name):
    tokens, height = left.shape
    groups, chips = place.groups, place.chips
    rows = height // place.shards
    half = rows // 2
    parts = right.shape[0] if right.ndim == 3 else 1
    width = right.shape[-1] * parts
    cols = width // groups
    own = received is not None
    step_chips = chips if split else max(1, 1024 // (2 * rows))
    steps = chips // step_chips
    if split:
        grid = (steps, groups)
        if parts > 1:
            right_spec = pl.BlockSpec(
                (parts, tokens, cols // parts), lambda i, j, s: (0, 0, j ^ s[2])
            )
        else:
            right_spec = pl.BlockSpec((tokens, cols), lambda i, j, s: (0, j ^ s[2]))
        passed = pl.BlockSpec((1, step_chips, 2, half, cols), lambda i, j, s: (j, i, 0, 0, 0))
    else:
        grid = (steps, 1)
        right_spec = pl.BlockSpec((tokens, width), lambda i, j, s: (0, 0))
        passed = pl.BlockSpec((groups, step_chips, 2, half, cols), lambda i, j, s: (0, i, 0, 0, 0))
    in_specs = [pl.BlockSpec((tokens, step_chips * 2 * rows), lambda i, j, s: (0, i)), right_spec]
    inputs = [left, right]
    if own:
        in_specs.append(passed)
        inputs.append(received)
        one = pl.BlockSpec((step_chips, half, cols), lambda i, j, s: (i, 0, 0))
        two = pl.BlockSpec((2, step_chips, half, cols), lambda i, j, s: (0, i, 0, 0))
        out_specs = [one, one, two] * 2
        shape = (chips, half, cols)
        out_shape = [
            shaped(shape, jnp.bfloat16),
            shaped(shape, jnp.bfloat16),
            shaped((2, *shape), jnp.bfloat16),
        ] * 2
    else:
        out_specs = passed
        out_shape = shaped((groups, chips, 2, half, cols), jnp.bfloat16)
    return pl.pallas_call(
        functools.partial(weight_grad_kernel, own=own, rows=rows, groups=groups, split=split),
        grid_spec=pltpu.PrefetchScalarGridSpec(
            num_scalar_prefetch=1,
            grid=grid,
            in_specs=in_specs,
            out_specs=out_specs,
            scratch_shapes=[pltpu.VMEM((step_chips * rows, tokens), jnp.bfloat16)],
        ),
        out_shape=out_shape,
        compiler_params=params(40),
        cost_estimate=pl.CostEstimate(
            flops=tokens * height * width,
            bytes_accessed=2 * (tokens * (height + width) + height * width),
            transcendentals=0,
        ),
        name="wgrad_" + name + ("_own" if own else "_sent"),
    )(place.scalars, *inputs)


def add(*terms):
    total = terms[0].astype(jnp.float32)
    for term in terms[1:]:
        total = total + term.astype(jnp.float32)
    return total.astype(jnp.bfloat16)


class Reduction:
    def __init__(self, place, left, right, split, name, *wait):
        self.place = place
        left = after(left, *wait) if wait else left
        self.call = (left, right, split, name)
        self.sent = weight_grad(place, left, right, None, split, name)
        self.received = place.swap(self.sent, core=1)

    def own(self, *wait):
        left, right, split, name = self.call
        received = after(self.received, *wait) if wait else self.received
        out = weight_grad(self.place, left, right, received, split, name)
        self.kept = out
        self.near = [self.place.swap(out[2], grp=1), self.place.swap(out[5], grp=2)]
        return out[0]

    def middle(self, *wait):
        near = after(self.near[0], *wait) if wait else self.near[0]
        self.near[0] = near
        upper = add(self.kept[1], near[1])
        lower = add(self.kept[4], self.near[1][1])
        self.far = [self.place.swap(upper, grp=2), self.place.swap(lower, grp=1)]
        return upper

    def along(self, *wait):
        place = self.place
        far = after(self.far[0], *wait) if wait else self.far[0]
        mine = jnp.concatenate(
            [
                add(self.kept[0], self.near[0][0], far),
                add(self.kept[3], self.near[1][0], self.far[1]),
            ],
            1,
        )
        self.terms = [lax.dynamic_index_in_dim(mine, place.chip, 0, False)]
        for k in range(1, place.chips):
            outgoing = lax.dynamic_index_in_dim(mine, place.chip ^ k, 0, False)
            self.terms.append(place.swap(outgoing, chip=k))
        return self.terms[0]

    def share(self, *wait):
        last = after(self.terms[-1], *wait) if wait else self.terms[-1]
        share = add(*self.terms[:-1], last)
        self.blocks = [share] + [self.place.swap(share, grp=k) for k in range(1, self.place.groups)]
        return share

    def result(self):
        return in_order(self.place, self.blocks)


def in_order(place, blocks):
    blocks = [b.astype(jnp.float32) for b in blocks]
    ordered = []
    for g in range(place.groups):
        block = blocks[0]
        for k in range(1, place.groups):
            block = jnp.where((place.grp ^ k) == g, blocks[k], block)
        ordered.append(block)
    return ordered


def sum_everywhere(place, vector):
    for how in ({"core": 1}, {"grp": 1}, {"grp": 2}):
        vector = vector + place.swap(vector, **how)
    step = 1
    while step < place.chips:
        vector = vector + place.swap(vector, chip=step)
        step *= 2
    return vector


def own_part(place, vector):
    size = vector.shape[0] // place.shards
    return lax.dynamic_slice_in_dim(vector, place.shard * size, size)


def on_device_permutes(
    tokens,
    segment_ids,
    keep_flag,
    cotangent,
    w_qkv,
    b_query,
    b_value,
    w_attn_out,
    b_attn_out,
    norm1_gain,
    norm1_bias,
    w_in,
    b_in,
    w_out,
    b_out,
    norm2_gain,
    norm2_bias,
    *,
    groups,
    shards,
):
    place = Place(groups, shards)
    _, length, width = tokens.shape
    vectors = (
        b_query,
        b_value,
        b_attn_out,
        norm1_gain,
        norm1_bias,
        b_in,
        b_out,
        norm2_gain,
        norm2_bias,
    )
    rows = tokens[0]
    seg_row = segment_ids.reshape(1, length)
    seg_col = segment_ids.reshape(length, 1)
    keep = keep_flag.reshape(length, 1).astype(jnp.float32)
    pairs = width // LANES

    flat = jnp.concatenate(vectors)
    extra = 16
    flat = jnp.pad(flat, (0, extra * w_qkv.shape[1] - flat.shape[0])).reshape(extra, -1)
    c1 = Gather(place, jnp.concatenate([w_qkv, flat], 0))
    c2 = Gather(place, jnp.concatenate([w_in, w_attn_out], 1))
    c3 = Gather(place, w_out)
    wait = c1.chips()
    rider = jnp.stack([p[-extra:] for p in c1.along])
    c1.held[0] = jnp.stack([p[:-extra] for p in c1.along])
    near = c1.near()
    both = [rider, place.swap(rider, core=1)]
    wait = c2.chips(wait)
    c1.cross(0)
    c1.far()
    c1.cross(1, 2)
    c2.near(near)
    c3.chips(near, wait)
    c1.cross(3, 4)

    def owner(shard):
        found = both[0][0]
        for other in range(1, shards):
            found = jnp.where(
                (place.shard ^ other) == shard, both[other % 2][other // 2], found
            )
        return found.reshape(-1)

    parts = [owner(shard).astype(jnp.float32) for shard in range(shards)]
    unpacked = []
    at = 0
    for vector in vectors:
        size = vector.shape[0]
        unpacked.append(jnp.concatenate([p[at : at + size] for p in parts]).reshape(1, -1))
        at += size
    (
        bias_query,
        bias_value,
        bias_attn,
        gain_one,
        shift_one,
        bias_in,
        bias_out,
        gain_two,
        shift_two,
    ) = unpacked
    blank = jnp.zeros_like(bias_query)
    qkv_bias = jnp.concatenate([bias_query, blank, bias_value], 1)
    qkv_scale = jnp.concatenate([blank + 1.0 / math.sqrt(HD), blank + 1.0, blank + 1.0], 1)

    mixed, full_qkv = project_qkv(place, rows, Window(c1, 0, w_qkv.shape[1]), qkv_bias, qkv_scale)
    c2.far(mixed)
    c2.cross(0, 1, 2, wait=(mixed,))
    forward = attention_forward(mixed, seg_col, seg_row, 0, pairs // 2)
    done = forward[1]
    c2.cross(3, 4, wait=(done,))
    c3.near(done, c2.held[3], c2.held[4])
    contexts, lse = attention_forward(
        after(mixed, c2.held[3], c2.held[4]), seg_col, seg_row, pairs // 2, pairs // 2, forward
    )
    normed, scale_one, normed_low, full_attn = project_out(
        place, contexts, Window(c2, w_in.shape[1], w_attn_out.shape[1]), rows, bias_attn, gain_one, shift_one
    )
    c3.far(normed_low)
    c3.cross(0, 1, 2, wait=(normed_low,))
    hidden, slope, full_in = feed_in(
        place, after(normed_low, c3.held[1], c3.held[2]), Window(c2, 0, w_in.shape[1]), bias_in
    )
    c3.cross(3, 4, wait=(hidden,))
    layer_out, second_grad, out_low, second_sums, full_out = feed_out(
        place,
        hidden,
        Window(c3, 0, w_out.shape[1]),
        normed,
        cotangent[0],
        keep,
        (gain_one, shift_one, bias_out, gain_two, shift_two),
    )

    r_out = Reduction(place, hidden, out_low, False, "out")
    pre_low, bias_in_grad = feed_out_back(after(out_low, r_out.sent), full_out, slope)
    own_out = r_out.own(pre_low)
    r_in = Reduction(place, normed_low, pre_low, True, "in", own_out)
    first_grad, attn_low, first_sums = feed_in_back(
        after(pre_low, r_in.sent), full_in, second_grad, normed, scale_one, gain_one
    )
    own_in = r_in.own(first_grad)
    r_attn = Reduction(place, contexts, attn_low, False, "attn", own_in)
    context_grad = project_out_back(after(attn_low, r_attn.sent), full_attn)
    own_attn = r_attn.own(context_grad)
    quarter = pairs // 4

    def back(start, at, before=None, *wait):
        return attention_backward(
            mixed,
            contexts,
            after(context_grad, *wait),
            seg_col,
            seg_row,
            lse,
            start,
            quarter,
            at,
            2 * quarter,
            before,
        )

    mid_out = r_out.middle(own_attn)
    part = back(0, 0, None, mid_out)
    mid_in = r_in.middle(part[1])
    low_a, late_a = back(quarter, quarter, part, mid_in)
    along_out = r_out.along(late_a)
    mid_attn = r_attn.middle(late_a)
    r_qkv_a = Reduction(place, rows, low_a, True, "qkv_a", along_out, mid_attn)
    part = back(2 * quarter, 0, None, r_qkv_a.sent)
    along_in = r_in.along(part[1])
    along_attn = r_attn.along(part[1])
    share_out = r_out.share(part[1])
    own_a = r_qkv_a.own(part[1], along_in, along_attn, share_out)
    low_b, late_b = back(3 * quarter, quarter, part, own_a)
    mid_a = r_qkv_a.middle(late_b)
    share_in = r_in.share(late_b)
    share_attn = r_attn.share(late_b)
    r_qkv_b = Reduction(place, rows, low_b, True, "qkv_b", mid_a, share_in, share_attn)
    input_grad = project_qkv_back((low_a, after(low_b, r_qkv_b.sent)), full_qkv, first_grad)
    own_b = r_qkv_b.own(input_grad)
    r_qkv_a.along(own_b)
    r_qkv_b.middle()
    r_qkv_a.share()
    r_qkv_b.along()
    r_qkv_b.share()

    sums = (
        jnp.concatenate([late_a[0], late_b[0]]),
        jnp.concatenate([late_a[1], late_b[1]]),
        first_sums[2],
        first_sums[0],
        first_sums[1],
        bias_in_grad[0],
        second_sums[2],
        second_sums[0],
        second_sums[1],
    )
    summed = sum_everywhere(place, jnp.concatenate(sums).reshape(-1, LANES)).reshape(-1)
    vectors = []
    at = 0
    for vector in sums:
        vectors.append(own_part(place, summed[at : at + vector.shape[0]]))
        at += vector.shape[0]

    parts_a, parts_b = r_qkv_a.result(), r_qkv_b.result()
    heads = parts_a[0].shape[1] // 3
    w_qkv_grad = jnp.concatenate(
        [
            block[:, n * heads : (n + 1) * heads]
            for n in range(3)
            for half in (parts_a, parts_b)
            for block in half
        ],
        1,
    )
    return (
        layer_out[None],
        input_grad[None],
        w_qkv_grad,
        vectors[0],
        vectors[1],
        jnp.concatenate(r_attn.result(), 1),
        vectors[2],
        vectors[3],
        vectors[4],
        jnp.concatenate(r_in.result(), 1),
        vectors[5],
        jnp.concatenate(r_out.result(), 1),
        vectors[6],
        vectors[7],
        vectors[8],
    )


def solution(mesh):
    groups, shards = mesh.shape["grp"], mesh.shape["shard"]
    if groups == 4 and shards == 8:
        body = functools.partial(on_device_permutes, groups=groups, shards=shards)
    else:
        body = on_device
    return jax.shard_map(
        body,
        mesh=mesh,
        in_specs=(
            P(("grp", "shard"), None, None),
            P(("grp", "shard"), None),
            P(("grp", "shard"), None),
            P(("grp", "shard"), None, None),
            P("shard", "grp"),
            P("shard"),
            P("shard"),
            P("shard", "grp"),
            P("shard"),
            P("shard"),
            P("shard"),
            P("shard", "grp"),
            P("shard"),
            P("shard", "grp"),
            P("shard"),
            P("shard"),
            P("shard"),
        ),
        out_specs=(
            P(("grp", "shard"), None, None),
            P(("grp", "shard"), None, None),
            P("shard", None),
            P("shard"),
            P("shard"),
            P("shard", None),
            P("shard"),
            P("shard"),
            P("shard"),
            P("shard", None),
            P("shard"),
            P("shard", None),
            P("shard"),
            P("shard"),
            P("shard"),
        ),
        check_vma=False,
    )
```

```python
import functools
import math

import jax
import jax.numpy as jnp
from jax import lax
from jax.experimental import pallas as pl
from jax.experimental.pallas import tpu as pltpu
from jax.sharding import PartitionSpec as P

H = 16
HD = 64


masked_score = -1e30
epsilon = 1e-05


def norm_layer(rows, gain_row, shift_row):
    row_mean = jnp.mean(rows, -1, keepdims=True)
    centered = rows - row_mean
    row_var = jnp.mean(centered * centered, -1, keepdims=True)
    return centered * lax.rsqrt(row_var + epsilon) * gain_row + shift_row


def gelu_exact(values):
    return 0.5 * values * (1.0 + lax.erf(values * (1.0 / math.sqrt(2.0))))


def contract_rows(left, right):
    return lax.dot_general(
        left, right, (((0,), (0,)), ((), ())), preferred_element_type=jnp.float32
    )


def contract_cols(left, right):
    return lax.dot_general(
        left, right, (((1,), (1,)), ((), ())), preferred_element_type=jnp.float32
    )


def attend_forward(queries, key_rows, value_rows, segment_row, block_rows):
    length, model_width = queries.shape
    scaling = 1.0 / math.sqrt(HD)
    key_heads = key_rows.reshape(length, H, HD)
    value_heads = value_rows.reshape(length, H, HD)
    query_blocks = queries.reshape(length // block_rows, block_rows, H, HD)
    segment_blocks = segment_row.reshape(length // block_rows, block_rows)

    def one_block(pieces):
        query_part, segment_part = pieces
        scores = (
            jnp.einsum("qhd,khd->hqk", query_part, key_heads, preferred_element_type=jnp.float32)
            * scaling
        )
        allowed = segment_part[:, None] == segment_row[None, :]
        scores = jnp.where(allowed[None], scores, masked_score)
        row_max = jnp.max(scores, -1, keepdims=True)
        powers = jnp.exp(scores - row_max)
        totals = jnp.sum(powers, -1, keepdims=True)
        attn_probs = (powers / totals).astype(jnp.bfloat16)
        context = jnp.einsum(
            "hqk,khd->qhd", attn_probs, value_heads, preferred_element_type=jnp.float32
        )
        return (
            context.reshape(block_rows, model_width).astype(jnp.bfloat16),
            (row_max + jnp.log(totals))[:, :, 0],
        )

    contexts, log_sums = lax.map(one_block, (query_blocks, segment_blocks))
    return (contexts.reshape(length, model_width), log_sums)


def attend_backward(queries, key_rows, value_rows, segment_row, log_sums, context_grad, block_rows):
    length, model_width = queries.shape
    scaling = 1.0 / math.sqrt(HD)
    key_heads = key_rows.reshape(length, H, HD)
    value_heads = value_rows.reshape(length, H, HD)
    query_blocks = queries.reshape(length // block_rows, block_rows, H, HD)
    segment_blocks = segment_row.reshape(length // block_rows, block_rows)
    grad_blocks = context_grad.reshape(length // block_rows, block_rows, H, HD)

    def one_block(running, pieces):
        key_acc, value_acc = running
        query_part, segment_part, lse_part, grad_part = pieces
        scores = (
            jnp.einsum("qhd,khd->hqk", query_part, key_heads, preferred_element_type=jnp.float32)
            * scaling
        )
        allowed = segment_part[:, None] == segment_row[None, :]
        scores = jnp.where(allowed[None], scores, masked_score)
        probs = jnp.exp(scores - lse_part[:, :, None])
        prob_low = probs.astype(jnp.bfloat16)
        prob_grad = jnp.einsum(
            "qhd,khd->hqk", grad_part, value_heads, preferred_element_type=jnp.float32
        )
        row_dot = jnp.sum(prob_grad * probs, -1, keepdims=True)
        score_grad = (probs * (prob_grad - row_dot)).astype(jnp.bfloat16)
        query_grad = (
            jnp.einsum("hqk,khd->qhd", score_grad, key_heads, preferred_element_type=jnp.float32)
            * scaling
        )
        key_acc = (
            key_acc
            + jnp.einsum("hqk,qhd->khd", score_grad, query_part, preferred_element_type=jnp.float32)
            * scaling
        )
        value_acc = value_acc + jnp.einsum(
            "hqk,qhd->khd", prob_low, grad_part, preferred_element_type=jnp.float32
        )
        return ((key_acc, value_acc), query_grad.reshape(block_rows, model_width))

    empty_acc = jnp.zeros((length, H, HD), jnp.float32)
    (key_grad, value_grad), query_grads = lax.scan(
        one_block, (empty_acc, empty_acc), (query_blocks, segment_blocks, log_sums, grad_blocks)
    )
    return (
        query_grads.reshape(length, model_width),
        key_grad.reshape(length, model_width),
        value_grad.reshape(length, model_width),
    )


def on_device(
    tokens,
    segment_ids,
    keep_flag,
    cotangent,
    w_qkv,
    b_query,
    b_value,
    w_attn_out,
    b_attn_out,
    norm1_gain,
    norm1_bias,
    w_in,
    b_in,
    w_out,
    b_out,
    norm2_gain,
    norm2_bias,
):
    seq_count, length, model_width = tokens.shape
    block_rows = min(512, length)
    within = (
        lax.all_gather(w_qkv, "shard", axis=0, tiled=True),
        lax.all_gather(w_attn_out, "shard", axis=0, tiled=True),
        lax.all_gather(w_in, "shard", axis=0, tiled=True),
        lax.all_gather(w_out, "shard", axis=0, tiled=True),
        lax.all_gather(b_query, "shard", axis=0, tiled=True),
        lax.all_gather(b_value, "shard", axis=0, tiled=True),
        lax.all_gather(b_attn_out, "shard", axis=0, tiled=True),
        lax.all_gather(norm1_gain, "shard", axis=0, tiled=True),
        lax.all_gather(norm1_bias, "shard", axis=0, tiled=True),
        lax.all_gather(b_in, "shard", axis=0, tiled=True),
        lax.all_gather(b_out, "shard", axis=0, tiled=True),
        lax.all_gather(norm2_gain, "shard", axis=0, tiled=True),
        lax.all_gather(norm2_bias, "shard", axis=0, tiled=True),
    )
    full_qkv, full_attn, full_in, full_out = (
        lax.all_gather(within[0], "grp", axis=1, tiled=True),
        lax.all_gather(within[1], "grp", axis=1, tiled=True),
        lax.all_gather(within[2], "grp", axis=1, tiled=True),
        lax.all_gather(within[3], "grp", axis=1, tiled=True),
    )
    (
        bias_query,
        bias_value,
        bias_attn,
        gain_one,
        shift_one,
        bias_in,
        bias_out,
        gain_two,
        shift_two,
    ) = [piece.astype(jnp.float32) for piece in within[4:]]
    flat_rows = tokens.reshape(seq_count * length, model_width)
    mixed_qkv = jnp.dot(flat_rows, full_qkv, preferred_element_type=jnp.float32)
    queries = (mixed_qkv[:, :model_width] + bias_query).astype(jnp.bfloat16)
    key_rows = mixed_qkv[:, model_width : 2 * model_width].astype(jnp.bfloat16)
    value_rows = (mixed_qkv[:, 2 * model_width :] + bias_value).astype(jnp.bfloat16)
    query_seqs = queries.reshape(seq_count, length, model_width)
    key_seqs = key_rows.reshape(seq_count, length, model_width)
    value_seqs = value_rows.reshape(seq_count, length, model_width)

    def forward_sequence(pieces):
        return attend_forward(pieces[0], pieces[1], pieces[2], pieces[3], block_rows)

    contexts, log_sums = lax.map(forward_sequence, (query_seqs, key_seqs, value_seqs, segment_ids))
    contexts = contexts.reshape(seq_count * length, model_width)
    attended = jnp.dot(contexts, full_attn, preferred_element_type=jnp.float32) + bias_attn
    first_sum = flat_rows.astype(jnp.float32) + attended
    normed_one, norm_one_back = jax.vjp(norm_layer, first_sum, gain_one, shift_one)
    normed_low = normed_one.astype(jnp.bfloat16)
    hidden_pre = jnp.dot(normed_low, full_in, preferred_element_type=jnp.float32) + bias_in
    hidden, gelu_back = jax.vjp(gelu_exact, hidden_pre)
    hidden_low = hidden.astype(jnp.bfloat16)
    second_sum = normed_one + (
        jnp.dot(hidden_low, full_out, preferred_element_type=jnp.float32) + bias_out
    )
    result, norm_two_back = jax.vjp(norm_layer, second_sum, gain_two, shift_two)
    layer_out = result.astype(jnp.bfloat16).reshape(seq_count, length, model_width)
    again = (
        lax.all_gather(w_qkv, "shard", axis=0, tiled=True),
        lax.all_gather(w_attn_out, "shard", axis=0, tiled=True),
        lax.all_gather(w_in, "shard", axis=0, tiled=True),
        lax.all_gather(w_out, "shard", axis=0, tiled=True),
    )
    back_qkv, back_attn, back_in, back_out = (
        lax.all_gather(again[0], "grp", axis=1, tiled=True),
        lax.all_gather(again[1], "grp", axis=1, tiled=True),
        lax.all_gather(again[2], "grp", axis=1, tiled=True),
        lax.all_gather(again[3], "grp", axis=1, tiled=True),
    )
    masked_cot = cotangent.astype(jnp.float32).reshape(
        seq_count * length, model_width
    ) * keep_flag.reshape(seq_count * length, 1).astype(jnp.float32)
    second_grad, gain_two_grad, shift_two_grad = norm_two_back(masked_cot)
    bias_out_grad = jnp.sum(second_grad, 0)
    out_low = second_grad.astype(jnp.bfloat16)
    w_out_grad = contract_rows(hidden_low, out_low)
    hidden_grad = contract_cols(out_low, back_out)
    (pre_grad,) = gelu_back(hidden_grad)
    bias_in_grad = jnp.sum(pre_grad, 0)
    pre_low = pre_grad.astype(jnp.bfloat16)
    w_in_grad = contract_rows(normed_low, pre_low)
    normed_grad = second_grad + contract_cols(pre_low, back_in)
    first_grad, gain_one_grad, shift_one_grad = norm_one_back(normed_grad)
    bias_attn_grad = jnp.sum(first_grad, 0)
    attn_low = first_grad.astype(jnp.bfloat16)
    w_attn_grad = contract_rows(contexts, attn_low)
    context_grad = contract_cols(attn_low, back_attn).astype(jnp.bfloat16)

    def backward_sequence(pieces):
        return attend_backward(
            pieces[0], pieces[1], pieces[2], pieces[3], pieces[4], pieces[5], block_rows
        )

    query_grad, key_grad, value_grad = lax.map(
        backward_sequence,
        (
            query_seqs,
            key_seqs,
            value_seqs,
            segment_ids,
            log_sums,
            context_grad.reshape(seq_count, length, model_width),
        ),
    )
    query_grad = query_grad.reshape(seq_count * length, model_width)
    key_grad = key_grad.reshape(seq_count * length, model_width)
    value_grad = value_grad.reshape(seq_count * length, model_width)
    bias_query_grad = jnp.sum(query_grad, 0)
    bias_value_grad = jnp.sum(value_grad, 0)
    qkv_low = jnp.concatenate([query_grad, key_grad, value_grad], 1).astype(jnp.bfloat16)
    w_qkv_grad = contract_rows(flat_rows, qkv_low)
    input_grad = first_grad + contract_cols(qkv_low, back_qkv)
    reduced = (
        lax.psum_scatter(
            w_qkv_grad.astype(jnp.bfloat16), "shard", scatter_dimension=0, tiled=True
        ).astype(jnp.float32),
        lax.psum_scatter(
            bias_query_grad.astype(jnp.bfloat16), "shard", scatter_dimension=0, tiled=True
        ).astype(jnp.float32),
        lax.psum_scatter(
            bias_value_grad.astype(jnp.bfloat16), "shard", scatter_dimension=0, tiled=True
        ).astype(jnp.float32),
        lax.psum_scatter(
            w_attn_grad.astype(jnp.bfloat16), "shard", scatter_dimension=0, tiled=True
        ).astype(jnp.float32),
        lax.psum_scatter(
            bias_attn_grad.astype(jnp.bfloat16), "shard", scatter_dimension=0, tiled=True
        ).astype(jnp.float32),
        lax.psum_scatter(
            gain_one_grad.astype(jnp.bfloat16), "shard", scatter_dimension=0, tiled=True
        ).astype(jnp.float32),
        lax.psum_scatter(
            shift_one_grad.astype(jnp.bfloat16), "shard", scatter_dimension=0, tiled=True
        ).astype(jnp.float32),
        lax.psum_scatter(
            w_in_grad.astype(jnp.bfloat16), "shard", scatter_dimension=0, tiled=True
        ).astype(jnp.float32),
        lax.psum_scatter(
            bias_in_grad.astype(jnp.bfloat16), "shard", scatter_dimension=0, tiled=True
        ).astype(jnp.float32),
        lax.psum_scatter(
            w_out_grad.astype(jnp.bfloat16), "shard", scatter_dimension=0, tiled=True
        ).astype(jnp.float32),
        lax.psum_scatter(
            bias_out_grad.astype(jnp.bfloat16), "shard", scatter_dimension=0, tiled=True
        ).astype(jnp.float32),
        lax.psum_scatter(
            gain_two_grad.astype(jnp.bfloat16), "shard", scatter_dimension=0, tiled=True
        ).astype(jnp.float32),
        lax.psum_scatter(
            shift_two_grad.astype(jnp.bfloat16), "shard", scatter_dimension=0, tiled=True
        ).astype(jnp.float32),
    )
    summed = (
        lax.psum(reduced[0].astype(jnp.bfloat16), "grp").astype(jnp.float32),
        lax.psum(reduced[1].astype(jnp.bfloat16), "grp").astype(jnp.float32),
        lax.psum(reduced[2].astype(jnp.bfloat16), "grp").astype(jnp.float32),
        lax.psum(reduced[3].astype(jnp.bfloat16), "grp").astype(jnp.float32),
        lax.psum(reduced[4].astype(jnp.bfloat16), "grp").astype(jnp.float32),
        lax.psum(reduced[5].astype(jnp.bfloat16), "grp").astype(jnp.float32),
        lax.psum(reduced[6].astype(jnp.bfloat16), "grp").astype(jnp.float32),
        lax.psum(reduced[7].astype(jnp.bfloat16), "grp").astype(jnp.float32),
        lax.psum(reduced[8].astype(jnp.bfloat16), "grp").astype(jnp.float32),
        lax.psum(reduced[9].astype(jnp.bfloat16), "grp").astype(jnp.float32),
        lax.psum(reduced[10].astype(jnp.bfloat16), "grp").astype(jnp.float32),
        lax.psum(reduced[11].astype(jnp.bfloat16), "grp").astype(jnp.float32),
        lax.psum(reduced[12].astype(jnp.bfloat16), "grp").astype(jnp.float32),
    )
    return (
        layer_out,
        input_grad.reshape(seq_count, length, model_width),
        summed[0],
        summed[1],
        summed[2],
        summed[3],
        summed[4],
        summed[5],
        summed[6],
        summed[7],
        summed[8],
        summed[9],
        summed[10],
        summed[11],
        summed[12],
    )


NT = (((1,), (1,)), ((), ()))
NN = (((1,), (0,)), ((), ()))
TN = (((0,), (0,)), ((), ()))
LANES = 128
AXES = ("grp", "shard")


def mxu(left, right, dims):
    return lax.dot_general(left, right, dims, preferred_element_type=jnp.float32)


def params(megabytes=60):
    return pltpu.CompilerParams(vmem_limit_bytes=megabytes << 20)


def attention_forward_kernel(q_ref, k_ref, v_ref, seg_col, seg_row, out_ref, lse_ref, *, rows):
    length = q_ref.shape[0]
    first = lax.broadcasted_iota(jnp.int32, (1, LANES), 1) < HD
    keys = k_ref[...]
    values = v_ref[...]
    zero = jnp.zeros_like(keys)
    head_keys = (jnp.where(first, keys, zero), jnp.where(first, zero, keys))
    key_segments = seg_col[...]
    for block in range(length // rows):
        here = pl.ds(block * rows, rows)
        q = q_ref[here, :]
        allowed = key_segments == seg_row[:, here]
        outs = []
        for head in range(2):
            scores = mxu(head_keys[head], q, NT)
            scores = jnp.where(allowed, scores, masked_score)
            top = jnp.max(scores, 0, keepdims=True)
            powers = jnp.exp(scores - top)
            total = jnp.sum(powers, 0, keepdims=True)
            part = mxu(powers.astype(jnp.bfloat16), values, TN)
            outs.append(part * jnp.transpose(jnp.broadcast_to(1.0 / total, (LANES, rows))))
            lse_ref[0, head : head + 1, here] = top + jnp.log(total)
        out_ref[here, :] = jnp.where(first, outs[0], outs[1]).astype(jnp.bfloat16)


def attention_forward(qkv, seg_col, seg_row, start, pairs, before=None):
    length, width = qkv.shape[0], qkv.shape[1] // 3
    total = width // LANES
    rows = min(512, length)
    anywhere = pl.BlockSpec(memory_space=pl.ANY)

    def pair(part):
        return pl.BlockSpec((length, LANES), lambda j: (0, part * total + start + j))

    def body(q_ref, k_ref, v_ref, seg_c, seg_r, *refs):
        attention_forward_kernel(q_ref, k_ref, v_ref, seg_c, seg_r, *refs[-2:], rows=rows)

    return pl.pallas_call(
        body,
        grid=(pairs,),
        in_specs=[
            pair(0),
            pair(1),
            pair(2),
            pl.BlockSpec((length, 1), lambda j: (0, 0)),
            pl.BlockSpec((1, length), lambda j: (0, 0)),
        ]
        + [anywhere] * (0 if before is None else 2),
        out_specs=[
            pl.BlockSpec((length, LANES), lambda j: (0, start + j)),
            pl.BlockSpec((1, 2, length), lambda j: (start + j, 0, 0)),
        ],
        out_shape=[
            jax.ShapeDtypeStruct((length, width), jnp.bfloat16),
            jax.ShapeDtypeStruct((total, 2, length), jnp.float32),
        ],
        input_output_aliases={} if before is None else {5: 0, 6: 1},
        compiler_params=params(60),
        cost_estimate=pl.CostEstimate(
            flops=16 * length * length * pairs * LANES,
            bytes_accessed=8 * length * pairs * LANES,
            transcendentals=0,
        ),
        name="attn_fwd",
    )(qkv, qkv, qkv, seg_col, seg_row, *(() if before is None else before))


def attention_backward_kernel(
    q_ref, k_ref, v_ref, o_ref, do_ref, seg_col, seg_row, lse_ref, grad_ref, sum_ref, *, rows
):
    length = q_ref.shape[0]
    lane = lax.broadcasted_iota(jnp.int32, (1, LANES), 1)
    first = lane < HD
    pick = (
        lax.broadcasted_iota(jnp.int32, (8, LANES), 0)
        == lax.broadcasted_iota(jnp.int32, (8, LANES), 1) // HD
    ).astype(jnp.float32)
    keys = k_ref[...]
    values = v_ref[...]
    zero = jnp.zeros_like(keys)
    head_keys = (jnp.where(first, keys, zero), jnp.where(first, zero, keys))
    head_values = (jnp.where(first, values, zero), jnp.where(first, zero, values))
    key_segments = seg_col[...]
    key_sum = [None, None]
    value_sum = [None, None]
    query_total = jnp.zeros((1, LANES), jnp.float32)
    for block in range(length // rows):
        here = pl.ds(block * rows, rows)
        q = q_ref[here, :]
        do = do_ref[here, :]
        allowed = key_segments == seg_row[:, here]
        dots = lax.dot_general(
            pick,
            do.astype(jnp.float32) * o_ref[here, :].astype(jnp.float32),
            NT,
            precision=lax.Precision.HIGHEST,
            preferred_element_type=jnp.float32,
        )
        parts = []
        for head in range(2):
            scores = mxu(head_keys[head], q, NT)
            scores = jnp.where(allowed, scores, masked_score)
            probs = jnp.exp(scores - lse_ref[0, head : head + 1, here])
            prob_grad = mxu(head_values[head], do, NT)
            score_grad = (probs * (prob_grad - dots[head : head + 1, :])).astype(jnp.bfloat16)
            value_part = mxu(probs.astype(jnp.bfloat16), do, NN)
            key_part = mxu(score_grad, q, NN)
            value_sum[head] = value_part if block == 0 else value_sum[head] + value_part
            key_sum[head] = key_part if block == 0 else key_sum[head] + key_part
            parts.append(mxu(score_grad, keys, TN))
        query_grad = jnp.where(first, parts[0], parts[1]) * (1.0 / math.sqrt(HD))
        query_total = query_total + jnp.sum(query_grad, 0, keepdims=True)
        grad_ref[0, here, :] = query_grad.astype(jnp.bfloat16)
    grad_ref[1, :, :] = jnp.where(first, key_sum[0], key_sum[1]).astype(jnp.bfloat16)
    value_grad = jnp.where(first, value_sum[0], value_sum[1])
    grad_ref[2, :, :] = value_grad.astype(jnp.bfloat16)
    sum_ref[0:1, :] = query_total
    sum_ref[1:2, :] = jnp.sum(value_grad, 0, keepdims=True)


def attention_backward(qkv, out, out_grad, seg_col, seg_row, lse, start, pairs, at, size, before=None):
    length, width = out.shape
    total = width // LANES
    rows = min(256, length)
    anywhere = pl.BlockSpec(memory_space=pl.ANY)

    def pair(part):
        return pl.BlockSpec((length, LANES), lambda j: (0, part * total + start + j))

    def body(*refs):
        attention_backward_kernel(*refs[:8], *refs[-2:], rows=rows)

    return pl.pallas_call(
        body,
        grid=(pairs,),
        in_specs=[
            pair(0),
            pair(1),
            pair(2),
            pair(0),
            pair(0),
            pl.BlockSpec((length, 1), lambda j: (0, 0)),
            pl.BlockSpec((1, length), lambda j: (0, 0)),
            pl.BlockSpec((1, 2, length), lambda j: (j + start, 0, 0)),
        ]
        + [anywhere] * (0 if before is None else 2),
        out_specs=[
            pl.BlockSpec((3, length, LANES), lambda j: (0, 0, j + at)),
            pl.BlockSpec((2, LANES), lambda j: (0, j + at)),
        ],
        out_shape=[
            jax.ShapeDtypeStruct((3, length, size * LANES), jnp.bfloat16),
            jax.ShapeDtypeStruct((2, size * LANES), jnp.float32),
        ],
        input_output_aliases={} if before is None else {8: 0, 9: 1},
        compiler_params=params(60),
        cost_estimate=pl.CostEstimate(
            flops=40 * length * length * pairs * LANES,
            bytes_accessed=16 * length * pairs * LANES,
            transcendentals=0,
        ),
        name="attn_bwd",
    )(qkv, qkv, qkv, out, out_grad, seg_col, seg_row, lse, *(() if before is None else before))


class Place:
    def __init__(self, groups, shards):
        self.groups = groups
        self.shards = shards
        self.chips = shards // 2
        self.grp = lax.axis_index("grp")
        self.shard = lax.axis_index("shard")
        self.core = self.shard % 2
        self.chip = self.shard // 2
        self.scalars = jnp.stack([self.core, self.chip, self.grp]).astype(jnp.int32)

    def permute(self, array, mask_of_core):
        pairs = [(i, i ^ mask_of_core[i % 2]) for i in range(self.groups * self.shards)]
        return lax.ppermute(array, AXES, pairs)

    def swap_core(self, array):
        return self.permute(array, (1, 1))

    def swap_grp(self, array, step):
        masks = (self.shards, 2 * self.shards)
        return self.permute(array, masks if step == 0 else masks[::-1])

    def swap_chip(self, array, step):
        masks = (2, 4)
        return self.permute(array, masks if step == 0 else masks[::-1])

    def slot_chip(self, slot):
        return self.chip ^ turn(slot, self.core)

    def slot_grp(self, slot):
        return self.grp ^ turn(slot, self.core)


def turn(slot, core):
    if isinstance(slot, int):
        return slot if slot in (0, 3) else jnp.where(core == 0, slot, 3 - slot)
    return jnp.where((core == 0) | (slot == 0) | (slot == 3), slot, 3 - slot)


def after(value, *others):
    return lax.optimization_barrier((value, *others))[0]


class Gather:
    def __init__(self, place, piece):
        self.place = place
        self.piece = piece
        self.held = [None] * 3
        self.crossed = [None] * 3

    def chips_near(self, *wait):
        piece = after(self.piece, *wait) if wait else self.piece
        self.pair = jnp.stack([piece, self.place.swap_chip(piece, 0)])
        return self.pair

    def chips_far(self, *wait):
        pair = after(self.pair, *wait) if wait else self.pair
        self.held[0] = jnp.concatenate([self.pair, self.place.swap_chip(pair, 1)])
        return self.held[0]

    def near(self, *wait):
        piece = after(self.held[0], *wait) if wait else self.held[0]
        self.held[1] = self.place.swap_grp(piece, 0)
        return self.held[1]

    def far(self, *wait):
        both = jnp.concatenate(self.held[:2])
        both = after(both, *wait) if wait else both
        self.held[2] = self.place.swap_grp(both, 1)
        return self.held[2]

    def cross(self, *which, wait=()):
        for n in which:
            piece = after(self.held[n], *wait) if wait else self.held[n]
            self.crossed[n] = self.place.swap_core(piece)

    def pieces(self):
        return self.held + self.crossed


class Window:
    def __init__(self, gather, start, cols):
        self.arrays = gather.pieces()
        self.start, self.cols = start, cols
        chips, rows, _ = self.arrays[0].shape
        self.chips, self.rows = chips, rows


def fetch(where, window, refs, whole, sem, by):
    rows, cols, chips = window.rows, window.cols, window.chips
    for slot in range(4):
        for side in range(2):
            core = where[0] ^ side
            ref = refs[3 * side + min(slot, 2)]
            distance = turn(slot, core)
            col = pl.multiple_of((where[2] ^ distance) * cols, LANES)
            for k in range(chips):
                row = ((where[1] ^ turn(k, core)) * 2 + core) * rows
                pltpu.make_async_copy(
                    ref.at[k + (chips if slot == 3 else 0), :, pl.ds(window.start, cols)],
                    whole.at[pl.ds(pl.multiple_of(row, rows), rows), pl.ds(col, cols)],
                    sem.at[distance if by == "grp" else 0],
                ).start()


def weight_call(place, kernel, window, inputs, in_specs, outs, out_specs, steps, by, name, flops, mb=60):
    cols, groups = window.cols, place.groups
    pieces = window.arrays
    shape = (window.chips * 2 * window.rows, groups * cols)
    slots = {"grp": groups, "all": 1}[by]
    anywhere = pl.BlockSpec(memory_space=pl.ANY)

    def body(where, *refs):
        taken, refs = refs[: len(pieces)], refs[len(pieces) :]
        *refs, written, weight, sem, out_sem = refs
        step = pl.program_id(0)

        @pl.when(step == 0)
        def _():
            fetch(where, window, taken, weight, sem, by)

        def ready():
            if by == "all":

                @pl.when(step == 0)
                def _():
                    pltpu.make_async_copy(weight, weight, sem.at[0]).wait()
                    pltpu.make_async_copy(weight, written, out_sem.at[0]).start()

            else:
                at = pl.ds(pl.multiple_of((where[2] ^ step) * cols, LANES), cols)
                view = weight.at[:, at]
                pltpu.make_async_copy(view, view, sem.at[step]).wait()
                pltpu.make_async_copy(view, written.at[:, at], out_sem.at[step]).start()

        kernel(where, ready, weight, *refs)

        @pl.when(step == steps - 1)
        def _():
            for slot in range(slots):
                width = shape[1] // slots
                view = weight.at[:, pl.ds(slot * width, width)]
                pltpu.make_async_copy(view, view, out_sem.at[slot]).wait()

    total = sum(math.prod(x.shape) * x.dtype.itemsize for x in list(inputs) + list(outs))
    return pl.pallas_call(
        body,
        grid_spec=pltpu.PrefetchScalarGridSpec(
            num_scalar_prefetch=1,
            grid=(steps,),
            in_specs=[anywhere] * len(pieces) + in_specs,
            out_specs=out_specs + [anywhere],
            scratch_shapes=[
                pltpu.VMEM(shape, jnp.bfloat16),
                pltpu.SemaphoreType.DMA((slots,)),
                pltpu.SemaphoreType.DMA((slots,)),
            ],
        ),
        out_shape=outs + [shaped(shape, jnp.bfloat16)],
        compiler_params=params(mb),
        cost_estimate=pl.CostEstimate(
            flops=flops, bytes_accessed=4 * shape[0] * shape[1] + total, transcendentals=0
        ),
        name=name,
    )(place.scalars, *pieces, *inputs)


def plain_call(kernel, inputs, in_specs, outs, out_specs, steps, name, flops, mb=60):
    total = sum(math.prod(x.shape) * x.dtype.itemsize for x in list(inputs) + list(outs))
    return pl.pallas_call(
        kernel,
        grid=(steps,),
        in_specs=in_specs,
        out_specs=out_specs,
        out_shape=outs,
        compiler_params=params(mb),
        cost_estimate=pl.CostEstimate(flops=flops, bytes_accessed=total, transcendentals=0),
        name=name,
    )(*inputs)


TILE = 256


def row_tiles(width):
    return pl.BlockSpec((TILE, width), lambda i, *s: (i, 0))


def fixed(*shape):
    return pl.BlockSpec(shape, lambda i, *s: (0,) * len(shape))


def whole_once(shape):
    return pl.BlockSpec(shape, lambda i: (0,) * len(shape), pipeline_mode=pl.Buffered(1))


def shaped(shape, dtype):
    return jax.ShapeDtypeStruct(shape, dtype)


def project_qkv(place, rows, window, bias, scale):
    length, width = rows.shape
    cols = window.cols

    def kernel(where, ready, weight, x_ref, bias_ref, scale_ref, out_ref):
        ready()
        at = pl.ds(pl.multiple_of((where[2] ^ pl.program_id(0)) * cols, LANES), cols)
        for tile in range(length // TILE):
            here = pl.ds(tile * TILE, TILE)
            mixed = mxu(x_ref[here, :], weight[:, at], NN) + bias_ref[:, at]
            mixed = mixed.astype(jnp.bfloat16).astype(jnp.float32) * scale_ref[:, at]
            out_ref[here, :] = mixed.astype(jnp.bfloat16)

    total = cols * place.groups
    return weight_call(
        place,
        kernel,
        window,
        (rows, bias, scale),
        [fixed(length, width), fixed(1, total), fixed(1, total)],
        [shaped((length, total), jnp.bfloat16)],
        [pl.BlockSpec((length, cols), lambda i, s: (0, i ^ s[2]))],
        place.groups,
        "grp",
        "qkv",
        2 * length * width * total,
    )


def norm_parts(rows):
    centered = rows - jnp.mean(rows, -1, keepdims=True)
    scale = lax.rsqrt(jnp.mean(centered * centered, -1, keepdims=True) + epsilon)
    return centered * scale, scale


def norm_back(grad, normed, scale):
    return scale * (
        grad
        - jnp.mean(grad, -1, keepdims=True)
        - normed * jnp.mean(grad * normed, -1, keepdims=True)
    )


def add_rows(sum_ref, *terms):
    @pl.when(pl.program_id(0) == 0)
    def _():
        sum_ref[...] = jnp.zeros_like(sum_ref)

    for n, term in enumerate(terms):
        sum_ref[n : n + 1, :] += jnp.sum(term, 0, keepdims=True)


def project_out(place, contexts, window, rows, bias, gain, shift):
    length, width = rows.shape

    def kernel(where, ready, weight, c_ref, x_ref, b_ref, g_ref, s_ref, n_ref, r_ref, low_ref):
        ready()
        first_sum = mxu(c_ref[...], weight[...], NN) + b_ref[...] + x_ref[...].astype(jnp.float32)
        normed, scale = norm_parts(first_sum)
        n_ref[...] = normed
        r_ref[...] = jnp.broadcast_to(scale, r_ref.shape)
        low_ref[...] = (normed * g_ref[...] + s_ref[...]).astype(jnp.bfloat16)

    return weight_call(
        place,
        kernel,
        window,
        (contexts, rows, bias, gain, shift),
        [row_tiles(width), row_tiles(width)] + [fixed(1, width)] * 3,
        [
            shaped((length, width), jnp.float32),
            shaped((length, LANES), jnp.float32),
            shaped((length, width), jnp.bfloat16),
        ],
        [row_tiles(width), row_tiles(LANES), row_tiles(width)],
        length // TILE,
        "all",
        "attn_out",
        2 * length * width * width,
    )


def feed_in(place, normed_low, window, bias):
    length, width = normed_low.shape
    cols = window.cols

    def kernel(where, ready, weight, x_ref, bias_ref, hid_ref, slope_ref):
        ready()
        at = pl.ds(pl.multiple_of((where[2] ^ pl.program_id(0)) * cols, LANES), cols)
        for tile in range(length // TILE):
            here = pl.ds(tile * TILE, TILE)
            pre = mxu(x_ref[here, :], weight[:, at], NN) + bias_ref[:, at]
            share = 0.5 + 0.5 * lax.erf(pre * (1.0 / math.sqrt(2.0)))
            bell = jnp.exp(-0.5 * pre * pre) * (1.0 / math.sqrt(2.0 * math.pi))
            hid_ref[here, :] = (pre * share).astype(jnp.bfloat16)
            slope_ref[here, :] = (share + pre * bell).astype(jnp.bfloat16)

    total = cols * place.groups
    block = pl.BlockSpec((length, cols), lambda i, s: (0, i ^ s[2]))
    return weight_call(
        place,
        kernel,
        window,
        (normed_low, bias),
        [fixed(length, width), fixed(1, total)],
        [shaped((length, total), jnp.bfloat16)] * 2,
        [block, block],
        place.groups,
        "grp",
        "feed_in",
        2 * length * width * total,
    )


def feed_out(place, hidden, window, normed, cot, keep, vectors):
    length, inner = hidden.shape
    width = normed.shape[1]

    def kernel(where, ready, weight, h_ref, n_ref, cot_ref, keep_ref, g1, s1, b2, g2, s2, *outs):
        out_ref, grad_ref, low_ref, sum_ref = outs
        ready()
        fed = mxu(h_ref[...], weight[...], NN)
        second_sum = n_ref[...] * g1[...] + s1[...] + (fed + b2[...])
        second, scale = norm_parts(second_sum)
        out_ref[...] = (second * g2[...] + s2[...]).astype(jnp.bfloat16)
        masked = cot_ref[...].astype(jnp.float32) * keep_ref[...]
        grad = norm_back(masked * g2[...], second, scale)
        grad_ref[...] = grad
        low_ref[...] = grad.astype(jnp.bfloat16)
        add_rows(sum_ref, masked * second, masked, grad)

    return weight_call(
        place,
        kernel,
        window,
        (hidden, normed, cot, keep, *vectors),
        [row_tiles(inner), row_tiles(width), row_tiles(width), row_tiles(1)] + [fixed(1, width)] * 5,
        [
            shaped((length, width), jnp.bfloat16),
            shaped((length, width), jnp.float32),
            shaped((length, width), jnp.bfloat16),
            shaped((8, width), jnp.float32),
        ],
        [row_tiles(width), row_tiles(width), row_tiles(width), fixed(8, width)],
        length // TILE,
        "all",
        "feed_out",
        2 * length * width * inner,
    )


def feed_out_back(out_low, weight, slope):
    length, width = out_low.shape
    inner = slope.shape[1]
    cols = min(1024, inner)

    def kernel(g_ref, w_ref, slope_ref, pre_ref, sum_ref):
        total = jnp.zeros((1, cols), jnp.float32)
        for tile in range(length // TILE):
            here = pl.ds(tile * TILE, TILE)
            grad = mxu(g_ref[here, :], w_ref[...], NT) * slope_ref[here, :].astype(jnp.float32)
            pre_ref[here, :] = grad.astype(jnp.bfloat16)
            total = total + jnp.sum(grad, 0, keepdims=True)
        sum_ref[...] = total

    block = pl.BlockSpec((length, cols), lambda i: (0, i))
    return plain_call(
        kernel,
        (out_low, weight, slope),
        [fixed(length, width), pl.BlockSpec((cols, width), lambda i: (i, 0)), block],
        [shaped((length, inner), jnp.bfloat16), shaped((1, inner), jnp.float32)],
        [block, pl.BlockSpec((1, cols), lambda i: (0, i))],
        inner // cols,
        "feed_out_back",
        2 * length * width * inner,
    )


def feed_in_back(pre_low, weight, second_grad, normed, scale, gain):
    length, inner = pre_low.shape
    width = normed.shape[1]

    def kernel(p_ref, w_ref, g_ref, n_ref, r_ref, gain_ref, first_ref, low_ref, sum_ref):
        grad = g_ref[...] + mxu(p_ref[...], w_ref[...], NT)
        first = norm_back(grad * gain_ref[...], n_ref[...], r_ref[:, :1])
        first_ref[...] = first
        low_ref[...] = first.astype(jnp.bfloat16)
        add_rows(sum_ref, grad * n_ref[...], grad, first)

    return plain_call(
        kernel,
        (pre_low, weight, second_grad, normed, scale, gain),
        [
            row_tiles(inner),
            whole_once(weight.shape),
            row_tiles(width),
            row_tiles(width),
            row_tiles(LANES),
            fixed(1, width),
        ],
        [
            shaped((length, width), jnp.float32),
            shaped((length, width), jnp.bfloat16),
            shaped((8, width), jnp.float32),
        ],
        [row_tiles(width), row_tiles(width), fixed(8, width)],
        length // TILE,
        "feed_in_back",
        2 * length * width * inner,
    )


def project_out_back(attn_low, weight):
    length, width = attn_low.shape

    def kernel(g_ref, w_ref, out_ref):
        out_ref[...] = mxu(g_ref[...], w_ref[...], NT).astype(jnp.bfloat16)

    return plain_call(
        kernel,
        (attn_low, weight),
        [row_tiles(width), whole_once(weight.shape)],
        [shaped((length, width), jnp.bfloat16)],
        [row_tiles(width)],
        length // TILE,
        "attn_out_back",
        2 * length * width * width,
    )[0]


def project_qkv_back(grads, weight, first_grad):
    length, width = first_grad.shape
    part = width // len(grads)

    def kernel(w_ref, *refs):
        *grad_refs, first_ref, out_ref = refs
        total = first_ref[...]
        for n in range(3):
            for m, grad_ref in enumerate(grad_refs):
                at = n * width + m * part
                total = total + mxu(grad_ref[n], w_ref[:, at : at + part], NT)
        out_ref[...] = total

    return plain_call(
        kernel,
        (weight, *grads, first_grad),
        [whole_once(weight.shape)]
        + [pl.BlockSpec((3, TILE, part), lambda i: (0, i, 0))] * len(grads)
        + [row_tiles(width)],
        [shaped((length, width), jnp.float32)],
        [row_tiles(width)],
        length // TILE,
        "qkv_back",
        6 * length * width * width,
    )[0]


def weight_grad_kernel(where, *refs, own, rows, groups, count, split):
    lefts, rights, refs = refs[:count], refs[count : 2 * count], refs[2 * count :]
    outs, kept = refs[:-count], refs[-count:]
    received = None
    if own:
        received, *outs = outs
    keep = where[0] if own else 1 - where[0]
    chips = lefts[0].shape[1] // (2 * rows)

    @pl.when(pl.program_id(1) == 0)
    def _():
        for left_ref, kept_ref in zip(lefts, kept):
            chosen = []
            for k in range(chips):
                even = left_ref[:, 2 * k * rows : (2 * k + 1) * rows]
                odd = left_ref[:, (2 * k + 1) * rows : (2 * k + 2) * rows]
                chosen.append(jnp.where(keep == 0, even, odd))
            left = chosen[0] if chips == 1 else jnp.concatenate(chosen, 1)
            kept_ref[...] = left.T

    def emit(slot, part, at):
        part = part.reshape(chips, rows, part.shape[-1])
        pos = 0 if split else slot
        if own:
            part = (part + received[pos, :, :, at].astype(jnp.float32)).astype(jnp.bfloat16)

            def store(slot):
                if slot in (1, 3):
                    outs[2][slot // 2, :, :, at] = part
                else:
                    outs[slot // 2][:, :, at] = part

            if split:
                for n in range(groups):
                    pl.when(pl.program_id(1) == n)(functools.partial(store, n))
            else:
                store(slot)
        else:
            outs[0][pos, :, :, at] = part.astype(jnp.bfloat16)

    if split:
        at = 0
        for right_ref, kept_ref in zip(rights, kept):
            if len(right_ref.shape) == 3:
                size = right_ref.shape[2]
                pieces = [right_ref[n] for n in range(right_ref.shape[0])]
            else:
                size = min(512, right_ref.shape[1])
                pieces = [
                    right_ref[:, n * size : (n + 1) * size]
                    for n in range(right_ref.shape[1] // size)
                ]
            for piece in pieces:
                emit(0, mxu(kept_ref[...], piece, NN), slice(at, at + size))
                at += size
    else:
        cols = rights[0].shape[1] // groups
        for slot in range(groups):
            start = pl.multiple_of((where[2] ^ turn(slot, keep)) * cols, LANES)
            emit(slot, mxu(kept[0][...], rights[0][:, pl.ds(start, cols)], NN), slice(0, cols))


def weight_grad(place, pairs, received, split, name):
    tokens, height = pairs[0][0].shape
    groups, chips = place.groups, place.chips
    rows = height // place.shards
    own = received is not None
    step_chips = chips if split else max(1, 1024 // (2 * rows))
    steps = chips // step_chips
    grid = (steps, groups if split else 1)

    def block(j, s):
        return s[2] ^ turn(j, s[0] if own else 1 - s[0])

    cols = 0
    right_specs = []
    for _, right in pairs:
        size = right.shape[-1] // groups
        if not split:
            right_specs.append(pl.BlockSpec(right.shape, lambda i, j, s: (0, 0)))
        elif right.ndim == 3:
            right_specs.append(
                pl.BlockSpec((right.shape[0], tokens, size), lambda i, j, s: (0, 0, block(j, s)))
            )
        else:
            right_specs.append(pl.BlockSpec((tokens, size), lambda i, j, s: (0, block(j, s))))
        cols += size * (right.shape[0] if right.ndim == 3 else 1)
    left_spec = pl.BlockSpec((tokens, step_chips * 2 * rows), lambda i, j, s: (0, i))
    if split:
        passed = pl.BlockSpec((1, step_chips, rows, cols), lambda i, j, s: (j, i, 0, 0))
    else:
        passed = pl.BlockSpec((groups, step_chips, rows, cols), lambda i, j, s: (0, i, 0, 0))
    in_specs = [left_spec] * len(pairs) + right_specs
    inputs = [left for left, _ in pairs] + [right for _, right in pairs]
    if own:
        in_specs.append(passed)
        inputs.append(received)
        one = pl.BlockSpec((step_chips, rows, cols), lambda i, j, s: (i, 0, 0))
        two = pl.BlockSpec((2, step_chips, rows, cols), lambda i, j, s: (0, i, 0, 0))
        out_specs = [one, one, two]
        shape = (chips, rows, cols)
        out_shape = [
            shaped(shape, jnp.bfloat16),
            shaped(shape, jnp.bfloat16),
            shaped((2, *shape), jnp.bfloat16),
        ]
    else:
        out_specs = passed
        out_shape = shaped((groups, chips, rows, cols), jnp.bfloat16)
    return pl.pallas_call(
        functools.partial(
            weight_grad_kernel, own=own, rows=rows, groups=groups, count=len(pairs), split=split
        ),
        grid_spec=pltpu.PrefetchScalarGridSpec(
            num_scalar_prefetch=1,
            grid=grid,
            in_specs=in_specs,
            out_specs=out_specs,
            scratch_shapes=[pltpu.VMEM((step_chips * rows, tokens), jnp.bfloat16)] * len(pairs),
        ),
        out_shape=out_shape,
        compiler_params=params(60),
        cost_estimate=pl.CostEstimate(
            flops=tokens * height * cols * groups,
            bytes_accessed=2 * (tokens * (height + cols * groups) + height * cols * groups),
            transcendentals=0,
        ),
        name="wgrad_" + name + ("_own" if own else "_sent"),
    )(place.scalars, *inputs)


def add(*terms):
    total = terms[0].astype(jnp.float32)
    for term in terms[1:]:
        total = total + term.astype(jnp.float32)
    return total.astype(jnp.bfloat16)


class Reduction:
    def __init__(self, place, pairs, split, name, *wait):
        self.place = place
        if wait:
            pairs = [(after(pairs[0][0], *wait), pairs[0][1])] + pairs[1:]
        self.call = (pairs, split, name)
        self.sent = weight_grad(place, pairs, None, split, name)
        self.received = place.swap_core(self.sent)

    def own(self, *wait):
        pairs, split, name = self.call
        received = after(self.received, *wait) if wait else self.received
        self.own_0, self.own_2, both = weight_grad(self.place, pairs, received, split, name)
        self.first = self.place.swap_grp(both, 0)
        return self.own_0

    def middle(self, *wait):
        self.first = after(self.first, *wait) if wait else self.first
        second = add(self.own_2, self.first[1])
        self.second = self.place.swap_grp(second, 1)
        return second

    def along(self, *wait):
        place = self.place
        second = after(self.second, *wait) if wait else self.second
        mine = add(self.own_0, self.first[0], second)
        blocks = [
            lax.dynamic_index_in_dim(mine, place.slot_chip(slot), 0, False) for slot in range(4)
        ]
        self.mine = blocks
        self.first = place.swap_chip(jnp.stack([blocks[1], blocks[3]]), 0)
        return mine

    def along_far(self, *wait):
        self.first = after(self.first, *wait) if wait else self.first
        second = add(self.mine[2], self.first[1])
        self.second = self.place.swap_chip(second, 1)
        return second

    def share(self, *wait):
        second = after(self.second, *wait) if wait else self.second
        return add(self.mine[0], self.first[0], second)


class Replication:
    def __init__(self, place, share):
        self.place = place
        self.pair = jnp.stack([share, place.swap_grp(share, 0)])

    def far(self, *wait):
        pair = after(self.pair, *wait) if wait else self.pair
        self.rest = self.place.swap_grp(pair, 1)
        return self.rest

    def result(self):
        place = self.place
        slots = [self.pair[0], self.pair[1], self.rest[0], self.rest[1]]
        ordered = []
        for g in range(place.groups):
            block = slots[0]
            for slot in range(1, place.groups):
                block = jnp.where(place.slot_grp(slot) == g, slots[slot], block)
            ordered.append(block.astype(jnp.float32))
        return ordered


def sum_everywhere(place, vector):
    vector = vector + place.swap_core(vector)
    for step in range(2):
        vector = vector + place.swap_grp(vector, step)
    for step in range(2):
        vector = vector + place.swap_chip(vector, step)
    return vector


def own_part(place, vector):
    size = vector.shape[0] // place.shards
    return lax.dynamic_slice_in_dim(vector, place.shard * size, size)


def on_device_permutes(
    tokens,
    segment_ids,
    keep_flag,
    cotangent,
    w_qkv,
    b_query,
    b_value,
    w_attn_out,
    b_attn_out,
    norm1_gain,
    norm1_bias,
    w_in,
    b_in,
    w_out,
    b_out,
    norm2_gain,
    norm2_bias,
    *,
    groups,
    shards,
):
    place = Place(groups, shards)
    _, length, width = tokens.shape
    vectors = (
        b_query,
        b_value,
        b_attn_out,
        norm1_gain,
        norm1_bias,
        b_in,
        b_out,
        norm2_gain,
        norm2_bias,
    )
    rows = tokens[0]
    seg_row = segment_ids.reshape(1, length)
    seg_col = segment_ids.reshape(length, 1)
    keep = keep_flag.reshape(length, 1).astype(jnp.float32)
    pairs = width // LANES

    c1 = Gather(place, w_qkv)
    wait = c1.chips_near()
    block = jnp.concatenate([w_in, w_attn_out], 1)
    flat = jnp.concatenate([after(vectors[0], wait), *vectors[1:]])
    extra = 16
    flat = jnp.pad(flat, (0, extra * block.shape[1] - flat.shape[0])).reshape(extra, -1)
    c2 = Gather(place, jnp.concatenate([block, flat], 0))
    c3 = Gather(place, w_out)
    c1.chips_far()
    near = c1.near()
    c1.cross(0)
    c2.chips_near(c1.held[0])
    far = c1.far()
    c2.chips_far(near)
    rider = c2.held[0][:, -extra:]
    c2.held[0] = c2.held[0][:, :-extra]
    both = [rider, place.swap_core(rider)]
    c1.cross(1)
    c1.cross(2)
    c2.near(far)

    def owner(shard):
        found = both[0][0]
        for side in range(2):
            for slot in range(4):
                here = (place.chip ^ turn(slot, place.core ^ side)) * 2 + (place.core ^ side)
                found = jnp.where(here == shard, both[side][slot], found)
        return found.reshape(-1)

    parts = [owner(shard).astype(jnp.float32) for shard in range(shards)]
    unpacked = []
    at = 0
    for vector in vectors:
        size = vector.shape[0]
        unpacked.append(jnp.concatenate([p[at : at + size] for p in parts]).reshape(1, -1))
        at += size
    (
        bias_query,
        bias_value,
        bias_attn,
        gain_one,
        shift_one,
        bias_in,
        bias_out,
        gain_two,
        shift_two,
    ) = unpacked
    blank = jnp.zeros_like(bias_query)
    qkv_bias = jnp.concatenate([bias_query, blank, bias_value], 1)
    qkv_scale = jnp.concatenate([blank + 1.0 / math.sqrt(HD), blank + 1.0, blank + 1.0], 1)

    mixed, full_qkv = project_qkv(place, rows, Window(c1, 0, w_qkv.shape[1]), qkv_bias, qkv_scale)
    c2.far(mixed)
    c2.cross(0, 1, wait=(mixed,))
    c3.chips_near(mixed)
    quarter = pairs // 4
    forward = None
    for n in range(4):
        gate = ((), (c3.pair,), (c3.held[0],), (c2.held[2],))[n]
        forward = attention_forward(
            after(mixed, *gate) if gate else mixed, seg_col, seg_row, n * quarter, quarter, forward
        )
        if n == 0:
            c3.chips_far(forward[1])
        if n == 2:
            c2.cross(2, wait=(forward[1],))
            c3.near(forward[1], c2.held[2])
    contexts, lse = forward
    normed, scale_one, normed_low, full_attn = project_out(
        place, contexts, Window(c2, w_in.shape[1], w_attn_out.shape[1]), rows, bias_attn, gain_one, shift_one
    )
    c3.far(normed_low)
    c3.cross(0, 1, wait=(normed_low,))
    hidden, slope, full_in = feed_in(
        place, after(normed_low, c3.held[1]), Window(c2, 0, w_in.shape[1]), bias_in
    )
    c3.cross(2, wait=(hidden,))
    layer_out, second_grad, out_low, second_sums, full_out = feed_out(
        place,
        hidden,
        Window(c3, 0, w_out.shape[1]),
        normed,
        cotangent[0],
        keep,
        (gain_one, shift_one, bias_out, gain_two, shift_two),
    )

    r_out = Reduction(place, [(hidden, out_low)], False, "out")
    pre_low, bias_in_grad = feed_out_back(after(out_low, r_out.sent), full_out, slope)
    own_out = r_out.own(pre_low)
    r_in = Reduction(place, [(normed_low, pre_low)], True, "in", own_out)
    first_grad, attn_low, first_sums = feed_in_back(
        after(pre_low, r_in.sent), full_in, second_grad, normed, scale_one, gain_one
    )
    mid_out = r_out.middle(first_grad)
    own_in = r_in.own(first_grad, mid_out)
    context_grad = project_out_back(after(attn_low, own_in), full_attn)

    def back(start, at, before=None, *wait):
        return attention_backward(
            mixed,
            contexts,
            after(context_grad, *wait) if wait else context_grad,
            seg_col,
            seg_row,
            lse,
            start,
            quarter,
            at,
            2 * quarter,
            before,
        )

    part = back(0, 0)
    along = r_out.along(part[1])
    low_a, late_a = back(quarter, quarter, part, along)
    mid_in = r_in.middle(late_a)
    along = r_out.along_far(late_a)
    r_a = Reduction(place, [(contexts, attn_low), (rows, low_a)], True, "a", mid_in, along)
    part = back(2 * quarter, 0, None, r_a.sent)
    along = r_in.along(part[1])
    share_out = r_out.share(part[1])
    own_a = r_a.own(along, share_out)
    low_b, late_b = back(3 * quarter, quarter, part, own_a)
    mid_a = r_a.middle(late_b)
    along = r_in.along_far(late_b)
    r_b = Reduction(place, [(rows, low_b)], True, "b", mid_a, along)
    along = r_a.along(r_b.sent)
    share_in = r_in.share(r_b.sent)
    inner = share_in.shape[1] // groups
    joined = jnp.concatenate(
        [share_out] + [share_in[:, n * inner : (n + 1) * inner] for n in range(groups)]
    )
    all_ffn = Replication(place, joined)
    own_b = r_b.own(along, share_in)
    input_grad = project_qkv_back((low_a, after(low_b, own_b)), full_qkv, first_grad)
    r_b.middle(input_grad)
    all_ffn.far(input_grad)
    r_a.along_far(input_grad)
    r_b.along()
    all_a = Replication(place, r_a.share())
    r_b.along_far()
    all_a.far()
    all_b = Replication(place, r_b.share())
    all_b.far()

    sums = (
        jnp.concatenate([late_a[0], late_b[0]]),
        jnp.concatenate([late_a[1], late_b[1]]),
        first_sums[2],
        first_sums[0],
        first_sums[1],
        bias_in_grad[0],
        second_sums[2],
        second_sums[0],
        second_sums[1],
    )
    summed = sum_everywhere(place, jnp.concatenate(sums).reshape(-1, LANES)).reshape(-1)
    vectors = []
    at = 0
    for vector in sums:
        vectors.append(own_part(place, summed[at : at + vector.shape[0]]))
        at += vector.shape[0]

    parts_a, parts_b = all_a.result(), all_b.result()
    heads = parts_b[0].shape[1] // 3
    skip = parts_a[0].shape[1] - 3 * heads
    w_attn_grad = jnp.concatenate([block[:, :skip] for block in parts_a], 1)
    parts_a = [block[:, skip:] for block in parts_a]
    w_qkv_grad = jnp.concatenate(
        [
            block[:, n * heads : (n + 1) * heads]
            for n in range(3)
            for half in (parts_a, parts_b)
            for block in half
        ],
        1,
    )
    parts = all_ffn.result()
    height = share_out.shape[0]
    w_out_grad = jnp.concatenate([block[:height] for block in parts], 1)
    size = share_in.shape[0]
    w_in_grad = jnp.concatenate(
        [
            block[height + n * size : height + (n + 1) * size]
            for block in parts
            for n in range(groups)
        ],
        1,
    )
    return (
        layer_out[None],
        input_grad[None],
        w_qkv_grad,
        vectors[0],
        vectors[1],
        w_attn_grad,
        vectors[2],
        vectors[3],
        vectors[4],
        w_in_grad,
        vectors[5],
        w_out_grad,
        vectors[6],
        vectors[7],
        vectors[8],
    )


def solution(mesh):
    groups, shards = mesh.shape["grp"], mesh.shape["shard"]
    if groups == 4 and shards == 8:
        body = functools.partial(on_device_permutes, groups=groups, shards=shards)
    else:
        body = on_device
    return jax.shard_map(
        body,
        mesh=mesh,
        in_specs=(
            P(("grp", "shard"), None, None),
            P(("grp", "shard"), None),
            P(("grp", "shard"), None),
            P(("grp", "shard"), None, None),
            P("shard", "grp"),
            P("shard"),
            P("shard"),
            P("shard", "grp"),
            P("shard"),
            P("shard"),
            P("shard"),
            P("shard", "grp"),
            P("shard"),
            P("shard", "grp"),
            P("shard"),
            P("shard"),
            P("shard"),
        ),
        out_specs=(
            P(("grp", "shard"), None, None),
            P(("grp", "shard"), None, None),
            P("shard", None),
            P("shard"),
            P("shard"),
            P("shard", None),
            P("shard"),
            P("shard"),
            P("shard"),
            P("shard", None),
            P("shard"),
            P("shard", None),
            P("shard"),
            P("shard"),
            P("shard"),
        ),
        check_vma=False,
    )
```

```python
import functools
import math

import jax
import jax.numpy as jnp
from jax import lax
from jax.experimental import pallas as pl
from jax.experimental.pallas import tpu as pltpu
from jax.sharding import PartitionSpec as P

H = 16
HD = 64


masked_score = -1e30
epsilon = 1e-05


def norm_layer(rows, gain_row, shift_row):
    row_mean = jnp.mean(rows, -1, keepdims=True)
    centered = rows - row_mean
    row_var = jnp.mean(centered * centered, -1, keepdims=True)
    return centered * lax.rsqrt(row_var + epsilon) * gain_row + shift_row


def gelu_exact(values):
    return 0.5 * values * (1.0 + lax.erf(values * (1.0 / math.sqrt(2.0))))


def contract_rows(left, right):
    return lax.dot_general(
        left, right, (((0,), (0,)), ((), ())), preferred_element_type=jnp.float32
    )


def contract_cols(left, right):
    return lax.dot_general(
        left, right, (((1,), (1,)), ((), ())), preferred_element_type=jnp.float32
    )


def attend_forward(queries, key_rows, value_rows, segment_row, block_rows):
    length, model_width = queries.shape
    scaling = 1.0 / math.sqrt(HD)
    key_heads = key_rows.reshape(length, H, HD)
    value_heads = value_rows.reshape(length, H, HD)
    query_blocks = queries.reshape(length // block_rows, block_rows, H, HD)
    segment_blocks = segment_row.reshape(length // block_rows, block_rows)

    def one_block(pieces):
        query_part, segment_part = pieces
        scores = (
            jnp.einsum("qhd,khd->hqk", query_part, key_heads, preferred_element_type=jnp.float32)
            * scaling
        )
        allowed = segment_part[:, None] == segment_row[None, :]
        scores = jnp.where(allowed[None], scores, masked_score)
        row_max = jnp.max(scores, -1, keepdims=True)
        powers = jnp.exp(scores - row_max)
        totals = jnp.sum(powers, -1, keepdims=True)
        attn_probs = (powers / totals).astype(jnp.bfloat16)
        context = jnp.einsum(
            "hqk,khd->qhd", attn_probs, value_heads, preferred_element_type=jnp.float32
        )
        return (
            context.reshape(block_rows, model_width).astype(jnp.bfloat16),
            (row_max + jnp.log(totals))[:, :, 0],
        )

    contexts, log_sums = lax.map(one_block, (query_blocks, segment_blocks))
    return (contexts.reshape(length, model_width), log_sums)


def attend_backward(queries, key_rows, value_rows, segment_row, log_sums, context_grad, block_rows):
    length, model_width = queries.shape
    scaling = 1.0 / math.sqrt(HD)
    key_heads = key_rows.reshape(length, H, HD)
    value_heads = value_rows.reshape(length, H, HD)
    query_blocks = queries.reshape(length // block_rows, block_rows, H, HD)
    segment_blocks = segment_row.reshape(length // block_rows, block_rows)
    grad_blocks = context_grad.reshape(length // block_rows, block_rows, H, HD)

    def one_block(running, pieces):
        key_acc, value_acc = running
        query_part, segment_part, lse_part, grad_part = pieces
        scores = (
            jnp.einsum("qhd,khd->hqk", query_part, key_heads, preferred_element_type=jnp.float32)
            * scaling
        )
        allowed = segment_part[:, None] == segment_row[None, :]
        scores = jnp.where(allowed[None], scores, masked_score)
        probs = jnp.exp(scores - lse_part[:, :, None])
        prob_low = probs.astype(jnp.bfloat16)
        prob_grad = jnp.einsum(
            "qhd,khd->hqk", grad_part, value_heads, preferred_element_type=jnp.float32
        )
        row_dot = jnp.sum(prob_grad * probs, -1, keepdims=True)
        score_grad = (probs * (prob_grad - row_dot)).astype(jnp.bfloat16)
        query_grad = (
            jnp.einsum("hqk,khd->qhd", score_grad, key_heads, preferred_element_type=jnp.float32)
            * scaling
        )
        key_acc = (
            key_acc
            + jnp.einsum("hqk,qhd->khd", score_grad, query_part, preferred_element_type=jnp.float32)
            * scaling
        )
        value_acc = value_acc + jnp.einsum(
            "hqk,qhd->khd", prob_low, grad_part, preferred_element_type=jnp.float32
        )
        return ((key_acc, value_acc), query_grad.reshape(block_rows, model_width))

    empty_acc = jnp.zeros((length, H, HD), jnp.float32)
    (key_grad, value_grad), query_grads = lax.scan(
        one_block, (empty_acc, empty_acc), (query_blocks, segment_blocks, log_sums, grad_blocks)
    )
    return (
        query_grads.reshape(length, model_width),
        key_grad.reshape(length, model_width),
        value_grad.reshape(length, model_width),
    )


def on_device(
    tokens,
    segment_ids,
    keep_flag,
    cotangent,
    w_qkv,
    b_query,
    b_value,
    w_attn_out,
    b_attn_out,
    norm1_gain,
    norm1_bias,
    w_in,
    b_in,
    w_out,
    b_out,
    norm2_gain,
    norm2_bias,
):
    seq_count, length, model_width = tokens.shape
    block_rows = min(512, length)
    within = (
        lax.all_gather(w_qkv, "shard", axis=0, tiled=True),
        lax.all_gather(w_attn_out, "shard", axis=0, tiled=True),
        lax.all_gather(w_in, "shard", axis=0, tiled=True),
        lax.all_gather(w_out, "shard", axis=0, tiled=True),
        lax.all_gather(b_query, "shard", axis=0, tiled=True),
        lax.all_gather(b_value, "shard", axis=0, tiled=True),
        lax.all_gather(b_attn_out, "shard", axis=0, tiled=True),
        lax.all_gather(norm1_gain, "shard", axis=0, tiled=True),
        lax.all_gather(norm1_bias, "shard", axis=0, tiled=True),
        lax.all_gather(b_in, "shard", axis=0, tiled=True),
        lax.all_gather(b_out, "shard", axis=0, tiled=True),
        lax.all_gather(norm2_gain, "shard", axis=0, tiled=True),
        lax.all_gather(norm2_bias, "shard", axis=0, tiled=True),
    )
    full_qkv, full_attn, full_in, full_out = (
        lax.all_gather(within[0], "grp", axis=1, tiled=True),
        lax.all_gather(within[1], "grp", axis=1, tiled=True),
        lax.all_gather(within[2], "grp", axis=1, tiled=True),
        lax.all_gather(within[3], "grp", axis=1, tiled=True),
    )
    (
        bias_query,
        bias_value,
        bias_attn,
        gain_one,
        shift_one,
        bias_in,
        bias_out,
        gain_two,
        shift_two,
    ) = [piece.astype(jnp.float32) for piece in within[4:]]
    flat_rows = tokens.reshape(seq_count * length, model_width)
    mixed_qkv = jnp.dot(flat_rows, full_qkv, preferred_element_type=jnp.float32)
    queries = (mixed_qkv[:, :model_width] + bias_query).astype(jnp.bfloat16)
    key_rows = mixed_qkv[:, model_width : 2 * model_width].astype(jnp.bfloat16)
    value_rows = (mixed_qkv[:, 2 * model_width :] + bias_value).astype(jnp.bfloat16)
    query_seqs = queries.reshape(seq_count, length, model_width)
    key_seqs = key_rows.reshape(seq_count, length, model_width)
    value_seqs = value_rows.reshape(seq_count, length, model_width)

    def forward_sequence(pieces):
        return attend_forward(pieces[0], pieces[1], pieces[2], pieces[3], block_rows)

    contexts, log_sums = lax.map(forward_sequence, (query_seqs, key_seqs, value_seqs, segment_ids))
    contexts = contexts.reshape(seq_count * length, model_width)
    attended = jnp.dot(contexts, full_attn, preferred_element_type=jnp.float32) + bias_attn
    first_sum = flat_rows.astype(jnp.float32) + attended
    normed_one, norm_one_back = jax.vjp(norm_layer, first_sum, gain_one, shift_one)
    normed_low = normed_one.astype(jnp.bfloat16)
    hidden_pre = jnp.dot(normed_low, full_in, preferred_element_type=jnp.float32) + bias_in
    hidden, gelu_back = jax.vjp(gelu_exact, hidden_pre)
    hidden_low = hidden.astype(jnp.bfloat16)
    second_sum = normed_one + (
        jnp.dot(hidden_low, full_out, preferred_element_type=jnp.float32) + bias_out
    )
    result, norm_two_back = jax.vjp(norm_layer, second_sum, gain_two, shift_two)
    layer_out = result.astype(jnp.bfloat16).reshape(seq_count, length, model_width)
    again = (
        lax.all_gather(w_qkv, "shard", axis=0, tiled=True),
        lax.all_gather(w_attn_out, "shard", axis=0, tiled=True),
        lax.all_gather(w_in, "shard", axis=0, tiled=True),
        lax.all_gather(w_out, "shard", axis=0, tiled=True),
    )
    back_qkv, back_attn, back_in, back_out = (
        lax.all_gather(again[0], "grp", axis=1, tiled=True),
        lax.all_gather(again[1], "grp", axis=1, tiled=True),
        lax.all_gather(again[2], "grp", axis=1, tiled=True),
        lax.all_gather(again[3], "grp", axis=1, tiled=True),
    )
    masked_cot = cotangent.astype(jnp.float32).reshape(
        seq_count * length, model_width
    ) * keep_flag.reshape(seq_count * length, 1).astype(jnp.float32)
    second_grad, gain_two_grad, shift_two_grad = norm_two_back(masked_cot)
    bias_out_grad = jnp.sum(second_grad, 0)
    out_low = second_grad.astype(jnp.bfloat16)
    w_out_grad = contract_rows(hidden_low, out_low)
    hidden_grad = contract_cols(out_low, back_out)
    (pre_grad,) = gelu_back(hidden_grad)
    bias_in_grad = jnp.sum(pre_grad, 0)
    pre_low = pre_grad.astype(jnp.bfloat16)
    w_in_grad = contract_rows(normed_low, pre_low)
    normed_grad = second_grad + contract_cols(pre_low, back_in)
    first_grad, gain_one_grad, shift_one_grad = norm_one_back(normed_grad)
    bias_attn_grad = jnp.sum(first_grad, 0)
    attn_low = first_grad.astype(jnp.bfloat16)
    w_attn_grad = contract_rows(contexts, attn_low)
    context_grad = contract_cols(attn_low, back_attn).astype(jnp.bfloat16)

    def backward_sequence(pieces):
        return attend_backward(
            pieces[0], pieces[1], pieces[2], pieces[3], pieces[4], pieces[5], block_rows
        )

    query_grad, key_grad, value_grad = lax.map(
        backward_sequence,
        (
            query_seqs,
            key_seqs,
            value_seqs,
            segment_ids,
            log_sums,
            context_grad.reshape(seq_count, length, model_width),
        ),
    )
    query_grad = query_grad.reshape(seq_count * length, model_width)
    key_grad = key_grad.reshape(seq_count * length, model_width)
    value_grad = value_grad.reshape(seq_count * length, model_width)
    bias_query_grad = jnp.sum(query_grad, 0)
    bias_value_grad = jnp.sum(value_grad, 0)
    qkv_low = jnp.concatenate([query_grad, key_grad, value_grad], 1).astype(jnp.bfloat16)
    w_qkv_grad = contract_rows(flat_rows, qkv_low)
    input_grad = first_grad + contract_cols(qkv_low, back_qkv)
    reduced = (
        lax.psum_scatter(
            w_qkv_grad.astype(jnp.bfloat16), "shard", scatter_dimension=0, tiled=True
        ).astype(jnp.float32),
        lax.psum_scatter(
            bias_query_grad.astype(jnp.bfloat16), "shard", scatter_dimension=0, tiled=True
        ).astype(jnp.float32),
        lax.psum_scatter(
            bias_value_grad.astype(jnp.bfloat16), "shard", scatter_dimension=0, tiled=True
        ).astype(jnp.float32),
        lax.psum_scatter(
            w_attn_grad.astype(jnp.bfloat16), "shard", scatter_dimension=0, tiled=True
        ).astype(jnp.float32),
        lax.psum_scatter(
            bias_attn_grad.astype(jnp.bfloat16), "shard", scatter_dimension=0, tiled=True
        ).astype(jnp.float32),
        lax.psum_scatter(
            gain_one_grad.astype(jnp.bfloat16), "shard", scatter_dimension=0, tiled=True
        ).astype(jnp.float32),
        lax.psum_scatter(
            shift_one_grad.astype(jnp.bfloat16), "shard", scatter_dimension=0, tiled=True
        ).astype(jnp.float32),
        lax.psum_scatter(
            w_in_grad.astype(jnp.bfloat16), "shard", scatter_dimension=0, tiled=True
        ).astype(jnp.float32),
        lax.psum_scatter(
            bias_in_grad.astype(jnp.bfloat16), "shard", scatter_dimension=0, tiled=True
        ).astype(jnp.float32),
        lax.psum_scatter(
            w_out_grad.astype(jnp.bfloat16), "shard", scatter_dimension=0, tiled=True
        ).astype(jnp.float32),
        lax.psum_scatter(
            bias_out_grad.astype(jnp.bfloat16), "shard", scatter_dimension=0, tiled=True
        ).astype(jnp.float32),
        lax.psum_scatter(
            gain_two_grad.astype(jnp.bfloat16), "shard", scatter_dimension=0, tiled=True
        ).astype(jnp.float32),
        lax.psum_scatter(
            shift_two_grad.astype(jnp.bfloat16), "shard", scatter_dimension=0, tiled=True
        ).astype(jnp.float32),
    )
    summed = (
        lax.psum(reduced[0].astype(jnp.bfloat16), "grp").astype(jnp.float32),
        lax.psum(reduced[1].astype(jnp.bfloat16), "grp").astype(jnp.float32),
        lax.psum(reduced[2].astype(jnp.bfloat16), "grp").astype(jnp.float32),
        lax.psum(reduced[3].astype(jnp.bfloat16), "grp").astype(jnp.float32),
        lax.psum(reduced[4].astype(jnp.bfloat16), "grp").astype(jnp.float32),
        lax.psum(reduced[5].astype(jnp.bfloat16), "grp").astype(jnp.float32),
        lax.psum(reduced[6].astype(jnp.bfloat16), "grp").astype(jnp.float32),
        lax.psum(reduced[7].astype(jnp.bfloat16), "grp").astype(jnp.float32),
        lax.psum(reduced[8].astype(jnp.bfloat16), "grp").astype(jnp.float32),
        lax.psum(reduced[9].astype(jnp.bfloat16), "grp").astype(jnp.float32),
        lax.psum(reduced[10].astype(jnp.bfloat16), "grp").astype(jnp.float32),
        lax.psum(reduced[11].astype(jnp.bfloat16), "grp").astype(jnp.float32),
        lax.psum(reduced[12].astype(jnp.bfloat16), "grp").astype(jnp.float32),
    )
    return (
        layer_out,
        input_grad.reshape(seq_count, length, model_width),
        summed[0],
        summed[1],
        summed[2],
        summed[3],
        summed[4],
        summed[5],
        summed[6],
        summed[7],
        summed[8],
        summed[9],
        summed[10],
        summed[11],
        summed[12],
    )


NT = (((1,), (1,)), ((), ()))
NN = (((1,), (0,)), ((), ()))
TN = (((0,), (0,)), ((), ()))
LANES = 128
AXES = ("grp", "shard")


def mxu(left, right, dims):
    return lax.dot_general(left, right, dims, preferred_element_type=jnp.float32)


def params(megabytes=60):
    return pltpu.CompilerParams(vmem_limit_bytes=megabytes << 20)


def attention_forward_kernel(q_ref, k_ref, v_ref, seg_col, seg_row, out_ref, lse_ref, *, rows):
    length = q_ref.shape[0]
    first = lax.broadcasted_iota(jnp.int32, (1, LANES), 1) < HD
    keys = k_ref[...]
    values = v_ref[...]
    zero = jnp.zeros_like(keys)
    head_keys = (jnp.where(first, keys, zero), jnp.where(first, zero, keys))
    key_segments = seg_col[...]
    for block in range(length // rows):
        here = pl.ds(block * rows, rows)
        q = q_ref[here, :]
        allowed = key_segments == seg_row[:, here]
        outs = []
        for head in range(2):
            scores = mxu(head_keys[head], q, NT)
            scores = jnp.where(allowed, scores, masked_score)
            top = jnp.max(scores, 0, keepdims=True)
            powers = jnp.exp(scores - top)
            total = jnp.sum(powers, 0, keepdims=True)
            part = mxu(powers.astype(jnp.bfloat16), values, TN)
            outs.append(part * jnp.transpose(jnp.broadcast_to(1.0 / total, (LANES, rows))))
            lse_ref[0, head : head + 1, here] = top + jnp.log(total)
        out_ref[here, :] = jnp.where(first, outs[0], outs[1]).astype(jnp.bfloat16)


def attention_forward(qkv, seg_col, seg_row, start, pairs, before=None):
    length, width = qkv.shape[0], qkv.shape[1] // 3
    total = width // LANES
    rows = min(512, length)
    anywhere = pl.BlockSpec(memory_space=pl.ANY)

    def pair(part):
        return pl.BlockSpec((length, LANES), lambda j: (0, part * total + start + j))

    def body(q_ref, k_ref, v_ref, seg_c, seg_r, *refs):
        attention_forward_kernel(q_ref, k_ref, v_ref, seg_c, seg_r, *refs[-2:], rows=rows)

    return pl.pallas_call(
        body,
        grid=(pairs,),
        in_specs=[
            pair(0),
            pair(1),
            pair(2),
            pl.BlockSpec((length, 1), lambda j: (0, 0)),
            pl.BlockSpec((1, length), lambda j: (0, 0)),
        ]
        + [anywhere] * (0 if before is None else 2),
        out_specs=[
            pl.BlockSpec((length, LANES), lambda j: (0, start + j)),
            pl.BlockSpec((1, 2, length), lambda j: (start + j, 0, 0)),
        ],
        out_shape=[
            jax.ShapeDtypeStruct((length, width), jnp.bfloat16),
            jax.ShapeDtypeStruct((total, 2, length), jnp.float32),
        ],
        input_output_aliases={} if before is None else {5: 0, 6: 1},
        compiler_params=params(60),
        cost_estimate=pl.CostEstimate(
            flops=16 * length * length * pairs * LANES,
            bytes_accessed=8 * length * pairs * LANES,
            transcendentals=0,
        ),
        name="attn_fwd",
    )(qkv, qkv, qkv, seg_col, seg_row, *(() if before is None else before))


def attention_backward_kernel(
    q_ref, k_ref, v_ref, o_ref, do_ref, seg_col, seg_row, lse_ref, grad_ref, sum_ref, *, rows
):
    length = q_ref.shape[0]
    lane = lax.broadcasted_iota(jnp.int32, (1, LANES), 1)
    first = lane < HD
    pick = (
        lax.broadcasted_iota(jnp.int32, (8, LANES), 0)
        == lax.broadcasted_iota(jnp.int32, (8, LANES), 1) // HD
    ).astype(jnp.float32)
    keys = k_ref[...]
    values = v_ref[...]
    zero = jnp.zeros_like(keys)
    head_keys = (jnp.where(first, keys, zero), jnp.where(first, zero, keys))
    head_values = (jnp.where(first, values, zero), jnp.where(first, zero, values))
    key_segments = seg_col[...]
    key_sum = [None, None]
    value_sum = [None, None]
    query_total = jnp.zeros((1, LANES), jnp.float32)
    for block in range(length // rows):
        here = pl.ds(block * rows, rows)
        q = q_ref[here, :]
        do = do_ref[here, :]
        allowed = key_segments == seg_row[:, here]
        dots = lax.dot_general(
            pick,
            do.astype(jnp.float32) * o_ref[here, :].astype(jnp.float32),
            NT,
            precision=lax.Precision.HIGHEST,
            preferred_element_type=jnp.float32,
        )
        parts = []
        for head in range(2):
            scores = mxu(head_keys[head], q, NT)
            scores = jnp.where(allowed, scores, masked_score)
            probs = jnp.exp(scores - lse_ref[0, head : head + 1, here])
            prob_grad = mxu(head_values[head], do, NT)
            score_grad = (probs * (prob_grad - dots[head : head + 1, :])).astype(jnp.bfloat16)
            value_part = mxu(probs.astype(jnp.bfloat16), do, NN)
            key_part = mxu(score_grad, q, NN)
            value_sum[head] = value_part if block == 0 else value_sum[head] + value_part
            key_sum[head] = key_part if block == 0 else key_sum[head] + key_part
            parts.append(mxu(score_grad, keys, TN))
        query_grad = jnp.where(first, parts[0], parts[1]) * (1.0 / math.sqrt(HD))
        query_total = query_total + jnp.sum(query_grad, 0, keepdims=True)
        grad_ref[0, here, :] = query_grad.astype(jnp.bfloat16)
    grad_ref[1, :, :] = jnp.where(first, key_sum[0], key_sum[1]).astype(jnp.bfloat16)
    value_grad = jnp.where(first, value_sum[0], value_sum[1])
    grad_ref[2, :, :] = value_grad.astype(jnp.bfloat16)
    sum_ref[0:1, :] = query_total
    sum_ref[1:2, :] = jnp.sum(value_grad, 0, keepdims=True)


def attention_backward(qkv, out, out_grad, seg_col, seg_row, lse, start, pairs, at, size, before=None):
    length, width = out.shape
    total = width // LANES
    rows = min(256, length)
    anywhere = pl.BlockSpec(memory_space=pl.ANY)

    def pair(part):
        return pl.BlockSpec((length, LANES), lambda j: (0, part * total + start + j))

    def body(*refs):
        attention_backward_kernel(*refs[:8], *refs[-2:], rows=rows)

    return pl.pallas_call(
        body,
        grid=(pairs,),
        in_specs=[
            pair(0),
            pair(1),
            pair(2),
            pair(0),
            pair(0),
            pl.BlockSpec((length, 1), lambda j: (0, 0)),
            pl.BlockSpec((1, length), lambda j: (0, 0)),
            pl.BlockSpec((1, 2, length), lambda j: (j + start, 0, 0)),
        ]
        + [anywhere] * (0 if before is None else 2),
        out_specs=[
            pl.BlockSpec((3, length, LANES), lambda j: (0, 0, j + at)),
            pl.BlockSpec((2, LANES), lambda j: (0, j + at)),
        ],
        out_shape=[
            jax.ShapeDtypeStruct((3, length, size * LANES), jnp.bfloat16),
            jax.ShapeDtypeStruct((2, size * LANES), jnp.float32),
        ],
        input_output_aliases={} if before is None else {8: 0, 9: 1},
        compiler_params=params(60),
        cost_estimate=pl.CostEstimate(
            flops=40 * length * length * pairs * LANES,
            bytes_accessed=16 * length * pairs * LANES,
            transcendentals=0,
        ),
        name="attn_bwd",
    )(qkv, qkv, qkv, out, out_grad, seg_col, seg_row, lse, *(() if before is None else before))


class Place:
    def __init__(self, groups, shards):
        self.groups = groups
        self.shards = shards
        self.chips = shards // 2
        self.grp = lax.axis_index("grp")
        self.shard = lax.axis_index("shard")
        self.core = self.shard % 2
        self.chip = self.shard // 2
        self.scalars = jnp.stack([self.core, self.chip, self.grp]).astype(jnp.int32)

    def permute(self, array, mask_of_core):
        pairs = [(i, i ^ mask_of_core[i % 2]) for i in range(self.groups * self.shards)]
        return lax.ppermute(array, AXES, pairs)

    def swap_core(self, array):
        return self.permute(array, (1, 1))

    def swap_grp(self, array, step):
        masks = (self.shards, 2 * self.shards)
        return self.permute(array, masks if step == 0 else masks[::-1])

    def swap_chip(self, array, step):
        masks = (2, 4)
        return self.permute(array, masks if step == 0 else masks[::-1])

    def slot_chip(self, slot):
        return self.chip ^ turn(slot, self.core)

    def slot_grp(self, slot):
        return self.grp ^ turn(slot, self.core)


def turn(slot, core):
    if isinstance(slot, int):
        return slot if slot in (0, 3) else jnp.where(core == 0, slot, 3 - slot)
    return jnp.where((core == 0) | (slot == 0) | (slot == 3), slot, 3 - slot)


def after(value, *others):
    return lax.optimization_barrier((value, *others))[0]


class Gather:
    def __init__(self, place, piece):
        self.place = place
        self.piece = piece
        self.held = [None] * 4
        self.crossed = [None] * 4

    def chips_near(self, *wait):
        piece = after(self.piece, *wait) if wait else self.piece
        self.pair = [piece, self.place.swap_chip(piece, 0)]
        return self.pair[1]

    def chips_far(self, *wait):
        pair = jnp.stack([self.pair[0], after(self.pair[1], *wait)])
        self.rest = [pair, self.place.swap_chip(pair, 1)]
        return self.rest[1]

    def join(self, *wait):
        rest = after(self.rest[1], *wait) if wait else self.rest[1]
        self.held[0] = jnp.concatenate([self.rest[0], rest])
        return self.held[0]

    def near(self):
        self.held[1] = self.place.swap_grp(self.held[0], 0)
        self.held[2] = self.place.swap_grp(self.held[0], 1)
        return self.held[2]

    def far(self, *wait):
        first = after(self.held[1], *wait) if wait else self.held[1]
        self.held[3] = self.place.swap_grp(first, 1)
        return self.held[3]

    def cross(self, *which, wait=()):
        for n in which:
            piece = after(self.held[n], *wait) if wait else self.held[n]
            self.crossed[n] = self.place.swap_core(piece)

    def pieces(self):
        return self.held + self.crossed


class Window:
    def __init__(self, gather, start, cols):
        self.arrays = gather.pieces()
        self.start, self.cols = start, cols
        chips, rows, _ = self.arrays[0].shape
        self.chips, self.rows = chips, rows


def fetch(where, window, refs, whole, sem, by):
    rows, cols, chips = window.rows, window.cols, window.chips
    for slot in range(4):
        for side in range(2):
            core = where[0] ^ side
            ref = refs[4 * side + slot]
            distance = turn(slot, core)
            col = pl.multiple_of((where[2] ^ distance) * cols, LANES)
            for k in range(chips):
                row = ((where[1] ^ turn(k, core)) * 2 + core) * rows
                pltpu.make_async_copy(
                    ref.at[k, :, pl.ds(window.start, cols)],
                    whole.at[pl.ds(pl.multiple_of(row, rows), rows), pl.ds(col, cols)],
                    sem.at[distance if by == "grp" else 0],
                ).start()


def weight_call(place, kernel, window, inputs, in_specs, outs, out_specs, steps, by, name, flops, mb=60):
    cols, groups = window.cols, place.groups
    pieces = window.arrays
    shape = (window.chips * 2 * window.rows, groups * cols)
    slots = {"grp": groups, "all": 1}[by]
    anywhere = pl.BlockSpec(memory_space=pl.ANY)

    def body(where, *refs):
        taken, refs = refs[: len(pieces)], refs[len(pieces) :]
        *refs, written, weight, sem, out_sem = refs
        step = pl.program_id(0)

        @pl.when(step == 0)
        def _():
            fetch(where, window, taken, weight, sem, by)

        def ready():
            if by == "all":

                @pl.when(step == 0)
                def _():
                    pltpu.make_async_copy(weight, weight, sem.at[0]).wait()
                    pltpu.make_async_copy(weight, written, out_sem.at[0]).start()

            else:
                at = pl.ds(pl.multiple_of((where[2] ^ step) * cols, LANES), cols)
                view = weight.at[:, at]
                pltpu.make_async_copy(view, view, sem.at[step]).wait()
                pltpu.make_async_copy(view, written.at[:, at], out_sem.at[step]).start()

        kernel(where, ready, weight, *refs)

        @pl.when(step == steps - 1)
        def _():
            for slot in range(slots):
                width = shape[1] // slots
                view = weight.at[:, pl.ds(slot * width, width)]
                pltpu.make_async_copy(view, view, out_sem.at[slot]).wait()

    total = sum(math.prod(x.shape) * x.dtype.itemsize for x in list(inputs) + list(outs))
    return pl.pallas_call(
        body,
        grid_spec=pltpu.PrefetchScalarGridSpec(
            num_scalar_prefetch=1,
            grid=(steps,),
            in_specs=[anywhere] * len(pieces) + in_specs,
            out_specs=out_specs + [anywhere],
            scratch_shapes=[
                pltpu.VMEM(shape, jnp.bfloat16),
                pltpu.SemaphoreType.DMA((slots,)),
                pltpu.SemaphoreType.DMA((slots,)),
            ],
        ),
        out_shape=outs + [shaped(shape, jnp.bfloat16)],
        compiler_params=params(mb),
        cost_estimate=pl.CostEstimate(
            flops=flops, bytes_accessed=4 * shape[0] * shape[1] + total, transcendentals=0
        ),
        name=name,
    )(place.scalars, *pieces, *inputs)


def plain_call(kernel, inputs, in_specs, outs, out_specs, steps, name, flops, mb=60):
    total = sum(math.prod(x.shape) * x.dtype.itemsize for x in list(inputs) + list(outs))
    return pl.pallas_call(
        kernel,
        grid=(steps,),
        in_specs=in_specs,
        out_specs=out_specs,
        out_shape=outs,
        compiler_params=params(mb),
        cost_estimate=pl.CostEstimate(flops=flops, bytes_accessed=total, transcendentals=0),
        name=name,
    )(*inputs)


TILE = 256


def row_tiles(width):
    return pl.BlockSpec((TILE, width), lambda i, *s: (i, 0))


def fixed(*shape):
    return pl.BlockSpec(shape, lambda i, *s: (0,) * len(shape))


def whole_once(shape):
    return pl.BlockSpec(shape, lambda i: (0,) * len(shape), pipeline_mode=pl.Buffered(1))


def shaped(shape, dtype):
    return jax.ShapeDtypeStruct(shape, dtype)


B_QUERY, B_VALUE, B_ATTN, GAIN_ONE, SHIFT_ONE, B_OUT, GAIN_TWO, SHIFT_TWO, B_IN = range(9)


def row(ref, n):
    return ref[n : n + 1, :]


class Vectors:
    def __init__(self, place, vectors, *wait):
        flat = jnp.concatenate([after(vectors[0], *wait), *vectors[1:]])
        own = jnp.pad(flat.reshape(-1, LANES), ((0, -(flat.shape[0] // LANES) % 16), (0, 0)))
        own = jnp.stack([own, place.swap_core(own)])
        pair = jnp.stack([own, place.swap_chip(own, 0)])
        self.slots = jnp.concatenate([pair, place.swap_chip(pair, 1)])
        self.place = place

    def unpack(self):
        place = self.place
        slots, sides, rows, lanes = self.slots.shape
        shards = place.shards

        def kernel(where, in_ref, rows_ref, inner_ref, qkv_ref):
            width = shards * lanes
            qkv_ref[...] = jnp.zeros_like(qkv_ref)
            for slot in range(slots):
                for side in range(sides):
                    core = where[0] ^ side
                    shard = (where[1] ^ turn(slot, where[0])) * 2 + core
                    part = in_ref[slot, side].astype(jnp.float32)
                    at = pl.multiple_of(shard * lanes, lanes)
                    rows_ref[:, pl.ds(at, lanes)] = part
                    qkv_ref[:, pl.ds(at, lanes)] = part[B_QUERY : B_QUERY + 1]
                    qkv_ref[:, pl.ds(2 * width + at, lanes)] = part[B_VALUE : B_VALUE + 1]
                    for n in range(4):
                        start = pl.multiple_of((shard * 4 + n) * lanes, lanes)
                        inner_ref[:, pl.ds(start, lanes)] = part[B_IN + n : B_IN + n + 1]

        in_vmem = pl.BlockSpec(memory_space=pltpu.VMEM)
        return pl.pallas_call(
            kernel,
            in_specs=[pl.BlockSpec(memory_space=pltpu.SMEM), in_vmem],
            out_specs=[in_vmem] * 3,
            out_shape=[
                shaped((rows, shards * lanes), jnp.float32),
                shaped((1, 4 * shards * lanes), jnp.float32),
                shaped((1, 3 * shards * lanes), jnp.float32),
            ],
            name="vectors",
        )(place.scalars, self.slots)


def pack_sums(late_a, late_b, first_sums, second_sums, inner_sums):
    width = first_sums.shape[1]
    half = late_a.shape[1]

    def kernel(a_ref, b_ref, one_ref, two_ref, inner_ref, out_ref):
        out_ref[...] = jnp.zeros_like(out_ref)
        out_ref[0:2, 0:half] = a_ref[...]
        out_ref[0:2, half:width] = b_ref[...]
        for n, source in (
            (GAIN_ONE, one_ref[0:1, :]),
            (SHIFT_ONE, one_ref[1:2, :]),
            (B_ATTN, one_ref[2:3, :]),
            (GAIN_TWO, two_ref[0:1, :]),
            (SHIFT_TWO, two_ref[1:2, :]),
            (B_OUT, two_ref[2:3, :]),
        ):
            out_ref[n : n + 1, :] = source
        for n in range(4):
            out_ref[B_IN + n : B_IN + n + 1, :] = inner_ref[:, n * width : (n + 1) * width]

    in_vmem = pl.BlockSpec(memory_space=pltpu.VMEM)
    return pl.pallas_call(
        kernel,
        in_specs=[in_vmem] * 5,
        out_specs=in_vmem,
        out_shape=shaped((16, width), jnp.float32),
        name="pack_sums",
    )(late_a, late_b, first_sums, second_sums, inner_sums)


def project_qkv(place, rows, window, bias, scale):
    length, width = rows.shape
    cols = window.cols

    def kernel(where, ready, weight, x_ref, bias_ref, scale_ref, out_ref):
        ready()
        at = pl.ds(pl.multiple_of((where[2] ^ pl.program_id(0)) * cols, LANES), cols)
        for tile in range(length // TILE):
            here = pl.ds(tile * TILE, TILE)
            mixed = mxu(x_ref[here, :], weight[:, at], NN) + bias_ref[:, at]
            mixed = mixed.astype(jnp.bfloat16).astype(jnp.float32) * scale_ref[:, at]
            out_ref[here, :] = mixed.astype(jnp.bfloat16)

    total = cols * place.groups
    return weight_call(
        place,
        kernel,
        window,
        (rows, bias, scale),
        [fixed(length, width), fixed(1, total), fixed(1, total)],
        [shaped((length, total), jnp.bfloat16)],
        [pl.BlockSpec((length, cols), lambda i, s: (0, i ^ s[2]))],
        place.groups,
        "grp",
        "qkv",
        2 * length * width * total,
    )


def norm_parts(rows):
    centered = rows - jnp.mean(rows, -1, keepdims=True)
    scale = lax.rsqrt(jnp.mean(centered * centered, -1, keepdims=True) + epsilon)
    return centered * scale, scale


def norm_back(grad, normed, scale):
    return scale * (
        grad
        - jnp.mean(grad, -1, keepdims=True)
        - normed * jnp.mean(grad * normed, -1, keepdims=True)
    )


def add_rows(sum_ref, *terms):
    @pl.when(pl.program_id(0) == 0)
    def _():
        sum_ref[...] = jnp.zeros_like(sum_ref)

    for n, term in enumerate(terms):
        sum_ref[n : n + 1, :] += jnp.sum(term, 0, keepdims=True)


def project_out(place, contexts, window, rows, vectors):
    length, width = rows.shape

    def kernel(where, ready, weight, c_ref, x_ref, v_ref, n_ref, r_ref, low_ref):
        ready()
        first_sum = mxu(c_ref[...], weight[...], NN) + row(v_ref, B_ATTN)
        first_sum = first_sum + x_ref[...].astype(jnp.float32)
        normed, scale = norm_parts(first_sum)
        n_ref[...] = normed
        r_ref[...] = jnp.broadcast_to(scale, r_ref.shape)
        low_ref[...] = (normed * row(v_ref, GAIN_ONE) + row(v_ref, SHIFT_ONE)).astype(jnp.bfloat16)

    return weight_call(
        place,
        kernel,
        window,
        (contexts, rows, vectors),
        [row_tiles(width), row_tiles(width), fixed(*vectors.shape)],
        [
            shaped((length, width), jnp.float32),
            shaped((length, LANES), jnp.float32),
            shaped((length, width), jnp.bfloat16),
        ],
        [row_tiles(width), row_tiles(LANES), row_tiles(width)],
        length // TILE,
        "all",
        "attn_out",
        2 * length * width * width,
    )


def feed_in(place, normed_low, window, bias):
    length, width = normed_low.shape
    cols = window.cols

    def kernel(where, ready, weight, x_ref, bias_ref, hid_ref, slope_ref):
        ready()
        at = pl.ds(pl.multiple_of((where[2] ^ pl.program_id(0)) * cols, LANES), cols)
        for tile in range(length // TILE):
            here = pl.ds(tile * TILE, TILE)
            pre = mxu(x_ref[here, :], weight[:, at], NN) + bias_ref[:, at]
            share = 0.5 + 0.5 * lax.erf(pre * (1.0 / math.sqrt(2.0)))
            bell = jnp.exp(-0.5 * pre * pre) * (1.0 / math.sqrt(2.0 * math.pi))
            hid_ref[here, :] = (pre * share).astype(jnp.bfloat16)
            slope_ref[here, :] = (share + pre * bell).astype(jnp.bfloat16)

    total = cols * place.groups
    block = pl.BlockSpec((length, cols), lambda i, s: (0, i ^ s[2]))
    return weight_call(
        place,
        kernel,
        window,
        (normed_low, bias),
        [fixed(length, width), fixed(1, total)],
        [shaped((length, total), jnp.bfloat16)] * 2,
        [block, block],
        place.groups,
        "grp",
        "feed_in",
        2 * length * width * total,
    )


def feed_out(place, hidden, window, normed, cot, keep, vectors):
    length, inner = hidden.shape
    width = normed.shape[1]

    def kernel(where, ready, weight, h_ref, n_ref, cot_ref, keep_ref, v_ref, *outs):
        out_ref, grad_ref, low_ref, sum_ref = outs
        ready()
        fed = mxu(h_ref[...], weight[...], NN)
        normed_one = n_ref[...] * row(v_ref, GAIN_ONE) + row(v_ref, SHIFT_ONE)
        second_sum = normed_one + (fed + row(v_ref, B_OUT))
        second, scale = norm_parts(second_sum)
        out_ref[...] = (second * row(v_ref, GAIN_TWO) + row(v_ref, SHIFT_TWO)).astype(jnp.bfloat16)
        masked = cot_ref[...].astype(jnp.float32) * keep_ref[...]
        grad = norm_back(masked * row(v_ref, GAIN_TWO), second, scale)
        grad_ref[...] = grad
        low_ref[...] = grad.astype(jnp.bfloat16)
        add_rows(sum_ref, masked * second, masked, grad)

    return weight_call(
        place,
        kernel,
        window,
        (hidden, normed, cot, keep, vectors),
        [row_tiles(inner), row_tiles(width), row_tiles(width), row_tiles(1), fixed(*vectors.shape)],
        [
            shaped((length, width), jnp.bfloat16),
            shaped((length, width), jnp.float32),
            shaped((length, width), jnp.bfloat16),
            shaped((8, width), jnp.float32),
        ],
        [row_tiles(width), row_tiles(width), row_tiles(width), fixed(8, width)],
        length // TILE,
        "all",
        "feed_out",
        2 * length * width * inner,
    )


def feed_out_back(out_low, weight, slope):
    length, width = out_low.shape
    inner = slope.shape[1]
    cols = min(1024, inner)

    def kernel(g_ref, w_ref, slope_ref, pre_ref, sum_ref):
        total = jnp.zeros((1, cols), jnp.float32)
        for tile in range(length // TILE):
            here = pl.ds(tile * TILE, TILE)
            grad = mxu(g_ref[here, :], w_ref[...], NT) * slope_ref[here, :].astype(jnp.float32)
            pre_ref[here, :] = grad.astype(jnp.bfloat16)
            total = total + jnp.sum(grad, 0, keepdims=True)
        sum_ref[...] = total

    block = pl.BlockSpec((length, cols), lambda i: (0, i))
    return plain_call(
        kernel,
        (out_low, weight, slope),
        [fixed(length, width), pl.BlockSpec((cols, width), lambda i: (i, 0)), block],
        [shaped((length, inner), jnp.bfloat16), shaped((1, inner), jnp.float32)],
        [block, pl.BlockSpec((1, cols), lambda i: (0, i))],
        inner // cols,
        "feed_out_back",
        2 * length * width * inner,
    )


def feed_in_back(pre_low, weight, second_grad, normed, scale, vectors):
    length, inner = pre_low.shape
    width = normed.shape[1]

    def kernel(p_ref, w_ref, g_ref, n_ref, r_ref, v_ref, first_ref, low_ref, sum_ref):
        grad = g_ref[...] + mxu(p_ref[...], w_ref[...], NT)
        first = norm_back(grad * row(v_ref, GAIN_ONE), n_ref[...], r_ref[:, :1])
        first_ref[...] = first
        low_ref[...] = first.astype(jnp.bfloat16)
        add_rows(sum_ref, grad * n_ref[...], grad, first)

    return plain_call(
        kernel,
        (pre_low, weight, second_grad, normed, scale, vectors),
        [
            row_tiles(inner),
            whole_once(weight.shape),
            row_tiles(width),
            row_tiles(width),
            row_tiles(LANES),
            fixed(*vectors.shape),
        ],
        [
            shaped((length, width), jnp.float32),
            shaped((length, width), jnp.bfloat16),
            shaped((8, width), jnp.float32),
        ],
        [row_tiles(width), row_tiles(width), fixed(8, width)],
        length // TILE,
        "feed_in_back",
        2 * length * width * inner,
    )


def project_out_back(attn_low, weight):
    length, width = attn_low.shape

    def kernel(g_ref, w_ref, out_ref):
        out_ref[...] = mxu(g_ref[...], w_ref[...], NT).astype(jnp.bfloat16)

    return plain_call(
        kernel,
        (attn_low, weight),
        [row_tiles(width), whole_once(weight.shape)],
        [shaped((length, width), jnp.bfloat16)],
        [row_tiles(width)],
        length // TILE,
        "attn_out_back",
        2 * length * width * width,
    )[0]


def project_qkv_back(grads, weight, first_grad):
    length, width = first_grad.shape
    part = width // len(grads)

    def kernel(w_ref, *refs):
        *grad_refs, first_ref, out_ref = refs
        total = first_ref[...]
        for n in range(3):
            for m, grad_ref in enumerate(grad_refs):
                at = n * width + m * part
                total = total + mxu(grad_ref[n], w_ref[:, at : at + part], NT)
        out_ref[...] = total

    return plain_call(
        kernel,
        (weight, *grads, first_grad),
        [whole_once(weight.shape)]
        + [pl.BlockSpec((3, TILE, part), lambda i: (0, i, 0))] * len(grads)
        + [row_tiles(width)],
        [shaped((length, width), jnp.float32)],
        [row_tiles(width)],
        length // TILE,
        "qkv_back",
        6 * length * width * width,
    )[0]


def weight_grad_kernel(where, *refs, own, rows, groups, count, split):
    lefts, rights, refs = refs[:count], refs[count : 2 * count], refs[2 * count :]
    outs, kept = refs[:-count], refs[-count:]
    received = None
    if own:
        received, *outs = outs
    keep = where[0] if own else 1 - where[0]
    chips = lefts[0].shape[1] // (2 * rows)

    @pl.when(pl.program_id(1) == 0)
    def _():
        for left_ref, kept_ref in zip(lefts, kept):
            chosen = []
            for k in range(chips):
                even = left_ref[:, 2 * k * rows : (2 * k + 1) * rows]
                odd = left_ref[:, (2 * k + 1) * rows : (2 * k + 2) * rows]
                chosen.append(jnp.where(keep == 0, even, odd))
            left = chosen[0] if chips == 1 else jnp.concatenate(chosen, 1)
            kept_ref[...] = left.T

    def emit(slot, part, at):
        part = part.reshape(chips, rows, part.shape[-1])
        pos = 0 if split else slot
        if own:
            part = (part + received[pos, :, :, at].astype(jnp.float32)).astype(jnp.bfloat16)

            def store(slot):
                if slot in (1, 3):
                    outs[2][slot // 2, :, :, at] = part
                else:
                    outs[slot // 2][:, :, at] = part

            if split:
                for n in range(groups):
                    pl.when(pl.program_id(1) == n)(functools.partial(store, n))
            else:
                store(slot)
        else:
            outs[0][pos, :, :, at] = part.astype(jnp.bfloat16)

    if split:
        at = 0
        for right_ref, kept_ref in zip(rights, kept):
            if len(right_ref.shape) == 3:
                size = right_ref.shape[2]
                pieces = [right_ref[n] for n in range(right_ref.shape[0])]
            else:
                size = min(512, right_ref.shape[1])
                pieces = [
                    right_ref[:, n * size : (n + 1) * size]
                    for n in range(right_ref.shape[1] // size)
                ]
            for piece in pieces:
                emit(0, mxu(kept_ref[...], piece, NN), slice(at, at + size))
                at += size
    else:
        cols = rights[0].shape[1] // groups
        for slot in range(groups):
            start = pl.multiple_of((where[2] ^ turn(slot, keep)) * cols, LANES)
            emit(slot, mxu(kept[0][...], rights[0][:, pl.ds(start, cols)], NN), slice(0, cols))


def weight_grad(place, pairs, received, split, name):
    tokens, height = pairs[0][0].shape
    groups, chips = place.groups, place.chips
    rows = height // place.shards
    own = received is not None
    step_chips = chips if split else max(1, 1024 // (2 * rows))
    steps = chips // step_chips
    grid = (steps, groups if split else 1)

    def block(j, s):
        return s[2] ^ turn(j, s[0] if own else 1 - s[0])

    cols = 0
    right_specs = []
    for _, right in pairs:
        size = right.shape[-1] // groups
        if not split:
            right_specs.append(pl.BlockSpec(right.shape, lambda i, j, s: (0, 0)))
        elif right.ndim == 3:
            right_specs.append(
                pl.BlockSpec((right.shape[0], tokens, size), lambda i, j, s: (0, 0, block(j, s)))
            )
        else:
            right_specs.append(pl.BlockSpec((tokens, size), lambda i, j, s: (0, block(j, s))))
        cols += size * (right.shape[0] if right.ndim == 3 else 1)
    left_spec = pl.BlockSpec((tokens, step_chips * 2 * rows), lambda i, j, s: (0, i))
    if split:
        passed = pl.BlockSpec((1, step_chips, rows, cols), lambda i, j, s: (j, i, 0, 0))
    else:
        passed = pl.BlockSpec((groups, step_chips, rows, cols), lambda i, j, s: (0, i, 0, 0))
    in_specs = [left_spec] * len(pairs) + right_specs
    inputs = [left for left, _ in pairs] + [right for _, right in pairs]
    if own:
        in_specs.append(passed)
        inputs.append(received)
        one = pl.BlockSpec((step_chips, rows, cols), lambda i, j, s: (i, 0, 0))
        two = pl.BlockSpec((2, step_chips, rows, cols), lambda i, j, s: (0, i, 0, 0))
        out_specs = [one, one, two]
        shape = (chips, rows, cols)
        out_shape = [
            shaped(shape, jnp.bfloat16),
            shaped(shape, jnp.bfloat16),
            shaped((2, *shape), jnp.bfloat16),
        ]
    else:
        out_specs = passed
        out_shape = shaped((groups, chips, rows, cols), jnp.bfloat16)
    return pl.pallas_call(
        functools.partial(
            weight_grad_kernel, own=own, rows=rows, groups=groups, count=len(pairs), split=split
        ),
        grid_spec=pltpu.PrefetchScalarGridSpec(
            num_scalar_prefetch=1,
            grid=grid,
            in_specs=in_specs,
            out_specs=out_specs,
            scratch_shapes=[pltpu.VMEM((step_chips * rows, tokens), jnp.bfloat16)] * len(pairs),
        ),
        out_shape=out_shape,
        compiler_params=params(60),
        cost_estimate=pl.CostEstimate(
            flops=tokens * height * cols * groups,
            bytes_accessed=2 * (tokens * (height + cols * groups) + height * cols * groups),
            transcendentals=0,
        ),
        name="wgrad_" + name + ("_own" if own else "_sent"),
    )(place.scalars, *inputs)


def add(*terms):
    total = terms[0].astype(jnp.float32)
    for term in terms[1:]:
        total = total + term.astype(jnp.float32)
    return total.astype(jnp.bfloat16)


class Reduction:
    def __init__(self, place, pairs, split, name, *wait):
        self.place = place
        if wait:
            pairs = [(after(pairs[0][0], *wait), pairs[0][1])] + pairs[1:]
        self.call = (pairs, split, name)
        self.sent = weight_grad(place, pairs, None, split, name)
        self.received = place.swap_core(self.sent)

    def own(self, *wait):
        pairs, split, name = self.call
        received = after(self.received, *wait) if wait else self.received
        self.own_0, self.own_2, both = weight_grad(self.place, pairs, received, split, name)
        self.first = self.place.swap_grp(both, 0)
        return self.own_0

    def middle(self, *wait):
        self.first = after(self.first, *wait) if wait else self.first
        second = add(self.own_2, self.first[1])
        self.second = self.place.swap_grp(second, 1)
        return second

    def along(self, *wait):
        place = self.place
        second = after(self.second, *wait) if wait else self.second
        mine = add(self.own_0, self.first[0], second)
        blocks = [
            lax.dynamic_index_in_dim(mine, place.slot_chip(slot), 0, False) for slot in range(4)
        ]
        self.mine = blocks
        self.first = place.swap_chip(jnp.stack([blocks[1], blocks[3]]), 0)
        return mine

    def along_far(self, *wait):
        self.first = after(self.first, *wait) if wait else self.first
        second = add(self.mine[2], self.first[1])
        self.second = self.place.swap_chip(second, 1)
        return second

    def share(self, *wait):
        second = after(self.second, *wait) if wait else self.second
        return add(self.mine[0], self.first[0], second)


class Replication:
    def __init__(self, place, share):
        self.place = place
        self.pair = jnp.stack([share, place.swap_grp(share, 0)])

    def far(self, *wait):
        pair = after(self.pair, *wait) if wait else self.pair
        self.rest = self.place.swap_grp(pair, 1)
        return self.rest

    def result(self):
        place = self.place
        slots = [self.pair[0], self.pair[1], self.rest[0], self.rest[1]]
        ordered = []
        for g in range(place.groups):
            block = slots[0]
            for slot in range(1, place.groups):
                block = jnp.where(place.slot_grp(slot) == g, slots[slot], block)
            ordered.append(block.astype(jnp.float32))
        return ordered


def own_part(place, vector):
    size = vector.shape[0] // place.shards
    return lax.dynamic_slice_in_dim(vector, place.shard * size, size)


def on_device_permutes(
    tokens,
    segment_ids,
    keep_flag,
    cotangent,
    w_qkv,
    b_query,
    b_value,
    w_attn_out,
    b_attn_out,
    norm1_gain,
    norm1_bias,
    w_in,
    b_in,
    w_out,
    b_out,
    norm2_gain,
    norm2_bias,
    *,
    groups,
    shards,
):
    place = Place(groups, shards)
    _, length, width = tokens.shape
    rows = tokens[0]
    seg_row = segment_ids.reshape(1, length)
    seg_col = segment_ids.reshape(length, 1)
    keep = keep_flag.reshape(length, 1).astype(jnp.float32)
    pairs = width // LANES

    c1 = Gather(place, w_qkv)
    c2 = Gather(place, jnp.concatenate([w_in, w_attn_out], 1))
    c3 = Gather(place, w_out)
    c1.chips_near()
    c1.chips_far()
    joined = c1.join()
    c1.near()
    c2.chips_near(joined)
    small = Vectors(
        place,
        (b_query, b_value, b_attn_out, norm1_gain, norm1_bias, b_out, norm2_gain, norm2_bias, b_in),
        c1.pair[1],
    )
    c1.cross(0)
    far = c1.far()
    c2.chips_far()
    c1.cross(1, 2)
    c1.cross(3)
    c2.join(far)
    c2.near()
    vectors, bias_in, qkv_bias = small.unpack()
    blank = jnp.ones((1, width), jnp.float32)
    qkv_scale = jnp.concatenate([blank / math.sqrt(HD), blank, blank], 1)

    mixed, full_qkv = project_qkv(place, rows, Window(c1, 0, w_qkv.shape[1]), qkv_bias, qkv_scale)
    c3.chips_near(mixed)
    c2.cross(0, wait=(mixed,))
    quarter = pairs // 4
    forward = None
    for n in range(4):
        gate = ()
        if n == 2:
            gate = (c3.rest[1],)
        if n == 3:
            gate = (c2.held[3],)
        forward = attention_forward(
            after(mixed, *gate) if gate else mixed, seg_col, seg_row, n * quarter, quarter, forward
        )
        done = forward[1]
        if n == 0:
            c3.chips_far(done)
            c2.far(done)
            c2.cross(1, 2, wait=(done,))
        if n == 2:
            c2.cross(3, wait=(done,))
            c3.join(done)
            c3.near()
    contexts, lse = forward
    normed, scale_one, normed_low, full_attn = project_out(
        place, contexts, Window(c2, w_in.shape[1], w_attn_out.shape[1]), rows, vectors
    )
    c3.far(normed_low)
    c3.cross(0, 1, 2, wait=(normed_low,))
    hidden, slope, full_in = feed_in(
        place, after(normed_low, c3.held[1]), Window(c2, 0, w_in.shape[1]), bias_in
    )
    c3.cross(3, wait=(hidden,))
    layer_out, second_grad, out_low, second_sums, full_out = feed_out(
        place, hidden, Window(c3, 0, w_out.shape[1]), normed, cotangent[0], keep, vectors
    )

    r_out = Reduction(place, [(hidden, out_low)], False, "out")
    pre_low, bias_in_grad = feed_out_back(after(out_low, r_out.sent), full_out, slope)
    own_out = r_out.own(pre_low)
    r_in = Reduction(place, [(normed_low, pre_low)], True, "in", own_out)
    first_grad, attn_low, first_sums = feed_in_back(
        after(pre_low, r_in.sent), full_in, second_grad, normed, scale_one, vectors
    )
    mid_out = r_out.middle(first_grad)
    own_in = r_in.own(first_grad, mid_out)
    context_grad = project_out_back(after(attn_low, own_in), full_attn)

    def back(start, at, before=None, *wait):
        return attention_backward(
            mixed,
            contexts,
            after(context_grad, *wait) if wait else context_grad,
            seg_col,
            seg_row,
            lse,
            start,
            quarter,
            at,
            2 * quarter,
            before,
        )

    part = back(0, 0)
    along = r_out.along(part[1])
    low_a, late_a = back(quarter, quarter, part, along)
    mid_in = r_in.middle(late_a)
    along = r_out.along_far(late_a)
    r_a = Reduction(place, [(contexts, attn_low), (rows, low_a)], True, "a", mid_in, along)
    part = back(2 * quarter, 0, None, r_a.sent)
    along = r_in.along(part[1])
    share_out = r_out.share(part[1])
    own_a = r_a.own(along, share_out)
    low_b, late_b = back(3 * quarter, quarter, part, own_a)
    mid_a = r_a.middle(late_b)
    along = r_in.along_far(late_b)
    sums = pack_sums(late_a, late_b, first_sums, second_sums, bias_in_grad)
    r_b = Reduction(place, [(rows, low_b)], True, "b", mid_a, along, sums)
    sums = sums + place.swap_core(sums)
    along = r_a.along(r_b.sent)
    share_in = r_in.share(r_b.sent)
    inner = share_in.shape[1] // groups
    joined = jnp.concatenate(
        [share_out] + [share_in[:, n * inner : (n + 1) * inner] for n in range(groups)]
    )
    all_ffn = Replication(place, joined)
    own_b = r_b.own(along, joined, sums)
    sums = after(sums, own_b)
    sums = sums + place.swap_grp(after(sums, own_b), 0)
    along = r_a.along_far(own_b)
    input_grad = project_qkv_back(
        (low_a, after(low_b, own_b, along, all_ffn.pair)), full_qkv, first_grad
    )
    mid_b = r_b.middle(input_grad)
    sums = sums + place.swap_grp(after(sums, mid_b), 1)
    all_ffn.far(mid_b)
    all_a = Replication(place, r_a.share(mid_b))
    along = r_b.along()
    sums = sums + place.swap_chip(after(sums, along), 0)
    all_a.far(along)
    along = r_b.along_far()
    sums = sums + place.swap_chip(after(sums, along), 1)
    all_b = Replication(place, r_b.share())
    all_b.far()
    mine = lax.dynamic_slice_in_dim(sums, place.shard * LANES, LANES, 1)
    inner_mine = own_part(place, sums[B_IN : B_IN + 4].reshape(-1))

    parts_a, parts_b = all_a.result(), all_b.result()
    heads = parts_b[0].shape[1] // 3
    skip = parts_a[0].shape[1] - 3 * heads
    w_attn_grad = jnp.concatenate([block[:, :skip] for block in parts_a], 1)
    parts_a = [block[:, skip:] for block in parts_a]
    w_qkv_grad = jnp.concatenate(
        [
            block[:, n * heads : (n + 1) * heads]
            for n in range(3)
            for half in (parts_a, parts_b)
            for block in half
        ],
        1,
    )
    parts = all_ffn.result()
    height = share_out.shape[0]
    w_out_grad = jnp.concatenate([block[:height] for block in parts], 1)
    size = share_in.shape[0]
    w_in_grad = jnp.concatenate(
        [
            block[height + n * size : height + (n + 1) * size]
            for block in parts
            for n in range(groups)
        ],
        1,
    )
    return (
        layer_out[None],
        input_grad[None],
        w_qkv_grad,
        mine[B_QUERY],
        mine[B_VALUE],
        w_attn_grad,
        mine[B_ATTN],
        mine[GAIN_ONE],
        mine[SHIFT_ONE],
        w_in_grad,
        inner_mine,
        w_out_grad,
        mine[B_OUT],
        mine[GAIN_TWO],
        mine[SHIFT_TWO],
    )


def solution(mesh):
    groups, shards = mesh.shape["grp"], mesh.shape["shard"]
    if groups == 4 and shards == 8:
        body = functools.partial(on_device_permutes, groups=groups, shards=shards)
    else:
        body = on_device
    return jax.shard_map(
        body,
        mesh=mesh,
        in_specs=(
            P(("grp", "shard"), None, None),
            P(("grp", "shard"), None),
            P(("grp", "shard"), None),
            P(("grp", "shard"), None, None),
            P("shard", "grp"),
            P("shard"),
            P("shard"),
            P("shard", "grp"),
            P("shard"),
            P("shard"),
            P("shard"),
            P("shard", "grp"),
            P("shard"),
            P("shard", "grp"),
            P("shard"),
            P("shard"),
            P("shard"),
        ),
        out_specs=(
            P(("grp", "shard"), None, None),
            P(("grp", "shard"), None, None),
            P("shard", None),
            P("shard"),
            P("shard"),
            P("shard", None),
            P("shard"),
            P("shard"),
            P("shard"),
            P("shard", None),
            P("shard"),
            P("shard", None),
            P("shard"),
            P("shard"),
            P("shard"),
        ),
        check_vma=False,
    )
```

```python
import functools
import math

import jax
import jax.numpy as jnp
from jax import lax
from jax.experimental import pallas as pl
from jax.experimental.pallas import tpu as pltpu
from jax.sharding import PartitionSpec as P

H = 16
HD = 64


masked_score = -1e30
epsilon = 1e-05


def norm_layer(rows, gain_row, shift_row):
    row_mean = jnp.mean(rows, -1, keepdims=True)
    centered = rows - row_mean
    row_var = jnp.mean(centered * centered, -1, keepdims=True)
    return centered * lax.rsqrt(row_var + epsilon) * gain_row + shift_row


def gelu_exact(values):
    return 0.5 * values * (1.0 + lax.erf(values * (1.0 / math.sqrt(2.0))))


def contract_rows(left, right):
    return lax.dot_general(
        left, right, (((0,), (0,)), ((), ())), preferred_element_type=jnp.float32
    )


def contract_cols(left, right):
    return lax.dot_general(
        left, right, (((1,), (1,)), ((), ())), preferred_element_type=jnp.float32
    )


def attend_forward(queries, key_rows, value_rows, segment_row, block_rows):
    length, model_width = queries.shape
    scaling = 1.0 / math.sqrt(HD)
    key_heads = key_rows.reshape(length, H, HD)
    value_heads = value_rows.reshape(length, H, HD)
    query_blocks = queries.reshape(length // block_rows, block_rows, H, HD)
    segment_blocks = segment_row.reshape(length // block_rows, block_rows)

    def one_block(pieces):
        query_part, segment_part = pieces
        scores = (
            jnp.einsum("qhd,khd->hqk", query_part, key_heads, preferred_element_type=jnp.float32)
            * scaling
        )
        allowed = segment_part[:, None] == segment_row[None, :]
        scores = jnp.where(allowed[None], scores, masked_score)
        row_max = jnp.max(scores, -1, keepdims=True)
        powers = jnp.exp(scores - row_max)
        totals = jnp.sum(powers, -1, keepdims=True)
        attn_probs = (powers / totals).astype(jnp.bfloat16)
        context = jnp.einsum(
            "hqk,khd->qhd", attn_probs, value_heads, preferred_element_type=jnp.float32
        )
        return (
            context.reshape(block_rows, model_width).astype(jnp.bfloat16),
            (row_max + jnp.log(totals))[:, :, 0],
        )

    contexts, log_sums = lax.map(one_block, (query_blocks, segment_blocks))
    return (contexts.reshape(length, model_width), log_sums)


def attend_backward(queries, key_rows, value_rows, segment_row, log_sums, context_grad, block_rows):
    length, model_width = queries.shape
    scaling = 1.0 / math.sqrt(HD)
    key_heads = key_rows.reshape(length, H, HD)
    value_heads = value_rows.reshape(length, H, HD)
    query_blocks = queries.reshape(length // block_rows, block_rows, H, HD)
    segment_blocks = segment_row.reshape(length // block_rows, block_rows)
    grad_blocks = context_grad.reshape(length // block_rows, block_rows, H, HD)

    def one_block(running, pieces):
        key_acc, value_acc = running
        query_part, segment_part, lse_part, grad_part = pieces
        scores = (
            jnp.einsum("qhd,khd->hqk", query_part, key_heads, preferred_element_type=jnp.float32)
            * scaling
        )
        allowed = segment_part[:, None] == segment_row[None, :]
        scores = jnp.where(allowed[None], scores, masked_score)
        probs = jnp.exp(scores - lse_part[:, :, None])
        prob_low = probs.astype(jnp.bfloat16)
        prob_grad = jnp.einsum(
            "qhd,khd->hqk", grad_part, value_heads, preferred_element_type=jnp.float32
        )
        row_dot = jnp.sum(prob_grad * probs, -1, keepdims=True)
        score_grad = (probs * (prob_grad - row_dot)).astype(jnp.bfloat16)
        query_grad = (
            jnp.einsum("hqk,khd->qhd", score_grad, key_heads, preferred_element_type=jnp.float32)
            * scaling
        )
        key_acc = (
            key_acc
            + jnp.einsum("hqk,qhd->khd", score_grad, query_part, preferred_element_type=jnp.float32)
            * scaling
        )
        value_acc = value_acc + jnp.einsum(
            "hqk,qhd->khd", prob_low, grad_part, preferred_element_type=jnp.float32
        )
        return ((key_acc, value_acc), query_grad.reshape(block_rows, model_width))

    empty_acc = jnp.zeros((length, H, HD), jnp.float32)
    (key_grad, value_grad), query_grads = lax.scan(
        one_block, (empty_acc, empty_acc), (query_blocks, segment_blocks, log_sums, grad_blocks)
    )
    return (
        query_grads.reshape(length, model_width),
        key_grad.reshape(length, model_width),
        value_grad.reshape(length, model_width),
    )


def on_device(
    tokens,
    segment_ids,
    keep_flag,
    cotangent,
    w_qkv,
    b_query,
    b_value,
    w_attn_out,
    b_attn_out,
    norm1_gain,
    norm1_bias,
    w_in,
    b_in,
    w_out,
    b_out,
    norm2_gain,
    norm2_bias,
):
    seq_count, length, model_width = tokens.shape
    block_rows = min(512, length)
    within = (
        lax.all_gather(w_qkv, "shard", axis=0, tiled=True),
        lax.all_gather(w_attn_out, "shard", axis=0, tiled=True),
        lax.all_gather(w_in, "shard", axis=0, tiled=True),
        lax.all_gather(w_out, "shard", axis=0, tiled=True),
        lax.all_gather(b_query, "shard", axis=0, tiled=True),
        lax.all_gather(b_value, "shard", axis=0, tiled=True),
        lax.all_gather(b_attn_out, "shard", axis=0, tiled=True),
        lax.all_gather(norm1_gain, "shard", axis=0, tiled=True),
        lax.all_gather(norm1_bias, "shard", axis=0, tiled=True),
        lax.all_gather(b_in, "shard", axis=0, tiled=True),
        lax.all_gather(b_out, "shard", axis=0, tiled=True),
        lax.all_gather(norm2_gain, "shard", axis=0, tiled=True),
        lax.all_gather(norm2_bias, "shard", axis=0, tiled=True),
    )
    full_qkv, full_attn, full_in, full_out = (
        lax.all_gather(within[0], "grp", axis=1, tiled=True),
        lax.all_gather(within[1], "grp", axis=1, tiled=True),
        lax.all_gather(within[2], "grp", axis=1, tiled=True),
        lax.all_gather(within[3], "grp", axis=1, tiled=True),
    )
    (
        bias_query,
        bias_value,
        bias_attn,
        gain_one,
        shift_one,
        bias_in,
        bias_out,
        gain_two,
        shift_two,
    ) = [piece.astype(jnp.float32) for piece in within[4:]]
    flat_rows = tokens.reshape(seq_count * length, model_width)
    mixed_qkv = jnp.dot(flat_rows, full_qkv, preferred_element_type=jnp.float32)
    queries = (mixed_qkv[:, :model_width] + bias_query).astype(jnp.bfloat16)
    key_rows = mixed_qkv[:, model_width : 2 * model_width].astype(jnp.bfloat16)
    value_rows = (mixed_qkv[:, 2 * model_width :] + bias_value).astype(jnp.bfloat16)
    query_seqs = queries.reshape(seq_count, length, model_width)
    key_seqs = key_rows.reshape(seq_count, length, model_width)
    value_seqs = value_rows.reshape(seq_count, length, model_width)

    def forward_sequence(pieces):
        return attend_forward(pieces[0], pieces[1], pieces[2], pieces[3], block_rows)

    contexts, log_sums = lax.map(forward_sequence, (query_seqs, key_seqs, value_seqs, segment_ids))
    contexts = contexts.reshape(seq_count * length, model_width)
    attended = jnp.dot(contexts, full_attn, preferred_element_type=jnp.float32) + bias_attn
    first_sum = flat_rows.astype(jnp.float32) + attended
    normed_one, norm_one_back = jax.vjp(norm_layer, first_sum, gain_one, shift_one)
    normed_low = normed_one.astype(jnp.bfloat16)
    hidden_pre = jnp.dot(normed_low, full_in, preferred_element_type=jnp.float32) + bias_in
    hidden, gelu_back = jax.vjp(gelu_exact, hidden_pre)
    hidden_low = hidden.astype(jnp.bfloat16)
    second_sum = normed_one + (
        jnp.dot(hidden_low, full_out, preferred_element_type=jnp.float32) + bias_out
    )
    result, norm_two_back = jax.vjp(norm_layer, second_sum, gain_two, shift_two)
    layer_out = result.astype(jnp.bfloat16).reshape(seq_count, length, model_width)
    again = (
        lax.all_gather(w_qkv, "shard", axis=0, tiled=True),
        lax.all_gather(w_attn_out, "shard", axis=0, tiled=True),
        lax.all_gather(w_in, "shard", axis=0, tiled=True),
        lax.all_gather(w_out, "shard", axis=0, tiled=True),
    )
    back_qkv, back_attn, back_in, back_out = (
        lax.all_gather(again[0], "grp", axis=1, tiled=True),
        lax.all_gather(again[1], "grp", axis=1, tiled=True),
        lax.all_gather(again[2], "grp", axis=1, tiled=True),
        lax.all_gather(again[3], "grp", axis=1, tiled=True),
    )
    masked_cot = cotangent.astype(jnp.float32).reshape(
        seq_count * length, model_width
    ) * keep_flag.reshape(seq_count * length, 1).astype(jnp.float32)
    second_grad, gain_two_grad, shift_two_grad = norm_two_back(masked_cot)
    bias_out_grad = jnp.sum(second_grad, 0)
    out_low = second_grad.astype(jnp.bfloat16)
    w_out_grad = contract_rows(hidden_low, out_low)
    hidden_grad = contract_cols(out_low, back_out)
    (pre_grad,) = gelu_back(hidden_grad)
    bias_in_grad = jnp.sum(pre_grad, 0)
    pre_low = pre_grad.astype(jnp.bfloat16)
    w_in_grad = contract_rows(normed_low, pre_low)
    normed_grad = second_grad + contract_cols(pre_low, back_in)
    first_grad, gain_one_grad, shift_one_grad = norm_one_back(normed_grad)
    bias_attn_grad = jnp.sum(first_grad, 0)
    attn_low = first_grad.astype(jnp.bfloat16)
    w_attn_grad = contract_rows(contexts, attn_low)
    context_grad = contract_cols(attn_low, back_attn).astype(jnp.bfloat16)

    def backward_sequence(pieces):
        return attend_backward(
            pieces[0], pieces[1], pieces[2], pieces[3], pieces[4], pieces[5], block_rows
        )

    query_grad, key_grad, value_grad = lax.map(
        backward_sequence,
        (
            query_seqs,
            key_seqs,
            value_seqs,
            segment_ids,
            log_sums,
            context_grad.reshape(seq_count, length, model_width),
        ),
    )
    query_grad = query_grad.reshape(seq_count * length, model_width)
    key_grad = key_grad.reshape(seq_count * length, model_width)
    value_grad = value_grad.reshape(seq_count * length, model_width)
    bias_query_grad = jnp.sum(query_grad, 0)
    bias_value_grad = jnp.sum(value_grad, 0)
    qkv_low = jnp.concatenate([query_grad, key_grad, value_grad], 1).astype(jnp.bfloat16)
    w_qkv_grad = contract_rows(flat_rows, qkv_low)
    input_grad = first_grad + contract_cols(qkv_low, back_qkv)
    reduced = (
        lax.psum_scatter(
            w_qkv_grad.astype(jnp.bfloat16), "shard", scatter_dimension=0, tiled=True
        ).astype(jnp.float32),
        lax.psum_scatter(
            bias_query_grad.astype(jnp.bfloat16), "shard", scatter_dimension=0, tiled=True
        ).astype(jnp.float32),
        lax.psum_scatter(
            bias_value_grad.astype(jnp.bfloat16), "shard", scatter_dimension=0, tiled=True
        ).astype(jnp.float32),
        lax.psum_scatter(
            w_attn_grad.astype(jnp.bfloat16), "shard", scatter_dimension=0, tiled=True
        ).astype(jnp.float32),
        lax.psum_scatter(
            bias_attn_grad.astype(jnp.bfloat16), "shard", scatter_dimension=0, tiled=True
        ).astype(jnp.float32),
        lax.psum_scatter(
            gain_one_grad.astype(jnp.bfloat16), "shard", scatter_dimension=0, tiled=True
        ).astype(jnp.float32),
        lax.psum_scatter(
            shift_one_grad.astype(jnp.bfloat16), "shard", scatter_dimension=0, tiled=True
        ).astype(jnp.float32),
        lax.psum_scatter(
            w_in_grad.astype(jnp.bfloat16), "shard", scatter_dimension=0, tiled=True
        ).astype(jnp.float32),
        lax.psum_scatter(
            bias_in_grad.astype(jnp.bfloat16), "shard", scatter_dimension=0, tiled=True
        ).astype(jnp.float32),
        lax.psum_scatter(
            w_out_grad.astype(jnp.bfloat16), "shard", scatter_dimension=0, tiled=True
        ).astype(jnp.float32),
        lax.psum_scatter(
            bias_out_grad.astype(jnp.bfloat16), "shard", scatter_dimension=0, tiled=True
        ).astype(jnp.float32),
        lax.psum_scatter(
            gain_two_grad.astype(jnp.bfloat16), "shard", scatter_dimension=0, tiled=True
        ).astype(jnp.float32),
        lax.psum_scatter(
            shift_two_grad.astype(jnp.bfloat16), "shard", scatter_dimension=0, tiled=True
        ).astype(jnp.float32),
    )
    summed = (
        lax.psum(reduced[0].astype(jnp.bfloat16), "grp").astype(jnp.float32),
        lax.psum(reduced[1].astype(jnp.bfloat16), "grp").astype(jnp.float32),
        lax.psum(reduced[2].astype(jnp.bfloat16), "grp").astype(jnp.float32),
        lax.psum(reduced[3].astype(jnp.bfloat16), "grp").astype(jnp.float32),
        lax.psum(reduced[4].astype(jnp.bfloat16), "grp").astype(jnp.float32),
        lax.psum(reduced[5].astype(jnp.bfloat16), "grp").astype(jnp.float32),
        lax.psum(reduced[6].astype(jnp.bfloat16), "grp").astype(jnp.float32),
        lax.psum(reduced[7].astype(jnp.bfloat16), "grp").astype(jnp.float32),
        lax.psum(reduced[8].astype(jnp.bfloat16), "grp").astype(jnp.float32),
        lax.psum(reduced[9].astype(jnp.bfloat16), "grp").astype(jnp.float32),
        lax.psum(reduced[10].astype(jnp.bfloat16), "grp").astype(jnp.float32),
        lax.psum(reduced[11].astype(jnp.bfloat16), "grp").astype(jnp.float32),
        lax.psum(reduced[12].astype(jnp.bfloat16), "grp").astype(jnp.float32),
    )
    return (
        layer_out,
        input_grad.reshape(seq_count, length, model_width),
        summed[0],
        summed[1],
        summed[2],
        summed[3],
        summed[4],
        summed[5],
        summed[6],
        summed[7],
        summed[8],
        summed[9],
        summed[10],
        summed[11],
        summed[12],
    )


NT = (((1,), (1,)), ((), ()))
NN = (((1,), (0,)), ((), ()))
TN = (((0,), (0,)), ((), ()))
LANES = 128
AXES = ("grp", "shard")


def mxu(left, right, dims):
    return lax.dot_general(left, right, dims, preferred_element_type=jnp.float32)


def params(megabytes=60):
    return pltpu.CompilerParams(vmem_limit_bytes=megabytes << 20)


def attention_forward_kernel(q_ref, k_ref, v_ref, seg_col, seg_row, out_ref, lse_ref, *, rows):
    length = q_ref.shape[0]
    first = lax.broadcasted_iota(jnp.int32, (1, LANES), 1) < HD
    keys = k_ref[...]
    values = v_ref[...]
    zero = jnp.zeros_like(keys)
    head_keys = (jnp.where(first, keys, zero), jnp.where(first, zero, keys))
    key_segments = seg_col[...]
    for block in range(length // rows):
        here = pl.ds(block * rows, rows)
        q = q_ref[here, :]
        allowed = key_segments == seg_row[:, here]
        outs = []
        for head in range(2):
            scores = mxu(head_keys[head], q, NT)
            scores = jnp.where(allowed, scores, masked_score)
            top = jnp.max(scores, 0, keepdims=True)
            powers = jnp.exp(scores - top)
            total = jnp.sum(powers, 0, keepdims=True)
            part = mxu(powers.astype(jnp.bfloat16), values, TN)
            outs.append(part * jnp.transpose(jnp.broadcast_to(1.0 / total, (LANES, rows))))
            lse_ref[0, head : head + 1, here] = top + jnp.log(total)
        out_ref[here, :] = jnp.where(first, outs[0], outs[1]).astype(jnp.bfloat16)


def attention_forward(qkv, seg_col, seg_row, start, pairs, before=None):
    length, width = qkv.shape[0], qkv.shape[1] // 3
    total = width // LANES
    rows = min(512, length)
    anywhere = pl.BlockSpec(memory_space=pl.ANY)

    def pair(part):
        return pl.BlockSpec((length, LANES), lambda j: (0, part * total + start + j))

    def body(q_ref, k_ref, v_ref, seg_c, seg_r, *refs):
        attention_forward_kernel(q_ref, k_ref, v_ref, seg_c, seg_r, *refs[-2:], rows=rows)

    return pl.pallas_call(
        body,
        grid=(pairs,),
        in_specs=[
            pair(0),
            pair(1),
            pair(2),
            pl.BlockSpec((length, 1), lambda j: (0, 0)),
            pl.BlockSpec((1, length), lambda j: (0, 0)),
        ]
        + [anywhere] * (0 if before is None else 2),
        out_specs=[
            pl.BlockSpec((length, LANES), lambda j: (0, start + j)),
            pl.BlockSpec((1, 2, length), lambda j: (start + j, 0, 0)),
        ],
        out_shape=[
            jax.ShapeDtypeStruct((length, width), jnp.bfloat16),
            jax.ShapeDtypeStruct((total, 2, length), jnp.float32),
        ],
        input_output_aliases={} if before is None else {5: 0, 6: 1},
        compiler_params=params(60),
        cost_estimate=pl.CostEstimate(
            flops=16 * length * length * pairs * LANES,
            bytes_accessed=8 * length * pairs * LANES,
            transcendentals=0,
        ),
        name="attn_fwd",
    )(qkv, qkv, qkv, seg_col, seg_row, *(() if before is None else before))


def attention_backward_kernel(
    q_ref, k_ref, v_ref, o_ref, do_ref, seg_col, seg_row, lse_ref, grad_ref, sum_ref, *, rows
):
    length = q_ref.shape[0]
    lane = lax.broadcasted_iota(jnp.int32, (1, LANES), 1)
    first = lane < HD
    pick = (
        lax.broadcasted_iota(jnp.int32, (8, LANES), 0)
        == lax.broadcasted_iota(jnp.int32, (8, LANES), 1) // HD
    ).astype(jnp.float32)
    keys = k_ref[...]
    values = v_ref[...]
    zero = jnp.zeros_like(keys)
    head_keys = (jnp.where(first, keys, zero), jnp.where(first, zero, keys))
    head_values = (jnp.where(first, values, zero), jnp.where(first, zero, values))
    key_segments = seg_col[...]
    key_sum = [None, None]
    value_sum = [None, None]
    query_total = jnp.zeros((1, LANES), jnp.float32)
    for block in range(length // rows):
        here = pl.ds(block * rows, rows)
        q = q_ref[here, :]
        do = do_ref[here, :]
        allowed = key_segments == seg_row[:, here]
        dots = lax.dot_general(
            pick,
            do.astype(jnp.float32) * o_ref[here, :].astype(jnp.float32),
            NT,
            precision=lax.Precision.HIGHEST,
            preferred_element_type=jnp.float32,
        )
        parts = []
        for head in range(2):
            scores = mxu(head_keys[head], q, NT)
            scores = jnp.where(allowed, scores, masked_score)
            probs = jnp.exp(scores - lse_ref[0, head : head + 1, here])
            prob_grad = mxu(head_values[head], do, NT)
            score_grad = (probs * (prob_grad - dots[head : head + 1, :])).astype(jnp.bfloat16)
            value_part = mxu(probs.astype(jnp.bfloat16), do, NN)
            key_part = mxu(score_grad, q, NN)
            value_sum[head] = value_part if block == 0 else value_sum[head] + value_part
            key_sum[head] = key_part if block == 0 else key_sum[head] + key_part
            parts.append(mxu(score_grad, keys, TN))
        query_grad = jnp.where(first, parts[0], parts[1]) * (1.0 / math.sqrt(HD))
        query_total = query_total + jnp.sum(query_grad, 0, keepdims=True)
        grad_ref[0, here, :] = query_grad.astype(jnp.bfloat16)
    grad_ref[1, :, :] = jnp.where(first, key_sum[0], key_sum[1]).astype(jnp.bfloat16)
    value_grad = jnp.where(first, value_sum[0], value_sum[1])
    grad_ref[2, :, :] = value_grad.astype(jnp.bfloat16)
    sum_ref[0:1, :] = query_total
    sum_ref[1:2, :] = jnp.sum(value_grad, 0, keepdims=True)


def attention_backward(qkv, out, out_grad, seg_col, seg_row, lse, start, pairs, at, size, before=None):
    length, width = out.shape
    total = width // LANES
    rows = min(256, length)
    anywhere = pl.BlockSpec(memory_space=pl.ANY)

    def pair(part):
        return pl.BlockSpec((length, LANES), lambda j: (0, part * total + start + j))

    def body(*refs):
        attention_backward_kernel(*refs[:8], *refs[-2:], rows=rows)

    return pl.pallas_call(
        body,
        grid=(pairs,),
        in_specs=[
            pair(0),
            pair(1),
            pair(2),
            pair(0),
            pair(0),
            pl.BlockSpec((length, 1), lambda j: (0, 0)),
            pl.BlockSpec((1, length), lambda j: (0, 0)),
            pl.BlockSpec((1, 2, length), lambda j: (j + start, 0, 0)),
        ]
        + [anywhere] * (0 if before is None else 2),
        out_specs=[
            pl.BlockSpec((3, length, LANES), lambda j: (0, 0, j + at)),
            pl.BlockSpec((2, LANES), lambda j: (0, j + at)),
        ],
        out_shape=[
            jax.ShapeDtypeStruct((3, length, size * LANES), jnp.bfloat16),
            jax.ShapeDtypeStruct((2, size * LANES), jnp.float32),
        ],
        input_output_aliases={} if before is None else {8: 0, 9: 1},
        compiler_params=params(60),
        cost_estimate=pl.CostEstimate(
            flops=40 * length * length * pairs * LANES,
            bytes_accessed=16 * length * pairs * LANES,
            transcendentals=0,
        ),
        name="attn_bwd",
    )(qkv, qkv, qkv, out, out_grad, seg_col, seg_row, lse, *(() if before is None else before))


class Place:
    def __init__(self, groups, shards):
        self.groups = groups
        self.shards = shards
        self.chips = shards // 2
        self.grp = lax.axis_index("grp")
        self.shard = lax.axis_index("shard")
        self.core = self.shard % 2
        self.chip = self.shard // 2
        self.scalars = jnp.stack([self.core, self.chip, self.grp]).astype(jnp.int32)

    def permute(self, array, mask_of_core):
        pairs = [(i, i ^ mask_of_core[i % 2]) for i in range(self.groups * self.shards)]
        return lax.ppermute(array, AXES, pairs)

    def swap_core(self, array):
        return self.permute(array, (1, 1))

    def swap_grp(self, array, step):
        masks = (self.shards, 2 * self.shards)
        return self.permute(array, masks if step == 0 else masks[::-1])

    def swap_chip(self, array, step):
        masks = (2, 4)
        return self.permute(array, masks if step == 0 else masks[::-1])

    def slot_chip(self, slot):
        return self.chip ^ turn(slot, self.core)

    def slot_grp(self, slot):
        return self.grp ^ turn(slot, self.core)


def turn(slot, core):
    if isinstance(slot, int):
        return slot if slot in (0, 3) else jnp.where(core == 0, slot, 3 - slot)
    return jnp.where((core == 0) | (slot == 0) | (slot == 3), slot, 3 - slot)


def after(value, *others):
    return lax.optimization_barrier((value, *others))[0]


class Gather:
    def __init__(self, place, piece):
        self.place = place
        self.piece = piece
        self.held = [None] * 4
        self.crossed = [None] * 4

    def chips_near(self, *wait):
        piece = after(self.piece, *wait) if wait else self.piece
        self.pair = [piece, self.place.swap_chip(piece, 0)]
        return self.pair[1]

    def chips_far(self, *wait):
        pair = jnp.stack([self.pair[0], after(self.pair[1], *wait)])
        self.rest = [pair, self.place.swap_chip(pair, 1)]
        return self.rest[1]

    def join(self, *wait):
        rest = after(self.rest[1], *wait) if wait else self.rest[1]
        self.held[0] = jnp.concatenate([self.rest[0], rest])
        return self.held[0]

    def near(self):
        self.held[1] = self.place.swap_grp(self.held[0], 0)
        self.held[2] = self.place.swap_grp(self.held[0], 1)
        return self.held[2]

    def far(self, *wait):
        first = after(self.held[1], *wait) if wait else self.held[1]
        self.held[3] = self.place.swap_grp(first, 1)
        return self.held[3]

    def cross(self, *which, wait=()):
        for n in which:
            piece = after(self.held[n], *wait) if wait else self.held[n]
            self.crossed[n] = self.place.swap_core(piece)

    def pieces(self):
        return self.held + self.crossed


class Window:
    def __init__(self, gather, start, cols):
        self.arrays = gather.pieces()
        self.start, self.cols = start, cols
        chips, rows, _ = self.arrays[0].shape
        self.chips, self.rows = chips, rows


def fetch(where, window, refs, whole, sem, by):
    rows, cols, chips = window.rows, window.cols, window.chips
    for slot in range(4):
        for side in range(2):
            core = where[0] ^ side
            ref = refs[4 * side + slot]
            distance = turn(slot, core)
            col = pl.multiple_of((where[2] ^ distance) * cols, LANES)
            for k in range(chips):
                row = ((where[1] ^ turn(k, core)) * 2 + core) * rows
                pltpu.make_async_copy(
                    ref.at[k, :, pl.ds(window.start, cols)],
                    whole.at[pl.ds(pl.multiple_of(row, rows), rows), pl.ds(col, cols)],
                    sem.at[distance if by == "grp" else 0],
                ).start()


def weight_call(place, kernel, window, inputs, in_specs, outs, out_specs, steps, by, name, flops, mb=60):
    cols, groups = window.cols, place.groups
    pieces = window.arrays
    shape = (window.chips * 2 * window.rows, groups * cols)
    slots = {"grp": groups, "all": 1}[by]
    anywhere = pl.BlockSpec(memory_space=pl.ANY)

    def body(where, *refs):
        taken, refs = refs[: len(pieces)], refs[len(pieces) :]
        *refs, written, weight, sem, out_sem = refs
        step = pl.program_id(0)

        @pl.when(step == 0)
        def _():
            fetch(where, window, taken, weight, sem, by)

        def ready():
            if by == "all":

                @pl.when(step == 0)
                def _():
                    pltpu.make_async_copy(weight, weight, sem.at[0]).wait()
                    pltpu.make_async_copy(weight, written, out_sem.at[0]).start()

            else:
                at = pl.ds(pl.multiple_of((where[2] ^ step) * cols, LANES), cols)
                view = weight.at[:, at]
                pltpu.make_async_copy(view, view, sem.at[step]).wait()
                pltpu.make_async_copy(view, written.at[:, at], out_sem.at[step]).start()

        kernel(where, ready, weight, *refs)

        @pl.when(step == steps - 1)
        def _():
            for slot in range(slots):
                width = shape[1] // slots
                view = weight.at[:, pl.ds(slot * width, width)]
                pltpu.make_async_copy(view, view, out_sem.at[slot]).wait()

    total = sum(math.prod(x.shape) * x.dtype.itemsize for x in list(inputs) + list(outs))
    return pl.pallas_call(
        body,
        grid_spec=pltpu.PrefetchScalarGridSpec(
            num_scalar_prefetch=1,
            grid=(steps,),
            in_specs=[anywhere] * len(pieces) + in_specs,
            out_specs=out_specs + [anywhere],
            scratch_shapes=[
                pltpu.VMEM(shape, jnp.bfloat16),
                pltpu.SemaphoreType.DMA((slots,)),
                pltpu.SemaphoreType.DMA((slots,)),
            ],
        ),
        out_shape=outs + [shaped(shape, jnp.bfloat16)],
        compiler_params=params(mb),
        cost_estimate=pl.CostEstimate(
            flops=flops, bytes_accessed=4 * shape[0] * shape[1] + total, transcendentals=0
        ),
        name=name,
    )(place.scalars, *pieces, *inputs)


def plain_call(kernel, inputs, in_specs, outs, out_specs, steps, name, flops, mb=60):
    total = sum(math.prod(x.shape) * x.dtype.itemsize for x in list(inputs) + list(outs))
    return pl.pallas_call(
        kernel,
        grid=(steps,),
        in_specs=in_specs,
        out_specs=out_specs,
        out_shape=outs,
        compiler_params=params(mb),
        cost_estimate=pl.CostEstimate(flops=flops, bytes_accessed=total, transcendentals=0),
        name=name,
    )(*inputs)


TILE = 256


def row_tiles(width):
    return pl.BlockSpec((TILE, width), lambda i, *s: (i, 0))


def fixed(*shape):
    return pl.BlockSpec(shape, lambda i, *s: (0,) * len(shape))


def whole_once(shape):
    return pl.BlockSpec(shape, lambda i: (0,) * len(shape), pipeline_mode=pl.Buffered(1))


def shaped(shape, dtype):
    return jax.ShapeDtypeStruct(shape, dtype)


B_QUERY, B_VALUE, B_ATTN, GAIN_ONE, SHIFT_ONE, B_OUT, GAIN_TWO, SHIFT_TWO, B_IN = range(9)


def row(ref, n):
    return ref[n : n + 1, :]


class Vectors:
    def __init__(self, place, vectors, *wait):
        flat = jnp.concatenate([after(vectors[0], *wait), *vectors[1:]])
        own = jnp.pad(flat.reshape(-1, LANES), ((0, -(flat.shape[0] // LANES) % 16), (0, 0)))
        own = jnp.stack([own, place.swap_core(own)])
        pair = jnp.stack([own, place.swap_chip(own, 0)])
        self.slots = jnp.concatenate([pair, place.swap_chip(pair, 1)])
        self.place = place

    def unpack(self):
        place = self.place
        slots, sides, rows, lanes = self.slots.shape
        shards = place.shards

        def kernel(where, in_ref, rows_ref, inner_ref, qkv_ref):
            width = shards * lanes
            qkv_ref[...] = jnp.zeros_like(qkv_ref)
            for slot in range(slots):
                for side in range(sides):
                    core = where[0] ^ side
                    shard = (where[1] ^ turn(slot, where[0])) * 2 + core
                    part = in_ref[slot, side].astype(jnp.float32)
                    at = pl.multiple_of(shard * lanes, lanes)
                    rows_ref[:, pl.ds(at, lanes)] = part
                    qkv_ref[:, pl.ds(at, lanes)] = part[B_QUERY : B_QUERY + 1]
                    qkv_ref[:, pl.ds(2 * width + at, lanes)] = part[B_VALUE : B_VALUE + 1]
                    for n in range(4):
                        start = pl.multiple_of((shard * 4 + n) * lanes, lanes)
                        inner_ref[:, pl.ds(start, lanes)] = part[B_IN + n : B_IN + n + 1]

        in_vmem = pl.BlockSpec(memory_space=pltpu.VMEM)
        return pl.pallas_call(
            kernel,
            in_specs=[pl.BlockSpec(memory_space=pltpu.SMEM), in_vmem],
            out_specs=[in_vmem] * 3,
            out_shape=[
                shaped((rows, shards * lanes), jnp.float32),
                shaped((1, 4 * shards * lanes), jnp.float32),
                shaped((1, 3 * shards * lanes), jnp.float32),
            ],
            name="vectors",
        )(place.scalars, self.slots)


def pack_sums(late_a, late_b, first_sums, second_sums, inner_sums):
    width = first_sums.shape[1]
    half = late_a.shape[1]

    def kernel(a_ref, b_ref, one_ref, two_ref, inner_ref, out_ref):
        def place_of(n):
            return n // 3 * 8 + n % 3

        out_ref[...] = jnp.zeros_like(out_ref)
        for n in (B_QUERY, B_VALUE):
            at = place_of(n)
            out_ref[at : at + 1, 0:half] = a_ref[n : n + 1, :]
            out_ref[at : at + 1, half:width] = b_ref[n : n + 1, :]
        for n, source, line in (
            (GAIN_ONE, one_ref, 0),
            (SHIFT_ONE, one_ref, 1),
            (B_ATTN, one_ref, 2),
            (GAIN_TWO, two_ref, 0),
            (SHIFT_TWO, two_ref, 1),
            (B_OUT, two_ref, 2),
        ):
            at = place_of(n)
            out_ref[at : at + 1, :] = source[line : line + 1, :]
        for n in range(4):
            at = place_of(B_IN + n)
            for shard in range(width // LANES):
                start = (4 * shard + n) * LANES
                out_ref[at : at + 1, shard * LANES : (shard + 1) * LANES] = inner_ref[
                    :, start : start + LANES
                ]

    in_vmem = pl.BlockSpec(memory_space=pltpu.VMEM)
    return pl.pallas_call(
        kernel,
        in_specs=[in_vmem] * 5,
        out_specs=in_vmem,
        out_shape=shaped((32, width), jnp.float32),
        name="pack_sums",
    )(late_a, late_b, first_sums, second_sums, inner_sums)


def project_qkv(place, rows, window, bias, scale):
    length, width = rows.shape
    cols = window.cols

    def kernel(where, ready, weight, x_ref, bias_ref, scale_ref, out_ref):
        ready()
        at = pl.ds(pl.multiple_of((where[2] ^ pl.program_id(0)) * cols, LANES), cols)
        for tile in range(length // TILE):
            here = pl.ds(tile * TILE, TILE)
            mixed = mxu(x_ref[here, :], weight[:, at], NN) + bias_ref[:, at]
            mixed = mixed.astype(jnp.bfloat16).astype(jnp.float32) * scale_ref[:, at]
            out_ref[here, :] = mixed.astype(jnp.bfloat16)

    total = cols * place.groups
    return weight_call(
        place,
        kernel,
        window,
        (rows, bias, scale),
        [fixed(length, width), fixed(1, total), fixed(1, total)],
        [shaped((length, total), jnp.bfloat16)],
        [pl.BlockSpec((length, cols), lambda i, s: (0, i ^ s[2]))],
        place.groups,
        "grp",
        "qkv",
        2 * length * width * total,
    )


def norm_parts(rows):
    centered = rows - jnp.mean(rows, -1, keepdims=True)
    scale = lax.rsqrt(jnp.mean(centered * centered, -1, keepdims=True) + epsilon)
    return centered * scale, scale


def norm_back(grad, normed, scale):
    return scale * (
        grad
        - jnp.mean(grad, -1, keepdims=True)
        - normed * jnp.mean(grad * normed, -1, keepdims=True)
    )


def add_rows(sum_ref, *terms):
    @pl.when(pl.program_id(0) == 0)
    def _():
        sum_ref[...] = jnp.zeros_like(sum_ref)

    for n, term in enumerate(terms):
        sum_ref[n : n + 1, :] += jnp.sum(term, 0, keepdims=True)


def project_out(place, contexts, window, rows, vectors):
    length, width = rows.shape

    def kernel(where, ready, weight, c_ref, x_ref, v_ref, n_ref, r_ref, low_ref):
        ready()
        first_sum = mxu(c_ref[...], weight[...], NN) + row(v_ref, B_ATTN)
        first_sum = first_sum + x_ref[...].astype(jnp.float32)
        normed, scale = norm_parts(first_sum)
        n_ref[...] = normed
        r_ref[...] = jnp.broadcast_to(scale, r_ref.shape)
        low_ref[...] = (normed * row(v_ref, GAIN_ONE) + row(v_ref, SHIFT_ONE)).astype(jnp.bfloat16)

    return weight_call(
        place,
        kernel,
        window,
        (contexts, rows, vectors),
        [row_tiles(width), row_tiles(width), fixed(*vectors.shape)],
        [
            shaped((length, width), jnp.float32),
            shaped((length, LANES), jnp.float32),
            shaped((length, width), jnp.bfloat16),
        ],
        [row_tiles(width), row_tiles(LANES), row_tiles(width)],
        length // TILE,
        "all",
        "attn_out",
        2 * length * width * width,
    )


def normal_share(values):
    power = jnp.exp(-0.5 * values * values)
    t = 1.0 / (1.0 + (0.3275911 / math.sqrt(2.0)) * jnp.abs(values))
    tail = 0.5 * 1.061405429
    for factor in (-1.453152027, 1.421413741, -0.284496736, 0.254829592):
        tail = tail * t + 0.5 * factor
    tail = tail * t * power
    return jnp.where(values >= 0, 1.0 - tail, tail), power * (1.0 / math.sqrt(2.0 * math.pi))


def feed_in(place, normed_low, window, bias):
    length, width = normed_low.shape
    cols = window.cols

    def kernel(where, ready, weight, x_ref, bias_ref, hid_ref, slope_ref):
        ready()
        at = pl.ds(pl.multiple_of((where[2] ^ pl.program_id(0)) * cols, LANES), cols)
        for tile in range(length // TILE):
            here = pl.ds(tile * TILE, TILE)
            pre = mxu(x_ref[here, :], weight[:, at], NN) + bias_ref[:, at]
            share, bell = normal_share(pre)
            hid_ref[here, :] = (pre * share).astype(jnp.bfloat16)
            slope_ref[here, :] = (share + pre * bell).astype(jnp.bfloat16)

    total = cols * place.groups
    block = pl.BlockSpec((length, cols), lambda i, s: (0, i ^ s[2]))
    return weight_call(
        place,
        kernel,
        window,
        (normed_low, bias),
        [fixed(length, width), fixed(1, total)],
        [shaped((length, total), jnp.bfloat16)] * 2,
        [block, block],
        place.groups,
        "grp",
        "feed_in",
        2 * length * width * total,
    )


def feed_out(place, hidden, window, normed, cot, keep, vectors):
    length, inner = hidden.shape
    width = normed.shape[1]

    def kernel(where, ready, weight, h_ref, n_ref, cot_ref, keep_ref, v_ref, *outs):
        out_ref, grad_ref, low_ref, sum_ref = outs
        ready()
        fed = mxu(h_ref[...], weight[...], NN)
        normed_one = n_ref[...] * row(v_ref, GAIN_ONE) + row(v_ref, SHIFT_ONE)
        second_sum = normed_one + (fed + row(v_ref, B_OUT))
        second, scale = norm_parts(second_sum)
        out_ref[...] = (second * row(v_ref, GAIN_TWO) + row(v_ref, SHIFT_TWO)).astype(jnp.bfloat16)
        masked = cot_ref[...].astype(jnp.float32) * keep_ref[...]
        grad = norm_back(masked * row(v_ref, GAIN_TWO), second, scale)
        grad_ref[...] = grad
        low_ref[...] = grad.astype(jnp.bfloat16)
        add_rows(sum_ref, masked * second, masked, grad)

    return weight_call(
        place,
        kernel,
        window,
        (hidden, normed, cot, keep, vectors),
        [row_tiles(inner), row_tiles(width), row_tiles(width), row_tiles(1), fixed(*vectors.shape)],
        [
            shaped((length, width), jnp.bfloat16),
            shaped((length, width), jnp.float32),
            shaped((length, width), jnp.bfloat16),
            shaped((8, width), jnp.float32),
        ],
        [row_tiles(width), row_tiles(width), row_tiles(width), fixed(8, width)],
        length // TILE,
        "all",
        "feed_out",
        2 * length * width * inner,
    )


def feed_out_back(out_low, weight, slope):
    length, width = out_low.shape
    inner = slope.shape[1]
    cols = min(1024, inner)

    def kernel(g_ref, w_ref, slope_ref, pre_ref, sum_ref):
        total = jnp.zeros((1, cols), jnp.float32)
        for tile in range(length // TILE):
            here = pl.ds(tile * TILE, TILE)
            grad = mxu(g_ref[here, :], w_ref[...], NT) * slope_ref[here, :].astype(jnp.float32)
            pre_ref[here, :] = grad.astype(jnp.bfloat16)
            total = total + jnp.sum(grad, 0, keepdims=True)
        sum_ref[...] = total

    block = pl.BlockSpec((length, cols), lambda i: (0, i))
    return plain_call(
        kernel,
        (out_low, weight, slope),
        [fixed(length, width), pl.BlockSpec((cols, width), lambda i: (i, 0)), block],
        [shaped((length, inner), jnp.bfloat16), shaped((1, inner), jnp.float32)],
        [block, pl.BlockSpec((1, cols), lambda i: (0, i))],
        inner // cols,
        "feed_out_back",
        2 * length * width * inner,
    )


def feed_in_back(pre_low, weight, second_grad, normed, scale, vectors, attn_weight):
    length, inner = pre_low.shape
    width = normed.shape[1]

    def kernel(p_ref, w_ref, g_ref, n_ref, r_ref, v_ref, a_ref, first_ref, low_ref, ctx_ref, sum_ref):
        grad = g_ref[...] + mxu(p_ref[...], w_ref[...], NT)
        first = norm_back(grad * row(v_ref, GAIN_ONE), n_ref[...], r_ref[:, :1])
        low = first.astype(jnp.bfloat16)
        first_ref[...] = first
        low_ref[...] = low
        ctx_ref[...] = mxu(low, a_ref[...], NT).astype(jnp.bfloat16)
        add_rows(sum_ref, grad * n_ref[...], grad, first)

    return plain_call(
        kernel,
        (pre_low, weight, second_grad, normed, scale, vectors, attn_weight),
        [
            row_tiles(inner),
            whole_once(weight.shape),
            row_tiles(width),
            row_tiles(width),
            row_tiles(LANES),
            fixed(*vectors.shape),
            whole_once(attn_weight.shape),
        ],
        [
            shaped((length, width), jnp.float32),
            shaped((length, width), jnp.bfloat16),
            shaped((length, width), jnp.bfloat16),
            shaped((8, width), jnp.float32),
        ],
        [row_tiles(width), row_tiles(width), row_tiles(width), fixed(8, width)],
        length // TILE,
        "feed_in_back",
        2 * length * width * (inner + width),
    )


def project_qkv_back(grads, weight, first_grad):
    length, width = first_grad.shape
    part = width // len(grads)

    def kernel(w_ref, *refs):
        *grad_refs, first_ref, out_ref = refs
        total = first_ref[...]
        for n in range(3):
            for m, grad_ref in enumerate(grad_refs):
                at = n * width + m * part
                total = total + mxu(grad_ref[n], w_ref[:, at : at + part], NT)
        out_ref[...] = total

    return plain_call(
        kernel,
        (weight, *grads, first_grad),
        [whole_once(weight.shape)]
        + [pl.BlockSpec((3, TILE, part), lambda i: (0, i, 0))] * len(grads)
        + [row_tiles(width)],
        [shaped((length, width), jnp.float32)],
        [row_tiles(width)],
        length // TILE,
        "qkv_back",
        6 * length * width * width,
    )[0]


ORDER = (1, 3, 0, 2)


def ordered_slot(j):
    return jnp.where(j < 2, 2 * j + 1, 2 * j - 4)


def weight_grad_kernel(where, *refs, rows, groups, count, split, extra):
    lefts, rights, refs = refs[:count], refs[count : 2 * count], refs[2 * count :]
    sums_ref = None
    if extra:
        sums_ref, *refs = refs
    (leave, keep, sent), kept = refs[:3], refs[3:]
    core = where[0]
    chips = lefts[0].shape[1] // (2 * rows)

    @pl.when(pl.program_id(1) == 0)
    def _():
        for left_ref, kept_ref in zip(lefts, kept):
            for side in range(2):
                chosen = []
                for k in range(chips):
                    even = left_ref[:, 2 * k * rows : (2 * k + 1) * rows]
                    odd = left_ref[:, (2 * k + 1) * rows : (2 * k + 2) * rows]
                    chosen.append(jnp.where(core == side, even, odd))
                left = chosen[0] if chips == 1 else jnp.concatenate(chosen, 1)
                kept_ref[side] = left.T

    def write(ref, pos, side):
        at = 0
        for right_ref, kept_ref in zip(rights, kept):
            if len(right_ref.shape) == 3:
                pieces = [right_ref[n] for n in range(right_ref.shape[0])]
            else:
                size = min(512, right_ref.shape[1])
                pieces = [
                    right_ref[:, n * size : (n + 1) * size]
                    for n in range(right_ref.shape[1] // size)
                ]
            for piece in pieces:
                part = mxu(kept_ref[side], piece, NN).astype(jnp.bfloat16)
                size = piece.shape[1]
                ref[pos, :, 0:rows, at : at + size] = part.reshape(chips, rows, size)
                at += size
        if extra:
            block = where[2] ^ turn(ordered_slot(pl.program_id(1)), core)
            blank = jnp.zeros((extra, at), jnp.bfloat16)
            for k in range(chips):
                start = pl.multiple_of((2 * k + (core ^ side)) * LANES, LANES)
                ref[pos, k, rows : rows + extra, :] = blank
                lines = sums_ref[pl.ds(pl.multiple_of(block * 8, 8), 8), pl.ds(start, LANES)]
                for n in range(3):
                    ref[pos, k, rows : rows + 1, n * LANES : (n + 1) * LANES] = lines[
                        n : n + 1
                    ].astype(jnp.bfloat16)

    if split:
        write(sent, 0, 1)

        @pl.when(pl.program_id(1) < 2)
        def _():
            write(leave, 0, 0)

        @pl.when(pl.program_id(1) >= 2)
        def _():
            write(keep, 0, 0)

    else:
        cols = rights[0].shape[1] // groups
        for side in range(2):
            for pos, slot in enumerate(ORDER):
                start = pl.multiple_of((where[2] ^ turn(slot, core ^ side)) * cols, LANES)
                part = mxu(kept[0][side], rights[0][:, pl.ds(start, cols)], NN)
                part = part.astype(jnp.bfloat16).reshape(chips, rows, cols)
                if side == 1:
                    sent[pos] = part
                else:
                    (leave if pos < 2 else keep)[pos % 2] = part


def weight_grad(place, pairs, split, name, sums=None):
    tokens, height = pairs[0][0].shape
    groups, chips = place.groups, place.chips
    rows = height // place.shards
    step_chips = chips if split else max(1, 1024 // (2 * rows))
    steps = chips // step_chips
    grid = (steps, groups if split else 1)
    extra = 0 if sums is None else 16

    def block(j, s):
        return s[2] ^ turn(ordered_slot(j), s[0])

    def position(j):
        return jnp.where(j == 0, 3, jnp.where(j == 3, 0, j))

    cols = 0
    right_specs = []
    for _, right in pairs:
        size = right.shape[-1] // groups
        if not split:
            right_specs.append(pl.BlockSpec(right.shape, lambda i, j, s: (0, 0)))
        elif right.ndim == 3:
            right_specs.append(
                pl.BlockSpec((right.shape[0], tokens, size), lambda i, j, s: (0, 0, block(j, s)))
            )
        else:
            right_specs.append(pl.BlockSpec((tokens, size), lambda i, j, s: (0, block(j, s))))
        cols += size * (right.shape[0] if right.ndim == 3 else 1)
    left_spec = pl.BlockSpec((tokens, step_chips * 2 * rows), lambda i, j, s: (0, i))
    in_specs = [left_spec] * len(pairs) + right_specs
    inputs = [left for left, _ in pairs] + [right for _, right in pairs]
    if extra:
        in_specs.append(pl.BlockSpec(sums.shape, lambda i, j, s: (0, 0)))
        inputs.append(sums)
    tall = rows + extra
    if split:
        one = (1, step_chips, tall, cols)
        out_specs = [
            pl.BlockSpec(one, lambda i, j, s: (jnp.minimum(j, 1), i, 0, 0)),
            pl.BlockSpec(one, lambda i, j, s: (jnp.maximum(j - 2, 0), i, 0, 0)),
            pl.BlockSpec(one, lambda i, j, s: (position(j), i, 0, 0)),
        ]
    else:
        out_specs = [
            pl.BlockSpec((n, step_chips, tall, cols), lambda i, j, s: (0, i, 0, 0))
            for n in (2, 2, groups)
        ]
    return pl.pallas_call(
        functools.partial(
            weight_grad_kernel,
            rows=rows,
            groups=groups,
            count=len(pairs),
            split=split,
            extra=extra,
        ),
        grid_spec=pltpu.PrefetchScalarGridSpec(
            num_scalar_prefetch=1,
            grid=grid,
            in_specs=in_specs,
            out_specs=out_specs,
            scratch_shapes=[pltpu.VMEM((2, step_chips * rows, tokens), jnp.bfloat16)] * len(pairs),
        ),
        out_shape=[shaped((n, chips, tall, cols), jnp.bfloat16) for n in (2, 2, groups)],
        compiler_params=params(60),
        cost_estimate=pl.CostEstimate(
            flops=2 * tokens * height * cols * groups,
            bytes_accessed=2 * (tokens * (height + cols * groups) + height * cols * groups),
            transcendentals=0,
        ),
        name="wgrad_" + name,
    )(place.scalars, *inputs)


def add(*terms):
    total = terms[0].astype(jnp.float32)
    for term in terms[1:]:
        total = total + term.astype(jnp.float32)
    return total.astype(jnp.bfloat16)


class Reduction:
    def __init__(self, place, pairs, split, name, *wait, sums=None):
        self.place = place
        if wait:
            pairs = [(after(pairs[0][0], *wait), pairs[0][1])] + pairs[1:]
        self.leave, self.keep, sent = weight_grad(place, pairs, split, name, sums)
        self.made = self.leave
        self.core = place.swap_core(sent)

    def near(self, *wait):
        self.core = after(self.core, *wait) if wait else self.core
        leave = add(self.leave, self.core[:2])
        self.first = self.place.swap_grp(leave, 0)
        return leave

    def middle(self, *wait):
        self.first = after(self.first, *wait) if wait else self.first
        second = add(self.keep[1], self.core[3], self.first[1])
        self.second = self.place.swap_grp(second, 1)
        return second

    def column(self, *wait):
        second = after(self.second, *wait) if wait else self.second
        mine = add(self.keep[0], self.core[2], self.first[0], second)
        return mine, lambda chip: lax.dynamic_index_in_dim(mine, chip, 0, False)

    def along(self, *wait):
        place = self.place
        mine, at = self.column(*wait)
        self.mine = [at(place.slot_chip(slot)) for slot in range(4)]
        self.first = place.swap_chip(jnp.stack([self.mine[1], self.mine[3]]), 0)
        return mine

    def along_far(self, *wait):
        self.first = after(self.first, *wait) if wait else self.first
        second = add(self.mine[2], self.first[1])
        self.second = self.place.swap_chip(second, 1)
        return second

    def share(self, *wait):
        second = after(self.second, *wait) if wait else self.second
        return add(self.mine[0], self.first[0], second)

    def share_direct(self, *wait):
        place = self.place
        mine, at = self.column(*wait)
        terms = [
            place.permute(at(place.chip ^ k), (2 * k, 2 * k)) for k in range(place.chips - 1, 0, -1)
        ]
        return add(at(place.chip), *terms)


class Replication:
    def __init__(self, place, share, direct=False):
        self.place = place
        if direct:
            size = place.shards
            self.blocks = [share] + [None] * 3
            for mask in (3, 1, 2):
                self.blocks[mask] = place.permute(share, (mask * size, mask * size))
            self.owner = lambda n: place.grp ^ n
        else:
            self.blocks = [share, place.swap_grp(share, 0), None, None]
            self.owner = place.slot_grp

    def far(self, *wait):
        pair = jnp.stack([self.blocks[0], after(self.blocks[1], *wait)])
        rest = self.place.swap_grp(pair, 1)
        self.blocks[2:] = [rest[0], rest[1]]
        return rest

    def result(self):
        ordered = []
        for g in range(self.place.groups):
            block = self.blocks[0]
            for n in range(1, self.place.groups):
                block = jnp.where(self.owner(n) == g, self.blocks[n], block)
            ordered.append(block.astype(jnp.float32))
        return ordered


def on_device_permutes(
    tokens,
    segment_ids,
    keep_flag,
    cotangent,
    w_qkv,
    b_query,
    b_value,
    w_attn_out,
    b_attn_out,
    norm1_gain,
    norm1_bias,
    w_in,
    b_in,
    w_out,
    b_out,
    norm2_gain,
    norm2_bias,
    *,
    groups,
    shards,
):
    place = Place(groups, shards)
    _, length, width = tokens.shape
    rows = tokens[0]
    seg_row = segment_ids.reshape(1, length)
    seg_col = segment_ids.reshape(length, 1)
    keep = keep_flag.reshape(length, 1).astype(jnp.float32)
    pairs = width // LANES

    c1 = Gather(place, w_qkv)
    c2 = Gather(place, jnp.concatenate([w_in, w_attn_out], 1))
    c3 = Gather(place, w_out)
    c1.chips_near()
    c1.chips_far()
    joined = c1.join()
    c1.near()
    small = Vectors(
        place,
        (b_query, b_value, b_attn_out, norm1_gain, norm1_bias, b_out, norm2_gain, norm2_bias, b_in),
        c1.pair[1],
    )
    vectors, bias_in, qkv_bias = small.unpack()
    c2.chips_near(joined)
    c1.cross(0)
    c2.chips_far()
    far = c1.far(c2.rest[0], vectors)
    c1.cross(1, 2)
    c1.cross(3)
    c2.join(far)
    c2.near()
    blank = jnp.ones((1, width), jnp.float32)
    qkv_scale = jnp.concatenate([blank / math.sqrt(HD), blank, blank], 1)

    mixed, full_qkv = project_qkv(place, rows, Window(c1, 0, w_qkv.shape[1]), qkv_bias, qkv_scale)
    c3.chips_near(mixed)
    c2.cross(0, wait=(mixed,))
    share_of = (pairs // 2 - pairs // 8, pairs // 4, pairs // 2 - pairs // 8)
    forward = None
    start = 0
    for n, count in enumerate(share_of):
        wait = (c2.held[3],) if n == 2 else ()
        forward = attention_forward(
            after(mixed, *wait) if wait else mixed, seg_col, seg_row, start, count, forward
        )
        start += count
        done = forward[1]
        if n == 0:
            c2.far(done)
            c3.chips_far(done)
            c2.cross(1, 2, wait=(done,))
        if n == 1:
            c3.join(done)
            c3.near()
            c2.cross(3, wait=(done,))
    contexts, lse = forward
    normed, scale_one, normed_low, full_attn = project_out(
        place, contexts, Window(c2, w_in.shape[1], w_attn_out.shape[1]), rows, vectors
    )
    c3.far(normed_low)
    c3.cross(0, 1, 2, wait=(normed_low,))
    hidden, slope, full_in = feed_in(
        place, after(normed_low, c3.held[1]), Window(c2, 0, w_in.shape[1]), bias_in
    )
    c3.cross(3, wait=(hidden,))
    layer_out, second_grad, out_low, second_sums, full_out = feed_out(
        place, hidden, Window(c3, 0, w_out.shape[1]), normed, cotangent[0], keep, vectors
    )

    r_out = Reduction(place, [(hidden, out_low)], False, "out")
    pre_low, bias_in_grad = feed_out_back(after(out_low, r_out.made), full_out, slope)
    near = r_out.near(pre_low)
    r_in = Reduction(place, [(normed_low, pre_low)], True, "in", near)
    first_grad, attn_low, context_grad, first_sums = feed_in_back(
        after(pre_low, r_in.made), full_in, second_grad, normed, scale_one, vectors, full_attn
    )
    quarter = pairs // 4

    def back(start, at, before=None, *wait):
        return attention_backward(
            mixed,
            contexts,
            after(context_grad, *wait) if wait else context_grad,
            seg_col,
            seg_row,
            lse,
            start,
            quarter,
            at,
            2 * quarter,
            before,
        )

    middle = r_out.middle(first_grad)
    near = r_in.near(first_grad)
    part = back(0, 0, None, middle, near)
    along = r_out.along(part[1])
    low_a, late_a = back(quarter, quarter, part, along)
    middle = r_in.middle(late_a)
    along = r_out.along_far(late_a)
    r_a = Reduction(place, [(contexts, attn_low), (rows, low_a)], True, "a", middle, along)
    part = back(2 * quarter, 0, None, r_a.made)
    share_out = r_out.share(part[1])
    along = r_in.along(part[1])
    near = r_a.near(part[1])
    low_b, late_b = back(3 * quarter, quarter, part, share_out, along, near)
    middle = r_a.middle(late_b)
    along = r_in.along_far(late_b)
    sums = pack_sums(late_a, late_b, first_sums, second_sums, bias_in_grad)
    r_b = Reduction(place, [(rows, low_b)], True, "b", middle, along, sums=sums)
    along = r_a.along(r_b.made)
    share_in = r_in.share(r_b.made)
    inner = share_in.shape[1] // groups
    joined = jnp.concatenate(
        [share_out] + [share_in[:, n * inner : (n + 1) * inner] for n in range(groups)]
    )
    all_ffn = Replication(place, joined)
    near = r_b.near(along, joined)
    input_grad = project_qkv_back((low_a, after(low_b, near)), full_qkv, first_grad)
    middle = r_b.middle(input_grad)
    along = r_a.along_far(middle)
    all_ffn.far(middle)
    share_b = r_b.share_direct()
    all_a = Replication(place, r_a.share(along))
    all_b = Replication(place, share_b, direct=True)
    all_a.far()

    parts_a, parts_b = all_a.result(), all_b.result()
    small = [
        block[-16, n * LANES : (n + 1) * LANES] for block in parts_b for n in range(3)
    ]
    inner_mine = jnp.concatenate(small[B_IN:])
    parts_b = [block[:-16] for block in parts_b]
    heads = parts_b[0].shape[1] // 3
    skip = parts_a[0].shape[1] - 3 * heads
    w_attn_grad = jnp.concatenate([block[:, :skip] for block in parts_a], 1)
    parts_a = [block[:, skip:] for block in parts_a]
    w_qkv_grad = jnp.concatenate(
        [
            block[:, n * heads : (n + 1) * heads]
            for n in range(3)
            for half in (parts_a, parts_b)
            for block in half
        ],
        1,
    )
    parts = all_ffn.result()
    height = share_out.shape[0]
    w_out_grad = jnp.concatenate([block[:height] for block in parts], 1)
    size = share_in.shape[0]
    w_in_grad = jnp.concatenate(
        [
            block[height + n * size : height + (n + 1) * size]
            for block in parts
            for n in range(groups)
        ],
        1,
    )
    return (
        layer_out[None],
        input_grad[None],
        w_qkv_grad,
        small[B_QUERY],
        small[B_VALUE],
        w_attn_grad,
        small[B_ATTN],
        small[GAIN_ONE],
        small[SHIFT_ONE],
        w_in_grad,
        inner_mine,
        w_out_grad,
        small[B_OUT],
        small[GAIN_TWO],
        small[SHIFT_TWO],
    )


def solution(mesh):
    groups, shards = mesh.shape["grp"], mesh.shape["shard"]
    if groups == 4 and shards == 8:
        body = functools.partial(on_device_permutes, groups=groups, shards=shards)
    else:
        body = on_device
    return jax.shard_map(
        body,
        mesh=mesh,
        in_specs=(
            P(("grp", "shard"), None, None),
            P(("grp", "shard"), None),
            P(("grp", "shard"), None),
            P(("grp", "shard"), None, None),
            P("shard", "grp"),
            P("shard"),
            P("shard"),
            P("shard", "grp"),
            P("shard"),
            P("shard"),
            P("shard"),
            P("shard", "grp"),
            P("shard"),
            P("shard", "grp"),
            P("shard"),
            P("shard"),
            P("shard"),
        ),
        out_specs=(
            P(("grp", "shard"), None, None),
            P(("grp", "shard"), None, None),
            P("shard", None),
            P("shard"),
            P("shard"),
            P("shard", None),
            P("shard"),
            P("shard"),
            P("shard"),
            P("shard", None),
            P("shard"),
            P("shard", None),
            P("shard"),
            P("shard"),
            P("shard"),
        ),
        check_vma=False,
    )
```

```python
import functools
import math

import jax
import jax.numpy as jnp
from jax import lax
from jax.experimental import pallas as pl
from jax.experimental.pallas import tpu as pltpu
from jax.sharding import PartitionSpec as P

H = 16
HD = 64


masked_score = -1e30
epsilon = 1e-05


def norm_layer(rows, gain_row, shift_row):
    row_mean = jnp.mean(rows, -1, keepdims=True)
    centered = rows - row_mean
    row_var = jnp.mean(centered * centered, -1, keepdims=True)
    return centered * lax.rsqrt(row_var + epsilon) * gain_row + shift_row


def gelu_exact(values):
    return 0.5 * values * (1.0 + lax.erf(values * (1.0 / math.sqrt(2.0))))


def contract_rows(left, right):
    return lax.dot_general(
        left, right, (((0,), (0,)), ((), ())), preferred_element_type=jnp.float32
    )


def contract_cols(left, right):
    return lax.dot_general(
        left, right, (((1,), (1,)), ((), ())), preferred_element_type=jnp.float32
    )


def attend_forward(queries, key_rows, value_rows, segment_row, block_rows):
    length, model_width = queries.shape
    scaling = 1.0 / math.sqrt(HD)
    key_heads = key_rows.reshape(length, H, HD)
    value_heads = value_rows.reshape(length, H, HD)
    query_blocks = queries.reshape(length // block_rows, block_rows, H, HD)
    segment_blocks = segment_row.reshape(length // block_rows, block_rows)

    def one_block(pieces):
        query_part, segment_part = pieces
        scores = (
            jnp.einsum("qhd,khd->hqk", query_part, key_heads, preferred_element_type=jnp.float32)
            * scaling
        )
        allowed = segment_part[:, None] == segment_row[None, :]
        scores = jnp.where(allowed[None], scores, masked_score)
        row_max = jnp.max(scores, -1, keepdims=True)
        powers = jnp.exp(scores - row_max)
        totals = jnp.sum(powers, -1, keepdims=True)
        attn_probs = (powers / totals).astype(jnp.bfloat16)
        context = jnp.einsum(
            "hqk,khd->qhd", attn_probs, value_heads, preferred_element_type=jnp.float32
        )
        return (
            context.reshape(block_rows, model_width).astype(jnp.bfloat16),
            (row_max + jnp.log(totals))[:, :, 0],
        )

    contexts, log_sums = lax.map(one_block, (query_blocks, segment_blocks))
    return (contexts.reshape(length, model_width), log_sums)


def attend_backward(queries, key_rows, value_rows, segment_row, log_sums, context_grad, block_rows):
    length, model_width = queries.shape
    scaling = 1.0 / math.sqrt(HD)
    key_heads = key_rows.reshape(length, H, HD)
    value_heads = value_rows.reshape(length, H, HD)
    query_blocks = queries.reshape(length // block_rows, block_rows, H, HD)
    segment_blocks = segment_row.reshape(length // block_rows, block_rows)
    grad_blocks = context_grad.reshape(length // block_rows, block_rows, H, HD)

    def one_block(running, pieces):
        key_acc, value_acc = running
        query_part, segment_part, lse_part, grad_part = pieces
        scores = (
            jnp.einsum("qhd,khd->hqk", query_part, key_heads, preferred_element_type=jnp.float32)
            * scaling
        )
        allowed = segment_part[:, None] == segment_row[None, :]
        scores = jnp.where(allowed[None], scores, masked_score)
        probs = jnp.exp(scores - lse_part[:, :, None])
        prob_low = probs.astype(jnp.bfloat16)
        prob_grad = jnp.einsum(
            "qhd,khd->hqk", grad_part, value_heads, preferred_element_type=jnp.float32
        )
        row_dot = jnp.sum(prob_grad * probs, -1, keepdims=True)
        score_grad = (probs * (prob_grad - row_dot)).astype(jnp.bfloat16)
        query_grad = (
            jnp.einsum("hqk,khd->qhd", score_grad, key_heads, preferred_element_type=jnp.float32)
            * scaling
        )
        key_acc = (
            key_acc
            + jnp.einsum("hqk,qhd->khd", score_grad, query_part, preferred_element_type=jnp.float32)
            * scaling
        )
        value_acc = value_acc + jnp.einsum(
            "hqk,qhd->khd", prob_low, grad_part, preferred_element_type=jnp.float32
        )
        return ((key_acc, value_acc), query_grad.reshape(block_rows, model_width))

    empty_acc = jnp.zeros((length, H, HD), jnp.float32)
    (key_grad, value_grad), query_grads = lax.scan(
        one_block, (empty_acc, empty_acc), (query_blocks, segment_blocks, log_sums, grad_blocks)
    )
    return (
        query_grads.reshape(length, model_width),
        key_grad.reshape(length, model_width),
        value_grad.reshape(length, model_width),
    )


def on_device(
    tokens,
    segment_ids,
    keep_flag,
    cotangent,
    w_qkv,
    b_query,
    b_value,
    w_attn_out,
    b_attn_out,
    norm1_gain,
    norm1_bias,
    w_in,
    b_in,
    w_out,
    b_out,
    norm2_gain,
    norm2_bias,
):
    seq_count, length, model_width = tokens.shape
    block_rows = min(512, length)
    within = (
        lax.all_gather(w_qkv, "shard", axis=0, tiled=True),
        lax.all_gather(w_attn_out, "shard", axis=0, tiled=True),
        lax.all_gather(w_in, "shard", axis=0, tiled=True),
        lax.all_gather(w_out, "shard", axis=0, tiled=True),
        lax.all_gather(b_query, "shard", axis=0, tiled=True),
        lax.all_gather(b_value, "shard", axis=0, tiled=True),
        lax.all_gather(b_attn_out, "shard", axis=0, tiled=True),
        lax.all_gather(norm1_gain, "shard", axis=0, tiled=True),
        lax.all_gather(norm1_bias, "shard", axis=0, tiled=True),
        lax.all_gather(b_in, "shard", axis=0, tiled=True),
        lax.all_gather(b_out, "shard", axis=0, tiled=True),
        lax.all_gather(norm2_gain, "shard", axis=0, tiled=True),
        lax.all_gather(norm2_bias, "shard", axis=0, tiled=True),
    )
    full_qkv, full_attn, full_in, full_out = (
        lax.all_gather(within[0], "grp", axis=1, tiled=True),
        lax.all_gather(within[1], "grp", axis=1, tiled=True),
        lax.all_gather(within[2], "grp", axis=1, tiled=True),
        lax.all_gather(within[3], "grp", axis=1, tiled=True),
    )
    (
        bias_query,
        bias_value,
        bias_attn,
        gain_one,
        shift_one,
        bias_in,
        bias_out,
        gain_two,
        shift_two,
    ) = [piece.astype(jnp.float32) for piece in within[4:]]
    flat_rows = tokens.reshape(seq_count * length, model_width)
    mixed_qkv = jnp.dot(flat_rows, full_qkv, preferred_element_type=jnp.float32)
    queries = (mixed_qkv[:, :model_width] + bias_query).astype(jnp.bfloat16)
    key_rows = mixed_qkv[:, model_width : 2 * model_width].astype(jnp.bfloat16)
    value_rows = (mixed_qkv[:, 2 * model_width :] + bias_value).astype(jnp.bfloat16)
    query_seqs = queries.reshape(seq_count, length, model_width)
    key_seqs = key_rows.reshape(seq_count, length, model_width)
    value_seqs = value_rows.reshape(seq_count, length, model_width)

    def forward_sequence(pieces):
        return attend_forward(pieces[0], pieces[1], pieces[2], pieces[3], block_rows)

    contexts, log_sums = lax.map(forward_sequence, (query_seqs, key_seqs, value_seqs, segment_ids))
    contexts = contexts.reshape(seq_count * length, model_width)
    attended = jnp.dot(contexts, full_attn, preferred_element_type=jnp.float32) + bias_attn
    first_sum = flat_rows.astype(jnp.float32) + attended
    normed_one, norm_one_back = jax.vjp(norm_layer, first_sum, gain_one, shift_one)
    normed_low = normed_one.astype(jnp.bfloat16)
    hidden_pre = jnp.dot(normed_low, full_in, preferred_element_type=jnp.float32) + bias_in
    hidden, gelu_back = jax.vjp(gelu_exact, hidden_pre)
    hidden_low = hidden.astype(jnp.bfloat16)
    second_sum = normed_one + (
        jnp.dot(hidden_low, full_out, preferred_element_type=jnp.float32) + bias_out
    )
    result, norm_two_back = jax.vjp(norm_layer, second_sum, gain_two, shift_two)
    layer_out = result.astype(jnp.bfloat16).reshape(seq_count, length, model_width)
    again = (
        lax.all_gather(w_qkv, "shard", axis=0, tiled=True),
        lax.all_gather(w_attn_out, "shard", axis=0, tiled=True),
        lax.all_gather(w_in, "shard", axis=0, tiled=True),
        lax.all_gather(w_out, "shard", axis=0, tiled=True),
    )
    back_qkv, back_attn, back_in, back_out = (
        lax.all_gather(again[0], "grp", axis=1, tiled=True),
        lax.all_gather(again[1], "grp", axis=1, tiled=True),
        lax.all_gather(again[2], "grp", axis=1, tiled=True),
        lax.all_gather(again[3], "grp", axis=1, tiled=True),
    )
    masked_cot = cotangent.astype(jnp.float32).reshape(
        seq_count * length, model_width
    ) * keep_flag.reshape(seq_count * length, 1).astype(jnp.float32)
    second_grad, gain_two_grad, shift_two_grad = norm_two_back(masked_cot)
    bias_out_grad = jnp.sum(second_grad, 0)
    out_low = second_grad.astype(jnp.bfloat16)
    w_out_grad = contract_rows(hidden_low, out_low)
    hidden_grad = contract_cols(out_low, back_out)
    (pre_grad,) = gelu_back(hidden_grad)
    bias_in_grad = jnp.sum(pre_grad, 0)
    pre_low = pre_grad.astype(jnp.bfloat16)
    w_in_grad = contract_rows(normed_low, pre_low)
    normed_grad = second_grad + contract_cols(pre_low, back_in)
    first_grad, gain_one_grad, shift_one_grad = norm_one_back(normed_grad)
    bias_attn_grad = jnp.sum(first_grad, 0)
    attn_low = first_grad.astype(jnp.bfloat16)
    w_attn_grad = contract_rows(contexts, attn_low)
    context_grad = contract_cols(attn_low, back_attn).astype(jnp.bfloat16)

    def backward_sequence(pieces):
        return attend_backward(
            pieces[0], pieces[1], pieces[2], pieces[3], pieces[4], pieces[5], block_rows
        )

    query_grad, key_grad, value_grad = lax.map(
        backward_sequence,
        (
            query_seqs,
            key_seqs,
            value_seqs,
            segment_ids,
            log_sums,
            context_grad.reshape(seq_count, length, model_width),
        ),
    )
    query_grad = query_grad.reshape(seq_count * length, model_width)
    key_grad = key_grad.reshape(seq_count * length, model_width)
    value_grad = value_grad.reshape(seq_count * length, model_width)
    bias_query_grad = jnp.sum(query_grad, 0)
    bias_value_grad = jnp.sum(value_grad, 0)
    qkv_low = jnp.concatenate([query_grad, key_grad, value_grad], 1).astype(jnp.bfloat16)
    w_qkv_grad = contract_rows(flat_rows, qkv_low)
    input_grad = first_grad + contract_cols(qkv_low, back_qkv)
    reduced = (
        lax.psum_scatter(
            w_qkv_grad.astype(jnp.bfloat16), "shard", scatter_dimension=0, tiled=True
        ).astype(jnp.float32),
        lax.psum_scatter(
            bias_query_grad.astype(jnp.bfloat16), "shard", scatter_dimension=0, tiled=True
        ).astype(jnp.float32),
        lax.psum_scatter(
            bias_value_grad.astype(jnp.bfloat16), "shard", scatter_dimension=0, tiled=True
        ).astype(jnp.float32),
        lax.psum_scatter(
            w_attn_grad.astype(jnp.bfloat16), "shard", scatter_dimension=0, tiled=True
        ).astype(jnp.float32),
        lax.psum_scatter(
            bias_attn_grad.astype(jnp.bfloat16), "shard", scatter_dimension=0, tiled=True
        ).astype(jnp.float32),
        lax.psum_scatter(
            gain_one_grad.astype(jnp.bfloat16), "shard", scatter_dimension=0, tiled=True
        ).astype(jnp.float32),
        lax.psum_scatter(
            shift_one_grad.astype(jnp.bfloat16), "shard", scatter_dimension=0, tiled=True
        ).astype(jnp.float32),
        lax.psum_scatter(
            w_in_grad.astype(jnp.bfloat16), "shard", scatter_dimension=0, tiled=True
        ).astype(jnp.float32),
        lax.psum_scatter(
            bias_in_grad.astype(jnp.bfloat16), "shard", scatter_dimension=0, tiled=True
        ).astype(jnp.float32),
        lax.psum_scatter(
            w_out_grad.astype(jnp.bfloat16), "shard", scatter_dimension=0, tiled=True
        ).astype(jnp.float32),
        lax.psum_scatter(
            bias_out_grad.astype(jnp.bfloat16), "shard", scatter_dimension=0, tiled=True
        ).astype(jnp.float32),
        lax.psum_scatter(
            gain_two_grad.astype(jnp.bfloat16), "shard", scatter_dimension=0, tiled=True
        ).astype(jnp.float32),
        lax.psum_scatter(
            shift_two_grad.astype(jnp.bfloat16), "shard", scatter_dimension=0, tiled=True
        ).astype(jnp.float32),
    )
    summed = (
        lax.psum(reduced[0].astype(jnp.bfloat16), "grp").astype(jnp.float32),
        lax.psum(reduced[1].astype(jnp.bfloat16), "grp").astype(jnp.float32),
        lax.psum(reduced[2].astype(jnp.bfloat16), "grp").astype(jnp.float32),
        lax.psum(reduced[3].astype(jnp.bfloat16), "grp").astype(jnp.float32),
        lax.psum(reduced[4].astype(jnp.bfloat16), "grp").astype(jnp.float32),
        lax.psum(reduced[5].astype(jnp.bfloat16), "grp").astype(jnp.float32),
        lax.psum(reduced[6].astype(jnp.bfloat16), "grp").astype(jnp.float32),
        lax.psum(reduced[7].astype(jnp.bfloat16), "grp").astype(jnp.float32),
        lax.psum(reduced[8].astype(jnp.bfloat16), "grp").astype(jnp.float32),
        lax.psum(reduced[9].astype(jnp.bfloat16), "grp").astype(jnp.float32),
        lax.psum(reduced[10].astype(jnp.bfloat16), "grp").astype(jnp.float32),
        lax.psum(reduced[11].astype(jnp.bfloat16), "grp").astype(jnp.float32),
        lax.psum(reduced[12].astype(jnp.bfloat16), "grp").astype(jnp.float32),
    )
    return (
        layer_out,
        input_grad.reshape(seq_count, length, model_width),
        summed[0],
        summed[1],
        summed[2],
        summed[3],
        summed[4],
        summed[5],
        summed[6],
        summed[7],
        summed[8],
        summed[9],
        summed[10],
        summed[11],
        summed[12],
    )


NT = (((1,), (1,)), ((), ()))
NN = (((1,), (0,)), ((), ()))
TN = (((0,), (0,)), ((), ()))
LANES = 128
AXES = ("grp", "shard")
CHEAP = pl.CostEstimate(flops=1024, bytes_accessed=1024, transcendentals=0)


def mxu(left, right, dims):
    return lax.dot_general(left, right, dims, preferred_element_type=jnp.float32)


def params(megabytes=60):
    return pltpu.CompilerParams(vmem_limit_bytes=megabytes << 20)


def attention_forward_kernel(q_ref, k_ref, v_ref, seg_col, seg_row, out_ref, lse_ref, *, rows):
    length = q_ref.shape[0]
    first = lax.broadcasted_iota(jnp.int32, (1, LANES), 1) < HD
    keys = k_ref[...]
    values = v_ref[...]
    zero = jnp.zeros_like(keys)
    head_keys = (jnp.where(first, keys, zero), jnp.where(first, zero, keys))
    key_segments = seg_col[...]
    for block in range(length // rows):
        here = pl.ds(block * rows, rows)
        q = q_ref[here, :]
        allowed = key_segments == seg_row[:, here]
        outs = []
        for head in range(2):
            scores = mxu(head_keys[head], q, NT)
            scores = jnp.where(allowed, scores, masked_score)
            top = jnp.max(scores, 0, keepdims=True)
            powers = jnp.exp(scores - top)
            total = jnp.sum(powers, 0, keepdims=True)
            part = mxu(powers.astype(jnp.bfloat16), values, TN)
            outs.append(part * jnp.transpose(jnp.broadcast_to(1.0 / total, (LANES, rows))))
            lse_ref[0, head : head + 1, here] = top + jnp.log(total)
        out_ref[here, :] = jnp.where(first, outs[0], outs[1]).astype(jnp.bfloat16)


def attention_forward(qkv, seg_col, seg_row, start, pairs, before=None):
    length, width = qkv.shape[0], qkv.shape[1] // 3
    total = width // LANES
    rows = min(512, length)
    anywhere = pl.BlockSpec(memory_space=pl.ANY)

    def pair(part):
        return pl.BlockSpec((length, LANES), lambda j: (0, part * total + start + j))

    def body(q_ref, k_ref, v_ref, seg_c, seg_r, *refs):
        attention_forward_kernel(q_ref, k_ref, v_ref, seg_c, seg_r, *refs[-2:], rows=rows)

    return pl.pallas_call(
        body,
        grid=(pairs,),
        in_specs=[
            pair(0),
            pair(1),
            pair(2),
            pl.BlockSpec((length, 1), lambda j: (0, 0)),
            pl.BlockSpec((1, length), lambda j: (0, 0)),
        ]
        + [anywhere] * (0 if before is None else 2),
        out_specs=[
            pl.BlockSpec((length, LANES), lambda j: (0, start + j)),
            pl.BlockSpec((1, 2, length), lambda j: (start + j, 0, 0)),
        ],
        out_shape=[
            jax.ShapeDtypeStruct((length, width), jnp.bfloat16),
            jax.ShapeDtypeStruct((total, 2, length), jnp.float32),
        ],
        input_output_aliases={} if before is None else {5: 0, 6: 1},
        compiler_params=params(60),
        cost_estimate=CHEAP,
        name="attn_fwd",
    )(qkv, qkv, qkv, seg_col, seg_row, *(() if before is None else before))


def attention_backward_kernel(
    q_ref, k_ref, v_ref, o_ref, do_ref, seg_col, seg_row, lse_ref, grad_ref, sum_ref, *, rows
):
    length = q_ref.shape[0]
    lane = lax.broadcasted_iota(jnp.int32, (1, LANES), 1)
    first = lane < HD
    pick = (
        lax.broadcasted_iota(jnp.int32, (8, LANES), 0)
        == lax.broadcasted_iota(jnp.int32, (8, LANES), 1) // HD
    ).astype(jnp.float32)
    keys = k_ref[...]
    values = v_ref[...]
    zero = jnp.zeros_like(keys)
    head_keys = (jnp.where(first, keys, zero), jnp.where(first, zero, keys))
    head_values = (jnp.where(first, values, zero), jnp.where(first, zero, values))
    key_segments = seg_col[...]
    key_sum = [None, None]
    value_sum = [None, None]
    query_total = jnp.zeros((1, LANES), jnp.float32)
    for block in range(length // rows):
        here = pl.ds(block * rows, rows)
        q = q_ref[here, :]
        do = do_ref[here, :]
        allowed = key_segments == seg_row[:, here]
        dots = lax.dot_general(
            pick,
            do.astype(jnp.float32) * o_ref[here, :].astype(jnp.float32),
            NT,
            precision=lax.Precision.HIGHEST,
            preferred_element_type=jnp.float32,
        )
        parts = []
        for head in range(2):
            scores = mxu(head_keys[head], q, NT)
            scores = jnp.where(allowed, scores, masked_score)
            probs = jnp.exp(scores - lse_ref[0, head : head + 1, here])
            prob_grad = mxu(head_values[head], do, NT)
            score_grad = (probs * (prob_grad - dots[head : head + 1, :])).astype(jnp.bfloat16)
            value_part = mxu(probs.astype(jnp.bfloat16), do, NN)
            key_part = mxu(score_grad, q, NN)
            value_sum[head] = value_part if block == 0 else value_sum[head] + value_part
            key_sum[head] = key_part if block == 0 else key_sum[head] + key_part
            parts.append(mxu(score_grad, keys, TN))
        query_grad = jnp.where(first, parts[0], parts[1]) * (1.0 / math.sqrt(HD))
        query_total = query_total + jnp.sum(query_grad, 0, keepdims=True)
        grad_ref[0, here, :] = query_grad.astype(jnp.bfloat16)
    grad_ref[1, :, :] = jnp.where(first, key_sum[0], key_sum[1]).astype(jnp.bfloat16)
    value_grad = jnp.where(first, value_sum[0], value_sum[1])
    grad_ref[2, :, :] = value_grad.astype(jnp.bfloat16)
    sum_ref[0:1, :] = query_total
    sum_ref[1:2, :] = jnp.sum(value_grad, 0, keepdims=True)


def attention_backward(qkv, out, out_grad, seg_col, seg_row, lse, start, pairs):
    length, width = out.shape
    total = width // LANES
    rows = min(256, length)

    def pair(part):
        return pl.BlockSpec((length, LANES), lambda j: (0, part * total + start + j))

    return pl.pallas_call(
        functools.partial(attention_backward_kernel, rows=rows),
        grid=(pairs,),
        in_specs=[
            pair(0),
            pair(1),
            pair(2),
            pair(0),
            pair(0),
            pl.BlockSpec((length, 1), lambda j: (0, 0)),
            pl.BlockSpec((1, length), lambda j: (0, 0)),
            pl.BlockSpec((1, 2, length), lambda j: (j + start, 0, 0)),
        ],
        out_specs=[
            pl.BlockSpec((3, length, LANES), lambda j: (0, 0, j)),
            pl.BlockSpec((2, LANES), lambda j: (0, j)),
        ],
        out_shape=[
            jax.ShapeDtypeStruct((3, length, pairs * LANES), jnp.bfloat16),
            jax.ShapeDtypeStruct((2, pairs * LANES), jnp.float32),
        ],
        compiler_params=params(60),
        cost_estimate=CHEAP,
        name="attn_bwd",
    )(qkv, qkv, qkv, out, out_grad, seg_col, seg_row, lse)


class Place:
    def __init__(self, groups, shards):
        self.groups = groups
        self.shards = shards
        self.chips = shards // 2
        self.grp = lax.axis_index("grp")
        self.shard = lax.axis_index("shard")
        self.core = self.shard % 2
        self.chip = self.shard // 2
        self.scalars = jnp.stack([self.core, self.chip, self.grp]).astype(jnp.int32)

    def permute(self, array, mask_of_core):
        pairs = [(i, i ^ mask_of_core[i % 2]) for i in range(self.groups * self.shards)]
        return lax.ppermute(array, AXES, pairs)

    def swap_core(self, array):
        return self.permute(array, (1, 1))

    def swap_grp(self, array, step):
        masks = (self.shards, 2 * self.shards)
        return self.permute(array, masks if step == 0 else masks[::-1])

    def swap_chip(self, array, step):
        masks = (2, 4)
        return self.permute(array, masks if step == 0 else masks[::-1])

    def slot_chip(self, slot):
        return self.chip ^ turn(slot, self.core)

    def slot_grp(self, slot):
        return self.grp ^ turn(slot, self.core)


def turn(slot, core):
    if isinstance(slot, int):
        return slot if slot in (0, 3) else jnp.where(core == 0, slot, 3 - slot)
    return jnp.where((core == 0) | (slot == 0) | (slot == 3), slot, 3 - slot)


def after(value, *others):
    return lax.optimization_barrier((value, *others))[0]


class Gather:
    def __init__(self, place, piece):
        self.place = place
        self.piece = piece
        self.held = [None] * 4
        self.crossed = [None] * 4

    def chips_near(self, *wait):
        piece = after(self.piece, *wait) if wait else self.piece
        self.pair = [piece, self.place.swap_chip(piece, 0)]
        return self.pair[1]

    def chips_far(self, *wait):
        pair = jnp.stack([self.pair[0], after(self.pair[1], *wait)])
        self.rest = [pair, self.place.swap_chip(pair, 1)]
        return self.rest[1]

    def join(self, *wait):
        rest = after(self.rest[1], *wait) if wait else self.rest[1]
        self.held[0] = jnp.concatenate([self.rest[0], rest])
        return self.held[0]

    def near(self):
        self.held[1] = self.place.swap_grp(self.held[0], 0)
        self.held[2] = self.place.swap_grp(self.held[0], 1)
        return self.held[2]

    def far(self, *wait):
        first = after(self.held[1], *wait) if wait else self.held[1]
        self.held[3] = self.place.swap_grp(first, 1)
        return self.held[3]

    def cross(self, *which, wait=()):
        for n in which:
            piece = after(self.held[n], *wait) if wait else self.held[n]
            self.crossed[n] = self.place.swap_core(piece)

    def pieces(self):
        return self.held + self.crossed


class Window:
    def __init__(self, gather, start, cols):
        self.arrays = gather.pieces()
        self.start, self.cols = start, cols
        chips, rows, _ = self.arrays[0].shape
        self.chips, self.rows = chips, rows


def fetch(where, window, refs, whole, sem, by):
    rows, cols, chips = window.rows, window.cols, window.chips
    for slot in range(4):
        for side in range(2):
            core = where[0] ^ side
            ref = refs[4 * side + slot]
            distance = turn(slot, core)
            col = pl.multiple_of((where[2] ^ distance) * cols, LANES)
            for k in range(chips):
                row = ((where[1] ^ turn(k, core)) * 2 + core) * rows
                pltpu.make_async_copy(
                    ref.at[k, :, pl.ds(window.start, cols)],
                    whole.at[pl.ds(pl.multiple_of(row, rows), rows), pl.ds(col, cols)],
                    sem.at[distance if by == "grp" else 0],
                ).start()


def weight_call(place, kernel, window, inputs, in_specs, outs, out_specs, steps, by, name, flops, mb=60):
    cols, groups = window.cols, place.groups
    pieces = window.arrays
    shape = (window.chips * 2 * window.rows, groups * cols)
    slots = {"grp": groups, "all": 1}[by]
    anywhere = pl.BlockSpec(memory_space=pl.ANY)

    def body(where, *refs):
        taken, refs = refs[: len(pieces)], refs[len(pieces) :]
        *refs, written, weight, sem, out_sem = refs
        step = pl.program_id(0)

        @pl.when(step == 0)
        def _():
            fetch(where, window, taken, weight, sem, by)

        def ready():
            if by == "all":

                @pl.when(step == 0)
                def _():
                    pltpu.make_async_copy(weight, weight, sem.at[0]).wait()
                    pltpu.make_async_copy(weight, written, out_sem.at[0]).start()

            else:
                at = pl.ds(pl.multiple_of((where[2] ^ step) * cols, LANES), cols)
                view = weight.at[:, at]
                pltpu.make_async_copy(view, view, sem.at[step]).wait()
                pltpu.make_async_copy(view, written.at[:, at], out_sem.at[step]).start()

        kernel(where, ready, weight, *refs)

        @pl.when(step == steps - 1)
        def _():
            for slot in range(slots):
                width = shape[1] // slots
                view = weight.at[:, pl.ds(slot * width, width)]
                pltpu.make_async_copy(view, view, out_sem.at[slot]).wait()

    total = sum(math.prod(x.shape) * x.dtype.itemsize for x in list(inputs) + list(outs))
    return pl.pallas_call(
        body,
        grid_spec=pltpu.PrefetchScalarGridSpec(
            num_scalar_prefetch=1,
            grid=(steps,),
            in_specs=[anywhere] * len(pieces) + in_specs,
            out_specs=out_specs + [anywhere],
            scratch_shapes=[
                pltpu.VMEM(shape, jnp.bfloat16),
                pltpu.SemaphoreType.DMA((slots,)),
                pltpu.SemaphoreType.DMA((slots,)),
            ],
        ),
        out_shape=outs + [shaped(shape, jnp.bfloat16)],
        compiler_params=params(mb),
        cost_estimate=CHEAP,
        name=name,
    )(place.scalars, *pieces, *inputs)


def plain_call(kernel, inputs, in_specs, outs, out_specs, steps, name, flops, mb=60):
    total = sum(math.prod(x.shape) * x.dtype.itemsize for x in list(inputs) + list(outs))
    return pl.pallas_call(
        kernel,
        grid=(steps,),
        in_specs=in_specs,
        out_specs=out_specs,
        out_shape=outs,
        compiler_params=params(mb),
        cost_estimate=CHEAP,
        name=name,
    )(*inputs)


TILE = 256


def row_tiles(width):
    return pl.BlockSpec((TILE, width), lambda i, *s: (i, 0))


def fixed(*shape):
    return pl.BlockSpec(shape, lambda i, *s: (0,) * len(shape))


def whole_once(shape):
    return pl.BlockSpec(shape, lambda i: (0,) * len(shape), pipeline_mode=pl.Buffered(1))


def shaped(shape, dtype):
    return jax.ShapeDtypeStruct(shape, dtype)


B_QUERY, B_VALUE, B_ATTN, GAIN_ONE, SHIFT_ONE, B_OUT, GAIN_TWO, SHIFT_TWO, B_IN = range(9)


def row(ref, n):
    return ref[n : n + 1, :]


class Vectors:
    def __init__(self, place, vectors, *wait):
        flat = jnp.concatenate([after(vectors[0], *wait), *vectors[1:]])
        own = jnp.pad(flat.reshape(-1, LANES), ((0, -(flat.shape[0] // LANES) % 16), (0, 0)))
        own = jnp.stack([own, place.swap_core(own)])
        pair = jnp.stack([own, place.swap_chip(own, 0)])
        self.slots = jnp.concatenate([pair, place.swap_chip(pair, 1)])
        self.place = place

    def unpack(self):
        place = self.place
        slots, sides, rows, lanes = self.slots.shape
        shards = place.shards

        def kernel(where, in_ref, rows_ref, inner_ref, qkv_ref):
            width = shards * lanes
            qkv_ref[...] = jnp.zeros_like(qkv_ref)
            for slot in range(slots):
                for side in range(sides):
                    core = where[0] ^ side
                    shard = (where[1] ^ turn(slot, where[0])) * 2 + core
                    part = in_ref[slot, side].astype(jnp.float32)
                    at = pl.multiple_of(shard * lanes, lanes)
                    rows_ref[:, pl.ds(at, lanes)] = part
                    qkv_ref[:, pl.ds(at, lanes)] = part[B_QUERY : B_QUERY + 1]
                    qkv_ref[:, pl.ds(2 * width + at, lanes)] = part[B_VALUE : B_VALUE + 1]
                    for n in range(4):
                        start = pl.multiple_of((shard * 4 + n) * lanes, lanes)
                        inner_ref[:, pl.ds(start, lanes)] = part[B_IN + n : B_IN + n + 1]

        in_vmem = pl.BlockSpec(memory_space=pltpu.VMEM)
        return pl.pallas_call(
            kernel,
            in_specs=[pl.BlockSpec(memory_space=pltpu.SMEM), in_vmem],
            out_specs=[in_vmem] * 3,
            out_shape=[
                shaped((rows, shards * lanes), jnp.float32),
                shaped((1, 4 * shards * lanes), jnp.float32),
                shaped((1, 3 * shards * lanes), jnp.float32),
            ],
            name="vectors",
        )(place.scalars, self.slots)


def pack_sums(late_a, late_b, first_sums, second_sums, inner_sums):
    width = first_sums.shape[1]
    half = late_a.shape[1]

    def kernel(a_ref, b_ref, one_ref, two_ref, inner_ref, out_ref):
        def place_of(n):
            return n // 3 * 8 + n % 3

        out_ref[...] = jnp.zeros_like(out_ref)
        for n in (B_QUERY, B_VALUE):
            at = place_of(n)
            out_ref[at : at + 1, 0:half] = a_ref[n : n + 1, :]
            out_ref[at : at + 1, half:width] = b_ref[n : n + 1, :]
        for n, source, line in (
            (GAIN_ONE, one_ref, 0),
            (SHIFT_ONE, one_ref, 1),
            (B_ATTN, one_ref, 2),
            (GAIN_TWO, two_ref, 0),
            (SHIFT_TWO, two_ref, 1),
            (B_OUT, two_ref, 2),
        ):
            at = place_of(n)
            out_ref[at : at + 1, :] = source[line : line + 1, :]
        for n in range(4):
            at = place_of(B_IN + n)
            for shard in range(width // LANES):
                start = (4 * shard + n) * LANES
                out_ref[at : at + 1, shard * LANES : (shard + 1) * LANES] = inner_ref[
                    :, start : start + LANES
                ]

    in_vmem = pl.BlockSpec(memory_space=pltpu.VMEM)
    return pl.pallas_call(
        kernel,
        in_specs=[in_vmem] * 5,
        out_specs=in_vmem,
        out_shape=shaped((32, width), jnp.float32),
        name="pack_sums",
    )(late_a, late_b, first_sums, second_sums, inner_sums)


def project_qkv(place, rows, window, bias, scale):
    length, width = rows.shape
    cols = window.cols

    def kernel(where, ready, weight, x_ref, bias_ref, scale_ref, out_ref):
        ready()
        at = pl.ds(pl.multiple_of((where[2] ^ pl.program_id(0)) * cols, LANES), cols)
        for tile in range(length // TILE):
            here = pl.ds(tile * TILE, TILE)
            mixed = mxu(x_ref[here, :], weight[:, at], NN) + bias_ref[:, at]
            mixed = mixed.astype(jnp.bfloat16).astype(jnp.float32) * scale_ref[:, at]
            out_ref[here, :] = mixed.astype(jnp.bfloat16)

    total = cols * place.groups
    return weight_call(
        place,
        kernel,
        window,
        (rows, bias, scale),
        [fixed(length, width), fixed(1, total), fixed(1, total)],
        [shaped((length, total), jnp.bfloat16)],
        [pl.BlockSpec((length, cols), lambda i, s: (0, i ^ s[2]))],
        place.groups,
        "grp",
        "qkv",
        2 * length * width * total,
    )


def norm_parts(rows):
    centered = rows - jnp.mean(rows, -1, keepdims=True)
    scale = lax.rsqrt(jnp.mean(centered * centered, -1, keepdims=True) + epsilon)
    return centered * scale, scale


def norm_back(grad, normed, scale):
    return scale * (
        grad
        - jnp.mean(grad, -1, keepdims=True)
        - normed * jnp.mean(grad * normed, -1, keepdims=True)
    )


def add_rows(sum_ref, *terms):
    @pl.when(pl.program_id(0) == 0)
    def _():
        sum_ref[...] = jnp.zeros_like(sum_ref)

    for n, term in enumerate(terms):
        sum_ref[n : n + 1, :] += jnp.sum(term, 0, keepdims=True)


def project_out(place, contexts, window, rows, vectors):
    length, width = rows.shape

    def kernel(where, ready, weight, c_ref, x_ref, v_ref, n_ref, r_ref, low_ref):
        ready()
        first_sum = mxu(c_ref[...], weight[...], NN) + row(v_ref, B_ATTN)
        first_sum = first_sum + x_ref[...].astype(jnp.float32)
        normed, scale = norm_parts(first_sum)
        n_ref[...] = normed
        r_ref[...] = jnp.broadcast_to(scale, r_ref.shape)
        low_ref[...] = (normed * row(v_ref, GAIN_ONE) + row(v_ref, SHIFT_ONE)).astype(jnp.bfloat16)

    return weight_call(
        place,
        kernel,
        window,
        (contexts, rows, vectors),
        [row_tiles(width), row_tiles(width), fixed(*vectors.shape)],
        [
            shaped((length, width), jnp.float32),
            shaped((length, LANES), jnp.float32),
            shaped((length, width), jnp.bfloat16),
        ],
        [row_tiles(width), row_tiles(LANES), row_tiles(width)],
        length // TILE,
        "all",
        "attn_out",
        2 * length * width * width,
    )


def feed_in(place, normed_low, window, bias):
    length, width = normed_low.shape
    cols = window.cols

    def kernel(where, ready, weight, x_ref, bias_ref, hid_ref, slope_ref):
        ready()
        at = pl.ds(pl.multiple_of((where[2] ^ pl.program_id(0)) * cols, LANES), cols)
        for tile in range(length // TILE):
            here = pl.ds(tile * TILE, TILE)
            pre = mxu(x_ref[here, :], weight[:, at], NN) + bias_ref[:, at]
            share = 0.5 + 0.5 * lax.erf(pre * (1.0 / math.sqrt(2.0)))
            bell = jnp.exp(-0.5 * pre * pre) * (1.0 / math.sqrt(2.0 * math.pi))
            hid_ref[here, :] = (pre * share).astype(jnp.bfloat16)
            slope_ref[here, :] = (share + pre * bell).astype(jnp.bfloat16)

    total = cols * place.groups
    block = pl.BlockSpec((length, cols), lambda i, s: (0, i ^ s[2]))
    return weight_call(
        place,
        kernel,
        window,
        (normed_low, bias),
        [fixed(length, width), fixed(1, total)],
        [shaped((length, total), jnp.bfloat16)] * 2,
        [block, block],
        place.groups,
        "grp",
        "feed_in",
        2 * length * width * total,
    )


def feed_out(place, hidden, window, normed, cot, keep, vectors):
    length, inner = hidden.shape
    width = normed.shape[1]

    def kernel(where, ready, weight, h_ref, n_ref, cot_ref, keep_ref, v_ref, *outs):
        out_ref, grad_ref, low_ref, sum_ref = outs
        ready()
        fed = mxu(h_ref[...], weight[...], NN)
        normed_one = n_ref[...] * row(v_ref, GAIN_ONE) + row(v_ref, SHIFT_ONE)
        second_sum = normed_one + (fed + row(v_ref, B_OUT))
        second, scale = norm_parts(second_sum)
        out_ref[...] = (second * row(v_ref, GAIN_TWO) + row(v_ref, SHIFT_TWO)).astype(jnp.bfloat16)
        masked = cot_ref[...].astype(jnp.float32) * keep_ref[...]
        grad = norm_back(masked * row(v_ref, GAIN_TWO), second, scale)
        grad_ref[...] = grad
        low_ref[...] = grad.astype(jnp.bfloat16)
        add_rows(sum_ref, masked * second, masked, grad)

    return weight_call(
        place,
        kernel,
        window,
        (hidden, normed, cot, keep, vectors),
        [row_tiles(inner), row_tiles(width), row_tiles(width), row_tiles(1), fixed(*vectors.shape)],
        [
            shaped((length, width), jnp.bfloat16),
            shaped((length, width), jnp.float32),
            shaped((length, width), jnp.bfloat16),
            shaped((8, width), jnp.float32),
        ],
        [row_tiles(width), row_tiles(width), row_tiles(width), fixed(8, width)],
        length // TILE,
        "all",
        "feed_out",
        2 * length * width * inner,
    )


def feed_out_back(out_low, weight, slope):
    length, width = out_low.shape
    inner = slope.shape[1]
    cols = min(1024, inner)

    def kernel(g_ref, w_ref, slope_ref, pre_ref, sum_ref):
        total = jnp.zeros((1, cols), jnp.float32)
        for tile in range(length // TILE):
            here = pl.ds(tile * TILE, TILE)
            grad = mxu(g_ref[here, :], w_ref[...], NT) * slope_ref[here, :].astype(jnp.float32)
            pre_ref[here, :] = grad.astype(jnp.bfloat16)
            total = total + jnp.sum(grad, 0, keepdims=True)
        sum_ref[...] = total

    block = pl.BlockSpec((length, cols), lambda i: (0, i))
    return plain_call(
        kernel,
        (out_low, weight, slope),
        [fixed(length, width), pl.BlockSpec((cols, width), lambda i: (i, 0)), block],
        [shaped((length, inner), jnp.bfloat16), shaped((1, inner), jnp.float32)],
        [block, pl.BlockSpec((1, cols), lambda i: (0, i))],
        inner // cols,
        "feed_out_back",
        2 * length * width * inner,
    )


def feed_in_back(pre_low, weight, second_grad, normed, scale, vectors, attn_weight):
    length, inner = pre_low.shape
    width = normed.shape[1]

    def kernel(p_ref, w_ref, g_ref, n_ref, r_ref, v_ref, a_ref, first_ref, low_ref, ctx_ref, sum_ref):
        grad = g_ref[...] + mxu(p_ref[...], w_ref[...], NT)
        first = norm_back(grad * row(v_ref, GAIN_ONE), n_ref[...], r_ref[:, :1])
        low = first.astype(jnp.bfloat16)
        first_ref[...] = first
        low_ref[...] = low
        ctx_ref[...] = mxu(low, a_ref[...], NT).astype(jnp.bfloat16)
        add_rows(sum_ref, grad * n_ref[...], grad, first)

    return plain_call(
        kernel,
        (pre_low, weight, second_grad, normed, scale, vectors, attn_weight),
        [
            row_tiles(inner),
            whole_once(weight.shape),
            row_tiles(width),
            row_tiles(width),
            row_tiles(LANES),
            fixed(*vectors.shape),
            whole_once(attn_weight.shape),
        ],
        [
            shaped((length, width), jnp.float32),
            shaped((length, width), jnp.bfloat16),
            shaped((length, width), jnp.bfloat16),
            shaped((8, width), jnp.float32),
        ],
        [row_tiles(width), row_tiles(width), row_tiles(width), fixed(8, width)],
        length // TILE,
        "feed_in_back",
        2 * length * width * (inner + width),
    )


def project_qkv_back(grads, weight, first_grad):
    length, width = first_grad.shape
    part = width // len(grads)

    def kernel(w_ref, *refs):
        *grad_refs, first_ref, out_ref = refs
        total = first_ref[...]
        for n in range(3):
            for m, grad_ref in enumerate(grad_refs):
                at = n * width + m * part
                total = total + mxu(grad_ref[n], w_ref[:, at : at + part], NT)
        out_ref[...] = total

    return plain_call(
        kernel,
        (weight, *grads, first_grad),
        [whole_once(weight.shape)]
        + [pl.BlockSpec((3, TILE, part), lambda i: (0, i, 0))] * len(grads)
        + [row_tiles(width)],
        [shaped((length, width), jnp.float32)],
        [row_tiles(width)],
        length // TILE,
        "qkv_back",
        6 * length * width * width,
    )[0]


ORDER = (1, 3, 0, 2)


def ordered_slot(j):
    return jnp.where(j < 2, 2 * j + 1, 2 * j - 4)


def weight_grad_kernel(where, *refs, rows, groups, count, split, extra):
    lefts, rights, refs = refs[:count], refs[count : 2 * count], refs[2 * count :]
    sums_ref = None
    if extra:
        sums_ref, *refs = refs
    (leave, keep, sent), kept = refs[:3], refs[3:]
    core = where[0]
    chips = lefts[0].shape[1] // (2 * rows)

    @pl.when(pl.program_id(1) == 0)
    def _():
        for left_ref, kept_ref in zip(lefts, kept):
            for side in range(2):
                chosen = []
                for k in range(chips):
                    even = left_ref[:, 2 * k * rows : (2 * k + 1) * rows]
                    odd = left_ref[:, (2 * k + 1) * rows : (2 * k + 2) * rows]
                    chosen.append(jnp.where(core == side, even, odd))
                left = chosen[0] if chips == 1 else jnp.concatenate(chosen, 1)
                kept_ref[side] = left.T

    def write(ref, pos, side):
        at = 0
        for right_ref, kept_ref in zip(rights, kept):
            if len(right_ref.shape) == 3:
                pieces = [right_ref[n] for n in range(right_ref.shape[0])]
            else:
                size = min(512, right_ref.shape[1])
                pieces = [
                    right_ref[:, n * size : (n + 1) * size]
                    for n in range(right_ref.shape[1] // size)
                ]
            for piece in pieces:
                part = mxu(kept_ref[side], piece, NN).astype(jnp.bfloat16)
                size = piece.shape[1]
                ref[pos, :, 0:rows, at : at + size] = part.reshape(chips, rows, size)
                at += size
        if extra:
            block = where[2] ^ turn(ordered_slot(pl.program_id(1)), core)
            blank = jnp.zeros((extra, at), jnp.bfloat16)
            for k in range(chips):
                start = pl.multiple_of((2 * k + (core ^ side)) * LANES, LANES)
                ref[pos, k, rows : rows + extra, :] = blank
                lines = sums_ref[pl.ds(pl.multiple_of(block * 8, 8), 8), pl.ds(start, LANES)]
                for n in range(3):
                    ref[pos, k, rows : rows + 1, n * LANES : (n + 1) * LANES] = lines[
                        n : n + 1
                    ].astype(jnp.bfloat16)

    if split:
        write(sent, 0, 1)

        @pl.when(pl.program_id(1) < 2)
        def _():
            write(leave, 0, 0)

        @pl.when(pl.program_id(1) >= 2)
        def _():
            write(keep, 0, 0)

    else:
        cols = rights[0].shape[1] // groups
        for side in range(2):
            for pos, slot in enumerate(ORDER):
                start = pl.multiple_of((where[2] ^ turn(slot, core ^ side)) * cols, LANES)
                part = mxu(kept[0][side], rights[0][:, pl.ds(start, cols)], NN)
                part = part.astype(jnp.bfloat16).reshape(chips, rows, cols)
                if side == 1:
                    sent[pos] = part
                else:
                    (leave if pos < 2 else keep)[pos % 2] = part


def weight_grad(place, pairs, split, name, sums=None):
    tokens, height = pairs[0][0].shape
    groups, chips = place.groups, place.chips
    rows = height // place.shards
    step_chips = chips if split else max(1, 1024 // (2 * rows))
    steps = chips // step_chips
    grid = (steps, groups if split else 1)
    extra = 0 if sums is None else 16

    def block(j, s):
        return s[2] ^ turn(ordered_slot(j), s[0])

    def position(j):
        return jnp.where(j == 0, 3, jnp.where(j == 3, 0, j))

    cols = 0
    right_specs = []
    for _, right in pairs:
        size = right.shape[-1] // groups
        if not split:
            right_specs.append(pl.BlockSpec(right.shape, lambda i, j, s: (0, 0)))
        elif right.ndim == 3:
            right_specs.append(
                pl.BlockSpec((right.shape[0], tokens, size), lambda i, j, s: (0, 0, block(j, s)))
            )
        else:
            right_specs.append(pl.BlockSpec((tokens, size), lambda i, j, s: (0, block(j, s))))
        cols += size * (right.shape[0] if right.ndim == 3 else 1)
    left_spec = pl.BlockSpec((tokens, step_chips * 2 * rows), lambda i, j, s: (0, i))
    in_specs = [left_spec] * len(pairs) + right_specs
    inputs = [left for left, _ in pairs] + [right for _, right in pairs]
    if extra:
        in_specs.append(pl.BlockSpec(sums.shape, lambda i, j, s: (0, 0)))
        inputs.append(sums)
    tall = rows + extra
    if split:
        one = (1, step_chips, tall, cols)
        out_specs = [
            pl.BlockSpec(one, lambda i, j, s: (jnp.minimum(j, 1), i, 0, 0)),
            pl.BlockSpec(one, lambda i, j, s: (jnp.maximum(j - 2, 0), i, 0, 0)),
            pl.BlockSpec(one, lambda i, j, s: (position(j), i, 0, 0)),
        ]
    else:
        out_specs = [
            pl.BlockSpec((n, step_chips, tall, cols), lambda i, j, s: (0, i, 0, 0))
            for n in (2, 2, groups)
        ]
    return pl.pallas_call(
        functools.partial(
            weight_grad_kernel,
            rows=rows,
            groups=groups,
            count=len(pairs),
            split=split,
            extra=extra,
        ),
        grid_spec=pltpu.PrefetchScalarGridSpec(
            num_scalar_prefetch=1,
            grid=grid,
            in_specs=in_specs,
            out_specs=out_specs,
            scratch_shapes=[pltpu.VMEM((2, step_chips * rows, tokens), jnp.bfloat16)] * len(pairs),
        ),
        out_shape=[shaped((n, chips, tall, cols), jnp.bfloat16) for n in (2, 2, groups)],
        compiler_params=params(60),
        cost_estimate=CHEAP,
        name="wgrad_" + name,
    )(place.scalars, *inputs)


def add(*terms):
    total = terms[0].astype(jnp.float32)
    for term in terms[1:]:
        total = total + term.astype(jnp.float32)
    return total.astype(jnp.bfloat16)


class Reduction:
    def __init__(self, place, pairs, split, name, *wait, sums=None):
        self.place = place
        if wait:
            pairs = [(after(pairs[0][0], *wait), pairs[0][1])] + pairs[1:]
        self.leave, self.keep, sent = weight_grad(place, pairs, split, name, sums)
        self.made = self.leave
        self.core = place.swap_core(sent)

    def near(self, *wait):
        self.core = after(self.core, *wait) if wait else self.core
        leave = add(self.leave, self.core[:2])
        self.first = self.place.swap_grp(leave, 0)
        return leave

    def middle(self, *wait):
        self.first = after(self.first, *wait) if wait else self.first
        second = add(self.keep[1], self.core[3], self.first[1])
        self.second = self.place.swap_grp(second, 1)
        return second

    def column(self, *wait):
        second = after(self.second, *wait) if wait else self.second
        mine = add(self.keep[0], self.core[2], self.first[0], second)
        return mine, lambda chip: lax.dynamic_index_in_dim(mine, chip, 0, False)

    def along(self, *wait):
        place = self.place
        mine, at = self.column(*wait)
        self.mine = [at(place.slot_chip(slot)) for slot in range(4)]
        self.first = place.swap_chip(jnp.stack([self.mine[1], self.mine[3]]), 0)
        return mine

    def along_far(self, *wait):
        self.first = after(self.first, *wait) if wait else self.first
        second = add(self.mine[2], self.first[1])
        self.second = self.place.swap_chip(second, 1)
        return second

    def share(self, *wait):
        second = after(self.second, *wait) if wait else self.second
        return add(self.mine[0], self.first[0], second)

    def share_direct(self, *wait):
        place = self.place
        mine, at = self.column(*wait)
        terms = [
            place.permute(at(place.chip ^ k), (2 * k, 2 * k)) for k in range(place.chips - 1, 0, -1)
        ]
        return add(at(place.chip), *terms)


class Replication:
    def __init__(self, place, share, direct=False):
        self.place = place
        if direct:
            size = place.shards
            self.blocks = [share] + [None] * 3
            for mask in (3, 1, 2):
                self.blocks[mask] = place.permute(share, (mask * size, mask * size))
            self.owner = lambda n: place.grp ^ n
        else:
            self.blocks = [share, place.swap_grp(share, 0), None, None]
            self.owner = place.slot_grp

    def far(self, *wait):
        pair = jnp.stack([self.blocks[0], after(self.blocks[1], *wait)])
        rest = self.place.swap_grp(pair, 1)
        self.blocks[2:] = [rest[0], rest[1]]
        return rest

    def result(self):
        ordered = []
        for g in range(self.place.groups):
            block = self.blocks[0]
            for n in range(1, self.place.groups):
                block = jnp.where(self.owner(n) == g, self.blocks[n], block)
            ordered.append(block.astype(jnp.float32))
        return ordered


def on_device_permutes(
    tokens,
    segment_ids,
    keep_flag,
    cotangent,
    w_qkv,
    b_query,
    b_value,
    w_attn_out,
    b_attn_out,
    norm1_gain,
    norm1_bias,
    w_in,
    b_in,
    w_out,
    b_out,
    norm2_gain,
    norm2_bias,
    *,
    groups,
    shards,
):
    place = Place(groups, shards)
    _, length, width = tokens.shape
    rows = tokens[0]
    seg_row = segment_ids.reshape(1, length)
    seg_col = segment_ids.reshape(length, 1)
    keep = keep_flag.reshape(length, 1).astype(jnp.float32)
    pairs = width // LANES

    c1 = Gather(place, w_qkv)
    c2 = Gather(place, jnp.concatenate([w_in, w_attn_out], 1))
    c3 = Gather(place, w_out)
    c1.chips_near()
    c1.chips_far()
    joined = c1.join()
    c1.near()
    small = Vectors(
        place,
        (b_query, b_value, b_attn_out, norm1_gain, norm1_bias, b_out, norm2_gain, norm2_bias, b_in),
        c1.pair[1],
    )
    vectors, bias_in, qkv_bias = small.unpack()
    c2.chips_near(joined)
    c1.cross(0)
    c2.chips_far()
    far = c1.far(c2.rest[0], vectors)
    c1.cross(1, 2)
    c1.cross(3)
    c2.join(far)
    c2.near()
    blank = jnp.ones((1, width), jnp.float32)
    qkv_scale = jnp.concatenate([blank / math.sqrt(HD), blank, blank], 1)

    mixed, full_qkv = project_qkv(place, rows, Window(c1, 0, w_qkv.shape[1]), qkv_bias, qkv_scale)
    c3.chips_near(mixed)
    c2.cross(0, wait=(mixed,))
    share_of = (pairs // 2 - pairs // 8, pairs // 4, pairs // 2 - pairs // 8)
    forward = None
    start = 0
    for n, count in enumerate(share_of):
        wait = (c2.held[3],) if n == 2 else ()
        forward = attention_forward(
            after(mixed, *wait) if wait else mixed, seg_col, seg_row, start, count, forward
        )
        start += count
        done = forward[1]
        if n == 0:
            c2.far(done)
            c3.chips_far(done)
            c2.cross(1, 2, wait=(done,))
        if n == 1:
            c3.join(done)
            c3.near()
            c2.cross(3, wait=(done,))
    contexts, lse = forward
    normed, scale_one, normed_low, full_attn = project_out(
        place, contexts, Window(c2, w_in.shape[1], w_attn_out.shape[1]), rows, vectors
    )
    c3.far(normed_low)
    c3.cross(0, 1, 2, wait=(normed_low,))
    hidden, slope, full_in = feed_in(
        place, after(normed_low, c3.held[1]), Window(c2, 0, w_in.shape[1]), bias_in
    )
    c3.cross(3, wait=(hidden,))
    layer_out, second_grad, out_low, second_sums, full_out = feed_out(
        place, hidden, Window(c3, 0, w_out.shape[1]), normed, cotangent[0], keep, vectors
    )

    r_out = Reduction(place, [(hidden, out_low)], False, "out")
    pre_low, bias_in_grad = feed_out_back(after(out_low, r_out.made), full_out, slope)
    near = r_out.near(pre_low)
    r_in = Reduction(place, [(normed_low, pre_low)], True, "in", near)
    first_grad, attn_low, context_grad, first_sums = feed_in_back(
        after(pre_low, r_in.made), full_in, second_grad, normed, scale_one, vectors, full_attn
    )
    half = pairs // 2

    def back(start, *wait):
        return attention_backward(
            mixed, contexts, after(context_grad, *wait), seg_col, seg_row, lse, start, half
        )

    middle = r_out.middle(first_grad)
    near = r_in.near(first_grad)
    low_a, late_a = back(0, middle, near)
    middle = r_in.middle(late_a)
    along = r_out.along(late_a)
    r_a = Reduction(place, [(contexts, attn_low), (rows, low_a)], True, "a", middle, along)
    far = r_out.along_far(r_a.made)
    along = r_in.along(r_a.made)
    near = r_a.near(r_a.made)
    low_b, late_b = back(half, far, along, near)
    middle = r_a.middle(late_b)
    along = r_in.along_far(late_b)
    share_out = r_out.share(late_b)
    sums = pack_sums(late_a, late_b, first_sums, second_sums, bias_in_grad)
    r_b = Reduction(place, [(rows, low_b)], True, "b", middle, along, share_out, sums=sums)
    along = r_a.along(r_b.made)
    share_in = r_in.share(r_b.made)
    inner = share_in.shape[1] // groups
    joined = jnp.concatenate(
        [share_out] + [share_in[:, n * inner : (n + 1) * inner] for n in range(groups)]
    )
    all_ffn = Replication(place, joined)
    near = r_b.near(along, joined)
    input_grad = project_qkv_back((low_a, after(low_b, near)), full_qkv, first_grad)
    middle = r_b.middle(input_grad)
    along = r_a.along_far(middle)
    all_ffn.far(middle)
    share_b = r_b.share_direct()
    all_a = Replication(place, r_a.share(along))
    all_b = Replication(place, share_b, direct=True)
    all_a.far()

    parts_a, parts_b = all_a.result(), all_b.result()
    small = [
        block[-16, n * LANES : (n + 1) * LANES] for block in parts_b for n in range(3)
    ]
    inner_mine = jnp.concatenate(small[B_IN:])
    parts_b = [block[:-16] for block in parts_b]
    heads = parts_b[0].shape[1] // 3
    skip = parts_a[0].shape[1] - 3 * heads
    w_attn_grad = jnp.concatenate([block[:, :skip] for block in parts_a], 1)
    parts_a = [block[:, skip:] for block in parts_a]
    w_qkv_grad = jnp.concatenate(
        [
            block[:, n * heads : (n + 1) * heads]
            for n in range(3)
            for half in (parts_a, parts_b)
            for block in half
        ],
        1,
    )
    parts = all_ffn.result()
    height = share_out.shape[0]
    w_out_grad = jnp.concatenate([block[:height] for block in parts], 1)
    size = share_in.shape[0]
    w_in_grad = jnp.concatenate(
        [
            block[height + n * size : height + (n + 1) * size]
            for block in parts
            for n in range(groups)
        ],
        1,
    )
    return (
        layer_out[None],
        input_grad[None],
        w_qkv_grad,
        small[B_QUERY],
        small[B_VALUE],
        w_attn_grad,
        small[B_ATTN],
        small[GAIN_ONE],
        small[SHIFT_ONE],
        w_in_grad,
        inner_mine,
        w_out_grad,
        small[B_OUT],
        small[GAIN_TWO],
        small[SHIFT_TWO],
    )


def solution(mesh):
    groups, shards = mesh.shape["grp"], mesh.shape["shard"]
    if groups == 4 and shards == 8:
        body = functools.partial(on_device_permutes, groups=groups, shards=shards)
    else:
        body = on_device
    return jax.shard_map(
        body,
        mesh=mesh,
        in_specs=(
            P(("grp", "shard"), None, None),
            P(("grp", "shard"), None),
            P(("grp", "shard"), None),
            P(("grp", "shard"), None, None),
            P("shard", "grp"),
            P("shard"),
            P("shard"),
            P("shard", "grp"),
            P("shard"),
            P("shard"),
            P("shard"),
            P("shard", "grp"),
            P("shard"),
            P("shard", "grp"),
            P("shard"),
            P("shard"),
            P("shard"),
        ),
        out_specs=(
            P(("grp", "shard"), None, None),
            P(("grp", "shard"), None, None),
            P("shard", None),
            P("shard"),
            P("shard"),
            P("shard", None),
            P("shard"),
            P("shard"),
            P("shard"),
            P("shard", None),
            P("shard"),
            P("shard", None),
            P("shard"),
            P("shard"),
            P("shard"),
        ),
        check_vma=False,
    )
```

```python
import functools
import math

import jax
import jax.numpy as jnp
from jax import lax
from jax.experimental import pallas as pl
from jax.experimental.pallas import tpu as pltpu
from jax.sharding import PartitionSpec as P

H = 16
HD = 64


masked_score = -1e30
epsilon = 1e-05


def norm_layer(rows, gain_row, shift_row):
    row_mean = jnp.mean(rows, -1, keepdims=True)
    centered = rows - row_mean
    row_var = jnp.mean(centered * centered, -1, keepdims=True)
    return centered * lax.rsqrt(row_var + epsilon) * gain_row + shift_row


def gelu_exact(values):
    return 0.5 * values * (1.0 + lax.erf(values * (1.0 / math.sqrt(2.0))))


def contract_rows(left, right):
    return lax.dot_general(
        left, right, (((0,), (0,)), ((), ())), preferred_element_type=jnp.float32
    )


def contract_cols(left, right):
    return lax.dot_general(
        left, right, (((1,), (1,)), ((), ())), preferred_element_type=jnp.float32
    )


def attend_forward(queries, key_rows, value_rows, segment_row, block_rows):
    length, model_width = queries.shape
    scaling = 1.0 / math.sqrt(HD)
    key_heads = key_rows.reshape(length, H, HD)
    value_heads = value_rows.reshape(length, H, HD)
    query_blocks = queries.reshape(length // block_rows, block_rows, H, HD)
    segment_blocks = segment_row.reshape(length // block_rows, block_rows)

    def one_block(pieces):
        query_part, segment_part = pieces
        scores = (
            jnp.einsum("qhd,khd->hqk", query_part, key_heads, preferred_element_type=jnp.float32)
            * scaling
        )
        allowed = segment_part[:, None] == segment_row[None, :]
        scores = jnp.where(allowed[None], scores, masked_score)
        row_max = jnp.max(scores, -1, keepdims=True)
        powers = jnp.exp(scores - row_max)
        totals = jnp.sum(powers, -1, keepdims=True)
        attn_probs = (powers / totals).astype(jnp.bfloat16)
        context = jnp.einsum(
            "hqk,khd->qhd", attn_probs, value_heads, preferred_element_type=jnp.float32
        )
        return (
            context.reshape(block_rows, model_width).astype(jnp.bfloat16),
            (row_max + jnp.log(totals))[:, :, 0],
        )

    contexts, log_sums = lax.map(one_block, (query_blocks, segment_blocks))
    return (contexts.reshape(length, model_width), log_sums)


def attend_backward(queries, key_rows, value_rows, segment_row, log_sums, context_grad, block_rows):
    length, model_width = queries.shape
    scaling = 1.0 / math.sqrt(HD)
    key_heads = key_rows.reshape(length, H, HD)
    value_heads = value_rows.reshape(length, H, HD)
    query_blocks = queries.reshape(length // block_rows, block_rows, H, HD)
    segment_blocks = segment_row.reshape(length // block_rows, block_rows)
    grad_blocks = context_grad.reshape(length // block_rows, block_rows, H, HD)

    def one_block(running, pieces):
        key_acc, value_acc = running
        query_part, segment_part, lse_part, grad_part = pieces
        scores = (
            jnp.einsum("qhd,khd->hqk", query_part, key_heads, preferred_element_type=jnp.float32)
            * scaling
        )
        allowed = segment_part[:, None] == segment_row[None, :]
        scores = jnp.where(allowed[None], scores, masked_score)
        probs = jnp.exp(scores - lse_part[:, :, None])
        prob_low = probs.astype(jnp.bfloat16)
        prob_grad = jnp.einsum(
            "qhd,khd->hqk", grad_part, value_heads, preferred_element_type=jnp.float32
        )
        row_dot = jnp.sum(prob_grad * probs, -1, keepdims=True)
        score_grad = (probs * (prob_grad - row_dot)).astype(jnp.bfloat16)
        query_grad = (
            jnp.einsum("hqk,khd->qhd", score_grad, key_heads, preferred_element_type=jnp.float32)
            * scaling
        )
        key_acc = (
            key_acc
            + jnp.einsum("hqk,qhd->khd", score_grad, query_part, preferred_element_type=jnp.float32)
            * scaling
        )
        value_acc = value_acc + jnp.einsum(
            "hqk,qhd->khd", prob_low, grad_part, preferred_element_type=jnp.float32
        )
        return ((key_acc, value_acc), query_grad.reshape(block_rows, model_width))

    empty_acc = jnp.zeros((length, H, HD), jnp.float32)
    (key_grad, value_grad), query_grads = lax.scan(
        one_block, (empty_acc, empty_acc), (query_blocks, segment_blocks, log_sums, grad_blocks)
    )
    return (
        query_grads.reshape(length, model_width),
        key_grad.reshape(length, model_width),
        value_grad.reshape(length, model_width),
    )


def on_device(
    tokens,
    segment_ids,
    keep_flag,
    cotangent,
    w_qkv,
    b_query,
    b_value,
    w_attn_out,
    b_attn_out,
    norm1_gain,
    norm1_bias,
    w_in,
    b_in,
    w_out,
    b_out,
    norm2_gain,
    norm2_bias,
):
    seq_count, length, model_width = tokens.shape
    block_rows = min(512, length)
    within = (
        lax.all_gather(w_qkv, "shard", axis=0, tiled=True),
        lax.all_gather(w_attn_out, "shard", axis=0, tiled=True),
        lax.all_gather(w_in, "shard", axis=0, tiled=True),
        lax.all_gather(w_out, "shard", axis=0, tiled=True),
        lax.all_gather(b_query, "shard", axis=0, tiled=True),
        lax.all_gather(b_value, "shard", axis=0, tiled=True),
        lax.all_gather(b_attn_out, "shard", axis=0, tiled=True),
        lax.all_gather(norm1_gain, "shard", axis=0, tiled=True),
        lax.all_gather(norm1_bias, "shard", axis=0, tiled=True),
        lax.all_gather(b_in, "shard", axis=0, tiled=True),
        lax.all_gather(b_out, "shard", axis=0, tiled=True),
        lax.all_gather(norm2_gain, "shard", axis=0, tiled=True),
        lax.all_gather(norm2_bias, "shard", axis=0, tiled=True),
    )
    full_qkv, full_attn, full_in, full_out = (
        lax.all_gather(within[0], "grp", axis=1, tiled=True),
        lax.all_gather(within[1], "grp", axis=1, tiled=True),
        lax.all_gather(within[2], "grp", axis=1, tiled=True),
        lax.all_gather(within[3], "grp", axis=1, tiled=True),
    )
    (
        bias_query,
        bias_value,
        bias_attn,
        gain_one,
        shift_one,
        bias_in,
        bias_out,
        gain_two,
        shift_two,
    ) = [piece.astype(jnp.float32) for piece in within[4:]]
    flat_rows = tokens.reshape(seq_count * length, model_width)
    mixed_qkv = jnp.dot(flat_rows, full_qkv, preferred_element_type=jnp.float32)
    queries = (mixed_qkv[:, :model_width] + bias_query).astype(jnp.bfloat16)
    key_rows = mixed_qkv[:, model_width : 2 * model_width].astype(jnp.bfloat16)
    value_rows = (mixed_qkv[:, 2 * model_width :] + bias_value).astype(jnp.bfloat16)
    query_seqs = queries.reshape(seq_count, length, model_width)
    key_seqs = key_rows.reshape(seq_count, length, model_width)
    value_seqs = value_rows.reshape(seq_count, length, model_width)

    def forward_sequence(pieces):
        return attend_forward(pieces[0], pieces[1], pieces[2], pieces[3], block_rows)

    contexts, log_sums = lax.map(forward_sequence, (query_seqs, key_seqs, value_seqs, segment_ids))
    contexts = contexts.reshape(seq_count * length, model_width)
    attended = jnp.dot(contexts, full_attn, preferred_element_type=jnp.float32) + bias_attn
    first_sum = flat_rows.astype(jnp.float32) + attended
    normed_one, norm_one_back = jax.vjp(norm_layer, first_sum, gain_one, shift_one)
    normed_low = normed_one.astype(jnp.bfloat16)
    hidden_pre = jnp.dot(normed_low, full_in, preferred_element_type=jnp.float32) + bias_in
    hidden, gelu_back = jax.vjp(gelu_exact, hidden_pre)
    hidden_low = hidden.astype(jnp.bfloat16)
    second_sum = normed_one + (
        jnp.dot(hidden_low, full_out, preferred_element_type=jnp.float32) + bias_out
    )
    result, norm_two_back = jax.vjp(norm_layer, second_sum, gain_two, shift_two)
    layer_out = result.astype(jnp.bfloat16).reshape(seq_count, length, model_width)
    again = (
        lax.all_gather(w_qkv, "shard", axis=0, tiled=True),
        lax.all_gather(w_attn_out, "shard", axis=0, tiled=True),
        lax.all_gather(w_in, "shard", axis=0, tiled=True),
        lax.all_gather(w_out, "shard", axis=0, tiled=True),
    )
    back_qkv, back_attn, back_in, back_out = (
        lax.all_gather(again[0], "grp", axis=1, tiled=True),
        lax.all_gather(again[1], "grp", axis=1, tiled=True),
        lax.all_gather(again[2], "grp", axis=1, tiled=True),
        lax.all_gather(again[3], "grp", axis=1, tiled=True),
    )
    masked_cot = cotangent.astype(jnp.float32).reshape(
        seq_count * length, model_width
    ) * keep_flag.reshape(seq_count * length, 1).astype(jnp.float32)
    second_grad, gain_two_grad, shift_two_grad = norm_two_back(masked_cot)
    bias_out_grad = jnp.sum(second_grad, 0)
    out_low = second_grad.astype(jnp.bfloat16)
    w_out_grad = contract_rows(hidden_low, out_low)
    hidden_grad = contract_cols(out_low, back_out)
    (pre_grad,) = gelu_back(hidden_grad)
    bias_in_grad = jnp.sum(pre_grad, 0)
    pre_low = pre_grad.astype(jnp.bfloat16)
    w_in_grad = contract_rows(normed_low, pre_low)
    normed_grad = second_grad + contract_cols(pre_low, back_in)
    first_grad, gain_one_grad, shift_one_grad = norm_one_back(normed_grad)
    bias_attn_grad = jnp.sum(first_grad, 0)
    attn_low = first_grad.astype(jnp.bfloat16)
    w_attn_grad = contract_rows(contexts, attn_low)
    context_grad = contract_cols(attn_low, back_attn).astype(jnp.bfloat16)

    def backward_sequence(pieces):
        return attend_backward(
            pieces[0], pieces[1], pieces[2], pieces[3], pieces[4], pieces[5], block_rows
        )

    query_grad, key_grad, value_grad = lax.map(
        backward_sequence,
        (
            query_seqs,
            key_seqs,
            value_seqs,
            segment_ids,
            log_sums,
            context_grad.reshape(seq_count, length, model_width),
        ),
    )
    query_grad = query_grad.reshape(seq_count * length, model_width)
    key_grad = key_grad.reshape(seq_count * length, model_width)
    value_grad = value_grad.reshape(seq_count * length, model_width)
    bias_query_grad = jnp.sum(query_grad, 0)
    bias_value_grad = jnp.sum(value_grad, 0)
    qkv_low = jnp.concatenate([query_grad, key_grad, value_grad], 1).astype(jnp.bfloat16)
    w_qkv_grad = contract_rows(flat_rows, qkv_low)
    input_grad = first_grad + contract_cols(qkv_low, back_qkv)
    reduced = (
        lax.psum_scatter(
            w_qkv_grad.astype(jnp.bfloat16), "shard", scatter_dimension=0, tiled=True
        ).astype(jnp.float32),
        lax.psum_scatter(
            bias_query_grad.astype(jnp.bfloat16), "shard", scatter_dimension=0, tiled=True
        ).astype(jnp.float32),
        lax.psum_scatter(
            bias_value_grad.astype(jnp.bfloat16), "shard", scatter_dimension=0, tiled=True
        ).astype(jnp.float32),
        lax.psum_scatter(
            w_attn_grad.astype(jnp.bfloat16), "shard", scatter_dimension=0, tiled=True
        ).astype(jnp.float32),
        lax.psum_scatter(
            bias_attn_grad.astype(jnp.bfloat16), "shard", scatter_dimension=0, tiled=True
        ).astype(jnp.float32),
        lax.psum_scatter(
            gain_one_grad.astype(jnp.bfloat16), "shard", scatter_dimension=0, tiled=True
        ).astype(jnp.float32),
        lax.psum_scatter(
            shift_one_grad.astype(jnp.bfloat16), "shard", scatter_dimension=0, tiled=True
        ).astype(jnp.float32),
        lax.psum_scatter(
            w_in_grad.astype(jnp.bfloat16), "shard", scatter_dimension=0, tiled=True
        ).astype(jnp.float32),
        lax.psum_scatter(
            bias_in_grad.astype(jnp.bfloat16), "shard", scatter_dimension=0, tiled=True
        ).astype(jnp.float32),
        lax.psum_scatter(
            w_out_grad.astype(jnp.bfloat16), "shard", scatter_dimension=0, tiled=True
        ).astype(jnp.float32),
        lax.psum_scatter(
            bias_out_grad.astype(jnp.bfloat16), "shard", scatter_dimension=0, tiled=True
        ).astype(jnp.float32),
        lax.psum_scatter(
            gain_two_grad.astype(jnp.bfloat16), "shard", scatter_dimension=0, tiled=True
        ).astype(jnp.float32),
        lax.psum_scatter(
            shift_two_grad.astype(jnp.bfloat16), "shard", scatter_dimension=0, tiled=True
        ).astype(jnp.float32),
    )
    summed = (
        lax.psum(reduced[0].astype(jnp.bfloat16), "grp").astype(jnp.float32),
        lax.psum(reduced[1].astype(jnp.bfloat16), "grp").astype(jnp.float32),
        lax.psum(reduced[2].astype(jnp.bfloat16), "grp").astype(jnp.float32),
        lax.psum(reduced[3].astype(jnp.bfloat16), "grp").astype(jnp.float32),
        lax.psum(reduced[4].astype(jnp.bfloat16), "grp").astype(jnp.float32),
        lax.psum(reduced[5].astype(jnp.bfloat16), "grp").astype(jnp.float32),
        lax.psum(reduced[6].astype(jnp.bfloat16), "grp").astype(jnp.float32),
        lax.psum(reduced[7].astype(jnp.bfloat16), "grp").astype(jnp.float32),
        lax.psum(reduced[8].astype(jnp.bfloat16), "grp").astype(jnp.float32),
        lax.psum(reduced[9].astype(jnp.bfloat16), "grp").astype(jnp.float32),
        lax.psum(reduced[10].astype(jnp.bfloat16), "grp").astype(jnp.float32),
        lax.psum(reduced[11].astype(jnp.bfloat16), "grp").astype(jnp.float32),
        lax.psum(reduced[12].astype(jnp.bfloat16), "grp").astype(jnp.float32),
    )
    return (
        layer_out,
        input_grad.reshape(seq_count, length, model_width),
        summed[0],
        summed[1],
        summed[2],
        summed[3],
        summed[4],
        summed[5],
        summed[6],
        summed[7],
        summed[8],
        summed[9],
        summed[10],
        summed[11],
        summed[12],
    )


NT = (((1,), (1,)), ((), ()))
NN = (((1,), (0,)), ((), ()))
TN = (((0,), (0,)), ((), ()))
LANES = 128
AXES = ("grp", "shard")


def mxu(left, right, dims):
    return lax.dot_general(left, right, dims, preferred_element_type=jnp.float32)


def cost(flops):
    return pl.CostEstimate(flops=2 * flops, bytes_accessed=0, transcendentals=0)


def params(megabytes=60):
    return pltpu.CompilerParams(vmem_limit_bytes=megabytes << 20)


def attention_forward_kernel(q_ref, k_ref, v_ref, seg_col, seg_row, out_ref, lse_ref, *, rows):
    length = q_ref.shape[0]
    first = lax.broadcasted_iota(jnp.int32, (1, LANES), 1) < HD
    keys = k_ref[...]
    values = v_ref[...]
    zero = jnp.zeros_like(keys)
    head_keys = (jnp.where(first, keys, zero), jnp.where(first, zero, keys))
    key_segments = seg_col[...]
    for block in range(length // rows):
        here = pl.ds(block * rows, rows)
        q = q_ref[here, :]
        allowed = key_segments == seg_row[:, here]
        outs = []
        for head in range(2):
            scores = mxu(head_keys[head], q, NT)
            scores = jnp.where(allowed, scores, masked_score)
            top = jnp.max(scores, 0, keepdims=True)
            powers = jnp.exp(scores - top)
            total = jnp.sum(powers, 0, keepdims=True)
            part = mxu(powers.astype(jnp.bfloat16), values, TN)
            outs.append(part * jnp.transpose(jnp.broadcast_to(1.0 / total, (LANES, rows))))
            lse_ref[0, head : head + 1, here] = top + jnp.log(total)
        out_ref[here, :] = jnp.where(first, outs[0], outs[1]).astype(jnp.bfloat16)


def attention_forward(qkv, seg_col, seg_row, start, pairs, before=None):
    length, width = qkv.shape[0], qkv.shape[1] // 3
    total = width // LANES
    rows = min(512, length)
    anywhere = pl.BlockSpec(memory_space=pl.ANY)

    def pair(part):
        return pl.BlockSpec((length, LANES), lambda j: (0, part * total + start + j))

    def body(q_ref, k_ref, v_ref, seg_c, seg_r, *refs):
        attention_forward_kernel(q_ref, k_ref, v_ref, seg_c, seg_r, *refs[-2:], rows=rows)

    return pl.pallas_call(
        body,
        grid=(pairs,),
        in_specs=[
            pair(0),
            pair(1),
            pair(2),
            pl.BlockSpec((length, 1), lambda j: (0, 0)),
            pl.BlockSpec((1, length), lambda j: (0, 0)),
        ]
        + [anywhere] * (0 if before is None else 2),
        out_specs=[
            pl.BlockSpec((length, LANES), lambda j: (0, start + j)),
            pl.BlockSpec((1, 2, length), lambda j: (start + j, 0, 0)),
        ],
        out_shape=[
            jax.ShapeDtypeStruct((length, width), jnp.bfloat16),
            jax.ShapeDtypeStruct((total, 2, length), jnp.float32),
        ],
        input_output_aliases={} if before is None else {5: 0, 6: 1},
        compiler_params=params(60),
        cost_estimate=cost(16 * length * length * pairs * LANES),
        name="attn_fwd",
    )(qkv, qkv, qkv, seg_col, seg_row, *(() if before is None else before))


def attention_backward_kernel(
    q_ref, k_ref, v_ref, o_ref, do_ref, seg_col, seg_row, lse_ref, grad_ref, sum_ref, *, rows
):
    length = q_ref.shape[0]
    lane = lax.broadcasted_iota(jnp.int32, (1, LANES), 1)
    first = lane < HD
    pick = (
        lax.broadcasted_iota(jnp.int32, (8, LANES), 0)
        == lax.broadcasted_iota(jnp.int32, (8, LANES), 1) // HD
    ).astype(jnp.float32)
    keys = k_ref[...]
    values = v_ref[...]
    zero = jnp.zeros_like(keys)
    head_keys = (jnp.where(first, keys, zero), jnp.where(first, zero, keys))
    head_values = (jnp.where(first, values, zero), jnp.where(first, zero, values))
    key_segments = seg_col[...]
    key_sum = [None, None]
    value_sum = [None, None]
    query_total = jnp.zeros((1, LANES), jnp.float32)
    for block in range(length // rows):
        here = pl.ds(block * rows, rows)
        q = q_ref[here, :]
        do = do_ref[here, :]
        allowed = key_segments == seg_row[:, here]
        dots = lax.dot_general(
            pick,
            do.astype(jnp.float32) * o_ref[here, :].astype(jnp.float32),
            NT,
            precision=lax.Precision.HIGHEST,
            preferred_element_type=jnp.float32,
        )
        parts = []
        for head in range(2):
            scores = mxu(head_keys[head], q, NT)
            scores = jnp.where(allowed, scores, masked_score)
            probs = jnp.exp(scores - lse_ref[0, head : head + 1, here])
            prob_grad = mxu(head_values[head], do, NT)
            score_grad = (probs * (prob_grad - dots[head : head + 1, :])).astype(jnp.bfloat16)
            value_part = mxu(probs.astype(jnp.bfloat16), do, NN)
            key_part = mxu(score_grad, q, NN)
            value_sum[head] = value_part if block == 0 else value_sum[head] + value_part
            key_sum[head] = key_part if block == 0 else key_sum[head] + key_part
            parts.append(mxu(score_grad, keys, TN))
        query_grad = jnp.where(first, parts[0], parts[1]) * (1.0 / math.sqrt(HD))
        query_total = query_total + jnp.sum(query_grad, 0, keepdims=True)
        grad_ref[0, here, :] = query_grad.astype(jnp.bfloat16)
    grad_ref[1, :, :] = jnp.where(first, key_sum[0], key_sum[1]).astype(jnp.bfloat16)
    value_grad = jnp.where(first, value_sum[0], value_sum[1])
    grad_ref[2, :, :] = value_grad.astype(jnp.bfloat16)
    sum_ref[0:1, :] = query_total
    sum_ref[1:2, :] = jnp.sum(value_grad, 0, keepdims=True)


def attention_backward(qkv, out, out_grad, seg_col, seg_row, lse, start, pairs, at, size, before=None):
    length, width = out.shape
    total = width // LANES
    rows = min(256, length)
    more = () if before is None else before

    def pair(part):
        return pl.BlockSpec((length, LANES), lambda j: (0, part * total + start + j))

    def body(*refs):
        attention_backward_kernel(*refs[:8], *refs[-2:], rows=rows)

    return pl.pallas_call(
        body,
        grid=(pairs,),
        in_specs=[
            pair(0),
            pair(1),
            pair(2),
            pair(0),
            pair(0),
            pl.BlockSpec((length, 1), lambda j: (0, 0)),
            pl.BlockSpec((1, length), lambda j: (0, 0)),
            pl.BlockSpec((1, 2, length), lambda j: (j + start, 0, 0)),
        ]
        + [pl.BlockSpec(memory_space=pl.ANY)] * len(more),
        out_specs=[
            pl.BlockSpec((3, length, LANES), lambda j: (0, 0, j + at)),
            pl.BlockSpec((2, LANES), lambda j: (0, j + at)),
        ],
        out_shape=[
            jax.ShapeDtypeStruct((3, length, size * LANES), jnp.bfloat16),
            jax.ShapeDtypeStruct((2, size * LANES), jnp.float32),
        ],
        input_output_aliases={} if before is None else {8: 0, 9: 1},
        compiler_params=params(60),
        cost_estimate=cost(40 * length * length * pairs * LANES),
        name="attn_bwd",
    )(qkv, qkv, qkv, out, out_grad, seg_col, seg_row, lse, *more)


class Place:
    def __init__(self, groups, shards):
        self.groups = groups
        self.shards = shards
        self.chips = shards // 2
        self.grp = lax.axis_index("grp")
        self.shard = lax.axis_index("shard")
        self.core = self.shard % 2
        self.chip = self.shard // 2
        self.scalars = jnp.stack([self.core, self.chip, self.grp]).astype(jnp.int32)

    def permute(self, array, mask_of_core):
        pairs = [(i, i ^ mask_of_core[i % 2]) for i in range(self.groups * self.shards)]
        return lax.ppermute(array, AXES, pairs)

    def swap_core(self, array):
        return self.permute(array, (1, 1))

    def swap_grp(self, array, step):
        masks = (self.shards, 2 * self.shards)
        return self.permute(array, masks if step == 0 else masks[::-1])

    def swap_chip(self, array, step):
        masks = (2, 4)
        return self.permute(array, masks if step == 0 else masks[::-1])

    def slot_chip(self, slot):
        return self.chip ^ turn(slot, self.core)

    def slot_grp(self, slot):
        return self.grp ^ turn(slot, self.core)


def turn(slot, core):
    if isinstance(slot, int):
        return slot if slot in (0, 3) else jnp.where(core == 0, slot, 3 - slot)
    return jnp.where((core == 0) | (slot == 0) | (slot == 3), slot, 3 - slot)


def after(value, *others):
    return lax.optimization_barrier((value, *others))[0]


def meet(anchor, *flights):
    arrays = [f.flying for f in flights]
    _, *arrays = lax.optimization_barrier((anchor, *arrays))
    for f, array in zip(flights, arrays):
        f.flying = array


class Gather:
    def __init__(self, place, piece):
        self.place = place
        self.piece = piece
        self.held = [None] * 4
        self.crossed = [None] * 4

    def chips_near(self, *wait):
        self.piece = after(self.piece, *wait)
        self.flying = self.place.swap_chip(self.piece, 0)

    def chips_far(self):
        self.pair = jnp.stack([self.piece, self.flying])
        self.flying = self.place.swap_chip(self.pair, 1)
        return self.pair

    def near(self, *wait):
        joined = jnp.concatenate([self.pair, self.flying])
        self.held[0] = after(joined, *wait)
        self.flying = (self.place.swap_grp(self.held[0], 0), self.place.swap_grp(self.held[0], 1))
        return self.held[0]

    def far(self, *wait):
        self.held[1:3] = self.flying
        first = after(self.held[1], *wait)
        self.flying = self.place.swap_grp(first, 1)

    def landed(self):
        self.held[3] = self.flying

    def cross(self, *which, wait=()):
        for n in which:
            self.crossed[n] = self.place.swap_core(after(self.held[n], *wait))

    def pieces(self):
        return self.held + self.crossed


class Window:
    def __init__(self, gather, start, cols):
        self.arrays = gather.pieces()
        self.start, self.cols = start, cols
        chips, rows, _ = self.arrays[0].shape
        self.chips, self.rows = chips, rows


def fetch(where, window, refs, whole, sem, by):
    rows, cols, chips = window.rows, window.cols, window.chips
    for slot in range(4):
        for side in range(2):
            core = where[0] ^ side
            ref = refs[4 * side + slot]
            distance = turn(slot, core)
            col = pl.multiple_of((where[2] ^ distance) * cols, LANES)
            for k in range(chips):
                row = ((where[1] ^ turn(k, core)) * 2 + core) * rows
                pltpu.make_async_copy(
                    ref.at[k, :, pl.ds(window.start, cols)],
                    whole.at[pl.ds(pl.multiple_of(row, rows), rows), pl.ds(col, cols)],
                    sem.at[distance if by == "grp" else 0],
                ).start()


def weight_call(place, kernel, window, inputs, in_specs, outs, out_specs, steps, by, name, flops, mb=60):
    cols, groups = window.cols, place.groups
    pieces = window.arrays
    shape = (window.chips * 2 * window.rows, groups * cols)
    slots = {"grp": groups, "all": 1}[by]
    anywhere = pl.BlockSpec(memory_space=pl.ANY)

    def body(where, *refs):
        taken, refs = refs[: len(pieces)], refs[len(pieces) :]
        *refs, written, weight, sem, out_sem = refs
        step = pl.program_id(0)

        @pl.when(step == 0)
        def _():
            fetch(where, window, taken, weight, sem, by)

        def ready():
            if by == "all":

                @pl.when(step == 0)
                def _():
                    pltpu.make_async_copy(weight, weight, sem.at[0]).wait()
                    pltpu.make_async_copy(weight, written, out_sem.at[0]).start()

            else:
                at = pl.ds(pl.multiple_of((where[2] ^ step) * cols, LANES), cols)
                view = weight.at[:, at]
                pltpu.make_async_copy(view, view, sem.at[step]).wait()
                pltpu.make_async_copy(view, written.at[:, at], out_sem.at[step]).start()

        kernel(where, ready, weight, *refs)

        @pl.when(step == steps - 1)
        def _():
            for slot in range(slots):
                width = shape[1] // slots
                view = weight.at[:, pl.ds(slot * width, width)]
                pltpu.make_async_copy(view, view, out_sem.at[slot]).wait()

    total = sum(math.prod(x.shape) * x.dtype.itemsize for x in list(inputs) + list(outs))
    return pl.pallas_call(
        body,
        grid_spec=pltpu.PrefetchScalarGridSpec(
            num_scalar_prefetch=1,
            grid=(steps,),
            in_specs=[anywhere] * len(pieces) + in_specs,
            out_specs=out_specs + [anywhere],
            scratch_shapes=[
                pltpu.VMEM(shape, jnp.bfloat16),
                pltpu.SemaphoreType.DMA((slots,)),
                pltpu.SemaphoreType.DMA((slots,)),
            ],
        ),
        out_shape=outs + [shaped(shape, jnp.bfloat16)],
        compiler_params=params(mb),
        cost_estimate=cost(flops),
        name=name,
    )(place.scalars, *pieces, *inputs)


def plain_call(kernel, inputs, in_specs, outs, out_specs, steps, name, flops, mb=60):
    total = sum(math.prod(x.shape) * x.dtype.itemsize for x in list(inputs) + list(outs))
    return pl.pallas_call(
        kernel,
        grid=(steps,),
        in_specs=in_specs,
        out_specs=out_specs,
        out_shape=outs,
        compiler_params=params(mb),
        cost_estimate=cost(flops),
        name=name,
    )(*inputs)


TILE = 256


def row_tiles(width):
    return pl.BlockSpec((TILE, width), lambda i, *s: (i, 0))


def fixed(*shape):
    return pl.BlockSpec(shape, lambda i, *s: (0,) * len(shape))


def whole_once(shape):
    return pl.BlockSpec(shape, lambda i: (0,) * len(shape), pipeline_mode=pl.Buffered(1))


def shaped(shape, dtype):
    return jax.ShapeDtypeStruct(shape, dtype)


B_QUERY, B_VALUE, B_ATTN, GAIN_ONE, SHIFT_ONE, B_OUT, GAIN_TWO, SHIFT_TWO, B_IN = range(9)


def row(ref, n):
    return ref[n : n + 1, :]


class Vectors:
    def __init__(self, place, vectors, *wait):
        lines = [v.reshape(-1, LANES) for v in (after(vectors[0], *wait), *vectors[1:])]
        blank = jnp.zeros((-sum(x.shape[0] for x in lines) % 16, LANES), jnp.bfloat16)
        own = jnp.concatenate([*lines, blank])
        own = jnp.stack([own, place.swap_core(own)])
        pair = jnp.stack([own, place.swap_chip(own, 0)])
        self.slots = jnp.concatenate([pair, place.swap_chip(pair, 1)])
        self.place = place

    def unpack(self):
        place = self.place
        slots, sides, rows, lanes = self.slots.shape
        shards = place.shards

        def kernel(where, in_ref, rows_ref, inner_ref, qkv_ref):
            width = shards * lanes
            qkv_ref[...] = jnp.zeros_like(qkv_ref)
            for slot in range(slots):
                for side in range(sides):
                    core = where[0] ^ side
                    shard = (where[1] ^ turn(slot, where[0])) * 2 + core
                    part = in_ref[slot, side].astype(jnp.float32)
                    at = pl.multiple_of(shard * lanes, lanes)
                    rows_ref[:, pl.ds(at, lanes)] = part
                    qkv_ref[:, pl.ds(at, lanes)] = part[B_QUERY : B_QUERY + 1]
                    qkv_ref[:, pl.ds(2 * width + at, lanes)] = part[B_VALUE : B_VALUE + 1]
                    for n in range(4):
                        start = pl.multiple_of((shard * 4 + n) * lanes, lanes)
                        inner_ref[:, pl.ds(start, lanes)] = part[B_IN + n : B_IN + n + 1]

        in_vmem = pl.BlockSpec(memory_space=pltpu.VMEM)
        return pl.pallas_call(
            kernel,
            in_specs=[pl.BlockSpec(memory_space=pltpu.SMEM), in_vmem],
            out_specs=[in_vmem] * 3,
            out_shape=[
                shaped((rows, shards * lanes), jnp.float32),
                shaped((1, 4 * shards * lanes), jnp.float32),
                shaped((1, 3 * shards * lanes), jnp.float32),
            ],
            name="vectors",
        )(place.scalars, self.slots)


def pack_sums(late_a, late_b, first_sums, second_sums, inner_sums):
    width = first_sums.shape[1]
    half = late_a.shape[1]

    def kernel(a_ref, b_ref, one_ref, two_ref, inner_ref, out_ref):
        def place_of(n):
            return n // 3 * 8 + n % 3

        out_ref[...] = jnp.zeros_like(out_ref)
        for n in (B_QUERY, B_VALUE):
            at = place_of(n)
            out_ref[at : at + 1, 0:half] = a_ref[n : n + 1, :]
            out_ref[at : at + 1, half:width] = b_ref[n : n + 1, :]
        for n, source, line in (
            (GAIN_ONE, one_ref, 0),
            (SHIFT_ONE, one_ref, 1),
            (B_ATTN, one_ref, 2),
            (GAIN_TWO, two_ref, 0),
            (SHIFT_TWO, two_ref, 1),
            (B_OUT, two_ref, 2),
        ):
            at = place_of(n)
            out_ref[at : at + 1, :] = source[line : line + 1, :]
        for n in range(4):
            at = place_of(B_IN + n)
            for shard in range(width // LANES):
                start = (4 * shard + n) * LANES
                out_ref[at : at + 1, shard * LANES : (shard + 1) * LANES] = inner_ref[
                    :, start : start + LANES
                ]

    in_vmem = pl.BlockSpec(memory_space=pltpu.VMEM)
    return pl.pallas_call(
        kernel,
        in_specs=[in_vmem] * 5,
        out_specs=in_vmem,
        out_shape=shaped((32, width), jnp.float32),
        name="pack_sums",
    )(late_a, late_b, first_sums, second_sums, inner_sums)


def project_qkv(place, rows, window, bias, scale):
    length, width = rows.shape
    cols = window.cols

    def kernel(where, ready, weight, x_ref, bias_ref, scale_ref, out_ref):
        ready()
        at = pl.ds(pl.multiple_of((where[2] ^ pl.program_id(0)) * cols, LANES), cols)
        for tile in range(length // TILE):
            here = pl.ds(tile * TILE, TILE)
            mixed = mxu(x_ref[here, :], weight[:, at], NN) + bias_ref[:, at]
            mixed = mixed.astype(jnp.bfloat16).astype(jnp.float32) * scale_ref[:, at]
            out_ref[here, :] = mixed.astype(jnp.bfloat16)

    total = cols * place.groups
    return weight_call(
        place,
        kernel,
        window,
        (rows, bias, scale),
        [fixed(length, width), fixed(1, total), fixed(1, total)],
        [shaped((length, total), jnp.bfloat16)],
        [pl.BlockSpec((length, cols), lambda i, s: (0, i ^ s[2]))],
        place.groups,
        "grp",
        "qkv",
        2 * length * width * total,
    )


def norm_parts(rows):
    centered = rows - jnp.mean(rows, -1, keepdims=True)
    scale = lax.rsqrt(jnp.mean(centered * centered, -1, keepdims=True) + epsilon)
    return centered * scale, scale


def norm_back(grad, normed, scale):
    return scale * (
        grad
        - jnp.mean(grad, -1, keepdims=True)
        - normed * jnp.mean(grad * normed, -1, keepdims=True)
    )


def add_rows(sum_ref, *terms):
    @pl.when(pl.program_id(0) == 0)
    def _():
        sum_ref[...] = jnp.zeros_like(sum_ref)

    for n, term in enumerate(terms):
        sum_ref[n : n + 1, :] += jnp.sum(term, 0, keepdims=True)


def project_out(place, contexts, window, rows, vectors):
    length, width = rows.shape

    def kernel(where, ready, weight, c_ref, x_ref, v_ref, n_ref, r_ref, low_ref):
        ready()
        first_sum = mxu(c_ref[...], weight[...], NN) + row(v_ref, B_ATTN)
        first_sum = first_sum + x_ref[...].astype(jnp.float32)
        normed, scale = norm_parts(first_sum)
        n_ref[...] = normed
        r_ref[...] = jnp.broadcast_to(scale, r_ref.shape)
        low_ref[...] = (normed * row(v_ref, GAIN_ONE) + row(v_ref, SHIFT_ONE)).astype(jnp.bfloat16)

    return weight_call(
        place,
        kernel,
        window,
        (contexts, rows, vectors),
        [row_tiles(width), row_tiles(width), fixed(*vectors.shape)],
        [
            shaped((length, width), jnp.float32),
            shaped((length, LANES), jnp.float32),
            shaped((length, width), jnp.bfloat16),
        ],
        [row_tiles(width), row_tiles(LANES), row_tiles(width)],
        length // TILE,
        "all",
        "attn_out",
        2 * length * width * width,
    )


def feed_in(place, normed_low, window, bias):
    length, width = normed_low.shape
    cols = window.cols

    def kernel(where, ready, weight, x_ref, bias_ref, hid_ref, slope_ref):
        ready()
        at = pl.ds(pl.multiple_of((where[2] ^ pl.program_id(0)) * cols, LANES), cols)
        for tile in range(length // TILE):
            here = pl.ds(tile * TILE, TILE)
            pre = mxu(x_ref[here, :], weight[:, at], NN) + bias_ref[:, at]
            share = 0.5 + 0.5 * lax.erf(pre * (1.0 / math.sqrt(2.0)))
            bell = jnp.exp(-0.5 * pre * pre) * (1.0 / math.sqrt(2.0 * math.pi))
            hid_ref[here, :] = (pre * share).astype(jnp.bfloat16)
            slope_ref[here, :] = (share + pre * bell).astype(jnp.bfloat16)

    total = cols * place.groups
    block = pl.BlockSpec((length, cols), lambda i, s: (0, i ^ s[2]))
    return weight_call(
        place,
        kernel,
        window,
        (normed_low, bias),
        [fixed(length, width), fixed(1, total)],
        [shaped((length, total), jnp.bfloat16)] * 2,
        [block, block],
        place.groups,
        "grp",
        "feed_in",
        2 * length * width * total,
    )


def feed_out(place, hidden, window, normed, cot, keep, vectors):
    length, inner = hidden.shape
    width = normed.shape[1]

    def kernel(where, ready, weight, h_ref, n_ref, cot_ref, keep_ref, v_ref, *outs):
        out_ref, grad_ref, low_ref, sum_ref = outs
        ready()
        fed = mxu(h_ref[...], weight[...], NN)
        normed_one = n_ref[...] * row(v_ref, GAIN_ONE) + row(v_ref, SHIFT_ONE)
        second_sum = normed_one + (fed + row(v_ref, B_OUT))
        second, scale = norm_parts(second_sum)
        out_ref[...] = (second * row(v_ref, GAIN_TWO) + row(v_ref, SHIFT_TWO)).astype(jnp.bfloat16)
        masked = cot_ref[...].astype(jnp.float32) * keep_ref[...]
        grad = norm_back(masked * row(v_ref, GAIN_TWO), second, scale)
        grad_ref[...] = grad
        low_ref[...] = grad.astype(jnp.bfloat16)
        add_rows(sum_ref, masked * second, masked, grad)

    return weight_call(
        place,
        kernel,
        window,
        (hidden, normed, cot, keep, vectors),
        [row_tiles(inner), row_tiles(width), row_tiles(width), row_tiles(1), fixed(*vectors.shape)],
        [
            shaped((length, width), jnp.bfloat16),
            shaped((length, width), jnp.float32),
            shaped((length, width), jnp.bfloat16),
            shaped((8, width), jnp.float32),
        ],
        [row_tiles(width), row_tiles(width), row_tiles(width), fixed(8, width)],
        length // TILE,
        "all",
        "feed_out",
        2 * length * width * inner,
    )


def feed_out_back(out_low, weight, slope):
    length, width = out_low.shape
    inner = slope.shape[1]
    cols = min(1024, inner)

    def kernel(g_ref, w_ref, slope_ref, pre_ref, sum_ref):
        total = jnp.zeros((1, cols), jnp.float32)
        for tile in range(length // TILE):
            here = pl.ds(tile * TILE, TILE)
            grad = mxu(g_ref[here, :], w_ref[...], NT) * slope_ref[here, :].astype(jnp.float32)
            pre_ref[here, :] = grad.astype(jnp.bfloat16)
            total = total + jnp.sum(grad, 0, keepdims=True)
        sum_ref[...] = total

    block = pl.BlockSpec((length, cols), lambda i: (0, i))
    return plain_call(
        kernel,
        (out_low, weight, slope),
        [fixed(length, width), pl.BlockSpec((cols, width), lambda i: (i, 0)), block],
        [shaped((length, inner), jnp.bfloat16), shaped((1, inner), jnp.float32)],
        [block, pl.BlockSpec((1, cols), lambda i: (0, i))],
        inner // cols,
        "feed_out_back",
        2 * length * width * inner,
    )


def feed_in_back(pre_low, weight, second_grad, normed, scale, vectors, attn_weight):
    length, inner = pre_low.shape
    width = normed.shape[1]

    def kernel(p_ref, w_ref, g_ref, n_ref, r_ref, v_ref, a_ref, first_ref, low_ref, ctx_ref, sum_ref):
        grad = g_ref[...] + mxu(p_ref[...], w_ref[...], NT)
        first = norm_back(grad * row(v_ref, GAIN_ONE), n_ref[...], r_ref[:, :1])
        low = first.astype(jnp.bfloat16)
        first_ref[...] = first
        low_ref[...] = low
        ctx_ref[...] = mxu(low, a_ref[...], NT).astype(jnp.bfloat16)
        add_rows(sum_ref, grad * n_ref[...], grad, first)

    return plain_call(
        kernel,
        (pre_low, weight, second_grad, normed, scale, vectors, attn_weight),
        [
            row_tiles(inner),
            whole_once(weight.shape),
            row_tiles(width),
            row_tiles(width),
            row_tiles(LANES),
            fixed(*vectors.shape),
            whole_once(attn_weight.shape),
        ],
        [
            shaped((length, width), jnp.float32),
            shaped((length, width), jnp.bfloat16),
            shaped((length, width), jnp.bfloat16),
            shaped((8, width), jnp.float32),
        ],
        [row_tiles(width), row_tiles(width), row_tiles(width), fixed(8, width)],
        length // TILE,
        "feed_in_back",
        2 * length * width * (inner + width),
    )


def project_qkv_back(grads, weight, first_grad, start, tiles, before=None):
    length, width = first_grad.shape
    part = width // len(grads)

    def kernel(w_ref, *refs):
        grad_refs, first_ref, out_ref = refs[: len(grads)], refs[len(grads)], refs[-1]
        total = first_ref[...]
        for n in range(3):
            for m, grad_ref in enumerate(grad_refs):
                at = n * width + m * part
                total = total + mxu(grad_ref[n], w_ref[:, at : at + part], NT)
        out_ref[...] = total

    tile = pl.BlockSpec((TILE, width), lambda i: (start + i, 0))
    more = () if before is None else (before,)
    return pl.pallas_call(
        kernel,
        grid=(tiles,),
        in_specs=[whole_once(weight.shape)]
        + [pl.BlockSpec((3, TILE, part), lambda i: (0, start + i, 0))] * len(grads)
        + [tile]
        + [pl.BlockSpec(memory_space=pl.ANY)] * len(more),
        out_specs=tile,
        out_shape=shaped((length, width), jnp.float32),
        input_output_aliases={} if before is None else {len(grads) + 2: 0},
        compiler_params=params(60),
        cost_estimate=cost(6 * tiles * TILE * width * width),
        name="qkv_back",
    )(weight, *grads, first_grad, *more)


ORDER = (1, 3, 0, 2)


def ordered_slot(j):
    return jnp.where(j < 2, 2 * j + 1, 2 * j - 4)


def weight_grad_kernel(where, *refs, rows, groups, count, split, extra):
    lefts, rights, refs = refs[:count], refs[count : 2 * count], refs[2 * count :]
    sums_ref = None
    if extra:
        sums_ref, *refs = refs
    (leave, keep, sent), kept = refs[:3], refs[3:]
    core = where[0]
    chips = lefts[0].shape[1] // (2 * rows)

    @pl.when(pl.program_id(1) == 0)
    def _():
        for left_ref, kept_ref in zip(lefts, kept):
            for side in range(2):
                chosen = []
                for k in range(chips):
                    even = left_ref[:, 2 * k * rows : (2 * k + 1) * rows]
                    odd = left_ref[:, (2 * k + 1) * rows : (2 * k + 2) * rows]
                    chosen.append(jnp.where(core == side, even, odd))
                left = chosen[0] if chips == 1 else jnp.concatenate(chosen, 1)
                kept_ref[side] = left.T

    def write(ref, pos, side):
        at = 0
        for right_ref, kept_ref in zip(rights, kept):
            if len(right_ref.shape) == 3:
                pieces = [right_ref[n] for n in range(right_ref.shape[0])]
            else:
                size = min(512, right_ref.shape[1])
                pieces = [
                    right_ref[:, n * size : (n + 1) * size]
                    for n in range(right_ref.shape[1] // size)
                ]
            for piece in pieces:
                part = mxu(kept_ref[side], piece, NN).astype(jnp.bfloat16)
                size = piece.shape[1]
                ref[pos, :, 0:rows, at : at + size] = part.reshape(chips, rows, size)
                at += size
        if extra:
            block = where[2] ^ turn(ordered_slot(pl.program_id(1)), core)
            blank = jnp.zeros((extra, at), jnp.bfloat16)
            for k in range(chips):
                start = pl.multiple_of((2 * k + (core ^ side)) * LANES, LANES)
                ref[pos, k, rows : rows + extra, :] = blank
                lines = sums_ref[pl.ds(pl.multiple_of(block * 8, 8), 8), pl.ds(start, LANES)]
                for n in range(3):
                    ref[pos, k, rows : rows + 1, n * LANES : (n + 1) * LANES] = lines[
                        n : n + 1
                    ].astype(jnp.bfloat16)

    if split:
        write(sent, 0, 1)

        @pl.when(pl.program_id(1) < 2)
        def _():
            write(leave, 0, 0)

        @pl.when(pl.program_id(1) >= 2)
        def _():
            write(keep, 0, 0)

    else:
        cols = rights[0].shape[1] // groups
        for side in range(2):
            for pos, slot in enumerate(ORDER):
                start = pl.multiple_of((where[2] ^ turn(slot, core ^ side)) * cols, LANES)
                part = mxu(kept[0][side], rights[0][:, pl.ds(start, cols)], NN)
                part = part.astype(jnp.bfloat16).reshape(chips, rows, cols)
                if side == 1:
                    sent[pos] = part
                else:
                    (leave if pos < 2 else keep)[pos % 2] = part


def weight_grad(place, pairs, split, name, sums=None):
    tokens, height = pairs[0][0].shape
    groups, chips = place.groups, place.chips
    rows = height // place.shards
    step_chips = chips if split else max(1, 1024 // (2 * rows))
    steps = chips // step_chips
    grid = (steps, groups if split else 1)
    extra = 0 if sums is None else 16

    def block(j, s):
        return s[2] ^ turn(ordered_slot(j), s[0])

    def position(j):
        return jnp.where(j == 0, 3, jnp.where(j == 3, 0, j))

    cols = 0
    right_specs = []
    for _, right in pairs:
        size = right.shape[-1] // groups
        if not split:
            right_specs.append(pl.BlockSpec(right.shape, lambda i, j, s: (0, 0)))
        elif right.ndim == 3:
            right_specs.append(
                pl.BlockSpec((right.shape[0], tokens, size), lambda i, j, s: (0, 0, block(j, s)))
            )
        else:
            right_specs.append(pl.BlockSpec((tokens, size), lambda i, j, s: (0, block(j, s))))
        cols += size * (right.shape[0] if right.ndim == 3 else 1)
    left_spec = pl.BlockSpec((tokens, step_chips * 2 * rows), lambda i, j, s: (0, i))
    in_specs = [left_spec] * len(pairs) + right_specs
    inputs = [left for left, _ in pairs] + [right for _, right in pairs]
    if extra:
        in_specs.append(pl.BlockSpec(sums.shape, lambda i, j, s: (0, 0)))
        inputs.append(sums)
    tall = rows + extra
    if split:
        one = (1, step_chips, tall, cols)
        out_specs = [
            pl.BlockSpec(one, lambda i, j, s: (jnp.minimum(j, 1), i, 0, 0)),
            pl.BlockSpec(one, lambda i, j, s: (jnp.maximum(j - 2, 0), i, 0, 0)),
            pl.BlockSpec(one, lambda i, j, s: (position(j), i, 0, 0)),
        ]
    else:
        out_specs = [
            pl.BlockSpec((n, step_chips, tall, cols), lambda i, j, s: (0, i, 0, 0))
            for n in (2, 2, groups)
        ]
    return pl.pallas_call(
        functools.partial(
            weight_grad_kernel,
            rows=rows,
            groups=groups,
            count=len(pairs),
            split=split,
            extra=extra,
        ),
        grid_spec=pltpu.PrefetchScalarGridSpec(
            num_scalar_prefetch=1,
            grid=grid,
            in_specs=in_specs,
            out_specs=out_specs,
            scratch_shapes=[pltpu.VMEM((2, step_chips * rows, tokens), jnp.bfloat16)] * len(pairs),
        ),
        out_shape=[shaped((n, chips, tall, cols), jnp.bfloat16) for n in (2, 2, groups)],
        compiler_params=params(60),
        cost_estimate=cost(2 * tokens * height * cols * groups),
        name="wgrad_" + name,
    )(place.scalars, *inputs)


def add(*terms):
    total = terms[0].astype(jnp.float32)
    for term in terms[1:]:
        total = total + term.astype(jnp.float32)
    return total.astype(jnp.bfloat16)


class Reduction:
    def __init__(self, place, pairs, split, name, *wait, sums=None):
        self.place = place
        pairs = [(after(pairs[0][0], *wait), pairs[0][1])] + pairs[1:]
        self.leave, self.keep, sent = weight_grad(place, pairs, split, name, sums)
        self.made = self.leave
        self.flying = place.swap_core(sent)

    def near(self):
        self.core = self.flying
        leave = add(self.leave, self.core[:2])
        self.flying = self.place.swap_grp(leave, 0)
        return leave

    def middle(self):
        self.first = self.flying
        second = add(self.keep[1], self.core[3], self.first[1])
        self.flying = self.place.swap_grp(second, 1)
        return second

    def column(self):
        mine = add(self.keep[0], self.core[2], self.first[0], self.flying)
        return mine, lambda chip: lax.dynamic_index_in_dim(mine, chip, 0, False)

    def along(self):
        place = self.place
        mine, at = self.column()
        self.mine = [at(place.slot_chip(slot)) for slot in range(4)]
        both = jnp.stack([self.mine[1], self.mine[3]])
        self.flying = place.swap_chip(both, 0)
        return both

    def along_far(self):
        self.first = self.flying
        second = add(self.mine[2], self.first[1])
        self.flying = self.place.swap_chip(second, 1)
        return second

    def share(self):
        return add(self.mine[0], self.first[0], self.flying)

    def share_direct(self):
        place = self.place
        mine, at = self.column()
        terms = [
            place.permute(at(place.chip ^ k), (2 * k, 2 * k)) for k in range(place.chips - 1, 0, -1)
        ]
        return add(at(place.chip), *terms)


class Replication:
    def __init__(self, place, share, direct=False):
        self.place = place
        self.blocks = [share] + [None] * 3
        if direct:
            size = place.shards
            for mask in (3, 1, 2):
                self.blocks[mask] = place.permute(share, (mask * size, mask * size))
            self.owner = lambda n: place.grp ^ n
        else:
            self.flying = place.swap_grp(share, 0)
            self.owner = place.slot_grp

    def far(self):
        pair = jnp.stack([self.blocks[0], self.flying])
        self.blocks[1] = self.flying
        self.flying = self.place.swap_grp(pair, 1)
        return pair

    def result(self):
        blocks = self.blocks
        if blocks[2] is None:
            blocks = [*blocks[:2], self.flying[0], self.flying[1]]
        ordered = []
        for g in range(self.place.groups):
            block = blocks[0]
            for n in range(1, self.place.groups):
                block = jnp.where(self.owner(n) == g, blocks[n], block)
            ordered.append(block.astype(jnp.float32))
        return ordered


def on_device_permutes(
    tokens,
    segment_ids,
    keep_flag,
    cotangent,
    w_qkv,
    b_query,
    b_value,
    w_attn_out,
    b_attn_out,
    norm1_gain,
    norm1_bias,
    w_in,
    b_in,
    w_out,
    b_out,
    norm2_gain,
    norm2_bias,
    *,
    groups,
    shards,
):
    place = Place(groups, shards)
    _, length, width = tokens.shape
    rows = tokens[0]
    seg_row = segment_ids.reshape(1, length)
    seg_col = segment_ids.reshape(length, 1)
    keep = keep_flag.reshape(length, 1).astype(jnp.float32)
    pairs = width // LANES

    c1 = Gather(place, w_qkv)
    c2 = Gather(place, jnp.concatenate([w_in, w_attn_out], 1))
    c3 = Gather(place, w_out)
    c1.chips_near()
    c1.chips_far()
    joined = c1.near()
    small = Vectors(
        place,
        (b_query, b_value, b_attn_out, norm1_gain, norm1_bias, b_out, norm2_gain, norm2_bias, b_in),
        joined,
    )
    c2.chips_near(joined)
    pair = c2.chips_far()
    c1.flying = lax.optimization_barrier(c1.flying)
    c1.far(pair)
    c1.cross(0, 1, 2)
    vectors, bias_in, qkv_bias = small.unpack()
    meet(vectors, c1, c2)
    c1.landed()
    c1.cross(3)
    c2.near()
    blank = jnp.ones((1, width), jnp.float32)
    qkv_scale = jnp.concatenate([blank / math.sqrt(HD), blank, blank], 1)

    mixed, full_qkv = project_qkv(place, rows, Window(c1, 0, w_qkv.shape[1]), qkv_bias, qkv_scale)
    c3.chips_near(mixed)
    c2.cross(0, wait=(mixed,))
    first, second = pairs * 3 // 8, pairs * 3 // 4
    forward = attention_forward(mixed, seg_col, seg_row, 0, first)
    meet(forward[1], c2, c3)
    c2.far()
    pair = c3.chips_far()
    c2.cross(1, 2)
    forward = attention_forward(after(mixed, pair), seg_col, seg_row, first, second - first, forward)
    meet(forward[1], c2, c3)
    c2.landed()
    c2.cross(3)
    joined = c3.near()
    contexts, lse = attention_forward(
        after(mixed, joined), seg_col, seg_row, second, pairs - second, forward
    )
    normed, scale_one, normed_low, full_attn = project_out(
        place, contexts, Window(c2, w_in.shape[1], w_attn_out.shape[1]), rows, vectors
    )
    meet(normed_low, c3)
    c3.far()
    c3.cross(0, 1, 2)
    hidden, slope, full_in = feed_in(
        place, after(normed_low, c3.held[1]), Window(c2, 0, w_in.shape[1]), bias_in
    )
    meet(hidden, c3)
    c3.landed()
    c3.cross(3)
    layer_out, second_grad, out_low, second_sums, full_out = feed_out(
        place, hidden, Window(c3, 0, w_out.shape[1]), normed, cotangent[0], keep, vectors
    )

    r_out = Reduction(place, [(hidden, out_low)], False, "out")
    pre_low, bias_in_grad = feed_out_back(after(out_low, r_out.made), full_out, slope)
    meet(pre_low, r_out)
    step = r_out.near()
    r_in = Reduction(place, [(normed_low, pre_low)], True, "in", step)
    first_grad, attn_low, context_grad, first_sums = feed_in_back(
        after(pre_low, r_in.made), full_in, second_grad, normed, scale_one, vectors, full_attn
    )
    meet(attn_low, r_out, r_in)
    steps = (r_out.middle(), r_in.near())
    half, quarter = pairs // 2, pairs // 4

    def back(wait, start, count, at, before=None):
        return attention_backward(
            mixed,
            contexts,
            after(context_grad, *wait),
            seg_col,
            seg_row,
            lse,
            start,
            count,
            at,
            half,
            before,
        )

    low_a, late_a = back(steps, 0, half, 0)
    meet(late_a, r_out, r_in)
    steps = (r_out.along(), r_in.middle())
    r_a = Reduction(place, [(contexts, attn_low), (rows, low_a)], True, "a", *steps)
    meet(r_a.made, r_out, r_in)
    steps = (r_out.along_far(), r_in.along())
    part = back((r_a.made, *steps), half, quarter, 0)
    meet(part[1], r_out, r_in, r_a)
    steps = (r_out.share(), r_in.along_far(), r_a.near())
    share_out = steps[0]
    low_b, late_b = back(steps, half + quarter, quarter, quarter, part)
    meet(late_b, r_in, r_a)
    share_in = r_in.share()
    inner = share_in.shape[1] // groups
    joined = jnp.concatenate(
        [share_out] + [share_in[:, n * inner : (n + 1) * inner] for n in range(groups)]
    )
    all_ffn = Replication(place, joined)
    sums = pack_sums(late_a, late_b, first_sums, second_sums, bias_in_grad)
    r_b = Reduction(place, [(rows, low_b)], True, "b", joined, r_a.middle(), sums=sums)
    meet(r_b.made, r_a, all_ffn)
    steps = (r_a.along(), all_ffn.far())
    grads = (low_a, after(low_b, r_b.made, *steps))
    tiles = length // TILE // 2
    input_grad = project_qkv_back(grads, full_qkv, first_grad, 0, tiles)
    meet(input_grad, r_b)
    step = r_b.near()
    input_grad = project_qkv_back(
        grads, full_qkv, after(first_grad, step), tiles, tiles, input_grad
    )
    meet(input_grad, r_b, r_a)
    r_b.middle()
    r_a.along_far()
    share_b = r_b.share_direct()
    all_a = Replication(place, r_a.share())
    all_b = Replication(place, share_b, direct=True)
    all_a.far()

    parts_a, parts_b = all_a.result(), all_b.result()
    small = [
        block[-16, n * LANES : (n + 1) * LANES] for block in parts_b for n in range(3)
    ]
    inner_mine = jnp.concatenate(small[B_IN:])
    parts_b = [block[:-16] for block in parts_b]
    heads = parts_b[0].shape[1] // 3
    skip = parts_a[0].shape[1] - 3 * heads
    w_attn_grad = jnp.concatenate([block[:, :skip] for block in parts_a], 1)
    parts_a = [block[:, skip:] for block in parts_a]
    w_qkv_grad = jnp.concatenate(
        [
            block[:, n * heads : (n + 1) * heads]
            for n in range(3)
            for half in (parts_a, parts_b)
            for block in half
        ],
        1,
    )
    parts = all_ffn.result()
    height = share_out.shape[0]
    w_out_grad = jnp.concatenate([block[:height] for block in parts], 1)
    size = share_in.shape[0]
    w_in_grad = jnp.concatenate(
        [
            block[height + n * size : height + (n + 1) * size]
            for block in parts
            for n in range(groups)
        ],
        1,
    )
    return (
        layer_out[None],
        input_grad[None],
        w_qkv_grad,
        small[B_QUERY],
        small[B_VALUE],
        w_attn_grad,
        small[B_ATTN],
        small[GAIN_ONE],
        small[SHIFT_ONE],
        w_in_grad,
        inner_mine,
        w_out_grad,
        small[B_OUT],
        small[GAIN_TWO],
        small[SHIFT_TWO],
    )


def solution(mesh):
    groups, shards = mesh.shape["grp"], mesh.shape["shard"]
    if groups == 4 and shards == 8:
        body = functools.partial(on_device_permutes, groups=groups, shards=shards)
    else:
        body = on_device
    return jax.shard_map(
        body,
        mesh=mesh,
        in_specs=(
            P(("grp", "shard"), None, None),
            P(("grp", "shard"), None),
            P(("grp", "shard"), None),
            P(("grp", "shard"), None, None),
            P("shard", "grp"),
            P("shard"),
            P("shard"),
            P("shard", "grp"),
            P("shard"),
            P("shard"),
            P("shard"),
            P("shard", "grp"),
            P("shard"),
            P("shard", "grp"),
            P("shard"),
            P("shard"),
            P("shard"),
        ),
        out_specs=(
            P(("grp", "shard"), None, None),
            P(("grp", "shard"), None, None),
            P("shard", None),
            P("shard"),
            P("shard"),
            P("shard", None),
            P("shard"),
            P("shard"),
            P("shard"),
            P("shard", None),
            P("shard"),
            P("shard", None),
            P("shard"),
            P("shard"),
            P("shard"),
        ),
        check_vma=False,
    )
```

```python
import functools
import math

import jax
import jax.numpy as jnp
from jax import lax
from jax.experimental import pallas as pl
from jax.experimental.pallas import tpu as pltpu
from jax.sharding import PartitionSpec as P

H = 16
HD = 64


masked_score = -1e30
epsilon = 1e-05


def norm_layer(rows, gain_row, shift_row):
    row_mean = jnp.mean(rows, -1, keepdims=True)
    centered = rows - row_mean
    row_var = jnp.mean(centered * centered, -1, keepdims=True)
    return centered * lax.rsqrt(row_var + epsilon) * gain_row + shift_row


def gelu_exact(values):
    return 0.5 * values * (1.0 + lax.erf(values * (1.0 / math.sqrt(2.0))))


def contract_rows(left, right):
    return lax.dot_general(
        left, right, (((0,), (0,)), ((), ())), preferred_element_type=jnp.float32
    )


def contract_cols(left, right):
    return lax.dot_general(
        left, right, (((1,), (1,)), ((), ())), preferred_element_type=jnp.float32
    )


def attend_forward(queries, key_rows, value_rows, segment_row, block_rows):
    length, model_width = queries.shape
    scaling = 1.0 / math.sqrt(HD)
    key_heads = key_rows.reshape(length, H, HD)
    value_heads = value_rows.reshape(length, H, HD)
    query_blocks = queries.reshape(length // block_rows, block_rows, H, HD)
    segment_blocks = segment_row.reshape(length // block_rows, block_rows)

    def one_block(pieces):
        query_part, segment_part = pieces
        scores = (
            jnp.einsum("qhd,khd->hqk", query_part, key_heads, preferred_element_type=jnp.float32)
            * scaling
        )
        allowed = segment_part[:, None] == segment_row[None, :]
        scores = jnp.where(allowed[None], scores, masked_score)
        row_max = jnp.max(scores, -1, keepdims=True)
        powers = jnp.exp(scores - row_max)
        totals = jnp.sum(powers, -1, keepdims=True)
        attn_probs = (powers / totals).astype(jnp.bfloat16)
        context = jnp.einsum(
            "hqk,khd->qhd", attn_probs, value_heads, preferred_element_type=jnp.float32
        )
        return (
            context.reshape(block_rows, model_width).astype(jnp.bfloat16),
            (row_max + jnp.log(totals))[:, :, 0],
        )

    contexts, log_sums = lax.map(one_block, (query_blocks, segment_blocks))
    return (contexts.reshape(length, model_width), log_sums)


def attend_backward(queries, key_rows, value_rows, segment_row, log_sums, context_grad, block_rows):
    length, model_width = queries.shape
    scaling = 1.0 / math.sqrt(HD)
    key_heads = key_rows.reshape(length, H, HD)
    value_heads = value_rows.reshape(length, H, HD)
    query_blocks = queries.reshape(length // block_rows, block_rows, H, HD)
    segment_blocks = segment_row.reshape(length // block_rows, block_rows)
    grad_blocks = context_grad.reshape(length // block_rows, block_rows, H, HD)

    def one_block(running, pieces):
        key_acc, value_acc = running
        query_part, segment_part, lse_part, grad_part = pieces
        scores = (
            jnp.einsum("qhd,khd->hqk", query_part, key_heads, preferred_element_type=jnp.float32)
            * scaling
        )
        allowed = segment_part[:, None] == segment_row[None, :]
        scores = jnp.where(allowed[None], scores, masked_score)
        probs = jnp.exp(scores - lse_part[:, :, None])
        prob_low = probs.astype(jnp.bfloat16)
        prob_grad = jnp.einsum(
            "qhd,khd->hqk", grad_part, value_heads, preferred_element_type=jnp.float32
        )
        row_dot = jnp.sum(prob_grad * probs, -1, keepdims=True)
        score_grad = (probs * (prob_grad - row_dot)).astype(jnp.bfloat16)
        query_grad = (
            jnp.einsum("hqk,khd->qhd", score_grad, key_heads, preferred_element_type=jnp.float32)
            * scaling
        )
        key_acc = (
            key_acc
            + jnp.einsum("hqk,qhd->khd", score_grad, query_part, preferred_element_type=jnp.float32)
            * scaling
        )
        value_acc = value_acc + jnp.einsum(
            "hqk,qhd->khd", prob_low, grad_part, preferred_element_type=jnp.float32
        )
        return ((key_acc, value_acc), query_grad.reshape(block_rows, model_width))

    empty_acc = jnp.zeros((length, H, HD), jnp.float32)
    (key_grad, value_grad), query_grads = lax.scan(
        one_block, (empty_acc, empty_acc), (query_blocks, segment_blocks, log_sums, grad_blocks)
    )
    return (
        query_grads.reshape(length, model_width),
        key_grad.reshape(length, model_width),
        value_grad.reshape(length, model_width),
    )


def on_device(
    tokens,
    segment_ids,
    keep_flag,
    cotangent,
    w_qkv,
    b_query,
    b_value,
    w_attn_out,
    b_attn_out,
    norm1_gain,
    norm1_bias,
    w_in,
    b_in,
    w_out,
    b_out,
    norm2_gain,
    norm2_bias,
):
    seq_count, length, model_width = tokens.shape
    block_rows = min(512, length)
    within = (
        lax.all_gather(w_qkv, "shard", axis=0, tiled=True),
        lax.all_gather(w_attn_out, "shard", axis=0, tiled=True),
        lax.all_gather(w_in, "shard", axis=0, tiled=True),
        lax.all_gather(w_out, "shard", axis=0, tiled=True),
        lax.all_gather(b_query, "shard", axis=0, tiled=True),
        lax.all_gather(b_value, "shard", axis=0, tiled=True),
        lax.all_gather(b_attn_out, "shard", axis=0, tiled=True),
        lax.all_gather(norm1_gain, "shard", axis=0, tiled=True),
        lax.all_gather(norm1_bias, "shard", axis=0, tiled=True),
        lax.all_gather(b_in, "shard", axis=0, tiled=True),
        lax.all_gather(b_out, "shard", axis=0, tiled=True),
        lax.all_gather(norm2_gain, "shard", axis=0, tiled=True),
        lax.all_gather(norm2_bias, "shard", axis=0, tiled=True),
    )
    full_qkv, full_attn, full_in, full_out = (
        lax.all_gather(within[0], "grp", axis=1, tiled=True),
        lax.all_gather(within[1], "grp", axis=1, tiled=True),
        lax.all_gather(within[2], "grp", axis=1, tiled=True),
        lax.all_gather(within[3], "grp", axis=1, tiled=True),
    )
    (
        bias_query,
        bias_value,
        bias_attn,
        gain_one,
        shift_one,
        bias_in,
        bias_out,
        gain_two,
        shift_two,
    ) = [piece.astype(jnp.float32) for piece in within[4:]]
    flat_rows = tokens.reshape(seq_count * length, model_width)
    mixed_qkv = jnp.dot(flat_rows, full_qkv, preferred_element_type=jnp.float32)
    queries = (mixed_qkv[:, :model_width] + bias_query).astype(jnp.bfloat16)
    key_rows = mixed_qkv[:, model_width : 2 * model_width].astype(jnp.bfloat16)
    value_rows = (mixed_qkv[:, 2 * model_width :] + bias_value).astype(jnp.bfloat16)
    query_seqs = queries.reshape(seq_count, length, model_width)
    key_seqs = key_rows.reshape(seq_count, length, model_width)
    value_seqs = value_rows.reshape(seq_count, length, model_width)

    def forward_sequence(pieces):
        return attend_forward(pieces[0], pieces[1], pieces[2], pieces[3], block_rows)

    contexts, log_sums = lax.map(forward_sequence, (query_seqs, key_seqs, value_seqs, segment_ids))
    contexts = contexts.reshape(seq_count * length, model_width)
    attended = jnp.dot(contexts, full_attn, preferred_element_type=jnp.float32) + bias_attn
    first_sum = flat_rows.astype(jnp.float32) + attended
    normed_one, norm_one_back = jax.vjp(norm_layer, first_sum, gain_one, shift_one)
    normed_low = normed_one.astype(jnp.bfloat16)
    hidden_pre = jnp.dot(normed_low, full_in, preferred_element_type=jnp.float32) + bias_in
    hidden, gelu_back = jax.vjp(gelu_exact, hidden_pre)
    hidden_low = hidden.astype(jnp.bfloat16)
    second_sum = normed_one + (
        jnp.dot(hidden_low, full_out, preferred_element_type=jnp.float32) + bias_out
    )
    result, norm_two_back = jax.vjp(norm_layer, second_sum, gain_two, shift_two)
    layer_out = result.astype(jnp.bfloat16).reshape(seq_count, length, model_width)
    again = (
        lax.all_gather(w_qkv, "shard", axis=0, tiled=True),
        lax.all_gather(w_attn_out, "shard", axis=0, tiled=True),
        lax.all_gather(w_in, "shard", axis=0, tiled=True),
        lax.all_gather(w_out, "shard", axis=0, tiled=True),
    )
    back_qkv, back_attn, back_in, back_out = (
        lax.all_gather(again[0], "grp", axis=1, tiled=True),
        lax.all_gather(again[1], "grp", axis=1, tiled=True),
        lax.all_gather(again[2], "grp", axis=1, tiled=True),
        lax.all_gather(again[3], "grp", axis=1, tiled=True),
    )
    masked_cot = cotangent.astype(jnp.float32).reshape(
        seq_count * length, model_width
    ) * keep_flag.reshape(seq_count * length, 1).astype(jnp.float32)
    second_grad, gain_two_grad, shift_two_grad = norm_two_back(masked_cot)
    bias_out_grad = jnp.sum(second_grad, 0)
    out_low = second_grad.astype(jnp.bfloat16)
    w_out_grad = contract_rows(hidden_low, out_low)
    hidden_grad = contract_cols(out_low, back_out)
    (pre_grad,) = gelu_back(hidden_grad)
    bias_in_grad = jnp.sum(pre_grad, 0)
    pre_low = pre_grad.astype(jnp.bfloat16)
    w_in_grad = contract_rows(normed_low, pre_low)
    normed_grad = second_grad + contract_cols(pre_low, back_in)
    first_grad, gain_one_grad, shift_one_grad = norm_one_back(normed_grad)
    bias_attn_grad = jnp.sum(first_grad, 0)
    attn_low = first_grad.astype(jnp.bfloat16)
    w_attn_grad = contract_rows(contexts, attn_low)
    context_grad = contract_cols(attn_low, back_attn).astype(jnp.bfloat16)

    def backward_sequence(pieces):
        return attend_backward(
            pieces[0], pieces[1], pieces[2], pieces[3], pieces[4], pieces[5], block_rows
        )

    query_grad, key_grad, value_grad = lax.map(
        backward_sequence,
        (
            query_seqs,
            key_seqs,
            value_seqs,
            segment_ids,
            log_sums,
            context_grad.reshape(seq_count, length, model_width),
        ),
    )
    query_grad = query_grad.reshape(seq_count * length, model_width)
    key_grad = key_grad.reshape(seq_count * length, model_width)
    value_grad = value_grad.reshape(seq_count * length, model_width)
    bias_query_grad = jnp.sum(query_grad, 0)
    bias_value_grad = jnp.sum(value_grad, 0)
    qkv_low = jnp.concatenate([query_grad, key_grad, value_grad], 1).astype(jnp.bfloat16)
    w_qkv_grad = contract_rows(flat_rows, qkv_low)
    input_grad = first_grad + contract_cols(qkv_low, back_qkv)
    reduced = (
        lax.psum_scatter(
            w_qkv_grad.astype(jnp.bfloat16), "shard", scatter_dimension=0, tiled=True
        ).astype(jnp.float32),
        lax.psum_scatter(
            bias_query_grad.astype(jnp.bfloat16), "shard", scatter_dimension=0, tiled=True
        ).astype(jnp.float32),
        lax.psum_scatter(
            bias_value_grad.astype(jnp.bfloat16), "shard", scatter_dimension=0, tiled=True
        ).astype(jnp.float32),
        lax.psum_scatter(
            w_attn_grad.astype(jnp.bfloat16), "shard", scatter_dimension=0, tiled=True
        ).astype(jnp.float32),
        lax.psum_scatter(
            bias_attn_grad.astype(jnp.bfloat16), "shard", scatter_dimension=0, tiled=True
        ).astype(jnp.float32),
        lax.psum_scatter(
            gain_one_grad.astype(jnp.bfloat16), "shard", scatter_dimension=0, tiled=True
        ).astype(jnp.float32),
        lax.psum_scatter(
            shift_one_grad.astype(jnp.bfloat16), "shard", scatter_dimension=0, tiled=True
        ).astype(jnp.float32),
        lax.psum_scatter(
            w_in_grad.astype(jnp.bfloat16), "shard", scatter_dimension=0, tiled=True
        ).astype(jnp.float32),
        lax.psum_scatter(
            bias_in_grad.astype(jnp.bfloat16), "shard", scatter_dimension=0, tiled=True
        ).astype(jnp.float32),
        lax.psum_scatter(
            w_out_grad.astype(jnp.bfloat16), "shard", scatter_dimension=0, tiled=True
        ).astype(jnp.float32),
        lax.psum_scatter(
            bias_out_grad.astype(jnp.bfloat16), "shard", scatter_dimension=0, tiled=True
        ).astype(jnp.float32),
        lax.psum_scatter(
            gain_two_grad.astype(jnp.bfloat16), "shard", scatter_dimension=0, tiled=True
        ).astype(jnp.float32),
        lax.psum_scatter(
            shift_two_grad.astype(jnp.bfloat16), "shard", scatter_dimension=0, tiled=True
        ).astype(jnp.float32),
    )
    summed = (
        lax.psum(reduced[0].astype(jnp.bfloat16), "grp").astype(jnp.float32),
        lax.psum(reduced[1].astype(jnp.bfloat16), "grp").astype(jnp.float32),
        lax.psum(reduced[2].astype(jnp.bfloat16), "grp").astype(jnp.float32),
        lax.psum(reduced[3].astype(jnp.bfloat16), "grp").astype(jnp.float32),
        lax.psum(reduced[4].astype(jnp.bfloat16), "grp").astype(jnp.float32),
        lax.psum(reduced[5].astype(jnp.bfloat16), "grp").astype(jnp.float32),
        lax.psum(reduced[6].astype(jnp.bfloat16), "grp").astype(jnp.float32),
        lax.psum(reduced[7].astype(jnp.bfloat16), "grp").astype(jnp.float32),
        lax.psum(reduced[8].astype(jnp.bfloat16), "grp").astype(jnp.float32),
        lax.psum(reduced[9].astype(jnp.bfloat16), "grp").astype(jnp.float32),
        lax.psum(reduced[10].astype(jnp.bfloat16), "grp").astype(jnp.float32),
        lax.psum(reduced[11].astype(jnp.bfloat16), "grp").astype(jnp.float32),
        lax.psum(reduced[12].astype(jnp.bfloat16), "grp").astype(jnp.float32),
    )
    return (
        layer_out,
        input_grad.reshape(seq_count, length, model_width),
        summed[0],
        summed[1],
        summed[2],
        summed[3],
        summed[4],
        summed[5],
        summed[6],
        summed[7],
        summed[8],
        summed[9],
        summed[10],
        summed[11],
        summed[12],
    )


NT = (((1,), (1,)), ((), ()))
NN = (((1,), (0,)), ((), ()))
TN = (((0,), (0,)), ((), ()))
LANES = 128
AXES = ("grp", "shard")


def mxu(left, right, dims):
    return lax.dot_general(left, right, dims, preferred_element_type=jnp.float32)


def cost(flops):
    return pl.CostEstimate(flops=2 * flops, bytes_accessed=0, transcendentals=0)


def params(megabytes=60):
    return pltpu.CompilerParams(vmem_limit_bytes=megabytes << 20)


def attention_forward_kernel(q_ref, k_ref, v_ref, seg_col, seg_row, out_ref, lse_ref, *, rows):
    length = q_ref.shape[0]
    first = lax.broadcasted_iota(jnp.int32, (1, LANES), 1) < HD
    keys = k_ref[...]
    values = v_ref[...]
    zero = jnp.zeros_like(keys)
    head_keys = (jnp.where(first, keys, zero), jnp.where(first, zero, keys))
    key_segments = seg_col[...]
    for block in range(length // rows):
        here = pl.ds(block * rows, rows)
        q = q_ref[here, :]
        allowed = key_segments == seg_row[:, here]
        outs = []
        for head in range(2):
            scores = mxu(head_keys[head], q, NT)
            scores = jnp.where(allowed, scores, masked_score)
            top = jnp.max(scores, 0, keepdims=True)
            powers = jnp.exp(scores - top)
            total = jnp.sum(powers, 0, keepdims=True)
            part = mxu(powers.astype(jnp.bfloat16), values, TN)
            outs.append(part * jnp.transpose(jnp.broadcast_to(1.0 / total, (LANES, rows))))
            lse_ref[0, head : head + 1, here] = top + jnp.log(total)
        out_ref[here, :] = jnp.where(first, outs[0], outs[1]).astype(jnp.bfloat16)


def attention_forward(qkv, seg_col, seg_row, start, pairs, before=None):
    length, width = qkv.shape[0], qkv.shape[1] // 3
    total = width // LANES
    rows = min(512, length)
    anywhere = pl.BlockSpec(memory_space=pl.ANY)

    def pair(part):
        return pl.BlockSpec((length, LANES), lambda j: (0, part * total + start + j))

    def body(q_ref, k_ref, v_ref, seg_c, seg_r, *refs):
        attention_forward_kernel(q_ref, k_ref, v_ref, seg_c, seg_r, *refs[-2:], rows=rows)

    return pl.pallas_call(
        body,
        grid=(pairs,),
        in_specs=[
            pair(0),
            pair(1),
            pair(2),
            pl.BlockSpec((length, 1), lambda j: (0, 0)),
            pl.BlockSpec((1, length), lambda j: (0, 0)),
        ]
        + [anywhere] * (0 if before is None else 2),
        out_specs=[
            pl.BlockSpec((length, LANES), lambda j: (0, start + j)),
            pl.BlockSpec((1, 2, length), lambda j: (start + j, 0, 0)),
        ],
        out_shape=[
            jax.ShapeDtypeStruct((length, width), jnp.bfloat16),
            jax.ShapeDtypeStruct((total, 2, length), jnp.float32),
        ],
        input_output_aliases={} if before is None else {5: 0, 6: 1},
        compiler_params=params(60),
        cost_estimate=cost(16 * length * length * pairs * LANES),
        name="attn_fwd",
    )(qkv, qkv, qkv, seg_col, seg_row, *(() if before is None else before))


def attention_backward_kernel(
    q_ref, k_ref, v_ref, o_ref, do_ref, seg_col, seg_row, lse_ref, grad_ref, sum_ref, *, rows
):
    length = q_ref.shape[0]
    lane = lax.broadcasted_iota(jnp.int32, (1, LANES), 1)
    first = lane < HD
    pick = (
        lax.broadcasted_iota(jnp.int32, (8, LANES), 0)
        == lax.broadcasted_iota(jnp.int32, (8, LANES), 1) // HD
    ).astype(jnp.float32)
    keys = k_ref[...]
    values = v_ref[...]
    zero = jnp.zeros_like(keys)
    head_keys = (jnp.where(first, keys, zero), jnp.where(first, zero, keys))
    head_values = (jnp.where(first, values, zero), jnp.where(first, zero, values))
    key_segments = seg_col[...]
    key_sum = [None, None]
    value_sum = [None, None]
    query_total = jnp.zeros((1, LANES), jnp.float32)
    for block in range(length // rows):
        here = pl.ds(block * rows, rows)
        q = q_ref[here, :]
        do = do_ref[here, :]
        allowed = key_segments == seg_row[:, here]
        dots = lax.dot_general(
            pick,
            do.astype(jnp.float32) * o_ref[here, :].astype(jnp.float32),
            NT,
            precision=lax.Precision.HIGHEST,
            preferred_element_type=jnp.float32,
        )
        parts = []
        for head in range(2):
            scores = mxu(head_keys[head], q, NT)
            scores = jnp.where(allowed, scores, masked_score)
            probs = jnp.exp(scores - lse_ref[0, head : head + 1, here])
            prob_grad = mxu(head_values[head], do, NT)
            score_grad = (probs * (prob_grad - dots[head : head + 1, :])).astype(jnp.bfloat16)
            value_part = mxu(probs.astype(jnp.bfloat16), do, NN)
            key_part = mxu(score_grad, q, NN)
            value_sum[head] = value_part if block == 0 else value_sum[head] + value_part
            key_sum[head] = key_part if block == 0 else key_sum[head] + key_part
            parts.append(mxu(score_grad, keys, TN))
        query_grad = jnp.where(first, parts[0], parts[1]) * (1.0 / math.sqrt(HD))
        query_total = query_total + jnp.sum(query_grad, 0, keepdims=True)
        grad_ref[0, here, :] = query_grad.astype(jnp.bfloat16)
    grad_ref[1, :, :] = jnp.where(first, key_sum[0], key_sum[1]).astype(jnp.bfloat16)
    value_grad = jnp.where(first, value_sum[0], value_sum[1])
    grad_ref[2, :, :] = value_grad.astype(jnp.bfloat16)
    sum_ref[0:1, :] = query_total
    sum_ref[1:2, :] = jnp.sum(value_grad, 0, keepdims=True)


def attention_backward(qkv, out, out_grad, seg_col, seg_row, lse, start, pairs, at, size, before=None):
    length, width = out.shape
    total = width // LANES
    rows = min(256, length)
    more = () if before is None else before

    def pair(part):
        return pl.BlockSpec((length, LANES), lambda j: (0, part * total + start + j))

    def body(*refs):
        attention_backward_kernel(*refs[:8], *refs[-2:], rows=rows)

    return pl.pallas_call(
        body,
        grid=(pairs,),
        in_specs=[
            pair(0),
            pair(1),
            pair(2),
            pair(0),
            pair(0),
            pl.BlockSpec((length, 1), lambda j: (0, 0)),
            pl.BlockSpec((1, length), lambda j: (0, 0)),
            pl.BlockSpec((1, 2, length), lambda j: (j + start, 0, 0)),
        ]
        + [pl.BlockSpec(memory_space=pl.ANY)] * len(more),
        out_specs=[
            pl.BlockSpec((3, length, LANES), lambda j: (0, 0, j + at)),
            pl.BlockSpec((2, LANES), lambda j: (0, j + at)),
        ],
        out_shape=[
            jax.ShapeDtypeStruct((3, length, size * LANES), jnp.bfloat16),
            jax.ShapeDtypeStruct((2, size * LANES), jnp.float32),
        ],
        input_output_aliases={} if before is None else {8: 0, 9: 1},
        compiler_params=params(60),
        cost_estimate=cost(40 * length * length * pairs * LANES),
        name="attn_bwd",
    )(qkv, qkv, qkv, out, out_grad, seg_col, seg_row, lse, *more)


class Place:
    def __init__(self, groups, shards):
        self.groups = groups
        self.shards = shards
        self.chips = shards // 2
        self.grp = lax.axis_index("grp")
        self.shard = lax.axis_index("shard")
        self.core = self.shard % 2
        self.chip = self.shard // 2
        self.scalars = jnp.stack([self.core, self.chip, self.grp]).astype(jnp.int32)

    def permute(self, array, mask_of_core):
        pairs = [(i, i ^ mask_of_core[i % 2]) for i in range(self.groups * self.shards)]
        return lax.ppermute(array, AXES, pairs)

    def swap_core(self, array):
        return self.permute(array, (1, 1))

    def swap_grp(self, array, step):
        masks = (self.shards, 2 * self.shards)
        return self.permute(array, masks if step == 0 else masks[::-1])

    def swap_chip(self, array, step):
        masks = (2, 4)
        return self.permute(array, masks if step == 0 else masks[::-1])

    def slot_chip(self, slot):
        return self.chip ^ turn(slot, self.core)

    def slot_grp(self, slot):
        return self.grp ^ turn(slot, self.core)


def turn(slot, core):
    if isinstance(slot, int):
        return slot if slot in (0, 3) else jnp.where(core == 0, slot, 3 - slot)
    return jnp.where((core == 0) | (slot == 0) | (slot == 3), slot, 3 - slot)


def after(value, *others):
    return lax.optimization_barrier((value, *others))[0]


def meet(anchor, *flights):
    arrays = [f.flying for f in flights]
    _, *arrays = lax.optimization_barrier((anchor, *arrays))
    for f, array in zip(flights, arrays):
        f.flying = array


class Gather:
    def __init__(self, place, piece):
        self.place = place
        self.piece = piece
        self.held = [None] * 4
        self.crossed = [None] * 4

    def chips_near(self, *wait):
        self.piece = after(self.piece, *wait)
        self.flying = self.place.swap_chip(self.piece, 0)

    def chips_far(self):
        self.pair = jnp.stack([self.piece, self.flying])
        self.flying = self.place.swap_chip(self.pair, 1)
        return self.pair

    def join(self):
        self.held[0] = jnp.concatenate([self.pair, self.flying])
        return self.held[0]

    def near(self, *wait):
        self.held[0] = after(self.held[0], *wait)
        self.flying = (self.place.swap_grp(self.held[0], 0), self.place.swap_grp(self.held[0], 1))
        return self.held[0]

    def far(self, *wait):
        self.held[1:3] = self.flying
        first = after(self.held[1], *wait)
        self.flying = self.place.swap_grp(first, 1)

    def landed(self):
        self.held[3] = self.flying

    def cross(self, *which, wait=()):
        for n in which:
            self.crossed[n] = self.place.swap_core(after(self.held[n], *wait))

    def pieces(self):
        return self.held + self.crossed


class Window:
    def __init__(self, gather, start, cols):
        self.arrays = gather.pieces()
        self.start, self.cols = start, cols
        chips, rows, _ = self.arrays[0].shape
        self.chips, self.rows = chips, rows


def fetch(where, window, refs, whole, sem, by):
    rows, cols, chips = window.rows, window.cols, window.chips
    for slot in range(4):
        for side in range(2):
            core = where[0] ^ side
            ref = refs[4 * side + slot]
            distance = turn(slot, core)
            col = pl.multiple_of((where[2] ^ distance) * cols, LANES)
            for k in range(chips):
                row = ((where[1] ^ turn(k, core)) * 2 + core) * rows
                pltpu.make_async_copy(
                    ref.at[k, :, pl.ds(window.start, cols)],
                    whole.at[pl.ds(pl.multiple_of(row, rows), rows), pl.ds(col, cols)],
                    sem.at[distance if by == "grp" else 0],
                ).start()


def weight_call(place, kernel, window, inputs, in_specs, outs, out_specs, steps, by, name, flops, mb=60):
    cols, groups = window.cols, place.groups
    pieces = window.arrays
    shape = (window.chips * 2 * window.rows, groups * cols)
    slots = {"grp": groups, "all": 1}[by]
    anywhere = pl.BlockSpec(memory_space=pl.ANY)

    def body(where, *refs):
        taken, refs = refs[: len(pieces)], refs[len(pieces) :]
        *refs, written, weight, sem, out_sem = refs
        step = pl.program_id(0)

        @pl.when(step == 0)
        def _():
            fetch(where, window, taken, weight, sem, by)

        def ready():
            if by == "all":

                @pl.when(step == 0)
                def _():
                    pltpu.make_async_copy(weight, weight, sem.at[0]).wait()
                    pltpu.make_async_copy(weight, written, out_sem.at[0]).start()

            else:
                at = pl.ds(pl.multiple_of((where[2] ^ step) * cols, LANES), cols)
                view = weight.at[:, at]
                pltpu.make_async_copy(view, view, sem.at[step]).wait()
                pltpu.make_async_copy(view, written.at[:, at], out_sem.at[step]).start()

        kernel(where, ready, weight, *refs)

        @pl.when(step == steps - 1)
        def _():
            for slot in range(slots):
                width = shape[1] // slots
                view = weight.at[:, pl.ds(slot * width, width)]
                pltpu.make_async_copy(view, view, out_sem.at[slot]).wait()

    total = sum(math.prod(x.shape) * x.dtype.itemsize for x in list(inputs) + list(outs))
    return pl.pallas_call(
        body,
        grid_spec=pltpu.PrefetchScalarGridSpec(
            num_scalar_prefetch=1,
            grid=(steps,),
            in_specs=[anywhere] * len(pieces) + in_specs,
            out_specs=out_specs + [anywhere],
            scratch_shapes=[
                pltpu.VMEM(shape, jnp.bfloat16),
                pltpu.SemaphoreType.DMA((slots,)),
                pltpu.SemaphoreType.DMA((slots,)),
            ],
        ),
        out_shape=outs + [shaped(shape, jnp.bfloat16)],
        compiler_params=params(mb),
        cost_estimate=cost(flops),
        name=name,
    )(place.scalars, *pieces, *inputs)


def plain_call(kernel, inputs, in_specs, outs, out_specs, steps, name, flops, mb=60):
    total = sum(math.prod(x.shape) * x.dtype.itemsize for x in list(inputs) + list(outs))
    return pl.pallas_call(
        kernel,
        grid=(steps,),
        in_specs=in_specs,
        out_specs=out_specs,
        out_shape=outs,
        compiler_params=params(mb),
        cost_estimate=cost(flops),
        name=name,
    )(*inputs)


TILE = 256


def row_tiles(width):
    return pl.BlockSpec((TILE, width), lambda i, *s: (i, 0))


def fixed(*shape):
    return pl.BlockSpec(shape, lambda i, *s: (0,) * len(shape))


def whole_once(shape):
    return pl.BlockSpec(shape, lambda i: (0,) * len(shape), pipeline_mode=pl.Buffered(1))


def shaped(shape, dtype):
    return jax.ShapeDtypeStruct(shape, dtype)


B_QUERY, B_VALUE, B_ATTN, GAIN_ONE, SHIFT_ONE, B_OUT, GAIN_TWO, SHIFT_TWO, B_IN = range(9)


def row(ref, n):
    return ref[n : n + 1, :]


class Vectors:
    def __init__(self, place, vectors):
        lines = [v.reshape(-1, LANES) for v in vectors]
        blank = jnp.zeros((-sum(x.shape[0] for x in lines) % 16, LANES), jnp.bfloat16)
        self.own = jnp.concatenate([*lines, blank])
        self.place = place
        self.flying = place.swap_core(self.own)

    def chips_near(self):
        self.own = jnp.stack([self.own, self.flying])
        self.flying = self.place.swap_chip(self.own, 0)

    def chips_far(self):
        self.own = jnp.stack([self.own, self.flying])
        self.flying = self.place.swap_chip(self.own, 1)

    def landed(self):
        self.slots = jnp.concatenate([self.own, self.flying])

    def unpack(self):
        place = self.place
        slots, sides, rows, lanes = self.slots.shape
        shards = place.shards

        def kernel(where, in_ref, rows_ref, inner_ref, qkv_ref):
            width = shards * lanes
            qkv_ref[...] = jnp.zeros_like(qkv_ref)
            for slot in range(slots):
                for side in range(sides):
                    core = where[0] ^ side
                    shard = (where[1] ^ turn(slot, where[0])) * 2 + core
                    part = in_ref[slot, side].astype(jnp.float32)
                    at = pl.multiple_of(shard * lanes, lanes)
                    rows_ref[:, pl.ds(at, lanes)] = part
                    qkv_ref[:, pl.ds(at, lanes)] = part[B_QUERY : B_QUERY + 1]
                    qkv_ref[:, pl.ds(2 * width + at, lanes)] = part[B_VALUE : B_VALUE + 1]
                    for n in range(4):
                        start = pl.multiple_of((shard * 4 + n) * lanes, lanes)
                        inner_ref[:, pl.ds(start, lanes)] = part[B_IN + n : B_IN + n + 1]

        in_vmem = pl.BlockSpec(memory_space=pltpu.VMEM)
        return pl.pallas_call(
            kernel,
            in_specs=[pl.BlockSpec(memory_space=pltpu.SMEM), in_vmem],
            out_specs=[in_vmem] * 3,
            out_shape=[
                shaped((rows, shards * lanes), jnp.float32),
                shaped((1, 4 * shards * lanes), jnp.float32),
                shaped((1, 3 * shards * lanes), jnp.float32),
            ],
            name="vectors",
        )(place.scalars, self.slots)


def pack_sums(late_a, late_b, first_sums, second_sums, inner_sums):
    width = first_sums.shape[1]
    half = late_a.shape[1]

    def kernel(a_ref, b_ref, one_ref, two_ref, inner_ref, out_ref):
        def place_of(n):
            return n // 3 * 8 + n % 3

        out_ref[...] = jnp.zeros_like(out_ref)
        for n in (B_QUERY, B_VALUE):
            at = place_of(n)
            out_ref[at : at + 1, 0:half] = a_ref[n : n + 1, :]
            out_ref[at : at + 1, half:width] = b_ref[n : n + 1, :]
        for n, source, line in (
            (GAIN_ONE, one_ref, 0),
            (SHIFT_ONE, one_ref, 1),
            (B_ATTN, one_ref, 2),
            (GAIN_TWO, two_ref, 0),
            (SHIFT_TWO, two_ref, 1),
            (B_OUT, two_ref, 2),
        ):
            at = place_of(n)
            out_ref[at : at + 1, :] = source[line : line + 1, :]
        for n in range(4):
            at = place_of(B_IN + n)
            for shard in range(width // LANES):
                start = (4 * shard + n) * LANES
                out_ref[at : at + 1, shard * LANES : (shard + 1) * LANES] = inner_ref[
                    :, start : start + LANES
                ]

    in_vmem = pl.BlockSpec(memory_space=pltpu.VMEM)
    return pl.pallas_call(
        kernel,
        in_specs=[in_vmem] * 5,
        out_specs=in_vmem,
        out_shape=shaped((32, width), jnp.float32),
        name="pack_sums",
    )(late_a, late_b, first_sums, second_sums, inner_sums)


def project_qkv(place, rows, window, bias, scale):
    length, width = rows.shape
    cols = window.cols

    def kernel(where, ready, weight, x_ref, bias_ref, scale_ref, out_ref):
        ready()
        at = pl.ds(pl.multiple_of((where[2] ^ pl.program_id(0)) * cols, LANES), cols)
        for tile in range(length // TILE):
            here = pl.ds(tile * TILE, TILE)
            mixed = mxu(x_ref[here, :], weight[:, at], NN) + bias_ref[:, at]
            mixed = mixed.astype(jnp.bfloat16).astype(jnp.float32) * scale_ref[:, at]
            out_ref[here, :] = mixed.astype(jnp.bfloat16)

    total = cols * place.groups
    return weight_call(
        place,
        kernel,
        window,
        (rows, bias, scale),
        [fixed(length, width), fixed(1, total), fixed(1, total)],
        [shaped((length, total), jnp.bfloat16)],
        [pl.BlockSpec((length, cols), lambda i, s: (0, i ^ s[2]))],
        place.groups,
        "grp",
        "qkv",
        2 * length * width * total,
    )


def norm_parts(rows):
    centered = rows - jnp.mean(rows, -1, keepdims=True)
    scale = lax.rsqrt(jnp.mean(centered * centered, -1, keepdims=True) + epsilon)
    return centered * scale, scale


def norm_back(grad, normed, scale):
    return scale * (
        grad
        - jnp.mean(grad, -1, keepdims=True)
        - normed * jnp.mean(grad * normed, -1, keepdims=True)
    )


def add_rows(sum_ref, *terms):
    @pl.when(pl.program_id(0) == 0)
    def _():
        sum_ref[...] = jnp.zeros_like(sum_ref)

    for n, term in enumerate(terms):
        sum_ref[n : n + 1, :] += jnp.sum(term, 0, keepdims=True)


def project_out(place, contexts, window, rows, vectors):
    length, width = rows.shape

    def kernel(where, ready, weight, c_ref, x_ref, v_ref, n_ref, r_ref, low_ref):
        ready()
        first_sum = mxu(c_ref[...], weight[...], NN) + row(v_ref, B_ATTN)
        first_sum = first_sum + x_ref[...].astype(jnp.float32)
        normed, scale = norm_parts(first_sum)
        n_ref[...] = normed
        r_ref[...] = jnp.broadcast_to(scale, r_ref.shape)
        low_ref[...] = (normed * row(v_ref, GAIN_ONE) + row(v_ref, SHIFT_ONE)).astype(jnp.bfloat16)

    return weight_call(
        place,
        kernel,
        window,
        (contexts, rows, vectors),
        [row_tiles(width), row_tiles(width), fixed(*vectors.shape)],
        [
            shaped((length, width), jnp.float32),
            shaped((length, LANES), jnp.float32),
            shaped((length, width), jnp.bfloat16),
        ],
        [row_tiles(width), row_tiles(LANES), row_tiles(width)],
        length // TILE,
        "all",
        "attn_out",
        2 * length * width * width,
    )


def feed_in(place, normed_low, window, bias):
    length, width = normed_low.shape
    cols = window.cols

    def kernel(where, ready, weight, x_ref, bias_ref, hid_ref, slope_ref):
        ready()
        at = pl.ds(pl.multiple_of((where[2] ^ pl.program_id(0)) * cols, LANES), cols)
        for tile in range(length // TILE):
            here = pl.ds(tile * TILE, TILE)
            pre = mxu(x_ref[here, :], weight[:, at], NN) + bias_ref[:, at]
            share = 0.5 + 0.5 * lax.erf(pre * (1.0 / math.sqrt(2.0)))
            bell = jnp.exp(-0.5 * pre * pre) * (1.0 / math.sqrt(2.0 * math.pi))
            hid_ref[here, :] = (pre * share).astype(jnp.bfloat16)
            slope_ref[here, :] = (share + pre * bell).astype(jnp.bfloat16)

    total = cols * place.groups
    block = pl.BlockSpec((length, cols), lambda i, s: (0, i ^ s[2]))
    return weight_call(
        place,
        kernel,
        window,
        (normed_low, bias),
        [fixed(length, width), fixed(1, total)],
        [shaped((length, total), jnp.bfloat16)] * 2,
        [block, block],
        place.groups,
        "grp",
        "feed_in",
        2 * length * width * total,
    )


def feed_out(place, hidden, window, normed, cot, keep, vectors):
    length, inner = hidden.shape
    width = normed.shape[1]

    def kernel(where, ready, weight, h_ref, n_ref, cot_ref, keep_ref, v_ref, *outs):
        out_ref, grad_ref, low_ref, sum_ref = outs
        ready()
        fed = mxu(h_ref[...], weight[...], NN)
        normed_one = n_ref[...] * row(v_ref, GAIN_ONE) + row(v_ref, SHIFT_ONE)
        second_sum = normed_one + (fed + row(v_ref, B_OUT))
        second, scale = norm_parts(second_sum)
        out_ref[...] = (second * row(v_ref, GAIN_TWO) + row(v_ref, SHIFT_TWO)).astype(jnp.bfloat16)
        masked = cot_ref[...].astype(jnp.float32) * keep_ref[...]
        grad = norm_back(masked * row(v_ref, GAIN_TWO), second, scale)
        grad_ref[...] = grad
        low_ref[...] = grad.astype(jnp.bfloat16)
        add_rows(sum_ref, masked * second, masked, grad)

    return weight_call(
        place,
        kernel,
        window,
        (hidden, normed, cot, keep, vectors),
        [row_tiles(inner), row_tiles(width), row_tiles(width), row_tiles(1), fixed(*vectors.shape)],
        [
            shaped((length, width), jnp.bfloat16),
            shaped((length, width), jnp.float32),
            shaped((length, width), jnp.bfloat16),
            shaped((8, width), jnp.float32),
        ],
        [row_tiles(width), row_tiles(width), row_tiles(width), fixed(8, width)],
        length // TILE,
        "all",
        "feed_out",
        2 * length * width * inner,
    )


def feed_out_back(out_low, weight, slope):
    length, width = out_low.shape
    inner = slope.shape[1]
    cols = min(1024, inner)

    def kernel(g_ref, w_ref, slope_ref, pre_ref, sum_ref):
        total = jnp.zeros((1, cols), jnp.float32)
        for tile in range(length // TILE):
            here = pl.ds(tile * TILE, TILE)
            grad = mxu(g_ref[here, :], w_ref[...], NT) * slope_ref[here, :].astype(jnp.float32)
            pre_ref[here, :] = grad.astype(jnp.bfloat16)
            total = total + jnp.sum(grad, 0, keepdims=True)
        sum_ref[...] = total

    block = pl.BlockSpec((length, cols), lambda i: (0, i))
    return plain_call(
        kernel,
        (out_low, weight, slope),
        [fixed(length, width), pl.BlockSpec((cols, width), lambda i: (i, 0)), block],
        [shaped((length, inner), jnp.bfloat16), shaped((1, inner), jnp.float32)],
        [block, pl.BlockSpec((1, cols), lambda i: (0, i))],
        inner // cols,
        "feed_out_back",
        2 * length * width * inner,
    )


def feed_in_back(pre_low, weight, second_grad, normed, scale, vectors, attn_weight):
    length, inner = pre_low.shape
    width = normed.shape[1]

    def kernel(p_ref, w_ref, g_ref, n_ref, r_ref, v_ref, a_ref, first_ref, low_ref, ctx_ref, sum_ref):
        grad = g_ref[...] + mxu(p_ref[...], w_ref[...], NT)
        first = norm_back(grad * row(v_ref, GAIN_ONE), n_ref[...], r_ref[:, :1])
        low = first.astype(jnp.bfloat16)
        first_ref[...] = first
        low_ref[...] = low
        ctx_ref[...] = mxu(low, a_ref[...], NT).astype(jnp.bfloat16)
        add_rows(sum_ref, grad * n_ref[...], grad, first)

    return plain_call(
        kernel,
        (pre_low, weight, second_grad, normed, scale, vectors, attn_weight),
        [
            row_tiles(inner),
            whole_once(weight.shape),
            row_tiles(width),
            row_tiles(width),
            row_tiles(LANES),
            fixed(*vectors.shape),
            whole_once(attn_weight.shape),
        ],
        [
            shaped((length, width), jnp.float32),
            shaped((length, width), jnp.bfloat16),
            shaped((length, width), jnp.bfloat16),
            shaped((8, width), jnp.float32),
        ],
        [row_tiles(width), row_tiles(width), row_tiles(width), fixed(8, width)],
        length // TILE,
        "feed_in_back",
        2 * length * width * (inner + width),
    )


def project_qkv_back(grads, weight, first_grad, start, tiles, before=None):
    length, width = first_grad.shape
    part = width // len(grads)

    def kernel(w_ref, *refs):
        grad_refs, first_ref, out_ref = refs[: len(grads)], refs[len(grads)], refs[-1]
        total = first_ref[...]
        for n in range(3):
            for m, grad_ref in enumerate(grad_refs):
                at = n * width + m * part
                total = total + mxu(grad_ref[n], w_ref[:, at : at + part], NT)
        out_ref[...] = total

    tile = pl.BlockSpec((TILE, width), lambda i: (start + i, 0))
    more = () if before is None else (before,)
    return pl.pallas_call(
        kernel,
        grid=(tiles,),
        in_specs=[whole_once(weight.shape)]
        + [pl.BlockSpec((3, TILE, part), lambda i: (0, start + i, 0))] * len(grads)
        + [tile]
        + [pl.BlockSpec(memory_space=pl.ANY)] * len(more),
        out_specs=tile,
        out_shape=shaped((length, width), jnp.float32),
        input_output_aliases={} if before is None else {len(grads) + 2: 0},
        compiler_params=params(60),
        cost_estimate=cost(6 * tiles * TILE * width * width),
        name="qkv_back",
    )(weight, *grads, first_grad, *more)


ORDER = (1, 3, 0, 2)


def ordered_slot(j):
    return jnp.where(j < 2, 2 * j + 1, 2 * j - 4)


def weight_grad_kernel(where, left_ref, right_ref, own, sent, kept, *, rows, groups, split):
    core = where[0]
    chips = left_ref.shape[1] // (2 * rows)

    @pl.when(pl.program_id(1) == 0)
    def _():
        for side in range(2):
            chosen = []
            for k in range(chips):
                even = left_ref[:, 2 * k * rows : (2 * k + 1) * rows]
                odd = left_ref[:, (2 * k + 1) * rows : (2 * k + 2) * rows]
                chosen.append(jnp.where(core == side, even, odd))
            left = chosen[0] if chips == 1 else jnp.concatenate(chosen, 1)
            kept[side] = left.T

    if split:
        size = min(512, right_ref.shape[1])
        for ref, side in ((sent, 1), (own, 0)):
            for n in range(right_ref.shape[1] // size):
                at = slice(n * size, (n + 1) * size)
                part = mxu(kept[side], right_ref[:, at], NN).astype(jnp.bfloat16)
                ref[0, :, :, at] = part.reshape(chips, rows, size)
    else:
        cols = right_ref.shape[1] // groups
        for ref, side in ((sent, 1), (own, 0)):
            for pos, slot in enumerate(ORDER):
                start = pl.multiple_of((where[2] ^ turn(slot, core ^ side)) * cols, LANES)
                part = mxu(kept[side], right_ref[:, pl.ds(start, cols)], NN)
                ref[pos] = part.astype(jnp.bfloat16).reshape(chips, rows, cols)


def attention_grads_kernel(where, *refs, rows, groups, extra):
    left_ref, right_ref, *refs = refs
    *more, own, sent, kept = refs
    core, grp = where[0], where[2]
    chips = left_ref.shape[1] // (2 * rows)
    step = pl.program_id(0)

    def keep_rows(ref):
        for side in range(2):
            chosen = []
            for k in range(chips):
                even = ref[:, 2 * k * rows : (2 * k + 1) * rows]
                odd = ref[:, (2 * k + 1) * rows : (2 * k + 2) * rows]
                chosen.append(jnp.where(core == side, even, odd))
            kept[side] = jnp.concatenate(chosen, 1).T

    def scatter(right, at, cols):
        for ref, side in ((sent, 1), (own, 0)):
            part = mxu(kept[side], right, NN).astype(jnp.bfloat16)
            for g in range(groups):
                pos = position(grp ^ g, core ^ side)
                block = part[:, g * cols : (g + 1) * cols].reshape(chips, rows, cols)
                ref[pos, :, 0:rows, pl.ds(at, cols)] = block

    skip = 0
    if not extra:
        other_left, other_right = more
        skip = other_right.shape[1] // groups

    @pl.when(step == 0)
    def _():
        if not extra:
            keep_rows(other_left)
            scatter(other_right[...], 0, skip)
        keep_rows(left_ref)

    cols = right_ref.shape[2] // groups
    scatter(right_ref[0], pl.multiple_of(skip + step * cols, LANES), cols)

    if extra:
        (sums_ref,) = more

        @pl.when(step == 2)
        def _():
            blank = jnp.zeros((extra, own.shape[3]), jnp.bfloat16)
            for ref, side in ((sent, 1), (own, 0)):
                for g in range(groups):
                    pos = position(grp ^ g, core ^ side)
                    for k in range(chips):
                        start = pl.multiple_of((2 * k + (core ^ side)) * LANES, LANES)
                        ref[pos, k, rows : rows + extra, :] = blank
                        lines = sums_ref[8 * g : 8 * g + 8, pl.ds(start, LANES)]
                        for n in range(3):
                            ref[pos, k, rows : rows + 1, n * LANES : (n + 1) * LANES] = lines[
                                n : n + 1
                            ].astype(jnp.bfloat16)


def position(distance, core):
    slot = turn(distance, core)
    return jnp.where(slot == 0, 2, jnp.where(slot == 1, 0, jnp.where(slot == 3, 1, 3)))


def attention_grads(place, left, right, more, name):
    tokens, height = left.shape
    groups, chips = place.groups, place.chips
    rows = height // place.shards
    extra = 16 if len(more) == 1 else 0
    size = right.shape[2]
    cols = 3 * size // groups + (0 if extra else more[1].shape[1] // groups)
    shape = (groups, chips, rows + extra, cols)
    once = [
        pl.BlockSpec(x.shape, lambda i, s: (0, 0), pipeline_mode=pl.Buffered(1)) for x in more
    ]
    return pl.pallas_call(
        functools.partial(attention_grads_kernel, rows=rows, groups=groups, extra=extra),
        grid_spec=pltpu.PrefetchScalarGridSpec(
            num_scalar_prefetch=1,
            grid=(3,),
            in_specs=[
                pl.BlockSpec(left.shape, lambda i, s: (0, 0), pipeline_mode=pl.Buffered(1)),
                pl.BlockSpec((1, tokens, size), lambda i, s: (i, 0, 0)),
            ]
            + once,
            out_specs=[pl.BlockSpec(shape, lambda i, s: (0, 0, 0, 0))] * 2,
            scratch_shapes=[pltpu.VMEM((2, height // 2, tokens), jnp.bfloat16)],
        ),
        out_shape=[shaped(shape, jnp.bfloat16)] * 2,
        compiler_params=params(60),
        cost_estimate=cost(2 * tokens * height * cols * groups),
        name="wgrad_" + name,
    )(place.scalars, left, right, *more)


def weight_grad(place, left, right, split, name):
    tokens, height = left.shape
    groups, chips = place.groups, place.chips
    rows = height // place.shards
    step_chips = chips if split else max(1, 1024 // (2 * rows))
    cols = right.shape[1] // groups
    if split:
        grid = (1, groups)
        block = lambda i, j, s: (0, s[2] ^ turn(ordered_slot(j), s[0]))
        right_spec = pl.BlockSpec((tokens, cols), block)
        one = (1, chips, rows, cols)
        other = lambda j: jnp.where(j == 0, 3, jnp.where(j == 3, 0, j))
        out_specs = [
            pl.BlockSpec(one, lambda i, j, s: (j, 0, 0, 0)),
            pl.BlockSpec(one, lambda i, j, s: (other(j), 0, 0, 0)),
        ]
    else:
        grid = (chips // step_chips, 1)
        right_spec = pl.BlockSpec(right.shape, lambda i, j, s: (0, 0))
        out_specs = [
            pl.BlockSpec((groups, step_chips, rows, cols), lambda i, j, s: (0, i, 0, 0))
        ] * 2
    return pl.pallas_call(
        functools.partial(weight_grad_kernel, rows=rows, groups=groups, split=split),
        grid_spec=pltpu.PrefetchScalarGridSpec(
            num_scalar_prefetch=1,
            grid=grid,
            in_specs=[
                pl.BlockSpec((tokens, step_chips * 2 * rows), lambda i, j, s: (0, i)),
                right_spec,
            ],
            out_specs=out_specs,
            scratch_shapes=[pltpu.VMEM((2, step_chips * rows, tokens), jnp.bfloat16)],
        ),
        out_shape=[shaped((groups, chips, rows, cols), jnp.bfloat16)] * 2,
        compiler_params=params(60),
        cost_estimate=cost(2 * tokens * height * cols * groups),
        name="wgrad_" + name,
    )(place.scalars, left, right)


def add(*terms):
    total = terms[0].astype(jnp.float32)
    for term in terms[1:]:
        total = total + term.astype(jnp.float32)
    return total.astype(jnp.bfloat16)


class Reduction:
    def __init__(self, place, made):
        self.place = place
        self.made, sent = made
        self.flying = place.swap_core(sent)

    def near(self):
        self.core = self.flying
        leave = add(self.made[:2], self.core[:2])
        self.flying = self.place.swap_grp(leave, 0)
        return leave

    def middle(self):
        self.first = self.flying
        second = add(self.made[3], self.core[3], self.first[1])
        self.flying = self.place.swap_grp(second, 1)
        return second

    def column(self):
        mine = add(self.made[2], self.core[2], self.first[0], self.flying)
        return mine, lambda chip: lax.dynamic_index_in_dim(mine, chip, 0, False)

    def along(self):
        place = self.place
        mine, at = self.column()
        self.mine = [at(place.slot_chip(slot)) for slot in range(4)]
        both = jnp.stack([self.mine[1], self.mine[3]])
        self.flying = place.swap_chip(both, 0)
        return both

    def along_far(self):
        self.first = self.flying
        second = add(self.mine[2], self.first[1])
        self.flying = self.place.swap_chip(second, 1)
        return second

    def share(self):
        return add(self.mine[0], self.first[0], self.flying)

    def share_direct(self):
        place = self.place
        mine, at = self.column()
        terms = [
            place.permute(at(place.chip ^ k), (2 * k, 2 * k)) for k in range(place.chips - 1, 0, -1)
        ]
        return add(at(place.chip), *terms)


class Replication:
    def __init__(self, place, share, direct=False):
        self.place = place
        self.blocks = [share] + [None] * 3
        if direct:
            size = place.shards
            for mask in (3, 1, 2):
                self.blocks[mask] = place.permute(share, (mask * size, mask * size))
        else:
            self.flying = place.swap_grp(share, 0)

    def far(self):
        pair = jnp.stack([self.blocks[0], self.flying])
        self.blocks[1] = self.flying
        self.flying = self.place.swap_grp(pair, 1)
        return pair

    def landed(self):
        if self.blocks[2] is None:
            self.blocks[2:] = [self.flying[0], self.flying[1]]
        return self.blocks


def order_feed_forward(place, blocks, rows_in):
    groups = place.groups
    height, cols = blocks[0].shape
    rows_out = height - groups * rows_in

    def kernel(where, *refs):
        *blocks, out_ref, in_ref = refs
        for slot, ref in enumerate(blocks):
            g = where[2] ^ turn(slot, where[0])
            at = pl.multiple_of(g * cols, LANES)
            out_ref[:, pl.ds(at, cols)] = ref[0:rows_out, :].astype(jnp.float32)
            for n in range(groups):
                at = pl.multiple_of((g * groups + n) * cols, LANES)
                part = ref[rows_out + n * rows_in : rows_out + (n + 1) * rows_in, :]
                in_ref[:, pl.ds(at, cols)] = part.astype(jnp.float32)

    in_vmem = pl.BlockSpec(memory_space=pltpu.VMEM)
    return pl.pallas_call(
        kernel,
        in_specs=[pl.BlockSpec(memory_space=pltpu.SMEM)] + [in_vmem] * groups,
        out_specs=[in_vmem] * 2,
        out_shape=[
            shaped((rows_out, groups * cols), jnp.float32),
            shaped((rows_in, groups * groups * cols), jnp.float32),
        ],
        compiler_params=params(40),
        cost_estimate=cost(height * cols * 1024),
        name="order_feed_forward",
    )(place.scalars, *blocks)


def order_attention(place, blocks_a, blocks_b, rows):
    groups = place.groups
    size = blocks_b[0].shape[1] // 3
    skip = blocks_a[0].shape[1] - 3 * size
    width = groups * skip

    def kernel(where, *refs):
        *blocks, attn_ref, qkv_ref, small_ref = refs
        for n in range(groups):
            ref = blocks[n]
            g = where[2] ^ turn(n, where[0])
            attn_ref[:, pl.ds(pl.multiple_of(g * skip, LANES), skip)] = ref[:, 0:skip].astype(
                jnp.float32
            )
            for part in range(3):
                at = pl.multiple_of(part * width + g * size, LANES)
                block = ref[:, skip + part * size : skip + (part + 1) * size]
                qkv_ref[:, pl.ds(at, size)] = block.astype(jnp.float32)
        for n in range(groups):
            ref = blocks[groups + n]
            g = where[2] ^ n
            lines = []
            for part in range(3):
                at = pl.multiple_of(part * width + width // 2 + g * size, LANES)
                here = slice(part * size, (part + 1) * size)
                qkv_ref[:, pl.ds(at, size)] = ref[0:rows, here].astype(jnp.float32)
                lines.append(ref[rows : rows + 16, here].astype(jnp.float32)[0:1])
            lines.append(jnp.zeros((5, size), jnp.float32))
            small_ref[pl.ds(pl.multiple_of(g * 8, 8), 8), :] = jnp.concatenate(lines)

    in_vmem = pl.BlockSpec(memory_space=pltpu.VMEM)
    return pl.pallas_call(
        kernel,
        in_specs=[pl.BlockSpec(memory_space=pltpu.SMEM)] + [in_vmem] * (2 * groups),
        out_specs=[in_vmem] * 3,
        out_shape=[
            shaped((rows, width), jnp.float32),
            shaped((rows, 3 * width), jnp.float32),
            shaped((8 * groups, size), jnp.float32),
        ],
        compiler_params=params(40),
        name="order_attention",
    )(place.scalars, *blocks_a, *blocks_b)


def on_device_permutes(
    tokens,
    segment_ids,
    keep_flag,
    cotangent,
    w_qkv,
    b_query,
    b_value,
    w_attn_out,
    b_attn_out,
    norm1_gain,
    norm1_bias,
    w_in,
    b_in,
    w_out,
    b_out,
    norm2_gain,
    norm2_bias,
    *,
    groups,
    shards,
):
    place = Place(groups, shards)
    _, length, width = tokens.shape
    rows = tokens[0]
    seg_row = segment_ids.reshape(1, length)
    seg_col = segment_ids.reshape(length, 1)
    keep = keep_flag.reshape(length, 1).astype(jnp.float32)
    pairs = width // LANES

    c1 = Gather(place, w_qkv)
    c2 = Gather(place, jnp.concatenate([w_in, w_attn_out], 1))
    c3 = Gather(place, w_out)
    c1.chips_near()
    small = Vectors(
        place,
        (b_query, b_value, b_attn_out, norm1_gain, norm1_bias, b_out, norm2_gain, norm2_bias, b_in),
    )
    meet(rows, c1, small)
    pair = c1.chips_far()
    small.chips_near()
    meet(pair, c1, small)
    joined = c1.join()
    c1.near()
    small.chips_far()
    c2.chips_near(joined)
    meet(joined, c2, small)
    small.landed()
    pair = c2.chips_far()
    vectors, bias_in, qkv_bias = small.unpack()
    c1.flying = lax.optimization_barrier(c1.flying)
    c1.far(pair, vectors)
    c1.cross(0, 1, 2)
    joined = c2.join()
    meet(joined, c1)
    c1.landed()
    c2.near(c1.held[3])
    c1.cross(3)
    blank = jnp.ones((1, width), jnp.float32)
    qkv_scale = jnp.concatenate([blank / math.sqrt(HD), blank, blank], 1)

    mixed, full_qkv = project_qkv(place, rows, Window(c1, 0, w_qkv.shape[1]), qkv_bias, qkv_scale)
    c3.chips_near(mixed)
    c2.cross(0, wait=(mixed,))
    first, second = pairs * 3 // 8, pairs * 3 // 4
    forward = attention_forward(mixed, seg_col, seg_row, 0, first)
    meet(forward[1], c2, c3)
    c2.far()
    pair = c3.chips_far()
    c2.cross(1, 2)
    forward = attention_forward(after(mixed, pair), seg_col, seg_row, first, second - first, forward)
    meet(forward[1], c2, c3)
    c2.landed()
    c2.cross(3)
    joined = c3.join()
    c3.near()
    contexts, lse = attention_forward(
        after(mixed, joined), seg_col, seg_row, second, pairs - second, forward
    )
    normed, scale_one, normed_low, full_attn = project_out(
        place, contexts, Window(c2, w_in.shape[1], w_attn_out.shape[1]), rows, vectors
    )
    meet(normed_low, c3)
    c3.far()
    c3.cross(0, 1, 2)
    hidden, slope, full_in = feed_in(
        place, after(normed_low, c3.held[1]), Window(c2, 0, w_in.shape[1]), bias_in
    )
    meet(hidden, c3)
    c3.landed()
    c3.cross(3)
    layer_out, second_grad, out_low, second_sums, full_out = feed_out(
        place, hidden, Window(c3, 0, w_out.shape[1]), normed, cotangent[0], keep, vectors
    )

    r_out = Reduction(place, weight_grad(place, hidden, out_low, False, "out"))
    pre_low, bias_in_grad = feed_out_back(after(out_low, r_out.made), full_out, slope)
    meet(pre_low, r_out)
    step = r_out.near()
    r_in = Reduction(place, weight_grad(place, after(normed_low, step), pre_low, True, "in"))
    first_grad, attn_low, context_grad, first_sums = feed_in_back(
        after(pre_low, r_in.made), full_in, second_grad, normed, scale_one, vectors, full_attn
    )
    meet(attn_low, r_out, r_in)
    steps = (r_out.middle(), r_in.near())
    half, quarter = pairs // 2, pairs // 4

    def back(wait, start, count, at, before=None):
        return attention_backward(
            mixed,
            contexts,
            after(context_grad, *wait),
            seg_col,
            seg_row,
            lse,
            start,
            count,
            at,
            half,
            before,
        )

    low_a, late_a = back(steps, 0, half, 0)
    meet(late_a, r_out, r_in)
    steps = (r_out.along(), r_in.middle())
    r_a = Reduction(
        place, attention_grads(place, after(rows, *steps), low_a, (contexts, attn_low), "a")
    )
    meet(r_a.made, r_out, r_in)
    steps = (r_out.along_far(), r_in.along())
    part = back((r_a.made, *steps), half, quarter, 0)
    meet(part[1], r_out, r_in, r_a)
    steps = (r_out.share(), r_in.along_far(), r_a.near())
    share_out = steps[0]
    low_b, late_b = back(steps, half + quarter, quarter, quarter, part)
    meet(late_b, r_in, r_a)
    share_in = r_in.share()
    inner = share_in.shape[1] // groups
    joined = jnp.concatenate(
        [share_out] + [share_in[:, n * inner : (n + 1) * inner] for n in range(groups)]
    )
    all_ffn = Replication(place, joined)
    sums = pack_sums(late_a, late_b, first_sums, second_sums, bias_in_grad)
    steps = (joined, r_a.middle())
    r_b = Reduction(place, attention_grads(place, after(rows, *steps), low_b, (sums,), "b"))
    meet(r_b.made, r_a, all_ffn)
    steps = (r_a.along(), all_ffn.far())
    grads = (low_a, after(low_b, r_b.made, *steps))
    tiles = length // TILE // 2
    input_grad = project_qkv_back(grads, full_qkv, first_grad, 0, tiles)
    meet(input_grad, r_b, r_a, all_ffn)
    steps = (r_b.near(), r_a.along_far())
    input_grad = project_qkv_back(
        grads, full_qkv, after(first_grad, *steps), tiles, tiles, input_grad
    )
    meet(input_grad, r_b, r_a)
    middle = r_b.middle()
    r_a.flying = after(r_a.flying, middle)
    all_a = Replication(place, r_a.share())
    blocks = all_ffn.landed()
    w_out_grad, w_in_grad = order_feed_forward(
        place, [after(blocks[0], all_a.blocks[0]), *blocks[1:]], share_in.shape[0]
    )
    meet(w_out_grad, r_b, all_a)
    share_b = r_b.share_direct()
    all_a.far()
    all_b = Replication(place, share_b, direct=True)
    w_attn_grad, w_qkv_grad, small = order_attention(
        place, all_a.landed(), all_b.landed(), w_attn_out.shape[0]
    )
    small = [small[8 * (n // 3) + n % 3] for n in range(12)]
    return (
        layer_out[None],
        input_grad[None],
        w_qkv_grad,
        small[B_QUERY],
        small[B_VALUE],
        w_attn_grad,
        small[B_ATTN],
        small[GAIN_ONE],
        small[SHIFT_ONE],
        w_in_grad,
        jnp.concatenate(small[B_IN:]),
        w_out_grad,
        small[B_OUT],
        small[GAIN_TWO],
        small[SHIFT_TWO],
    )


def solution(mesh):
    groups, shards = mesh.shape["grp"], mesh.shape["shard"]
    if groups == 4 and shards == 8:
        body = functools.partial(on_device_permutes, groups=groups, shards=shards)
    else:
        body = on_device
    return jax.shard_map(
        body,
        mesh=mesh,
        in_specs=(
            P(("grp", "shard"), None, None),
            P(("grp", "shard"), None),
            P(("grp", "shard"), None),
            P(("grp", "shard"), None, None),
            P("shard", "grp"),
            P("shard"),
            P("shard"),
            P("shard", "grp"),
            P("shard"),
            P("shard"),
            P("shard"),
            P("shard", "grp"),
            P("shard"),
            P("shard", "grp"),
            P("shard"),
            P("shard"),
            P("shard"),
        ),
        out_specs=(
            P(("grp", "shard"), None, None),
            P(("grp", "shard"), None, None),
            P("shard", None),
            P("shard"),
            P("shard"),
            P("shard", None),
            P("shard"),
            P("shard"),
            P("shard"),
            P("shard", None),
            P("shard"),
            P("shard", None),
            P("shard"),
            P("shard"),
            P("shard"),
        ),
        check_vma=False,
    )
```

```python
import functools
import math

import jax
import jax.numpy as jnp
from jax import lax
from jax.experimental import pallas as pl
from jax.experimental.pallas import tpu as pltpu
from jax.sharding import PartitionSpec as P

H = 16
HD = 64


masked_score = -1e30
epsilon = 1e-05


def norm_layer(rows, gain_row, shift_row):
    row_mean = jnp.mean(rows, -1, keepdims=True)
    centered = rows - row_mean
    row_var = jnp.mean(centered * centered, -1, keepdims=True)
    return centered * lax.rsqrt(row_var + epsilon) * gain_row + shift_row


def gelu_exact(values):
    return 0.5 * values * (1.0 + lax.erf(values * (1.0 / math.sqrt(2.0))))


def contract_rows(left, right):
    return lax.dot_general(
        left, right, (((0,), (0,)), ((), ())), preferred_element_type=jnp.float32
    )


def contract_cols(left, right):
    return lax.dot_general(
        left, right, (((1,), (1,)), ((), ())), preferred_element_type=jnp.float32
    )


def attend_forward(queries, key_rows, value_rows, segment_row, block_rows):
    length, model_width = queries.shape
    scaling = 1.0 / math.sqrt(HD)
    key_heads = key_rows.reshape(length, H, HD)
    value_heads = value_rows.reshape(length, H, HD)
    query_blocks = queries.reshape(length // block_rows, block_rows, H, HD)
    segment_blocks = segment_row.reshape(length // block_rows, block_rows)

    def one_block(pieces):
        query_part, segment_part = pieces
        scores = (
            jnp.einsum("qhd,khd->hqk", query_part, key_heads, preferred_element_type=jnp.float32)
            * scaling
        )
        allowed = segment_part[:, None] == segment_row[None, :]
        scores = jnp.where(allowed[None], scores, masked_score)
        row_max = jnp.max(scores, -1, keepdims=True)
        powers = jnp.exp(scores - row_max)
        totals = jnp.sum(powers, -1, keepdims=True)
        attn_probs = (powers / totals).astype(jnp.bfloat16)
        context = jnp.einsum(
            "hqk,khd->qhd", attn_probs, value_heads, preferred_element_type=jnp.float32
        )
        return (
            context.reshape(block_rows, model_width).astype(jnp.bfloat16),
            (row_max + jnp.log(totals))[:, :, 0],
        )

    contexts, log_sums = lax.map(one_block, (query_blocks, segment_blocks))
    return (contexts.reshape(length, model_width), log_sums)


def attend_backward(queries, key_rows, value_rows, segment_row, log_sums, context_grad, block_rows):
    length, model_width = queries.shape
    scaling = 1.0 / math.sqrt(HD)
    key_heads = key_rows.reshape(length, H, HD)
    value_heads = value_rows.reshape(length, H, HD)
    query_blocks = queries.reshape(length // block_rows, block_rows, H, HD)
    segment_blocks = segment_row.reshape(length // block_rows, block_rows)
    grad_blocks = context_grad.reshape(length // block_rows, block_rows, H, HD)

    def one_block(running, pieces):
        key_acc, value_acc = running
        query_part, segment_part, lse_part, grad_part = pieces
        scores = (
            jnp.einsum("qhd,khd->hqk", query_part, key_heads, preferred_element_type=jnp.float32)
            * scaling
        )
        allowed = segment_part[:, None] == segment_row[None, :]
        scores = jnp.where(allowed[None], scores, masked_score)
        probs = jnp.exp(scores - lse_part[:, :, None])
        prob_low = probs.astype(jnp.bfloat16)
        prob_grad = jnp.einsum(
            "qhd,khd->hqk", grad_part, value_heads, preferred_element_type=jnp.float32
        )
        row_dot = jnp.sum(prob_grad * probs, -1, keepdims=True)
        score_grad = (probs * (prob_grad - row_dot)).astype(jnp.bfloat16)
        query_grad = (
            jnp.einsum("hqk,khd->qhd", score_grad, key_heads, preferred_element_type=jnp.float32)
            * scaling
        )
        key_acc = (
            key_acc
            + jnp.einsum("hqk,qhd->khd", score_grad, query_part, preferred_element_type=jnp.float32)
            * scaling
        )
        value_acc = value_acc + jnp.einsum(
            "hqk,qhd->khd", prob_low, grad_part, preferred_element_type=jnp.float32
        )
        return ((key_acc, value_acc), query_grad.reshape(block_rows, model_width))

    empty_acc = jnp.zeros((length, H, HD), jnp.float32)
    (key_grad, value_grad), query_grads = lax.scan(
        one_block, (empty_acc, empty_acc), (query_blocks, segment_blocks, log_sums, grad_blocks)
    )
    return (
        query_grads.reshape(length, model_width),
        key_grad.reshape(length, model_width),
        value_grad.reshape(length, model_width),
    )


def on_device(
    tokens,
    segment_ids,
    keep_flag,
    cotangent,
    w_qkv,
    b_query,
    b_value,
    w_attn_out,
    b_attn_out,
    norm1_gain,
    norm1_bias,
    w_in,
    b_in,
    w_out,
    b_out,
    norm2_gain,
    norm2_bias,
):
    seq_count, length, model_width = tokens.shape
    block_rows = min(512, length)
    within = (
        lax.all_gather(w_qkv, "shard", axis=0, tiled=True),
        lax.all_gather(w_attn_out, "shard", axis=0, tiled=True),
        lax.all_gather(w_in, "shard", axis=0, tiled=True),
        lax.all_gather(w_out, "shard", axis=0, tiled=True),
        lax.all_gather(b_query, "shard", axis=0, tiled=True),
        lax.all_gather(b_value, "shard", axis=0, tiled=True),
        lax.all_gather(b_attn_out, "shard", axis=0, tiled=True),
        lax.all_gather(norm1_gain, "shard", axis=0, tiled=True),
        lax.all_gather(norm1_bias, "shard", axis=0, tiled=True),
        lax.all_gather(b_in, "shard", axis=0, tiled=True),
        lax.all_gather(b_out, "shard", axis=0, tiled=True),
        lax.all_gather(norm2_gain, "shard", axis=0, tiled=True),
        lax.all_gather(norm2_bias, "shard", axis=0, tiled=True),
    )
    full_qkv, full_attn, full_in, full_out = (
        lax.all_gather(within[0], "grp", axis=1, tiled=True),
        lax.all_gather(within[1], "grp", axis=1, tiled=True),
        lax.all_gather(within[2], "grp", axis=1, tiled=True),
        lax.all_gather(within[3], "grp", axis=1, tiled=True),
    )
    (
        bias_query,
        bias_value,
        bias_attn,
        gain_one,
        shift_one,
        bias_in,
        bias_out,
        gain_two,
        shift_two,
    ) = [piece.astype(jnp.float32) for piece in within[4:]]
    flat_rows = tokens.reshape(seq_count * length, model_width)
    mixed_qkv = jnp.dot(flat_rows, full_qkv, preferred_element_type=jnp.float32)
    queries = (mixed_qkv[:, :model_width] + bias_query).astype(jnp.bfloat16)
    key_rows = mixed_qkv[:, model_width : 2 * model_width].astype(jnp.bfloat16)
    value_rows = (mixed_qkv[:, 2 * model_width :] + bias_value).astype(jnp.bfloat16)
    query_seqs = queries.reshape(seq_count, length, model_width)
    key_seqs = key_rows.reshape(seq_count, length, model_width)
    value_seqs = value_rows.reshape(seq_count, length, model_width)

    def forward_sequence(pieces):
        return attend_forward(pieces[0], pieces[1], pieces[2], pieces[3], block_rows)

    contexts, log_sums = lax.map(forward_sequence, (query_seqs, key_seqs, value_seqs, segment_ids))
    contexts = contexts.reshape(seq_count * length, model_width)
    attended = jnp.dot(contexts, full_attn, preferred_element_type=jnp.float32) + bias_attn
    first_sum = flat_rows.astype(jnp.float32) + attended
    normed_one, norm_one_back = jax.vjp(norm_layer, first_sum, gain_one, shift_one)
    normed_low = normed_one.astype(jnp.bfloat16)
    hidden_pre = jnp.dot(normed_low, full_in, preferred_element_type=jnp.float32) + bias_in
    hidden, gelu_back = jax.vjp(gelu_exact, hidden_pre)
    hidden_low = hidden.astype(jnp.bfloat16)
    second_sum = normed_one + (
        jnp.dot(hidden_low, full_out, preferred_element_type=jnp.float32) + bias_out
    )
    result, norm_two_back = jax.vjp(norm_layer, second_sum, gain_two, shift_two)
    layer_out = result.astype(jnp.bfloat16).reshape(seq_count, length, model_width)
    again = (
        lax.all_gather(w_qkv, "shard", axis=0, tiled=True),
        lax.all_gather(w_attn_out, "shard", axis=0, tiled=True),
        lax.all_gather(w_in, "shard", axis=0, tiled=True),
        lax.all_gather(w_out, "shard", axis=0, tiled=True),
    )
    back_qkv, back_attn, back_in, back_out = (
        lax.all_gather(again[0], "grp", axis=1, tiled=True),
        lax.all_gather(again[1], "grp", axis=1, tiled=True),
        lax.all_gather(again[2], "grp", axis=1, tiled=True),
        lax.all_gather(again[3], "grp", axis=1, tiled=True),
    )
    masked_cot = cotangent.astype(jnp.float32).reshape(
        seq_count * length, model_width
    ) * keep_flag.reshape(seq_count * length, 1).astype(jnp.float32)
    second_grad, gain_two_grad, shift_two_grad = norm_two_back(masked_cot)
    bias_out_grad = jnp.sum(second_grad, 0)
    out_low = second_grad.astype(jnp.bfloat16)
    w_out_grad = contract_rows(hidden_low, out_low)
    hidden_grad = contract_cols(out_low, back_out)
    (pre_grad,) = gelu_back(hidden_grad)
    bias_in_grad = jnp.sum(pre_grad, 0)
    pre_low = pre_grad.astype(jnp.bfloat16)
    w_in_grad = contract_rows(normed_low, pre_low)
    normed_grad = second_grad + contract_cols(pre_low, back_in)
    first_grad, gain_one_grad, shift_one_grad = norm_one_back(normed_grad)
    bias_attn_grad = jnp.sum(first_grad, 0)
    attn_low = first_grad.astype(jnp.bfloat16)
    w_attn_grad = contract_rows(contexts, attn_low)
    context_grad = contract_cols(attn_low, back_attn).astype(jnp.bfloat16)

    def backward_sequence(pieces):
        return attend_backward(
            pieces[0], pieces[1], pieces[2], pieces[3], pieces[4], pieces[5], block_rows
        )

    query_grad, key_grad, value_grad = lax.map(
        backward_sequence,
        (
            query_seqs,
            key_seqs,
            value_seqs,
            segment_ids,
            log_sums,
            context_grad.reshape(seq_count, length, model_width),
        ),
    )
    query_grad = query_grad.reshape(seq_count * length, model_width)
    key_grad = key_grad.reshape(seq_count * length, model_width)
    value_grad = value_grad.reshape(seq_count * length, model_width)
    bias_query_grad = jnp.sum(query_grad, 0)
    bias_value_grad = jnp.sum(value_grad, 0)
    qkv_low = jnp.concatenate([query_grad, key_grad, value_grad], 1).astype(jnp.bfloat16)
    w_qkv_grad = contract_rows(flat_rows, qkv_low)
    input_grad = first_grad + contract_cols(qkv_low, back_qkv)
    reduced = (
        lax.psum_scatter(
            w_qkv_grad.astype(jnp.bfloat16), "shard", scatter_dimension=0, tiled=True
        ).astype(jnp.float32),
        lax.psum_scatter(
            bias_query_grad.astype(jnp.bfloat16), "shard", scatter_dimension=0, tiled=True
        ).astype(jnp.float32),
        lax.psum_scatter(
            bias_value_grad.astype(jnp.bfloat16), "shard", scatter_dimension=0, tiled=True
        ).astype(jnp.float32),
        lax.psum_scatter(
            w_attn_grad.astype(jnp.bfloat16), "shard", scatter_dimension=0, tiled=True
        ).astype(jnp.float32),
        lax.psum_scatter(
            bias_attn_grad.astype(jnp.bfloat16), "shard", scatter_dimension=0, tiled=True
        ).astype(jnp.float32),
        lax.psum_scatter(
            gain_one_grad.astype(jnp.bfloat16), "shard", scatter_dimension=0, tiled=True
        ).astype(jnp.float32),
        lax.psum_scatter(
            shift_one_grad.astype(jnp.bfloat16), "shard", scatter_dimension=0, tiled=True
        ).astype(jnp.float32),
        lax.psum_scatter(
            w_in_grad.astype(jnp.bfloat16), "shard", scatter_dimension=0, tiled=True
        ).astype(jnp.float32),
        lax.psum_scatter(
            bias_in_grad.astype(jnp.bfloat16), "shard", scatter_dimension=0, tiled=True
        ).astype(jnp.float32),
        lax.psum_scatter(
            w_out_grad.astype(jnp.bfloat16), "shard", scatter_dimension=0, tiled=True
        ).astype(jnp.float32),
        lax.psum_scatter(
            bias_out_grad.astype(jnp.bfloat16), "shard", scatter_dimension=0, tiled=True
        ).astype(jnp.float32),
        lax.psum_scatter(
            gain_two_grad.astype(jnp.bfloat16), "shard", scatter_dimension=0, tiled=True
        ).astype(jnp.float32),
        lax.psum_scatter(
            shift_two_grad.astype(jnp.bfloat16), "shard", scatter_dimension=0, tiled=True
        ).astype(jnp.float32),
    )
    summed = (
        lax.psum(reduced[0].astype(jnp.bfloat16), "grp").astype(jnp.float32),
        lax.psum(reduced[1].astype(jnp.bfloat16), "grp").astype(jnp.float32),
        lax.psum(reduced[2].astype(jnp.bfloat16), "grp").astype(jnp.float32),
        lax.psum(reduced[3].astype(jnp.bfloat16), "grp").astype(jnp.float32),
        lax.psum(reduced[4].astype(jnp.bfloat16), "grp").astype(jnp.float32),
        lax.psum(reduced[5].astype(jnp.bfloat16), "grp").astype(jnp.float32),
        lax.psum(reduced[6].astype(jnp.bfloat16), "grp").astype(jnp.float32),
        lax.psum(reduced[7].astype(jnp.bfloat16), "grp").astype(jnp.float32),
        lax.psum(reduced[8].astype(jnp.bfloat16), "grp").astype(jnp.float32),
        lax.psum(reduced[9].astype(jnp.bfloat16), "grp").astype(jnp.float32),
        lax.psum(reduced[10].astype(jnp.bfloat16), "grp").astype(jnp.float32),
        lax.psum(reduced[11].astype(jnp.bfloat16), "grp").astype(jnp.float32),
        lax.psum(reduced[12].astype(jnp.bfloat16), "grp").astype(jnp.float32),
    )
    return (
        layer_out,
        input_grad.reshape(seq_count, length, model_width),
        summed[0],
        summed[1],
        summed[2],
        summed[3],
        summed[4],
        summed[5],
        summed[6],
        summed[7],
        summed[8],
        summed[9],
        summed[10],
        summed[11],
        summed[12],
    )


NT = (((1,), (1,)), ((), ()))
NN = (((1,), (0,)), ((), ()))
TN = (((0,), (0,)), ((), ()))
LANES = 128
AXES = ("grp", "shard")


def mxu(left, right, dims):
    return lax.dot_general(left, right, dims, preferred_element_type=jnp.float32)


def cost(flops):
    return pl.CostEstimate(flops=2 * flops, bytes_accessed=0, transcendentals=0)


def params(megabytes=60):
    return pltpu.CompilerParams(vmem_limit_bytes=megabytes << 20)


def attention_forward_kernel(q_ref, k_ref, v_ref, seg_col, seg_row, out_ref, lse_ref, *, rows):
    length = q_ref.shape[0]
    first = lax.broadcasted_iota(jnp.int32, (1, LANES), 1) < HD
    keys = k_ref[...]
    values = v_ref[...]
    zero = jnp.zeros_like(keys)
    head_keys = (jnp.where(first, keys, zero), jnp.where(first, zero, keys))
    key_segments = seg_col[...]
    for block in range(length // rows):
        here = pl.ds(block * rows, rows)
        q = q_ref[here, :]
        allowed = key_segments == seg_row[:, here]
        outs = []
        for head in range(2):
            scores = mxu(head_keys[head], q, NT)
            scores = jnp.where(allowed, scores, masked_score)
            top = jnp.max(scores, 0, keepdims=True)
            powers = jnp.exp(scores - top)
            total = jnp.sum(powers, 0, keepdims=True)
            part = mxu(powers.astype(jnp.bfloat16), values, TN)
            outs.append(part * jnp.transpose(jnp.broadcast_to(1.0 / total, (LANES, rows))))
            lse_ref[0, head : head + 1, here] = top + jnp.log(total)
        out_ref[here, :] = jnp.where(first, outs[0], outs[1]).astype(jnp.bfloat16)


def attention_forward(qkv, seg_col, seg_row, start, pairs, before=None):
    length, width = qkv.shape[0], qkv.shape[1] // 3
    total = width // LANES
    rows = min(512, length)
    anywhere = pl.BlockSpec(memory_space=pl.ANY)

    def pair(part):
        return pl.BlockSpec((length, LANES), lambda j: (0, part * total + start + j))

    def body(q_ref, k_ref, v_ref, seg_c, seg_r, *refs):
        attention_forward_kernel(q_ref, k_ref, v_ref, seg_c, seg_r, *refs[-2:], rows=rows)

    return pl.pallas_call(
        body,
        grid=(pairs,),
        in_specs=[
            pair(0),
            pair(1),
            pair(2),
            pl.BlockSpec((length, 1), lambda j: (0, 0)),
            pl.BlockSpec((1, length), lambda j: (0, 0)),
        ]
        + [anywhere] * (0 if before is None else 2),
        out_specs=[
            pl.BlockSpec((length, LANES), lambda j: (0, start + j)),
            pl.BlockSpec((1, 2, length), lambda j: (start + j, 0, 0)),
        ],
        out_shape=[
            jax.ShapeDtypeStruct((length, width), jnp.bfloat16),
            jax.ShapeDtypeStruct((total, 2, length), jnp.float32),
        ],
        input_output_aliases={} if before is None else {5: 0, 6: 1},
        compiler_params=params(60),
        cost_estimate=cost(16 * length * length * pairs * LANES),
        name="attn_fwd",
    )(qkv, qkv, qkv, seg_col, seg_row, *(() if before is None else before))


def attention_backward_kernel(
    q_ref, k_ref, v_ref, o_ref, do_ref, seg_col, seg_row, lse_ref, grad_ref, sum_ref, *, rows
):
    length = q_ref.shape[0]
    lane = lax.broadcasted_iota(jnp.int32, (1, LANES), 1)
    first = lane < HD
    pick = (
        lax.broadcasted_iota(jnp.int32, (8, LANES), 0)
        == lax.broadcasted_iota(jnp.int32, (8, LANES), 1) // HD
    ).astype(jnp.float32)
    keys = k_ref[...]
    values = v_ref[...]
    zero = jnp.zeros_like(keys)
    head_keys = (jnp.where(first, keys, zero), jnp.where(first, zero, keys))
    head_values = (jnp.where(first, values, zero), jnp.where(first, zero, values))
    key_segments = seg_col[...]
    key_sum = [None, None]
    value_sum = [None, None]
    query_total = jnp.zeros((1, LANES), jnp.float32)
    for block in range(length // rows):
        here = pl.ds(block * rows, rows)
        q = q_ref[here, :]
        do = do_ref[here, :]
        allowed = key_segments == seg_row[:, here]
        dots = lax.dot_general(
            pick,
            do.astype(jnp.float32) * o_ref[here, :].astype(jnp.float32),
            NT,
            precision=lax.Precision.HIGHEST,
            preferred_element_type=jnp.float32,
        )
        parts = []
        for head in range(2):
            scores = mxu(head_keys[head], q, NT)
            scores = jnp.where(allowed, scores, masked_score)
            probs = jnp.exp(scores - lse_ref[0, head : head + 1, here])
            prob_grad = mxu(head_values[head], do, NT)
            score_grad = (probs * (prob_grad - dots[head : head + 1, :])).astype(jnp.bfloat16)
            value_part = mxu(probs.astype(jnp.bfloat16), do, NN)
            key_part = mxu(score_grad, q, NN)
            value_sum[head] = value_part if block == 0 else value_sum[head] + value_part
            key_sum[head] = key_part if block == 0 else key_sum[head] + key_part
            parts.append(mxu(score_grad, keys, TN))
        query_grad = jnp.where(first, parts[0], parts[1]) * (1.0 / math.sqrt(HD))
        query_total = query_total + jnp.sum(query_grad, 0, keepdims=True)
        grad_ref[0, here, :] = query_grad.astype(jnp.bfloat16)
    grad_ref[1, :, :] = jnp.where(first, key_sum[0], key_sum[1]).astype(jnp.bfloat16)
    value_grad = jnp.where(first, value_sum[0], value_sum[1])
    grad_ref[2, :, :] = value_grad.astype(jnp.bfloat16)
    sum_ref[0:1, :] = query_total
    sum_ref[1:2, :] = jnp.sum(value_grad, 0, keepdims=True)


def attention_backward(qkv, out, out_grad, seg_col, seg_row, lse, start, pairs, at, size, before=None):
    length, width = out.shape
    total = width // LANES
    rows = min(256, length)
    more = () if before is None else before

    def pair(part):
        return pl.BlockSpec((length, LANES), lambda j: (0, part * total + start + j))

    def body(*refs):
        attention_backward_kernel(*refs[:8], *refs[-2:], rows=rows)

    return pl.pallas_call(
        body,
        grid=(pairs,),
        in_specs=[
            pair(0),
            pair(1),
            pair(2),
            pair(0),
            pair(0),
            pl.BlockSpec((length, 1), lambda j: (0, 0)),
            pl.BlockSpec((1, length), lambda j: (0, 0)),
            pl.BlockSpec((1, 2, length), lambda j: (j + start, 0, 0)),
        ]
        + [pl.BlockSpec(memory_space=pl.ANY)] * len(more),
        out_specs=[
            pl.BlockSpec((3, length, LANES), lambda j: (0, 0, j + at)),
            pl.BlockSpec((2, LANES), lambda j: (0, j + at)),
        ],
        out_shape=[
            jax.ShapeDtypeStruct((3, length, size * LANES), jnp.bfloat16),
            jax.ShapeDtypeStruct((2, size * LANES), jnp.float32),
        ],
        input_output_aliases={} if before is None else {8: 0, 9: 1},
        compiler_params=params(60),
        cost_estimate=cost(40 * length * length * pairs * LANES),
        name="attn_bwd",
    )(qkv, qkv, qkv, out, out_grad, seg_col, seg_row, lse, *more)


class Place:
    def __init__(self, groups, shards):
        self.groups = groups
        self.shards = shards
        self.chips = shards // 2
        self.grp = lax.axis_index("grp")
        self.shard = lax.axis_index("shard")
        self.core = self.shard % 2
        self.chip = self.shard // 2
        self.scalars = jnp.stack([self.core, self.chip, self.grp]).astype(jnp.int32)

    def permute(self, array, mask_of_core):
        pairs = [(i, i ^ mask_of_core[i % 2]) for i in range(self.groups * self.shards)]
        return lax.ppermute(array, AXES, pairs)

    def swap_core(self, array):
        return self.permute(array, (1, 1))

    def swap_grp(self, array, step):
        masks = (self.shards, 2 * self.shards)
        return self.permute(array, masks if step == 0 else masks[::-1])

    def swap_chip(self, array, step):
        masks = (2, 4)
        return self.permute(array, masks if step == 0 else masks[::-1])

    def slot_chip(self, slot):
        return self.chip ^ turn(slot, self.core)

    def slot_grp(self, slot):
        return self.grp ^ turn(slot, self.core)


def turn(slot, core):
    if isinstance(slot, int):
        return slot if slot in (0, 3) else jnp.where(core == 0, slot, 3 - slot)
    return jnp.where((core == 0) | (slot == 0) | (slot == 3), slot, 3 - slot)


def after(value, *others):
    return lax.optimization_barrier((value, *others))[0]


def meet(anchor, *flights):
    arrays = [f.flying for f in flights]
    _, *arrays = lax.optimization_barrier((anchor, *arrays))
    for f, array in zip(flights, arrays):
        f.flying = array


class Gather:
    def __init__(self, place, piece):
        self.place = place
        self.piece = piece
        self.held = [None] * 4
        self.crossed = [None] * 4

    def chips_near(self, *wait):
        self.piece = after(self.piece, *wait)
        self.flying = self.place.swap_chip(self.piece, 0)

    def chips_far(self):
        self.pair = jnp.stack([self.piece, self.flying])
        self.flying = self.place.swap_chip(self.pair, 1)
        return self.pair

    def join(self):
        self.held[0] = jnp.concatenate([self.pair, self.flying])
        return self.held[0]

    def near(self, *wait):
        self.held[0] = after(self.held[0], *wait)
        self.flying = (self.place.swap_grp(self.held[0], 0), self.place.swap_grp(self.held[0], 1))
        return self.held[0]

    def far(self, *wait):
        self.held[1:3] = self.flying
        first = after(self.held[1], *wait)
        self.flying = self.place.swap_grp(first, 1)

    def landed(self):
        self.held[3] = self.flying

    def cross(self, *which, wait=()):
        for n in which:
            self.crossed[n] = self.place.swap_core(after(self.held[n], *wait))

    def pieces(self):
        return self.held + self.crossed


class Window:
    def __init__(self, gather, start, cols):
        self.arrays = gather.pieces()
        self.start, self.cols = start, cols
        chips, rows, _ = self.arrays[0].shape
        self.chips, self.rows = chips, rows


def fetch(where, window, refs, whole, sem, by):
    rows, cols, chips = window.rows, window.cols, window.chips
    for slot in range(4):
        for side in range(2):
            core = where[0] ^ side
            ref = refs[4 * side + slot]
            distance = turn(slot, core)
            col = pl.multiple_of((where[2] ^ distance) * cols, LANES)
            for k in range(chips):
                row = ((where[1] ^ turn(k, core)) * 2 + core) * rows
                pltpu.make_async_copy(
                    ref.at[k, :, pl.ds(window.start, cols)],
                    whole.at[pl.ds(pl.multiple_of(row, rows), rows), pl.ds(col, cols)],
                    sem.at[distance if by == "grp" else 0],
                ).start()


def weight_call(place, kernel, window, inputs, in_specs, outs, out_specs, steps, by, name, flops, mb=60):
    cols, groups = window.cols, place.groups
    pieces = window.arrays
    shape = (window.chips * 2 * window.rows, groups * cols)
    slots = {"grp": groups, "all": 1}[by]
    anywhere = pl.BlockSpec(memory_space=pl.ANY)

    def body(where, *refs):
        taken, refs = refs[: len(pieces)], refs[len(pieces) :]
        *refs, written, weight, sem, out_sem = refs
        step = pl.program_id(0)

        @pl.when(step == 0)
        def _():
            fetch(where, window, taken, weight, sem, by)

        def ready():
            if by == "all":

                @pl.when(step == 0)
                def _():
                    pltpu.make_async_copy(weight, weight, sem.at[0]).wait()
                    pltpu.make_async_copy(weight, written, out_sem.at[0]).start()

            else:
                at = pl.ds(pl.multiple_of((where[2] ^ step) * cols, LANES), cols)
                view = weight.at[:, at]
                pltpu.make_async_copy(view, view, sem.at[step]).wait()
                pltpu.make_async_copy(view, written.at[:, at], out_sem.at[step]).start()

        kernel(where, ready, weight, *refs)

        @pl.when(step == steps - 1)
        def _():
            for slot in range(slots):
                width = shape[1] // slots
                view = weight.at[:, pl.ds(slot * width, width)]
                pltpu.make_async_copy(view, view, out_sem.at[slot]).wait()

    total = sum(math.prod(x.shape) * x.dtype.itemsize for x in list(inputs) + list(outs))
    return pl.pallas_call(
        body,
        grid_spec=pltpu.PrefetchScalarGridSpec(
            num_scalar_prefetch=1,
            grid=(steps,),
            in_specs=[anywhere] * len(pieces) + in_specs,
            out_specs=out_specs + [anywhere],
            scratch_shapes=[
                pltpu.VMEM(shape, jnp.bfloat16),
                pltpu.SemaphoreType.DMA((slots,)),
                pltpu.SemaphoreType.DMA((slots,)),
            ],
        ),
        out_shape=outs + [shaped(shape, jnp.bfloat16)],
        compiler_params=params(mb),
        cost_estimate=cost(flops),
        name=name,
    )(place.scalars, *pieces, *inputs)


def plain_call(kernel, inputs, in_specs, outs, out_specs, steps, name, flops, mb=60):
    total = sum(math.prod(x.shape) * x.dtype.itemsize for x in list(inputs) + list(outs))
    return pl.pallas_call(
        kernel,
        grid=(steps,),
        in_specs=in_specs,
        out_specs=out_specs,
        out_shape=outs,
        compiler_params=params(mb),
        cost_estimate=cost(flops),
        name=name,
    )(*inputs)


TILE = 256


def row_tiles(width):
    return pl.BlockSpec((TILE, width), lambda i, *s: (i, 0))


def fixed(*shape):
    return pl.BlockSpec(shape, lambda i, *s: (0,) * len(shape))


def whole_once(shape):
    return pl.BlockSpec(shape, lambda i: (0,) * len(shape), pipeline_mode=pl.Buffered(1))


def shaped(shape, dtype):
    return jax.ShapeDtypeStruct(shape, dtype)


B_QUERY, B_VALUE, B_ATTN, GAIN_ONE, SHIFT_ONE, B_OUT, GAIN_TWO, SHIFT_TWO, B_IN = range(9)


def row(ref, n):
    return ref[n : n + 1, :]


class Vectors:
    def __init__(self, place, vectors):
        lines = [v.reshape(-1, LANES) for v in vectors]
        blank = jnp.zeros((-sum(x.shape[0] for x in lines) % 16, LANES), jnp.bfloat16)
        self.own = jnp.concatenate([*lines, blank])
        self.place = place
        self.flying = place.swap_core(self.own)

    def chips_near(self):
        self.own = jnp.stack([self.own, self.flying])
        self.flying = self.place.swap_chip(self.own, 0)

    def chips_far(self):
        self.own = jnp.stack([self.own, self.flying])
        self.flying = self.place.swap_chip(self.own, 1)

    def landed(self):
        self.slots = jnp.concatenate([self.own, self.flying])

    def unpack(self):
        place = self.place
        slots, sides, rows, lanes = self.slots.shape
        shards = place.shards

        def kernel(where, in_ref, rows_ref, inner_ref, qkv_ref):
            width = shards * lanes
            qkv_ref[...] = jnp.zeros_like(qkv_ref)
            for slot in range(slots):
                for side in range(sides):
                    core = where[0] ^ side
                    shard = (where[1] ^ turn(slot, where[0])) * 2 + core
                    part = in_ref[slot, side].astype(jnp.float32)
                    at = pl.multiple_of(shard * lanes, lanes)
                    rows_ref[:, pl.ds(at, lanes)] = part
                    qkv_ref[:, pl.ds(at, lanes)] = part[B_QUERY : B_QUERY + 1]
                    qkv_ref[:, pl.ds(2 * width + at, lanes)] = part[B_VALUE : B_VALUE + 1]
                    for n in range(4):
                        start = pl.multiple_of((shard * 4 + n) * lanes, lanes)
                        inner_ref[:, pl.ds(start, lanes)] = part[B_IN + n : B_IN + n + 1]

        in_vmem = pl.BlockSpec(memory_space=pltpu.VMEM)
        return pl.pallas_call(
            kernel,
            in_specs=[pl.BlockSpec(memory_space=pltpu.SMEM), in_vmem],
            out_specs=[in_vmem] * 3,
            out_shape=[
                shaped((rows, shards * lanes), jnp.float32),
                shaped((1, 4 * shards * lanes), jnp.float32),
                shaped((1, 3 * shards * lanes), jnp.float32),
            ],
            name="vectors",
        )(place.scalars, self.slots)


def pack_sums(late_a, late_b, first_sums, second_sums, inner_sums):
    width = first_sums.shape[1]
    half = late_a.shape[1]

    def kernel(a_ref, b_ref, one_ref, two_ref, inner_ref, out_ref):
        def place_of(n):
            return n // 3 * 8 + n % 3

        out_ref[...] = jnp.zeros_like(out_ref)
        for n in (B_QUERY, B_VALUE):
            at = place_of(n)
            out_ref[at : at + 1, 0:half] = a_ref[n : n + 1, :]
            out_ref[at : at + 1, half:width] = b_ref[n : n + 1, :]
        for n, source, line in (
            (GAIN_ONE, one_ref, 0),
            (SHIFT_ONE, one_ref, 1),
            (B_ATTN, one_ref, 2),
            (GAIN_TWO, two_ref, 0),
            (SHIFT_TWO, two_ref, 1),
            (B_OUT, two_ref, 2),
        ):
            at = place_of(n)
            out_ref[at : at + 1, :] = source[line : line + 1, :]
        for n in range(4):
            at = place_of(B_IN + n)
            for shard in range(width // LANES):
                start = (4 * shard + n) * LANES
                out_ref[at : at + 1, shard * LANES : (shard + 1) * LANES] = inner_ref[
                    :, start : start + LANES
                ]

    in_vmem = pl.BlockSpec(memory_space=pltpu.VMEM)
    return pl.pallas_call(
        kernel,
        in_specs=[in_vmem] * 5,
        out_specs=in_vmem,
        out_shape=shaped((32, width), jnp.float32),
        name="pack_sums",
    )(late_a, late_b, first_sums, second_sums, inner_sums)


def project_qkv(place, rows, window, bias, scale):
    length, width = rows.shape
    cols = window.cols

    def kernel(where, ready, weight, x_ref, bias_ref, scale_ref, out_ref):
        ready()
        at = pl.ds(pl.multiple_of((where[2] ^ pl.program_id(0)) * cols, LANES), cols)
        for tile in range(length // TILE):
            here = pl.ds(tile * TILE, TILE)
            mixed = mxu(x_ref[here, :], weight[:, at], NN) + bias_ref[:, at]
            mixed = mixed.astype(jnp.bfloat16).astype(jnp.float32) * scale_ref[:, at]
            out_ref[here, :] = mixed.astype(jnp.bfloat16)

    total = cols * place.groups
    return weight_call(
        place,
        kernel,
        window,
        (rows, bias, scale),
        [fixed(length, width), fixed(1, total), fixed(1, total)],
        [shaped((length, total), jnp.bfloat16)],
        [pl.BlockSpec((length, cols), lambda i, s: (0, i ^ s[2]))],
        place.groups,
        "grp",
        "qkv",
        2 * length * width * total,
    )


def norm_parts(rows):
    centered = rows - jnp.mean(rows, -1, keepdims=True)
    scale = lax.rsqrt(jnp.mean(centered * centered, -1, keepdims=True) + epsilon)
    return centered * scale, scale


def norm_back(grad, normed, scale):
    return scale * (
        grad
        - jnp.mean(grad, -1, keepdims=True)
        - normed * jnp.mean(grad * normed, -1, keepdims=True)
    )


def add_rows(sum_ref, *terms):
    @pl.when(pl.program_id(0) == 0)
    def _():
        sum_ref[...] = jnp.zeros_like(sum_ref)

    for n, term in enumerate(terms):
        sum_ref[n : n + 1, :] += jnp.sum(term, 0, keepdims=True)


def project_out(place, contexts, window, rows, vectors):
    length, width = rows.shape

    def kernel(where, ready, weight, c_ref, x_ref, v_ref, n_ref, r_ref, low_ref):
        ready()
        first_sum = mxu(c_ref[...], weight[...], NN) + row(v_ref, B_ATTN)
        first_sum = first_sum + x_ref[...].astype(jnp.float32)
        normed, scale = norm_parts(first_sum)
        n_ref[...] = normed
        r_ref[...] = jnp.broadcast_to(scale, r_ref.shape)
        low_ref[...] = (normed * row(v_ref, GAIN_ONE) + row(v_ref, SHIFT_ONE)).astype(jnp.bfloat16)

    return weight_call(
        place,
        kernel,
        window,
        (contexts, rows, vectors),
        [row_tiles(width), row_tiles(width), fixed(*vectors.shape)],
        [
            shaped((length, width), jnp.float32),
            shaped((length, LANES), jnp.float32),
            shaped((length, width), jnp.bfloat16),
        ],
        [row_tiles(width), row_tiles(LANES), row_tiles(width)],
        length // TILE,
        "all",
        "attn_out",
        2 * length * width * width,
    )


def feed_in(place, normed_low, window, bias):
    length, width = normed_low.shape
    cols = window.cols

    def kernel(where, ready, weight, x_ref, bias_ref, hid_ref, slope_ref):
        ready()
        at = pl.ds(pl.multiple_of((where[2] ^ pl.program_id(0)) * cols, LANES), cols)
        for tile in range(length // TILE):
            here = pl.ds(tile * TILE, TILE)
            pre = mxu(x_ref[here, :], weight[:, at], NN) + bias_ref[:, at]
            share = 0.5 + 0.5 * lax.erf(pre * (1.0 / math.sqrt(2.0)))
            bell = jnp.exp(-0.5 * pre * pre) * (1.0 / math.sqrt(2.0 * math.pi))
            hid_ref[here, :] = (pre * share).astype(jnp.bfloat16)
            slope_ref[here, :] = (share + pre * bell).astype(jnp.bfloat16)

    total = cols * place.groups
    block = pl.BlockSpec((length, cols), lambda i, s: (0, i ^ s[2]))
    return weight_call(
        place,
        kernel,
        window,
        (normed_low, bias),
        [fixed(length, width), fixed(1, total)],
        [shaped((length, total), jnp.bfloat16)] * 2,
        [block, block],
        place.groups,
        "grp",
        "feed_in",
        2 * length * width * total,
    )


def feed_out(place, hidden, window, normed, cot, keep, vectors):
    length, inner = hidden.shape
    width = normed.shape[1]

    def kernel(where, ready, weight, h_ref, n_ref, cot_ref, keep_ref, v_ref, *outs):
        out_ref, grad_ref, low_ref, sum_ref = outs
        ready()
        fed = mxu(h_ref[...], weight[...], NN)
        normed_one = n_ref[...] * row(v_ref, GAIN_ONE) + row(v_ref, SHIFT_ONE)
        second_sum = normed_one + (fed + row(v_ref, B_OUT))
        second, scale = norm_parts(second_sum)
        out_ref[...] = (second * row(v_ref, GAIN_TWO) + row(v_ref, SHIFT_TWO)).astype(jnp.bfloat16)
        masked = cot_ref[...].astype(jnp.float32) * keep_ref[...]
        grad = norm_back(masked * row(v_ref, GAIN_TWO), second, scale)
        grad_ref[...] = grad
        low_ref[...] = grad.astype(jnp.bfloat16)
        add_rows(sum_ref, masked * second, masked, grad)

    return weight_call(
        place,
        kernel,
        window,
        (hidden, normed, cot, keep, vectors),
        [row_tiles(inner), row_tiles(width), row_tiles(width), row_tiles(1), fixed(*vectors.shape)],
        [
            shaped((length, width), jnp.bfloat16),
            shaped((length, width), jnp.float32),
            shaped((length, width), jnp.bfloat16),
            shaped((8, width), jnp.float32),
        ],
        [row_tiles(width), row_tiles(width), row_tiles(width), fixed(8, width)],
        length // TILE,
        "all",
        "feed_out",
        2 * length * width * inner,
    )


def feed_out_back(out_low, weight, slope):
    length, width = out_low.shape
    inner = slope.shape[1]
    cols = min(1024, inner)

    def kernel(g_ref, w_ref, slope_ref, pre_ref, sum_ref):
        total = jnp.zeros((1, cols), jnp.float32)
        for tile in range(length // TILE):
            here = pl.ds(tile * TILE, TILE)
            grad = mxu(g_ref[here, :], w_ref[...], NT) * slope_ref[here, :].astype(jnp.float32)
            pre_ref[here, :] = grad.astype(jnp.bfloat16)
            total = total + jnp.sum(grad, 0, keepdims=True)
        sum_ref[...] = total

    block = pl.BlockSpec((length, cols), lambda i: (0, i))
    return plain_call(
        kernel,
        (out_low, weight, slope),
        [fixed(length, width), pl.BlockSpec((cols, width), lambda i: (i, 0)), block],
        [shaped((length, inner), jnp.bfloat16), shaped((1, inner), jnp.float32)],
        [block, pl.BlockSpec((1, cols), lambda i: (0, i))],
        inner // cols,
        "feed_out_back",
        2 * length * width * inner,
    )


def feed_in_back(pre_low, weight, second_grad, normed, scale, vectors, attn_weight):
    length, inner = pre_low.shape
    width = normed.shape[1]

    def kernel(p_ref, w_ref, g_ref, n_ref, r_ref, v_ref, a_ref, first_ref, low_ref, ctx_ref, sum_ref):
        grad = g_ref[...] + mxu(p_ref[...], w_ref[...], NT)
        first = norm_back(grad * row(v_ref, GAIN_ONE), n_ref[...], r_ref[:, :1])
        low = first.astype(jnp.bfloat16)
        first_ref[...] = first
        low_ref[...] = low
        ctx_ref[...] = mxu(low, a_ref[...], NT).astype(jnp.bfloat16)
        add_rows(sum_ref, grad * n_ref[...], grad, first)

    return plain_call(
        kernel,
        (pre_low, weight, second_grad, normed, scale, vectors, attn_weight),
        [
            row_tiles(inner),
            whole_once(weight.shape),
            row_tiles(width),
            row_tiles(width),
            row_tiles(LANES),
            fixed(*vectors.shape),
            whole_once(attn_weight.shape),
        ],
        [
            shaped((length, width), jnp.float32),
            shaped((length, width), jnp.bfloat16),
            shaped((length, width), jnp.bfloat16),
            shaped((8, width), jnp.float32),
        ],
        [row_tiles(width), row_tiles(width), row_tiles(width), fixed(8, width)],
        length // TILE,
        "feed_in_back",
        2 * length * width * (inner + width),
    )


def project_qkv_back(grads, weight, first_grad, start, tiles, before=None):
    length, width = first_grad.shape
    part = width // len(grads)

    def kernel(w_ref, *refs):
        grad_refs, first_ref, out_ref = refs[: len(grads)], refs[len(grads)], refs[-1]
        total = first_ref[...]
        for n in range(3):
            for m, grad_ref in enumerate(grad_refs):
                at = n * width + m * part
                total = total + mxu(grad_ref[n], w_ref[:, at : at + part], NT)
        out_ref[...] = total

    tile = pl.BlockSpec((TILE, width), lambda i: (start + i, 0))
    more = () if before is None else (before,)
    return pl.pallas_call(
        kernel,
        grid=(tiles,),
        in_specs=[whole_once(weight.shape)]
        + [pl.BlockSpec((3, TILE, part), lambda i: (0, start + i, 0))] * len(grads)
        + [tile]
        + [pl.BlockSpec(memory_space=pl.ANY)] * len(more),
        out_specs=tile,
        out_shape=shaped((length, width), jnp.float32),
        input_output_aliases={} if before is None else {len(grads) + 2: 0},
        compiler_params=params(60),
        cost_estimate=cost(6 * tiles * TILE * width * width),
        name="qkv_back",
    )(weight, *grads, first_grad, *more)


ORDER = (1, 3, 0, 2)


def ordered_slot(j):
    return jnp.where(j < 2, 2 * j + 1, 2 * j - 4)


def weight_grad_kernel(where, left_ref, right_ref, own, sent, kept, *, rows, groups, split):
    core = where[0]
    chips = left_ref.shape[1] // (2 * rows)

    @pl.when(pl.program_id(1) == 0)
    def _():
        for side in range(2):
            chosen = []
            for k in range(chips):
                even = left_ref[:, 2 * k * rows : (2 * k + 1) * rows]
                odd = left_ref[:, (2 * k + 1) * rows : (2 * k + 2) * rows]
                chosen.append(jnp.where(core == side, even, odd))
            left = chosen[0] if chips == 1 else jnp.concatenate(chosen, 1)
            kept[side] = left.T

    if split:
        size = min(512, right_ref.shape[1])
        for ref, side in ((sent, 1), (own, 0)):
            for n in range(right_ref.shape[1] // size):
                at = slice(n * size, (n + 1) * size)
                part = mxu(kept[side], right_ref[:, at], NN).astype(jnp.bfloat16)
                ref[0, :, :, at] = part.reshape(chips, rows, size)
    else:
        cols = right_ref.shape[1] // groups
        for ref, side in ((sent, 1), (own, 0)):
            for pos, slot in enumerate(ORDER):
                start = pl.multiple_of((where[2] ^ turn(slot, core ^ side)) * cols, LANES)
                part = mxu(kept[side], right_ref[:, pl.ds(start, cols)], NN)
                ref[pos] = part.astype(jnp.bfloat16).reshape(chips, rows, cols)


def attention_grads_kernel(where, *refs, rows, groups, extra):
    left_ref, right_ref, *refs = refs
    *more, own, sent, kept = refs
    core, grp = where[0], where[2]
    chips = left_ref.shape[1] // (2 * rows)
    step = pl.program_id(0)

    def keep_rows(ref):
        for side in range(2):
            chosen = []
            for k in range(chips):
                even = ref[:, 2 * k * rows : (2 * k + 1) * rows]
                odd = ref[:, (2 * k + 1) * rows : (2 * k + 2) * rows]
                chosen.append(jnp.where(core == side, even, odd))
            kept[side] = jnp.concatenate(chosen, 1).T

    def scatter(right, at, cols):
        for ref, side in ((sent, 1), (own, 0)):
            part = mxu(kept[side], right, NN).astype(jnp.bfloat16)
            for g in range(groups):
                pos = position(grp ^ g, core ^ side)
                block = part[:, g * cols : (g + 1) * cols].reshape(chips, rows, cols)
                ref[pos, :, 0:rows, pl.ds(at, cols)] = block

    skip = 0
    if not extra:
        other_left, other_right = more
        skip = other_right.shape[1] // groups

    @pl.when(step == 0)
    def _():
        if not extra:
            keep_rows(other_left)
            scatter(other_right[...], 0, skip)
        keep_rows(left_ref)

    cols = right_ref.shape[2] // groups
    scatter(right_ref[0], pl.multiple_of(skip + step * cols, LANES), cols)

    if extra:
        (sums_ref,) = more

        @pl.when(step == 2)
        def _():
            blank = jnp.zeros((extra, own.shape[3]), jnp.bfloat16)
            for ref, side in ((sent, 1), (own, 0)):
                for g in range(groups):
                    pos = position(grp ^ g, core ^ side)
                    for k in range(chips):
                        start = pl.multiple_of((2 * k + (core ^ side)) * LANES, LANES)
                        ref[pos, k, rows : rows + extra, :] = blank
                        lines = sums_ref[8 * g : 8 * g + 8, pl.ds(start, LANES)]
                        for n in range(3):
                            ref[pos, k, rows : rows + 1, n * LANES : (n + 1) * LANES] = lines[
                                n : n + 1
                            ].astype(jnp.bfloat16)


def position(distance, core):
    slot = turn(distance, core)
    return jnp.where(slot == 0, 2, jnp.where(slot == 1, 0, jnp.where(slot == 3, 1, 3)))


def attention_grads(place, left, right, more, name):
    tokens, height = left.shape
    groups, chips = place.groups, place.chips
    rows = height // place.shards
    extra = 16 if len(more) == 1 else 0
    size = right.shape[2]
    cols = 3 * size // groups + (0 if extra else more[1].shape[1] // groups)
    shape = (groups, chips, rows + extra, cols)
    once = [
        pl.BlockSpec(x.shape, lambda i, s: (0, 0), pipeline_mode=pl.Buffered(1)) for x in more
    ]
    return pl.pallas_call(
        functools.partial(attention_grads_kernel, rows=rows, groups=groups, extra=extra),
        grid_spec=pltpu.PrefetchScalarGridSpec(
            num_scalar_prefetch=1,
            grid=(3,),
            in_specs=[
                pl.BlockSpec(left.shape, lambda i, s: (0, 0), pipeline_mode=pl.Buffered(1)),
                pl.BlockSpec((1, tokens, size), lambda i, s: (i, 0, 0)),
            ]
            + once,
            out_specs=[pl.BlockSpec(shape, lambda i, s: (0, 0, 0, 0))] * 2,
            scratch_shapes=[pltpu.VMEM((2, height // 2, tokens), jnp.bfloat16)],
        ),
        out_shape=[shaped(shape, jnp.bfloat16)] * 2,
        compiler_params=params(60),
        cost_estimate=cost(2 * tokens * height * cols * groups),
        name="wgrad_" + name,
    )(place.scalars, left, right, *more)


def weight_grad(place, left, right, split, name):
    tokens, height = left.shape
    groups, chips = place.groups, place.chips
    rows = height // place.shards
    step_chips = chips if split else max(1, 1024 // (2 * rows))
    cols = right.shape[1] // groups
    if split:
        grid = (1, groups)
        block = lambda i, j, s: (0, s[2] ^ turn(ordered_slot(j), s[0]))
        right_spec = pl.BlockSpec((tokens, cols), block)
        one = (1, chips, rows, cols)
        other = lambda j: jnp.where(j == 0, 3, jnp.where(j == 3, 0, j))
        out_specs = [
            pl.BlockSpec(one, lambda i, j, s: (j, 0, 0, 0)),
            pl.BlockSpec(one, lambda i, j, s: (other(j), 0, 0, 0)),
        ]
    else:
        grid = (chips // step_chips, 1)
        right_spec = pl.BlockSpec(right.shape, lambda i, j, s: (0, 0))
        out_specs = [
            pl.BlockSpec((groups, step_chips, rows, cols), lambda i, j, s: (0, i, 0, 0))
        ] * 2
    return pl.pallas_call(
        functools.partial(weight_grad_kernel, rows=rows, groups=groups, split=split),
        grid_spec=pltpu.PrefetchScalarGridSpec(
            num_scalar_prefetch=1,
            grid=grid,
            in_specs=[
                pl.BlockSpec((tokens, step_chips * 2 * rows), lambda i, j, s: (0, i)),
                right_spec,
            ],
            out_specs=out_specs,
            scratch_shapes=[pltpu.VMEM((2, step_chips * rows, tokens), jnp.bfloat16)],
        ),
        out_shape=[shaped((groups, chips, rows, cols), jnp.bfloat16)] * 2,
        compiler_params=params(60),
        cost_estimate=cost(2 * tokens * height * cols * groups),
        name="wgrad_" + name,
    )(place.scalars, left, right)


def add(*terms):
    total = terms[0].astype(jnp.float32)
    for term in terms[1:]:
        total = total + term.astype(jnp.float32)
    return total.astype(jnp.bfloat16)


class Reduction:
    def __init__(self, place, made):
        self.place = place
        self.made, sent = made
        self.flying = place.swap_core(sent)

    def near(self):
        self.core = self.flying
        leave = add(self.made[:2], self.core[:2])
        self.flying = self.place.swap_grp(leave, 0)
        return leave

    def middle(self):
        self.first = self.flying
        second = add(self.made[3], self.core[3], self.first[1])
        self.flying = self.place.swap_grp(second, 1)
        return second

    def column(self):
        mine = add(self.made[2], self.core[2], self.first[0], self.flying)
        return mine, lambda chip: lax.dynamic_index_in_dim(mine, chip, 0, False)

    def along(self):
        place = self.place
        mine, at = self.column()
        self.mine = [at(place.slot_chip(slot)) for slot in range(4)]
        both = jnp.stack([self.mine[1], self.mine[3]])
        self.flying = place.swap_chip(both, 0)
        return both

    def along_far(self):
        self.first = self.flying
        second = add(self.mine[2], self.first[1])
        self.flying = self.place.swap_chip(second, 1)
        return second

    def share(self):
        return add(self.mine[0], self.first[0], self.flying)

    def share_direct(self):
        place = self.place
        mine, at = self.column()
        terms = [
            place.permute(at(place.chip ^ k), (2 * k, 2 * k)) for k in range(place.chips - 1, 0, -1)
        ]
        return add(at(place.chip), *terms)


class Replication:
    def __init__(self, place, share, direct=False):
        self.place = place
        self.blocks = [share] + [None] * 3
        if direct:
            size = place.shards
            for mask in (3, 1, 2):
                self.blocks[mask] = place.permute(share, (mask * size, mask * size))
        else:
            self.flying = place.swap_grp(share, 0)

    def far(self):
        pair = jnp.stack([self.blocks[0], self.flying])
        self.blocks[1] = self.flying
        self.flying = self.place.swap_grp(pair, 1)
        return pair

    def landed(self):
        if self.blocks[2] is None:
            self.blocks[2:] = [self.flying[0], self.flying[1]]
        return self.blocks


def order_feed_forward(place, blocks, rows_in):
    groups = place.groups
    height, cols = blocks[0].shape
    rows_out = height - groups * rows_in

    def kernel(where, *refs):
        *blocks, out_ref, in_ref = refs
        for slot, ref in enumerate(blocks):
            g = where[2] ^ turn(slot, where[0])
            at = pl.multiple_of(g * cols, LANES)
            out_ref[:, pl.ds(at, cols)] = ref[0:rows_out, :].astype(jnp.float32)
            for n in range(groups):
                at = pl.multiple_of((g * groups + n) * cols, LANES)
                part = ref[rows_out + n * rows_in : rows_out + (n + 1) * rows_in, :]
                in_ref[:, pl.ds(at, cols)] = part.astype(jnp.float32)

    in_vmem = pl.BlockSpec(memory_space=pltpu.VMEM)
    return pl.pallas_call(
        kernel,
        in_specs=[pl.BlockSpec(memory_space=pltpu.SMEM)] + [in_vmem] * groups,
        out_specs=[in_vmem] * 2,
        out_shape=[
            shaped((rows_out, groups * cols), jnp.float32),
            shaped((rows_in, groups * groups * cols), jnp.float32),
        ],
        compiler_params=params(40),
        cost_estimate=cost(height * cols * 1024),
        name="order_feed_forward",
    )(place.scalars, *blocks)


def order_attention(place, blocks_a, blocks_b, rows):
    groups = place.groups
    size = blocks_b[0].shape[1] // 3
    skip = blocks_a[0].shape[1] - 3 * size
    width = groups * skip

    def kernel(where, *refs):
        *blocks, attn_ref, qkv_ref, small_ref = refs
        for n in range(groups):
            ref = blocks[n]
            g = where[2] ^ turn(n, where[0])
            attn_ref[:, pl.ds(pl.multiple_of(g * skip, LANES), skip)] = ref[:, 0:skip].astype(
                jnp.float32
            )
            for part in range(3):
                at = pl.multiple_of(part * width + g * size, LANES)
                block = ref[:, skip + part * size : skip + (part + 1) * size]
                qkv_ref[:, pl.ds(at, size)] = block.astype(jnp.float32)
        for n in range(groups):
            ref = blocks[groups + n]
            g = where[2] ^ n
            lines = []
            for part in range(3):
                at = pl.multiple_of(part * width + width // 2 + g * size, LANES)
                here = slice(part * size, (part + 1) * size)
                qkv_ref[:, pl.ds(at, size)] = ref[0:rows, here].astype(jnp.float32)
                lines.append(ref[rows : rows + 16, here].astype(jnp.float32)[0:1])
            lines.append(jnp.zeros((5, size), jnp.float32))
            small_ref[pl.ds(pl.multiple_of(g * 8, 8), 8), :] = jnp.concatenate(lines)

    in_vmem = pl.BlockSpec(memory_space=pltpu.VMEM)
    return pl.pallas_call(
        kernel,
        in_specs=[pl.BlockSpec(memory_space=pltpu.SMEM)] + [in_vmem] * (2 * groups),
        out_specs=[in_vmem] * 3,
        out_shape=[
            shaped((rows, width), jnp.float32),
            shaped((rows, 3 * width), jnp.float32),
            shaped((8 * groups, size), jnp.float32),
        ],
        compiler_params=params(40),
        name="order_attention",
    )(place.scalars, *blocks_a, *blocks_b)


def on_device_permutes(
    tokens,
    segment_ids,
    keep_flag,
    cotangent,
    w_qkv,
    b_query,
    b_value,
    w_attn_out,
    b_attn_out,
    norm1_gain,
    norm1_bias,
    w_in,
    b_in,
    w_out,
    b_out,
    norm2_gain,
    norm2_bias,
    *,
    groups,
    shards,
):
    place = Place(groups, shards)
    _, length, width = tokens.shape
    rows = tokens[0]
    seg_row = segment_ids.reshape(1, length)
    seg_col = segment_ids.reshape(length, 1)
    keep = keep_flag.reshape(length, 1).astype(jnp.float32)
    pairs = width // LANES

    c1 = Gather(place, w_qkv)
    c2 = Gather(place, jnp.concatenate([w_in, w_attn_out], 1))
    c3 = Gather(place, w_out)
    c1.chips_near()
    small = Vectors(
        place,
        (b_query, b_value, b_attn_out, norm1_gain, norm1_bias, b_out, norm2_gain, norm2_bias, b_in),
    )
    seg_col, keep, _ = lax.optimization_barrier((seg_col, keep, c1.flying))
    meet(seg_col, c1, small)
    pair = c1.chips_far()
    small.chips_near()
    meet(pair, c1, small)
    joined = c1.join()
    c1.near()
    small.chips_far()
    c2.chips_near(joined)
    meet(joined, c2, small)
    small.landed()
    pair = c2.chips_far()
    vectors, bias_in, qkv_bias = small.unpack()
    c1.flying = lax.optimization_barrier(c1.flying)
    c1.far(pair, vectors)
    c1.cross(0, 1, 2)
    joined = c2.join()
    meet(joined, c1)
    c1.landed()
    c2.near(c1.held[3])
    c1.cross(3)
    c3.chips_near(c1.held[3])
    blank = jnp.ones((1, width), jnp.float32)
    qkv_scale = jnp.concatenate([blank / math.sqrt(HD), blank, blank], 1)

    mixed, full_qkv = project_qkv(place, rows, Window(c1, 0, w_qkv.shape[1]), qkv_bias, qkv_scale)
    meet(mixed, c3)
    pair = c3.chips_far()
    c2.cross(0, wait=(mixed,))
    first, second = pairs * 3 // 8, pairs * 3 // 4
    forward = attention_forward(after(mixed, pair), seg_col, seg_row, 0, first)
    meet(forward[1], c2, c3)
    c2.far()
    joined = c3.join()
    c3.near()
    c2.cross(1, 2)
    forward = attention_forward(
        after(mixed, joined), seg_col, seg_row, first, second - first, forward
    )
    meet(forward[1], c2)
    c2.landed()
    c2.cross(3)
    contexts, lse = attention_forward(
        after(mixed, c2.held[3]), seg_col, seg_row, second, pairs - second, forward
    )
    normed, scale_one, normed_low, full_attn = project_out(
        place, contexts, Window(c2, w_in.shape[1], w_attn_out.shape[1]), rows, vectors
    )
    meet(normed_low, c3)
    c3.far()
    c3.cross(0, 1, 2)
    hidden, slope, full_in = feed_in(
        place, after(normed_low, c3.held[1]), Window(c2, 0, w_in.shape[1]), bias_in
    )
    meet(hidden, c3)
    c3.landed()
    c3.cross(3)
    layer_out, second_grad, out_low, second_sums, full_out = feed_out(
        place, hidden, Window(c3, 0, w_out.shape[1]), normed, cotangent[0], keep, vectors
    )

    r_out = Reduction(place, weight_grad(place, hidden, out_low, False, "out"))
    pre_low, bias_in_grad = feed_out_back(after(out_low, r_out.made), full_out, slope)
    meet(pre_low, r_out)
    step = r_out.near()
    r_in = Reduction(place, weight_grad(place, after(normed_low, step), pre_low, True, "in"))
    first_grad, attn_low, context_grad, first_sums = feed_in_back(
        after(pre_low, r_in.made), full_in, second_grad, normed, scale_one, vectors, full_attn
    )
    meet(attn_low, r_in)
    step = r_in.near()
    half, quarter = pairs // 2, pairs // 4

    def back(wait, start, count, at, before=None):
        return attention_backward(
            mixed,
            contexts,
            after(context_grad, *wait),
            seg_col,
            seg_row,
            lse,
            start,
            count,
            at,
            half,
            before,
        )

    low_a, late_a = back((step,), 0, half, 0)
    meet(late_a, r_out, r_in)
    steps = (r_out.middle(), r_in.middle())
    r_a = Reduction(
        place, attention_grads(place, after(rows, *steps), low_a, (contexts, attn_low), "a")
    )
    meet(r_a.made, r_out)
    step = r_out.along()
    part = back((r_a.made, step), half, quarter, 0)
    meet(part[1], r_out, r_in, r_a)
    steps = (r_out.along_far(), r_in.along(), r_a.near())
    low_b, late_b = back(steps, half + quarter, quarter, quarter, part)
    meet(late_b, r_out, r_in, r_a)
    sums = pack_sums(late_a, late_b, first_sums, second_sums, bias_in_grad)
    share_out = r_out.share()
    steps = (r_in.along_far(), r_a.middle(), share_out)
    r_b = Reduction(place, attention_grads(place, after(rows, *steps), low_b, (sums,), "b"))
    meet(r_b.made, r_in, r_a)
    share_in = r_in.share()
    inner = share_in.shape[1] // groups
    joined = jnp.concatenate(
        [share_out] + [share_in[:, n * inner : (n + 1) * inner] for n in range(groups)]
    )
    all_ffn = Replication(place, joined)
    grads = (low_a, after(low_b, r_b.made, joined, r_a.along()))
    tiles = length // TILE // 2
    input_grad = project_qkv_back(grads, full_qkv, first_grad, 0, tiles)
    meet(input_grad, r_b, r_a, all_ffn)
    steps = (r_b.near(), r_a.along_far(), all_ffn.far())
    input_grad = project_qkv_back(
        grads, full_qkv, after(first_grad, *steps), tiles, tiles, input_grad
    )
    meet(input_grad, r_b, r_a, all_ffn)
    middle = r_b.middle()
    r_a.flying = after(r_a.flying, middle)
    all_a = Replication(place, r_a.share())
    blocks = all_ffn.landed()
    w_out_grad, w_in_grad = order_feed_forward(
        place, [after(blocks[0], all_a.blocks[0]), *blocks[1:]], share_in.shape[0]
    )
    meet(w_out_grad, r_b, all_a)
    share_b = r_b.share_direct()
    all_a.far()
    all_b = Replication(place, share_b, direct=True)
    w_attn_grad, w_qkv_grad, small = order_attention(
        place, all_a.landed(), all_b.landed(), w_attn_out.shape[0]
    )
    small = [small[8 * (n // 3) + n % 3] for n in range(12)]
    return (
        layer_out[None],
        input_grad[None],
        w_qkv_grad,
        small[B_QUERY],
        small[B_VALUE],
        w_attn_grad,
        small[B_ATTN],
        small[GAIN_ONE],
        small[SHIFT_ONE],
        w_in_grad,
        jnp.concatenate(small[B_IN:]),
        w_out_grad,
        small[B_OUT],
        small[GAIN_TWO],
        small[SHIFT_TWO],
    )


def solution(mesh):
    groups, shards = mesh.shape["grp"], mesh.shape["shard"]
    if groups == 4 and shards == 8:
        body = functools.partial(on_device_permutes, groups=groups, shards=shards)
    else:
        body = on_device
    return jax.shard_map(
        body,
        mesh=mesh,
        in_specs=(
            P(("grp", "shard"), None, None),
            P(("grp", "shard"), None),
            P(("grp", "shard"), None),
            P(("grp", "shard"), None, None),
            P("shard", "grp"),
            P("shard"),
            P("shard"),
            P("shard", "grp"),
            P("shard"),
            P("shard"),
            P("shard"),
            P("shard", "grp"),
            P("shard"),
            P("shard", "grp"),
            P("shard"),
            P("shard"),
            P("shard"),
        ),
        out_specs=(
            P(("grp", "shard"), None, None),
            P(("grp", "shard"), None, None),
            P("shard", None),
            P("shard"),
            P("shard"),
            P("shard", None),
            P("shard"),
            P("shard"),
            P("shard"),
            P("shard", None),
            P("shard"),
            P("shard", None),
            P("shard"),
            P("shard"),
            P("shard"),
        ),
        check_vma=False,
    )
```

```python
import functools
import math

import jax
import jax.numpy as jnp
from jax import lax
from jax.experimental import pallas as pl
from jax.experimental.pallas import tpu as pltpu
from jax.sharding import PartitionSpec as P

H = 16
HD = 64


masked_score = -1e30
epsilon = 1e-05


def norm_layer(rows, gain_row, shift_row):
    row_mean = jnp.mean(rows, -1, keepdims=True)
    centered = rows - row_mean
    row_var = jnp.mean(centered * centered, -1, keepdims=True)
    return centered * lax.rsqrt(row_var + epsilon) * gain_row + shift_row


def gelu_exact(values):
    return 0.5 * values * (1.0 + lax.erf(values * (1.0 / math.sqrt(2.0))))


def contract_rows(left, right):
    return lax.dot_general(
        left, right, (((0,), (0,)), ((), ())), preferred_element_type=jnp.float32
    )


def contract_cols(left, right):
    return lax.dot_general(
        left, right, (((1,), (1,)), ((), ())), preferred_element_type=jnp.float32
    )


def attend_forward(queries, key_rows, value_rows, segment_row, block_rows):
    length, model_width = queries.shape
    scaling = 1.0 / math.sqrt(HD)
    key_heads = key_rows.reshape(length, H, HD)
    value_heads = value_rows.reshape(length, H, HD)
    query_blocks = queries.reshape(length // block_rows, block_rows, H, HD)
    segment_blocks = segment_row.reshape(length // block_rows, block_rows)

    def one_block(pieces):
        query_part, segment_part = pieces
        scores = (
            jnp.einsum("qhd,khd->hqk", query_part, key_heads, preferred_element_type=jnp.float32)
            * scaling
        )
        allowed = segment_part[:, None] == segment_row[None, :]
        scores = jnp.where(allowed[None], scores, masked_score)
        row_max = jnp.max(scores, -1, keepdims=True)
        powers = jnp.exp(scores - row_max)
        totals = jnp.sum(powers, -1, keepdims=True)
        attn_probs = (powers / totals).astype(jnp.bfloat16)
        context = jnp.einsum(
            "hqk,khd->qhd", attn_probs, value_heads, preferred_element_type=jnp.float32
        )
        return (
            context.reshape(block_rows, model_width).astype(jnp.bfloat16),
            (row_max + jnp.log(totals))[:, :, 0],
        )

    contexts, log_sums = lax.map(one_block, (query_blocks, segment_blocks))
    return (contexts.reshape(length, model_width), log_sums)


def attend_backward(queries, key_rows, value_rows, segment_row, log_sums, context_grad, block_rows):
    length, model_width = queries.shape
    scaling = 1.0 / math.sqrt(HD)
    key_heads = key_rows.reshape(length, H, HD)
    value_heads = value_rows.reshape(length, H, HD)
    query_blocks = queries.reshape(length // block_rows, block_rows, H, HD)
    segment_blocks = segment_row.reshape(length // block_rows, block_rows)
    grad_blocks = context_grad.reshape(length // block_rows, block_rows, H, HD)

    def one_block(running, pieces):
        key_acc, value_acc = running
        query_part, segment_part, lse_part, grad_part = pieces
        scores = (
            jnp.einsum("qhd,khd->hqk", query_part, key_heads, preferred_element_type=jnp.float32)
            * scaling
        )
        allowed = segment_part[:, None] == segment_row[None, :]
        scores = jnp.where(allowed[None], scores, masked_score)
        probs = jnp.exp(scores - lse_part[:, :, None])
        prob_low = probs.astype(jnp.bfloat16)
        prob_grad = jnp.einsum(
            "qhd,khd->hqk", grad_part, value_heads, preferred_element_type=jnp.float32
        )
        row_dot = jnp.sum(prob_grad * probs, -1, keepdims=True)
        score_grad = (probs * (prob_grad - row_dot)).astype(jnp.bfloat16)
        query_grad = (
            jnp.einsum("hqk,khd->qhd", score_grad, key_heads, preferred_element_type=jnp.float32)
            * scaling
        )
        key_acc = (
            key_acc
            + jnp.einsum("hqk,qhd->khd", score_grad, query_part, preferred_element_type=jnp.float32)
            * scaling
        )
        value_acc = value_acc + jnp.einsum(
            "hqk,qhd->khd", prob_low, grad_part, preferred_element_type=jnp.float32
        )
        return ((key_acc, value_acc), query_grad.reshape(block_rows, model_width))

    empty_acc = jnp.zeros((length, H, HD), jnp.float32)
    (key_grad, value_grad), query_grads = lax.scan(
        one_block, (empty_acc, empty_acc), (query_blocks, segment_blocks, log_sums, grad_blocks)
    )
    return (
        query_grads.reshape(length, model_width),
        key_grad.reshape(length, model_width),
        value_grad.reshape(length, model_width),
    )


def on_device(
    tokens,
    segment_ids,
    keep_flag,
    cotangent,
    w_qkv,
    b_query,
    b_value,
    w_attn_out,
    b_attn_out,
    norm1_gain,
    norm1_bias,
    w_in,
    b_in,
    w_out,
    b_out,
    norm2_gain,
    norm2_bias,
):
    seq_count, length, model_width = tokens.shape
    block_rows = min(512, length)
    within = (
        lax.all_gather(w_qkv, "shard", axis=0, tiled=True),
        lax.all_gather(w_attn_out, "shard", axis=0, tiled=True),
        lax.all_gather(w_in, "shard", axis=0, tiled=True),
        lax.all_gather(w_out, "shard", axis=0, tiled=True),
        lax.all_gather(b_query, "shard", axis=0, tiled=True),
        lax.all_gather(b_value, "shard", axis=0, tiled=True),
        lax.all_gather(b_attn_out, "shard", axis=0, tiled=True),
        lax.all_gather(norm1_gain, "shard", axis=0, tiled=True),
        lax.all_gather(norm1_bias, "shard", axis=0, tiled=True),
        lax.all_gather(b_in, "shard", axis=0, tiled=True),
        lax.all_gather(b_out, "shard", axis=0, tiled=True),
        lax.all_gather(norm2_gain, "shard", axis=0, tiled=True),
        lax.all_gather(norm2_bias, "shard", axis=0, tiled=True),
    )
    full_qkv, full_attn, full_in, full_out = (
        lax.all_gather(within[0], "grp", axis=1, tiled=True),
        lax.all_gather(within[1], "grp", axis=1, tiled=True),
        lax.all_gather(within[2], "grp", axis=1, tiled=True),
        lax.all_gather(within[3], "grp", axis=1, tiled=True),
    )
    (
        bias_query,
        bias_value,
        bias_attn,
        gain_one,
        shift_one,
        bias_in,
        bias_out,
        gain_two,
        shift_two,
    ) = [piece.astype(jnp.float32) for piece in within[4:]]
    flat_rows = tokens.reshape(seq_count * length, model_width)
    mixed_qkv = jnp.dot(flat_rows, full_qkv, preferred_element_type=jnp.float32)
    queries = (mixed_qkv[:, :model_width] + bias_query).astype(jnp.bfloat16)
    key_rows = mixed_qkv[:, model_width : 2 * model_width].astype(jnp.bfloat16)
    value_rows = (mixed_qkv[:, 2 * model_width :] + bias_value).astype(jnp.bfloat16)
    query_seqs = queries.reshape(seq_count, length, model_width)
    key_seqs = key_rows.reshape(seq_count, length, model_width)
    value_seqs = value_rows.reshape(seq_count, length, model_width)

    def forward_sequence(pieces):
        return attend_forward(pieces[0], pieces[1], pieces[2], pieces[3], block_rows)

    contexts, log_sums = lax.map(forward_sequence, (query_seqs, key_seqs, value_seqs, segment_ids))
    contexts = contexts.reshape(seq_count * length, model_width)
    attended = jnp.dot(contexts, full_attn, preferred_element_type=jnp.float32) + bias_attn
    first_sum = flat_rows.astype(jnp.float32) + attended
    normed_one, norm_one_back = jax.vjp(norm_layer, first_sum, gain_one, shift_one)
    normed_low = normed_one.astype(jnp.bfloat16)
    hidden_pre = jnp.dot(normed_low, full_in, preferred_element_type=jnp.float32) + bias_in
    hidden, gelu_back = jax.vjp(gelu_exact, hidden_pre)
    hidden_low = hidden.astype(jnp.bfloat16)
    second_sum = normed_one + (
        jnp.dot(hidden_low, full_out, preferred_element_type=jnp.float32) + bias_out
    )
    result, norm_two_back = jax.vjp(norm_layer, second_sum, gain_two, shift_two)
    layer_out = result.astype(jnp.bfloat16).reshape(seq_count, length, model_width)
    again = (
        lax.all_gather(w_qkv, "shard", axis=0, tiled=True),
        lax.all_gather(w_attn_out, "shard", axis=0, tiled=True),
        lax.all_gather(w_in, "shard", axis=0, tiled=True),
        lax.all_gather(w_out, "shard", axis=0, tiled=True),
    )
    back_qkv, back_attn, back_in, back_out = (
        lax.all_gather(again[0], "grp", axis=1, tiled=True),
        lax.all_gather(again[1], "grp", axis=1, tiled=True),
        lax.all_gather(again[2], "grp", axis=1, tiled=True),
        lax.all_gather(again[3], "grp", axis=1, tiled=True),
    )
    masked_cot = cotangent.astype(jnp.float32).reshape(
        seq_count * length, model_width
    ) * keep_flag.reshape(seq_count * length, 1).astype(jnp.float32)
    second_grad, gain_two_grad, shift_two_grad = norm_two_back(masked_cot)
    bias_out_grad = jnp.sum(second_grad, 0)
    out_low = second_grad.astype(jnp.bfloat16)
    w_out_grad = contract_rows(hidden_low, out_low)
    hidden_grad = contract_cols(out_low, back_out)
    (pre_grad,) = gelu_back(hidden_grad)
    bias_in_grad = jnp.sum(pre_grad, 0)
    pre_low = pre_grad.astype(jnp.bfloat16)
    w_in_grad = contract_rows(normed_low, pre_low)
    normed_grad = second_grad + contract_cols(pre_low, back_in)
    first_grad, gain_one_grad, shift_one_grad = norm_one_back(normed_grad)
    bias_attn_grad = jnp.sum(first_grad, 0)
    attn_low = first_grad.astype(jnp.bfloat16)
    w_attn_grad = contract_rows(contexts, attn_low)
    context_grad = contract_cols(attn_low, back_attn).astype(jnp.bfloat16)

    def backward_sequence(pieces):
        return attend_backward(
            pieces[0], pieces[1], pieces[2], pieces[3], pieces[4], pieces[5], block_rows
        )

    query_grad, key_grad, value_grad = lax.map(
        backward_sequence,
        (
            query_seqs,
            key_seqs,
            value_seqs,
            segment_ids,
            log_sums,
            context_grad.reshape(seq_count, length, model_width),
        ),
    )
    query_grad = query_grad.reshape(seq_count * length, model_width)
    key_grad = key_grad.reshape(seq_count * length, model_width)
    value_grad = value_grad.reshape(seq_count * length, model_width)
    bias_query_grad = jnp.sum(query_grad, 0)
    bias_value_grad = jnp.sum(value_grad, 0)
    qkv_low = jnp.concatenate([query_grad, key_grad, value_grad], 1).astype(jnp.bfloat16)
    w_qkv_grad = contract_rows(flat_rows, qkv_low)
    input_grad = first_grad + contract_cols(qkv_low, back_qkv)
    reduced = (
        lax.psum_scatter(
            w_qkv_grad.astype(jnp.bfloat16), "shard", scatter_dimension=0, tiled=True
        ).astype(jnp.float32),
        lax.psum_scatter(
            bias_query_grad.astype(jnp.bfloat16), "shard", scatter_dimension=0, tiled=True
        ).astype(jnp.float32),
        lax.psum_scatter(
            bias_value_grad.astype(jnp.bfloat16), "shard", scatter_dimension=0, tiled=True
        ).astype(jnp.float32),
        lax.psum_scatter(
            w_attn_grad.astype(jnp.bfloat16), "shard", scatter_dimension=0, tiled=True
        ).astype(jnp.float32),
        lax.psum_scatter(
            bias_attn_grad.astype(jnp.bfloat16), "shard", scatter_dimension=0, tiled=True
        ).astype(jnp.float32),
        lax.psum_scatter(
            gain_one_grad.astype(jnp.bfloat16), "shard", scatter_dimension=0, tiled=True
        ).astype(jnp.float32),
        lax.psum_scatter(
            shift_one_grad.astype(jnp.bfloat16), "shard", scatter_dimension=0, tiled=True
        ).astype(jnp.float32),
        lax.psum_scatter(
            w_in_grad.astype(jnp.bfloat16), "shard", scatter_dimension=0, tiled=True
        ).astype(jnp.float32),
        lax.psum_scatter(
            bias_in_grad.astype(jnp.bfloat16), "shard", scatter_dimension=0, tiled=True
        ).astype(jnp.float32),
        lax.psum_scatter(
            w_out_grad.astype(jnp.bfloat16), "shard", scatter_dimension=0, tiled=True
        ).astype(jnp.float32),
        lax.psum_scatter(
            bias_out_grad.astype(jnp.bfloat16), "shard", scatter_dimension=0, tiled=True
        ).astype(jnp.float32),
        lax.psum_scatter(
            gain_two_grad.astype(jnp.bfloat16), "shard", scatter_dimension=0, tiled=True
        ).astype(jnp.float32),
        lax.psum_scatter(
            shift_two_grad.astype(jnp.bfloat16), "shard", scatter_dimension=0, tiled=True
        ).astype(jnp.float32),
    )
    summed = (
        lax.psum(reduced[0].astype(jnp.bfloat16), "grp").astype(jnp.float32),
        lax.psum(reduced[1].astype(jnp.bfloat16), "grp").astype(jnp.float32),
        lax.psum(reduced[2].astype(jnp.bfloat16), "grp").astype(jnp.float32),
        lax.psum(reduced[3].astype(jnp.bfloat16), "grp").astype(jnp.float32),
        lax.psum(reduced[4].astype(jnp.bfloat16), "grp").astype(jnp.float32),
        lax.psum(reduced[5].astype(jnp.bfloat16), "grp").astype(jnp.float32),
        lax.psum(reduced[6].astype(jnp.bfloat16), "grp").astype(jnp.float32),
        lax.psum(reduced[7].astype(jnp.bfloat16), "grp").astype(jnp.float32),
        lax.psum(reduced[8].astype(jnp.bfloat16), "grp").astype(jnp.float32),
        lax.psum(reduced[9].astype(jnp.bfloat16), "grp").astype(jnp.float32),
        lax.psum(reduced[10].astype(jnp.bfloat16), "grp").astype(jnp.float32),
        lax.psum(reduced[11].astype(jnp.bfloat16), "grp").astype(jnp.float32),
        lax.psum(reduced[12].astype(jnp.bfloat16), "grp").astype(jnp.float32),
    )
    return (
        layer_out,
        input_grad.reshape(seq_count, length, model_width),
        summed[0],
        summed[1],
        summed[2],
        summed[3],
        summed[4],
        summed[5],
        summed[6],
        summed[7],
        summed[8],
        summed[9],
        summed[10],
        summed[11],
        summed[12],
    )


NT = (((1,), (1,)), ((), ()))
NN = (((1,), (0,)), ((), ()))
TN = (((0,), (0,)), ((), ()))
LANES = 128
AXES = ("grp", "shard")


def mxu(left, right, dims):
    return lax.dot_general(left, right, dims, preferred_element_type=jnp.float32)


def cost(flops):
    return pl.CostEstimate(flops=2 * flops, bytes_accessed=0, transcendentals=0)


def params(megabytes=60):
    return pltpu.CompilerParams(vmem_limit_bytes=megabytes << 20)


def attention_forward_kernel(q_ref, k_ref, v_ref, seg_col, seg_row, out_ref, lse_ref, *, rows):
    length = q_ref.shape[0]
    first = lax.broadcasted_iota(jnp.int32, (1, LANES), 1) < HD
    keys = k_ref[...]
    values = v_ref[...]
    zero = jnp.zeros_like(keys)
    head_keys = (jnp.where(first, keys, zero), jnp.where(first, zero, keys))
    key_segments = seg_col[...]
    for block in range(length // rows):
        here = pl.ds(block * rows, rows)
        q = q_ref[here, :]
        allowed = key_segments == seg_row[:, here]
        outs = []
        for head in range(2):
            scores = mxu(head_keys[head], q, NT)
            scores = jnp.where(allowed, scores, masked_score)
            top = jnp.max(scores, 0, keepdims=True)
            powers = jnp.exp(scores - top)
            total = jnp.sum(powers, 0, keepdims=True)
            part = mxu(powers.astype(jnp.bfloat16), values, TN)
            outs.append(part * jnp.transpose(jnp.broadcast_to(1.0 / total, (LANES, rows))))
            lse_ref[0, head : head + 1, here] = top + jnp.log(total)
        out_ref[here, :] = jnp.where(first, outs[0], outs[1]).astype(jnp.bfloat16)


def attention_forward(qkv, seg_col, seg_row, start, pairs, before=None):
    length, width = qkv.shape[0], qkv.shape[1] // 3
    total = width // LANES
    rows = min(512, length)
    anywhere = pl.BlockSpec(memory_space=pl.ANY)

    def pair(part):
        return pl.BlockSpec((length, LANES), lambda j: (0, part * total + start + j))

    def body(q_ref, k_ref, v_ref, seg_c, seg_r, *refs):
        attention_forward_kernel(q_ref, k_ref, v_ref, seg_c, seg_r, *refs[-2:], rows=rows)

    return pl.pallas_call(
        body,
        grid=(pairs,),
        in_specs=[
            pair(0),
            pair(1),
            pair(2),
            pl.BlockSpec((length, 1), lambda j: (0, 0)),
            pl.BlockSpec((1, length), lambda j: (0, 0)),
        ]
        + [anywhere] * (0 if before is None else 2),
        out_specs=[
            pl.BlockSpec((length, LANES), lambda j: (0, start + j)),
            pl.BlockSpec((1, 2, length), lambda j: (start + j, 0, 0)),
        ],
        out_shape=[
            jax.ShapeDtypeStruct((length, width), jnp.bfloat16),
            jax.ShapeDtypeStruct((total, 2, length), jnp.float32),
        ],
        input_output_aliases={} if before is None else {5: 0, 6: 1},
        compiler_params=params(60),
        cost_estimate=cost(16 * length * length * pairs * LANES),
        name="attn_fwd",
    )(qkv, qkv, qkv, seg_col, seg_row, *(() if before is None else before))


def attention_backward_kernel(
    q_ref, k_ref, v_ref, o_ref, do_ref, seg_col, seg_row, lse_ref, grad_ref, sum_ref, *, rows
):
    length = q_ref.shape[0]
    lane = lax.broadcasted_iota(jnp.int32, (1, LANES), 1)
    first = lane < HD
    pick = (
        lax.broadcasted_iota(jnp.int32, (8, LANES), 0)
        == lax.broadcasted_iota(jnp.int32, (8, LANES), 1) // HD
    ).astype(jnp.float32)
    keys = k_ref[...]
    values = v_ref[...]
    zero = jnp.zeros_like(keys)
    head_keys = (jnp.where(first, keys, zero), jnp.where(first, zero, keys))
    head_values = (jnp.where(first, values, zero), jnp.where(first, zero, values))
    key_segments = seg_col[...]
    key_sum = [None, None]
    value_sum = [None, None]
    query_total = jnp.zeros((1, LANES), jnp.float32)
    for block in range(length // rows):
        here = pl.ds(block * rows, rows)
        q = q_ref[here, :]
        do = do_ref[here, :]
        allowed = key_segments == seg_row[:, here]
        dots = lax.dot_general(
            pick,
            do.astype(jnp.float32) * o_ref[here, :].astype(jnp.float32),
            NT,
            precision=lax.Precision.HIGHEST,
            preferred_element_type=jnp.float32,
        )
        parts = []
        for head in range(2):
            scores = mxu(head_keys[head], q, NT)
            scores = jnp.where(allowed, scores, masked_score)
            probs = jnp.exp(scores - lse_ref[0, head : head + 1, here])
            prob_grad = mxu(head_values[head], do, NT)
            score_grad = (probs * (prob_grad - dots[head : head + 1, :])).astype(jnp.bfloat16)
            value_part = mxu(probs.astype(jnp.bfloat16), do, NN)
            key_part = mxu(score_grad, q, NN)
            value_sum[head] = value_part if block == 0 else value_sum[head] + value_part
            key_sum[head] = key_part if block == 0 else key_sum[head] + key_part
            parts.append(mxu(score_grad, keys, TN))
        query_grad = jnp.where(first, parts[0], parts[1]) * (1.0 / math.sqrt(HD))
        query_total = query_total + jnp.sum(query_grad, 0, keepdims=True)
        grad_ref[0, here, :] = query_grad.astype(jnp.bfloat16)
    grad_ref[1, :, :] = jnp.where(first, key_sum[0], key_sum[1]).astype(jnp.bfloat16)
    value_grad = jnp.where(first, value_sum[0], value_sum[1])
    grad_ref[2, :, :] = value_grad.astype(jnp.bfloat16)
    sum_ref[0:1, :] = query_total
    sum_ref[1:2, :] = jnp.sum(value_grad, 0, keepdims=True)


def attention_backward(qkv, out, out_grad, seg_col, seg_row, lse, start, pairs, at, size, before=None):
    length, width = out.shape
    total = width // LANES
    rows = min(256, length)
    more = () if before is None else before

    def pair(part):
        return pl.BlockSpec((length, LANES), lambda j: (0, part * total + start + j))

    def body(*refs):
        attention_backward_kernel(*refs[:8], *refs[-2:], rows=rows)

    return pl.pallas_call(
        body,
        grid=(pairs,),
        in_specs=[
            pair(0),
            pair(1),
            pair(2),
            pair(0),
            pair(0),
            pl.BlockSpec((length, 1), lambda j: (0, 0)),
            pl.BlockSpec((1, length), lambda j: (0, 0)),
            pl.BlockSpec((1, 2, length), lambda j: (j + start, 0, 0)),
        ]
        + [pl.BlockSpec(memory_space=pl.ANY)] * len(more),
        out_specs=[
            pl.BlockSpec((3, length, LANES), lambda j: (0, 0, j + at)),
            pl.BlockSpec((2, LANES), lambda j: (0, j + at)),
        ],
        out_shape=[
            jax.ShapeDtypeStruct((3, length, size * LANES), jnp.bfloat16),
            jax.ShapeDtypeStruct((2, size * LANES), jnp.float32),
        ],
        input_output_aliases={} if before is None else {8: 0, 9: 1},
        compiler_params=params(60),
        cost_estimate=cost(40 * length * length * pairs * LANES),
        name="attn_bwd",
    )(qkv, qkv, qkv, out, out_grad, seg_col, seg_row, lse, *more)


class Place:
    def __init__(self, groups, shards):
        self.groups = groups
        self.shards = shards
        self.chips = shards // 2
        self.grp = lax.axis_index("grp")
        self.shard = lax.axis_index("shard")
        self.core = self.shard % 2
        self.chip = self.shard // 2
        self.scalars = jnp.stack([self.core, self.chip, self.grp]).astype(jnp.int32)

    def permute(self, array, mask_of_core):
        pairs = [(i, i ^ mask_of_core[i % 2]) for i in range(self.groups * self.shards)]
        return lax.ppermute(array, AXES, pairs)

    def swap_core(self, array):
        return self.permute(array, (1, 1))

    def swap_grp(self, array, step):
        masks = (self.shards, 2 * self.shards)
        return self.permute(array, masks if step == 0 else masks[::-1])

    def swap_chip(self, array, step):
        masks = (2, 4)
        return self.permute(array, masks if step == 0 else masks[::-1])

    def slot_chip(self, slot):
        return self.chip ^ turn(slot, self.core)

    def slot_grp(self, slot):
        return self.grp ^ turn(slot, self.core)


def turn(slot, core):
    if isinstance(slot, int):
        return slot if slot in (0, 3) else jnp.where(core == 0, slot, 3 - slot)
    return jnp.where((core == 0) | (slot == 0) | (slot == 3), slot, 3 - slot)


def after(value, *others):
    return lax.optimization_barrier((value, *others))[0]


def meet(anchor, *flights):
    arrays = [f.flying for f in flights]
    _, *arrays = lax.optimization_barrier((anchor, *arrays))
    for f, array in zip(flights, arrays):
        f.flying = array


class Gather:
    def __init__(self, place, piece):
        self.place = place
        self.piece = piece
        self.held = [None] * 4
        self.crossed = [None] * 4

    def chips_near(self, *wait):
        self.piece = after(self.piece, *wait)
        self.flying = self.place.swap_chip(self.piece, 0)

    def chips_far(self):
        self.pair = jnp.stack([self.piece, self.flying])
        self.flying = self.place.swap_chip(self.pair, 1)
        return self.pair

    def join(self):
        self.held[0] = jnp.concatenate([self.pair, self.flying])
        return self.held[0]

    def near(self, *wait):
        self.held[0] = after(self.held[0], *wait)
        self.flying = (self.place.swap_grp(self.held[0], 0), self.place.swap_grp(self.held[0], 1))
        return self.held[0]

    def far(self, *wait):
        self.held[1:3] = self.flying
        first = after(self.held[1], *wait)
        self.flying = self.place.swap_grp(first, 1)

    def landed(self):
        self.held[3] = self.flying

    def cross(self, *which, wait=()):
        for n in which:
            self.crossed[n] = self.place.swap_core(after(self.held[n], *wait))

    def pieces(self):
        return self.held + self.crossed


class Window:
    def __init__(self, gather, start, cols):
        self.arrays = gather.pieces()
        self.start, self.cols = start, cols
        chips, rows, _ = self.arrays[0].shape
        self.chips, self.rows = chips, rows


def fetch(where, window, refs, whole, sem):
    rows, cols, chips = window.rows, window.cols, window.chips
    for slot in range(4):
        for side in range(2):
            core = where[0] ^ side
            ref = refs[4 * side + slot]
            distance = turn(slot, core)
            col = pl.multiple_of((where[2] ^ distance) * cols, LANES)
            for k in range(chips):
                row = ((where[1] ^ turn(k, core)) * 2 + core) * rows
                pltpu.make_async_copy(
                    ref.at[k, :, pl.ds(window.start, cols)],
                    whole.at[pl.ds(pl.multiple_of(row, rows), rows), pl.ds(col, cols)],
                    sem.at[distance],
                ).start()


def weight_call(place, kernel, window, inputs, in_specs, outs, out_specs, steps, tiled, name, flops):
    cols, groups = window.cols, place.groups
    pieces = window.arrays
    shape = (window.chips * 2 * window.rows, groups * cols)
    anywhere = pl.BlockSpec(memory_space=pl.ANY)

    def body(where, *refs):
        taken, refs = refs[: len(pieces)], refs[len(pieces) :]
        *refs, written, weight, acc, sem, out_sem = refs
        step = pl.program_id(0)

        @pl.when(step == 0)
        def _():
            fetch(where, window, taken, weight, sem)

        def arrive(slot):
            at = pl.ds(pl.multiple_of((where[2] ^ slot) * cols, LANES), cols)
            view = weight.at[:, at]
            pltpu.make_async_copy(view, view, sem.at[slot]).wait()
            pltpu.make_async_copy(view, written.at[:, at], out_sem.at[slot]).start()
            return at

        def multiply(left):
            @pl.when(step == 0)
            def _():
                for slot in range(groups):
                    at = arrive(slot)
                    acc[:, at] = mxu(left[...], weight[:, at], NN)

            @pl.when(step > 0)
            def _():
                acc[...] = mxu(left[...], weight[...], NN)

            return acc[...]

        if tiled:
            kernel(multiply, *refs)
        else:
            kernel(arrive(step), weight, *refs)

        @pl.when(step == steps - 1)
        def _():
            for slot in range(groups):
                view = weight.at[:, pl.ds(slot * cols, cols)]
                pltpu.make_async_copy(view, view, out_sem.at[slot]).wait()

    return pl.pallas_call(
        body,
        grid_spec=pltpu.PrefetchScalarGridSpec(
            num_scalar_prefetch=1,
            grid=(steps,),
            in_specs=[anywhere] * len(pieces) + in_specs,
            out_specs=out_specs + [anywhere],
            scratch_shapes=[
                pltpu.VMEM(shape, jnp.bfloat16),
                pltpu.VMEM((TILE, shape[1]) if tiled else (8, LANES), jnp.float32),
                pltpu.SemaphoreType.DMA((groups,)),
                pltpu.SemaphoreType.DMA((groups,)),
            ],
        ),
        out_shape=outs + [shaped(shape, jnp.bfloat16)],
        compiler_params=params(60),
        cost_estimate=cost(flops),
        name=name,
    )(place.scalars, *pieces, *inputs)


CHUNKS = 4


def fetch_rows(weight, whole, sem):
    @pl.when(pl.program_id(0) == 0)
    def _():
        size = weight.shape[0] // CHUNKS
        for n in range(CHUNKS):
            here = pl.ds(n * size, size)
            pltpu.make_async_copy(weight.at[here, :], whole.at[here, :], sem.at[n]).start()


def multiply_rows(product, whole, acc, sem):
    @pl.when(pl.program_id(0) == 0)
    def _():
        size = whole.shape[0] // CHUNKS
        for n in range(CHUNKS):
            here = pl.ds(n * size, size)
            view = whole.at[here, :]
            pltpu.make_async_copy(view, view, sem.at[n]).wait()
            acc[:, here] = product(here)

    @pl.when(pl.program_id(0) > 0)
    def _():
        acc[...] = product(slice(None))

    return acc[...]


def fetch_scratch(weight):
    return [
        pltpu.VMEM(weight.shape, jnp.bfloat16),
        pltpu.VMEM((TILE, weight.shape[0]), jnp.float32),
        pltpu.SemaphoreType.DMA((CHUNKS,)),
    ]


def plain_call(kernel, inputs, in_specs, outs, out_specs, steps, name, flops, scratch=()):
    return pl.pallas_call(
        kernel,
        grid=(steps,),
        in_specs=in_specs,
        out_specs=out_specs,
        out_shape=outs,
        scratch_shapes=list(scratch),
        compiler_params=params(60),
        cost_estimate=cost(flops),
        name=name,
    )(*inputs)


TILE = 256


def row_tiles(width):
    return pl.BlockSpec((TILE, width), lambda i, *s: (i, 0))


def fixed(*shape):
    return pl.BlockSpec(shape, lambda i, *s: (0,) * len(shape))


def shaped(shape, dtype):
    return jax.ShapeDtypeStruct(shape, dtype)


B_QUERY, B_VALUE, B_ATTN, GAIN_ONE, SHIFT_ONE, B_OUT, GAIN_TWO, SHIFT_TWO, B_IN = range(9)


def row(ref, n):
    return ref[n : n + 1, :]


class Vectors:
    def __init__(self, place, vectors):
        lines = [v.reshape(-1, LANES) for v in vectors]
        blank = jnp.zeros((-sum(x.shape[0] for x in lines) % 16, LANES), jnp.bfloat16)
        self.own = jnp.concatenate([*lines, blank])
        self.place = place
        self.flying = place.swap_core(self.own)

    def chips_near(self):
        self.own = jnp.stack([self.own, self.flying])
        self.flying = self.place.swap_chip(self.own, 0)

    def chips_far(self):
        self.own = jnp.stack([self.own, self.flying])
        self.flying = self.place.swap_chip(self.own, 1)

    def landed(self):
        self.slots = jnp.concatenate([self.own, self.flying])

    def unpack(self):
        place = self.place
        slots, sides, rows, lanes = self.slots.shape
        shards = place.shards

        def kernel(where, in_ref, rows_ref, inner_ref, qkv_ref):
            width = shards * lanes
            qkv_ref[...] = jnp.zeros_like(qkv_ref)
            for slot in range(slots):
                for side in range(sides):
                    core = where[0] ^ side
                    shard = (where[1] ^ turn(slot, where[0])) * 2 + core
                    part = in_ref[slot, side].astype(jnp.float32)
                    at = pl.multiple_of(shard * lanes, lanes)
                    rows_ref[:, pl.ds(at, lanes)] = part
                    qkv_ref[:, pl.ds(at, lanes)] = part[B_QUERY : B_QUERY + 1]
                    qkv_ref[:, pl.ds(2 * width + at, lanes)] = part[B_VALUE : B_VALUE + 1]
                    for n in range(4):
                        start = pl.multiple_of((shard * 4 + n) * lanes, lanes)
                        inner_ref[:, pl.ds(start, lanes)] = part[B_IN + n : B_IN + n + 1]

        in_vmem = pl.BlockSpec(memory_space=pltpu.VMEM)
        return pl.pallas_call(
            kernel,
            in_specs=[pl.BlockSpec(memory_space=pltpu.SMEM), in_vmem],
            out_specs=[in_vmem] * 3,
            out_shape=[
                shaped((rows, shards * lanes), jnp.float32),
                shaped((1, 4 * shards * lanes), jnp.float32),
                shaped((1, 3 * shards * lanes), jnp.float32),
            ],
            name="vectors",
        )(place.scalars, self.slots)


def pack_sums(late_a, late_b, first_sums, second_sums, inner_sums):
    width = first_sums.shape[1]
    half = late_a.shape[1]

    def kernel(a_ref, b_ref, one_ref, two_ref, inner_ref, out_ref):
        def place_of(n):
            return n // 3 * 8 + n % 3

        out_ref[...] = jnp.zeros_like(out_ref)
        for n in (B_QUERY, B_VALUE):
            at = place_of(n)
            out_ref[at : at + 1, 0:half] = a_ref[n : n + 1, :]
            out_ref[at : at + 1, half:width] = b_ref[n : n + 1, :]
        for n, source, line in (
            (GAIN_ONE, one_ref, 0),
            (SHIFT_ONE, one_ref, 1),
            (B_ATTN, one_ref, 2),
            (GAIN_TWO, two_ref, 0),
            (SHIFT_TWO, two_ref, 1),
            (B_OUT, two_ref, 2),
        ):
            at = place_of(n)
            out_ref[at : at + 1, :] = source[line : line + 1, :]
        for n in range(4):
            at = place_of(B_IN + n)
            for shard in range(width // LANES):
                start = (4 * shard + n) * LANES
                out_ref[at : at + 1, shard * LANES : (shard + 1) * LANES] = inner_ref[
                    :, start : start + LANES
                ]

    in_vmem = pl.BlockSpec(memory_space=pltpu.VMEM)
    return pl.pallas_call(
        kernel,
        in_specs=[in_vmem] * 5,
        out_specs=in_vmem,
        out_shape=shaped((32, width), jnp.float32),
        name="pack_sums",
    )(late_a, late_b, first_sums, second_sums, inner_sums)


def project_qkv(place, rows, window, bias, scale):
    length, width = rows.shape
    cols = window.cols

    def kernel(at, weight, x_ref, bias_ref, scale_ref, out_ref):
        for tile in range(length // TILE):
            here = pl.ds(tile * TILE, TILE)
            mixed = mxu(x_ref[here, :], weight[:, at], NN) + bias_ref[:, at]
            mixed = mixed.astype(jnp.bfloat16).astype(jnp.float32) * scale_ref[:, at]
            out_ref[here, :] = mixed.astype(jnp.bfloat16)

    total = cols * place.groups
    return weight_call(
        place,
        kernel,
        window,
        (rows, bias, scale),
        [fixed(length, width), fixed(1, total), fixed(1, total)],
        [shaped((length, total), jnp.bfloat16)],
        [pl.BlockSpec((length, cols), lambda i, s: (0, i ^ s[2]))],
        place.groups,
        False,
        "qkv",
        2 * length * width * total,
    )


def norm_parts(rows):
    centered = rows - jnp.mean(rows, -1, keepdims=True)
    scale = lax.rsqrt(jnp.mean(centered * centered, -1, keepdims=True) + epsilon)
    return centered * scale, scale


def norm_back(grad, normed, scale):
    return scale * (
        grad
        - jnp.mean(grad, -1, keepdims=True)
        - normed * jnp.mean(grad * normed, -1, keepdims=True)
    )


def add_rows(sum_ref, *terms):
    @pl.when(pl.program_id(0) == 0)
    def _():
        sum_ref[...] = jnp.zeros_like(sum_ref)

    for n, term in enumerate(terms):
        sum_ref[n : n + 1, :] += jnp.sum(term, 0, keepdims=True)


def project_out(place, contexts, window, rows, vectors):
    length, width = rows.shape

    def kernel(multiply, c_ref, x_ref, v_ref, n_ref, r_ref, low_ref):
        first_sum = multiply(c_ref) + row(v_ref, B_ATTN)
        first_sum = first_sum + x_ref[...].astype(jnp.float32)
        normed, scale = norm_parts(first_sum)
        n_ref[...] = normed
        r_ref[...] = jnp.broadcast_to(scale, r_ref.shape)
        low_ref[...] = (normed * row(v_ref, GAIN_ONE) + row(v_ref, SHIFT_ONE)).astype(jnp.bfloat16)

    return weight_call(
        place,
        kernel,
        window,
        (contexts, rows, vectors),
        [row_tiles(width), row_tiles(width), fixed(*vectors.shape)],
        [
            shaped((length, width), jnp.float32),
            shaped((length, LANES), jnp.float32),
            shaped((length, width), jnp.bfloat16),
        ],
        [row_tiles(width), row_tiles(LANES), row_tiles(width)],
        length // TILE,
        True,
        "attn_out",
        2 * length * width * width,
    )


def feed_in(place, normed_low, window, bias):
    length, width = normed_low.shape
    cols = window.cols

    def kernel(at, weight, x_ref, bias_ref, hid_ref, slope_ref):
        for tile in range(length // TILE):
            here = pl.ds(tile * TILE, TILE)
            pre = mxu(x_ref[here, :], weight[:, at], NN) + bias_ref[:, at]
            share = 0.5 + 0.5 * lax.erf(pre * (1.0 / math.sqrt(2.0)))
            bell = jnp.exp(-0.5 * pre * pre) * (1.0 / math.sqrt(2.0 * math.pi))
            hid_ref[here, :] = (pre * share).astype(jnp.bfloat16)
            slope_ref[here, :] = (share + pre * bell).astype(jnp.bfloat16)

    total = cols * place.groups
    block = pl.BlockSpec((length, cols), lambda i, s: (0, i ^ s[2]))
    return weight_call(
        place,
        kernel,
        window,
        (normed_low, bias),
        [fixed(length, width), fixed(1, total)],
        [shaped((length, total), jnp.bfloat16)] * 2,
        [block, block],
        place.groups,
        False,
        "feed_in",
        2 * length * width * total,
    )


def feed_out(place, hidden, window, normed, cot, keep, vectors):
    length, inner = hidden.shape
    width = normed.shape[1]

    def kernel(multiply, h_ref, n_ref, cot_ref, keep_ref, v_ref, *outs):
        out_ref, grad_ref, low_ref, sum_ref = outs
        fed = multiply(h_ref)
        normed_one = n_ref[...] * row(v_ref, GAIN_ONE) + row(v_ref, SHIFT_ONE)
        second_sum = normed_one + (fed + row(v_ref, B_OUT))
        second, scale = norm_parts(second_sum)
        out_ref[...] = (second * row(v_ref, GAIN_TWO) + row(v_ref, SHIFT_TWO)).astype(jnp.bfloat16)
        masked = cot_ref[...].astype(jnp.float32) * keep_ref[...]
        grad = norm_back(masked * row(v_ref, GAIN_TWO), second, scale)
        grad_ref[...] = grad
        low_ref[...] = grad.astype(jnp.bfloat16)
        add_rows(sum_ref, masked * second, masked, grad)

    return weight_call(
        place,
        kernel,
        window,
        (hidden, normed, cot, keep, vectors),
        [row_tiles(inner), row_tiles(width), row_tiles(width), row_tiles(1), fixed(*vectors.shape)],
        [
            shaped((length, width), jnp.bfloat16),
            shaped((length, width), jnp.float32),
            shaped((length, width), jnp.bfloat16),
            shaped((8, width), jnp.float32),
        ],
        [row_tiles(width), row_tiles(width), row_tiles(width), fixed(8, width)],
        length // TILE,
        True,
        "feed_out",
        2 * length * width * inner,
    )


def feed_out_back(out_low, weight, slope):
    length, width = out_low.shape
    inner = slope.shape[1]
    cols = min(1024, inner)

    def kernel(g_ref, w_ref, slope_ref, pre_ref, sum_ref):
        total = jnp.zeros((1, cols), jnp.float32)
        for tile in range(length // TILE):
            here = pl.ds(tile * TILE, TILE)
            grad = mxu(g_ref[here, :], w_ref[...], NT) * slope_ref[here, :].astype(jnp.float32)
            pre_ref[here, :] = grad.astype(jnp.bfloat16)
            total = total + jnp.sum(grad, 0, keepdims=True)
        sum_ref[...] = total

    block = pl.BlockSpec((length, cols), lambda i: (0, i))
    return plain_call(
        kernel,
        (out_low, weight, slope),
        [fixed(length, width), pl.BlockSpec((cols, width), lambda i: (i, 0)), block],
        [shaped((length, inner), jnp.bfloat16), shaped((1, inner), jnp.float32)],
        [block, pl.BlockSpec((1, cols), lambda i: (0, i))],
        inner // cols,
        "feed_out_back",
        2 * length * width * inner,
    )


def feed_in_back(pre_low, weight, second_grad, normed, scale, vectors, attn_weight):
    length, inner = pre_low.shape
    width = normed.shape[1]

    def kernel(p_ref, w_ref, g_ref, n_ref, r_ref, v_ref, a_ref, *refs):
        first_ref, low_ref, ctx_ref, sum_ref, whole, acc, sem, attn_whole, attn_sem = refs
        fetch_rows(w_ref, whole, sem)
        attn_copy = pltpu.make_async_copy(a_ref, attn_whole, attn_sem)
        pl.when(pl.program_id(0) == 0)(attn_copy.start)
        grad = multiply_rows(lambda here: mxu(p_ref[...], whole[here, :], NT), whole, acc, sem)
        grad = g_ref[...] + grad
        first = norm_back(grad * row(v_ref, GAIN_ONE), n_ref[...], r_ref[:, :1])
        low = first.astype(jnp.bfloat16)
        first_ref[...] = first
        low_ref[...] = low
        pl.when(pl.program_id(0) == 0)(attn_copy.wait)
        ctx_ref[...] = mxu(low, attn_whole[...], NT).astype(jnp.bfloat16)
        add_rows(sum_ref, grad * n_ref[...], grad, first)

    return plain_call(
        kernel,
        (pre_low, weight, second_grad, normed, scale, vectors, attn_weight),
        [
            row_tiles(inner),
            pl.BlockSpec(memory_space=pl.ANY),
            row_tiles(width),
            row_tiles(width),
            row_tiles(LANES),
            fixed(*vectors.shape),
            pl.BlockSpec(memory_space=pl.ANY),
        ],
        [
            shaped((length, width), jnp.float32),
            shaped((length, width), jnp.bfloat16),
            shaped((length, width), jnp.bfloat16),
            shaped((8, width), jnp.float32),
        ],
        [row_tiles(width), row_tiles(width), row_tiles(width), fixed(8, width)],
        length // TILE,
        "feed_in_back",
        2 * length * width * (inner + width),
        fetch_scratch(weight)
        + [pltpu.VMEM(attn_weight.shape, jnp.bfloat16), pltpu.SemaphoreType.DMA],
    )


def project_qkv_back(grads, weight, first_grad, start, tiles, before=None):
    length, width = first_grad.shape
    part = width // len(grads)

    def kernel(w_ref, *refs):
        grad_refs, first_ref = refs[: len(grads)], refs[len(grads)]
        out_ref, whole, acc, sem = refs[-4:]
        fetch_rows(w_ref, whole, sem)

        def product(here):
            total = first_ref[:, here]
            for n in range(3):
                for m, grad_ref in enumerate(grad_refs):
                    at = n * width + m * part
                    total = total + mxu(grad_ref[n], whole[here, at : at + part], NT)
            return total

        out_ref[...] = multiply_rows(product, whole, acc, sem)

    tile = pl.BlockSpec((TILE, width), lambda i: (start + i, 0))
    more = () if before is None else (before,)
    return pl.pallas_call(
        kernel,
        grid=(tiles,),
        in_specs=[pl.BlockSpec(memory_space=pl.ANY)]
        + [pl.BlockSpec((3, TILE, part), lambda i: (0, start + i, 0))] * len(grads)
        + [tile]
        + [pl.BlockSpec(memory_space=pl.ANY)] * len(more),
        out_specs=tile,
        out_shape=shaped((length, width), jnp.float32),
        scratch_shapes=fetch_scratch(weight),
        input_output_aliases={} if before is None else {len(grads) + 2: 0},
        compiler_params=params(60),
        cost_estimate=cost(6 * tiles * TILE * width * width),
        name="qkv_back",
    )(weight, *grads, first_grad, *more)


ORDER = (1, 3, 0, 2)


def ordered_slot(j):
    return jnp.where(j < 2, 2 * j + 1, 2 * j - 4)


def weight_grad_kernel(where, left_ref, right_ref, own, sent, kept, *, rows, groups, split):
    core = where[0]
    chips = left_ref.shape[1] // (2 * rows)

    @pl.when(pl.program_id(1) == 0)
    def _():
        for side in range(2):
            chosen = []
            for k in range(chips):
                even = left_ref[:, 2 * k * rows : (2 * k + 1) * rows]
                odd = left_ref[:, (2 * k + 1) * rows : (2 * k + 2) * rows]
                chosen.append(jnp.where(core == side, even, odd))
            left = chosen[0] if chips == 1 else jnp.concatenate(chosen, 1)
            kept[side] = left.T

    if split:
        size = min(512, right_ref.shape[1])
        for ref, side in ((sent, 1), (own, 0)):
            for n in range(right_ref.shape[1] // size):
                at = slice(n * size, (n + 1) * size)
                part = mxu(kept[side], right_ref[:, at], NN).astype(jnp.bfloat16)
                ref[0, :, :, at] = part.reshape(chips, rows, size)
    else:
        cols = right_ref.shape[1] // groups
        for ref, side in ((sent, 1), (own, 0)):
            for pos, slot in enumerate(ORDER):
                start = pl.multiple_of((where[2] ^ turn(slot, core ^ side)) * cols, LANES)
                part = mxu(kept[side], right_ref[:, pl.ds(start, cols)], NN)
                ref[pos] = part.astype(jnp.bfloat16).reshape(chips, rows, cols)


def attention_grads_kernel(where, *refs, rows, groups, extra):
    left_ref, right_ref, *refs = refs
    *more, own, sent, kept = refs
    core, grp = where[0], where[2]
    chips = left_ref.shape[1] // (2 * rows)
    step = pl.program_id(0)

    def keep_rows(ref):
        for side in range(2):
            chosen = []
            for k in range(chips):
                even = ref[:, 2 * k * rows : (2 * k + 1) * rows]
                odd = ref[:, (2 * k + 1) * rows : (2 * k + 2) * rows]
                chosen.append(jnp.where(core == side, even, odd))
            kept[side] = jnp.concatenate(chosen, 1).T

    def scatter(right, at, cols):
        for ref, side in ((sent, 1), (own, 0)):
            part = mxu(kept[side], right, NN).astype(jnp.bfloat16)
            for g in range(groups):
                pos = position(grp ^ g, core ^ side)
                block = part[:, g * cols : (g + 1) * cols].reshape(chips, rows, cols)
                ref[pos, :, 0:rows, pl.ds(at, cols)] = block

    skip = 0
    if not extra:
        other_left, other_right = more
        skip = other_right.shape[1] // groups

    @pl.when(step == 0)
    def _():
        if not extra:
            keep_rows(other_left)
            scatter(other_right[...], 0, skip)
        keep_rows(left_ref)

    cols = right_ref.shape[2] // groups
    scatter(right_ref[0], pl.multiple_of(skip + step * cols, LANES), cols)

    if extra:
        (sums_ref,) = more

        @pl.when(step == 2)
        def _():
            blank = jnp.zeros((extra, own.shape[3]), jnp.bfloat16)
            for ref, side in ((sent, 1), (own, 0)):
                for g in range(groups):
                    pos = position(grp ^ g, core ^ side)
                    for k in range(chips):
                        start = pl.multiple_of((2 * k + (core ^ side)) * LANES, LANES)
                        ref[pos, k, rows : rows + extra, :] = blank
                        lines = sums_ref[8 * g : 8 * g + 8, pl.ds(start, LANES)]
                        for n in range(3):
                            ref[pos, k, rows : rows + 1, n * LANES : (n + 1) * LANES] = lines[
                                n : n + 1
                            ].astype(jnp.bfloat16)


def position(distance, core):
    slot = turn(distance, core)
    return jnp.where(slot == 0, 2, jnp.where(slot == 1, 0, jnp.where(slot == 3, 1, 3)))


def attention_grads(place, left, right, more, name):
    tokens, height = left.shape
    groups, chips = place.groups, place.chips
    rows = height // place.shards
    extra = 16 if len(more) == 1 else 0
    size = right.shape[2]
    cols = 3 * size // groups + (0 if extra else more[1].shape[1] // groups)
    shape = (groups, chips, rows + extra, cols)
    once = [
        pl.BlockSpec(x.shape, lambda i, s: (0, 0), pipeline_mode=pl.Buffered(1)) for x in more
    ]
    return pl.pallas_call(
        functools.partial(attention_grads_kernel, rows=rows, groups=groups, extra=extra),
        grid_spec=pltpu.PrefetchScalarGridSpec(
            num_scalar_prefetch=1,
            grid=(3,),
            in_specs=[
                pl.BlockSpec(left.shape, lambda i, s: (0, 0), pipeline_mode=pl.Buffered(1)),
                pl.BlockSpec((1, tokens, size), lambda i, s: (i, 0, 0)),
            ]
            + once,
            out_specs=[pl.BlockSpec(shape, lambda i, s: (0, 0, 0, 0))] * 2,
            scratch_shapes=[pltpu.VMEM((2, height // 2, tokens), jnp.bfloat16)],
        ),
        out_shape=[shaped(shape, jnp.bfloat16)] * 2,
        compiler_params=params(60),
        cost_estimate=cost(2 * tokens * height * cols * groups),
        name="wgrad_" + name,
    )(place.scalars, left, right, *more)


def weight_grad(place, left, right, split, name):
    tokens, height = left.shape
    groups, chips = place.groups, place.chips
    rows = height // place.shards
    step_chips = chips if split else max(1, 1024 // (2 * rows))
    cols = right.shape[1] // groups
    if split:
        grid = (1, groups)
        block = lambda i, j, s: (0, s[2] ^ turn(ordered_slot(j), s[0]))
        right_spec = pl.BlockSpec((tokens, cols), block)
        one = (1, chips, rows, cols)
        other = lambda j: jnp.where(j == 0, 3, jnp.where(j == 3, 0, j))
        out_specs = [
            pl.BlockSpec(one, lambda i, j, s: (j, 0, 0, 0)),
            pl.BlockSpec(one, lambda i, j, s: (other(j), 0, 0, 0)),
        ]
    else:
        grid = (chips // step_chips, 1)
        right_spec = pl.BlockSpec(right.shape, lambda i, j, s: (0, 0))
        out_specs = [
            pl.BlockSpec((groups, step_chips, rows, cols), lambda i, j, s: (0, i, 0, 0))
        ] * 2
    return pl.pallas_call(
        functools.partial(weight_grad_kernel, rows=rows, groups=groups, split=split),
        grid_spec=pltpu.PrefetchScalarGridSpec(
            num_scalar_prefetch=1,
            grid=grid,
            in_specs=[
                pl.BlockSpec((tokens, step_chips * 2 * rows), lambda i, j, s: (0, i)),
                right_spec,
            ],
            out_specs=out_specs,
            scratch_shapes=[pltpu.VMEM((2, step_chips * rows, tokens), jnp.bfloat16)],
        ),
        out_shape=[shaped((groups, chips, rows, cols), jnp.bfloat16)] * 2,
        compiler_params=params(60),
        cost_estimate=cost(2 * tokens * height * cols * groups),
        name="wgrad_" + name,
    )(place.scalars, left, right)


def add(*terms):
    total = terms[0].astype(jnp.float32)
    for term in terms[1:]:
        total = total + term.astype(jnp.float32)
    return total.astype(jnp.bfloat16)


class Reduction:
    def __init__(self, place, made):
        self.place = place
        self.made, sent = made
        self.flying = place.swap_core(sent)

    def near(self):
        self.core = self.flying
        leave = add(self.made[:2], self.core[:2])
        self.flying = self.place.swap_grp(leave, 0)
        return leave

    def middle(self):
        self.first = self.flying
        second = add(self.made[3], self.core[3], self.first[1])
        self.flying = self.place.swap_grp(second, 1)
        return second

    def column(self):
        mine = add(self.made[2], self.core[2], self.first[0], self.flying)
        return mine, lambda chip: lax.dynamic_index_in_dim(mine, chip, 0, False)

    def along(self):
        place = self.place
        mine, at = self.column()
        self.mine = [at(place.slot_chip(slot)) for slot in range(4)]
        both = jnp.stack([self.mine[1], self.mine[3]])
        self.flying = place.swap_chip(both, 0)
        return both

    def along_far(self):
        self.first = self.flying
        second = add(self.mine[2], self.first[1])
        self.flying = self.place.swap_chip(second, 1)
        return second

    def share(self):
        return add(self.mine[0], self.first[0], self.flying)

    def along_direct(self):
        place = self.place
        mine, at = self.column()
        self.mine = at(place.chip)
        self.flying = tuple(
            place.permute(at(place.chip ^ k), (2 * k, 2 * k)) for k in range(place.chips - 1, 0, -1)
        )
        return mine

    def share_direct(self):
        return add(self.mine, *self.flying)


class Replication:
    def __init__(self, place, share, direct=False):
        self.place = place
        self.blocks = [share] + [None] * 3
        if direct:
            size = place.shards
            for mask in (3, 1, 2):
                self.blocks[mask] = place.permute(share, (mask * size, mask * size))
        else:
            self.flying = place.swap_grp(share, 0)

    def far(self):
        pair = jnp.stack([self.blocks[0], self.flying])
        self.blocks[1] = self.flying
        self.flying = self.place.swap_grp(pair, 1)
        return pair

    def landed(self):
        if self.blocks[2] is None:
            self.blocks[2:] = [self.flying[0], self.flying[1]]
        return self.blocks


def order_feed_forward(place, blocks, rows_in):
    groups = place.groups
    height, cols = blocks[0].shape
    rows_out = height - groups * rows_in

    def kernel(where, *refs):
        *blocks, out_ref, in_ref = refs
        for slot, ref in enumerate(blocks):
            g = where[2] ^ turn(slot, where[0])
            at = pl.multiple_of(g * cols, LANES)
            out_ref[:, pl.ds(at, cols)] = ref[0:rows_out, :].astype(jnp.float32)
            for n in range(groups):
                at = pl.multiple_of((g * groups + n) * cols, LANES)
                part = ref[rows_out + n * rows_in : rows_out + (n + 1) * rows_in, :]
                in_ref[:, pl.ds(at, cols)] = part.astype(jnp.float32)

    in_vmem = pl.BlockSpec(memory_space=pltpu.VMEM)
    return pl.pallas_call(
        kernel,
        in_specs=[pl.BlockSpec(memory_space=pltpu.SMEM)] + [in_vmem] * groups,
        out_specs=[in_vmem] * 2,
        out_shape=[
            shaped((rows_out, groups * cols), jnp.float32),
            shaped((rows_in, groups * groups * cols), jnp.float32),
        ],
        compiler_params=params(40),
        cost_estimate=cost(height * cols * 1024),
        name="order_feed_forward",
    )(place.scalars, *blocks)


def order_attention(place, blocks_a, blocks_b, rows):
    groups = place.groups
    size = blocks_b[0].shape[1] // 3
    skip = blocks_a[0].shape[1] - 3 * size
    width = groups * skip

    def kernel(where, *refs):
        *blocks, attn_ref, qkv_ref, small_ref = refs
        for n in range(groups):
            ref = blocks[n]
            g = where[2] ^ turn(n, where[0])
            attn_ref[:, pl.ds(pl.multiple_of(g * skip, LANES), skip)] = ref[:, 0:skip].astype(
                jnp.float32
            )
            for part in range(3):
                at = pl.multiple_of(part * width + g * size, LANES)
                block = ref[:, skip + part * size : skip + (part + 1) * size]
                qkv_ref[:, pl.ds(at, size)] = block.astype(jnp.float32)
        for n in range(groups):
            ref = blocks[groups + n]
            g = where[2] ^ n
            lines = []
            for part in range(3):
                at = pl.multiple_of(part * width + width // 2 + g * size, LANES)
                here = slice(part * size, (part + 1) * size)
                qkv_ref[:, pl.ds(at, size)] = ref[0:rows, here].astype(jnp.float32)
                lines.append(ref[rows : rows + 16, here].astype(jnp.float32)[0:1])
            lines.append(jnp.zeros((5, size), jnp.float32))
            small_ref[pl.ds(pl.multiple_of(g * 8, 8), 8), :] = jnp.concatenate(lines)

    in_vmem = pl.BlockSpec(memory_space=pltpu.VMEM)
    return pl.pallas_call(
        kernel,
        in_specs=[pl.BlockSpec(memory_space=pltpu.SMEM)] + [in_vmem] * (2 * groups),
        out_specs=[in_vmem] * 3,
        out_shape=[
            shaped((rows, width), jnp.float32),
            shaped((rows, 3 * width), jnp.float32),
            shaped((8 * groups, size), jnp.float32),
        ],
        compiler_params=params(40),
        name="order_attention",
    )(place.scalars, *blocks_a, *blocks_b)


def on_device_permutes(
    tokens,
    segment_ids,
    keep_flag,
    cotangent,
    w_qkv,
    b_query,
    b_value,
    w_attn_out,
    b_attn_out,
    norm1_gain,
    norm1_bias,
    w_in,
    b_in,
    w_out,
    b_out,
    norm2_gain,
    norm2_bias,
    *,
    groups,
    shards,
):
    place = Place(groups, shards)
    _, length, width = tokens.shape
    rows = tokens[0]
    seg_row = segment_ids.reshape(1, length)
    seg_col = segment_ids.reshape(length, 1)
    keep = keep_flag.reshape(length, 1).astype(jnp.float32)
    pairs = width // LANES

    c1 = Gather(place, w_qkv)
    c2 = Gather(place, jnp.concatenate([w_in, w_attn_out], 1))
    c3 = Gather(place, w_out)
    c1.chips_near()
    small = Vectors(
        place,
        (b_query, b_value, b_attn_out, norm1_gain, norm1_bias, b_out, norm2_gain, norm2_bias, b_in),
    )
    seg_col, keep, _ = lax.optimization_barrier((seg_col, keep, c1.flying))
    meet(seg_col, c1, small)
    pair = c1.chips_far()
    small.chips_near()
    meet(pair, c1, small)
    joined = c1.join()
    c1.near()
    small.chips_far()
    c2.chips_near(joined)
    meet(joined, c2, small)
    small.landed()
    pair = c2.chips_far()
    vectors, bias_in, qkv_bias = small.unpack()
    c1.flying = lax.optimization_barrier(c1.flying)
    c1.far(pair, vectors)
    c1.cross(0, 1, 2)
    joined = c2.join()
    meet(joined, c1)
    c1.landed()
    c2.near(c1.held[3])
    c1.cross(3)
    c3.chips_near(c1.held[3])
    blank = jnp.ones((1, width), jnp.float32)
    qkv_scale = jnp.concatenate([blank / math.sqrt(HD), blank, blank], 1)

    mixed, full_qkv = project_qkv(place, rows, Window(c1, 0, w_qkv.shape[1]), qkv_bias, qkv_scale)
    meet(mixed, c3)
    pair = c3.chips_far()
    c2.cross(0, wait=(mixed,))
    first, second = pairs * 3 // 8, pairs * 3 // 4
    forward = attention_forward(after(mixed, pair), seg_col, seg_row, 0, first)
    meet(forward[1], c2, c3)
    c2.far()
    joined = c3.join()
    c3.near()
    c2.cross(1, 2)
    forward = attention_forward(
        after(mixed, joined), seg_col, seg_row, first, second - first, forward
    )
    meet(forward[1], c2)
    c2.landed()
    c2.cross(3)
    contexts, lse = attention_forward(
        after(mixed, c2.held[3]), seg_col, seg_row, second, pairs - second, forward
    )
    normed, scale_one, normed_low, full_attn = project_out(
        place, contexts, Window(c2, w_in.shape[1], w_attn_out.shape[1]), rows, vectors
    )
    meet(normed_low, c3)
    c3.far()
    c3.cross(0, 1, 2)
    hidden, slope, full_in = feed_in(
        place, after(normed_low, c3.held[1]), Window(c2, 0, w_in.shape[1]), bias_in
    )
    meet(hidden, c3)
    c3.landed()
    c3.cross(3)
    layer_out, second_grad, out_low, second_sums, full_out = feed_out(
        place, hidden, Window(c3, 0, w_out.shape[1]), normed, cotangent[0], keep, vectors
    )

    r_out = Reduction(place, weight_grad(place, hidden, out_low, False, "out"))
    pre_low, bias_in_grad = feed_out_back(after(out_low, r_out.made), full_out, slope)
    meet(pre_low, r_out)
    step = r_out.near()
    r_in = Reduction(place, weight_grad(place, after(normed_low, step), pre_low, True, "in"))
    first_grad, attn_low, context_grad, first_sums = feed_in_back(
        after(pre_low, r_in.made), full_in, second_grad, normed, scale_one, vectors, full_attn
    )
    meet(attn_low, r_in)
    step = r_in.near()
    half, quarter = pairs // 2, pairs // 4

    def back(wait, start, count, at, before=None):
        return attention_backward(
            mixed,
            contexts,
            after(context_grad, *wait),
            seg_col,
            seg_row,
            lse,
            start,
            count,
            at,
            half,
            before,
        )

    low_a, late_a = back((step,), 0, half, 0)
    meet(late_a, r_out, r_in)
    steps = (r_out.middle(), r_in.middle())
    r_a = Reduction(
        place, attention_grads(place, after(rows, *steps), low_a, (contexts, attn_low), "a")
    )
    meet(r_a.made, r_out)
    step = r_out.along()
    part = back((r_a.made, step), half, quarter, 0)
    meet(part[1], r_out, r_in, r_a)
    steps = (r_out.along_far(), r_in.along(), r_a.near())
    low_b, late_b = back(steps, half + quarter, quarter, quarter, part)
    meet(late_b, r_out, r_in, r_a)
    sums = pack_sums(late_a, late_b, first_sums, second_sums, bias_in_grad)
    share_out = r_out.share()
    steps = (r_in.along_far(), r_a.middle(), share_out)
    r_b = Reduction(place, attention_grads(place, after(rows, *steps), low_b, (sums,), "b"))
    meet(r_b.made, r_in, r_a)
    share_in = r_in.share()
    inner = share_in.shape[1] // groups
    joined = jnp.concatenate(
        [share_out] + [share_in[:, n * inner : (n + 1) * inner] for n in range(groups)]
    )
    all_ffn = Replication(place, joined)
    grads = (low_a, after(low_b, r_b.made, joined, r_a.along()))
    tiles = length // TILE // 2
    input_grad = project_qkv_back(grads, full_qkv, first_grad, 0, tiles)
    meet(input_grad, r_b, r_a, all_ffn)
    steps = (r_b.near(), r_a.along_far())
    input_grad = project_qkv_back(
        grads, full_qkv, after(first_grad, *steps), tiles, tiles, input_grad
    )
    meet(input_grad, r_b, r_a)
    middle = r_b.middle()
    r_a.flying = after(r_a.flying, middle)
    all_a = Replication(place, r_a.share())
    meet(all_a.blocks[0], r_b, all_a)
    along = r_b.along_direct()
    all_a.flying = after(all_a.flying, along)
    all_ffn.flying = after(all_ffn.flying, along)
    pairs_made = (all_a.far(), all_ffn.far())
    meet(pairs_made, r_b)
    share_b = r_b.share_direct()
    all_b = Replication(place, share_b, direct=True)
    meet(share_b, all_ffn)
    w_out_grad, w_in_grad = order_feed_forward(place, all_ffn.landed(), share_in.shape[0])
    all_a.flying = after(all_a.flying, w_out_grad)
    w_attn_grad, w_qkv_grad, small = order_attention(
        place, all_a.landed(), all_b.landed(), w_attn_out.shape[0]
    )
    small = [small[8 * (n // 3) + n % 3] for n in range(12)]
    return (
        layer_out[None],
        input_grad[None],
        w_qkv_grad,
        small[B_QUERY],
        small[B_VALUE],
        w_attn_grad,
        small[B_ATTN],
        small[GAIN_ONE],
        small[SHIFT_ONE],
        w_in_grad,
        jnp.concatenate(small[B_IN:]),
        w_out_grad,
        small[B_OUT],
        small[GAIN_TWO],
        small[SHIFT_TWO],
    )


def solution(mesh):
    groups, shards = mesh.shape["grp"], mesh.shape["shard"]
    if groups == 4 and shards == 8:
        body = functools.partial(on_device_permutes, groups=groups, shards=shards)
    else:
        body = on_device
    return jax.shard_map(
        body,
        mesh=mesh,
        in_specs=(
            P(("grp", "shard"), None, None),
            P(("grp", "shard"), None),
            P(("grp", "shard"), None),
            P(("grp", "shard"), None, None),
            P("shard", "grp"),
            P("shard"),
            P("shard"),
            P("shard", "grp"),
            P("shard"),
            P("shard"),
            P("shard"),
            P("shard", "grp"),
            P("shard"),
            P("shard", "grp"),
            P("shard"),
            P("shard"),
            P("shard"),
        ),
        out_specs=(
            P(("grp", "shard"), None, None),
            P(("grp", "shard"), None, None),
            P("shard", None),
            P("shard"),
            P("shard"),
            P("shard", None),
            P("shard"),
            P("shard"),
            P("shard"),
            P("shard", None),
            P("shard"),
            P("shard", None),
            P("shard"),
            P("shard"),
            P("shard"),
        ),
        check_vma=False,
    )
```

```python
import functools
import math

import jax
import jax.numpy as jnp
from jax import lax
from jax.experimental import pallas as pl
from jax.experimental.pallas import tpu as pltpu
from jax.sharding import PartitionSpec as P

H = 16
HD = 64


masked_score = -1e30
epsilon = 1e-05


def norm_layer(rows, gain_row, shift_row):
    row_mean = jnp.mean(rows, -1, keepdims=True)
    centered = rows - row_mean
    row_var = jnp.mean(centered * centered, -1, keepdims=True)
    return centered * lax.rsqrt(row_var + epsilon) * gain_row + shift_row


def gelu_exact(values):
    return 0.5 * values * (1.0 + lax.erf(values * (1.0 / math.sqrt(2.0))))


def contract_rows(left, right):
    return lax.dot_general(
        left, right, (((0,), (0,)), ((), ())), preferred_element_type=jnp.float32
    )


def contract_cols(left, right):
    return lax.dot_general(
        left, right, (((1,), (1,)), ((), ())), preferred_element_type=jnp.float32
    )


def attend_forward(queries, key_rows, value_rows, segment_row, block_rows):
    length, model_width = queries.shape
    scaling = 1.0 / math.sqrt(HD)
    key_heads = key_rows.reshape(length, H, HD)
    value_heads = value_rows.reshape(length, H, HD)
    query_blocks = queries.reshape(length // block_rows, block_rows, H, HD)
    segment_blocks = segment_row.reshape(length // block_rows, block_rows)

    def one_block(pieces):
        query_part, segment_part = pieces
        scores = (
            jnp.einsum("qhd,khd->hqk", query_part, key_heads, preferred_element_type=jnp.float32)
            * scaling
        )
        allowed = segment_part[:, None] == segment_row[None, :]
        scores = jnp.where(allowed[None], scores, masked_score)
        row_max = jnp.max(scores, -1, keepdims=True)
        powers = jnp.exp(scores - row_max)
        totals = jnp.sum(powers, -1, keepdims=True)
        attn_probs = (powers / totals).astype(jnp.bfloat16)
        context = jnp.einsum(
            "hqk,khd->qhd", attn_probs, value_heads, preferred_element_type=jnp.float32
        )
        return (
            context.reshape(block_rows, model_width).astype(jnp.bfloat16),
            (row_max + jnp.log(totals))[:, :, 0],
        )

    contexts, log_sums = lax.map(one_block, (query_blocks, segment_blocks))
    return (contexts.reshape(length, model_width), log_sums)


def attend_backward(queries, key_rows, value_rows, segment_row, log_sums, context_grad, block_rows):
    length, model_width = queries.shape
    scaling = 1.0 / math.sqrt(HD)
    key_heads = key_rows.reshape(length, H, HD)
    value_heads = value_rows.reshape(length, H, HD)
    query_blocks = queries.reshape(length // block_rows, block_rows, H, HD)
    segment_blocks = segment_row.reshape(length // block_rows, block_rows)
    grad_blocks = context_grad.reshape(length // block_rows, block_rows, H, HD)

    def one_block(running, pieces):
        key_acc, value_acc = running
        query_part, segment_part, lse_part, grad_part = pieces
        scores = (
            jnp.einsum("qhd,khd->hqk", query_part, key_heads, preferred_element_type=jnp.float32)
            * scaling
        )
        allowed = segment_part[:, None] == segment_row[None, :]
        scores = jnp.where(allowed[None], scores, masked_score)
        probs = jnp.exp(scores - lse_part[:, :, None])
        prob_low = probs.astype(jnp.bfloat16)
        prob_grad = jnp.einsum(
            "qhd,khd->hqk", grad_part, value_heads, preferred_element_type=jnp.float32
        )
        row_dot = jnp.sum(prob_grad * probs, -1, keepdims=True)
        score_grad = (probs * (prob_grad - row_dot)).astype(jnp.bfloat16)
        query_grad = (
            jnp.einsum("hqk,khd->qhd", score_grad, key_heads, preferred_element_type=jnp.float32)
            * scaling
        )
        key_acc = (
            key_acc
            + jnp.einsum("hqk,qhd->khd", score_grad, query_part, preferred_element_type=jnp.float32)
            * scaling
        )
        value_acc = value_acc + jnp.einsum(
            "hqk,qhd->khd", prob_low, grad_part, preferred_element_type=jnp.float32
        )
        return ((key_acc, value_acc), query_grad.reshape(block_rows, model_width))

    empty_acc = jnp.zeros((length, H, HD), jnp.float32)
    (key_grad, value_grad), query_grads = lax.scan(
        one_block, (empty_acc, empty_acc), (query_blocks, segment_blocks, log_sums, grad_blocks)
    )
    return (
        query_grads.reshape(length, model_width),
        key_grad.reshape(length, model_width),
        value_grad.reshape(length, model_width),
    )


def on_device(
    tokens,
    segment_ids,
    keep_flag,
    cotangent,
    w_qkv,
    b_query,
    b_value,
    w_attn_out,
    b_attn_out,
    norm1_gain,
    norm1_bias,
    w_in,
    b_in,
    w_out,
    b_out,
    norm2_gain,
    norm2_bias,
):
    seq_count, length, model_width = tokens.shape
    block_rows = min(512, length)
    within = (
        lax.all_gather(w_qkv, "shard", axis=0, tiled=True),
        lax.all_gather(w_attn_out, "shard", axis=0, tiled=True),
        lax.all_gather(w_in, "shard", axis=0, tiled=True),
        lax.all_gather(w_out, "shard", axis=0, tiled=True),
        lax.all_gather(b_query, "shard", axis=0, tiled=True),
        lax.all_gather(b_value, "shard", axis=0, tiled=True),
        lax.all_gather(b_attn_out, "shard", axis=0, tiled=True),
        lax.all_gather(norm1_gain, "shard", axis=0, tiled=True),
        lax.all_gather(norm1_bias, "shard", axis=0, tiled=True),
        lax.all_gather(b_in, "shard", axis=0, tiled=True),
        lax.all_gather(b_out, "shard", axis=0, tiled=True),
        lax.all_gather(norm2_gain, "shard", axis=0, tiled=True),
        lax.all_gather(norm2_bias, "shard", axis=0, tiled=True),
    )
    full_qkv, full_attn, full_in, full_out = (
        lax.all_gather(within[0], "grp", axis=1, tiled=True),
        lax.all_gather(within[1], "grp", axis=1, tiled=True),
        lax.all_gather(within[2], "grp", axis=1, tiled=True),
        lax.all_gather(within[3], "grp", axis=1, tiled=True),
    )
    (
        bias_query,
        bias_value,
        bias_attn,
        gain_one,
        shift_one,
        bias_in,
        bias_out,
        gain_two,
        shift_two,
    ) = [piece.astype(jnp.float32) for piece in within[4:]]
    flat_rows = tokens.reshape(seq_count * length, model_width)
    mixed_qkv = jnp.dot(flat_rows, full_qkv, preferred_element_type=jnp.float32)
    queries = (mixed_qkv[:, :model_width] + bias_query).astype(jnp.bfloat16)
    key_rows = mixed_qkv[:, model_width : 2 * model_width].astype(jnp.bfloat16)
    value_rows = (mixed_qkv[:, 2 * model_width :] + bias_value).astype(jnp.bfloat16)
    query_seqs = queries.reshape(seq_count, length, model_width)
    key_seqs = key_rows.reshape(seq_count, length, model_width)
    value_seqs = value_rows.reshape(seq_count, length, model_width)

    def forward_sequence(pieces):
        return attend_forward(pieces[0], pieces[1], pieces[2], pieces[3], block_rows)

    contexts, log_sums = lax.map(forward_sequence, (query_seqs, key_seqs, value_seqs, segment_ids))
    contexts = contexts.reshape(seq_count * length, model_width)
    attended = jnp.dot(contexts, full_attn, preferred_element_type=jnp.float32) + bias_attn
    first_sum = flat_rows.astype(jnp.float32) + attended
    normed_one, norm_one_back = jax.vjp(norm_layer, first_sum, gain_one, shift_one)
    normed_low = normed_one.astype(jnp.bfloat16)
    hidden_pre = jnp.dot(normed_low, full_in, preferred_element_type=jnp.float32) + bias_in
    hidden, gelu_back = jax.vjp(gelu_exact, hidden_pre)
    hidden_low = hidden.astype(jnp.bfloat16)
    second_sum = normed_one + (
        jnp.dot(hidden_low, full_out, preferred_element_type=jnp.float32) + bias_out
    )
    result, norm_two_back = jax.vjp(norm_layer, second_sum, gain_two, shift_two)
    layer_out = result.astype(jnp.bfloat16).reshape(seq_count, length, model_width)
    again = (
        lax.all_gather(w_qkv, "shard", axis=0, tiled=True),
        lax.all_gather(w_attn_out, "shard", axis=0, tiled=True),
        lax.all_gather(w_in, "shard", axis=0, tiled=True),
        lax.all_gather(w_out, "shard", axis=0, tiled=True),
    )
    back_qkv, back_attn, back_in, back_out = (
        lax.all_gather(again[0], "grp", axis=1, tiled=True),
        lax.all_gather(again[1], "grp", axis=1, tiled=True),
        lax.all_gather(again[2], "grp", axis=1, tiled=True),
        lax.all_gather(again[3], "grp", axis=1, tiled=True),
    )
    masked_cot = cotangent.astype(jnp.float32).reshape(
        seq_count * length, model_width
    ) * keep_flag.reshape(seq_count * length, 1).astype(jnp.float32)
    second_grad, gain_two_grad, shift_two_grad = norm_two_back(masked_cot)
    bias_out_grad = jnp.sum(second_grad, 0)
    out_low = second_grad.astype(jnp.bfloat16)
    w_out_grad = contract_rows(hidden_low, out_low)
    hidden_grad = contract_cols(out_low, back_out)
    (pre_grad,) = gelu_back(hidden_grad)
    bias_in_grad = jnp.sum(pre_grad, 0)
    pre_low = pre_grad.astype(jnp.bfloat16)
    w_in_grad = contract_rows(normed_low, pre_low)
    normed_grad = second_grad + contract_cols(pre_low, back_in)
    first_grad, gain_one_grad, shift_one_grad = norm_one_back(normed_grad)
    bias_attn_grad = jnp.sum(first_grad, 0)
    attn_low = first_grad.astype(jnp.bfloat16)
    w_attn_grad = contract_rows(contexts, attn_low)
    context_grad = contract_cols(attn_low, back_attn).astype(jnp.bfloat16)

    def backward_sequence(pieces):
        return attend_backward(
            pieces[0], pieces[1], pieces[2], pieces[3], pieces[4], pieces[5], block_rows
        )

    query_grad, key_grad, value_grad = lax.map(
        backward_sequence,
        (
            query_seqs,
            key_seqs,
            value_seqs,
            segment_ids,
            log_sums,
            context_grad.reshape(seq_count, length, model_width),
        ),
    )
    query_grad = query_grad.reshape(seq_count * length, model_width)
    key_grad = key_grad.reshape(seq_count * length, model_width)
    value_grad = value_grad.reshape(seq_count * length, model_width)
    bias_query_grad = jnp.sum(query_grad, 0)
    bias_value_grad = jnp.sum(value_grad, 0)
    qkv_low = jnp.concatenate([query_grad, key_grad, value_grad], 1).astype(jnp.bfloat16)
    w_qkv_grad = contract_rows(flat_rows, qkv_low)
    input_grad = first_grad + contract_cols(qkv_low, back_qkv)
    reduced = (
        lax.psum_scatter(
            w_qkv_grad.astype(jnp.bfloat16), "shard", scatter_dimension=0, tiled=True
        ).astype(jnp.float32),
        lax.psum_scatter(
            bias_query_grad.astype(jnp.bfloat16), "shard", scatter_dimension=0, tiled=True
        ).astype(jnp.float32),
        lax.psum_scatter(
            bias_value_grad.astype(jnp.bfloat16), "shard", scatter_dimension=0, tiled=True
        ).astype(jnp.float32),
        lax.psum_scatter(
            w_attn_grad.astype(jnp.bfloat16), "shard", scatter_dimension=0, tiled=True
        ).astype(jnp.float32),
        lax.psum_scatter(
            bias_attn_grad.astype(jnp.bfloat16), "shard", scatter_dimension=0, tiled=True
        ).astype(jnp.float32),
        lax.psum_scatter(
            gain_one_grad.astype(jnp.bfloat16), "shard", scatter_dimension=0, tiled=True
        ).astype(jnp.float32),
        lax.psum_scatter(
            shift_one_grad.astype(jnp.bfloat16), "shard", scatter_dimension=0, tiled=True
        ).astype(jnp.float32),
        lax.psum_scatter(
            w_in_grad.astype(jnp.bfloat16), "shard", scatter_dimension=0, tiled=True
        ).astype(jnp.float32),
        lax.psum_scatter(
            bias_in_grad.astype(jnp.bfloat16), "shard", scatter_dimension=0, tiled=True
        ).astype(jnp.float32),
        lax.psum_scatter(
            w_out_grad.astype(jnp.bfloat16), "shard", scatter_dimension=0, tiled=True
        ).astype(jnp.float32),
        lax.psum_scatter(
            bias_out_grad.astype(jnp.bfloat16), "shard", scatter_dimension=0, tiled=True
        ).astype(jnp.float32),
        lax.psum_scatter(
            gain_two_grad.astype(jnp.bfloat16), "shard", scatter_dimension=0, tiled=True
        ).astype(jnp.float32),
        lax.psum_scatter(
            shift_two_grad.astype(jnp.bfloat16), "shard", scatter_dimension=0, tiled=True
        ).astype(jnp.float32),
    )
    summed = (
        lax.psum(reduced[0].astype(jnp.bfloat16), "grp").astype(jnp.float32),
        lax.psum(reduced[1].astype(jnp.bfloat16), "grp").astype(jnp.float32),
        lax.psum(reduced[2].astype(jnp.bfloat16), "grp").astype(jnp.float32),
        lax.psum(reduced[3].astype(jnp.bfloat16), "grp").astype(jnp.float32),
        lax.psum(reduced[4].astype(jnp.bfloat16), "grp").astype(jnp.float32),
        lax.psum(reduced[5].astype(jnp.bfloat16), "grp").astype(jnp.float32),
        lax.psum(reduced[6].astype(jnp.bfloat16), "grp").astype(jnp.float32),
        lax.psum(reduced[7].astype(jnp.bfloat16), "grp").astype(jnp.float32),
        lax.psum(reduced[8].astype(jnp.bfloat16), "grp").astype(jnp.float32),
        lax.psum(reduced[9].astype(jnp.bfloat16), "grp").astype(jnp.float32),
        lax.psum(reduced[10].astype(jnp.bfloat16), "grp").astype(jnp.float32),
        lax.psum(reduced[11].astype(jnp.bfloat16), "grp").astype(jnp.float32),
        lax.psum(reduced[12].astype(jnp.bfloat16), "grp").astype(jnp.float32),
    )
    return (
        layer_out,
        input_grad.reshape(seq_count, length, model_width),
        summed[0],
        summed[1],
        summed[2],
        summed[3],
        summed[4],
        summed[5],
        summed[6],
        summed[7],
        summed[8],
        summed[9],
        summed[10],
        summed[11],
        summed[12],
    )


NT = (((1,), (1,)), ((), ()))
NN = (((1,), (0,)), ((), ()))
TN = (((0,), (0,)), ((), ()))
LANES = 128
AXES = ("grp", "shard")


def mxu(left, right, dims):
    return lax.dot_general(left, right, dims, preferred_element_type=jnp.float32)


def cost(flops):
    return pl.CostEstimate(flops=2 * flops, bytes_accessed=0, transcendentals=0)


def params(megabytes=60):
    return pltpu.CompilerParams(vmem_limit_bytes=megabytes << 20)


def attention_forward_kernel(q_ref, k_ref, v_ref, seg_col, seg_row, out_ref, probs_ref, *, rows):
    length = q_ref.shape[0]
    first = lax.broadcasted_iota(jnp.int32, (1, LANES), 1) < HD
    keys = k_ref[...]
    values = v_ref[...]
    zero = jnp.zeros_like(keys)
    head_keys = (jnp.where(first, keys, zero), jnp.where(first, zero, keys))
    key_segments = seg_col[...]
    for block in range(length // rows):
        here = pl.ds(block * rows, rows)
        q = q_ref[here, :]
        allowed = key_segments == seg_row[:, here]
        outs = []
        for head in range(2):
            scores = mxu(head_keys[head], q, NT)
            scores = jnp.where(allowed, scores, masked_score)
            powers = jnp.exp(scores - jnp.max(scores, 0, keepdims=True))
            probs = powers * (1.0 / jnp.sum(powers, 0, keepdims=True))
            probs = probs.astype(jnp.bfloat16)
            probs_ref[head, :, here] = probs
            outs.append(mxu(probs, values, TN))
        out_ref[here, :] = jnp.where(first, outs[0], outs[1]).astype(jnp.bfloat16)


def attention_forward(qkv, seg_col, seg_row, start, pairs, before=None):
    length, width = qkv.shape[0], qkv.shape[1] // 3
    total = width // LANES
    rows = min(512, length)
    more = () if before is None else before

    def pair(part):
        return pl.BlockSpec((length, LANES), lambda j: (0, part * total + start + j))

    def body(q_ref, k_ref, v_ref, seg_c, seg_r, *refs):
        attention_forward_kernel(q_ref, k_ref, v_ref, seg_c, seg_r, *refs[-2:], rows=rows)

    return pl.pallas_call(
        body,
        grid=(pairs,),
        in_specs=[
            pair(0),
            pair(1),
            pair(2),
            pl.BlockSpec((length, 1), lambda j: (0, 0)),
            pl.BlockSpec((1, length), lambda j: (0, 0)),
        ]
        + [pl.BlockSpec(memory_space=pl.ANY)] * len(more),
        out_specs=[
            pl.BlockSpec((length, LANES), lambda j: (0, start + j)),
            pl.BlockSpec((2, length, length), lambda j: (start + j, 0, 0)),
        ],
        out_shape=[
            jax.ShapeDtypeStruct((length, width), jnp.bfloat16),
            jax.ShapeDtypeStruct((2 * total, length, length), jnp.bfloat16),
        ],
        input_output_aliases={} if before is None else {5: 0, 6: 1},
        compiler_params=params(60),
        cost_estimate=cost(16 * length * length * pairs * LANES),
        name="attn_fwd",
    )(qkv, qkv, qkv, seg_col, seg_row, *more)


def attention_backward_kernel(q_ref, k_ref, v_ref, o_ref, do_ref, probs_ref, grad_ref, sum_ref):
    first = lax.broadcasted_iota(jnp.int32, (1, LANES), 1) < HD
    pick = (
        lax.broadcasted_iota(jnp.int32, (8, LANES), 0)
        == lax.broadcasted_iota(jnp.int32, (8, LANES), 1) // HD
    ).astype(jnp.float32)
    q = q_ref[...]
    do = do_ref[...]
    keys = k_ref[...]
    values = v_ref[...]
    zero = jnp.zeros_like(values)
    head_values = (jnp.where(first, values, zero), jnp.where(first, zero, values))
    dots = lax.dot_general(
        pick,
        do.astype(jnp.float32) * o_ref[...].astype(jnp.float32),
        NT,
        precision=lax.Precision.HIGHEST,
        preferred_element_type=jnp.float32,
    )
    query_parts, key_parts, value_parts = [], [], []
    for head in range(2):
        probs = probs_ref[head]
        prob_grad = mxu(head_values[head], do, NT)
        score_grad = probs.astype(jnp.float32) * (prob_grad - dots[head : head + 1, :])
        score_grad = score_grad.astype(jnp.bfloat16)
        value_parts.append(mxu(probs, do, NN))
        key_parts.append(mxu(score_grad, q, NN))
        query_parts.append(mxu(score_grad, keys, TN))
    query_grad = jnp.where(first, *query_parts) * (1.0 / math.sqrt(HD))
    value_grad = jnp.where(first, *value_parts)
    grad_ref[0] = query_grad.astype(jnp.bfloat16)
    grad_ref[1] = jnp.where(first, *key_parts).astype(jnp.bfloat16)
    grad_ref[2] = value_grad.astype(jnp.bfloat16)
    sum_ref[0:1, :] = jnp.sum(query_grad, 0, keepdims=True)
    sum_ref[1:2, :] = jnp.sum(value_grad, 0, keepdims=True)


def attention_backward(qkv, out, out_grad, probs, start, pairs, at, size, before=None):
    length, width = out.shape
    total = width // LANES
    more = () if before is None else before

    def pair(part):
        return pl.BlockSpec((length, LANES), lambda j: (0, part * total + start + j))

    def body(*refs):
        attention_backward_kernel(*refs[:6], *refs[-2:])

    return pl.pallas_call(
        body,
        grid=(pairs,),
        in_specs=[
            pair(0),
            pair(1),
            pair(2),
            pair(0),
            pair(0),
            pl.BlockSpec((2, length, length), lambda j: (start + j, 0, 0)),
        ]
        + [pl.BlockSpec(memory_space=pl.ANY)] * len(more),
        out_specs=[
            pl.BlockSpec((3, length, LANES), lambda j: (0, 0, j + at)),
            pl.BlockSpec((2, LANES), lambda j: (0, j + at)),
        ],
        out_shape=[
            jax.ShapeDtypeStruct((3, length, size * LANES), jnp.bfloat16),
            jax.ShapeDtypeStruct((2, size * LANES), jnp.float32),
        ],
        input_output_aliases={} if before is None else {6: 0, 7: 1},
        compiler_params=params(60),
        cost_estimate=cost(32 * length * length * pairs * LANES),
        name="attn_bwd",
    )(qkv, qkv, qkv, out, out_grad, probs, *more)


class Place:
    def __init__(self, groups, shards):
        self.groups = groups
        self.shards = shards
        self.chips = shards // 2
        self.grp = lax.axis_index("grp")
        self.shard = lax.axis_index("shard")
        self.core = self.shard % 2
        self.chip = self.shard // 2
        self.scalars = jnp.stack([self.core, self.chip, self.grp]).astype(jnp.int32)

    def permute(self, array, mask_of_core):
        pairs = [(i, i ^ mask_of_core[i % 2]) for i in range(self.groups * self.shards)]
        return lax.ppermute(array, AXES, pairs)

    def swap_core(self, array):
        return self.permute(array, (1, 1))

    def swap_grp(self, array, step):
        masks = (self.shards, 2 * self.shards)
        return self.permute(array, masks if step == 0 else masks[::-1])

    def swap_chip(self, array, step):
        masks = (2, 4)
        return self.permute(array, masks if step == 0 else masks[::-1])

    def slot_chip(self, slot):
        return self.chip ^ turn(slot, self.core)

    def slot_grp(self, slot):
        return self.grp ^ turn(slot, self.core)


def turn(slot, core):
    if isinstance(slot, int):
        return slot if slot in (0, 3) else jnp.where(core == 0, slot, 3 - slot)
    return jnp.where((core == 0) | (slot == 0) | (slot == 3), slot, 3 - slot)


def after(value, *others):
    return lax.optimization_barrier((value, *others))[0]


def meet(anchor, *flights):
    arrays = [f.flying for f in flights]
    _, *arrays = lax.optimization_barrier((anchor, *arrays))
    for f, array in zip(flights, arrays):
        f.flying = array


class Gather:
    def __init__(self, place, piece):
        self.place = place
        self.piece = piece
        self.held = [None] * 4
        self.crossed = [None] * 4

    def chips_near(self, *wait):
        self.piece = after(self.piece, *wait)
        self.flying = self.place.swap_chip(self.piece, 0)

    def chips_far(self):
        self.pair = jnp.stack([self.piece, self.flying])
        self.flying = self.place.swap_chip(self.pair, 1)
        return self.pair

    def join(self):
        self.held[0] = jnp.concatenate([self.pair, self.flying])
        return self.held[0]

    def near(self, *wait):
        self.held[0] = after(self.held[0], *wait)
        self.flying = (self.place.swap_grp(self.held[0], 0), self.place.swap_grp(self.held[0], 1))
        return self.held[0]

    def far(self, *wait):
        self.held[1:3] = self.flying
        first = after(self.held[1], *wait)
        self.flying = self.place.swap_grp(first, 1)

    def landed(self):
        self.held[3] = self.flying

    def cross(self, *which, wait=()):
        for n in which:
            self.crossed[n] = self.place.swap_core(after(self.held[n], *wait))

    def pieces(self):
        return self.held + self.crossed


class Window:
    def __init__(self, gather, start, cols):
        self.arrays = gather.pieces()
        self.start, self.cols = start, cols
        chips, rows, _ = self.arrays[0].shape
        self.chips, self.rows = chips, rows


def fetch(where, window, refs, whole, sem, by):
    rows, cols, chips = window.rows, window.cols, window.chips
    for slot in range(4):
        for side in range(2):
            core = where[0] ^ side
            ref = refs[4 * side + slot]
            distance = turn(slot, core)
            col = pl.multiple_of((where[2] ^ distance) * cols, LANES)
            for k in range(chips):
                row = ((where[1] ^ turn(k, core)) * 2 + core) * rows
                pltpu.make_async_copy(
                    ref.at[k, :, pl.ds(window.start, cols)],
                    whole.at[pl.ds(pl.multiple_of(row, rows), rows), pl.ds(col, cols)],
                    sem.at[distance if by == "grp" else 0],
                ).start()


def weight_call(place, kernel, window, inputs, in_specs, outs, out_specs, steps, by, name, flops, mb=60):
    cols, groups = window.cols, place.groups
    pieces = window.arrays
    shape = (window.chips * 2 * window.rows, groups * cols)
    slots = {"grp": groups, "all": 1}[by]
    anywhere = pl.BlockSpec(memory_space=pl.ANY)

    def body(where, *refs):
        taken, refs = refs[: len(pieces)], refs[len(pieces) :]
        *refs, written, weight, sem, out_sem = refs
        step = pl.program_id(0)

        @pl.when(step == 0)
        def _():
            fetch(where, window, taken, weight, sem, by)

        def ready():
            if by == "all":

                @pl.when(step == 0)
                def _():
                    pltpu.make_async_copy(weight, weight, sem.at[0]).wait()
                    pltpu.make_async_copy(weight, written, out_sem.at[0]).start()

            else:
                at = pl.ds(pl.multiple_of((where[2] ^ step) * cols, LANES), cols)
                view = weight.at[:, at]
                pltpu.make_async_copy(view, view, sem.at[step]).wait()
                pltpu.make_async_copy(view, written.at[:, at], out_sem.at[step]).start()

        kernel(where, ready, weight, *refs)

        @pl.when(step == steps - 1)
        def _():
            for slot in range(slots):
                width = shape[1] // slots
                view = weight.at[:, pl.ds(slot * width, width)]
                pltpu.make_async_copy(view, view, out_sem.at[slot]).wait()

    total = sum(math.prod(x.shape) * x.dtype.itemsize for x in list(inputs) + list(outs))
    return pl.pallas_call(
        body,
        grid_spec=pltpu.PrefetchScalarGridSpec(
            num_scalar_prefetch=1,
            grid=(steps,),
            in_specs=[anywhere] * len(pieces) + in_specs,
            out_specs=out_specs + [anywhere],
            scratch_shapes=[
                pltpu.VMEM(shape, jnp.bfloat16),
                pltpu.SemaphoreType.DMA((slots,)),
                pltpu.SemaphoreType.DMA((slots,)),
            ],
        ),
        out_shape=outs + [shaped(shape, jnp.bfloat16)],
        compiler_params=params(mb),
        cost_estimate=cost(flops),
        name=name,
    )(place.scalars, *pieces, *inputs)


def plain_call(kernel, inputs, in_specs, outs, out_specs, steps, name, flops, mb=60):
    total = sum(math.prod(x.shape) * x.dtype.itemsize for x in list(inputs) + list(outs))
    return pl.pallas_call(
        kernel,
        grid=(steps,),
        in_specs=in_specs,
        out_specs=out_specs,
        out_shape=outs,
        compiler_params=params(mb),
        cost_estimate=cost(flops),
        name=name,
    )(*inputs)


TILE = 256


def row_tiles(width):
    return pl.BlockSpec((TILE, width), lambda i, *s: (i, 0))


def fixed(*shape):
    return pl.BlockSpec(shape, lambda i, *s: (0,) * len(shape))


def whole_once(shape):
    return pl.BlockSpec(shape, lambda i: (0,) * len(shape), pipeline_mode=pl.Buffered(1))


def shaped(shape, dtype):
    return jax.ShapeDtypeStruct(shape, dtype)


B_QUERY, B_VALUE, B_ATTN, GAIN_ONE, SHIFT_ONE, B_OUT, GAIN_TWO, SHIFT_TWO, B_IN = range(9)


def row(ref, n):
    return ref[n : n + 1, :]


class Vectors:
    def __init__(self, place, vectors):
        lines = [v.reshape(-1, LANES) for v in vectors]
        blank = jnp.zeros((-sum(x.shape[0] for x in lines) % 16, LANES), jnp.bfloat16)
        self.own = jnp.concatenate([*lines, blank])
        self.place = place
        self.flying = place.swap_core(self.own)

    def chips_near(self):
        self.own = jnp.stack([self.own, self.flying])
        self.flying = self.place.swap_chip(self.own, 0)

    def chips_far(self):
        self.own = jnp.stack([self.own, self.flying])
        self.flying = self.place.swap_chip(self.own, 1)

    def landed(self):
        self.slots = jnp.concatenate([self.own, self.flying])

    def unpack(self, seg_row, keep_row):
        place = self.place
        length = seg_row.shape[1]
        slots, sides, rows, lanes = self.slots.shape
        shards = place.shards

        def kernel(where, in_ref, seg_ref, keep_ref, *outs):
            rows_ref, inner_ref, qkv_ref, seg_col_ref, keep_col_ref = outs
            for line_ref, col_ref in ((seg_ref, seg_col_ref), (keep_ref, keep_col_ref)):
                line = jnp.broadcast_to(line_ref[...].astype(jnp.float32), (8, length))
                col_ref[...] = line.T[:, 0:1].astype(col_ref.dtype)
            width = shards * lanes
            qkv_ref[...] = jnp.zeros_like(qkv_ref)
            for slot in range(slots):
                for side in range(sides):
                    core = where[0] ^ side
                    shard = (where[1] ^ turn(slot, where[0])) * 2 + core
                    part = in_ref[slot, side].astype(jnp.float32)
                    at = pl.multiple_of(shard * lanes, lanes)
                    rows_ref[:, pl.ds(at, lanes)] = part
                    qkv_ref[:, pl.ds(at, lanes)] = part[B_QUERY : B_QUERY + 1]
                    qkv_ref[:, pl.ds(2 * width + at, lanes)] = part[B_VALUE : B_VALUE + 1]
                    for n in range(4):
                        start = pl.multiple_of((shard * 4 + n) * lanes, lanes)
                        inner_ref[:, pl.ds(start, lanes)] = part[B_IN + n : B_IN + n + 1]

        in_vmem = pl.BlockSpec(memory_space=pltpu.VMEM)
        return pl.pallas_call(
            kernel,
            in_specs=[pl.BlockSpec(memory_space=pltpu.SMEM)] + [in_vmem] * 3,
            out_specs=[in_vmem] * 5,
            out_shape=[
                shaped((rows, shards * lanes), jnp.float32),
                shaped((1, 4 * shards * lanes), jnp.float32),
                shaped((1, 3 * shards * lanes), jnp.float32),
                shaped((length, 1), jnp.int32),
                shaped((length, 1), jnp.float32),
            ],
            name="vectors",
        )(place.scalars, self.slots, seg_row, keep_row)


def pack_sums(late_a, late_b, first_sums, second_sums, inner_sums):
    width = first_sums.shape[1]
    half = late_a.shape[1]

    def kernel(a_ref, b_ref, one_ref, two_ref, inner_ref, out_ref):
        def place_of(n):
            return n // 3 * 8 + n % 3

        out_ref[...] = jnp.zeros_like(out_ref)
        for n in (B_QUERY, B_VALUE):
            at = place_of(n)
            out_ref[at : at + 1, 0:half] = a_ref[n : n + 1, :]
            out_ref[at : at + 1, half:width] = b_ref[n : n + 1, :]
        for n, source, line in (
            (GAIN_ONE, one_ref, 0),
            (SHIFT_ONE, one_ref, 1),
            (B_ATTN, one_ref, 2),
            (GAIN_TWO, two_ref, 0),
            (SHIFT_TWO, two_ref, 1),
            (B_OUT, two_ref, 2),
        ):
            at = place_of(n)
            out_ref[at : at + 1, :] = source[line : line + 1, :]
        for n in range(4):
            at = place_of(B_IN + n)
            for shard in range(width // LANES):
                start = (4 * shard + n) * LANES
                out_ref[at : at + 1, shard * LANES : (shard + 1) * LANES] = inner_ref[
                    :, start : start + LANES
                ]

    in_vmem = pl.BlockSpec(memory_space=pltpu.VMEM)
    return pl.pallas_call(
        kernel,
        in_specs=[in_vmem] * 5,
        out_specs=in_vmem,
        out_shape=shaped((32, width), jnp.float32),
        name="pack_sums",
    )(late_a, late_b, first_sums, second_sums, inner_sums)


def project_qkv(place, rows, window, bias, scale):
    length, width = rows.shape
    cols = window.cols

    def kernel(where, ready, weight, x_ref, bias_ref, scale_ref, out_ref):
        ready()
        at = pl.ds(pl.multiple_of((where[2] ^ pl.program_id(0)) * cols, LANES), cols)
        for tile in range(length // TILE):
            here = pl.ds(tile * TILE, TILE)
            mixed = mxu(x_ref[here, :], weight[:, at], NN) + bias_ref[:, at]
            mixed = mixed.astype(jnp.bfloat16).astype(jnp.float32) * scale_ref[:, at]
            out_ref[here, :] = mixed.astype(jnp.bfloat16)

    total = cols * place.groups
    return weight_call(
        place,
        kernel,
        window,
        (rows, bias, scale),
        [fixed(length, width), fixed(1, total), fixed(1, total)],
        [shaped((length, total), jnp.bfloat16)],
        [pl.BlockSpec((length, cols), lambda i, s: (0, i ^ s[2]))],
        place.groups,
        "grp",
        "qkv",
        2 * length * width * total,
    )


def norm_parts(rows):
    centered = rows - jnp.mean(rows, -1, keepdims=True)
    scale = lax.rsqrt(jnp.mean(centered * centered, -1, keepdims=True) + epsilon)
    return centered * scale, scale


def norm_back(grad, normed, scale):
    return scale * (
        grad
        - jnp.mean(grad, -1, keepdims=True)
        - normed * jnp.mean(grad * normed, -1, keepdims=True)
    )


def add_rows(sum_ref, *terms):
    @pl.when(pl.program_id(0) == 0)
    def _():
        sum_ref[...] = jnp.zeros_like(sum_ref)

    for n, term in enumerate(terms):
        sum_ref[n : n + 1, :] += jnp.sum(term, 0, keepdims=True)


def project_out(place, contexts, window, rows, vectors):
    length, width = rows.shape

    def kernel(where, ready, weight, c_ref, x_ref, v_ref, n_ref, r_ref, low_ref):
        ready()
        first_sum = mxu(c_ref[...], weight[...], NN) + row(v_ref, B_ATTN)
        first_sum = first_sum + x_ref[...].astype(jnp.float32)
        normed, scale = norm_parts(first_sum)
        n_ref[...] = normed
        r_ref[...] = jnp.broadcast_to(scale, r_ref.shape)
        low_ref[...] = (normed * row(v_ref, GAIN_ONE) + row(v_ref, SHIFT_ONE)).astype(jnp.bfloat16)

    return weight_call(
        place,
        kernel,
        window,
        (contexts, rows, vectors),
        [row_tiles(width), row_tiles(width), fixed(*vectors.shape)],
        [
            shaped((length, width), jnp.float32),
            shaped((length, LANES), jnp.float32),
            shaped((length, width), jnp.bfloat16),
        ],
        [row_tiles(width), row_tiles(LANES), row_tiles(width)],
        length // TILE,
        "all",
        "attn_out",
        2 * length * width * width,
    )


def feed_in(place, normed_low, window, bias):
    length, width = normed_low.shape
    cols = window.cols

    def kernel(where, ready, weight, x_ref, bias_ref, hid_ref, slope_ref):
        ready()
        at = pl.ds(pl.multiple_of((where[2] ^ pl.program_id(0)) * cols, LANES), cols)
        for tile in range(length // TILE):
            here = pl.ds(tile * TILE, TILE)
            pre = mxu(x_ref[here, :], weight[:, at], NN) + bias_ref[:, at]
            share = 0.5 + 0.5 * lax.erf(pre * (1.0 / math.sqrt(2.0)))
            bell = jnp.exp(-0.5 * pre * pre) * (1.0 / math.sqrt(2.0 * math.pi))
            hid_ref[here, :] = (pre * share).astype(jnp.bfloat16)
            slope_ref[here, :] = (share + pre * bell).astype(jnp.bfloat16)

    total = cols * place.groups
    block = pl.BlockSpec((length, cols), lambda i, s: (0, i ^ s[2]))
    return weight_call(
        place,
        kernel,
        window,
        (normed_low, bias),
        [fixed(length, width), fixed(1, total)],
        [shaped((length, total), jnp.bfloat16)] * 2,
        [block, block],
        place.groups,
        "grp",
        "feed_in",
        2 * length * width * total,
    )


def feed_out(place, hidden, window, normed, cot, keep, vectors):
    length, inner = hidden.shape
    width = normed.shape[1]

    def kernel(where, ready, weight, h_ref, n_ref, cot_ref, keep_ref, v_ref, *outs):
        out_ref, grad_ref, low_ref, sum_ref = outs
        ready()
        fed = mxu(h_ref[...], weight[...], NN)
        normed_one = n_ref[...] * row(v_ref, GAIN_ONE) + row(v_ref, SHIFT_ONE)
        second_sum = normed_one + (fed + row(v_ref, B_OUT))
        second, scale = norm_parts(second_sum)
        out_ref[...] = (second * row(v_ref, GAIN_TWO) + row(v_ref, SHIFT_TWO)).astype(jnp.bfloat16)
        masked = cot_ref[...].astype(jnp.float32) * keep_ref[...]
        grad = norm_back(masked * row(v_ref, GAIN_TWO), second, scale)
        grad_ref[...] = grad
        low_ref[...] = grad.astype(jnp.bfloat16)
        add_rows(sum_ref, masked * second, masked, grad)

    return weight_call(
        place,
        kernel,
        window,
        (hidden, normed, cot, keep, vectors),
        [row_tiles(inner), row_tiles(width), row_tiles(width), row_tiles(1), fixed(*vectors.shape)],
        [
            shaped((length, width), jnp.bfloat16),
            shaped((length, width), jnp.float32),
            shaped((length, width), jnp.bfloat16),
            shaped((8, width), jnp.float32),
        ],
        [row_tiles(width), row_tiles(width), row_tiles(width), fixed(8, width)],
        length // TILE,
        "all",
        "feed_out",
        2 * length * width * inner,
    )


def feed_out_back(out_low, weight, slope):
    length, width = out_low.shape
    inner = slope.shape[1]
    cols = min(1024, inner)

    def kernel(g_ref, w_ref, slope_ref, pre_ref, sum_ref):
        total = jnp.zeros((1, cols), jnp.float32)
        for tile in range(length // TILE):
            here = pl.ds(tile * TILE, TILE)
            grad = mxu(g_ref[here, :], w_ref[...], NT) * slope_ref[here, :].astype(jnp.float32)
            pre_ref[here, :] = grad.astype(jnp.bfloat16)
            total = total + jnp.sum(grad, 0, keepdims=True)
        sum_ref[...] = total

    block = pl.BlockSpec((length, cols), lambda i: (0, i))
    return plain_call(
        kernel,
        (out_low, weight, slope),
        [fixed(length, width), pl.BlockSpec((cols, width), lambda i: (i, 0)), block],
        [shaped((length, inner), jnp.bfloat16), shaped((1, inner), jnp.float32)],
        [block, pl.BlockSpec((1, cols), lambda i: (0, i))],
        inner // cols,
        "feed_out_back",
        2 * length * width * inner,
    )


def feed_in_back(pre_low, weight, second_grad, normed, scale, vectors, attn_weight):
    length, inner = pre_low.shape
    width = normed.shape[1]

    def kernel(p_ref, w_ref, g_ref, n_ref, r_ref, v_ref, a_ref, first_ref, low_ref, ctx_ref, sum_ref):
        grad = g_ref[...] + mxu(p_ref[...], w_ref[...], NT)
        first = norm_back(grad * row(v_ref, GAIN_ONE), n_ref[...], r_ref[:, :1])
        low = first.astype(jnp.bfloat16)
        first_ref[...] = first
        low_ref[...] = low
        ctx_ref[...] = mxu(low, a_ref[...], NT).astype(jnp.bfloat16)
        add_rows(sum_ref, grad * n_ref[...], grad, first)

    return plain_call(
        kernel,
        (pre_low, weight, second_grad, normed, scale, vectors, attn_weight),
        [
            row_tiles(inner),
            whole_once(weight.shape),
            row_tiles(width),
            row_tiles(width),
            row_tiles(LANES),
            fixed(*vectors.shape),
            whole_once(attn_weight.shape),
        ],
        [
            shaped((length, width), jnp.float32),
            shaped((length, width), jnp.bfloat16),
            shaped((length, width), jnp.bfloat16),
            shaped((8, width), jnp.float32),
        ],
        [row_tiles(width), row_tiles(width), row_tiles(width), fixed(8, width)],
        length // TILE,
        "feed_in_back",
        2 * length * width * (inner + width),
    )


def project_qkv_back(grads, weight, first_grad, start, tiles, before=None):
    length, width = first_grad.shape
    part = width // len(grads)

    def kernel(w_ref, *refs):
        grad_refs, first_ref, out_ref = refs[: len(grads)], refs[len(grads)], refs[-1]
        total = first_ref[...]
        for n in range(3):
            for m, grad_ref in enumerate(grad_refs):
                at = n * width + m * part
                total = total + mxu(grad_ref[n], w_ref[:, at : at + part], NT)
        out_ref[...] = total

    tile = pl.BlockSpec((TILE, width), lambda i: (start + i, 0))
    more = () if before is None else (before,)
    return pl.pallas_call(
        kernel,
        grid=(tiles,),
        in_specs=[whole_once(weight.shape)]
        + [pl.BlockSpec((3, TILE, part), lambda i: (0, start + i, 0))] * len(grads)
        + [tile]
        + [pl.BlockSpec(memory_space=pl.ANY)] * len(more),
        out_specs=tile,
        out_shape=shaped((length, width), jnp.float32),
        input_output_aliases={} if before is None else {len(grads) + 2: 0},
        compiler_params=params(60),
        cost_estimate=cost(6 * tiles * TILE * width * width),
        name="qkv_back",
    )(weight, *grads, first_grad, *more)


ORDER = (1, 3, 0, 2)


def ordered_slot(j):
    return jnp.where(j < 2, 2 * j + 1, 2 * j - 4)


def weight_grad_kernel(where, left_ref, right_ref, own, sent, kept, *, rows, groups, split):
    core = where[0]
    chips = left_ref.shape[1] // (2 * rows)

    @pl.when(pl.program_id(1) == 0)
    def _():
        for side in range(2):
            chosen = []
            for k in range(chips):
                even = left_ref[:, 2 * k * rows : (2 * k + 1) * rows]
                odd = left_ref[:, (2 * k + 1) * rows : (2 * k + 2) * rows]
                chosen.append(jnp.where(core == side, even, odd))
            left = chosen[0] if chips == 1 else jnp.concatenate(chosen, 1)
            kept[side] = left.T

    if split:
        size = min(512, right_ref.shape[1])
        for ref, side in ((sent, 1), (own, 0)):
            for n in range(right_ref.shape[1] // size):
                at = slice(n * size, (n + 1) * size)
                part = mxu(kept[side], right_ref[:, at], NN).astype(jnp.bfloat16)
                ref[0, :, :, at] = part.reshape(chips, rows, size)
    else:
        cols = right_ref.shape[1] // groups
        for ref, side in ((sent, 1), (own, 0)):
            for pos, slot in enumerate(ORDER):
                start = pl.multiple_of((where[2] ^ turn(slot, core ^ side)) * cols, LANES)
                part = mxu(kept[side], right_ref[:, pl.ds(start, cols)], NN)
                ref[pos] = part.astype(jnp.bfloat16).reshape(chips, rows, cols)


def attention_grads_kernel(where, *refs, rows, groups, extra):
    left_ref, right_ref, *refs = refs
    *more, own, sent, kept = refs
    core, grp = where[0], where[2]
    chips = left_ref.shape[1] // (2 * rows)
    step = pl.program_id(0)

    def keep_rows(ref):
        for side in range(2):
            chosen = []
            for k in range(chips):
                even = ref[:, 2 * k * rows : (2 * k + 1) * rows]
                odd = ref[:, (2 * k + 1) * rows : (2 * k + 2) * rows]
                chosen.append(jnp.where(core == side, even, odd))
            kept[side] = jnp.concatenate(chosen, 1).T

    def scatter(right, at, cols):
        for ref, side in ((sent, 1), (own, 0)):
            part = mxu(kept[side], right, NN).astype(jnp.bfloat16)
            for g in range(groups):
                pos = position(grp ^ g, core ^ side)
                block = part[:, g * cols : (g + 1) * cols].reshape(chips, rows, cols)
                ref[pos, :, 0:rows, pl.ds(at, cols)] = block

    skip = 0
    if not extra:
        other_left, other_right = more
        skip = other_right.shape[1] // groups

    @pl.when(step == 0)
    def _():
        if not extra:
            keep_rows(other_left)
            scatter(other_right[...], 0, skip)
        keep_rows(left_ref)

    cols = right_ref.shape[2] // groups
    scatter(right_ref[0], pl.multiple_of(skip + step * cols, LANES), cols)

    if extra:
        (sums_ref,) = more

        @pl.when(step == 2)
        def _():
            blank = jnp.zeros((extra, own.shape[3]), jnp.bfloat16)
            for ref, side in ((sent, 1), (own, 0)):
                for g in range(groups):
                    pos = position(grp ^ g, core ^ side)
                    for k in range(chips):
                        start = pl.multiple_of((2 * k + (core ^ side)) * LANES, LANES)
                        ref[pos, k, rows : rows + extra, :] = blank
                        lines = sums_ref[8 * g : 8 * g + 8, pl.ds(start, LANES)]
                        for n in range(3):
                            ref[pos, k, rows : rows + 1, n * LANES : (n + 1) * LANES] = lines[
                                n : n + 1
                            ].astype(jnp.bfloat16)


def position(distance, core):
    slot = turn(distance, core)
    return jnp.where(slot == 0, 2, jnp.where(slot == 1, 0, jnp.where(slot == 3, 1, 3)))


def attention_grads(place, left, right, more, name):
    tokens, height = left.shape
    groups, chips = place.groups, place.chips
    rows = height // place.shards
    extra = 16 if len(more) == 1 else 0
    size = right.shape[2]
    cols = 3 * size // groups + (0 if extra else more[1].shape[1] // groups)
    shape = (groups, chips, rows + extra, cols)
    once = [
        pl.BlockSpec(x.shape, lambda i, s: (0, 0), pipeline_mode=pl.Buffered(1)) for x in more
    ]
    return pl.pallas_call(
        functools.partial(attention_grads_kernel, rows=rows, groups=groups, extra=extra),
        grid_spec=pltpu.PrefetchScalarGridSpec(
            num_scalar_prefetch=1,
            grid=(3,),
            in_specs=[
                pl.BlockSpec(left.shape, lambda i, s: (0, 0), pipeline_mode=pl.Buffered(1)),
                pl.BlockSpec((1, tokens, size), lambda i, s: (i, 0, 0)),
            ]
            + once,
            out_specs=[pl.BlockSpec(shape, lambda i, s: (0, 0, 0, 0))] * 2,
            scratch_shapes=[pltpu.VMEM((2, height // 2, tokens), jnp.bfloat16)],
        ),
        out_shape=[shaped(shape, jnp.bfloat16)] * 2,
        compiler_params=params(60),
        cost_estimate=cost(2 * tokens * height * cols * groups),
        name="wgrad_" + name,
    )(place.scalars, left, right, *more)


def weight_grad(place, left, right, split, name):
    tokens, height = left.shape
    groups, chips = place.groups, place.chips
    rows = height // place.shards
    step_chips = chips if split else max(1, 1024 // (2 * rows))
    cols = right.shape[1] // groups
    if split:
        grid = (1, groups)
        block = lambda i, j, s: (0, s[2] ^ turn(ordered_slot(j), s[0]))
        right_spec = pl.BlockSpec((tokens, cols), block)
        one = (1, chips, rows, cols)
        other = lambda j: jnp.where(j == 0, 3, jnp.where(j == 3, 0, j))
        out_specs = [
            pl.BlockSpec(one, lambda i, j, s: (j, 0, 0, 0)),
            pl.BlockSpec(one, lambda i, j, s: (other(j), 0, 0, 0)),
        ]
    else:
        grid = (chips // step_chips, 1)
        right_spec = pl.BlockSpec(right.shape, lambda i, j, s: (0, 0))
        out_specs = [
            pl.BlockSpec((groups, step_chips, rows, cols), lambda i, j, s: (0, i, 0, 0))
        ] * 2
    return pl.pallas_call(
        functools.partial(weight_grad_kernel, rows=rows, groups=groups, split=split),
        grid_spec=pltpu.PrefetchScalarGridSpec(
            num_scalar_prefetch=1,
            grid=grid,
            in_specs=[
                pl.BlockSpec((tokens, step_chips * 2 * rows), lambda i, j, s: (0, i)),
                right_spec,
            ],
            out_specs=out_specs,
            scratch_shapes=[pltpu.VMEM((2, step_chips * rows, tokens), jnp.bfloat16)],
        ),
        out_shape=[shaped((groups, chips, rows, cols), jnp.bfloat16)] * 2,
        compiler_params=params(60),
        cost_estimate=cost(2 * tokens * height * cols * groups),
        name="wgrad_" + name,
    )(place.scalars, left, right)


def add(*terms):
    total = terms[0].astype(jnp.float32)
    for term in terms[1:]:
        total = total + term.astype(jnp.float32)
    return total.astype(jnp.bfloat16)


class Reduction:
    def __init__(self, place, made):
        self.place = place
        self.made, sent = made
        self.flying = place.swap_core(sent)

    def near(self):
        self.core = self.flying
        leave = add(self.made[:2], self.core[:2])
        self.flying = self.place.swap_grp(leave, 0)
        return leave

    def middle(self):
        self.first = self.flying
        second = add(self.made[3], self.core[3], self.first[1])
        self.flying = self.place.swap_grp(second, 1)
        return second

    def column(self):
        mine = add(self.made[2], self.core[2], self.first[0], self.flying)
        return mine, lambda chip: lax.dynamic_index_in_dim(mine, chip, 0, False)

    def along(self):
        place = self.place
        mine, at = self.column()
        self.mine = [at(place.slot_chip(slot)) for slot in range(4)]
        both = jnp.stack([self.mine[1], self.mine[3]])
        self.flying = place.swap_chip(both, 0)
        return both

    def along_far(self):
        self.first = self.flying
        second = add(self.mine[2], self.first[1])
        self.flying = self.place.swap_chip(second, 1)
        return second

    def share(self):
        return add(self.mine[0], self.first[0], self.flying)

    def along_direct(self):
        place = self.place
        mine, at = self.column()
        self.mine = at(place.chip)
        self.flying = tuple(
            place.permute(at(place.chip ^ k), (2 * k, 2 * k)) for k in range(place.chips - 1, 0, -1)
        )
        return mine

    def share_direct(self):
        return add(self.mine, *self.flying)


class Replication:
    def __init__(self, place, share, direct=False):
        self.place = place
        self.blocks = [share] + [None] * 3
        if direct:
            size = place.shards
            for mask in (3, 1, 2):
                self.blocks[mask] = place.permute(share, (mask * size, mask * size))
        else:
            self.flying = place.swap_grp(share, 0)

    def far(self):
        pair = jnp.stack([self.blocks[0], self.flying])
        self.blocks[1] = self.flying
        self.flying = self.place.swap_grp(pair, 1)
        return pair

    def landed(self):
        if self.blocks[2] is None:
            self.blocks[2:] = [self.flying[0], self.flying[1]]
        return self.blocks


def order_feed_forward(place, blocks, rows_in):
    groups = place.groups
    height, cols = blocks[0].shape
    rows_out = height - groups * rows_in

    def kernel(where, *refs):
        *blocks, out_ref, in_ref = refs
        for slot, ref in enumerate(blocks):
            g = where[2] ^ turn(slot, where[0])
            at = pl.multiple_of(g * cols, LANES)
            out_ref[:, pl.ds(at, cols)] = ref[0:rows_out, :].astype(jnp.float32)
            for n in range(groups):
                at = pl.multiple_of((g * groups + n) * cols, LANES)
                part = ref[rows_out + n * rows_in : rows_out + (n + 1) * rows_in, :]
                in_ref[:, pl.ds(at, cols)] = part.astype(jnp.float32)

    in_vmem = pl.BlockSpec(memory_space=pltpu.VMEM)
    return pl.pallas_call(
        kernel,
        in_specs=[pl.BlockSpec(memory_space=pltpu.SMEM)] + [in_vmem] * groups,
        out_specs=[in_vmem] * 2,
        out_shape=[
            shaped((rows_out, groups * cols), jnp.float32),
            shaped((rows_in, groups * groups * cols), jnp.float32),
        ],
        compiler_params=params(40),
        cost_estimate=cost(height * cols * 1024),
        name="order_feed_forward",
    )(place.scalars, *blocks)


def order_attention(place, blocks_a, blocks_b, rows):
    groups = place.groups
    size = blocks_b[0].shape[1] // 3
    skip = blocks_a[0].shape[1] - 3 * size
    width = groups * skip

    def kernel(where, *refs):
        *blocks, attn_ref, qkv_ref, small_ref = refs
        for n in range(groups):
            ref = blocks[n]
            g = where[2] ^ turn(n, where[0])
            attn_ref[:, pl.ds(pl.multiple_of(g * skip, LANES), skip)] = ref[:, 0:skip].astype(
                jnp.float32
            )
            for part in range(3):
                at = pl.multiple_of(part * width + g * size, LANES)
                block = ref[:, skip + part * size : skip + (part + 1) * size]
                qkv_ref[:, pl.ds(at, size)] = block.astype(jnp.float32)
        for n in range(groups):
            ref = blocks[groups + n]
            g = where[2] ^ n
            lines = []
            for part in range(3):
                at = pl.multiple_of(part * width + width // 2 + g * size, LANES)
                here = slice(part * size, (part + 1) * size)
                qkv_ref[:, pl.ds(at, size)] = ref[0:rows, here].astype(jnp.float32)
                lines.append(ref[rows : rows + 16, here].astype(jnp.float32)[0:1])
            lines.append(jnp.zeros((5, size), jnp.float32))
            small_ref[pl.ds(pl.multiple_of(g * 8, 8), 8), :] = jnp.concatenate(lines)

    in_vmem = pl.BlockSpec(memory_space=pltpu.VMEM)
    return pl.pallas_call(
        kernel,
        in_specs=[pl.BlockSpec(memory_space=pltpu.SMEM)] + [in_vmem] * (2 * groups),
        out_specs=[in_vmem] * 3,
        out_shape=[
            shaped((rows, width), jnp.float32),
            shaped((rows, 3 * width), jnp.float32),
            shaped((8 * groups, size), jnp.float32),
        ],
        compiler_params=params(40),
        name="order_attention",
    )(place.scalars, *blocks_a, *blocks_b)


def on_device_permutes(
    tokens,
    segment_ids,
    keep_flag,
    cotangent,
    w_qkv,
    b_query,
    b_value,
    w_attn_out,
    b_attn_out,
    norm1_gain,
    norm1_bias,
    w_in,
    b_in,
    w_out,
    b_out,
    norm2_gain,
    norm2_bias,
    *,
    groups,
    shards,
):
    place = Place(groups, shards)
    _, length, width = tokens.shape
    rows = tokens[0]
    seg_row = segment_ids.reshape(1, length)
    pairs = width // LANES

    c1 = Gather(place, w_qkv)
    c2 = Gather(place, jnp.concatenate([w_in, w_attn_out], 1))
    c3 = Gather(place, w_out)
    c1.chips_near()
    small = Vectors(
        place,
        (b_query, b_value, b_attn_out, norm1_gain, norm1_bias, b_out, norm2_gain, norm2_bias, b_in),
    )
    meet(rows, c1, small)
    pair = c1.chips_far()
    small.chips_near()
    meet(pair, c1, small)
    joined = c1.join()
    c1.near()
    small.chips_far()
    c2.chips_near(joined)
    meet(joined, c2, small)
    small.landed()
    pair = c2.chips_far()
    vectors, bias_in, qkv_bias, seg_col, keep = small.unpack(
        seg_row, keep_flag.reshape(1, length)
    )
    c1.flying = lax.optimization_barrier(c1.flying)
    c1.far(pair, vectors)
    c1.cross(0, 1, 2)
    joined = c2.join()
    meet(joined, c1)
    c1.landed()
    c2.near(c1.held[3])
    c1.cross(3)
    c3.chips_near(c1.held[3])
    blank = jnp.ones((1, width), jnp.float32)
    qkv_scale = jnp.concatenate([blank / math.sqrt(HD), blank, blank], 1)

    mixed, full_qkv = project_qkv(place, rows, Window(c1, 0, w_qkv.shape[1]), qkv_bias, qkv_scale)
    meet(mixed, c3)
    pair = c3.chips_far()
    c2.cross(0, wait=(mixed,))
    first, second = pairs * 3 // 8, pairs * 3 // 4
    forward = attention_forward(after(mixed, pair), seg_col, seg_row, 0, first)
    meet(forward[0], c2, c3)
    c2.far()
    joined = c3.join()
    c3.near()
    c2.cross(1, 2)
    forward = attention_forward(
        after(mixed, joined), seg_col, seg_row, first, second - first, forward
    )
    meet(forward[0], c2)
    c2.landed()
    c2.cross(3)
    contexts, probs = attention_forward(
        after(mixed, c2.held[3]), seg_col, seg_row, second, pairs - second, forward
    )
    normed, scale_one, normed_low, full_attn = project_out(
        place, contexts, Window(c2, w_in.shape[1], w_attn_out.shape[1]), rows, vectors
    )
    meet(normed_low, c3)
    c3.far()
    c3.cross(0, 1, 2)
    hidden, slope, full_in = feed_in(
        place, after(normed_low, c3.held[1]), Window(c2, 0, w_in.shape[1]), bias_in
    )
    meet(hidden, c3)
    c3.landed()
    c3.cross(3)
    layer_out, second_grad, out_low, second_sums, full_out = feed_out(
        place, hidden, Window(c3, 0, w_out.shape[1]), normed, cotangent[0], keep, vectors
    )

    r_out = Reduction(place, weight_grad(place, hidden, out_low, False, "out"))
    pre_low, bias_in_grad = feed_out_back(after(out_low, r_out.made), full_out, slope)
    meet(pre_low, r_out)
    step = r_out.near()
    r_in = Reduction(place, weight_grad(place, after(normed_low, step), pre_low, True, "in"))
    first_grad, attn_low, context_grad, first_sums = feed_in_back(
        after(pre_low, r_in.made), full_in, second_grad, normed, scale_one, vectors, full_attn
    )
    meet(attn_low, r_in)
    step = r_in.near()
    half, quarter = pairs // 2, pairs // 4

    def back(wait, start, count, at, before=None):
        return attention_backward(
            mixed,
            contexts,
            after(context_grad, *wait),
            probs,
            start,
            count,
            at,
            half,
            before,
        )

    low_a, late_a = back((step,), 0, half, 0)
    meet(late_a, r_out, r_in)
    steps = (r_out.middle(), r_in.middle())
    r_a = Reduction(
        place, attention_grads(place, after(rows, *steps), low_a, (contexts, attn_low), "a")
    )
    meet(r_a.made, r_out)
    step = r_out.along()
    part = back((r_a.made, step), half, quarter, 0)
    meet(part[1], r_out, r_in, r_a)
    steps = (r_out.along_far(), r_in.along(), r_a.near())
    low_b, late_b = back(steps, half + quarter, quarter, quarter, part)
    meet(late_b, r_out, r_in, r_a)
    sums = pack_sums(late_a, late_b, first_sums, second_sums, bias_in_grad)
    share_out = r_out.share()
    steps = (r_in.along_far(), r_a.middle(), share_out)
    r_b = Reduction(place, attention_grads(place, after(rows, *steps), low_b, (sums,), "b"))
    meet(r_b.made, r_in, r_a)
    share_in = r_in.share()
    inner = share_in.shape[1] // groups
    joined = jnp.concatenate(
        [share_out] + [share_in[:, n * inner : (n + 1) * inner] for n in range(groups)]
    )
    all_ffn = Replication(place, joined)
    grads = (low_a, after(low_b, r_b.made, joined, r_a.along()))
    tiles = length // TILE // 2
    input_grad = project_qkv_back(grads, full_qkv, first_grad, 0, tiles)
    meet(input_grad, r_b, r_a, all_ffn)
    steps = (r_b.near(), r_a.along_far())
    input_grad = project_qkv_back(
        grads, full_qkv, after(first_grad, *steps), tiles, tiles, input_grad
    )
    meet(input_grad, r_b, r_a)
    middle = r_b.middle()
    r_a.flying = after(r_a.flying, middle)
    all_a = Replication(place, r_a.share())
    meet(all_a.blocks[0], r_b, all_a)
    along = r_b.along_direct()
    all_a.flying = after(all_a.flying, along)
    all_ffn.flying = after(all_ffn.flying, along)
    pairs_made = (all_a.far(), all_ffn.far())
    meet(pairs_made, r_b)
    share_b = r_b.share_direct()
    all_b = Replication(place, share_b, direct=True)
    meet(share_b, all_ffn)
    w_out_grad, w_in_grad = order_feed_forward(place, all_ffn.landed(), share_in.shape[0])
    all_a.flying = after(all_a.flying, w_out_grad)
    w_attn_grad, w_qkv_grad, small = order_attention(
        place, all_a.landed(), all_b.landed(), w_attn_out.shape[0]
    )
    small = [small[8 * (n // 3) + n % 3] for n in range(12)]
    return (
        layer_out[None],
        input_grad[None],
        w_qkv_grad,
        small[B_QUERY],
        small[B_VALUE],
        w_attn_grad,
        small[B_ATTN],
        small[GAIN_ONE],
        small[SHIFT_ONE],
        w_in_grad,
        jnp.concatenate(small[B_IN:]),
        w_out_grad,
        small[B_OUT],
        small[GAIN_TWO],
        small[SHIFT_TWO],
    )


def solution(mesh):
    groups, shards = mesh.shape["grp"], mesh.shape["shard"]
    if groups == 4 and shards == 8:
        body = functools.partial(on_device_permutes, groups=groups, shards=shards)
    else:
        body = on_device
    return jax.shard_map(
        body,
        mesh=mesh,
        in_specs=(
            P(("grp", "shard"), None, None),
            P(("grp", "shard"), None),
            P(("grp", "shard"), None),
            P(("grp", "shard"), None, None),
            P("shard", "grp"),
            P("shard"),
            P("shard"),
            P("shard", "grp"),
            P("shard"),
            P("shard"),
            P("shard"),
            P("shard", "grp"),
            P("shard"),
            P("shard", "grp"),
            P("shard"),
            P("shard"),
            P("shard"),
        ),
        out_specs=(
            P(("grp", "shard"), None, None),
            P(("grp", "shard"), None, None),
            P("shard", None),
            P("shard"),
            P("shard"),
            P("shard", None),
            P("shard"),
            P("shard"),
            P("shard"),
            P("shard", None),
            P("shard"),
            P("shard", None),
            P("shard"),
            P("shard"),
            P("shard"),
        ),
        check_vma=False,
    )
```

```python
import functools
import math

import jax
import jax.numpy as jnp
from jax import lax
from jax.experimental import pallas as pl
from jax.experimental.pallas import tpu as pltpu
from jax.sharding import PartitionSpec as P

H = 16
HD = 64


masked_score = -1e30
epsilon = 1e-05


def norm_layer(rows, gain_row, shift_row):
    row_mean = jnp.mean(rows, -1, keepdims=True)
    centered = rows - row_mean
    row_var = jnp.mean(centered * centered, -1, keepdims=True)
    return centered * lax.rsqrt(row_var + epsilon) * gain_row + shift_row


def gelu_exact(values):
    return 0.5 * values * (1.0 + lax.erf(values * (1.0 / math.sqrt(2.0))))


def contract_rows(left, right):
    return lax.dot_general(
        left, right, (((0,), (0,)), ((), ())), preferred_element_type=jnp.float32
    )


def contract_cols(left, right):
    return lax.dot_general(
        left, right, (((1,), (1,)), ((), ())), preferred_element_type=jnp.float32
    )


def attend_forward(queries, key_rows, value_rows, segment_row, block_rows):
    length, model_width = queries.shape
    scaling = 1.0 / math.sqrt(HD)
    key_heads = key_rows.reshape(length, H, HD)
    value_heads = value_rows.reshape(length, H, HD)
    query_blocks = queries.reshape(length // block_rows, block_rows, H, HD)
    segment_blocks = segment_row.reshape(length // block_rows, block_rows)

    def one_block(pieces):
        query_part, segment_part = pieces
        scores = (
            jnp.einsum("qhd,khd->hqk", query_part, key_heads, preferred_element_type=jnp.float32)
            * scaling
        )
        allowed = segment_part[:, None] == segment_row[None, :]
        scores = jnp.where(allowed[None], scores, masked_score)
        row_max = jnp.max(scores, -1, keepdims=True)
        powers = jnp.exp(scores - row_max)
        totals = jnp.sum(powers, -1, keepdims=True)
        attn_probs = (powers / totals).astype(jnp.bfloat16)
        context = jnp.einsum(
            "hqk,khd->qhd", attn_probs, value_heads, preferred_element_type=jnp.float32
        )
        return (
            context.reshape(block_rows, model_width).astype(jnp.bfloat16),
            (row_max + jnp.log(totals))[:, :, 0],
        )

    contexts, log_sums = lax.map(one_block, (query_blocks, segment_blocks))
    return (contexts.reshape(length, model_width), log_sums)


def attend_backward(queries, key_rows, value_rows, segment_row, log_sums, context_grad, block_rows):
    length, model_width = queries.shape
    scaling = 1.0 / math.sqrt(HD)
    key_heads = key_rows.reshape(length, H, HD)
    value_heads = value_rows.reshape(length, H, HD)
    query_blocks = queries.reshape(length // block_rows, block_rows, H, HD)
    segment_blocks = segment_row.reshape(length // block_rows, block_rows)
    grad_blocks = context_grad.reshape(length // block_rows, block_rows, H, HD)

    def one_block(running, pieces):
        key_acc, value_acc = running
        query_part, segment_part, lse_part, grad_part = pieces
        scores = (
            jnp.einsum("qhd,khd->hqk", query_part, key_heads, preferred_element_type=jnp.float32)
            * scaling
        )
        allowed = segment_part[:, None] == segment_row[None, :]
        scores = jnp.where(allowed[None], scores, masked_score)
        probs = jnp.exp(scores - lse_part[:, :, None])
        prob_low = probs.astype(jnp.bfloat16)
        prob_grad = jnp.einsum(
            "qhd,khd->hqk", grad_part, value_heads, preferred_element_type=jnp.float32
        )
        row_dot = jnp.sum(prob_grad * probs, -1, keepdims=True)
        score_grad = (probs * (prob_grad - row_dot)).astype(jnp.bfloat16)
        query_grad = (
            jnp.einsum("hqk,khd->qhd", score_grad, key_heads, preferred_element_type=jnp.float32)
            * scaling
        )
        key_acc = (
            key_acc
            + jnp.einsum("hqk,qhd->khd", score_grad, query_part, preferred_element_type=jnp.float32)
            * scaling
        )
        value_acc = value_acc + jnp.einsum(
            "hqk,qhd->khd", prob_low, grad_part, preferred_element_type=jnp.float32
        )
        return ((key_acc, value_acc), query_grad.reshape(block_rows, model_width))

    empty_acc = jnp.zeros((length, H, HD), jnp.float32)
    (key_grad, value_grad), query_grads = lax.scan(
        one_block, (empty_acc, empty_acc), (query_blocks, segment_blocks, log_sums, grad_blocks)
    )
    return (
        query_grads.reshape(length, model_width),
        key_grad.reshape(length, model_width),
        value_grad.reshape(length, model_width),
    )


def on_device(
    tokens,
    segment_ids,
    keep_flag,
    cotangent,
    w_qkv,
    b_query,
    b_value,
    w_attn_out,
    b_attn_out,
    norm1_gain,
    norm1_bias,
    w_in,
    b_in,
    w_out,
    b_out,
    norm2_gain,
    norm2_bias,
):
    seq_count, length, model_width = tokens.shape
    block_rows = min(512, length)
    within = (
        lax.all_gather(w_qkv, "shard", axis=0, tiled=True),
        lax.all_gather(w_attn_out, "shard", axis=0, tiled=True),
        lax.all_gather(w_in, "shard", axis=0, tiled=True),
        lax.all_gather(w_out, "shard", axis=0, tiled=True),
        lax.all_gather(b_query, "shard", axis=0, tiled=True),
        lax.all_gather(b_value, "shard", axis=0, tiled=True),
        lax.all_gather(b_attn_out, "shard", axis=0, tiled=True),
        lax.all_gather(norm1_gain, "shard", axis=0, tiled=True),
        lax.all_gather(norm1_bias, "shard", axis=0, tiled=True),
        lax.all_gather(b_in, "shard", axis=0, tiled=True),
        lax.all_gather(b_out, "shard", axis=0, tiled=True),
        lax.all_gather(norm2_gain, "shard", axis=0, tiled=True),
        lax.all_gather(norm2_bias, "shard", axis=0, tiled=True),
    )
    full_qkv, full_attn, full_in, full_out = (
        lax.all_gather(within[0], "grp", axis=1, tiled=True),
        lax.all_gather(within[1], "grp", axis=1, tiled=True),
        lax.all_gather(within[2], "grp", axis=1, tiled=True),
        lax.all_gather(within[3], "grp", axis=1, tiled=True),
    )
    (
        bias_query,
        bias_value,
        bias_attn,
        gain_one,
        shift_one,
        bias_in,
        bias_out,
        gain_two,
        shift_two,
    ) = [piece.astype(jnp.float32) for piece in within[4:]]
    flat_rows = tokens.reshape(seq_count * length, model_width)
    mixed_qkv = jnp.dot(flat_rows, full_qkv, preferred_element_type=jnp.float32)
    queries = (mixed_qkv[:, :model_width] + bias_query).astype(jnp.bfloat16)
    key_rows = mixed_qkv[:, model_width : 2 * model_width].astype(jnp.bfloat16)
    value_rows = (mixed_qkv[:, 2 * model_width :] + bias_value).astype(jnp.bfloat16)
    query_seqs = queries.reshape(seq_count, length, model_width)
    key_seqs = key_rows.reshape(seq_count, length, model_width)
    value_seqs = value_rows.reshape(seq_count, length, model_width)

    def forward_sequence(pieces):
        return attend_forward(pieces[0], pieces[1], pieces[2], pieces[3], block_rows)

    contexts, log_sums = lax.map(forward_sequence, (query_seqs, key_seqs, value_seqs, segment_ids))
    contexts = contexts.reshape(seq_count * length, model_width)
    attended = jnp.dot(contexts, full_attn, preferred_element_type=jnp.float32) + bias_attn
    first_sum = flat_rows.astype(jnp.float32) + attended
    normed_one, norm_one_back = jax.vjp(norm_layer, first_sum, gain_one, shift_one)
    normed_low = normed_one.astype(jnp.bfloat16)
    hidden_pre = jnp.dot(normed_low, full_in, preferred_element_type=jnp.float32) + bias_in
    hidden, gelu_back = jax.vjp(gelu_exact, hidden_pre)
    hidden_low = hidden.astype(jnp.bfloat16)
    second_sum = normed_one + (
        jnp.dot(hidden_low, full_out, preferred_element_type=jnp.float32) + bias_out
    )
    result, norm_two_back = jax.vjp(norm_layer, second_sum, gain_two, shift_two)
    layer_out = result.astype(jnp.bfloat16).reshape(seq_count, length, model_width)
    again = (
        lax.all_gather(w_qkv, "shard", axis=0, tiled=True),
        lax.all_gather(w_attn_out, "shard", axis=0, tiled=True),
        lax.all_gather(w_in, "shard", axis=0, tiled=True),
        lax.all_gather(w_out, "shard", axis=0, tiled=True),
    )
    back_qkv, back_attn, back_in, back_out = (
        lax.all_gather(again[0], "grp", axis=1, tiled=True),
        lax.all_gather(again[1], "grp", axis=1, tiled=True),
        lax.all_gather(again[2], "grp", axis=1, tiled=True),
        lax.all_gather(again[3], "grp", axis=1, tiled=True),
    )
    masked_cot = cotangent.astype(jnp.float32).reshape(
        seq_count * length, model_width
    ) * keep_flag.reshape(seq_count * length, 1).astype(jnp.float32)
    second_grad, gain_two_grad, shift_two_grad = norm_two_back(masked_cot)
    bias_out_grad = jnp.sum(second_grad, 0)
    out_low = second_grad.astype(jnp.bfloat16)
    w_out_grad = contract_rows(hidden_low, out_low)
    hidden_grad = contract_cols(out_low, back_out)
    (pre_grad,) = gelu_back(hidden_grad)
    bias_in_grad = jnp.sum(pre_grad, 0)
    pre_low = pre_grad.astype(jnp.bfloat16)
    w_in_grad = contract_rows(normed_low, pre_low)
    normed_grad = second_grad + contract_cols(pre_low, back_in)
    first_grad, gain_one_grad, shift_one_grad = norm_one_back(normed_grad)
    bias_attn_grad = jnp.sum(first_grad, 0)
    attn_low = first_grad.astype(jnp.bfloat16)
    w_attn_grad = contract_rows(contexts, attn_low)
    context_grad = contract_cols(attn_low, back_attn).astype(jnp.bfloat16)

    def backward_sequence(pieces):
        return attend_backward(
            pieces[0], pieces[1], pieces[2], pieces[3], pieces[4], pieces[5], block_rows
        )

    query_grad, key_grad, value_grad = lax.map(
        backward_sequence,
        (
            query_seqs,
            key_seqs,
            value_seqs,
            segment_ids,
            log_sums,
            context_grad.reshape(seq_count, length, model_width),
        ),
    )
    query_grad = query_grad.reshape(seq_count * length, model_width)
    key_grad = key_grad.reshape(seq_count * length, model_width)
    value_grad = value_grad.reshape(seq_count * length, model_width)
    bias_query_grad = jnp.sum(query_grad, 0)
    bias_value_grad = jnp.sum(value_grad, 0)
    qkv_low = jnp.concatenate([query_grad, key_grad, value_grad], 1).astype(jnp.bfloat16)
    w_qkv_grad = contract_rows(flat_rows, qkv_low)
    input_grad = first_grad + contract_cols(qkv_low, back_qkv)
    reduced = (
        lax.psum_scatter(
            w_qkv_grad.astype(jnp.bfloat16), "shard", scatter_dimension=0, tiled=True
        ).astype(jnp.float32),
        lax.psum_scatter(
            bias_query_grad.astype(jnp.bfloat16), "shard", scatter_dimension=0, tiled=True
        ).astype(jnp.float32),
        lax.psum_scatter(
            bias_value_grad.astype(jnp.bfloat16), "shard", scatter_dimension=0, tiled=True
        ).astype(jnp.float32),
        lax.psum_scatter(
            w_attn_grad.astype(jnp.bfloat16), "shard", scatter_dimension=0, tiled=True
        ).astype(jnp.float32),
        lax.psum_scatter(
            bias_attn_grad.astype(jnp.bfloat16), "shard", scatter_dimension=0, tiled=True
        ).astype(jnp.float32),
        lax.psum_scatter(
            gain_one_grad.astype(jnp.bfloat16), "shard", scatter_dimension=0, tiled=True
        ).astype(jnp.float32),
        lax.psum_scatter(
            shift_one_grad.astype(jnp.bfloat16), "shard", scatter_dimension=0, tiled=True
        ).astype(jnp.float32),
        lax.psum_scatter(
            w_in_grad.astype(jnp.bfloat16), "shard", scatter_dimension=0, tiled=True
        ).astype(jnp.float32),
        lax.psum_scatter(
            bias_in_grad.astype(jnp.bfloat16), "shard", scatter_dimension=0, tiled=True
        ).astype(jnp.float32),
        lax.psum_scatter(
            w_out_grad.astype(jnp.bfloat16), "shard", scatter_dimension=0, tiled=True
        ).astype(jnp.float32),
        lax.psum_scatter(
            bias_out_grad.astype(jnp.bfloat16), "shard", scatter_dimension=0, tiled=True
        ).astype(jnp.float32),
        lax.psum_scatter(
            gain_two_grad.astype(jnp.bfloat16), "shard", scatter_dimension=0, tiled=True
        ).astype(jnp.float32),
        lax.psum_scatter(
            shift_two_grad.astype(jnp.bfloat16), "shard", scatter_dimension=0, tiled=True
        ).astype(jnp.float32),
    )
    summed = (
        lax.psum(reduced[0].astype(jnp.bfloat16), "grp").astype(jnp.float32),
        lax.psum(reduced[1].astype(jnp.bfloat16), "grp").astype(jnp.float32),
        lax.psum(reduced[2].astype(jnp.bfloat16), "grp").astype(jnp.float32),
        lax.psum(reduced[3].astype(jnp.bfloat16), "grp").astype(jnp.float32),
        lax.psum(reduced[4].astype(jnp.bfloat16), "grp").astype(jnp.float32),
        lax.psum(reduced[5].astype(jnp.bfloat16), "grp").astype(jnp.float32),
        lax.psum(reduced[6].astype(jnp.bfloat16), "grp").astype(jnp.float32),
        lax.psum(reduced[7].astype(jnp.bfloat16), "grp").astype(jnp.float32),
        lax.psum(reduced[8].astype(jnp.bfloat16), "grp").astype(jnp.float32),
        lax.psum(reduced[9].astype(jnp.bfloat16), "grp").astype(jnp.float32),
        lax.psum(reduced[10].astype(jnp.bfloat16), "grp").astype(jnp.float32),
        lax.psum(reduced[11].astype(jnp.bfloat16), "grp").astype(jnp.float32),
        lax.psum(reduced[12].astype(jnp.bfloat16), "grp").astype(jnp.float32),
    )
    return (
        layer_out,
        input_grad.reshape(seq_count, length, model_width),
        summed[0],
        summed[1],
        summed[2],
        summed[3],
        summed[4],
        summed[5],
        summed[6],
        summed[7],
        summed[8],
        summed[9],
        summed[10],
        summed[11],
        summed[12],
    )


NT = (((1,), (1,)), ((), ()))
NN = (((1,), (0,)), ((), ()))
TN = (((0,), (0,)), ((), ()))
LANES = 128
AXES = ("grp", "shard")


def mxu(left, right, dims):
    return lax.dot_general(left, right, dims, preferred_element_type=jnp.float32)


def cost(flops):
    return pl.CostEstimate(flops=2 * flops, bytes_accessed=0, transcendentals=0)


def params(megabytes=60):
    return pltpu.CompilerParams(vmem_limit_bytes=megabytes << 20)


def attention_forward_kernel(q_ref, k_ref, v_ref, seg_col, seg_row, out_ref, probs_ref, *, rows):
    length = q_ref.shape[0]
    first = lax.broadcasted_iota(jnp.int32, (1, LANES), 1) < HD
    keys = k_ref[...]
    values = v_ref[...]
    zero = jnp.zeros_like(keys)
    head_keys = (jnp.where(first, keys, zero), jnp.where(first, zero, keys))
    key_segments = seg_col[...]
    for block in range(length // rows):
        here = pl.ds(block * rows, rows)
        q = q_ref[here, :]
        allowed = key_segments == seg_row[:, here]
        outs = []
        for head in range(2):
            scores = mxu(head_keys[head], q, NT)
            scores = jnp.where(allowed, scores, masked_score)
            powers = jnp.exp(scores - jnp.max(scores, 0, keepdims=True))
            probs = powers * (1.0 / jnp.sum(powers, 0, keepdims=True))
            probs = probs.astype(jnp.bfloat16)
            probs_ref[head, :, here] = probs
            outs.append(mxu(probs, values, TN))
        out_ref[here, :] = jnp.where(first, outs[0], outs[1]).astype(jnp.bfloat16)


def attention_forward(qkv, seg_col, seg_row, start, pairs, before=None):
    length, width = qkv.shape[0], qkv.shape[1] // 3
    total = width // LANES
    rows = min(512, length)
    more = () if before is None else before

    def pair(part):
        return pl.BlockSpec((length, LANES), lambda j: (0, part * total + start + j))

    def body(q_ref, k_ref, v_ref, seg_c, seg_r, *refs):
        attention_forward_kernel(q_ref, k_ref, v_ref, seg_c, seg_r, *refs[-2:], rows=rows)

    return pl.pallas_call(
        body,
        grid=(pairs,),
        in_specs=[
            pair(0),
            pair(1),
            pair(2),
            pl.BlockSpec((length, 1), lambda j: (0, 0)),
            pl.BlockSpec((1, length), lambda j: (0, 0)),
        ]
        + [pl.BlockSpec(memory_space=pl.ANY)] * len(more),
        out_specs=[
            pl.BlockSpec((length, LANES), lambda j: (0, start + j)),
            pl.BlockSpec((2, length, length), lambda j: (start + j, 0, 0)),
        ],
        out_shape=[
            jax.ShapeDtypeStruct((length, width), jnp.bfloat16),
            jax.ShapeDtypeStruct((2 * total, length, length), jnp.bfloat16),
        ],
        input_output_aliases={} if before is None else {5: 0, 6: 1},
        compiler_params=params(60),
        cost_estimate=cost(16 * length * length * pairs * LANES),
        name="attn_fwd",
    )(qkv, qkv, qkv, seg_col, seg_row, *more)


def attention_backward_kernel(q_ref, k_ref, v_ref, o_ref, do_ref, probs_ref, grad_ref, sum_ref):
    first = lax.broadcasted_iota(jnp.int32, (1, LANES), 1) < HD
    pick = (
        lax.broadcasted_iota(jnp.int32, (8, LANES), 0)
        == lax.broadcasted_iota(jnp.int32, (8, LANES), 1) // HD
    ).astype(jnp.float32)
    q = q_ref[...]
    do = do_ref[...]
    keys = k_ref[...]
    values = v_ref[...]
    zero = jnp.zeros_like(values)
    head_values = (jnp.where(first, values, zero), jnp.where(first, zero, values))
    dots = lax.dot_general(
        pick,
        do.astype(jnp.float32) * o_ref[...].astype(jnp.float32),
        NT,
        precision=lax.Precision.HIGHEST,
        preferred_element_type=jnp.float32,
    )
    query_parts, key_parts, value_parts = [], [], []
    for head in range(2):
        probs = probs_ref[head]
        prob_grad = mxu(head_values[head], do, NT)
        score_grad = probs.astype(jnp.float32) * (prob_grad - dots[head : head + 1, :])
        score_grad = score_grad.astype(jnp.bfloat16)
        value_parts.append(mxu(probs, do, NN))
        key_parts.append(mxu(score_grad, q, NN))
        query_parts.append(mxu(score_grad, keys, TN))
    query_grad = jnp.where(first, *query_parts) * (1.0 / math.sqrt(HD))
    value_grad = jnp.where(first, *value_parts)
    grad_ref[0] = query_grad.astype(jnp.bfloat16)
    grad_ref[1] = jnp.where(first, *key_parts).astype(jnp.bfloat16)
    grad_ref[2] = value_grad.astype(jnp.bfloat16)
    sum_ref[0:1, :] = jnp.sum(query_grad, 0, keepdims=True)
    sum_ref[1:2, :] = jnp.sum(value_grad, 0, keepdims=True)


def attention_backward(qkv, out, out_grad, probs, start, pairs, at, size, before=None):
    length, width = out.shape
    total = width // LANES
    more = () if before is None else before

    def pair(part):
        return pl.BlockSpec((length, LANES), lambda j: (0, part * total + start + j))

    def body(*refs):
        attention_backward_kernel(*refs[:6], *refs[-2:])

    return pl.pallas_call(
        body,
        grid=(pairs,),
        in_specs=[
            pair(0),
            pair(1),
            pair(2),
            pair(0),
            pair(0),
            pl.BlockSpec((2, length, length), lambda j: (start + j, 0, 0)),
        ]
        + [pl.BlockSpec(memory_space=pl.ANY)] * len(more),
        out_specs=[
            pl.BlockSpec((3, length, LANES), lambda j: (0, 0, j + at)),
            pl.BlockSpec((2, LANES), lambda j: (0, j + at)),
        ],
        out_shape=[
            jax.ShapeDtypeStruct((3, length, size * LANES), jnp.bfloat16),
            jax.ShapeDtypeStruct((2, size * LANES), jnp.float32),
        ],
        input_output_aliases={} if before is None else {6: 0, 7: 1},
        compiler_params=params(60),
        cost_estimate=cost(32 * length * length * pairs * LANES),
        name="attn_bwd",
    )(qkv, qkv, qkv, out, out_grad, probs, *more)


class Place:
    def __init__(self, groups, shards):
        self.groups = groups
        self.shards = shards
        self.chips = shards // 2
        self.grp = lax.axis_index("grp")
        self.shard = lax.axis_index("shard")
        self.core = self.shard % 2
        self.chip = self.shard // 2
        self.scalars = jnp.stack([self.core, self.chip, self.grp]).astype(jnp.int32)

    def permute(self, array, mask_of_core):
        pairs = [(i, i ^ mask_of_core[i % 2]) for i in range(self.groups * self.shards)]
        return lax.ppermute(array, AXES, pairs)

    def swap_core(self, array):
        return self.permute(array, (1, 1))

    def swap_grp(self, array, step):
        masks = (self.shards, 2 * self.shards)
        return self.permute(array, masks if step == 0 else masks[::-1])

    def swap_chip(self, array, step):
        masks = (2, 4)
        return self.permute(array, masks if step == 0 else masks[::-1])

    def slot_chip(self, slot):
        return self.chip ^ turn(slot, self.core)

    def slot_grp(self, slot):
        return self.grp ^ turn(slot, self.core)


def turn(slot, core):
    if isinstance(slot, int):
        return slot if slot in (0, 3) else jnp.where(core == 0, slot, 3 - slot)
    return jnp.where((core == 0) | (slot == 0) | (slot == 3), slot, 3 - slot)


def after(value, *others):
    return lax.optimization_barrier((value, *others))[0]


def meet(anchor, *flights):
    arrays = [f.flying for f in flights]
    _, *arrays = lax.optimization_barrier((anchor, *arrays))
    for f, array in zip(flights, arrays):
        f.flying = array


class Gather:
    def __init__(self, place, piece):
        self.place = place
        self.piece = piece
        self.held = [None] * 4
        self.crossed = [None] * 4

    def chips_near(self, *wait):
        self.piece = after(self.piece, *wait)
        self.flying = self.place.swap_chip(self.piece, 0)

    def chips_far(self):
        self.pair = jnp.stack([self.piece, self.flying])
        self.flying = self.place.swap_chip(self.pair, 1)
        return self.pair

    def join(self):
        self.held[0] = jnp.concatenate([self.pair, self.flying])
        return self.held[0]

    def near(self, *wait):
        self.held[0] = after(self.held[0], *wait)
        self.flying = (self.place.swap_grp(self.held[0], 0), self.place.swap_grp(self.held[0], 1))
        return self.held[0]

    def far(self, *wait):
        self.held[1:3] = self.flying
        first = after(self.held[1], *wait)
        self.flying = self.place.swap_grp(first, 1)

    def landed(self):
        self.held[3] = self.flying

    def cross(self, *which, wait=()):
        for n in which:
            self.crossed[n] = self.place.swap_core(after(self.held[n], *wait))

    def pieces(self):
        return self.held + self.crossed


class Window:
    def __init__(self, gather, start, cols):
        self.arrays = gather.pieces()
        self.start, self.cols = start, cols
        chips, rows, _ = self.arrays[0].shape
        self.chips, self.rows = chips, rows


def fetch(where, window, refs, whole, sem, by):
    rows, cols, chips = window.rows, window.cols, window.chips
    for slot in range(4):
        for side in range(2):
            core = where[0] ^ side
            ref = refs[4 * side + slot]
            distance = turn(slot, core)
            col = pl.multiple_of((where[2] ^ distance) * cols, LANES)
            for k in range(chips):
                row = ((where[1] ^ turn(k, core)) * 2 + core) * rows
                pltpu.make_async_copy(
                    ref.at[k, :, pl.ds(window.start, cols)],
                    whole.at[pl.ds(pl.multiple_of(row, rows), rows), pl.ds(col, cols)],
                    sem.at[distance if by == "grp" else 0],
                ).start()


def weight_call(place, kernel, window, inputs, in_specs, outs, out_specs, steps, by, name, flops, write=True):
    cols, groups = window.cols, place.groups
    pieces = window.arrays
    shape = (window.chips * 2 * window.rows, groups * cols)
    slots = {"grp": groups, "all": 1}[by]
    anywhere = pl.BlockSpec(memory_space=pl.ANY)

    def body(where, *refs):
        taken, refs = refs[: len(pieces)], refs[len(pieces) :]
        *refs, weight, sem, out_sem = refs
        if write:
            *refs, written = refs
        step = pl.program_id(0)

        @pl.when(step == 0)
        def _():
            fetch(where, window, taken, weight, sem, by)

        def ready():
            if by == "all":

                @pl.when(step == 0)
                def _():
                    pltpu.make_async_copy(weight, weight, sem.at[0]).wait()
                    if write:
                        pltpu.make_async_copy(weight, written, out_sem.at[0]).start()

            else:
                at = pl.ds(pl.multiple_of((where[2] ^ step) * cols, LANES), cols)
                view = weight.at[:, at]
                pltpu.make_async_copy(view, view, sem.at[step]).wait()
                pltpu.make_async_copy(view, written.at[:, at], out_sem.at[step]).start()

        kernel(where, ready, weight, *refs)

        @pl.when(step == (steps - 1 if write else -1))
        def _():
            for slot in range(slots if write else 0):
                width = shape[1] // slots
                view = weight.at[:, pl.ds(slot * width, width)]
                pltpu.make_async_copy(view, view, out_sem.at[slot]).wait()

    total = sum(math.prod(x.shape) * x.dtype.itemsize for x in list(inputs) + list(outs))
    return pl.pallas_call(
        body,
        grid_spec=pltpu.PrefetchScalarGridSpec(
            num_scalar_prefetch=1,
            grid=(steps,),
            in_specs=[anywhere] * len(pieces) + in_specs,
            out_specs=out_specs + [anywhere] * write,
            scratch_shapes=[
                pltpu.VMEM(shape, jnp.bfloat16),
                pltpu.SemaphoreType.DMA((slots,)),
                pltpu.SemaphoreType.DMA((slots,)),
            ],
        ),
        out_shape=outs + [shaped(shape, jnp.bfloat16)] * write,
        compiler_params=params(60),
        cost_estimate=cost(flops),
        name=name,
    )(place.scalars, *pieces, *inputs)


def plain_call(kernel, inputs, in_specs, outs, out_specs, steps, name, flops):
    total = sum(math.prod(x.shape) * x.dtype.itemsize for x in list(inputs) + list(outs))
    return pl.pallas_call(
        kernel,
        grid=(steps,),
        in_specs=in_specs,
        out_specs=out_specs,
        out_shape=outs,
        compiler_params=params(60),
        cost_estimate=cost(flops),
        name=name,
    )(*inputs)


TILE = 256


def row_tiles(width):
    return pl.BlockSpec((TILE, width), lambda i, *s: (i, 0))


def fixed(*shape):
    return pl.BlockSpec(shape, lambda i, *s: (0,) * len(shape))


def whole_once(shape):
    return pl.BlockSpec(shape, lambda i: (0,) * len(shape), pipeline_mode=pl.Buffered(1))


def shaped(shape, dtype):
    return jax.ShapeDtypeStruct(shape, dtype)


B_QUERY, B_VALUE, B_ATTN, GAIN_ONE, SHIFT_ONE, B_OUT, GAIN_TWO, SHIFT_TWO, B_IN = range(9)


def row(ref, n):
    return ref[n : n + 1, :]


class Vectors:
    def __init__(self, place, vectors):
        lines = [v.reshape(-1, LANES) for v in vectors]
        blank = jnp.zeros((-sum(x.shape[0] for x in lines) % 16, LANES), jnp.bfloat16)
        self.own = jnp.concatenate([*lines, blank])
        self.place = place
        self.flying = place.swap_core(self.own)

    def chips_near(self):
        self.own = jnp.stack([self.own, self.flying])
        self.flying = self.place.swap_chip(self.own, 0)

    def chips_far(self):
        self.own = jnp.stack([self.own, self.flying])
        self.flying = self.place.swap_chip(self.own, 1)

    def landed(self):
        self.slots = jnp.concatenate([self.own, self.flying])

    def unpack(self, seg_row, keep_row):
        place = self.place
        length = seg_row.shape[1]
        slots, sides, rows, lanes = self.slots.shape
        shards = place.shards

        def kernel(where, in_ref, seg_ref, keep_ref, *outs):
            rows_ref, inner_ref, qkv_ref, seg_col_ref, keep_col_ref = outs
            for line_ref, col_ref in ((seg_ref, seg_col_ref), (keep_ref, keep_col_ref)):
                line = jnp.broadcast_to(line_ref[...].astype(jnp.float32), (8, length))
                col_ref[...] = line.T[:, 0:1].astype(col_ref.dtype)
            width = shards * lanes
            qkv_ref[...] = jnp.zeros_like(qkv_ref)
            for slot in range(slots):
                for side in range(sides):
                    core = where[0] ^ side
                    shard = (where[1] ^ turn(slot, where[0])) * 2 + core
                    part = in_ref[slot, side].astype(jnp.float32)
                    at = pl.multiple_of(shard * lanes, lanes)
                    rows_ref[:, pl.ds(at, lanes)] = part
                    qkv_ref[:, pl.ds(at, lanes)] = part[B_QUERY : B_QUERY + 1]
                    qkv_ref[:, pl.ds(2 * width + at, lanes)] = part[B_VALUE : B_VALUE + 1]
                    for n in range(4):
                        start = pl.multiple_of((shard * 4 + n) * lanes, lanes)
                        inner_ref[:, pl.ds(start, lanes)] = part[B_IN + n : B_IN + n + 1]

        in_vmem = pl.BlockSpec(memory_space=pltpu.VMEM)
        return pl.pallas_call(
            kernel,
            in_specs=[pl.BlockSpec(memory_space=pltpu.SMEM)] + [in_vmem] * 3,
            out_specs=[in_vmem] * 5,
            out_shape=[
                shaped((rows, shards * lanes), jnp.float32),
                shaped((1, 4 * shards * lanes), jnp.float32),
                shaped((1, 3 * shards * lanes), jnp.float32),
                shaped((length, 1), jnp.int32),
                shaped((length, 1), jnp.float32),
            ],
            name="vectors",
        )(place.scalars, self.slots, seg_row, keep_row)


def pack_sums(late_a, late_b, first_sums, second_sums, inner_sums):
    width = first_sums.shape[1]
    half = late_a.shape[1]

    def kernel(a_ref, b_ref, one_ref, two_ref, inner_ref, out_ref):
        def place_of(n):
            return n // 3 * 8 + n % 3

        out_ref[...] = jnp.zeros_like(out_ref)
        for n in (B_QUERY, B_VALUE):
            at = place_of(n)
            out_ref[at : at + 1, 0:half] = a_ref[n : n + 1, :]
            out_ref[at : at + 1, half:width] = b_ref[n : n + 1, :]
        for n, source, line in (
            (GAIN_ONE, one_ref, 0),
            (SHIFT_ONE, one_ref, 1),
            (B_ATTN, one_ref, 2),
            (GAIN_TWO, two_ref, 0),
            (SHIFT_TWO, two_ref, 1),
            (B_OUT, two_ref, 2),
        ):
            at = place_of(n)
            out_ref[at : at + 1, :] = source[line : line + 1, :]
        for n in range(4):
            at = place_of(B_IN + n)
            for shard in range(width // LANES):
                start = (4 * shard + n) * LANES
                out_ref[at : at + 1, shard * LANES : (shard + 1) * LANES] = inner_ref[
                    :, start : start + LANES
                ]

    in_vmem = pl.BlockSpec(memory_space=pltpu.VMEM)
    return pl.pallas_call(
        kernel,
        in_specs=[in_vmem] * 5,
        out_specs=in_vmem,
        out_shape=shaped((32, width), jnp.float32),
        name="pack_sums",
    )(late_a, late_b, first_sums, second_sums, inner_sums)


def project_qkv(place, rows, window, bias, scale):
    length, width = rows.shape
    cols = window.cols

    def kernel(where, ready, weight, x_ref, bias_ref, scale_ref, out_ref):
        ready()
        at = pl.ds(pl.multiple_of((where[2] ^ pl.program_id(0)) * cols, LANES), cols)
        for tile in range(length // TILE):
            here = pl.ds(tile * TILE, TILE)
            mixed = mxu(x_ref[here, :], weight[:, at], NN) + bias_ref[:, at]
            mixed = mixed.astype(jnp.bfloat16).astype(jnp.float32) * scale_ref[:, at]
            out_ref[here, :] = mixed.astype(jnp.bfloat16)

    total = cols * place.groups
    return weight_call(
        place,
        kernel,
        window,
        (rows, bias, scale),
        [fixed(length, width), fixed(1, total), fixed(1, total)],
        [shaped((length, total), jnp.bfloat16)],
        [pl.BlockSpec((length, cols), lambda i, s: (0, i ^ s[2]))],
        place.groups,
        "grp",
        "qkv",
        2 * length * width * total,
    )


def norm_parts(rows):
    centered = rows - jnp.mean(rows, -1, keepdims=True)
    scale = lax.rsqrt(jnp.mean(centered * centered, -1, keepdims=True) + epsilon)
    return centered * scale, scale


def norm_back(grad, normed, scale):
    return scale * (
        grad
        - jnp.mean(grad, -1, keepdims=True)
        - normed * jnp.mean(grad * normed, -1, keepdims=True)
    )


def add_rows(sum_ref, *terms):
    @pl.when(pl.program_id(0) == 0)
    def _():
        sum_ref[...] = jnp.zeros_like(sum_ref)

    for n, term in enumerate(terms):
        sum_ref[n : n + 1, :] += jnp.sum(term, 0, keepdims=True)


def project_out(place, contexts, window, rows, vectors):
    length, width = rows.shape

    def kernel(where, ready, weight, c_ref, x_ref, v_ref, n_ref, r_ref, low_ref):
        ready()
        first_sum = mxu(c_ref[...], weight[...], NN) + row(v_ref, B_ATTN)
        first_sum = first_sum + x_ref[...].astype(jnp.float32)
        normed, scale = norm_parts(first_sum)
        n_ref[...] = normed
        r_ref[...] = jnp.broadcast_to(scale, r_ref.shape)
        low_ref[...] = (normed * row(v_ref, GAIN_ONE) + row(v_ref, SHIFT_ONE)).astype(jnp.bfloat16)

    return weight_call(
        place,
        kernel,
        window,
        (contexts, rows, vectors),
        [row_tiles(width), row_tiles(width), fixed(*vectors.shape)],
        [
            shaped((length, width), jnp.float32),
            shaped((length, LANES), jnp.float32),
            shaped((length, width), jnp.bfloat16),
        ],
        [row_tiles(width), row_tiles(LANES), row_tiles(width)],
        length // TILE,
        "all",
        "attn_out",
        2 * length * width * width,
    )


def feed_in(place, normed_low, window, bias):
    length, width = normed_low.shape
    cols = window.cols

    def kernel(where, ready, weight, x_ref, bias_ref, hid_ref, slope_ref):
        ready()
        at = pl.ds(pl.multiple_of((where[2] ^ pl.program_id(0)) * cols, LANES), cols)
        for tile in range(length // TILE):
            here = pl.ds(tile * TILE, TILE)
            pre = mxu(x_ref[here, :], weight[:, at], NN) + bias_ref[:, at]
            share = 0.5 + 0.5 * lax.erf(pre * (1.0 / math.sqrt(2.0)))
            bell = jnp.exp(-0.5 * pre * pre) * (1.0 / math.sqrt(2.0 * math.pi))
            hid_ref[here, :] = (pre * share).astype(jnp.bfloat16)
            slope_ref[here, :] = (share + pre * bell).astype(jnp.bfloat16)

    total = cols * place.groups
    block = pl.BlockSpec((length, cols), lambda i, s: (0, i ^ s[2]))
    return weight_call(
        place,
        kernel,
        window,
        (normed_low, bias),
        [fixed(length, width), fixed(1, total)],
        [shaped((length, total), jnp.bfloat16)] * 2,
        [block, block],
        place.groups,
        "grp",
        "feed_in",
        2 * length * width * total,
    )


def feed_out(place, hidden, window, normed, cot, keep, vectors, slope):
    length, inner = hidden.shape
    width = normed.shape[1]

    def kernel(where, ready, weight, h_ref, n_ref, cot_ref, keep_ref, v_ref, slope_ref, *outs):
        out_ref, grad_ref, low_ref, sum_ref, pre_ref, inner_ref = outs
        ready()
        fed = mxu(h_ref[...], weight[...], NN)
        normed_one = n_ref[...] * row(v_ref, GAIN_ONE) + row(v_ref, SHIFT_ONE)
        second_sum = normed_one + (fed + row(v_ref, B_OUT))
        second, scale = norm_parts(second_sum)
        out_ref[...] = (second * row(v_ref, GAIN_TWO) + row(v_ref, SHIFT_TWO)).astype(jnp.bfloat16)
        masked = cot_ref[...].astype(jnp.float32) * keep_ref[...]
        grad = norm_back(masked * row(v_ref, GAIN_TWO), second, scale)
        grad_ref[...] = grad
        low = grad.astype(jnp.bfloat16)
        low_ref[...] = low
        add_rows(sum_ref, masked * second, masked, grad)

        @pl.when(pl.program_id(0) == 0)
        def _():
            inner_ref[...] = jnp.zeros_like(inner_ref)

        size = min(1024, inner)
        for n in range(inner // size):
            at = slice(n * size, (n + 1) * size)
            pre = mxu(low, weight[at, :], NT) * slope_ref[:, at].astype(jnp.float32)
            pre_ref[:, at] = pre.astype(jnp.bfloat16)
            inner_ref[:, at] += jnp.sum(pre, 0, keepdims=True)

    return weight_call(
        place,
        kernel,
        window,
        (hidden, normed, cot, keep, vectors, slope),
        [
            row_tiles(inner),
            row_tiles(width),
            row_tiles(width),
            row_tiles(1),
            fixed(*vectors.shape),
            row_tiles(inner),
        ],
        [
            shaped((length, width), jnp.bfloat16),
            shaped((length, width), jnp.float32),
            shaped((length, width), jnp.bfloat16),
            shaped((8, width), jnp.float32),
            shaped((length, inner), jnp.bfloat16),
            shaped((1, inner), jnp.float32),
        ],
        [
            row_tiles(width),
            row_tiles(width),
            row_tiles(width),
            fixed(8, width),
            row_tiles(inner),
            fixed(1, inner),
        ],
        length // TILE,
        "all",
        "feed_out",
        4 * length * width * inner,
        write=False,
    )


def feed_in_back(pre_low, weight, second_grad, normed, scale, vectors, attn_weight):
    length, inner = pre_low.shape
    width = normed.shape[1]

    def kernel(p_ref, w_ref, g_ref, n_ref, r_ref, v_ref, a_ref, first_ref, low_ref, ctx_ref, sum_ref):
        grad = g_ref[...] + mxu(p_ref[...], w_ref[...], NT)
        first = norm_back(grad * row(v_ref, GAIN_ONE), n_ref[...], r_ref[:, :1])
        low = first.astype(jnp.bfloat16)
        first_ref[...] = first
        low_ref[...] = low
        ctx_ref[...] = mxu(low, a_ref[...], NT).astype(jnp.bfloat16)
        add_rows(sum_ref, grad * n_ref[...], grad, first)

    return plain_call(
        kernel,
        (pre_low, weight, second_grad, normed, scale, vectors, attn_weight),
        [
            row_tiles(inner),
            whole_once(weight.shape),
            row_tiles(width),
            row_tiles(width),
            row_tiles(LANES),
            fixed(*vectors.shape),
            whole_once(attn_weight.shape),
        ],
        [
            shaped((length, width), jnp.float32),
            shaped((length, width), jnp.bfloat16),
            shaped((length, width), jnp.bfloat16),
            shaped((8, width), jnp.float32),
        ],
        [row_tiles(width), row_tiles(width), row_tiles(width), fixed(8, width)],
        length // TILE,
        "feed_in_back",
        2 * length * width * (inner + width),
    )


def project_qkv_back(grads, weight, first_grad, start, tiles, before=None):
    length, width = first_grad.shape
    part = width // len(grads)

    def kernel(w_ref, *refs):
        grad_refs, first_ref, out_ref = refs[: len(grads)], refs[len(grads)], refs[-1]
        total = first_ref[...]
        for n in range(3):
            for m, grad_ref in enumerate(grad_refs):
                at = n * width + m * part
                total = total + mxu(grad_ref[n], w_ref[:, at : at + part], NT)
        out_ref[...] = total

    tile = pl.BlockSpec((TILE, width), lambda i: (start + i, 0))
    more = () if before is None else (before,)
    return pl.pallas_call(
        kernel,
        grid=(tiles,),
        in_specs=[whole_once(weight.shape)]
        + [pl.BlockSpec((3, TILE, part), lambda i: (0, start + i, 0))] * len(grads)
        + [tile]
        + [pl.BlockSpec(memory_space=pl.ANY)] * len(more),
        out_specs=tile,
        out_shape=shaped((length, width), jnp.float32),
        input_output_aliases={} if before is None else {len(grads) + 2: 0},
        compiler_params=params(60),
        cost_estimate=cost(6 * tiles * TILE * width * width),
        name="qkv_back",
    )(weight, *grads, first_grad, *more)


ORDER = (1, 3, 0, 2)


def ordered_slot(j):
    return jnp.where(j < 2, 2 * j + 1, 2 * j - 4)


def weight_grad_kernel(where, left_ref, right_ref, own, sent, kept, *, rows, groups, split):
    core = where[0]
    chips = left_ref.shape[1] // (2 * rows)

    @pl.when(pl.program_id(1) == 0)
    def _():
        keep_rows(core, left_ref, rows, kept)

    if split:
        size = min(512, right_ref.shape[1])
        for ref, side in ((sent, 1), (own, 0)):
            for n in range(right_ref.shape[1] // size):
                at = slice(n * size, (n + 1) * size)
                part = mxu(kept[side], right_ref[:, at], NN).astype(jnp.bfloat16)
                ref[0, :, :, at] = part.reshape(chips, rows, size)
    else:
        cols = right_ref.shape[1] // groups
        for ref, side in ((sent, 1), (own, 0)):
            for pos, slot in enumerate(ORDER):
                start = pl.multiple_of((where[2] ^ turn(slot, core ^ side)) * cols, LANES)
                part = mxu(kept[side], right_ref[:, pl.ds(start, cols)], NN)
                ref[pos] = part.astype(jnp.bfloat16).reshape(chips, rows, cols)


def keep_rows(core, left_ref, rows, kept):
    chips = left_ref.shape[1] // (2 * rows)
    for side in range(2):
        chosen = []
        for k in range(chips):
            even = left_ref[:, 2 * k * rows : (2 * k + 1) * rows]
            odd = left_ref[:, (2 * k + 1) * rows : (2 * k + 2) * rows]
            chosen.append(jnp.where(core == side, even, odd))
        left = chosen[0] if chips == 1 else jnp.concatenate(chosen, 1)
        kept[side] = left.T


def turned_rows(place, left):
    tokens, height = left.shape

    def kernel(where, left_ref, out_ref):
        keep_rows(where[0], left_ref, height // place.shards, out_ref)

    in_vmem = pl.BlockSpec(memory_space=pltpu.VMEM)
    return pl.pallas_call(
        kernel,
        in_specs=[pl.BlockSpec(memory_space=pltpu.SMEM), in_vmem],
        out_specs=in_vmem,
        out_shape=shaped((2, height // 2, tokens), jnp.bfloat16),
        compiler_params=params(40),
        name="turned_rows",
    )(place.scalars, left)


def attention_grads_kernel(where, *refs, rows, groups, extra):
    turned, right_ref, *refs = refs
    *more, own, sent, kept = refs
    core, grp = where[0], where[2]
    chips = turned.shape[1] // rows
    step = pl.program_id(0)

    def scatter(lefts, right, at, cols):
        for ref, side in ((sent, 1), (own, 0)):
            part = mxu(lefts[side], right, NN).astype(jnp.bfloat16)
            for g in range(groups):
                pos = position(grp ^ g, core ^ side)
                block = part[:, g * cols : (g + 1) * cols].reshape(chips, rows, cols)
                ref[pos, :, 0:rows, pl.ds(at, cols)] = block

    skip = 0
    if not extra:
        other_left, other_right = more
        skip = other_right.shape[1] // groups

        @pl.when(step == 0)
        def _():
            keep_rows(core, other_left, rows, kept)
            scatter(kept, other_right[...], 0, skip)

    cols = right_ref.shape[2] // groups
    scatter(turned, right_ref[0], pl.multiple_of(skip + step * cols, LANES), cols)

    if extra:
        (sums_ref,) = more

        @pl.when(step == 2)
        def _():
            blank = jnp.zeros((extra, own.shape[3]), jnp.bfloat16)
            for ref, side in ((sent, 1), (own, 0)):
                for g in range(groups):
                    pos = position(grp ^ g, core ^ side)
                    for k in range(chips):
                        start = pl.multiple_of((2 * k + (core ^ side)) * LANES, LANES)
                        ref[pos, k, rows : rows + extra, :] = blank
                        lines = sums_ref[8 * g : 8 * g + 8, pl.ds(start, LANES)]
                        for n in range(3):
                            ref[pos, k, rows : rows + 1, n * LANES : (n + 1) * LANES] = lines[
                                n : n + 1
                            ].astype(jnp.bfloat16)


def position(distance, core):
    slot = turn(distance, core)
    return jnp.where(slot == 0, 2, jnp.where(slot == 1, 0, jnp.where(slot == 3, 1, 3)))


def attention_grads(place, turned, right, more, name):
    height, tokens = 2 * turned.shape[1], turned.shape[2]
    groups, chips = place.groups, place.chips
    rows = height // place.shards
    extra = 16 if len(more) == 1 else 0
    size = right.shape[2]
    cols = 3 * size // groups + (0 if extra else more[1].shape[1] // groups)
    shape = (groups, chips, rows + extra, cols)
    once = [
        pl.BlockSpec(x.shape, lambda i, s: (0, 0), pipeline_mode=pl.Buffered(1)) for x in more
    ]
    return pl.pallas_call(
        functools.partial(attention_grads_kernel, rows=rows, groups=groups, extra=extra),
        grid_spec=pltpu.PrefetchScalarGridSpec(
            num_scalar_prefetch=1,
            grid=(3,),
            in_specs=[
                pl.BlockSpec(turned.shape, lambda i, s: (0, 0, 0), pipeline_mode=pl.Buffered(1)),
                pl.BlockSpec((1, tokens, size), lambda i, s: (i, 0, 0)),
            ]
            + once,
            out_specs=[pl.BlockSpec(shape, lambda i, s: (0, 0, 0, 0))] * 2,
            scratch_shapes=[pltpu.VMEM((8, LANES) if extra else turned.shape, jnp.bfloat16)],
        ),
        out_shape=[shaped(shape, jnp.bfloat16)] * 2,
        compiler_params=params(60),
        cost_estimate=cost(2 * tokens * height * cols * groups),
        name="wgrad_" + name,
    )(place.scalars, turned, right, *more)


def weight_grad(place, left, right, split, name):
    tokens, height = left.shape
    groups, chips = place.groups, place.chips
    rows = height // place.shards
    step_chips = chips if split else max(1, 1024 // (2 * rows))
    cols = right.shape[1] // groups
    if split:
        grid = (1, groups)
        block = lambda i, j, s: (0, s[2] ^ turn(ordered_slot(j), s[0]))
        right_spec = pl.BlockSpec((tokens, cols), block)
        one = (1, chips, rows, cols)
        other = lambda j: jnp.where(j == 0, 3, jnp.where(j == 3, 0, j))
        out_specs = [
            pl.BlockSpec(one, lambda i, j, s: (j, 0, 0, 0)),
            pl.BlockSpec(one, lambda i, j, s: (other(j), 0, 0, 0)),
        ]
    else:
        grid = (chips // step_chips, 1)
        right_spec = pl.BlockSpec(right.shape, lambda i, j, s: (0, 0))
        out_specs = [
            pl.BlockSpec((groups, step_chips, rows, cols), lambda i, j, s: (0, i, 0, 0))
        ] * 2
    return pl.pallas_call(
        functools.partial(weight_grad_kernel, rows=rows, groups=groups, split=split),
        grid_spec=pltpu.PrefetchScalarGridSpec(
            num_scalar_prefetch=1,
            grid=grid,
            in_specs=[
                pl.BlockSpec((tokens, step_chips * 2 * rows), lambda i, j, s: (0, i)),
                right_spec,
            ],
            out_specs=out_specs,
            scratch_shapes=[pltpu.VMEM((2, step_chips * rows, tokens), jnp.bfloat16)],
        ),
        out_shape=[shaped((groups, chips, rows, cols), jnp.bfloat16)] * 2,
        compiler_params=params(60),
        cost_estimate=cost(2 * tokens * height * cols * groups),
        name="wgrad_" + name,
    )(place.scalars, left, right)


def add(*terms):
    total = terms[0].astype(jnp.float32)
    for term in terms[1:]:
        total = total + term.astype(jnp.float32)
    return total.astype(jnp.bfloat16)


class Reduction:
    def __init__(self, place, made):
        self.place = place
        self.made, sent = made
        self.flying = place.swap_core(sent)

    def near(self):
        self.core = self.flying
        leave = add(self.made[:2], self.core[:2])
        self.flying = self.place.swap_grp(leave, 0)
        return leave

    def middle(self):
        self.first = self.flying
        second = add(self.made[3], self.core[3], self.first[1])
        self.flying = self.place.swap_grp(second, 1)
        return second

    def column(self):
        mine = add(self.made[2], self.core[2], self.first[0], self.flying)
        return mine, lambda chip: lax.dynamic_index_in_dim(mine, chip, 0, False)

    def along(self):
        place = self.place
        mine, at = self.column()
        self.mine = [at(place.slot_chip(slot)) for slot in range(4)]
        both = jnp.stack([self.mine[1], self.mine[3]])
        self.flying = place.swap_chip(both, 0)
        return both

    def along_far(self):
        self.first = self.flying
        second = add(self.mine[2], self.first[1])
        self.flying = self.place.swap_chip(second, 1)
        return second

    def share(self):
        return add(self.mine[0], self.first[0], self.flying)

    def along_direct(self):
        place = self.place
        mine, at = self.column()
        self.mine = at(place.chip)
        self.flying = tuple(
            place.permute(at(place.chip ^ k), (2 * k, 2 * k)) for k in range(place.chips - 1, 0, -1)
        )
        return mine

    def share_direct(self):
        return add(self.mine, *self.flying)


class Replication:
    def __init__(self, place, share, direct=False):
        self.place = place
        self.blocks = [share] + [None] * 3
        if direct:
            size = place.shards
            for mask in (3, 1, 2):
                self.blocks[mask] = place.permute(share, (mask * size, mask * size))
        else:
            self.flying = place.swap_grp(share, 0)

    def far(self):
        pair = jnp.stack([self.blocks[0], self.flying])
        self.blocks[1] = self.flying
        self.flying = self.place.swap_grp(pair, 1)
        return pair

    def landed(self):
        if self.blocks[2] is None:
            self.blocks[2:] = [self.flying[0], self.flying[1]]
        return self.blocks


def order_feed_forward(place, blocks, rows_in):
    groups = place.groups
    height, cols = blocks[0].shape
    rows_out = height - groups * rows_in

    def kernel(where, *refs):
        *blocks, out_ref, in_ref = refs
        for slot, ref in enumerate(blocks):
            g = where[2] ^ turn(slot, where[0])
            at = pl.multiple_of(g * cols, LANES)
            out_ref[:, pl.ds(at, cols)] = ref[0:rows_out, :].astype(jnp.float32)
            for n in range(groups):
                at = pl.multiple_of((g * groups + n) * cols, LANES)
                part = ref[rows_out + n * rows_in : rows_out + (n + 1) * rows_in, :]
                in_ref[:, pl.ds(at, cols)] = part.astype(jnp.float32)

    in_vmem = pl.BlockSpec(memory_space=pltpu.VMEM)
    return pl.pallas_call(
        kernel,
        in_specs=[pl.BlockSpec(memory_space=pltpu.SMEM)] + [in_vmem] * groups,
        out_specs=[in_vmem] * 2,
        out_shape=[
            shaped((rows_out, groups * cols), jnp.float32),
            shaped((rows_in, groups * groups * cols), jnp.float32),
        ],
        compiler_params=params(40),
        cost_estimate=cost(height * cols * 1024),
        name="order_feed_forward",
    )(place.scalars, *blocks)


def order_attention(place, blocks_a, blocks_b, rows):
    groups = place.groups
    size = blocks_b[0].shape[1] // 3
    skip = blocks_a[0].shape[1] - 3 * size
    width = groups * skip

    def kernel(where, *refs):
        *blocks, attn_ref, qkv_ref, small_ref = refs
        for n in range(groups):
            ref = blocks[n]
            g = where[2] ^ turn(n, where[0])
            attn_ref[:, pl.ds(pl.multiple_of(g * skip, LANES), skip)] = ref[:, 0:skip].astype(
                jnp.float32
            )
            for part in range(3):
                at = pl.multiple_of(part * width + g * size, LANES)
                block = ref[:, skip + part * size : skip + (part + 1) * size]
                qkv_ref[:, pl.ds(at, size)] = block.astype(jnp.float32)
        for n in range(groups):
            ref = blocks[groups + n]
            g = where[2] ^ n
            lines = []
            for part in range(3):
                at = pl.multiple_of(part * width + width // 2 + g * size, LANES)
                here = slice(part * size, (part + 1) * size)
                qkv_ref[:, pl.ds(at, size)] = ref[0:rows, here].astype(jnp.float32)
                lines.append(ref[rows : rows + 16, here].astype(jnp.float32)[0:1])
            lines.append(jnp.zeros((5, size), jnp.float32))
            small_ref[pl.ds(pl.multiple_of(g * 8, 8), 8), :] = jnp.concatenate(lines)

    in_vmem = pl.BlockSpec(memory_space=pltpu.VMEM)
    return pl.pallas_call(
        kernel,
        in_specs=[pl.BlockSpec(memory_space=pltpu.SMEM)] + [in_vmem] * (2 * groups),
        out_specs=[in_vmem] * 3,
        out_shape=[
            shaped((rows, width), jnp.float32),
            shaped((rows, 3 * width), jnp.float32),
            shaped((8 * groups, size), jnp.float32),
        ],
        compiler_params=params(40),
        name="order_attention",
    )(place.scalars, *blocks_a, *blocks_b)


def on_device_permutes(
    tokens,
    segment_ids,
    keep_flag,
    cotangent,
    w_qkv,
    b_query,
    b_value,
    w_attn_out,
    b_attn_out,
    norm1_gain,
    norm1_bias,
    w_in,
    b_in,
    w_out,
    b_out,
    norm2_gain,
    norm2_bias,
    *,
    groups,
    shards,
):
    place = Place(groups, shards)
    _, length, width = tokens.shape
    rows = tokens[0]
    seg_row = segment_ids.reshape(1, length)
    pairs = width // LANES

    c1 = Gather(place, w_qkv)
    c2 = Gather(place, jnp.concatenate([w_in, w_attn_out], 1))
    c3 = Gather(place, w_out)
    c1.chips_near()
    small = Vectors(
        place,
        (b_query, b_value, b_attn_out, norm1_gain, norm1_bias, b_out, norm2_gain, norm2_bias, b_in),
    )
    meet(rows, c1, small)
    pair = c1.chips_far()
    small.chips_near()
    meet(pair, c1, small)
    joined = c1.join()
    c1.near()
    small.chips_far()
    c2.chips_near(joined)
    meet(joined, c2, small)
    small.landed()
    pair = c2.chips_far()
    vectors, bias_in, qkv_bias, seg_col, keep = small.unpack(
        seg_row, keep_flag.reshape(1, length)
    )
    c1.flying = lax.optimization_barrier(c1.flying)
    turned = turned_rows(place, after(rows, vectors))
    c1.far(pair, vectors)
    c1.cross(0, 1, 2)
    joined = c2.join()
    meet((joined, turned), c1)
    c1.landed()
    c2.near(c1.held[3])
    c1.cross(3)
    c3.chips_near(c1.held[3])
    blank = jnp.ones((1, width), jnp.float32)
    qkv_scale = jnp.concatenate([blank / math.sqrt(HD), blank, blank], 1)

    mixed, full_qkv = project_qkv(place, rows, Window(c1, 0, w_qkv.shape[1]), qkv_bias, qkv_scale)
    meet(mixed, c3)
    pair = c3.chips_far()
    c2.cross(0, wait=(mixed,))
    first, second = pairs * 3 // 8, pairs * 3 // 4
    forward = attention_forward(after(mixed, pair), seg_col, seg_row, 0, first)
    meet(forward[0], c2, c3)
    c2.far()
    joined = c3.join()
    c3.near()
    c2.cross(1, 2)
    forward = attention_forward(
        after(mixed, joined), seg_col, seg_row, first, second - first, forward
    )
    meet(forward[0], c2)
    c2.landed()
    c2.cross(3)
    contexts, probs = attention_forward(
        after(mixed, c2.held[3]), seg_col, seg_row, second, pairs - second, forward
    )
    normed, scale_one, normed_low, full_attn = project_out(
        place, contexts, Window(c2, w_in.shape[1], w_attn_out.shape[1]), rows, vectors
    )
    meet(normed_low, c3)
    c3.far()
    c3.cross(0, 1, 2)
    hidden, slope, full_in = feed_in(
        place, after(normed_low, c3.held[1]), Window(c2, 0, w_in.shape[1]), bias_in
    )
    meet(hidden, c3)
    c3.landed()
    c3.cross(3)
    layer_out, second_grad, out_low, second_sums, pre_low, bias_in_grad = feed_out(
        place, hidden, Window(c3, 0, w_out.shape[1]), normed, cotangent[0], keep, vectors, slope
    )

    r_out = Reduction(place, weight_grad(place, hidden, out_low, False, "out"))
    r_in = Reduction(place, weight_grad(place, after(normed_low, r_out.made), pre_low, True, "in"))
    meet(r_in.made, r_out)
    step = r_out.near()
    first_grad, attn_low, context_grad, first_sums = feed_in_back(
        after(pre_low, r_in.made, step), full_in, second_grad, normed, scale_one, vectors, full_attn
    )
    meet(attn_low, r_in)
    step = r_in.near()
    half, quarter = pairs // 2, pairs // 4

    def back(wait, start, count, at, before=None):
        return attention_backward(
            mixed,
            contexts,
            after(context_grad, *wait),
            probs,
            start,
            count,
            at,
            half,
            before,
        )

    low_a, late_a = back((step,), 0, half, 0)
    meet(late_a, r_out, r_in)
    steps = (r_out.middle(), r_in.middle())
    r_a = Reduction(
        place, attention_grads(place, after(turned, *steps), low_a, (contexts, attn_low), "a")
    )
    meet(r_a.made, r_out)
    step = r_out.along()
    part = back((r_a.made, step), half, quarter, 0)
    meet(part[1], r_out, r_in, r_a)
    steps = (r_out.along_far(), r_in.along(), r_a.near())
    low_b, late_b = back(steps, half + quarter, quarter, quarter, part)
    meet(late_b, r_out, r_in, r_a)
    sums = pack_sums(late_a, late_b, first_sums, second_sums, bias_in_grad)
    share_out = r_out.share()
    steps = (r_in.along_far(), r_a.middle(), share_out)
    r_b = Reduction(place, attention_grads(place, after(turned, *steps), low_b, (sums,), "b"))
    meet(r_b.made, r_in, r_a)
    share_in = r_in.share()
    inner = share_in.shape[1] // groups
    joined = jnp.concatenate(
        [share_out] + [share_in[:, n * inner : (n + 1) * inner] for n in range(groups)]
    )
    all_ffn = Replication(place, joined)
    grads = (low_a, after(low_b, r_b.made, joined, r_a.along()))
    tiles = length // TILE // 2
    input_grad = project_qkv_back(grads, full_qkv, first_grad, 0, tiles)
    meet(input_grad, r_b, r_a, all_ffn)
    steps = (r_b.near(), r_a.along_far())
    input_grad = project_qkv_back(
        grads, full_qkv, after(first_grad, *steps), tiles, tiles, input_grad
    )
    meet(input_grad, r_b, r_a)
    middle = r_b.middle()
    r_a.flying = after(r_a.flying, middle)
    all_a = Replication(place, r_a.share())
    meet(all_a.blocks[0], r_b, all_a)
    along = r_b.along_direct()
    all_a.flying = after(all_a.flying, along)
    all_ffn.flying = after(all_ffn.flying, along)
    pairs_made = (all_a.far(), all_ffn.far())
    meet(pairs_made, r_b)
    share_b = r_b.share_direct()
    all_b = Replication(place, share_b, direct=True)
    meet(share_b, all_ffn)
    w_out_grad, w_in_grad = order_feed_forward(place, all_ffn.landed(), share_in.shape[0])
    all_a.flying = after(all_a.flying, w_out_grad)
    w_attn_grad, w_qkv_grad, small = order_attention(
        place, all_a.landed(), all_b.landed(), w_attn_out.shape[0]
    )
    small = [small[8 * (n // 3) + n % 3] for n in range(12)]
    return (
        layer_out[None],
        input_grad[None],
        w_qkv_grad,
        small[B_QUERY],
        small[B_VALUE],
        w_attn_grad,
        small[B_ATTN],
        small[GAIN_ONE],
        small[SHIFT_ONE],
        w_in_grad,
        jnp.concatenate(small[B_IN:]),
        w_out_grad,
        small[B_OUT],
        small[GAIN_TWO],
        small[SHIFT_TWO],
    )


def solution(mesh):
    groups, shards = mesh.shape["grp"], mesh.shape["shard"]
    if groups == 4 and shards == 8:
        body = functools.partial(on_device_permutes, groups=groups, shards=shards)
    else:
        body = on_device
    return jax.shard_map(
        body,
        mesh=mesh,
        in_specs=(
            P(("grp", "shard"), None, None),
            P(("grp", "shard"), None),
            P(("grp", "shard"), None),
            P(("grp", "shard"), None, None),
            P("shard", "grp"),
            P("shard"),
            P("shard"),
            P("shard", "grp"),
            P("shard"),
            P("shard"),
            P("shard"),
            P("shard", "grp"),
            P("shard"),
            P("shard", "grp"),
            P("shard"),
            P("shard"),
            P("shard"),
        ),
        out_specs=(
            P(("grp", "shard"), None, None),
            P(("grp", "shard"), None, None),
            P("shard", None),
            P("shard"),
            P("shard"),
            P("shard", None),
            P("shard"),
            P("shard"),
            P("shard"),
            P("shard", None),
            P("shard"),
            P("shard", None),
            P("shard"),
            P("shard"),
            P("shard"),
        ),
        check_vma=False,
    )
```

```python
import functools
import math

import jax
import jax.numpy as jnp
from jax import lax
from jax.experimental import pallas as pl
from jax.experimental.pallas import tpu as pltpu
from jax.sharding import PartitionSpec as P

H = 16
HD = 64


masked_score = -1e30
epsilon = 1e-05


def norm_layer(rows, gain_row, shift_row):
    row_mean = jnp.mean(rows, -1, keepdims=True)
    centered = rows - row_mean
    row_var = jnp.mean(centered * centered, -1, keepdims=True)
    return centered * lax.rsqrt(row_var + epsilon) * gain_row + shift_row


def gelu_exact(values):
    return 0.5 * values * (1.0 + lax.erf(values * (1.0 / math.sqrt(2.0))))


def contract_rows(left, right):
    return lax.dot_general(
        left, right, (((0,), (0,)), ((), ())), preferred_element_type=jnp.float32
    )


def contract_cols(left, right):
    return lax.dot_general(
        left, right, (((1,), (1,)), ((), ())), preferred_element_type=jnp.float32
    )


def attend_forward(queries, key_rows, value_rows, segment_row, block_rows):
    length, model_width = queries.shape
    scaling = 1.0 / math.sqrt(HD)
    key_heads = key_rows.reshape(length, H, HD)
    value_heads = value_rows.reshape(length, H, HD)
    query_blocks = queries.reshape(length // block_rows, block_rows, H, HD)
    segment_blocks = segment_row.reshape(length // block_rows, block_rows)

    def one_block(pieces):
        query_part, segment_part = pieces
        scores = (
            jnp.einsum("qhd,khd->hqk", query_part, key_heads, preferred_element_type=jnp.float32)
            * scaling
        )
        allowed = segment_part[:, None] == segment_row[None, :]
        scores = jnp.where(allowed[None], scores, masked_score)
        row_max = jnp.max(scores, -1, keepdims=True)
        powers = jnp.exp(scores - row_max)
        totals = jnp.sum(powers, -1, keepdims=True)
        attn_probs = (powers / totals).astype(jnp.bfloat16)
        context = jnp.einsum(
            "hqk,khd->qhd", attn_probs, value_heads, preferred_element_type=jnp.float32
        )
        return (
            context.reshape(block_rows, model_width).astype(jnp.bfloat16),
            (row_max + jnp.log(totals))[:, :, 0],
        )

    contexts, log_sums = lax.map(one_block, (query_blocks, segment_blocks))
    return (contexts.reshape(length, model_width), log_sums)


def attend_backward(queries, key_rows, value_rows, segment_row, log_sums, context_grad, block_rows):
    length, model_width = queries.shape
    scaling = 1.0 / math.sqrt(HD)
    key_heads = key_rows.reshape(length, H, HD)
    value_heads = value_rows.reshape(length, H, HD)
    query_blocks = queries.reshape(length // block_rows, block_rows, H, HD)
    segment_blocks = segment_row.reshape(length // block_rows, block_rows)
    grad_blocks = context_grad.reshape(length // block_rows, block_rows, H, HD)

    def one_block(running, pieces):
        key_acc, value_acc = running
        query_part, segment_part, lse_part, grad_part = pieces
        scores = (
            jnp.einsum("qhd,khd->hqk", query_part, key_heads, preferred_element_type=jnp.float32)
            * scaling
        )
        allowed = segment_part[:, None] == segment_row[None, :]
        scores = jnp.where(allowed[None], scores, masked_score)
        probs = jnp.exp(scores - lse_part[:, :, None])
        prob_low = probs.astype(jnp.bfloat16)
        prob_grad = jnp.einsum(
            "qhd,khd->hqk", grad_part, value_heads, preferred_element_type=jnp.float32
        )
        row_dot = jnp.sum(prob_grad * probs, -1, keepdims=True)
        score_grad = (probs * (prob_grad - row_dot)).astype(jnp.bfloat16)
        query_grad = (
            jnp.einsum("hqk,khd->qhd", score_grad, key_heads, preferred_element_type=jnp.float32)
            * scaling
        )
        key_acc = (
            key_acc
            + jnp.einsum("hqk,qhd->khd", score_grad, query_part, preferred_element_type=jnp.float32)
            * scaling
        )
        value_acc = value_acc + jnp.einsum(
            "hqk,qhd->khd", prob_low, grad_part, preferred_element_type=jnp.float32
        )
        return ((key_acc, value_acc), query_grad.reshape(block_rows, model_width))

    empty_acc = jnp.zeros((length, H, HD), jnp.float32)
    (key_grad, value_grad), query_grads = lax.scan(
        one_block, (empty_acc, empty_acc), (query_blocks, segment_blocks, log_sums, grad_blocks)
    )
    return (
        query_grads.reshape(length, model_width),
        key_grad.reshape(length, model_width),
        value_grad.reshape(length, model_width),
    )


def on_device(
    tokens,
    segment_ids,
    keep_flag,
    cotangent,
    w_qkv,
    b_query,
    b_value,
    w_attn_out,
    b_attn_out,
    norm1_gain,
    norm1_bias,
    w_in,
    b_in,
    w_out,
    b_out,
    norm2_gain,
    norm2_bias,
):
    seq_count, length, model_width = tokens.shape
    block_rows = min(512, length)
    within = (
        lax.all_gather(w_qkv, "shard", axis=0, tiled=True),
        lax.all_gather(w_attn_out, "shard", axis=0, tiled=True),
        lax.all_gather(w_in, "shard", axis=0, tiled=True),
        lax.all_gather(w_out, "shard", axis=0, tiled=True),
        lax.all_gather(b_query, "shard", axis=0, tiled=True),
        lax.all_gather(b_value, "shard", axis=0, tiled=True),
        lax.all_gather(b_attn_out, "shard", axis=0, tiled=True),
        lax.all_gather(norm1_gain, "shard", axis=0, tiled=True),
        lax.all_gather(norm1_bias, "shard", axis=0, tiled=True),
        lax.all_gather(b_in, "shard", axis=0, tiled=True),
        lax.all_gather(b_out, "shard", axis=0, tiled=True),
        lax.all_gather(norm2_gain, "shard", axis=0, tiled=True),
        lax.all_gather(norm2_bias, "shard", axis=0, tiled=True),
    )
    full_qkv, full_attn, full_in, full_out = (
        lax.all_gather(within[0], "grp", axis=1, tiled=True),
        lax.all_gather(within[1], "grp", axis=1, tiled=True),
        lax.all_gather(within[2], "grp", axis=1, tiled=True),
        lax.all_gather(within[3], "grp", axis=1, tiled=True),
    )
    (
        bias_query,
        bias_value,
        bias_attn,
        gain_one,
        shift_one,
        bias_in,
        bias_out,
        gain_two,
        shift_two,
    ) = [piece.astype(jnp.float32) for piece in within[4:]]
    flat_rows = tokens.reshape(seq_count * length, model_width)
    mixed_qkv = jnp.dot(flat_rows, full_qkv, preferred_element_type=jnp.float32)
    queries = (mixed_qkv[:, :model_width] + bias_query).astype(jnp.bfloat16)
    key_rows = mixed_qkv[:, model_width : 2 * model_width].astype(jnp.bfloat16)
    value_rows = (mixed_qkv[:, 2 * model_width :] + bias_value).astype(jnp.bfloat16)
    query_seqs = queries.reshape(seq_count, length, model_width)
    key_seqs = key_rows.reshape(seq_count, length, model_width)
    value_seqs = value_rows.reshape(seq_count, length, model_width)

    def forward_sequence(pieces):
        return attend_forward(pieces[0], pieces[1], pieces[2], pieces[3], block_rows)

    contexts, log_sums = lax.map(forward_sequence, (query_seqs, key_seqs, value_seqs, segment_ids))
    contexts = contexts.reshape(seq_count * length, model_width)
    attended = jnp.dot(contexts, full_attn, preferred_element_type=jnp.float32) + bias_attn
    first_sum = flat_rows.astype(jnp.float32) + attended
    normed_one, norm_one_back = jax.vjp(norm_layer, first_sum, gain_one, shift_one)
    normed_low = normed_one.astype(jnp.bfloat16)
    hidden_pre = jnp.dot(normed_low, full_in, preferred_element_type=jnp.float32) + bias_in
    hidden, gelu_back = jax.vjp(gelu_exact, hidden_pre)
    hidden_low = hidden.astype(jnp.bfloat16)
    second_sum = normed_one + (
        jnp.dot(hidden_low, full_out, preferred_element_type=jnp.float32) + bias_out
    )
    result, norm_two_back = jax.vjp(norm_layer, second_sum, gain_two, shift_two)
    layer_out = result.astype(jnp.bfloat16).reshape(seq_count, length, model_width)
    again = (
        lax.all_gather(w_qkv, "shard", axis=0, tiled=True),
        lax.all_gather(w_attn_out, "shard", axis=0, tiled=True),
        lax.all_gather(w_in, "shard", axis=0, tiled=True),
        lax.all_gather(w_out, "shard", axis=0, tiled=True),
    )
    back_qkv, back_attn, back_in, back_out = (
        lax.all_gather(again[0], "grp", axis=1, tiled=True),
        lax.all_gather(again[1], "grp", axis=1, tiled=True),
        lax.all_gather(again[2], "grp", axis=1, tiled=True),
        lax.all_gather(again[3], "grp", axis=1, tiled=True),
    )
    masked_cot = cotangent.astype(jnp.float32).reshape(
        seq_count * length, model_width
    ) * keep_flag.reshape(seq_count * length, 1).astype(jnp.float32)
    second_grad, gain_two_grad, shift_two_grad = norm_two_back(masked_cot)
    bias_out_grad = jnp.sum(second_grad, 0)
    out_low = second_grad.astype(jnp.bfloat16)
    w_out_grad = contract_rows(hidden_low, out_low)
    hidden_grad = contract_cols(out_low, back_out)
    (pre_grad,) = gelu_back(hidden_grad)
    bias_in_grad = jnp.sum(pre_grad, 0)
    pre_low = pre_grad.astype(jnp.bfloat16)
    w_in_grad = contract_rows(normed_low, pre_low)
    normed_grad = second_grad + contract_cols(pre_low, back_in)
    first_grad, gain_one_grad, shift_one_grad = norm_one_back(normed_grad)
    bias_attn_grad = jnp.sum(first_grad, 0)
    attn_low = first_grad.astype(jnp.bfloat16)
    w_attn_grad = contract_rows(contexts, attn_low)
    context_grad = contract_cols(attn_low, back_attn).astype(jnp.bfloat16)

    def backward_sequence(pieces):
        return attend_backward(
            pieces[0], pieces[1], pieces[2], pieces[3], pieces[4], pieces[5], block_rows
        )

    query_grad, key_grad, value_grad = lax.map(
        backward_sequence,
        (
            query_seqs,
            key_seqs,
            value_seqs,
            segment_ids,
            log_sums,
            context_grad.reshape(seq_count, length, model_width),
        ),
    )
    query_grad = query_grad.reshape(seq_count * length, model_width)
    key_grad = key_grad.reshape(seq_count * length, model_width)
    value_grad = value_grad.reshape(seq_count * length, model_width)
    bias_query_grad = jnp.sum(query_grad, 0)
    bias_value_grad = jnp.sum(value_grad, 0)
    qkv_low = jnp.concatenate([query_grad, key_grad, value_grad], 1).astype(jnp.bfloat16)
    w_qkv_grad = contract_rows(flat_rows, qkv_low)
    input_grad = first_grad + contract_cols(qkv_low, back_qkv)
    reduced = (
        lax.psum_scatter(
            w_qkv_grad.astype(jnp.bfloat16), "shard", scatter_dimension=0, tiled=True
        ).astype(jnp.float32),
        lax.psum_scatter(
            bias_query_grad.astype(jnp.bfloat16), "shard", scatter_dimension=0, tiled=True
        ).astype(jnp.float32),
        lax.psum_scatter(
            bias_value_grad.astype(jnp.bfloat16), "shard", scatter_dimension=0, tiled=True
        ).astype(jnp.float32),
        lax.psum_scatter(
            w_attn_grad.astype(jnp.bfloat16), "shard", scatter_dimension=0, tiled=True
        ).astype(jnp.float32),
        lax.psum_scatter(
            bias_attn_grad.astype(jnp.bfloat16), "shard", scatter_dimension=0, tiled=True
        ).astype(jnp.float32),
        lax.psum_scatter(
            gain_one_grad.astype(jnp.bfloat16), "shard", scatter_dimension=0, tiled=True
        ).astype(jnp.float32),
        lax.psum_scatter(
            shift_one_grad.astype(jnp.bfloat16), "shard", scatter_dimension=0, tiled=True
        ).astype(jnp.float32),
        lax.psum_scatter(
            w_in_grad.astype(jnp.bfloat16), "shard", scatter_dimension=0, tiled=True
        ).astype(jnp.float32),
        lax.psum_scatter(
            bias_in_grad.astype(jnp.bfloat16), "shard", scatter_dimension=0, tiled=True
        ).astype(jnp.float32),
        lax.psum_scatter(
            w_out_grad.astype(jnp.bfloat16), "shard", scatter_dimension=0, tiled=True
        ).astype(jnp.float32),
        lax.psum_scatter(
            bias_out_grad.astype(jnp.bfloat16), "shard", scatter_dimension=0, tiled=True
        ).astype(jnp.float32),
        lax.psum_scatter(
            gain_two_grad.astype(jnp.bfloat16), "shard", scatter_dimension=0, tiled=True
        ).astype(jnp.float32),
        lax.psum_scatter(
            shift_two_grad.astype(jnp.bfloat16), "shard", scatter_dimension=0, tiled=True
        ).astype(jnp.float32),
    )
    summed = (
        lax.psum(reduced[0].astype(jnp.bfloat16), "grp").astype(jnp.float32),
        lax.psum(reduced[1].astype(jnp.bfloat16), "grp").astype(jnp.float32),
        lax.psum(reduced[2].astype(jnp.bfloat16), "grp").astype(jnp.float32),
        lax.psum(reduced[3].astype(jnp.bfloat16), "grp").astype(jnp.float32),
        lax.psum(reduced[4].astype(jnp.bfloat16), "grp").astype(jnp.float32),
        lax.psum(reduced[5].astype(jnp.bfloat16), "grp").astype(jnp.float32),
        lax.psum(reduced[6].astype(jnp.bfloat16), "grp").astype(jnp.float32),
        lax.psum(reduced[7].astype(jnp.bfloat16), "grp").astype(jnp.float32),
        lax.psum(reduced[8].astype(jnp.bfloat16), "grp").astype(jnp.float32),
        lax.psum(reduced[9].astype(jnp.bfloat16), "grp").astype(jnp.float32),
        lax.psum(reduced[10].astype(jnp.bfloat16), "grp").astype(jnp.float32),
        lax.psum(reduced[11].astype(jnp.bfloat16), "grp").astype(jnp.float32),
        lax.psum(reduced[12].astype(jnp.bfloat16), "grp").astype(jnp.float32),
    )
    return (
        layer_out,
        input_grad.reshape(seq_count, length, model_width),
        summed[0],
        summed[1],
        summed[2],
        summed[3],
        summed[4],
        summed[5],
        summed[6],
        summed[7],
        summed[8],
        summed[9],
        summed[10],
        summed[11],
        summed[12],
    )


NT = (((1,), (1,)), ((), ()))
NN = (((1,), (0,)), ((), ()))
TN = (((0,), (0,)), ((), ()))
LANES = 128
AXES = ("grp", "shard")


def mxu(left, right, dims):
    return lax.dot_general(left, right, dims, preferred_element_type=jnp.float32)


def cost(flops):
    return pl.CostEstimate(flops=2 * flops, bytes_accessed=0, transcendentals=0)


def params(megabytes=60):
    return pltpu.CompilerParams(vmem_limit_bytes=megabytes << 20)


def attention_forward_kernel(q_ref, k_ref, v_ref, seg_col, seg_row, out_ref, probs_ref, scale_ref, *, rows):
    length = q_ref.shape[0]
    first = lax.broadcasted_iota(jnp.int32, (1, LANES), 1) < HD
    keys = k_ref[...]
    values = v_ref[...]
    zero = jnp.zeros_like(keys)
    head_keys = (jnp.where(first, keys, zero), jnp.where(first, zero, keys))
    key_segments = seg_col[...]
    for block in range(length // rows):
        here = pl.ds(block * rows, rows)
        q = q_ref[here, :]
        allowed = key_segments == seg_row[:, here]
        outs, scales = [], []
        for head in range(2):
            scores = mxu(head_keys[head], q, NT)
            scores = jnp.where(allowed, scores, masked_score)
            powers = jnp.exp(scores - jnp.max(scores, 0, keepdims=True))
            scale = 1.0 / jnp.sum(powers, 0, keepdims=True)
            scales.append(jnp.transpose(jnp.broadcast_to(scale, (LANES, rows))))
            powers = powers.astype(jnp.bfloat16)
            probs_ref[head, :, here] = powers
            outs.append(mxu(powers, values, TN))
        scale = jnp.where(first, scales[0], scales[1])
        scale_ref[here, :] = scale
        out_ref[here, :] = (jnp.where(first, outs[0], outs[1]) * scale).astype(jnp.bfloat16)


def attention_forward(qkv, seg_col, seg_row, start, pairs, before=None):
    length, width = qkv.shape[0], qkv.shape[1] // 3
    total = width // LANES
    rows = min(512, length)
    more = () if before is None else before

    def pair(part):
        return pl.BlockSpec((length, LANES), lambda j: (0, part * total + start + j))

    def body(q_ref, k_ref, v_ref, seg_c, seg_r, *refs):
        attention_forward_kernel(q_ref, k_ref, v_ref, seg_c, seg_r, *refs[-3:], rows=rows)

    return pl.pallas_call(
        body,
        grid=(pairs,),
        in_specs=[
            pair(0),
            pair(1),
            pair(2),
            pl.BlockSpec((length, 1), lambda j: (0, 0)),
            pl.BlockSpec((1, length), lambda j: (0, 0)),
        ]
        + [pl.BlockSpec(memory_space=pl.ANY)] * len(more),
        out_specs=[
            pl.BlockSpec((length, LANES), lambda j: (0, start + j)),
            pl.BlockSpec((2, length, length), lambda j: (start + j, 0, 0)),
            pl.BlockSpec((length, LANES), lambda j: (0, start + j)),
        ],
        out_shape=[
            jax.ShapeDtypeStruct((length, width), jnp.bfloat16),
            jax.ShapeDtypeStruct((2 * total, length, length), jnp.bfloat16),
            jax.ShapeDtypeStruct((length, width), jnp.float32),
        ],
        input_output_aliases={} if before is None else {5: 0, 6: 1, 7: 2},
        compiler_params=params(60),
        cost_estimate=cost(16 * length * length * pairs * LANES),
        name="attn_fwd",
    )(qkv, qkv, qkv, seg_col, seg_row, *more)


def attention_backward_kernel(
    q_ref, k_ref, v_ref, o_ref, do_ref, probs_ref, scale_ref, grad_ref, sum_ref
):
    first = lax.broadcasted_iota(jnp.int32, (1, LANES), 1) < HD
    pick = (
        lax.broadcasted_iota(jnp.int32, (8, LANES), 0)
        == lax.broadcasted_iota(jnp.int32, (8, LANES), 1) // HD
    ).astype(jnp.float32)
    q = q_ref[...]
    scaled = do_ref[...].astype(jnp.float32) * scale_ref[...]
    do = scaled.astype(jnp.bfloat16)
    keys = k_ref[...]
    values = v_ref[...]
    zero = jnp.zeros_like(values)
    head_values = (jnp.where(first, values, zero), jnp.where(first, zero, values))
    dots = lax.dot_general(
        pick,
        scaled * o_ref[...].astype(jnp.float32),
        NT,
        precision=lax.Precision.HIGHEST,
        preferred_element_type=jnp.float32,
    )
    query_parts, key_parts, value_parts = [], [], []
    for head in range(2):
        probs = probs_ref[head]
        prob_grad = mxu(head_values[head], do, NT)
        score_grad = probs.astype(jnp.float32) * (prob_grad - dots[head : head + 1, :])
        score_grad = score_grad.astype(jnp.bfloat16)
        value_parts.append(mxu(probs, do, NN))
        key_parts.append(mxu(score_grad, q, NN))
        query_parts.append(mxu(score_grad, keys, TN))
    query_grad = jnp.where(first, *query_parts) * (1.0 / math.sqrt(HD))
    value_grad = jnp.where(first, *value_parts)
    grad_ref[0] = query_grad.astype(jnp.bfloat16)
    grad_ref[1] = jnp.where(first, *key_parts).astype(jnp.bfloat16)
    grad_ref[2] = value_grad.astype(jnp.bfloat16)
    sum_ref[0:1, :] = jnp.sum(query_grad, 0, keepdims=True)
    sum_ref[1:2, :] = jnp.sum(value_grad, 0, keepdims=True)


def attention_backward(qkv, out, out_grad, probs, scale, start, pairs, at, size, before=None):
    length, width = out.shape
    total = width // LANES
    more = () if before is None else before

    def pair(part):
        return pl.BlockSpec((length, LANES), lambda j: (0, part * total + start + j))

    def body(*refs):
        attention_backward_kernel(*refs[:7], *refs[-2:])

    return pl.pallas_call(
        body,
        grid=(pairs,),
        in_specs=[
            pair(0),
            pair(1),
            pair(2),
            pair(0),
            pair(0),
            pl.BlockSpec((2, length, length), lambda j: (start + j, 0, 0)),
            pair(0),
        ]
        + [pl.BlockSpec(memory_space=pl.ANY)] * len(more),
        out_specs=[
            pl.BlockSpec((3, length, LANES), lambda j: (0, 0, j + at)),
            pl.BlockSpec((2, LANES), lambda j: (0, j + at)),
        ],
        out_shape=[
            jax.ShapeDtypeStruct((3, length, size * LANES), jnp.bfloat16),
            jax.ShapeDtypeStruct((2, size * LANES), jnp.float32),
        ],
        input_output_aliases={} if before is None else {7: 0, 8: 1},
        compiler_params=params(60),
        cost_estimate=cost(32 * length * length * pairs * LANES),
        name="attn_bwd",
    )(qkv, qkv, qkv, out, out_grad, probs, scale, *more)


class Place:
    def __init__(self, groups, shards):
        self.groups = groups
        self.shards = shards
        self.chips = shards // 2
        self.grp = lax.axis_index("grp")
        self.shard = lax.axis_index("shard")
        self.core = self.shard % 2
        self.chip = self.shard // 2
        self.scalars = jnp.stack([self.core, self.chip, self.grp]).astype(jnp.int32)

    def permute(self, array, mask_of_core):
        pairs = [(i, i ^ mask_of_core[i % 2]) for i in range(self.groups * self.shards)]
        return lax.ppermute(array, AXES, pairs)

    def swap_core(self, array):
        return self.permute(array, (1, 1))

    def swap_grp(self, array, step):
        masks = (self.shards, 2 * self.shards)
        return self.permute(array, masks if step == 0 else masks[::-1])

    def swap_chip(self, array, step):
        masks = (2, 4)
        return self.permute(array, masks if step == 0 else masks[::-1])

    def slot_chip(self, slot):
        return self.chip ^ turn(slot, self.core)

    def slot_grp(self, slot):
        return self.grp ^ turn(slot, self.core)


def turn(slot, core):
    if isinstance(slot, int):
        return slot if slot in (0, 3) else jnp.where(core == 0, slot, 3 - slot)
    return jnp.where((core == 0) | (slot == 0) | (slot == 3), slot, 3 - slot)


def after(value, *others):
    return lax.optimization_barrier((value, *others))[0]


def meet(anchor, *flights):
    arrays = [f.flying for f in flights]
    _, *arrays = lax.optimization_barrier((anchor, *arrays))
    for f, array in zip(flights, arrays):
        f.flying = array


class Gather:
    def __init__(self, place, piece):
        self.place = place
        self.piece = piece
        self.held = [None] * 4
        self.crossed = [None] * 4

    def chips_near(self, *wait):
        self.piece = after(self.piece, *wait)
        self.flying = self.place.swap_chip(self.piece, 0)

    def chips_far(self):
        self.pair = jnp.stack([self.piece, self.flying])
        self.flying = self.place.swap_chip(self.pair, 1)
        return self.pair

    def join(self):
        self.held[0] = jnp.concatenate([self.pair, self.flying])
        return self.held[0]

    def near(self, *wait):
        self.held[0] = after(self.held[0], *wait)
        self.flying = (self.place.swap_grp(self.held[0], 0), self.place.swap_grp(self.held[0], 1))
        return self.held[0]

    def far(self, *wait):
        self.held[1:3] = self.flying
        first = after(self.held[1], *wait)
        self.flying = self.place.swap_grp(first, 1)

    def landed(self):
        self.held[3] = self.flying

    def cross(self, *which, wait=()):
        for n in which:
            self.crossed[n] = self.place.swap_core(after(self.held[n], *wait))

    def pieces(self):
        return self.held + self.crossed


class Window:
    def __init__(self, gather, start, cols):
        self.arrays = gather.pieces()
        self.start, self.cols = start, cols
        chips, rows, _ = self.arrays[0].shape
        self.chips, self.rows = chips, rows


def fetch(where, window, refs, whole, sem, by):
    rows, cols, chips = window.rows, window.cols, window.chips
    for slot in range(4):
        for side in range(2):
            core = where[0] ^ side
            ref = refs[4 * side + slot]
            distance = turn(slot, core)
            col = pl.multiple_of((where[2] ^ distance) * cols, LANES)
            for k in range(chips):
                row = ((where[1] ^ turn(k, core)) * 2 + core) * rows
                pltpu.make_async_copy(
                    ref.at[k, :, pl.ds(window.start, cols)],
                    whole.at[pl.ds(pl.multiple_of(row, rows), rows), pl.ds(col, cols)],
                    sem.at[distance if by == "grp" else 0],
                ).start()


def weight_call(place, kernel, window, inputs, in_specs, outs, out_specs, steps, by, name, flops, write=True):
    cols, groups = window.cols, place.groups
    pieces = window.arrays
    shape = (window.chips * 2 * window.rows, groups * cols)
    slots = {"grp": groups, "all": 1}[by]
    anywhere = pl.BlockSpec(memory_space=pl.ANY)

    def body(where, *refs):
        taken, refs = refs[: len(pieces)], refs[len(pieces) :]
        *refs, weight, sem, out_sem = refs
        if write:
            *refs, written = refs
        step = pl.program_id(0)

        @pl.when(step == 0)
        def _():
            fetch(where, window, taken, weight, sem, by)

        def ready():
            if by == "all":

                @pl.when(step == 0)
                def _():
                    pltpu.make_async_copy(weight, weight, sem.at[0]).wait()
                    if write:
                        pltpu.make_async_copy(weight, written, out_sem.at[0]).start()

            else:
                at = pl.ds(pl.multiple_of((where[2] ^ step) * cols, LANES), cols)
                view = weight.at[:, at]
                pltpu.make_async_copy(view, view, sem.at[step]).wait()
                pltpu.make_async_copy(view, written.at[:, at], out_sem.at[step]).start()

        kernel(where, ready, weight, *refs)

        @pl.when(step == (steps - 1 if write else -1))
        def _():
            for slot in range(slots if write else 0):
                width = shape[1] // slots
                view = weight.at[:, pl.ds(slot * width, width)]
                pltpu.make_async_copy(view, view, out_sem.at[slot]).wait()

    total = sum(math.prod(x.shape) * x.dtype.itemsize for x in list(inputs) + list(outs))
    return pl.pallas_call(
        body,
        grid_spec=pltpu.PrefetchScalarGridSpec(
            num_scalar_prefetch=1,
            grid=(steps,),
            in_specs=[anywhere] * len(pieces) + in_specs,
            out_specs=out_specs + [anywhere] * write,
            scratch_shapes=[
                pltpu.VMEM(shape, jnp.bfloat16),
                pltpu.SemaphoreType.DMA((slots,)),
                pltpu.SemaphoreType.DMA((slots,)),
            ],
        ),
        out_shape=outs + [shaped(shape, jnp.bfloat16)] * write,
        compiler_params=params(60),
        cost_estimate=cost(flops),
        name=name,
    )(place.scalars, *pieces, *inputs)


def plain_call(kernel, inputs, in_specs, outs, out_specs, steps, name, flops):
    total = sum(math.prod(x.shape) * x.dtype.itemsize for x in list(inputs) + list(outs))
    return pl.pallas_call(
        kernel,
        grid=(steps,),
        in_specs=in_specs,
        out_specs=out_specs,
        out_shape=outs,
        compiler_params=params(60),
        cost_estimate=cost(flops),
        name=name,
    )(*inputs)


TILE = 256


def row_tiles(width):
    return pl.BlockSpec((TILE, width), lambda i, *s: (i, 0))


def fixed(*shape):
    return pl.BlockSpec(shape, lambda i, *s: (0,) * len(shape))


def whole_once(shape):
    return pl.BlockSpec(shape, lambda i: (0,) * len(shape), pipeline_mode=pl.Buffered(1))


def shaped(shape, dtype):
    return jax.ShapeDtypeStruct(shape, dtype)


B_QUERY, B_VALUE, B_ATTN, GAIN_ONE, SHIFT_ONE, B_OUT, GAIN_TWO, SHIFT_TWO, B_IN = range(9)


def row(ref, n):
    return ref[n : n + 1, :]


class Vectors:
    def __init__(self, place, vectors):
        lines = [v.reshape(-1, LANES) for v in vectors]
        blank = jnp.zeros((-sum(x.shape[0] for x in lines) % 16, LANES), jnp.bfloat16)
        self.own = jnp.concatenate([*lines, blank])
        self.place = place
        self.flying = place.swap_core(self.own)

    def chips_near(self):
        self.own = jnp.stack([self.own, self.flying])
        self.flying = self.place.swap_chip(self.own, 0)

    def chips_far(self):
        self.own = jnp.stack([self.own, self.flying])
        self.flying = self.place.swap_chip(self.own, 1)

    def landed(self):
        self.slots = jnp.concatenate([self.own, self.flying])

    def unpack(self, seg_row, keep_row):
        place = self.place
        length = seg_row.shape[1]
        slots, sides, rows, lanes = self.slots.shape
        shards = place.shards

        def kernel(where, in_ref, seg_ref, keep_ref, *outs):
            rows_ref, inner_ref, qkv_ref, seg_col_ref, keep_col_ref = outs
            for line_ref, col_ref in ((seg_ref, seg_col_ref), (keep_ref, keep_col_ref)):
                line = jnp.broadcast_to(line_ref[...].astype(jnp.float32), (8, length))
                col_ref[...] = line.T[:, 0:1].astype(col_ref.dtype)
            width = shards * lanes
            qkv_ref[...] = jnp.zeros_like(qkv_ref)
            for slot in range(slots):
                for side in range(sides):
                    core = where[0] ^ side
                    shard = (where[1] ^ turn(slot, where[0])) * 2 + core
                    part = in_ref[slot, side].astype(jnp.float32)
                    at = pl.multiple_of(shard * lanes, lanes)
                    rows_ref[:, pl.ds(at, lanes)] = part
                    qkv_ref[:, pl.ds(at, lanes)] = part[B_QUERY : B_QUERY + 1]
                    qkv_ref[:, pl.ds(2 * width + at, lanes)] = part[B_VALUE : B_VALUE + 1]
                    for n in range(4):
                        start = pl.multiple_of((shard * 4 + n) * lanes, lanes)
                        inner_ref[:, pl.ds(start, lanes)] = part[B_IN + n : B_IN + n + 1]

        in_vmem = pl.BlockSpec(memory_space=pltpu.VMEM)
        return pl.pallas_call(
            kernel,
            in_specs=[pl.BlockSpec(memory_space=pltpu.SMEM)] + [in_vmem] * 3,
            out_specs=[in_vmem] * 5,
            out_shape=[
                shaped((rows, shards * lanes), jnp.float32),
                shaped((1, 4 * shards * lanes), jnp.float32),
                shaped((1, 3 * shards * lanes), jnp.float32),
                shaped((length, 1), jnp.int32),
                shaped((length, 1), jnp.float32),
            ],
            name="vectors",
        )(place.scalars, self.slots, seg_row, keep_row)


def project_qkv(place, rows, window, bias, scale):
    length, width = rows.shape
    cols = window.cols

    def kernel(where, ready, weight, x_ref, bias_ref, scale_ref, out_ref):
        ready()
        at = pl.ds(pl.multiple_of((where[2] ^ pl.program_id(0)) * cols, LANES), cols)
        for tile in range(length // TILE):
            here = pl.ds(tile * TILE, TILE)
            mixed = mxu(x_ref[here, :], weight[:, at], NN) + bias_ref[:, at]
            mixed = mixed.astype(jnp.bfloat16).astype(jnp.float32) * scale_ref[:, at]
            out_ref[here, :] = mixed.astype(jnp.bfloat16)

    total = cols * place.groups
    return weight_call(
        place,
        kernel,
        window,
        (rows, bias, scale),
        [fixed(length, width), fixed(1, total), fixed(1, total)],
        [shaped((length, total), jnp.bfloat16)],
        [pl.BlockSpec((length, cols), lambda i, s: (0, i ^ s[2]))],
        place.groups,
        "grp",
        "qkv",
        2 * length * width * total,
    )


def norm_parts(rows):
    centered = rows - jnp.mean(rows, -1, keepdims=True)
    scale = lax.rsqrt(jnp.mean(centered * centered, -1, keepdims=True) + epsilon)
    return centered * scale, scale


def norm_back(grad, normed, scale):
    return scale * (
        grad
        - jnp.mean(grad, -1, keepdims=True)
        - normed * jnp.mean(grad * normed, -1, keepdims=True)
    )


def add_rows(sum_ref, *terms):
    @pl.when(pl.program_id(0) == 0)
    def _():
        sum_ref[...] = jnp.zeros_like(sum_ref)

    for n, term in enumerate(terms):
        sum_ref[n : n + 1, :] += jnp.sum(term, 0, keepdims=True)


def project_out(place, contexts, window, rows, vectors):
    length, width = rows.shape

    def kernel(where, ready, weight, c_ref, x_ref, v_ref, n_ref, r_ref, low_ref):
        ready()
        first_sum = mxu(c_ref[...], weight[...], NN) + row(v_ref, B_ATTN)
        first_sum = first_sum + x_ref[...].astype(jnp.float32)
        normed, scale = norm_parts(first_sum)
        n_ref[...] = normed
        r_ref[...] = jnp.broadcast_to(scale, r_ref.shape)
        low_ref[...] = (normed * row(v_ref, GAIN_ONE) + row(v_ref, SHIFT_ONE)).astype(jnp.bfloat16)

    return weight_call(
        place,
        kernel,
        window,
        (contexts, rows, vectors),
        [row_tiles(width), row_tiles(width), fixed(*vectors.shape)],
        [
            shaped((length, width), jnp.float32),
            shaped((length, LANES), jnp.float32),
            shaped((length, width), jnp.bfloat16),
        ],
        [row_tiles(width), row_tiles(LANES), row_tiles(width)],
        length // TILE,
        "all",
        "attn_out",
        2 * length * width * width,
    )


def feed_in(place, normed_low, window, bias):
    length, width = normed_low.shape
    cols = window.cols

    def kernel(where, ready, weight, x_ref, bias_ref, hid_ref, slope_ref):
        ready()
        at = pl.ds(pl.multiple_of((where[2] ^ pl.program_id(0)) * cols, LANES), cols)
        for tile in range(length // TILE):
            here = pl.ds(tile * TILE, TILE)
            pre = mxu(x_ref[here, :], weight[:, at], NN) + bias_ref[:, at]
            share = 0.5 + 0.5 * lax.erf(pre * (1.0 / math.sqrt(2.0)))
            bell = jnp.exp(-0.5 * pre * pre) * (1.0 / math.sqrt(2.0 * math.pi))
            hid_ref[here, :] = (pre * share).astype(jnp.bfloat16)
            slope_ref[here, :] = (share + pre * bell).astype(jnp.bfloat16)

    total = cols * place.groups
    block = pl.BlockSpec((length, cols), lambda i, s: (0, i ^ s[2]))
    return weight_call(
        place,
        kernel,
        window,
        (normed_low, bias),
        [fixed(length, width), fixed(1, total)],
        [shaped((length, total), jnp.bfloat16)] * 2,
        [block, block],
        place.groups,
        "grp",
        "feed_in",
        2 * length * width * total,
    )


def feed_out(place, hidden, window, normed, cot, keep, vectors, slope):
    length, inner = hidden.shape
    width = normed.shape[1]

    def kernel(where, ready, weight, h_ref, n_ref, cot_ref, keep_ref, v_ref, slope_ref, *outs):
        out_ref, grad_ref, low_ref, sum_ref, pre_ref, inner_ref = outs
        ready()
        fed = mxu(h_ref[...], weight[...], NN)
        normed_one = n_ref[...] * row(v_ref, GAIN_ONE) + row(v_ref, SHIFT_ONE)
        second_sum = normed_one + (fed + row(v_ref, B_OUT))
        second, scale = norm_parts(second_sum)
        out_ref[...] = (second * row(v_ref, GAIN_TWO) + row(v_ref, SHIFT_TWO)).astype(jnp.bfloat16)
        masked = cot_ref[...].astype(jnp.float32) * keep_ref[...]
        grad = norm_back(masked * row(v_ref, GAIN_TWO), second, scale)
        grad_ref[...] = grad
        low = grad.astype(jnp.bfloat16)
        low_ref[...] = low
        add_rows(sum_ref, masked * second, masked, grad)

        @pl.when(pl.program_id(0) == 0)
        def _():
            inner_ref[...] = jnp.zeros_like(inner_ref)

        size = min(1024, inner)
        for n in range(inner // size):
            at = slice(n * size, (n + 1) * size)
            pre = mxu(low, weight[at, :], NT) * slope_ref[:, at].astype(jnp.float32)
            pre_ref[:, at] = pre.astype(jnp.bfloat16)
            inner_ref[:, at] += jnp.sum(pre, 0, keepdims=True)

    return weight_call(
        place,
        kernel,
        window,
        (hidden, normed, cot, keep, vectors, slope),
        [
            row_tiles(inner),
            row_tiles(width),
            row_tiles(width),
            row_tiles(1),
            fixed(*vectors.shape),
            row_tiles(inner),
        ],
        [
            shaped((length, width), jnp.bfloat16),
            shaped((length, width), jnp.float32),
            shaped((length, width), jnp.bfloat16),
            shaped((8, width), jnp.float32),
            shaped((length, inner), jnp.bfloat16),
            shaped((1, inner), jnp.float32),
        ],
        [
            row_tiles(width),
            row_tiles(width),
            row_tiles(width),
            fixed(8, width),
            row_tiles(inner),
            fixed(1, inner),
        ],
        length // TILE,
        "all",
        "feed_out",
        4 * length * width * inner,
        write=False,
    )


def feed_in_back(pre_low, weight, second_grad, normed, scale, vectors, attn_weight):
    length, inner = pre_low.shape
    width = normed.shape[1]

    def kernel(p_ref, w_ref, g_ref, n_ref, r_ref, v_ref, a_ref, first_ref, low_ref, ctx_ref, sum_ref):
        grad = g_ref[...] + mxu(p_ref[...], w_ref[...], NT)
        first = norm_back(grad * row(v_ref, GAIN_ONE), n_ref[...], r_ref[:, :1])
        low = first.astype(jnp.bfloat16)
        first_ref[...] = first
        low_ref[...] = low
        ctx_ref[...] = mxu(low, a_ref[...], NT).astype(jnp.bfloat16)
        add_rows(sum_ref, grad * n_ref[...], grad, first)

    return plain_call(
        kernel,
        (pre_low, weight, second_grad, normed, scale, vectors, attn_weight),
        [
            row_tiles(inner),
            whole_once(weight.shape),
            row_tiles(width),
            row_tiles(width),
            row_tiles(LANES),
            fixed(*vectors.shape),
            whole_once(attn_weight.shape),
        ],
        [
            shaped((length, width), jnp.float32),
            shaped((length, width), jnp.bfloat16),
            shaped((length, width), jnp.bfloat16),
            shaped((8, width), jnp.float32),
        ],
        [row_tiles(width), row_tiles(width), row_tiles(width), fixed(8, width)],
        length // TILE,
        "feed_in_back",
        2 * length * width * (inner + width),
    )


def project_qkv_back(grads, weight, first_grad, start, tiles, before=None):
    length, width = first_grad.shape
    part = width // len(grads)

    def kernel(w_ref, *refs):
        grad_refs, first_ref, out_ref = refs[: len(grads)], refs[len(grads)], refs[-1]
        total = first_ref[...]
        for n in range(3):
            for m, grad_ref in enumerate(grad_refs):
                at = n * width + m * part
                total = total + mxu(grad_ref[n], w_ref[:, at : at + part], NT)
        out_ref[...] = total

    tile = pl.BlockSpec((TILE, width), lambda i: (start + i, 0))
    more = () if before is None else (before,)
    return pl.pallas_call(
        kernel,
        grid=(tiles,),
        in_specs=[whole_once(weight.shape)]
        + [pl.BlockSpec((3, TILE, part), lambda i: (0, start + i, 0))] * len(grads)
        + [tile]
        + [pl.BlockSpec(memory_space=pl.ANY)] * len(more),
        out_specs=tile,
        out_shape=shaped((length, width), jnp.float32),
        input_output_aliases={} if before is None else {len(grads) + 2: 0},
        compiler_params=params(60),
        cost_estimate=cost(6 * tiles * TILE * width * width),
        name="qkv_back",
    )(weight, *grads, first_grad, *more)


ORDER = (1, 3, 0, 2)


def ordered_slot(j):
    return jnp.where(j < 2, 2 * j + 1, 2 * j - 4)


def weight_grad_kernel(where, left_ref, right_ref, own, sent, kept, *, rows, groups, split):
    core = where[0]
    chips = left_ref.shape[1] // (2 * rows)

    @pl.when(pl.program_id(1) == 0)
    def _():
        keep_rows(core, left_ref, rows, kept)

    if split:
        size = min(512, right_ref.shape[1])
        for ref, side in ((sent, 1), (own, 0)):
            for n in range(right_ref.shape[1] // size):
                at = slice(n * size, (n + 1) * size)
                part = mxu(kept[side], right_ref[:, at], NN).astype(jnp.bfloat16)
                ref[0, :, :, at] = part.reshape(chips, rows, size)
    else:
        cols = right_ref.shape[1] // groups
        for ref, side in ((sent, 1), (own, 0)):
            for pos, slot in enumerate(ORDER):
                start = pl.multiple_of((where[2] ^ turn(slot, core ^ side)) * cols, LANES)
                part = mxu(kept[side], right_ref[:, pl.ds(start, cols)], NN)
                ref[pos] = part.astype(jnp.bfloat16).reshape(chips, rows, cols)


def keep_rows(core, left_ref, rows, kept):
    chips = left_ref.shape[1] // (2 * rows)
    for side in range(2):
        chosen = []
        for k in range(chips):
            even = left_ref[:, 2 * k * rows : (2 * k + 1) * rows]
            odd = left_ref[:, (2 * k + 1) * rows : (2 * k + 2) * rows]
            chosen.append(jnp.where(core == side, even, odd))
        left = chosen[0] if chips == 1 else jnp.concatenate(chosen, 1)
        kept[side] = left.T


def turned_rows(place, left):
    tokens, height = left.shape

    def kernel(where, left_ref, out_ref):
        keep_rows(where[0], left_ref, height // place.shards, out_ref)

    in_vmem = pl.BlockSpec(memory_space=pltpu.VMEM)
    return pl.pallas_call(
        kernel,
        in_specs=[pl.BlockSpec(memory_space=pltpu.SMEM), in_vmem],
        out_specs=in_vmem,
        out_shape=shaped((2, height // 2, tokens), jnp.bfloat16),
        compiler_params=params(40),
        name="turned_rows",
    )(place.scalars, left)


def attention_grads_kernel(where, *refs, rows, groups, extra):
    turned, right_ref, *refs = refs
    *more, own, sent, kept = refs
    core, grp = where[0], where[2]
    chips = turned.shape[1] // rows
    step = pl.program_id(0)

    def scatter(lefts, right, at, cols):
        for ref, side in ((sent, 1), (own, 0)):
            part = mxu(lefts[side], right, NN).astype(jnp.bfloat16)
            for g in range(groups):
                pos = position(grp ^ g, core ^ side)
                block = part[:, g * cols : (g + 1) * cols].reshape(chips, rows, cols)
                ref[pos, :, 0:rows, pl.ds(at, cols)] = block

    skip = 0
    if not extra:
        other_left, other_right = more
        skip = other_right.shape[1] // groups

        @pl.when(step == 0)
        def _():
            keep_rows(core, other_left, rows, kept)
            scatter(kept, other_right[...], 0, skip)

    cols = right_ref.shape[2] // groups
    scatter(turned, right_ref[0], pl.multiple_of(skip + step * cols, LANES), cols)

    if extra:

        @pl.when(step == 2)
        def _():
            blank = jnp.zeros((extra, own.shape[3]), jnp.bfloat16)
            for ref, side in ((sent, 1), (own, 0)):
                for k in range(chips):
                    lines = vector_sums(2 * k + (core ^ side), *more)
                    for g in range(groups):
                        pos = position(grp ^ g, core ^ side)
                        ref[pos, k, rows : rows + extra, :] = blank
                        for n in range(3):
                            ref[pos, k, rows : rows + 1, n * LANES : (n + 1) * LANES] = lines[
                                3 * g + n
                            ].astype(jnp.bfloat16)


def vector_sums(shard, a_ref, b_ref, one_ref, two_ref, inner_ref):
    half = a_ref.shape[1]
    start = shard * LANES

    def part(ref, start):
        return ref[:, pl.ds(pl.multiple_of(start, LANES), LANES)]

    late = jnp.where(
        start < half,
        part(a_ref, jnp.minimum(start, half - LANES)),
        part(b_ref, jnp.maximum(start - half, 0)),
    )
    one, two = part(one_ref, start), part(two_ref, start)
    lines = [None] * 12
    lines[B_QUERY], lines[B_VALUE] = late[0:1], late[1:2]
    lines[GAIN_ONE], lines[SHIFT_ONE], lines[B_ATTN] = one[0:1], one[1:2], one[2:3]
    lines[GAIN_TWO], lines[SHIFT_TWO], lines[B_OUT] = two[0:1], two[1:2], two[2:3]
    for n in range(4):
        lines[B_IN + n] = part(inner_ref, (4 * shard + n) * LANES)
    return lines


def position(distance, core):
    slot = turn(distance, core)
    return jnp.where(slot == 0, 2, jnp.where(slot == 1, 0, jnp.where(slot == 3, 1, 3)))


def attention_grads(place, turned, right, more, name):
    height, tokens = 2 * turned.shape[1], turned.shape[2]
    groups, chips = place.groups, place.chips
    rows = height // place.shards
    extra = 16 if len(more) > 2 else 0
    size = right.shape[2]
    cols = 3 * size // groups + (0 if extra else more[1].shape[1] // groups)
    shape = (groups, chips, rows + extra, cols)
    once = [
        pl.BlockSpec(x.shape, lambda i, s: (0, 0), pipeline_mode=pl.Buffered(1)) for x in more
    ]
    return pl.pallas_call(
        functools.partial(attention_grads_kernel, rows=rows, groups=groups, extra=extra),
        grid_spec=pltpu.PrefetchScalarGridSpec(
            num_scalar_prefetch=1,
            grid=(3,),
            in_specs=[
                pl.BlockSpec(turned.shape, lambda i, s: (0, 0, 0), pipeline_mode=pl.Buffered(1)),
                pl.BlockSpec((1, tokens, size), lambda i, s: (i, 0, 0)),
            ]
            + once,
            out_specs=[pl.BlockSpec(shape, lambda i, s: (0, 0, 0, 0))] * 2,
            scratch_shapes=[pltpu.VMEM((8, LANES) if extra else turned.shape, jnp.bfloat16)],
        ),
        out_shape=[shaped(shape, jnp.bfloat16)] * 2,
        compiler_params=params(60),
        cost_estimate=cost(2 * tokens * height * cols * groups),
        name="wgrad_" + name,
    )(place.scalars, turned, right, *more)


def weight_grad(place, left, right, split, name):
    tokens, height = left.shape
    groups, chips = place.groups, place.chips
    rows = height // place.shards
    step_chips = chips if split else max(1, 1024 // (2 * rows))
    cols = right.shape[1] // groups
    if split:
        grid = (1, groups)
        block = lambda i, j, s: (0, s[2] ^ turn(ordered_slot(j), s[0]))
        right_spec = pl.BlockSpec((tokens, cols), block)
        one = (1, chips, rows, cols)
        other = lambda j: jnp.where(j == 0, 3, jnp.where(j == 3, 0, j))
        out_specs = [
            pl.BlockSpec(one, lambda i, j, s: (j, 0, 0, 0)),
            pl.BlockSpec(one, lambda i, j, s: (other(j), 0, 0, 0)),
        ]
    else:
        grid = (chips // step_chips, 1)
        right_spec = pl.BlockSpec(right.shape, lambda i, j, s: (0, 0))
        out_specs = [
            pl.BlockSpec((groups, step_chips, rows, cols), lambda i, j, s: (0, i, 0, 0))
        ] * 2
    return pl.pallas_call(
        functools.partial(weight_grad_kernel, rows=rows, groups=groups, split=split),
        grid_spec=pltpu.PrefetchScalarGridSpec(
            num_scalar_prefetch=1,
            grid=grid,
            in_specs=[
                pl.BlockSpec((tokens, step_chips * 2 * rows), lambda i, j, s: (0, i)),
                right_spec,
            ],
            out_specs=out_specs,
            scratch_shapes=[pltpu.VMEM((2, step_chips * rows, tokens), jnp.bfloat16)],
        ),
        out_shape=[shaped((groups, chips, rows, cols), jnp.bfloat16)] * 2,
        compiler_params=params(60),
        cost_estimate=cost(2 * tokens * height * cols * groups),
        name="wgrad_" + name,
    )(place.scalars, left, right)


def add(*terms):
    total = terms[0].astype(jnp.float32)
    for term in terms[1:]:
        total = total + term.astype(jnp.float32)
    return total.astype(jnp.bfloat16)


def add_leading(left, right):
    _, chips, rows, cols = left.shape

    def kernel(left_ref, right_ref, out_ref):
        total = left_ref[...].astype(jnp.float32) + right_ref[...].astype(jnp.float32)
        out_ref[...] = total.astype(jnp.bfloat16)

    block = pl.BlockSpec((1, chips, rows, cols), lambda i: (i, 0, 0, 0))
    return pl.pallas_call(
        kernel,
        grid=(2,),
        in_specs=[block, block],
        out_specs=block,
        out_shape=shaped((2, chips, rows, cols), jnp.bfloat16),
        compiler_params=params(60),
        cost_estimate=cost(512 * chips * rows * cols),
        name="add_leading",
    )(left, right)


class Reduction:
    def __init__(self, place, made):
        self.place = place
        self.made, sent = made
        self.flying = place.swap_core(sent)

    def near(self):
        self.core = self.flying
        leave = add_leading(self.made, self.core)
        self.flying = self.place.swap_grp(leave, 0)
        return leave

    def middle(self):
        self.first = self.flying
        second = add(self.made[3], self.core[3], self.first[1])
        self.flying = self.place.swap_grp(second, 1)
        return second

    def column(self):
        mine = add(self.made[2], self.core[2], self.first[0], self.flying)
        return mine, lambda chip: lax.dynamic_index_in_dim(mine, chip, 0, False)

    def along(self):
        place = self.place
        mine, at = self.column()
        self.mine = [at(place.slot_chip(slot)) for slot in range(4)]
        both = jnp.stack([self.mine[1], self.mine[3]])
        self.flying = place.swap_chip(both, 0)
        return both

    def along_far(self):
        self.first = self.flying
        second = add(self.mine[2], self.first[1])
        self.flying = self.place.swap_chip(second, 1)
        return second

    def share(self):
        return add(self.mine[0], self.first[0], self.flying)

    def along_direct(self):
        place = self.place
        mine, at = self.column()
        self.mine = at(place.chip)
        self.flying = tuple(
            place.permute(at(place.chip ^ k), (2 * k, 2 * k)) for k in range(place.chips - 1, 0, -1)
        )
        return mine

    def share_direct(self):
        return add(self.mine, *self.flying)


class Replication:
    def __init__(self, place, share, direct=False):
        self.place = place
        self.blocks = [share] + [None] * 3
        if direct:
            size = place.shards
            for mask in (3, 1, 2):
                self.blocks[mask] = place.permute(share, (mask * size, mask * size))
        else:
            self.flying = place.swap_grp(share, 0)

    def far(self):
        pair = jnp.stack([self.blocks[0], self.flying])
        self.blocks[1] = self.flying
        self.flying = self.place.swap_grp(pair, 1)
        return pair

    def landed(self):
        if self.blocks[2] is None:
            self.blocks[2:] = [self.flying[0], self.flying[1]]
        return self.blocks


def order_feed_forward(place, blocks, rows_in):
    groups = place.groups
    height, cols = blocks[0].shape
    rows_out = height - groups * rows_in

    def kernel(where, *refs):
        *blocks, out_ref, in_ref = refs
        for slot, ref in enumerate(blocks):
            g = where[2] ^ turn(slot, where[0])
            at = pl.multiple_of(g * cols, LANES)
            out_ref[:, pl.ds(at, cols)] = ref[0:rows_out, :].astype(jnp.float32)
            for n in range(groups):
                at = pl.multiple_of((g * groups + n) * cols, LANES)
                part = ref[rows_out + n * rows_in : rows_out + (n + 1) * rows_in, :]
                in_ref[:, pl.ds(at, cols)] = part.astype(jnp.float32)

    in_vmem = pl.BlockSpec(memory_space=pltpu.VMEM)
    return pl.pallas_call(
        kernel,
        in_specs=[pl.BlockSpec(memory_space=pltpu.SMEM)] + [in_vmem] * groups,
        out_specs=[in_vmem] * 2,
        out_shape=[
            shaped((rows_out, groups * cols), jnp.float32),
            shaped((rows_in, groups * groups * cols), jnp.float32),
        ],
        compiler_params=params(40),
        cost_estimate=cost(height * cols * 1024),
        name="order_feed_forward",
    )(place.scalars, *blocks)


def order_attention(place, blocks_a, blocks_b, rows):
    groups = place.groups
    size = blocks_b[0].shape[1] // 3
    skip = blocks_a[0].shape[1] - 3 * size
    width = groups * skip

    def kernel(where, *refs):
        *blocks, attn_ref, qkv_ref, small_ref = refs
        for n in range(groups):
            ref = blocks[n]
            g = where[2] ^ turn(n, where[0])
            attn_ref[:, pl.ds(pl.multiple_of(g * skip, LANES), skip)] = ref[:, 0:skip].astype(
                jnp.float32
            )
            for part in range(3):
                at = pl.multiple_of(part * width + g * size, LANES)
                block = ref[:, skip + part * size : skip + (part + 1) * size]
                qkv_ref[:, pl.ds(at, size)] = block.astype(jnp.float32)
        for n in range(groups):
            ref = blocks[groups + n]
            g = where[2] ^ n
            lines = []
            for part in range(3):
                at = pl.multiple_of(part * width + width // 2 + g * size, LANES)
                here = slice(part * size, (part + 1) * size)
                qkv_ref[:, pl.ds(at, size)] = ref[0:rows, here].astype(jnp.float32)
                lines.append(ref[rows : rows + 16, here].astype(jnp.float32)[0:1])
            lines.append(jnp.zeros((5, size), jnp.float32))
            small_ref[pl.ds(pl.multiple_of(g * 8, 8), 8), :] = jnp.concatenate(lines)

    in_vmem = pl.BlockSpec(memory_space=pltpu.VMEM)
    return pl.pallas_call(
        kernel,
        in_specs=[pl.BlockSpec(memory_space=pltpu.SMEM)] + [in_vmem] * (2 * groups),
        out_specs=[in_vmem] * 3,
        out_shape=[
            shaped((rows, width), jnp.float32),
            shaped((rows, 3 * width), jnp.float32),
            shaped((8 * groups, size), jnp.float32),
        ],
        compiler_params=params(40),
        name="order_attention",
    )(place.scalars, *blocks_a, *blocks_b)


def on_device_permutes(
    tokens,
    segment_ids,
    keep_flag,
    cotangent,
    w_qkv,
    b_query,
    b_value,
    w_attn_out,
    b_attn_out,
    norm1_gain,
    norm1_bias,
    w_in,
    b_in,
    w_out,
    b_out,
    norm2_gain,
    norm2_bias,
    *,
    groups,
    shards,
):
    place = Place(groups, shards)
    _, length, width = tokens.shape
    rows = tokens[0]
    seg_row = segment_ids.reshape(1, length)
    pairs = width // LANES

    c1 = Gather(place, w_qkv)
    c2 = Gather(place, jnp.concatenate([w_in, w_attn_out], 1))
    c3 = Gather(place, w_out)
    c1.chips_near()
    small = Vectors(
        place,
        (b_query, b_value, b_attn_out, norm1_gain, norm1_bias, b_out, norm2_gain, norm2_bias, b_in),
    )
    meet(rows, c1, small)
    pair = c1.chips_far()
    small.chips_near()
    meet(pair, c1, small)
    joined = c1.join()
    c1.near()
    small.chips_far()
    c2.chips_near(joined)
    meet(joined, c2, small)
    small.landed()
    pair = c2.chips_far()
    vectors, bias_in, qkv_bias, seg_col, keep = small.unpack(
        seg_row, keep_flag.reshape(1, length)
    )
    c1.flying = lax.optimization_barrier(c1.flying)
    turned = turned_rows(place, after(rows, vectors))
    c1.far(pair, vectors)
    c1.cross(0, 1, 2)
    joined = c2.join()
    meet((joined, turned), c1)
    c1.landed()
    c2.near(c1.held[3])
    c1.cross(3)
    c3.chips_near(c1.held[3])
    blank = jnp.ones((1, width), jnp.float32)
    qkv_scale = jnp.concatenate([blank / math.sqrt(HD), blank, blank], 1)

    mixed, full_qkv = project_qkv(place, rows, Window(c1, 0, w_qkv.shape[1]), qkv_bias, qkv_scale)
    meet(mixed, c3)
    pair = c3.chips_far()
    c2.cross(0, wait=(mixed,))
    first, second = pairs * 3 // 8, pairs * 3 // 4
    forward = attention_forward(after(mixed, pair), seg_col, seg_row, 0, first)
    meet(forward[0], c2, c3)
    c2.far()
    joined = c3.join()
    c3.near()
    c2.cross(1, 2)
    forward = attention_forward(
        after(mixed, joined), seg_col, seg_row, first, second - first, forward
    )
    meet(forward[0], c2)
    c2.landed()
    c2.cross(3)
    contexts, probs, probs_scale = attention_forward(
        after(mixed, c2.held[3]), seg_col, seg_row, second, pairs - second, forward
    )
    normed, scale_one, normed_low, full_attn = project_out(
        place, contexts, Window(c2, w_in.shape[1], w_attn_out.shape[1]), rows, vectors
    )
    meet(normed_low, c3)
    c3.far()
    c3.cross(0, 1, 2)
    hidden, slope, full_in = feed_in(
        place, after(normed_low, c3.held[1]), Window(c2, 0, w_in.shape[1]), bias_in
    )
    meet(hidden, c3)
    c3.landed()
    c3.cross(3)
    layer_out, second_grad, out_low, second_sums, pre_low, bias_in_grad = feed_out(
        place, hidden, Window(c3, 0, w_out.shape[1]), normed, cotangent[0], keep, vectors, slope
    )

    r_out = Reduction(place, weight_grad(place, hidden, out_low, False, "out"))
    r_in = Reduction(place, weight_grad(place, after(normed_low, r_out.made), pre_low, True, "in"))
    meet(r_in.made, r_out)
    step = r_out.near()
    first_grad, attn_low, context_grad, first_sums = feed_in_back(
        after(pre_low, r_in.made, step), full_in, second_grad, normed, scale_one, vectors, full_attn
    )
    meet(attn_low, r_in)
    step = r_in.near()
    half, quarter = pairs // 2, pairs // 4

    def back(wait, start, count, at, before=None):
        return attention_backward(
            mixed,
            contexts,
            after(context_grad, *wait),
            probs,
            probs_scale,
            start,
            count,
            at,
            half,
            before,
        )

    low_a, late_a = back((step,), 0, half, 0)
    meet(late_a, r_out, r_in)
    steps = (r_out.middle(), r_in.middle())
    r_a = Reduction(
        place, attention_grads(place, after(turned, *steps), low_a, (contexts, attn_low), "a")
    )
    meet(r_a.made, r_out)
    step = r_out.along()
    part = back((r_a.made, step), half, quarter, 0)
    meet(part[1], r_out, r_in, r_a)
    steps = (r_out.along_far(), r_in.along(), r_a.near())
    low_b, late_b = back(steps, half + quarter, quarter, quarter, part)
    meet(late_b, r_out, r_in, r_a)
    sums = (late_a, late_b, first_sums, second_sums, bias_in_grad)
    share_out = r_out.share()
    steps = (r_in.along_far(), r_a.middle(), share_out)
    r_b = Reduction(place, attention_grads(place, after(turned, *steps), low_b, sums, "b"))
    meet(r_b.made, r_in, r_a)
    share_in = r_in.share()
    inner = share_in.shape[1] // groups
    joined = jnp.concatenate(
        [share_out] + [share_in[:, n * inner : (n + 1) * inner] for n in range(groups)]
    )
    all_ffn = Replication(place, joined)
    grads = (low_a, after(low_b, r_b.made, joined, r_a.along()))
    tiles = length // TILE // 2
    input_grad = project_qkv_back(grads, full_qkv, first_grad, 0, tiles)
    meet(input_grad, r_b, r_a, all_ffn)
    steps = (r_b.near(), r_a.along_far())
    input_grad = project_qkv_back(
        grads, full_qkv, after(first_grad, *steps), tiles, tiles, input_grad
    )
    meet(input_grad, r_b, r_a)
    middle = r_b.middle()
    r_a.flying = after(r_a.flying, middle)
    all_a = Replication(place, r_a.share())
    meet(all_a.blocks[0], r_b, all_a)
    along = r_b.along_direct()
    all_a.flying = after(all_a.flying, along)
    all_ffn.flying = after(all_ffn.flying, along)
    pairs_made = (all_a.far(), all_ffn.far())
    meet(pairs_made, r_b)
    share_b = r_b.share_direct()
    all_b = Replication(place, share_b, direct=True)
    meet(share_b, all_ffn)
    w_out_grad, w_in_grad = order_feed_forward(place, all_ffn.landed(), share_in.shape[0])
    all_a.flying = after(all_a.flying, w_out_grad)
    w_attn_grad, w_qkv_grad, small = order_attention(
        place, all_a.landed(), all_b.landed(), w_attn_out.shape[0]
    )
    small = [small[8 * (n // 3) + n % 3] for n in range(12)]
    return (
        layer_out[None],
        input_grad[None],
        w_qkv_grad,
        small[B_QUERY],
        small[B_VALUE],
        w_attn_grad,
        small[B_ATTN],
        small[GAIN_ONE],
        small[SHIFT_ONE],
        w_in_grad,
        jnp.concatenate(small[B_IN:]),
        w_out_grad,
        small[B_OUT],
        small[GAIN_TWO],
        small[SHIFT_TWO],
    )


def solution(mesh):
    groups, shards = mesh.shape["grp"], mesh.shape["shard"]
    if groups == 4 and shards == 8:
        body = functools.partial(on_device_permutes, groups=groups, shards=shards)
    else:
        body = on_device
    return jax.shard_map(
        body,
        mesh=mesh,
        in_specs=(
            P(("grp", "shard"), None, None),
            P(("grp", "shard"), None),
            P(("grp", "shard"), None),
            P(("grp", "shard"), None, None),
            P("shard", "grp"),
            P("shard"),
            P("shard"),
            P("shard", "grp"),
            P("shard"),
            P("shard"),
            P("shard"),
            P("shard", "grp"),
            P("shard"),
            P("shard", "grp"),
            P("shard"),
            P("shard"),
            P("shard"),
        ),
        out_specs=(
            P(("grp", "shard"), None, None),
            P(("grp", "shard"), None, None),
            P("shard", None),
            P("shard"),
            P("shard"),
            P("shard", None),
            P("shard"),
            P("shard"),
            P("shard"),
            P("shard", None),
            P("shard"),
            P("shard", None),
            P("shard"),
            P("shard"),
            P("shard"),
        ),
        check_vma=False,
    )
```

```python
import functools
import math

import jax
import jax.numpy as jnp
from jax import lax
from jax.experimental import pallas as pl
from jax.experimental.pallas import tpu as pltpu
from jax.sharding import PartitionSpec as P

H = 16
HD = 64


masked_score = -1e30
epsilon = 1e-05


def norm_layer(rows, gain_row, shift_row):
    row_mean = jnp.mean(rows, -1, keepdims=True)
    centered = rows - row_mean
    row_var = jnp.mean(centered * centered, -1, keepdims=True)
    return centered * lax.rsqrt(row_var + epsilon) * gain_row + shift_row


def gelu_exact(values):
    return 0.5 * values * (1.0 + lax.erf(values * (1.0 / math.sqrt(2.0))))


def contract_rows(left, right):
    return lax.dot_general(
        left, right, (((0,), (0,)), ((), ())), preferred_element_type=jnp.float32
    )


def contract_cols(left, right):
    return lax.dot_general(
        left, right, (((1,), (1,)), ((), ())), preferred_element_type=jnp.float32
    )


def attend_forward(queries, key_rows, value_rows, segment_row, block_rows):
    length, model_width = queries.shape
    scaling = 1.0 / math.sqrt(HD)
    key_heads = key_rows.reshape(length, H, HD)
    value_heads = value_rows.reshape(length, H, HD)
    query_blocks = queries.reshape(length // block_rows, block_rows, H, HD)
    segment_blocks = segment_row.reshape(length // block_rows, block_rows)

    def one_block(pieces):
        query_part, segment_part = pieces
        scores = (
            jnp.einsum("qhd,khd->hqk", query_part, key_heads, preferred_element_type=jnp.float32)
            * scaling
        )
        allowed = segment_part[:, None] == segment_row[None, :]
        scores = jnp.where(allowed[None], scores, masked_score)
        row_max = jnp.max(scores, -1, keepdims=True)
        powers = jnp.exp(scores - row_max)
        totals = jnp.sum(powers, -1, keepdims=True)
        attn_probs = (powers / totals).astype(jnp.bfloat16)
        context = jnp.einsum(
            "hqk,khd->qhd", attn_probs, value_heads, preferred_element_type=jnp.float32
        )
        return (
            context.reshape(block_rows, model_width).astype(jnp.bfloat16),
            (row_max + jnp.log(totals))[:, :, 0],
        )

    contexts, log_sums = lax.map(one_block, (query_blocks, segment_blocks))
    return (contexts.reshape(length, model_width), log_sums)


def attend_backward(queries, key_rows, value_rows, segment_row, log_sums, context_grad, block_rows):
    length, model_width = queries.shape
    scaling = 1.0 / math.sqrt(HD)
    key_heads = key_rows.reshape(length, H, HD)
    value_heads = value_rows.reshape(length, H, HD)
    query_blocks = queries.reshape(length // block_rows, block_rows, H, HD)
    segment_blocks = segment_row.reshape(length // block_rows, block_rows)
    grad_blocks = context_grad.reshape(length // block_rows, block_rows, H, HD)

    def one_block(running, pieces):
        key_acc, value_acc = running
        query_part, segment_part, lse_part, grad_part = pieces
        scores = (
            jnp.einsum("qhd,khd->hqk", query_part, key_heads, preferred_element_type=jnp.float32)
            * scaling
        )
        allowed = segment_part[:, None] == segment_row[None, :]
        scores = jnp.where(allowed[None], scores, masked_score)
        probs = jnp.exp(scores - lse_part[:, :, None])
        prob_low = probs.astype(jnp.bfloat16)
        prob_grad = jnp.einsum(
            "qhd,khd->hqk", grad_part, value_heads, preferred_element_type=jnp.float32
        )
        row_dot = jnp.sum(prob_grad * probs, -1, keepdims=True)
        score_grad = (probs * (prob_grad - row_dot)).astype(jnp.bfloat16)
        query_grad = (
            jnp.einsum("hqk,khd->qhd", score_grad, key_heads, preferred_element_type=jnp.float32)
            * scaling
        )
        key_acc = (
            key_acc
            + jnp.einsum("hqk,qhd->khd", score_grad, query_part, preferred_element_type=jnp.float32)
            * scaling
        )
        value_acc = value_acc + jnp.einsum(
            "hqk,qhd->khd", prob_low, grad_part, preferred_element_type=jnp.float32
        )
        return ((key_acc, value_acc), query_grad.reshape(block_rows, model_width))

    empty_acc = jnp.zeros((length, H, HD), jnp.float32)
    (key_grad, value_grad), query_grads = lax.scan(
        one_block, (empty_acc, empty_acc), (query_blocks, segment_blocks, log_sums, grad_blocks)
    )
    return (
        query_grads.reshape(length, model_width),
        key_grad.reshape(length, model_width),
        value_grad.reshape(length, model_width),
    )


def on_device(
    tokens,
    segment_ids,
    keep_flag,
    cotangent,
    w_qkv,
    b_query,
    b_value,
    w_attn_out,
    b_attn_out,
    norm1_gain,
    norm1_bias,
    w_in,
    b_in,
    w_out,
    b_out,
    norm2_gain,
    norm2_bias,
):
    seq_count, length, model_width = tokens.shape
    block_rows = min(512, length)
    within = (
        lax.all_gather(w_qkv, "shard", axis=0, tiled=True),
        lax.all_gather(w_attn_out, "shard", axis=0, tiled=True),
        lax.all_gather(w_in, "shard", axis=0, tiled=True),
        lax.all_gather(w_out, "shard", axis=0, tiled=True),
        lax.all_gather(b_query, "shard", axis=0, tiled=True),
        lax.all_gather(b_value, "shard", axis=0, tiled=True),
        lax.all_gather(b_attn_out, "shard", axis=0, tiled=True),
        lax.all_gather(norm1_gain, "shard", axis=0, tiled=True),
        lax.all_gather(norm1_bias, "shard", axis=0, tiled=True),
        lax.all_gather(b_in, "shard", axis=0, tiled=True),
        lax.all_gather(b_out, "shard", axis=0, tiled=True),
        lax.all_gather(norm2_gain, "shard", axis=0, tiled=True),
        lax.all_gather(norm2_bias, "shard", axis=0, tiled=True),
    )
    full_qkv, full_attn, full_in, full_out = (
        lax.all_gather(within[0], "grp", axis=1, tiled=True),
        lax.all_gather(within[1], "grp", axis=1, tiled=True),
        lax.all_gather(within[2], "grp", axis=1, tiled=True),
        lax.all_gather(within[3], "grp", axis=1, tiled=True),
    )
    (
        bias_query,
        bias_value,
        bias_attn,
        gain_one,
        shift_one,
        bias_in,
        bias_out,
        gain_two,
        shift_two,
    ) = [piece.astype(jnp.float32) for piece in within[4:]]
    flat_rows = tokens.reshape(seq_count * length, model_width)
    mixed_qkv = jnp.dot(flat_rows, full_qkv, preferred_element_type=jnp.float32)
    queries = (mixed_qkv[:, :model_width] + bias_query).astype(jnp.bfloat16)
    key_rows = mixed_qkv[:, model_width : 2 * model_width].astype(jnp.bfloat16)
    value_rows = (mixed_qkv[:, 2 * model_width :] + bias_value).astype(jnp.bfloat16)
    query_seqs = queries.reshape(seq_count, length, model_width)
    key_seqs = key_rows.reshape(seq_count, length, model_width)
    value_seqs = value_rows.reshape(seq_count, length, model_width)

    def forward_sequence(pieces):
        return attend_forward(pieces[0], pieces[1], pieces[2], pieces[3], block_rows)

    contexts, log_sums = lax.map(forward_sequence, (query_seqs, key_seqs, value_seqs, segment_ids))
    contexts = contexts.reshape(seq_count * length, model_width)
    attended = jnp.dot(contexts, full_attn, preferred_element_type=jnp.float32) + bias_attn
    first_sum = flat_rows.astype(jnp.float32) + attended
    normed_one, norm_one_back = jax.vjp(norm_layer, first_sum, gain_one, shift_one)
    normed_low = normed_one.astype(jnp.bfloat16)
    hidden_pre = jnp.dot(normed_low, full_in, preferred_element_type=jnp.float32) + bias_in
    hidden, gelu_back = jax.vjp(gelu_exact, hidden_pre)
    hidden_low = hidden.astype(jnp.bfloat16)
    second_sum = normed_one + (
        jnp.dot(hidden_low, full_out, preferred_element_type=jnp.float32) + bias_out
    )
    result, norm_two_back = jax.vjp(norm_layer, second_sum, gain_two, shift_two)
    layer_out = result.astype(jnp.bfloat16).reshape(seq_count, length, model_width)
    again = (
        lax.all_gather(w_qkv, "shard", axis=0, tiled=True),
        lax.all_gather(w_attn_out, "shard", axis=0, tiled=True),
        lax.all_gather(w_in, "shard", axis=0, tiled=True),
        lax.all_gather(w_out, "shard", axis=0, tiled=True),
    )
    back_qkv, back_attn, back_in, back_out = (
        lax.all_gather(again[0], "grp", axis=1, tiled=True),
        lax.all_gather(again[1], "grp", axis=1, tiled=True),
        lax.all_gather(again[2], "grp", axis=1, tiled=True),
        lax.all_gather(again[3], "grp", axis=1, tiled=True),
    )
    masked_cot = cotangent.astype(jnp.float32).reshape(
        seq_count * length, model_width
    ) * keep_flag.reshape(seq_count * length, 1).astype(jnp.float32)
    second_grad, gain_two_grad, shift_two_grad = norm_two_back(masked_cot)
    bias_out_grad = jnp.sum(second_grad, 0)
    out_low = second_grad.astype(jnp.bfloat16)
    w_out_grad = contract_rows(hidden_low, out_low)
    hidden_grad = contract_cols(out_low, back_out)
    (pre_grad,) = gelu_back(hidden_grad)
    bias_in_grad = jnp.sum(pre_grad, 0)
    pre_low = pre_grad.astype(jnp.bfloat16)
    w_in_grad = contract_rows(normed_low, pre_low)
    normed_grad = second_grad + contract_cols(pre_low, back_in)
    first_grad, gain_one_grad, shift_one_grad = norm_one_back(normed_grad)
    bias_attn_grad = jnp.sum(first_grad, 0)
    attn_low = first_grad.astype(jnp.bfloat16)
    w_attn_grad = contract_rows(contexts, attn_low)
    context_grad = contract_cols(attn_low, back_attn).astype(jnp.bfloat16)

    def backward_sequence(pieces):
        return attend_backward(
            pieces[0], pieces[1], pieces[2], pieces[3], pieces[4], pieces[5], block_rows
        )

    query_grad, key_grad, value_grad = lax.map(
        backward_sequence,
        (
            query_seqs,
            key_seqs,
            value_seqs,
            segment_ids,
            log_sums,
            context_grad.reshape(seq_count, length, model_width),
        ),
    )
    query_grad = query_grad.reshape(seq_count * length, model_width)
    key_grad = key_grad.reshape(seq_count * length, model_width)
    value_grad = value_grad.reshape(seq_count * length, model_width)
    bias_query_grad = jnp.sum(query_grad, 0)
    bias_value_grad = jnp.sum(value_grad, 0)
    qkv_low = jnp.concatenate([query_grad, key_grad, value_grad], 1).astype(jnp.bfloat16)
    w_qkv_grad = contract_rows(flat_rows, qkv_low)
    input_grad = first_grad + contract_cols(qkv_low, back_qkv)
    reduced = (
        lax.psum_scatter(
            w_qkv_grad.astype(jnp.bfloat16), "shard", scatter_dimension=0, tiled=True
        ).astype(jnp.float32),
        lax.psum_scatter(
            bias_query_grad.astype(jnp.bfloat16), "shard", scatter_dimension=0, tiled=True
        ).astype(jnp.float32),
        lax.psum_scatter(
            bias_value_grad.astype(jnp.bfloat16), "shard", scatter_dimension=0, tiled=True
        ).astype(jnp.float32),
        lax.psum_scatter(
            w_attn_grad.astype(jnp.bfloat16), "shard", scatter_dimension=0, tiled=True
        ).astype(jnp.float32),
        lax.psum_scatter(
            bias_attn_grad.astype(jnp.bfloat16), "shard", scatter_dimension=0, tiled=True
        ).astype(jnp.float32),
        lax.psum_scatter(
            gain_one_grad.astype(jnp.bfloat16), "shard", scatter_dimension=0, tiled=True
        ).astype(jnp.float32),
        lax.psum_scatter(
            shift_one_grad.astype(jnp.bfloat16), "shard", scatter_dimension=0, tiled=True
        ).astype(jnp.float32),
        lax.psum_scatter(
            w_in_grad.astype(jnp.bfloat16), "shard", scatter_dimension=0, tiled=True
        ).astype(jnp.float32),
        lax.psum_scatter(
            bias_in_grad.astype(jnp.bfloat16), "shard", scatter_dimension=0, tiled=True
        ).astype(jnp.float32),
        lax.psum_scatter(
            w_out_grad.astype(jnp.bfloat16), "shard", scatter_dimension=0, tiled=True
        ).astype(jnp.float32),
        lax.psum_scatter(
            bias_out_grad.astype(jnp.bfloat16), "shard", scatter_dimension=0, tiled=True
        ).astype(jnp.float32),
        lax.psum_scatter(
            gain_two_grad.astype(jnp.bfloat16), "shard", scatter_dimension=0, tiled=True
        ).astype(jnp.float32),
        lax.psum_scatter(
            shift_two_grad.astype(jnp.bfloat16), "shard", scatter_dimension=0, tiled=True
        ).astype(jnp.float32),
    )
    summed = (
        lax.psum(reduced[0].astype(jnp.bfloat16), "grp").astype(jnp.float32),
        lax.psum(reduced[1].astype(jnp.bfloat16), "grp").astype(jnp.float32),
        lax.psum(reduced[2].astype(jnp.bfloat16), "grp").astype(jnp.float32),
        lax.psum(reduced[3].astype(jnp.bfloat16), "grp").astype(jnp.float32),
        lax.psum(reduced[4].astype(jnp.bfloat16), "grp").astype(jnp.float32),
        lax.psum(reduced[5].astype(jnp.bfloat16), "grp").astype(jnp.float32),
        lax.psum(reduced[6].astype(jnp.bfloat16), "grp").astype(jnp.float32),
        lax.psum(reduced[7].astype(jnp.bfloat16), "grp").astype(jnp.float32),
        lax.psum(reduced[8].astype(jnp.bfloat16), "grp").astype(jnp.float32),
        lax.psum(reduced[9].astype(jnp.bfloat16), "grp").astype(jnp.float32),
        lax.psum(reduced[10].astype(jnp.bfloat16), "grp").astype(jnp.float32),
        lax.psum(reduced[11].astype(jnp.bfloat16), "grp").astype(jnp.float32),
        lax.psum(reduced[12].astype(jnp.bfloat16), "grp").astype(jnp.float32),
    )
    return (
        layer_out,
        input_grad.reshape(seq_count, length, model_width),
        summed[0],
        summed[1],
        summed[2],
        summed[3],
        summed[4],
        summed[5],
        summed[6],
        summed[7],
        summed[8],
        summed[9],
        summed[10],
        summed[11],
        summed[12],
    )


NT = (((1,), (1,)), ((), ()))
NN = (((1,), (0,)), ((), ()))
TN = (((0,), (0,)), ((), ()))
LANES = 128
AXES = ("grp", "shard")


def mxu(left, right, dims):
    return lax.dot_general(left, right, dims, preferred_element_type=jnp.float32)


def cost(flops):
    return pl.CostEstimate(flops=2 * flops, bytes_accessed=0, transcendentals=0)


def params(megabytes=60):
    return pltpu.CompilerParams(vmem_limit_bytes=megabytes << 20)


def attention_forward_kernel(q_ref, k_ref, v_ref, seg_col, seg_row, out_ref, probs_ref, scale_ref, *, rows):
    length = q_ref.shape[0]
    first = lax.broadcasted_iota(jnp.int32, (1, LANES), 1) < HD
    keys = k_ref[...]
    values = v_ref[...]
    zero = jnp.zeros_like(keys)
    head_keys = (jnp.where(first, keys, zero), jnp.where(first, zero, keys))
    key_segments = seg_col[...]
    for block in range(length // rows):
        here = pl.ds(block * rows, rows)
        q = q_ref[here, :]
        allowed = key_segments == seg_row[:, here]
        outs, scales = [], []
        for head in range(2):
            scores = mxu(head_keys[head], q, NT)
            scores = jnp.where(allowed, scores, masked_score)
            powers = jnp.exp(scores - jnp.max(scores, 0, keepdims=True))
            scale = 1.0 / jnp.sum(powers, 0, keepdims=True)
            scales.append(jnp.transpose(jnp.broadcast_to(scale, (LANES, rows))))
            powers = powers.astype(jnp.bfloat16)
            probs_ref[head, :, here] = powers
            outs.append(mxu(powers, values, TN))
        scale = jnp.where(first, scales[0], scales[1])
        scale_ref[here, :] = scale
        out_ref[here, :] = (jnp.where(first, outs[0], outs[1]) * scale).astype(jnp.bfloat16)


def attention_forward(qkv, seg_col, seg_row, start, pairs, before=None):
    length, width = qkv.shape[0], qkv.shape[1] // 3
    total = width // LANES
    rows = min(512, length)
    more = () if before is None else before

    def pair(part):
        return pl.BlockSpec((length, LANES), lambda j: (0, part * total + start + j))

    def body(q_ref, k_ref, v_ref, seg_c, seg_r, *refs):
        attention_forward_kernel(q_ref, k_ref, v_ref, seg_c, seg_r, *refs[-3:], rows=rows)

    return pl.pallas_call(
        body,
        grid=(pairs,),
        in_specs=[
            pair(0),
            pair(1),
            pair(2),
            pl.BlockSpec((length, 1), lambda j: (0, 0)),
            pl.BlockSpec((1, length), lambda j: (0, 0)),
        ]
        + [pl.BlockSpec(memory_space=pl.ANY)] * len(more),
        out_specs=[
            pl.BlockSpec((length, LANES), lambda j: (0, start + j)),
            pl.BlockSpec((2, length, length), lambda j: (start + j, 0, 0)),
            pl.BlockSpec((length, LANES), lambda j: (0, start + j)),
        ],
        out_shape=[
            jax.ShapeDtypeStruct((length, width), jnp.bfloat16),
            jax.ShapeDtypeStruct((2 * total, length, length), jnp.bfloat16),
            jax.ShapeDtypeStruct((length, width), jnp.float32),
        ],
        input_output_aliases={} if before is None else {5: 0, 6: 1, 7: 2},
        compiler_params=params(60),
        cost_estimate=cost(16 * length * length * pairs * LANES),
        name="attn_fwd",
    )(qkv, qkv, qkv, seg_col, seg_row, *more)


def attention_backward_kernel(
    q_ref, k_ref, v_ref, o_ref, do_ref, probs_ref, scale_ref, grad_ref, sum_ref
):
    first = lax.broadcasted_iota(jnp.int32, (1, LANES), 1) < HD
    pick = (
        lax.broadcasted_iota(jnp.int32, (8, LANES), 0)
        == lax.broadcasted_iota(jnp.int32, (8, LANES), 1) // HD
    ).astype(jnp.float32)
    q = q_ref[...]
    scaled = do_ref[...].astype(jnp.float32) * scale_ref[...]
    do = scaled.astype(jnp.bfloat16)
    keys = k_ref[...]
    values = v_ref[...]
    zero = jnp.zeros_like(values)
    head_values = (jnp.where(first, values, zero), jnp.where(first, zero, values))
    dots = lax.dot_general(
        pick,
        scaled * o_ref[...].astype(jnp.float32),
        NT,
        precision=lax.Precision.HIGHEST,
        preferred_element_type=jnp.float32,
    )
    query_parts, key_parts, value_parts = [], [], []
    for head in range(2):
        probs = probs_ref[head]
        prob_grad = mxu(head_values[head], do, NT)
        score_grad = probs.astype(jnp.float32) * (prob_grad - dots[head : head + 1, :])
        score_grad = score_grad.astype(jnp.bfloat16)
        value_parts.append(mxu(probs, do, NN))
        key_parts.append(mxu(score_grad, q, NN))
        query_parts.append(mxu(score_grad, keys, TN))
    query_grad = jnp.where(first, *query_parts) * (1.0 / math.sqrt(HD))
    value_grad = jnp.where(first, *value_parts)
    grad_ref[0] = query_grad.astype(jnp.bfloat16)
    grad_ref[1] = jnp.where(first, *key_parts).astype(jnp.bfloat16)
    grad_ref[2] = value_grad.astype(jnp.bfloat16)
    sum_ref[0:1, :] = jnp.sum(query_grad, 0, keepdims=True)
    sum_ref[1:2, :] = jnp.sum(value_grad, 0, keepdims=True)


def attention_backward(qkv, out, out_grad, probs, scale, start, pairs, at, size, before=None):
    length, width = out.shape
    total = width // LANES
    more = () if before is None else before

    def pair(part):
        return pl.BlockSpec((length, LANES), lambda j: (0, part * total + start + j))

    def body(*refs):
        attention_backward_kernel(*refs[:7], *refs[-2:])

    return pl.pallas_call(
        body,
        grid=(pairs,),
        in_specs=[
            pair(0),
            pair(1),
            pair(2),
            pair(0),
            pair(0),
            pl.BlockSpec((2, length, length), lambda j: (start + j, 0, 0)),
            pair(0),
        ]
        + [pl.BlockSpec(memory_space=pl.ANY)] * len(more),
        out_specs=[
            pl.BlockSpec((3, length, LANES), lambda j: (0, 0, j + at)),
            pl.BlockSpec((2, LANES), lambda j: (0, j + at)),
        ],
        out_shape=[
            jax.ShapeDtypeStruct((3, length, size * LANES), jnp.bfloat16),
            jax.ShapeDtypeStruct((2, size * LANES), jnp.float32),
        ],
        input_output_aliases={} if before is None else {7: 0, 8: 1},
        compiler_params=params(60),
        cost_estimate=cost(32 * length * length * pairs * LANES),
        name="attn_bwd",
    )(qkv, qkv, qkv, out, out_grad, probs, scale, *more)


class Place:
    def __init__(self, groups, shards):
        self.groups = groups
        self.shards = shards
        self.chips = shards // 2
        self.grp = lax.axis_index("grp")
        self.shard = lax.axis_index("shard")
        self.core = self.shard % 2
        self.chip = self.shard // 2
        self.scalars = jnp.stack([self.core, self.chip, self.grp]).astype(jnp.int32)

    def permute(self, array, mask_of_core):
        pairs = [(i, i ^ mask_of_core[i % 2]) for i in range(self.groups * self.shards)]
        return lax.ppermute(array, AXES, pairs)

    def swap_core(self, array):
        return self.permute(array, (1, 1))

    def swap_grp(self, array, step):
        masks = (self.shards, 2 * self.shards)
        return self.permute(array, masks if step == 0 else masks[::-1])

    def swap_chip(self, array, step):
        masks = (2, 4)
        return self.permute(array, masks if step == 0 else masks[::-1])

    def slot_chip(self, slot):
        return self.chip ^ turn(slot, self.core)

    def slot_grp(self, slot):
        return self.grp ^ turn(slot, self.core)


def turn(slot, core):
    if isinstance(slot, int):
        return slot if slot in (0, 3) else jnp.where(core == 0, slot, 3 - slot)
    return jnp.where((core == 0) | (slot == 0) | (slot == 3), slot, 3 - slot)


def after(value, *others):
    return lax.optimization_barrier((value, *others))[0]


def meet(anchor, *flights):
    arrays = [f.flying for f in flights]
    _, *arrays = lax.optimization_barrier((anchor, *arrays))
    for f, array in zip(flights, arrays):
        f.flying = array


class Gather:
    def __init__(self, place, piece):
        self.place = place
        self.piece = piece
        self.held = [None] * 4
        self.crossed = [None] * 4

    def chips_near(self, *wait):
        self.piece = after(self.piece, *wait)
        self.flying = self.place.swap_chip(self.piece, 0)

    def chips_far(self):
        self.pair = jnp.stack([self.piece, self.flying])
        self.flying = self.place.swap_chip(self.pair, 1)
        return self.pair

    def join(self):
        self.held[0] = jnp.concatenate([self.pair, self.flying])
        return self.held[0]

    def near(self, *wait):
        self.held[0] = after(self.held[0], *wait)
        self.flying = (self.place.swap_grp(self.held[0], 0), self.place.swap_grp(self.held[0], 1))
        return self.held[0]

    def far(self, *wait):
        self.held[1:3] = self.flying
        first = after(self.held[1], *wait)
        self.flying = self.place.swap_grp(first, 1)

    def landed(self):
        self.held[3] = self.flying

    def cross(self, *which, wait=()):
        for n in which:
            self.crossed[n] = self.place.swap_core(after(self.held[n], *wait))

    def pieces(self):
        return self.held + self.crossed


class Window:
    def __init__(self, gather, start, cols):
        self.arrays = gather.pieces()
        self.start, self.cols = start, cols
        chips, rows, _ = self.arrays[0].shape
        self.chips, self.rows = chips, rows


def fetch(where, window, refs, whole, sem, by):
    rows, cols, chips = window.rows, window.cols, window.chips
    for slot in range(4):
        for side in range(2):
            core = where[0] ^ side
            ref = refs[4 * side + slot]
            distance = turn(slot, core)
            col = pl.multiple_of((where[2] ^ distance) * cols, LANES)
            for k in range(chips):
                row = ((where[1] ^ turn(k, core)) * 2 + core) * rows
                pltpu.make_async_copy(
                    ref.at[k, :, pl.ds(window.start, cols)],
                    whole.at[pl.ds(pl.multiple_of(row, rows), rows), pl.ds(col, cols)],
                    sem.at[distance if by == "grp" else 0],
                ).start()


def weight_call(place, kernel, window, inputs, in_specs, outs, out_specs, steps, by, name, flops, write=True):
    cols, groups = window.cols, place.groups
    pieces = window.arrays
    shape = (window.chips * 2 * window.rows, groups * cols)
    slots = {"grp": groups, "all": 1}[by]
    anywhere = pl.BlockSpec(memory_space=pl.ANY)

    def body(where, *refs):
        taken, refs = refs[: len(pieces)], refs[len(pieces) :]
        *refs, weight, sem, out_sem = refs
        if write:
            *refs, written = refs
        step = pl.program_id(0)

        @pl.when(step == 0)
        def _():
            fetch(where, window, taken, weight, sem, by)

        def ready():
            if by == "all":

                @pl.when(step == 0)
                def _():
                    pltpu.make_async_copy(weight, weight, sem.at[0]).wait()
                    if write:
                        pltpu.make_async_copy(weight, written, out_sem.at[0]).start()

            else:
                at = pl.ds(pl.multiple_of((where[2] ^ step) * cols, LANES), cols)
                view = weight.at[:, at]
                pltpu.make_async_copy(view, view, sem.at[step]).wait()
                pltpu.make_async_copy(view, written.at[:, at], out_sem.at[step]).start()

        kernel(where, ready, weight, *refs)

        @pl.when(step == (steps - 1 if write else -1))
        def _():
            for slot in range(slots if write else 0):
                width = shape[1] // slots
                view = weight.at[:, pl.ds(slot * width, width)]
                pltpu.make_async_copy(view, view, out_sem.at[slot]).wait()

    total = sum(math.prod(x.shape) * x.dtype.itemsize for x in list(inputs) + list(outs))
    return pl.pallas_call(
        body,
        grid_spec=pltpu.PrefetchScalarGridSpec(
            num_scalar_prefetch=1,
            grid=(steps,),
            in_specs=[anywhere] * len(pieces) + in_specs,
            out_specs=out_specs + [anywhere] * write,
            scratch_shapes=[
                pltpu.VMEM(shape, jnp.bfloat16),
                pltpu.SemaphoreType.DMA((slots,)),
                pltpu.SemaphoreType.DMA((slots,)),
            ],
        ),
        out_shape=outs + [shaped(shape, jnp.bfloat16)] * write,
        compiler_params=params(60),
        cost_estimate=cost(flops),
        name=name,
    )(place.scalars, *pieces, *inputs)


def plain_call(kernel, inputs, in_specs, outs, out_specs, steps, name, flops):
    total = sum(math.prod(x.shape) * x.dtype.itemsize for x in list(inputs) + list(outs))
    return pl.pallas_call(
        kernel,
        grid=(steps,),
        in_specs=in_specs,
        out_specs=out_specs,
        out_shape=outs,
        compiler_params=params(60),
        cost_estimate=cost(flops),
        name=name,
    )(*inputs)


TILE = 256


def row_tiles(width):
    return pl.BlockSpec((TILE, width), lambda i, *s: (i, 0))


def fixed(*shape):
    return pl.BlockSpec(shape, lambda i, *s: (0,) * len(shape))


def whole_once(shape):
    return pl.BlockSpec(shape, lambda i: (0,) * len(shape), pipeline_mode=pl.Buffered(1))


def shaped(shape, dtype):
    return jax.ShapeDtypeStruct(shape, dtype)


B_QUERY, B_VALUE, B_ATTN, GAIN_ONE, SHIFT_ONE, B_OUT, GAIN_TWO, SHIFT_TWO, B_IN = range(9)


def row(ref, n):
    return ref[n : n + 1, :]


class Vectors:
    def __init__(self, place, vectors):
        lines = [v.reshape(-1, LANES) for v in vectors]
        blank = jnp.zeros((-sum(x.shape[0] for x in lines) % 16, LANES), jnp.bfloat16)
        self.own = jnp.concatenate([*lines, blank])
        self.place = place
        self.flying = place.swap_core(self.own)

    def chips_near(self):
        self.own = jnp.stack([self.own, self.flying])
        self.flying = self.place.swap_chip(self.own, 0)

    def chips_far(self):
        self.own = jnp.stack([self.own, self.flying])
        self.flying = self.place.swap_chip(self.own, 1)

    def landed(self):
        self.slots = jnp.concatenate([self.own, self.flying])

    def unpack(self, seg_row, keep_row):
        place = self.place
        length = seg_row.shape[1]
        slots, sides, rows, lanes = self.slots.shape
        shards = place.shards

        def kernel(where, in_ref, seg_ref, keep_ref, *outs):
            rows_ref, inner_ref, qkv_ref, seg_col_ref, keep_col_ref = outs
            for line_ref, col_ref in ((seg_ref, seg_col_ref), (keep_ref, keep_col_ref)):
                line = jnp.broadcast_to(line_ref[...].astype(jnp.float32), (8, length))
                col_ref[...] = line.T[:, 0:1].astype(col_ref.dtype)
            width = shards * lanes
            qkv_ref[...] = jnp.zeros_like(qkv_ref)
            for slot in range(slots):
                for side in range(sides):
                    core = where[0] ^ side
                    shard = (where[1] ^ turn(slot, where[0])) * 2 + core
                    part = in_ref[slot, side].astype(jnp.float32)
                    at = pl.multiple_of(shard * lanes, lanes)
                    rows_ref[:, pl.ds(at, lanes)] = part
                    qkv_ref[:, pl.ds(at, lanes)] = part[B_QUERY : B_QUERY + 1]
                    qkv_ref[:, pl.ds(2 * width + at, lanes)] = part[B_VALUE : B_VALUE + 1]
                    for n in range(4):
                        start = pl.multiple_of((shard * 4 + n) * lanes, lanes)
                        inner_ref[:, pl.ds(start, lanes)] = part[B_IN + n : B_IN + n + 1]

        in_vmem = pl.BlockSpec(memory_space=pltpu.VMEM)
        return pl.pallas_call(
            kernel,
            in_specs=[pl.BlockSpec(memory_space=pltpu.SMEM)] + [in_vmem] * 3,
            out_specs=[in_vmem] * 5,
            out_shape=[
                shaped((rows, shards * lanes), jnp.float32),
                shaped((1, 4 * shards * lanes), jnp.float32),
                shaped((1, 3 * shards * lanes), jnp.float32),
                shaped((length, 1), jnp.int32),
                shaped((length, 1), jnp.float32),
            ],
            name="vectors",
        )(place.scalars, self.slots, seg_row, keep_row)


def project_qkv(place, rows, window, bias, scale):
    length, width = rows.shape
    cols = window.cols

    def kernel(where, ready, weight, x_ref, bias_ref, scale_ref, out_ref):
        ready()
        at = pl.ds(pl.multiple_of((where[2] ^ pl.program_id(0)) * cols, LANES), cols)
        for tile in range(length // TILE):
            here = pl.ds(tile * TILE, TILE)
            mixed = mxu(x_ref[here, :], weight[:, at], NN) + bias_ref[:, at]
            mixed = mixed.astype(jnp.bfloat16).astype(jnp.float32) * scale_ref[:, at]
            out_ref[here, :] = mixed.astype(jnp.bfloat16)

    total = cols * place.groups
    return weight_call(
        place,
        kernel,
        window,
        (rows, bias, scale),
        [fixed(length, width), fixed(1, total), fixed(1, total)],
        [shaped((length, total), jnp.bfloat16)],
        [pl.BlockSpec((length, cols), lambda i, s: (0, i ^ s[2]))],
        place.groups,
        "grp",
        "qkv",
        2 * length * width * total,
    )


def norm_parts(rows):
    centered = rows - jnp.mean(rows, -1, keepdims=True)
    scale = lax.rsqrt(jnp.mean(centered * centered, -1, keepdims=True) + epsilon)
    return centered * scale, scale


def norm_back(grad, normed, scale):
    return scale * (
        grad
        - jnp.mean(grad, -1, keepdims=True)
        - normed * jnp.mean(grad * normed, -1, keepdims=True)
    )


def add_rows(sum_ref, *terms):
    @pl.when(pl.program_id(0) == 0)
    def _():
        sum_ref[...] = jnp.zeros_like(sum_ref)

    for n, term in enumerate(terms):
        sum_ref[n : n + 1, :] += jnp.sum(term, 0, keepdims=True)


def project_out(place, contexts, window, rows, vectors):
    length, width = rows.shape

    def kernel(where, ready, weight, c_ref, x_ref, v_ref, n_ref, r_ref, low_ref):
        ready()
        first_sum = mxu(c_ref[...], weight[...], NN) + row(v_ref, B_ATTN)
        first_sum = first_sum + x_ref[...].astype(jnp.float32)
        normed, scale = norm_parts(first_sum)
        n_ref[...] = normed
        r_ref[...] = jnp.broadcast_to(scale, r_ref.shape)
        low_ref[...] = (normed * row(v_ref, GAIN_ONE) + row(v_ref, SHIFT_ONE)).astype(jnp.bfloat16)

    return weight_call(
        place,
        kernel,
        window,
        (contexts, rows, vectors),
        [row_tiles(width), row_tiles(width), fixed(*vectors.shape)],
        [
            shaped((length, width), jnp.float32),
            shaped((length, LANES), jnp.float32),
            shaped((length, width), jnp.bfloat16),
        ],
        [row_tiles(width), row_tiles(LANES), row_tiles(width)],
        length // TILE,
        "all",
        "attn_out",
        2 * length * width * width,
    )


def feed_in(place, normed_low, window, bias):
    length, width = normed_low.shape
    cols = window.cols

    def kernel(where, ready, weight, x_ref, bias_ref, hid_ref, slope_ref):
        ready()
        at = pl.ds(pl.multiple_of((where[2] ^ pl.program_id(0)) * cols, LANES), cols)
        size = min(512, length)
        for tile in range(length // size):
            here = pl.ds(tile * size, size)
            pre = mxu(x_ref[here, :], weight[:, at], NN) + bias_ref[:, at]
            share = 0.5 + 0.5 * lax.erf(pre * (1.0 / math.sqrt(2.0)))
            bell = jnp.exp(-0.5 * pre * pre) * (1.0 / math.sqrt(2.0 * math.pi))
            hid_ref[here, :] = (pre * share).astype(jnp.bfloat16)
            slope_ref[here, :] = (share + pre * bell).astype(jnp.bfloat16)

    total = cols * place.groups
    block = pl.BlockSpec((length, cols), lambda i, s: (0, i ^ s[2]))
    return weight_call(
        place,
        kernel,
        window,
        (normed_low, bias),
        [fixed(length, width), fixed(1, total)],
        [shaped((length, total), jnp.bfloat16)] * 2,
        [block, block],
        place.groups,
        "grp",
        "feed_in",
        2 * length * width * total,
    )


def feed_out(place, hidden, window, normed, cot, keep, vectors, slope):
    length, inner = hidden.shape
    width = normed.shape[1]

    def kernel(where, ready, weight, h_ref, n_ref, cot_ref, keep_ref, v_ref, slope_ref, *outs):
        out_ref, grad_ref, low_ref, sum_ref, pre_ref, inner_ref = outs
        ready()
        fed = mxu(h_ref[...], weight[...], NN)
        normed_one = n_ref[...] * row(v_ref, GAIN_ONE) + row(v_ref, SHIFT_ONE)
        second_sum = normed_one + (fed + row(v_ref, B_OUT))
        second, scale = norm_parts(second_sum)
        out_ref[...] = (second * row(v_ref, GAIN_TWO) + row(v_ref, SHIFT_TWO)).astype(jnp.bfloat16)
        masked = cot_ref[...].astype(jnp.float32) * keep_ref[...]
        grad = norm_back(masked * row(v_ref, GAIN_TWO), second, scale)
        grad_ref[...] = grad
        low = grad.astype(jnp.bfloat16)
        low_ref[...] = low
        add_rows(sum_ref, masked * second, masked, grad)

        @pl.when(pl.program_id(0) == 0)
        def _():
            inner_ref[...] = jnp.zeros_like(inner_ref)

        size = min(1024, inner)
        for n in range(inner // size):
            at = slice(n * size, (n + 1) * size)
            pre = mxu(low, weight[at, :], NT) * slope_ref[:, at].astype(jnp.float32)
            pre_ref[:, at] = pre.astype(jnp.bfloat16)
            inner_ref[:, at] += jnp.sum(pre, 0, keepdims=True)

    return weight_call(
        place,
        kernel,
        window,
        (hidden, normed, cot, keep, vectors, slope),
        [
            row_tiles(inner),
            row_tiles(width),
            row_tiles(width),
            row_tiles(1),
            fixed(*vectors.shape),
            row_tiles(inner),
        ],
        [
            shaped((length, width), jnp.bfloat16),
            shaped((length, width), jnp.float32),
            shaped((length, width), jnp.bfloat16),
            shaped((8, width), jnp.float32),
            shaped((length, inner), jnp.bfloat16),
            shaped((1, inner), jnp.float32),
        ],
        [
            row_tiles(width),
            row_tiles(width),
            row_tiles(width),
            fixed(8, width),
            row_tiles(inner),
            fixed(1, inner),
        ],
        length // TILE,
        "all",
        "feed_out",
        4 * length * width * inner,
        write=False,
    )


def feed_in_back(pre_low, weight, second_grad, normed, scale, vectors, attn_weight):
    length, inner = pre_low.shape
    width = normed.shape[1]

    def kernel(p_ref, w_ref, g_ref, n_ref, r_ref, v_ref, a_ref, first_ref, low_ref, ctx_ref, sum_ref):
        grad = g_ref[...] + mxu(p_ref[...], w_ref[...], NT)
        first = norm_back(grad * row(v_ref, GAIN_ONE), n_ref[...], r_ref[:, :1])
        low = first.astype(jnp.bfloat16)
        first_ref[...] = first
        low_ref[...] = low
        ctx_ref[...] = mxu(low, a_ref[...], NT).astype(jnp.bfloat16)
        add_rows(sum_ref, grad * n_ref[...], grad, first)

    return plain_call(
        kernel,
        (pre_low, weight, second_grad, normed, scale, vectors, attn_weight),
        [
            row_tiles(inner),
            whole_once(weight.shape),
            row_tiles(width),
            row_tiles(width),
            row_tiles(LANES),
            fixed(*vectors.shape),
            whole_once(attn_weight.shape),
        ],
        [
            shaped((length, width), jnp.float32),
            shaped((length, width), jnp.bfloat16),
            shaped((length, width), jnp.bfloat16),
            shaped((8, width), jnp.float32),
        ],
        [row_tiles(width), row_tiles(width), row_tiles(width), fixed(8, width)],
        length // TILE,
        "feed_in_back",
        2 * length * width * (inner + width),
    )


def project_qkv_back(grads, weight, first_grad, start, tiles, before=None):
    length, width = first_grad.shape
    part = width // len(grads)

    def kernel(w_ref, *refs):
        grad_refs, first_ref, out_ref = refs[: len(grads)], refs[len(grads)], refs[-1]
        total = first_ref[...]
        for n in range(3):
            for m, grad_ref in enumerate(grad_refs):
                at = n * width + m * part
                total = total + mxu(grad_ref[n], w_ref[:, at : at + part], NT)
        out_ref[...] = total

    tile = pl.BlockSpec((TILE, width), lambda i: (start + i, 0))
    more = () if before is None else (before,)
    return pl.pallas_call(
        kernel,
        grid=(tiles,),
        in_specs=[whole_once(weight.shape)]
        + [pl.BlockSpec((3, TILE, part), lambda i: (0, start + i, 0))] * len(grads)
        + [tile]
        + [pl.BlockSpec(memory_space=pl.ANY)] * len(more),
        out_specs=tile,
        out_shape=shaped((length, width), jnp.float32),
        input_output_aliases={} if before is None else {len(grads) + 2: 0},
        compiler_params=params(60),
        cost_estimate=cost(6 * tiles * TILE * width * width),
        name="qkv_back",
    )(weight, *grads, first_grad, *more)


ORDER = (1, 3, 0, 2)


def ordered_slot(j):
    return jnp.where(j < 2, 2 * j + 1, 2 * j - 4)


def weight_grad_kernel(where, left_ref, right_ref, own, sent, kept, *, rows, groups, split):
    core = where[0]
    chips = left_ref.shape[1] // (2 * rows)

    @pl.when(pl.program_id(1) == 0)
    def _():
        keep_rows(core, left_ref, rows, kept)

    if split:
        size = min(512, right_ref.shape[1])
        for ref, side in ((sent, 1), (own, 0)):
            for n in range(right_ref.shape[1] // size):
                at = slice(n * size, (n + 1) * size)
                part = mxu(kept[side], right_ref[:, at], NN).astype(jnp.bfloat16)
                ref[0, :, :, at] = part.reshape(chips, rows, size)
    else:
        cols = right_ref.shape[1] // groups
        for ref, side in ((sent, 1), (own, 0)):
            for pos, slot in enumerate(ORDER):
                start = pl.multiple_of((where[2] ^ turn(slot, core ^ side)) * cols, LANES)
                part = mxu(kept[side], right_ref[:, pl.ds(start, cols)], NN)
                ref[pos] = part.astype(jnp.bfloat16).reshape(chips, rows, cols)


def keep_rows(core, left_ref, rows, kept):
    chips = left_ref.shape[1] // (2 * rows)
    for side in range(2):
        chosen = []
        for k in range(chips):
            even = left_ref[:, 2 * k * rows : (2 * k + 1) * rows]
            odd = left_ref[:, (2 * k + 1) * rows : (2 * k + 2) * rows]
            chosen.append(jnp.where(core == side, even, odd))
        left = chosen[0] if chips == 1 else jnp.concatenate(chosen, 1)
        kept[side] = left.T


def turned_rows(place, left):
    tokens, height = left.shape

    def kernel(where, left_ref, out_ref):
        keep_rows(where[0], left_ref, height // place.shards, out_ref)

    in_vmem = pl.BlockSpec(memory_space=pltpu.VMEM)
    return pl.pallas_call(
        kernel,
        in_specs=[pl.BlockSpec(memory_space=pltpu.SMEM), in_vmem],
        out_specs=in_vmem,
        out_shape=shaped((2, height // 2, tokens), jnp.bfloat16),
        compiler_params=params(40),
        name="turned_rows",
    )(place.scalars, left)


def attention_grads_kernel(where, *refs, rows, groups, extra):
    turned, right_ref, *refs = refs
    *more, own, sent, kept = refs
    core, grp = where[0], where[2]
    chips = turned.shape[1] // rows
    step = pl.program_id(0)

    def scatter(lefts, right, at, cols):
        for ref, side in ((sent, 1), (own, 0)):
            part = mxu(lefts[side], right, NN).astype(jnp.bfloat16)
            for g in range(groups):
                pos = position(grp ^ g, core ^ side)
                block = part[:, g * cols : (g + 1) * cols].reshape(chips, rows, cols)
                ref[pos, :, 0:rows, pl.ds(at, cols)] = block

    skip = 0
    if not extra:
        other_left, other_right = more
        skip = other_right.shape[1] // groups

        @pl.when(step == 0)
        def _():
            keep_rows(core, other_left, rows, kept)
            scatter(kept, other_right[...], 0, skip)

    cols = right_ref.shape[2] // groups
    scatter(turned, right_ref[0], pl.multiple_of(skip + step * cols, LANES), cols)

    if extra:

        @pl.when(step == 2)
        def _():
            blank = jnp.zeros((extra, own.shape[3]), jnp.bfloat16)
            for ref, side in ((sent, 1), (own, 0)):
                for k in range(chips):
                    lines = vector_sums(2 * k + (core ^ side), *more)
                    for g in range(groups):
                        pos = position(grp ^ g, core ^ side)
                        ref[pos, k, rows : rows + extra, :] = blank
                        for n in range(3):
                            ref[pos, k, rows : rows + 1, n * LANES : (n + 1) * LANES] = lines[
                                3 * g + n
                            ].astype(jnp.bfloat16)


def vector_sums(shard, a_ref, b_ref, one_ref, two_ref, inner_ref):
    half = a_ref.shape[1]
    start = shard * LANES

    def part(ref, start):
        return ref[:, pl.ds(pl.multiple_of(start, LANES), LANES)]

    late = jnp.where(
        start < half,
        part(a_ref, jnp.minimum(start, half - LANES)),
        part(b_ref, jnp.maximum(start - half, 0)),
    )
    one, two = part(one_ref, start), part(two_ref, start)
    lines = [None] * 12
    lines[B_QUERY], lines[B_VALUE] = late[0:1], late[1:2]
    lines[GAIN_ONE], lines[SHIFT_ONE], lines[B_ATTN] = one[0:1], one[1:2], one[2:3]
    lines[GAIN_TWO], lines[SHIFT_TWO], lines[B_OUT] = two[0:1], two[1:2], two[2:3]
    for n in range(4):
        lines[B_IN + n] = part(inner_ref, (4 * shard + n) * LANES)
    return lines


def position(distance, core):
    slot = turn(distance, core)
    return jnp.where(slot == 0, 2, jnp.where(slot == 1, 0, jnp.where(slot == 3, 1, 3)))


def attention_grads(place, turned, right, more, name):
    height, tokens = 2 * turned.shape[1], turned.shape[2]
    groups, chips = place.groups, place.chips
    rows = height // place.shards
    extra = 16 if len(more) > 2 else 0
    size = right.shape[2]
    cols = 3 * size // groups + (0 if extra else more[1].shape[1] // groups)
    shape = (groups, chips, rows + extra, cols)
    once = [
        pl.BlockSpec(x.shape, lambda i, s: (0, 0), pipeline_mode=pl.Buffered(1)) for x in more
    ]
    return pl.pallas_call(
        functools.partial(attention_grads_kernel, rows=rows, groups=groups, extra=extra),
        grid_spec=pltpu.PrefetchScalarGridSpec(
            num_scalar_prefetch=1,
            grid=(3,),
            in_specs=[
                pl.BlockSpec(turned.shape, lambda i, s: (0, 0, 0), pipeline_mode=pl.Buffered(1)),
                pl.BlockSpec((1, tokens, size), lambda i, s: (i, 0, 0)),
            ]
            + once,
            out_specs=[pl.BlockSpec(shape, lambda i, s: (0, 0, 0, 0))] * 2,
            scratch_shapes=[pltpu.VMEM((8, LANES) if extra else turned.shape, jnp.bfloat16)],
        ),
        out_shape=[shaped(shape, jnp.bfloat16)] * 2,
        compiler_params=params(60),
        cost_estimate=cost(2 * tokens * height * cols * groups),
        name="wgrad_" + name,
    )(place.scalars, turned, right, *more)


def weight_grad(place, left, right, split, name):
    tokens, height = left.shape
    groups, chips = place.groups, place.chips
    rows = height // place.shards
    step_chips = chips if split else max(1, 1024 // (2 * rows))
    cols = right.shape[1] // groups
    if split:
        grid = (1, groups)
        block = lambda i, j, s: (0, s[2] ^ turn(ordered_slot(j), s[0]))
        right_spec = pl.BlockSpec((tokens, cols), block)
        one = (1, chips, rows, cols)
        other = lambda j: jnp.where(j == 0, 3, jnp.where(j == 3, 0, j))
        out_specs = [
            pl.BlockSpec(one, lambda i, j, s: (j, 0, 0, 0)),
            pl.BlockSpec(one, lambda i, j, s: (other(j), 0, 0, 0)),
        ]
    else:
        grid = (chips // step_chips, 1)
        right_spec = pl.BlockSpec(right.shape, lambda i, j, s: (0, 0))
        out_specs = [
            pl.BlockSpec((groups, step_chips, rows, cols), lambda i, j, s: (0, i, 0, 0))
        ] * 2
    return pl.pallas_call(
        functools.partial(weight_grad_kernel, rows=rows, groups=groups, split=split),
        grid_spec=pltpu.PrefetchScalarGridSpec(
            num_scalar_prefetch=1,
            grid=grid,
            in_specs=[
                pl.BlockSpec((tokens, step_chips * 2 * rows), lambda i, j, s: (0, i)),
                right_spec,
            ],
            out_specs=out_specs,
            scratch_shapes=[pltpu.VMEM((2, step_chips * rows, tokens), jnp.bfloat16)],
        ),
        out_shape=[shaped((groups, chips, rows, cols), jnp.bfloat16)] * 2,
        compiler_params=params(60),
        cost_estimate=cost(2 * tokens * height * cols * groups),
        name="wgrad_" + name,
    )(place.scalars, left, right)


def add(*terms):
    total = terms[0].astype(jnp.float32)
    for term in terms[1:]:
        total = total + term.astype(jnp.float32)
    return total.astype(jnp.bfloat16)


class Reduction:
    def __init__(self, place, made):
        self.place = place
        self.made, sent = made
        self.flying = place.swap_core(sent)

    def near(self):
        self.core = self.flying
        leave = add(self.made[:2], self.core[:2])
        self.flying = self.place.swap_grp(leave, 0)
        return leave

    def middle(self):
        self.first = self.flying
        second = add(self.made[3], self.core[3], self.first[1])
        self.flying = self.place.swap_grp(second, 1)
        return second

    def column(self):
        terms = (self.made[2], self.core[2], self.first[0], self.flying)
        return lambda chip: [lax.dynamic_index_in_dim(t, chip, 0, False) for t in terms]

    def along(self):
        place = self.place
        at = self.column()
        self.mine = [at(place.slot_chip(slot)) for slot in (0, 2)]
        both = jnp.stack([add(*at(place.slot_chip(slot))) for slot in (1, 3)])
        self.flying = place.swap_chip(both, 0)
        return both

    def along_far(self):
        self.first = self.flying
        second = add(*self.mine[1], self.first[1])
        self.flying = self.place.swap_chip(second, 1)
        return second

    def share(self):
        return add(*self.mine[0], self.first[0], self.flying)

    def along_direct(self):
        place = self.place
        at = self.column()
        self.mine = at(place.chip)
        sent = [add(*at(place.chip ^ k)) for k in range(place.chips - 1, 0, -1)]
        self.flying = tuple(
            place.permute(block, (2 * k, 2 * k))
            for k, block in zip(range(place.chips - 1, 0, -1), sent)
        )
        return sent

    def share_direct(self):
        return add(*self.mine, *self.flying)


class Replication:
    def __init__(self, place, share, direct=False):
        self.place = place
        self.blocks = [share] + [None] * 3
        if direct:
            size = place.shards
            for mask in (3, 1, 2):
                self.blocks[mask] = place.permute(share, (mask * size, mask * size))
        else:
            self.flying = place.swap_grp(share, 0)

    def far(self):
        pair = jnp.stack([self.blocks[0], self.flying])
        self.blocks[1] = self.flying
        self.flying = self.place.swap_grp(pair, 1)
        return pair

    def landed(self):
        if self.blocks[2] is None:
            self.blocks[2:] = [self.flying[0], self.flying[1]]
        return self.blocks


def order_feed_forward(place, blocks, rows_in):
    groups = place.groups
    height, cols = blocks[0].shape
    rows_out = height - groups * rows_in

    def kernel(where, *refs):
        *blocks, out_ref, in_ref = refs
        for slot, ref in enumerate(blocks):
            g = where[2] ^ turn(slot, where[0])
            at = pl.multiple_of(g * cols, LANES)
            out_ref[:, pl.ds(at, cols)] = ref[0:rows_out, :].astype(jnp.float32)
            for n in range(groups):
                at = pl.multiple_of((g * groups + n) * cols, LANES)
                part = ref[rows_out + n * rows_in : rows_out + (n + 1) * rows_in, :]
                in_ref[:, pl.ds(at, cols)] = part.astype(jnp.float32)

    in_vmem = pl.BlockSpec(memory_space=pltpu.VMEM)
    return pl.pallas_call(
        kernel,
        in_specs=[pl.BlockSpec(memory_space=pltpu.SMEM)] + [in_vmem] * groups,
        out_specs=[in_vmem] * 2,
        out_shape=[
            shaped((rows_out, groups * cols), jnp.float32),
            shaped((rows_in, groups * groups * cols), jnp.float32),
        ],
        compiler_params=params(40),
        cost_estimate=cost(height * cols * 1024),
        name="order_feed_forward",
    )(place.scalars, *blocks)


def order_attention(place, blocks_a, blocks_b, rows):
    groups = place.groups
    size = blocks_b[0].shape[1] // 3
    skip = blocks_a[0].shape[1] - 3 * size
    width = groups * skip

    def kernel(where, *refs):
        *blocks, attn_ref, qkv_ref, small_ref = refs
        for n in range(groups):
            ref = blocks[n]
            g = where[2] ^ turn(n, where[0])
            attn_ref[:, pl.ds(pl.multiple_of(g * skip, LANES), skip)] = ref[:, 0:skip].astype(
                jnp.float32
            )
            for part in range(3):
                at = pl.multiple_of(part * width + g * size, LANES)
                block = ref[:, skip + part * size : skip + (part + 1) * size]
                qkv_ref[:, pl.ds(at, size)] = block.astype(jnp.float32)
        for n in range(groups):
            ref = blocks[groups + n]
            g = where[2] ^ n
            lines = []
            for part in range(3):
                at = pl.multiple_of(part * width + width // 2 + g * size, LANES)
                here = slice(part * size, (part + 1) * size)
                qkv_ref[:, pl.ds(at, size)] = ref[0:rows, here].astype(jnp.float32)
                lines.append(ref[rows : rows + 16, here].astype(jnp.float32)[0:1])
            lines.append(jnp.zeros((5, size), jnp.float32))
            small_ref[pl.ds(pl.multiple_of(g * 8, 8), 8), :] = jnp.concatenate(lines)

    in_vmem = pl.BlockSpec(memory_space=pltpu.VMEM)
    return pl.pallas_call(
        kernel,
        in_specs=[pl.BlockSpec(memory_space=pltpu.SMEM)] + [in_vmem] * (2 * groups),
        out_specs=[in_vmem] * 3,
        out_shape=[
            shaped((rows, width), jnp.float32),
            shaped((rows, 3 * width), jnp.float32),
            shaped((8 * groups, size), jnp.float32),
        ],
        compiler_params=params(40),
        name="order_attention",
    )(place.scalars, *blocks_a, *blocks_b)


def on_device_permutes(
    tokens,
    segment_ids,
    keep_flag,
    cotangent,
    w_qkv,
    b_query,
    b_value,
    w_attn_out,
    b_attn_out,
    norm1_gain,
    norm1_bias,
    w_in,
    b_in,
    w_out,
    b_out,
    norm2_gain,
    norm2_bias,
    *,
    groups,
    shards,
):
    place = Place(groups, shards)
    _, length, width = tokens.shape
    rows = tokens[0]
    seg_row = segment_ids.reshape(1, length)
    pairs = width // LANES

    c1 = Gather(place, w_qkv)
    c2 = Gather(place, jnp.concatenate([w_in, w_attn_out], 1))
    c3 = Gather(place, w_out)
    c1.chips_near()
    small = Vectors(
        place,
        (b_query, b_value, b_attn_out, norm1_gain, norm1_bias, b_out, norm2_gain, norm2_bias, b_in),
    )
    meet(rows, c1, small)
    pair = c1.chips_far()
    small.chips_near()
    meet(pair, c1, small)
    joined = c1.join()
    c1.near()
    small.chips_far()
    c2.chips_near(joined)
    meet(joined, c2, small)
    small.landed()
    pair = c2.chips_far()
    vectors, bias_in, qkv_bias, seg_col, keep = small.unpack(
        seg_row, keep_flag.reshape(1, length)
    )
    c1.flying = lax.optimization_barrier(c1.flying)
    turned = turned_rows(place, after(rows, vectors))
    c1.far(pair, vectors)
    c1.cross(0, 1, 2)
    joined = c2.join()
    meet((joined, turned), c1)
    c1.landed()
    c2.near(c1.held[3])
    c1.cross(3)
    c3.chips_near(c1.held[3])
    blank = jnp.ones((1, width), jnp.float32)
    qkv_scale = jnp.concatenate([blank / math.sqrt(HD), blank, blank], 1)

    mixed, full_qkv = project_qkv(place, rows, Window(c1, 0, w_qkv.shape[1]), qkv_bias, qkv_scale)
    meet(mixed, c3)
    pair = c3.chips_far()
    c2.cross(0, wait=(mixed,))
    first, second = pairs * 3 // 8, pairs * 3 // 4
    forward = attention_forward(after(mixed, pair), seg_col, seg_row, 0, first)
    meet(forward[0], c2, c3)
    c2.far()
    joined = c3.join()
    c3.near()
    c2.cross(1, 2)
    forward = attention_forward(
        after(mixed, joined), seg_col, seg_row, first, second - first, forward
    )
    meet(forward[0], c2)
    c2.landed()
    c2.cross(3)
    contexts, probs, probs_scale = attention_forward(
        after(mixed, c2.held[3]), seg_col, seg_row, second, pairs - second, forward
    )
    normed, scale_one, normed_low, full_attn = project_out(
        place, contexts, Window(c2, w_in.shape[1], w_attn_out.shape[1]), rows, vectors
    )
    meet(normed_low, c3)
    c3.far()
    c3.cross(0, 1, 2)
    hidden, slope, full_in = feed_in(
        place, after(normed_low, c3.held[1]), Window(c2, 0, w_in.shape[1]), bias_in
    )
    meet(hidden, c3)
    c3.landed()
    c3.cross(3)
    layer_out, second_grad, out_low, second_sums, pre_low, bias_in_grad = feed_out(
        place, hidden, Window(c3, 0, w_out.shape[1]), normed, cotangent[0], keep, vectors, slope
    )

    r_out = Reduction(place, weight_grad(place, hidden, out_low, False, "out"))
    r_in = Reduction(place, weight_grad(place, after(normed_low, r_out.made), pre_low, True, "in"))
    meet(r_in.made, r_out)
    step = r_out.near()
    first_grad, attn_low, context_grad, first_sums = feed_in_back(
        after(pre_low, r_in.made, step), full_in, second_grad, normed, scale_one, vectors, full_attn
    )
    meet(attn_low, r_in)
    step = r_in.near()
    half, quarter = pairs // 2, pairs // 4

    def back(wait, start, count, at, before=None):
        return attention_backward(
            mixed,
            contexts,
            after(context_grad, *wait),
            probs,
            probs_scale,
            start,
            count,
            at,
            half,
            before,
        )

    low_a, late_a = back((step,), 0, half, 0)
    meet(late_a, r_out, r_in)
    steps = (r_out.middle(), r_in.middle())
    r_a = Reduction(
        place, attention_grads(place, after(turned, *steps), low_a, (contexts, attn_low), "a")
    )
    meet(r_a.made, r_out)
    step = r_out.along()
    part = back((r_a.made, step), half, quarter, 0)
    meet(part[1], r_out, r_in, r_a)
    steps = (r_out.along_far(), r_in.along(), r_a.near())
    low_b, late_b = back(steps, half + quarter, quarter, quarter, part)
    meet(late_b, r_out, r_in, r_a)
    sums = (late_a, late_b, first_sums, second_sums, bias_in_grad)
    share_out = r_out.share()
    steps = (r_in.along_far(), r_a.middle(), share_out)
    r_b = Reduction(place, attention_grads(place, after(turned, *steps), low_b, sums, "b"))
    meet(r_b.made, r_in, r_a)
    share_in = r_in.share()
    inner = share_in.shape[1] // groups
    joined = jnp.concatenate(
        [share_out] + [share_in[:, n * inner : (n + 1) * inner] for n in range(groups)]
    )
    all_ffn = Replication(place, joined)
    grads = (low_a, after(low_b, r_b.made, joined, r_a.along()))
    tiles = length // TILE // 2
    input_grad = project_qkv_back(grads, full_qkv, first_grad, 0, tiles)
    meet(input_grad, r_b, r_a, all_ffn)
    steps = (r_b.near(), r_a.along_far())
    input_grad = project_qkv_back(
        grads, full_qkv, after(first_grad, *steps), tiles, tiles, input_grad
    )
    meet(input_grad, r_b, r_a)
    middle = r_b.middle()
    r_a.flying = after(r_a.flying, middle)
    all_a = Replication(place, r_a.share())
    meet(all_a.blocks[0], r_b, all_a)
    along = r_b.along_direct()
    all_a.flying = after(all_a.flying, *along)
    all_ffn.flying = after(all_ffn.flying, *along)
    pairs_made = (all_a.far(), all_ffn.far())
    meet(pairs_made, r_b)
    share_b = r_b.share_direct()
    all_b = Replication(place, share_b, direct=True)
    meet(share_b, all_ffn)
    w_out_grad, w_in_grad = order_feed_forward(place, all_ffn.landed(), share_in.shape[0])
    all_a.flying = after(all_a.flying, w_out_grad)
    w_attn_grad, w_qkv_grad, small = order_attention(
        place, all_a.landed(), all_b.landed(), w_attn_out.shape[0]
    )
    small = [small[8 * (n // 3) + n % 3] for n in range(12)]
    return (
        layer_out[None],
        input_grad[None],
        w_qkv_grad,
        small[B_QUERY],
        small[B_VALUE],
        w_attn_grad,
        small[B_ATTN],
        small[GAIN_ONE],
        small[SHIFT_ONE],
        w_in_grad,
        jnp.concatenate(small[B_IN:]),
        w_out_grad,
        small[B_OUT],
        small[GAIN_TWO],
        small[SHIFT_TWO],
    )


def solution(mesh):
    groups, shards = mesh.shape["grp"], mesh.shape["shard"]
    if groups == 4 and shards == 8:
        body = functools.partial(on_device_permutes, groups=groups, shards=shards)
    else:
        body = on_device
    return jax.shard_map(
        body,
        mesh=mesh,
        in_specs=(
            P(("grp", "shard"), None, None),
            P(("grp", "shard"), None),
            P(("grp", "shard"), None),
            P(("grp", "shard"), None, None),
            P("shard", "grp"),
            P("shard"),
            P("shard"),
            P("shard", "grp"),
            P("shard"),
            P("shard"),
            P("shard"),
            P("shard", "grp"),
            P("shard"),
            P("shard", "grp"),
            P("shard"),
            P("shard"),
            P("shard"),
        ),
        out_specs=(
            P(("grp", "shard"), None, None),
            P(("grp", "shard"), None, None),
            P("shard", None),
            P("shard"),
            P("shard"),
            P("shard", None),
            P("shard"),
            P("shard"),
            P("shard"),
            P("shard", None),
            P("shard"),
            P("shard", None),
            P("shard"),
            P("shard"),
            P("shard"),
        ),
        check_vma=False,
    )
```

```python
import functools
import math

import jax
import jax.numpy as jnp
from jax import lax
from jax.experimental import pallas as pl
from jax.experimental.pallas import tpu as pltpu
from jax.sharding import PartitionSpec as P

H = 16
HD = 64


masked_score = -1e30
epsilon = 1e-05


def norm_layer(rows, gain_row, shift_row):
    row_mean = jnp.mean(rows, -1, keepdims=True)
    centered = rows - row_mean
    row_var = jnp.mean(centered * centered, -1, keepdims=True)
    return centered * lax.rsqrt(row_var + epsilon) * gain_row + shift_row


def gelu_exact(values):
    return 0.5 * values * (1.0 + lax.erf(values * (1.0 / math.sqrt(2.0))))


def contract_rows(left, right):
    return lax.dot_general(
        left, right, (((0,), (0,)), ((), ())), preferred_element_type=jnp.float32
    )


def contract_cols(left, right):
    return lax.dot_general(
        left, right, (((1,), (1,)), ((), ())), preferred_element_type=jnp.float32
    )


def attend_forward(queries, key_rows, value_rows, segment_row, block_rows):
    length, model_width = queries.shape
    scaling = 1.0 / math.sqrt(HD)
    key_heads = key_rows.reshape(length, H, HD)
    value_heads = value_rows.reshape(length, H, HD)
    query_blocks = queries.reshape(length // block_rows, block_rows, H, HD)
    segment_blocks = segment_row.reshape(length // block_rows, block_rows)

    def one_block(pieces):
        query_part, segment_part = pieces
        scores = (
            jnp.einsum("qhd,khd->hqk", query_part, key_heads, preferred_element_type=jnp.float32)
            * scaling
        )
        allowed = segment_part[:, None] == segment_row[None, :]
        scores = jnp.where(allowed[None], scores, masked_score)
        row_max = jnp.max(scores, -1, keepdims=True)
        powers = jnp.exp(scores - row_max)
        totals = jnp.sum(powers, -1, keepdims=True)
        attn_probs = (powers / totals).astype(jnp.bfloat16)
        context = jnp.einsum(
            "hqk,khd->qhd", attn_probs, value_heads, preferred_element_type=jnp.float32
        )
        return (
            context.reshape(block_rows, model_width).astype(jnp.bfloat16),
            (row_max + jnp.log(totals))[:, :, 0],
        )

    contexts, log_sums = lax.map(one_block, (query_blocks, segment_blocks))
    return (contexts.reshape(length, model_width), log_sums)


def attend_backward(queries, key_rows, value_rows, segment_row, log_sums, context_grad, block_rows):
    length, model_width = queries.shape
    scaling = 1.0 / math.sqrt(HD)
    key_heads = key_rows.reshape(length, H, HD)
    value_heads = value_rows.reshape(length, H, HD)
    query_blocks = queries.reshape(length // block_rows, block_rows, H, HD)
    segment_blocks = segment_row.reshape(length // block_rows, block_rows)
    grad_blocks = context_grad.reshape(length // block_rows, block_rows, H, HD)

    def one_block(running, pieces):
        key_acc, value_acc = running
        query_part, segment_part, lse_part, grad_part = pieces
        scores = (
            jnp.einsum("qhd,khd->hqk", query_part, key_heads, preferred_element_type=jnp.float32)
            * scaling
        )
        allowed = segment_part[:, None] == segment_row[None, :]
        scores = jnp.where(allowed[None], scores, masked_score)
        probs = jnp.exp(scores - lse_part[:, :, None])
        prob_low = probs.astype(jnp.bfloat16)
        prob_grad = jnp.einsum(
            "qhd,khd->hqk", grad_part, value_heads, preferred_element_type=jnp.float32
        )
        row_dot = jnp.sum(prob_grad * probs, -1, keepdims=True)
        score_grad = (probs * (prob_grad - row_dot)).astype(jnp.bfloat16)
        query_grad = (
            jnp.einsum("hqk,khd->qhd", score_grad, key_heads, preferred_element_type=jnp.float32)
            * scaling
        )
        key_acc = (
            key_acc
            + jnp.einsum("hqk,qhd->khd", score_grad, query_part, preferred_element_type=jnp.float32)
            * scaling
        )
        value_acc = value_acc + jnp.einsum(
            "hqk,qhd->khd", prob_low, grad_part, preferred_element_type=jnp.float32
        )
        return ((key_acc, value_acc), query_grad.reshape(block_rows, model_width))

    empty_acc = jnp.zeros((length, H, HD), jnp.float32)
    (key_grad, value_grad), query_grads = lax.scan(
        one_block, (empty_acc, empty_acc), (query_blocks, segment_blocks, log_sums, grad_blocks)
    )
    return (
        query_grads.reshape(length, model_width),
        key_grad.reshape(length, model_width),
        value_grad.reshape(length, model_width),
    )


def on_device(
    tokens,
    segment_ids,
    keep_flag,
    cotangent,
    w_qkv,
    b_query,
    b_value,
    w_attn_out,
    b_attn_out,
    norm1_gain,
    norm1_bias,
    w_in,
    b_in,
    w_out,
    b_out,
    norm2_gain,
    norm2_bias,
):
    seq_count, length, model_width = tokens.shape
    block_rows = min(512, length)
    within = (
        lax.all_gather(w_qkv, "shard", axis=0, tiled=True),
        lax.all_gather(w_attn_out, "shard", axis=0, tiled=True),
        lax.all_gather(w_in, "shard", axis=0, tiled=True),
        lax.all_gather(w_out, "shard", axis=0, tiled=True),
        lax.all_gather(b_query, "shard", axis=0, tiled=True),
        lax.all_gather(b_value, "shard", axis=0, tiled=True),
        lax.all_gather(b_attn_out, "shard", axis=0, tiled=True),
        lax.all_gather(norm1_gain, "shard", axis=0, tiled=True),
        lax.all_gather(norm1_bias, "shard", axis=0, tiled=True),
        lax.all_gather(b_in, "shard", axis=0, tiled=True),
        lax.all_gather(b_out, "shard", axis=0, tiled=True),
        lax.all_gather(norm2_gain, "shard", axis=0, tiled=True),
        lax.all_gather(norm2_bias, "shard", axis=0, tiled=True),
    )
    full_qkv, full_attn, full_in, full_out = (
        lax.all_gather(within[0], "grp", axis=1, tiled=True),
        lax.all_gather(within[1], "grp", axis=1, tiled=True),
        lax.all_gather(within[2], "grp", axis=1, tiled=True),
        lax.all_gather(within[3], "grp", axis=1, tiled=True),
    )
    (
        bias_query,
        bias_value,
        bias_attn,
        gain_one,
        shift_one,
        bias_in,
        bias_out,
        gain_two,
        shift_two,
    ) = [piece.astype(jnp.float32) for piece in within[4:]]
    flat_rows = tokens.reshape(seq_count * length, model_width)
    mixed_qkv = jnp.dot(flat_rows, full_qkv, preferred_element_type=jnp.float32)
    queries = (mixed_qkv[:, :model_width] + bias_query).astype(jnp.bfloat16)
    key_rows = mixed_qkv[:, model_width : 2 * model_width].astype(jnp.bfloat16)
    value_rows = (mixed_qkv[:, 2 * model_width :] + bias_value).astype(jnp.bfloat16)
    query_seqs = queries.reshape(seq_count, length, model_width)
    key_seqs = key_rows.reshape(seq_count, length, model_width)
    value_seqs = value_rows.reshape(seq_count, length, model_width)

    def forward_sequence(pieces):
        return attend_forward(pieces[0], pieces[1], pieces[2], pieces[3], block_rows)

    contexts, log_sums = lax.map(forward_sequence, (query_seqs, key_seqs, value_seqs, segment_ids))
    contexts = contexts.reshape(seq_count * length, model_width)
    attended = jnp.dot(contexts, full_attn, preferred_element_type=jnp.float32) + bias_attn
    first_sum = flat_rows.astype(jnp.float32) + attended
    normed_one, norm_one_back = jax.vjp(norm_layer, first_sum, gain_one, shift_one)
    normed_low = normed_one.astype(jnp.bfloat16)
    hidden_pre = jnp.dot(normed_low, full_in, preferred_element_type=jnp.float32) + bias_in
    hidden, gelu_back = jax.vjp(gelu_exact, hidden_pre)
    hidden_low = hidden.astype(jnp.bfloat16)
    second_sum = normed_one + (
        jnp.dot(hidden_low, full_out, preferred_element_type=jnp.float32) + bias_out
    )
    result, norm_two_back = jax.vjp(norm_layer, second_sum, gain_two, shift_two)
    layer_out = result.astype(jnp.bfloat16).reshape(seq_count, length, model_width)
    again = (
        lax.all_gather(w_qkv, "shard", axis=0, tiled=True),
        lax.all_gather(w_attn_out, "shard", axis=0, tiled=True),
        lax.all_gather(w_in, "shard", axis=0, tiled=True),
        lax.all_gather(w_out, "shard", axis=0, tiled=True),
    )
    back_qkv, back_attn, back_in, back_out = (
        lax.all_gather(again[0], "grp", axis=1, tiled=True),
        lax.all_gather(again[1], "grp", axis=1, tiled=True),
        lax.all_gather(again[2], "grp", axis=1, tiled=True),
        lax.all_gather(again[3], "grp", axis=1, tiled=True),
    )
    masked_cot = cotangent.astype(jnp.float32).reshape(
        seq_count * length, model_width
    ) * keep_flag.reshape(seq_count * length, 1).astype(jnp.float32)
    second_grad, gain_two_grad, shift_two_grad = norm_two_back(masked_cot)
    bias_out_grad = jnp.sum(second_grad, 0)
    out_low = second_grad.astype(jnp.bfloat16)
    w_out_grad = contract_rows(hidden_low, out_low)
    hidden_grad = contract_cols(out_low, back_out)
    (pre_grad,) = gelu_back(hidden_grad)
    bias_in_grad = jnp.sum(pre_grad, 0)
    pre_low = pre_grad.astype(jnp.bfloat16)
    w_in_grad = contract_rows(normed_low, pre_low)
    normed_grad = second_grad + contract_cols(pre_low, back_in)
    first_grad, gain_one_grad, shift_one_grad = norm_one_back(normed_grad)
    bias_attn_grad = jnp.sum(first_grad, 0)
    attn_low = first_grad.astype(jnp.bfloat16)
    w_attn_grad = contract_rows(contexts, attn_low)
    context_grad = contract_cols(attn_low, back_attn).astype(jnp.bfloat16)

    def backward_sequence(pieces):
        return attend_backward(
            pieces[0], pieces[1], pieces[2], pieces[3], pieces[4], pieces[5], block_rows
        )

    query_grad, key_grad, value_grad = lax.map(
        backward_sequence,
        (
            query_seqs,
            key_seqs,
            value_seqs,
            segment_ids,
            log_sums,
            context_grad.reshape(seq_count, length, model_width),
        ),
    )
    query_grad = query_grad.reshape(seq_count * length, model_width)
    key_grad = key_grad.reshape(seq_count * length, model_width)
    value_grad = value_grad.reshape(seq_count * length, model_width)
    bias_query_grad = jnp.sum(query_grad, 0)
    bias_value_grad = jnp.sum(value_grad, 0)
    qkv_low = jnp.concatenate([query_grad, key_grad, value_grad], 1).astype(jnp.bfloat16)
    w_qkv_grad = contract_rows(flat_rows, qkv_low)
    input_grad = first_grad + contract_cols(qkv_low, back_qkv)
    reduced = (
        lax.psum_scatter(
            w_qkv_grad.astype(jnp.bfloat16), "shard", scatter_dimension=0, tiled=True
        ).astype(jnp.float32),
        lax.psum_scatter(
            bias_query_grad.astype(jnp.bfloat16), "shard", scatter_dimension=0, tiled=True
        ).astype(jnp.float32),
        lax.psum_scatter(
            bias_value_grad.astype(jnp.bfloat16), "shard", scatter_dimension=0, tiled=True
        ).astype(jnp.float32),
        lax.psum_scatter(
            w_attn_grad.astype(jnp.bfloat16), "shard", scatter_dimension=0, tiled=True
        ).astype(jnp.float32),
        lax.psum_scatter(
            bias_attn_grad.astype(jnp.bfloat16), "shard", scatter_dimension=0, tiled=True
        ).astype(jnp.float32),
        lax.psum_scatter(
            gain_one_grad.astype(jnp.bfloat16), "shard", scatter_dimension=0, tiled=True
        ).astype(jnp.float32),
        lax.psum_scatter(
            shift_one_grad.astype(jnp.bfloat16), "shard", scatter_dimension=0, tiled=True
        ).astype(jnp.float32),
        lax.psum_scatter(
            w_in_grad.astype(jnp.bfloat16), "shard", scatter_dimension=0, tiled=True
        ).astype(jnp.float32),
        lax.psum_scatter(
            bias_in_grad.astype(jnp.bfloat16), "shard", scatter_dimension=0, tiled=True
        ).astype(jnp.float32),
        lax.psum_scatter(
            w_out_grad.astype(jnp.bfloat16), "shard", scatter_dimension=0, tiled=True
        ).astype(jnp.float32),
        lax.psum_scatter(
            bias_out_grad.astype(jnp.bfloat16), "shard", scatter_dimension=0, tiled=True
        ).astype(jnp.float32),
        lax.psum_scatter(
            gain_two_grad.astype(jnp.bfloat16), "shard", scatter_dimension=0, tiled=True
        ).astype(jnp.float32),
        lax.psum_scatter(
            shift_two_grad.astype(jnp.bfloat16), "shard", scatter_dimension=0, tiled=True
        ).astype(jnp.float32),
    )
    summed = (
        lax.psum(reduced[0].astype(jnp.bfloat16), "grp").astype(jnp.float32),
        lax.psum(reduced[1].astype(jnp.bfloat16), "grp").astype(jnp.float32),
        lax.psum(reduced[2].astype(jnp.bfloat16), "grp").astype(jnp.float32),
        lax.psum(reduced[3].astype(jnp.bfloat16), "grp").astype(jnp.float32),
        lax.psum(reduced[4].astype(jnp.bfloat16), "grp").astype(jnp.float32),
        lax.psum(reduced[5].astype(jnp.bfloat16), "grp").astype(jnp.float32),
        lax.psum(reduced[6].astype(jnp.bfloat16), "grp").astype(jnp.float32),
        lax.psum(reduced[7].astype(jnp.bfloat16), "grp").astype(jnp.float32),
        lax.psum(reduced[8].astype(jnp.bfloat16), "grp").astype(jnp.float32),
        lax.psum(reduced[9].astype(jnp.bfloat16), "grp").astype(jnp.float32),
        lax.psum(reduced[10].astype(jnp.bfloat16), "grp").astype(jnp.float32),
        lax.psum(reduced[11].astype(jnp.bfloat16), "grp").astype(jnp.float32),
        lax.psum(reduced[12].astype(jnp.bfloat16), "grp").astype(jnp.float32),
    )
    return (
        layer_out,
        input_grad.reshape(seq_count, length, model_width),
        summed[0],
        summed[1],
        summed[2],
        summed[3],
        summed[4],
        summed[5],
        summed[6],
        summed[7],
        summed[8],
        summed[9],
        summed[10],
        summed[11],
        summed[12],
    )


NT = (((1,), (1,)), ((), ()))
NN = (((1,), (0,)), ((), ()))
TN = (((0,), (0,)), ((), ()))
LANES = 128
AXES = ("grp", "shard")


def mxu(left, right, dims):
    return lax.dot_general(left, right, dims, preferred_element_type=jnp.float32)


def cost(flops):
    return pl.CostEstimate(flops=2 * flops, bytes_accessed=0, transcendentals=0)


def params(megabytes=60):
    return pltpu.CompilerParams(vmem_limit_bytes=megabytes << 20)


def attention_forward_kernel(q_ref, k_ref, v_ref, seg_col, seg_row, out_ref, probs_ref, scale_ref, *, rows):
    length = q_ref.shape[0]
    first = lax.broadcasted_iota(jnp.int32, (1, LANES), 1) < HD
    keys = k_ref[...]
    values = v_ref[...]
    zero = jnp.zeros_like(keys)
    head_keys = (jnp.where(first, keys, zero), jnp.where(first, zero, keys))
    key_segments = seg_col[...]
    for block in range(length // rows):
        here = pl.ds(block * rows, rows)
        q = q_ref[here, :]
        allowed = key_segments == seg_row[:, here]
        outs, scales = [], []
        for head in range(2):
            scores = mxu(head_keys[head], q, NT)
            scores = jnp.where(allowed, scores, masked_score)
            powers = jnp.exp(scores - jnp.max(scores, 0, keepdims=True))
            scale = 1.0 / jnp.sum(powers, 0, keepdims=True)
            scales.append(jnp.transpose(jnp.broadcast_to(scale, (LANES, rows))))
            powers = powers.astype(jnp.bfloat16)
            probs_ref[head, :, here] = powers
            outs.append(mxu(powers, values, TN))
        scale = jnp.where(first, scales[0], scales[1])
        scale_ref[here, :] = scale
        out_ref[here, :] = (jnp.where(first, outs[0], outs[1]) * scale).astype(jnp.bfloat16)


def attention_forward(qkv, seg_col, seg_row, start, pairs, before=None):
    length, width = qkv.shape[0], qkv.shape[1] // 3
    total = width // LANES
    rows = min(512, length)
    more = () if before is None else before

    def pair(part):
        return pl.BlockSpec((length, LANES), lambda j: (0, part * total + start + j))

    def body(q_ref, k_ref, v_ref, seg_c, seg_r, *refs):
        attention_forward_kernel(q_ref, k_ref, v_ref, seg_c, seg_r, *refs[-3:], rows=rows)

    return pl.pallas_call(
        body,
        grid=(pairs,),
        in_specs=[
            pair(0),
            pair(1),
            pair(2),
            pl.BlockSpec((length, 1), lambda j: (0, 0)),
            pl.BlockSpec((1, length), lambda j: (0, 0)),
        ]
        + [pl.BlockSpec(memory_space=pl.ANY)] * len(more),
        out_specs=[
            pl.BlockSpec((length, LANES), lambda j: (0, start + j)),
            pl.BlockSpec((2, length, length), lambda j: (start + j, 0, 0)),
            pl.BlockSpec((length, LANES), lambda j: (0, start + j)),
        ],
        out_shape=[
            jax.ShapeDtypeStruct((length, width), jnp.bfloat16),
            jax.ShapeDtypeStruct((2 * total, length, length), jnp.bfloat16),
            jax.ShapeDtypeStruct((length, width), jnp.float32),
        ],
        input_output_aliases={} if before is None else {5: 0, 6: 1, 7: 2},
        compiler_params=params(60),
        cost_estimate=cost(16 * length * length * pairs * LANES),
        name="attn_fwd",
    )(qkv, qkv, qkv, seg_col, seg_row, *more)


def attention_backward_kernel(
    q_ref, k_ref, v_ref, o_ref, do_ref, probs_ref, scale_ref, grad_ref, sum_ref
):
    first = lax.broadcasted_iota(jnp.int32, (1, LANES), 1) < HD
    pick = (
        lax.broadcasted_iota(jnp.int32, (8, LANES), 0)
        == lax.broadcasted_iota(jnp.int32, (8, LANES), 1) // HD
    ).astype(jnp.float32)
    q = q_ref[...]
    scaled = do_ref[...].astype(jnp.float32) * scale_ref[...]
    do = scaled.astype(jnp.bfloat16)
    keys = k_ref[...]
    values = v_ref[...]
    zero = jnp.zeros_like(values)
    head_values = (jnp.where(first, values, zero), jnp.where(first, zero, values))
    dots = lax.dot_general(
        pick,
        scaled * o_ref[...].astype(jnp.float32),
        NT,
        precision=lax.Precision.HIGHEST,
        preferred_element_type=jnp.float32,
    )
    query_parts, key_parts, value_parts = [], [], []
    for head in range(2):
        probs = probs_ref[head]
        prob_grad = mxu(head_values[head], do, NT)
        score_grad = probs.astype(jnp.float32) * (prob_grad - dots[head : head + 1, :])
        score_grad = score_grad.astype(jnp.bfloat16)
        value_parts.append(mxu(probs, do, NN))
        key_parts.append(mxu(score_grad, q, NN))
        query_parts.append(mxu(score_grad, keys, TN))
    query_grad = jnp.where(first, *query_parts) * (1.0 / math.sqrt(HD))
    value_grad = jnp.where(first, *value_parts)
    grad_ref[0] = query_grad.astype(jnp.bfloat16)
    grad_ref[1] = jnp.where(first, *key_parts).astype(jnp.bfloat16)
    grad_ref[2] = value_grad.astype(jnp.bfloat16)
    sum_ref[0:1, :] = jnp.sum(query_grad, 0, keepdims=True)
    sum_ref[1:2, :] = jnp.sum(value_grad, 0, keepdims=True)


def attention_backward(qkv, out, out_grad, probs, scale, start, pairs, at, size, before=None):
    length, width = out.shape
    total = width // LANES
    more = () if before is None else before

    def pair(part):
        return pl.BlockSpec((length, LANES), lambda j: (0, part * total + start + j))

    def body(*refs):
        attention_backward_kernel(*refs[:7], *refs[-2:])

    return pl.pallas_call(
        body,
        grid=(pairs,),
        in_specs=[
            pair(0),
            pair(1),
            pair(2),
            pair(0),
            pair(0),
            pl.BlockSpec((2, length, length), lambda j: (start + j, 0, 0)),
            pair(0),
        ]
        + [pl.BlockSpec(memory_space=pl.ANY)] * len(more),
        out_specs=[
            pl.BlockSpec((3, length, LANES), lambda j: (0, 0, j + at)),
            pl.BlockSpec((2, LANES), lambda j: (0, j + at)),
        ],
        out_shape=[
            jax.ShapeDtypeStruct((3, length, size * LANES), jnp.bfloat16),
            jax.ShapeDtypeStruct((2, size * LANES), jnp.float32),
        ],
        input_output_aliases={} if before is None else {7: 0, 8: 1},
        compiler_params=params(60),
        cost_estimate=cost(32 * length * length * pairs * LANES),
        name="attn_bwd",
    )(qkv, qkv, qkv, out, out_grad, probs, scale, *more)


class Place:
    def __init__(self, groups, shards):
        self.groups = groups
        self.shards = shards
        self.chips = shards // 2
        self.grp = lax.axis_index("grp")
        self.shard = lax.axis_index("shard")
        self.core = self.shard % 2
        self.chip = self.shard // 2
        self.scalars = jnp.stack([self.core, self.chip, self.grp]).astype(jnp.int32)

    def permute(self, array, mask_of_core):
        pairs = [(i, i ^ mask_of_core[i % 2]) for i in range(self.groups * self.shards)]
        return lax.ppermute(array, AXES, pairs)

    def swap_core(self, array):
        return self.permute(array, (1, 1))

    def swap_grp(self, array, step):
        masks = (self.shards, 2 * self.shards)
        return self.permute(array, masks if step == 0 else masks[::-1])

    def swap_chip(self, array, step):
        masks = (2, 4)
        return self.permute(array, masks if step == 0 else masks[::-1])

    def slot_chip(self, slot):
        return self.chip ^ turn(slot, self.core)

    def slot_grp(self, slot):
        return self.grp ^ turn(slot, self.core)


def turn(slot, core):
    if isinstance(slot, int):
        return slot if slot in (0, 3) else jnp.where(core == 0, slot, 3 - slot)
    return jnp.where((core == 0) | (slot == 0) | (slot == 3), slot, 3 - slot)


def after(value, *others):
    return lax.optimization_barrier((value, *others))[0]


def meet(anchor, *flights):
    arrays = [f.flying for f in flights]
    _, *arrays = lax.optimization_barrier((anchor, *arrays))
    for f, array in zip(flights, arrays):
        f.flying = array


class Gather:
    def __init__(self, place, piece):
        self.place = place
        self.piece = piece
        self.held = [None] * 4
        self.crossed = [None] * 4

    def chips_near(self, *wait):
        self.piece = after(self.piece, *wait)
        self.flying = self.place.swap_chip(self.piece, 0)

    def chips_far(self):
        self.pair = jnp.stack([self.piece, self.flying])
        self.flying = self.place.swap_chip(self.pair, 1)
        return self.pair

    def join(self):
        self.held[0] = jnp.concatenate([self.pair, self.flying])
        return self.held[0]

    def near(self, *wait):
        self.held[0] = after(self.held[0], *wait)
        self.flying = (self.place.swap_grp(self.held[0], 0), self.place.swap_grp(self.held[0], 1))
        return self.held[0]

    def far(self, *wait):
        self.held[1:3] = self.flying
        first = after(self.held[1], *wait)
        self.flying = self.place.swap_grp(first, 1)

    def landed(self):
        self.held[3] = self.flying

    def cross(self, *which, wait=()):
        for n in which:
            self.crossed[n] = self.place.swap_core(after(self.held[n], *wait))

    def pieces(self):
        return self.held + self.crossed


class Window:
    def __init__(self, gather, start, cols):
        self.arrays = gather.pieces()
        self.start, self.cols = start, cols
        chips, rows, _ = self.arrays[0].shape
        self.chips, self.rows = chips, rows


def fetch(where, window, refs, whole, sem, by):
    rows, cols, chips = window.rows, window.cols, window.chips
    for slot in range(4):
        for side in range(2):
            core = where[0] ^ side
            ref = refs[4 * side + slot]
            distance = turn(slot, core)
            col = pl.multiple_of((where[2] ^ distance) * cols, LANES)
            for k in range(chips):
                row = ((where[1] ^ turn(k, core)) * 2 + core) * rows
                pltpu.make_async_copy(
                    ref.at[k, :, pl.ds(window.start, cols)],
                    whole.at[pl.ds(pl.multiple_of(row, rows), rows), pl.ds(col, cols)],
                    sem.at[distance if by == "grp" else 0],
                ).start()


def weight_call(place, kernel, window, inputs, in_specs, outs, out_specs, steps, by, name, flops, write=True):
    cols, groups = window.cols, place.groups
    pieces = window.arrays
    shape = (window.chips * 2 * window.rows, groups * cols)
    slots = {"grp": groups, "all": 1}[by]
    anywhere = pl.BlockSpec(memory_space=pl.ANY)

    def body(where, *refs):
        taken, refs = refs[: len(pieces)], refs[len(pieces) :]
        *refs, weight, sem, out_sem = refs
        if write:
            *refs, written = refs
        step = pl.program_id(0)

        @pl.when(step == 0)
        def _():
            fetch(where, window, taken, weight, sem, by)

        def ready():
            if by == "all":

                @pl.when(step == 0)
                def _():
                    pltpu.make_async_copy(weight, weight, sem.at[0]).wait()
                    if write:
                        pltpu.make_async_copy(weight, written, out_sem.at[0]).start()

            else:
                at = pl.ds(pl.multiple_of((where[2] ^ step) * cols, LANES), cols)
                view = weight.at[:, at]
                pltpu.make_async_copy(view, view, sem.at[step]).wait()
                pltpu.make_async_copy(view, written.at[:, at], out_sem.at[step]).start()

        kernel(where, ready, weight, *refs)

        @pl.when(step == (steps - 1 if write else -1))
        def _():
            for slot in range(slots if write else 0):
                width = shape[1] // slots
                view = weight.at[:, pl.ds(slot * width, width)]
                pltpu.make_async_copy(view, view, out_sem.at[slot]).wait()

    total = sum(math.prod(x.shape) * x.dtype.itemsize for x in list(inputs) + list(outs))
    return pl.pallas_call(
        body,
        grid_spec=pltpu.PrefetchScalarGridSpec(
            num_scalar_prefetch=1,
            grid=(steps,),
            in_specs=[anywhere] * len(pieces) + in_specs,
            out_specs=out_specs + [anywhere] * write,
            scratch_shapes=[
                pltpu.VMEM(shape, jnp.bfloat16),
                pltpu.SemaphoreType.DMA((slots,)),
                pltpu.SemaphoreType.DMA((slots,)),
            ],
        ),
        out_shape=outs + [shaped(shape, jnp.bfloat16)] * write,
        compiler_params=params(60),
        cost_estimate=cost(flops),
        name=name,
    )(place.scalars, *pieces, *inputs)


def plain_call(kernel, inputs, in_specs, outs, out_specs, steps, name, flops):
    total = sum(math.prod(x.shape) * x.dtype.itemsize for x in list(inputs) + list(outs))
    return pl.pallas_call(
        kernel,
        grid=(steps,),
        in_specs=in_specs,
        out_specs=out_specs,
        out_shape=outs,
        compiler_params=params(60),
        cost_estimate=cost(flops),
        name=name,
    )(*inputs)


TILE = 256


def row_tiles(width):
    return pl.BlockSpec((TILE, width), lambda i, *s: (i, 0))


def fixed(*shape):
    return pl.BlockSpec(shape, lambda i, *s: (0,) * len(shape))


def whole_once(shape):
    return pl.BlockSpec(shape, lambda i: (0,) * len(shape), pipeline_mode=pl.Buffered(1))


def shaped(shape, dtype):
    return jax.ShapeDtypeStruct(shape, dtype)


B_QUERY, B_VALUE, B_ATTN, GAIN_ONE, SHIFT_ONE, B_OUT, GAIN_TWO, SHIFT_TWO, B_IN = range(9)


def row(ref, n):
    return ref[n : n + 1, :]


class Vectors:
    def __init__(self, place, vectors):
        lines = [v.reshape(-1, LANES) for v in vectors]
        blank = jnp.zeros((-sum(x.shape[0] for x in lines) % 16, LANES), jnp.bfloat16)
        self.own = jnp.concatenate([*lines, blank])
        self.place = place
        self.flying = place.swap_core(self.own)

    def chips_near(self):
        self.own = jnp.stack([self.own, self.flying])
        self.flying = self.place.swap_chip(self.own, 0)

    def chips_far(self):
        self.own = jnp.stack([self.own, self.flying])
        self.flying = self.place.swap_chip(self.own, 1)

    def landed(self):
        self.slots = jnp.concatenate([self.own, self.flying])

    def unpack(self, seg_row, keep_row):
        place = self.place
        length = seg_row.shape[1]
        slots, sides, rows, lanes = self.slots.shape
        shards = place.shards

        def kernel(where, in_ref, seg_ref, keep_ref, *outs):
            rows_ref, inner_ref, qkv_ref, seg_col_ref, keep_col_ref = outs
            for line_ref, col_ref in ((seg_ref, seg_col_ref), (keep_ref, keep_col_ref)):
                line = jnp.broadcast_to(line_ref[...].astype(jnp.float32), (8, length))
                col_ref[...] = line.T[:, 0:1].astype(col_ref.dtype)
            width = shards * lanes
            qkv_ref[...] = jnp.zeros_like(qkv_ref)
            for slot in range(slots):
                for side in range(sides):
                    core = where[0] ^ side
                    shard = (where[1] ^ turn(slot, where[0])) * 2 + core
                    part = in_ref[slot, side].astype(jnp.float32)
                    at = pl.multiple_of(shard * lanes, lanes)
                    rows_ref[:, pl.ds(at, lanes)] = part
                    qkv_ref[:, pl.ds(at, lanes)] = part[B_QUERY : B_QUERY + 1]
                    qkv_ref[:, pl.ds(2 * width + at, lanes)] = part[B_VALUE : B_VALUE + 1]
                    for n in range(4):
                        start = pl.multiple_of((shard * 4 + n) * lanes, lanes)
                        inner_ref[:, pl.ds(start, lanes)] = part[B_IN + n : B_IN + n + 1]

        in_vmem = pl.BlockSpec(memory_space=pltpu.VMEM)
        return pl.pallas_call(
            kernel,
            in_specs=[pl.BlockSpec(memory_space=pltpu.SMEM)] + [in_vmem] * 3,
            out_specs=[in_vmem] * 5,
            out_shape=[
                shaped((rows, shards * lanes), jnp.float32),
                shaped((1, 4 * shards * lanes), jnp.float32),
                shaped((1, 3 * shards * lanes), jnp.float32),
                shaped((length, 1), jnp.int32),
                shaped((length, 1), jnp.float32),
            ],
            name="vectors",
        )(place.scalars, self.slots, seg_row, keep_row)


def project_qkv(place, rows, window, bias, scale):
    length, width = rows.shape
    cols = window.cols

    def kernel(where, ready, weight, x_ref, bias_ref, scale_ref, out_ref):
        ready()
        at = pl.ds(pl.multiple_of((where[2] ^ pl.program_id(0)) * cols, LANES), cols)
        size = min(512, length)
        for tile in range(length // size):
            here = pl.ds(tile * size, size)
            mixed = mxu(x_ref[here, :], weight[:, at], NN) + bias_ref[:, at]
            mixed = mixed.astype(jnp.bfloat16).astype(jnp.float32) * scale_ref[:, at]
            out_ref[here, :] = mixed.astype(jnp.bfloat16)

    total = cols * place.groups
    return weight_call(
        place,
        kernel,
        window,
        (rows, bias, scale),
        [fixed(length, width), fixed(1, total), fixed(1, total)],
        [shaped((length, total), jnp.bfloat16)],
        [pl.BlockSpec((length, cols), lambda i, s: (0, i ^ s[2]))],
        place.groups,
        "grp",
        "qkv",
        2 * length * width * total,
    )


def norm_parts(rows):
    centered = rows - jnp.mean(rows, -1, keepdims=True)
    scale = lax.rsqrt(jnp.mean(centered * centered, -1, keepdims=True) + epsilon)
    return centered * scale, scale


def norm_back(grad, normed, scale):
    return scale * (
        grad
        - jnp.mean(grad, -1, keepdims=True)
        - normed * jnp.mean(grad * normed, -1, keepdims=True)
    )


def add_rows(sum_ref, *terms):
    @pl.when(pl.program_id(0) == 0)
    def _():
        sum_ref[...] = jnp.zeros_like(sum_ref)

    for n, term in enumerate(terms):
        sum_ref[n : n + 1, :] += jnp.sum(term, 0, keepdims=True)


def project_out(place, contexts, window, rows, vectors):
    length, width = rows.shape

    def kernel(where, ready, weight, c_ref, x_ref, v_ref, n_ref, r_ref, low_ref):
        ready()
        first_sum = mxu(c_ref[...], weight[...], NN) + row(v_ref, B_ATTN)
        first_sum = first_sum + x_ref[...].astype(jnp.float32)
        normed, scale = norm_parts(first_sum)
        n_ref[...] = normed
        r_ref[...] = jnp.broadcast_to(scale, r_ref.shape)
        low_ref[...] = (normed * row(v_ref, GAIN_ONE) + row(v_ref, SHIFT_ONE)).astype(jnp.bfloat16)

    return weight_call(
        place,
        kernel,
        window,
        (contexts, rows, vectors),
        [row_tiles(width), row_tiles(width), fixed(*vectors.shape)],
        [
            shaped((length, width), jnp.float32),
            shaped((length, LANES), jnp.float32),
            shaped((length, width), jnp.bfloat16),
        ],
        [row_tiles(width), row_tiles(LANES), row_tiles(width)],
        length // TILE,
        "all",
        "attn_out",
        2 * length * width * width,
    )


def feed_in(place, normed_low, window, bias):
    length, width = normed_low.shape
    cols = window.cols

    def kernel(where, ready, weight, x_ref, bias_ref, hid_ref, slope_ref):
        ready()
        at = pl.ds(pl.multiple_of((where[2] ^ pl.program_id(0)) * cols, LANES), cols)
        size = min(512, length)
        for tile in range(length // size):
            here = pl.ds(tile * size, size)
            pre = mxu(x_ref[here, :], weight[:, at], NN) + bias_ref[:, at]
            share = 0.5 + 0.5 * lax.erf(pre * (1.0 / math.sqrt(2.0)))
            bell = jnp.exp(-0.5 * pre * pre) * (1.0 / math.sqrt(2.0 * math.pi))
            hid_ref[here, :] = (pre * share).astype(jnp.bfloat16)
            slope_ref[here, :] = (share + pre * bell).astype(jnp.bfloat16)

    total = cols * place.groups
    block = pl.BlockSpec((length, cols), lambda i, s: (0, i ^ s[2]))
    return weight_call(
        place,
        kernel,
        window,
        (normed_low, bias),
        [fixed(length, width), fixed(1, total)],
        [shaped((length, total), jnp.bfloat16)] * 2,
        [block, block],
        place.groups,
        "grp",
        "feed_in",
        2 * length * width * total,
    )


def feed_out(place, hidden, window, normed, cot, keep, vectors, slope):
    length, inner = hidden.shape
    width = normed.shape[1]

    def kernel(where, ready, weight, h_ref, n_ref, cot_ref, keep_ref, v_ref, slope_ref, *outs):
        out_ref, grad_ref, low_ref, sum_ref, pre_ref, inner_ref = outs
        ready()
        fed = mxu(h_ref[...], weight[...], NN)
        normed_one = n_ref[...] * row(v_ref, GAIN_ONE) + row(v_ref, SHIFT_ONE)
        second_sum = normed_one + (fed + row(v_ref, B_OUT))
        second, scale = norm_parts(second_sum)
        out_ref[...] = (second * row(v_ref, GAIN_TWO) + row(v_ref, SHIFT_TWO)).astype(jnp.bfloat16)
        masked = cot_ref[...].astype(jnp.float32) * keep_ref[...]
        grad = norm_back(masked * row(v_ref, GAIN_TWO), second, scale)
        grad_ref[...] = grad
        low = grad.astype(jnp.bfloat16)
        low_ref[...] = low
        add_rows(sum_ref, masked * second, masked, grad)

        @pl.when(pl.program_id(0) == 0)
        def _():
            inner_ref[...] = jnp.zeros_like(inner_ref)

        size = min(1024, inner)
        for n in range(inner // size):
            at = slice(n * size, (n + 1) * size)
            pre = mxu(low, weight[at, :], NT) * slope_ref[:, at].astype(jnp.float32)
            pre_ref[:, at] = pre.astype(jnp.bfloat16)
            inner_ref[:, at] += jnp.sum(pre, 0, keepdims=True)

    return weight_call(
        place,
        kernel,
        window,
        (hidden, normed, cot, keep, vectors, slope),
        [
            row_tiles(inner),
            row_tiles(width),
            row_tiles(width),
            row_tiles(1),
            fixed(*vectors.shape),
            row_tiles(inner),
        ],
        [
            shaped((length, width), jnp.bfloat16),
            shaped((length, width), jnp.float32),
            shaped((length, width), jnp.bfloat16),
            shaped((8, width), jnp.float32),
            shaped((length, inner), jnp.bfloat16),
            shaped((1, inner), jnp.float32),
        ],
        [
            row_tiles(width),
            row_tiles(width),
            row_tiles(width),
            fixed(8, width),
            row_tiles(inner),
            fixed(1, inner),
        ],
        length // TILE,
        "all",
        "feed_out",
        4 * length * width * inner,
        write=False,
    )


def feed_in_back(pre_low, weight, second_grad, normed, scale, vectors, attn_weight):
    length, inner = pre_low.shape
    width = normed.shape[1]

    def kernel(p_ref, w_ref, g_ref, n_ref, r_ref, v_ref, a_ref, first_ref, low_ref, ctx_ref, sum_ref):
        grad = g_ref[...] + mxu(p_ref[...], w_ref[...], NT)
        first = norm_back(grad * row(v_ref, GAIN_ONE), n_ref[...], r_ref[:, :1])
        low = first.astype(jnp.bfloat16)
        first_ref[...] = first
        low_ref[...] = low
        ctx_ref[...] = mxu(low, a_ref[...], NT).astype(jnp.bfloat16)
        add_rows(sum_ref, grad * n_ref[...], grad, first)

    return plain_call(
        kernel,
        (pre_low, weight, second_grad, normed, scale, vectors, attn_weight),
        [
            row_tiles(inner),
            whole_once(weight.shape),
            row_tiles(width),
            row_tiles(width),
            row_tiles(LANES),
            fixed(*vectors.shape),
            whole_once(attn_weight.shape),
        ],
        [
            shaped((length, width), jnp.float32),
            shaped((length, width), jnp.bfloat16),
            shaped((length, width), jnp.bfloat16),
            shaped((8, width), jnp.float32),
        ],
        [row_tiles(width), row_tiles(width), row_tiles(width), fixed(8, width)],
        length // TILE,
        "feed_in_back",
        2 * length * width * (inner + width),
    )


def project_qkv_back(grads, weight, first_grad, start, tiles, before=None):
    length, width = first_grad.shape
    part = width // len(grads)

    def kernel(w_ref, *refs):
        grad_refs, first_ref, out_ref = refs[: len(grads)], refs[len(grads)], refs[-1]
        total = first_ref[...]
        for n in range(3):
            for m, grad_ref in enumerate(grad_refs):
                at = n * width + m * part
                total = total + mxu(grad_ref[n], w_ref[:, at : at + part], NT)
        out_ref[...] = total

    tile = pl.BlockSpec((TILE, width), lambda i: (start + i, 0))
    more = () if before is None else (before,)
    return pl.pallas_call(
        kernel,
        grid=(tiles,),
        in_specs=[whole_once(weight.shape)]
        + [pl.BlockSpec((3, TILE, part), lambda i: (0, start + i, 0))] * len(grads)
        + [tile]
        + [pl.BlockSpec(memory_space=pl.ANY)] * len(more),
        out_specs=tile,
        out_shape=shaped((length, width), jnp.float32),
        input_output_aliases={} if before is None else {len(grads) + 2: 0},
        compiler_params=params(60),
        cost_estimate=cost(6 * tiles * TILE * width * width),
        name="qkv_back",
    )(weight, *grads, first_grad, *more)


ORDER = (1, 3, 0, 2)


def ordered_slot(j):
    return jnp.where(j < 2, 2 * j + 1, 2 * j - 4)


def weight_grad_kernel(where, left_ref, right_ref, own, sent, kept, *, rows, groups, split):
    core = where[0]
    chips = left_ref.shape[1] // (2 * rows)

    @pl.when(pl.program_id(1) == 0)
    def _():
        keep_rows(core, left_ref, rows, kept)

    if split:
        size = min(512, right_ref.shape[1])
        for ref, side in ((sent, 1), (own, 0)):
            for n in range(right_ref.shape[1] // size):
                at = slice(n * size, (n + 1) * size)
                part = mxu(kept[side], right_ref[:, at], NN).astype(jnp.bfloat16)
                ref[0, :, :, at] = part.reshape(chips, rows, size)
    else:
        cols = right_ref.shape[1] // groups
        for ref, side in ((sent, 1), (own, 0)):
            for pos, slot in enumerate(ORDER):
                start = pl.multiple_of((where[2] ^ turn(slot, core ^ side)) * cols, LANES)
                part = mxu(kept[side], right_ref[:, pl.ds(start, cols)], NN)
                ref[pos] = part.astype(jnp.bfloat16).reshape(chips, rows, cols)


def keep_rows(core, left_ref, rows, kept):
    chips = left_ref.shape[1] // (2 * rows)
    for side in range(2):
        chosen = []
        for k in range(chips):
            even = left_ref[:, 2 * k * rows : (2 * k + 1) * rows]
            odd = left_ref[:, (2 * k + 1) * rows : (2 * k + 2) * rows]
            chosen.append(jnp.where(core == side, even, odd))
        left = chosen[0] if chips == 1 else jnp.concatenate(chosen, 1)
        kept[side] = left.T


def turned_rows(place, left):
    tokens, height = left.shape

    def kernel(where, left_ref, out_ref):
        keep_rows(where[0], left_ref, height // place.shards, out_ref)

    in_vmem = pl.BlockSpec(memory_space=pltpu.VMEM)
    return pl.pallas_call(
        kernel,
        in_specs=[pl.BlockSpec(memory_space=pltpu.SMEM), in_vmem],
        out_specs=in_vmem,
        out_shape=shaped((2, height // 2, tokens), jnp.bfloat16),
        compiler_params=params(40),
        name="turned_rows",
    )(place.scalars, left)


def attention_grads_kernel(where, *refs, rows, groups, extra):
    turned, right_ref, *refs = refs
    *more, own, sent, kept = refs
    core, grp = where[0], where[2]
    chips = turned.shape[1] // rows
    step = pl.program_id(0)

    def scatter(lefts, right, at, cols):
        for ref, side in ((sent, 1), (own, 0)):
            part = mxu(lefts[side], right, NN).astype(jnp.bfloat16)
            for g in range(groups):
                pos = position(grp ^ g, core ^ side)
                block = part[:, g * cols : (g + 1) * cols].reshape(chips, rows, cols)
                ref[pos, :, 0:rows, pl.ds(at, cols)] = block

    skip = 0
    if not extra:
        other_left, other_right = more
        skip = other_right.shape[1] // groups

        @pl.when(step == 0)
        def _():
            keep_rows(core, other_left, rows, kept)
            scatter(kept, other_right[...], 0, skip)

    cols = right_ref.shape[2] // groups
    scatter(turned, right_ref[0], pl.multiple_of(skip + step * cols, LANES), cols)

    if extra:

        @pl.when(step == 2)
        def _():
            blank = jnp.zeros((extra, own.shape[3]), jnp.bfloat16)
            for ref, side in ((sent, 1), (own, 0)):
                for k in range(chips):
                    lines = vector_sums(2 * k + (core ^ side), *more)
                    for g in range(groups):
                        pos = position(grp ^ g, core ^ side)
                        ref[pos, k, rows : rows + extra, :] = blank
                        for n in range(3):
                            ref[pos, k, rows : rows + 1, n * LANES : (n + 1) * LANES] = lines[
                                3 * g + n
                            ].astype(jnp.bfloat16)


def vector_sums(shard, a_ref, b_ref, one_ref, two_ref, inner_ref):
    half = a_ref.shape[1]
    start = shard * LANES

    def part(ref, start):
        return ref[:, pl.ds(pl.multiple_of(start, LANES), LANES)]

    late = jnp.where(
        start < half,
        part(a_ref, jnp.minimum(start, half - LANES)),
        part(b_ref, jnp.maximum(start - half, 0)),
    )
    one, two = part(one_ref, start), part(two_ref, start)
    lines = [None] * 12
    lines[B_QUERY], lines[B_VALUE] = late[0:1], late[1:2]
    lines[GAIN_ONE], lines[SHIFT_ONE], lines[B_ATTN] = one[0:1], one[1:2], one[2:3]
    lines[GAIN_TWO], lines[SHIFT_TWO], lines[B_OUT] = two[0:1], two[1:2], two[2:3]
    for n in range(4):
        lines[B_IN + n] = part(inner_ref, (4 * shard + n) * LANES)
    return lines


def position(distance, core):
    slot = turn(distance, core)
    return jnp.where(slot == 0, 2, jnp.where(slot == 1, 0, jnp.where(slot == 3, 1, 3)))


def attention_grads(place, turned, right, more, name):
    height, tokens = 2 * turned.shape[1], turned.shape[2]
    groups, chips = place.groups, place.chips
    rows = height // place.shards
    extra = 16 if len(more) > 2 else 0
    size = right.shape[2]
    cols = 3 * size // groups + (0 if extra else more[1].shape[1] // groups)
    shape = (groups, chips, rows + extra, cols)
    once = [
        pl.BlockSpec(x.shape, lambda i, s: (0, 0), pipeline_mode=pl.Buffered(1)) for x in more
    ]
    return pl.pallas_call(
        functools.partial(attention_grads_kernel, rows=rows, groups=groups, extra=extra),
        grid_spec=pltpu.PrefetchScalarGridSpec(
            num_scalar_prefetch=1,
            grid=(3,),
            in_specs=[
                pl.BlockSpec(turned.shape, lambda i, s: (0, 0, 0), pipeline_mode=pl.Buffered(1)),
                pl.BlockSpec((1, tokens, size), lambda i, s: (i, 0, 0)),
            ]
            + once,
            out_specs=[pl.BlockSpec(shape, lambda i, s: (0, 0, 0, 0))] * 2,
            scratch_shapes=[pltpu.VMEM((8, LANES) if extra else turned.shape, jnp.bfloat16)],
        ),
        out_shape=[shaped(shape, jnp.bfloat16)] * 2,
        compiler_params=params(60),
        cost_estimate=cost(2 * tokens * height * cols * groups),
        name="wgrad_" + name,
    )(place.scalars, turned, right, *more)


def weight_grad(place, left, right, split, name):
    tokens, height = left.shape
    groups, chips = place.groups, place.chips
    rows = height // place.shards
    step_chips = chips if split else max(1, 1024 // (2 * rows))
    cols = right.shape[1] // groups
    if split:
        grid = (1, groups)
        block = lambda i, j, s: (0, s[2] ^ turn(ordered_slot(j), s[0]))
        right_spec = pl.BlockSpec((tokens, cols), block)
        one = (1, chips, rows, cols)
        other = lambda j: jnp.where(j == 0, 3, jnp.where(j == 3, 0, j))
        out_specs = [
            pl.BlockSpec(one, lambda i, j, s: (j, 0, 0, 0)),
            pl.BlockSpec(one, lambda i, j, s: (other(j), 0, 0, 0)),
        ]
    else:
        grid = (chips // step_chips, 1)
        right_spec = pl.BlockSpec(right.shape, lambda i, j, s: (0, 0))
        out_specs = [
            pl.BlockSpec((groups, step_chips, rows, cols), lambda i, j, s: (0, i, 0, 0))
        ] * 2
    return pl.pallas_call(
        functools.partial(weight_grad_kernel, rows=rows, groups=groups, split=split),
        grid_spec=pltpu.PrefetchScalarGridSpec(
            num_scalar_prefetch=1,
            grid=grid,
            in_specs=[
                pl.BlockSpec((tokens, step_chips * 2 * rows), lambda i, j, s: (0, i)),
                right_spec,
            ],
            out_specs=out_specs,
            scratch_shapes=[pltpu.VMEM((2, step_chips * rows, tokens), jnp.bfloat16)],
        ),
        out_shape=[shaped((groups, chips, rows, cols), jnp.bfloat16)] * 2,
        compiler_params=params(60),
        cost_estimate=cost(2 * tokens * height * cols * groups),
        name="wgrad_" + name,
    )(place.scalars, left, right)


def add(*terms):
    total = terms[0].astype(jnp.float32)
    for term in terms[1:]:
        total = total + term.astype(jnp.float32)
    return total.astype(jnp.bfloat16)


class Reduction:
    def __init__(self, place, made):
        self.place = place
        self.made, sent = made
        self.flying = place.swap_core(sent)

    def near(self):
        self.core = self.flying
        leave = add(self.made[:2], self.core[:2])
        self.flying = self.place.swap_grp(leave, 0)
        return leave

    def middle(self):
        self.first = self.flying
        second = add(self.made[3], self.core[3], self.first[1])
        self.flying = self.place.swap_grp(second, 1)
        return second

    def column(self):
        mine = add(self.made[2], self.core[2], self.first[0], self.flying)
        return mine, lambda chip: lax.dynamic_index_in_dim(mine, chip, 0, False)

    def along(self):
        place = self.place
        mine, at = self.column()
        self.mine = [at(place.slot_chip(slot)) for slot in range(4)]
        both = jnp.stack([self.mine[1], self.mine[3]])
        self.flying = place.swap_chip(both, 0)
        return both

    def along_far(self):
        self.first = self.flying
        second = add(self.mine[2], self.first[1])
        self.flying = self.place.swap_chip(second, 1)
        return second

    def share(self):
        return add(self.mine[0], self.first[0], self.flying)

    def along_direct(self):
        place = self.place
        mine, at = self.column()
        self.mine = at(place.chip)
        self.flying = tuple(
            place.permute(at(place.chip ^ k), (2 * k, 2 * k)) for k in range(place.chips - 1, 0, -1)
        )
        return mine

    def share_direct(self):
        return add(self.mine, *self.flying)


class Replication:
    def __init__(self, place, share, direct=False):
        self.place = place
        self.blocks = [share] + [None] * 3
        if direct:
            size = place.shards
            for mask in (3, 1, 2):
                self.blocks[mask] = place.permute(share, (mask * size, mask * size))
        else:
            self.flying = place.swap_grp(share, 0)

    def far(self):
        pair = jnp.stack([self.blocks[0], self.flying])
        self.blocks[1] = self.flying
        self.flying = self.place.swap_grp(pair, 1)
        return pair

    def landed(self):
        if self.blocks[2] is None:
            self.blocks[2:] = [self.flying[0], self.flying[1]]
        return self.blocks


def order_feed_forward(place, blocks, rows_in):
    groups = place.groups
    height, cols = blocks[0].shape
    rows_out = height - groups * rows_in

    def kernel(where, *refs):
        *blocks, out_ref, in_ref = refs
        for slot, ref in enumerate(blocks):
            g = where[2] ^ turn(slot, where[0])
            at = pl.multiple_of(g * cols, LANES)
            out_ref[:, pl.ds(at, cols)] = ref[0:rows_out, :].astype(jnp.float32)
            for n in range(groups):
                at = pl.multiple_of((g * groups + n) * cols, LANES)
                part = ref[rows_out + n * rows_in : rows_out + (n + 1) * rows_in, :]
                in_ref[:, pl.ds(at, cols)] = part.astype(jnp.float32)

    in_vmem = pl.BlockSpec(memory_space=pltpu.VMEM)
    return pl.pallas_call(
        kernel,
        in_specs=[pl.BlockSpec(memory_space=pltpu.SMEM)] + [in_vmem] * groups,
        out_specs=[in_vmem] * 2,
        out_shape=[
            shaped((rows_out, groups * cols), jnp.float32),
            shaped((rows_in, groups * groups * cols), jnp.float32),
        ],
        compiler_params=params(40),
        cost_estimate=cost(height * cols * 1024),
        name="order_feed_forward",
    )(place.scalars, *blocks)


def order_attention(place, blocks_a, blocks_b, rows):
    groups = place.groups
    size = blocks_b[0].shape[1] // 3
    skip = blocks_a[0].shape[1] - 3 * size
    width = groups * skip

    def kernel(where, *refs):
        *blocks, attn_ref, qkv_ref, small_ref = refs
        for n in range(groups):
            ref = blocks[n]
            g = where[2] ^ turn(n, where[0])
            attn_ref[:, pl.ds(pl.multiple_of(g * skip, LANES), skip)] = ref[:, 0:skip].astype(
                jnp.float32
            )
            for part in range(3):
                at = pl.multiple_of(part * width + g * size, LANES)
                block = ref[:, skip + part * size : skip + (part + 1) * size]
                qkv_ref[:, pl.ds(at, size)] = block.astype(jnp.float32)
        for n in range(groups):
            ref = blocks[groups + n]
            g = where[2] ^ n
            lines = []
            for part in range(3):
                at = pl.multiple_of(part * width + width // 2 + g * size, LANES)
                here = slice(part * size, (part + 1) * size)
                qkv_ref[:, pl.ds(at, size)] = ref[0:rows, here].astype(jnp.float32)
                lines.append(ref[rows : rows + 16, here].astype(jnp.float32)[0:1])
            lines.append(jnp.zeros((5, size), jnp.float32))
            small_ref[pl.ds(pl.multiple_of(g * 8, 8), 8), :] = jnp.concatenate(lines)

    in_vmem = pl.BlockSpec(memory_space=pltpu.VMEM)
    return pl.pallas_call(
        kernel,
        in_specs=[pl.BlockSpec(memory_space=pltpu.SMEM)] + [in_vmem] * (2 * groups),
        out_specs=[in_vmem] * 3,
        out_shape=[
            shaped((rows, width), jnp.float32),
            shaped((rows, 3 * width), jnp.float32),
            shaped((8 * groups, size), jnp.float32),
        ],
        compiler_params=params(40),
        name="order_attention",
    )(place.scalars, *blocks_a, *blocks_b)


def on_device_permutes(
    tokens,
    segment_ids,
    keep_flag,
    cotangent,
    w_qkv,
    b_query,
    b_value,
    w_attn_out,
    b_attn_out,
    norm1_gain,
    norm1_bias,
    w_in,
    b_in,
    w_out,
    b_out,
    norm2_gain,
    norm2_bias,
    *,
    groups,
    shards,
):
    place = Place(groups, shards)
    _, length, width = tokens.shape
    rows = tokens[0]
    seg_row = segment_ids.reshape(1, length)
    pairs = width // LANES

    c1 = Gather(place, w_qkv)
    c2 = Gather(place, jnp.concatenate([w_in, w_attn_out], 1))
    c3 = Gather(place, w_out)
    c1.chips_near()
    small = Vectors(
        place,
        (b_query, b_value, b_attn_out, norm1_gain, norm1_bias, b_out, norm2_gain, norm2_bias, b_in),
    )
    meet(rows, c1, small)
    pair = c1.chips_far()
    small.chips_near()
    meet(pair, c1, small)
    joined = c1.join()
    c1.near()
    small.chips_far()
    c2.chips_near(joined)
    meet(joined, c2, small)
    small.landed()
    pair = c2.chips_far()
    vectors, bias_in, qkv_bias, seg_col, keep = small.unpack(
        seg_row, keep_flag.reshape(1, length)
    )
    c1.flying = lax.optimization_barrier(c1.flying)
    turned = turned_rows(place, after(rows, vectors))
    c1.far(pair, vectors)
    c1.cross(0, 1, 2)
    joined = c2.join()
    meet((joined, turned), c1)
    c1.landed()
    c2.near(c1.held[3])
    c1.cross(3)
    c3.chips_near(c1.held[3])
    blank = jnp.ones((1, width), jnp.float32)
    qkv_scale = jnp.concatenate([blank / math.sqrt(HD), blank, blank], 1)

    mixed, full_qkv = project_qkv(place, rows, Window(c1, 0, w_qkv.shape[1]), qkv_bias, qkv_scale)
    meet(mixed, c3)
    pair = c3.chips_far()
    c2.cross(0, wait=(mixed,))
    first, second = pairs * 3 // 8, pairs * 3 // 4
    forward = attention_forward(after(mixed, pair), seg_col, seg_row, 0, first)
    meet(forward[0], c2, c3)
    c2.far()
    joined = c3.join()
    c3.near()
    c2.cross(1, 2)
    forward = attention_forward(
        after(mixed, joined), seg_col, seg_row, first, second - first, forward
    )
    meet(forward[0], c2)
    c2.landed()
    c2.cross(3)
    contexts, probs, probs_scale = attention_forward(
        after(mixed, c2.held[3]), seg_col, seg_row, second, pairs - second, forward
    )
    normed, scale_one, normed_low, full_attn = project_out(
        place, contexts, Window(c2, w_in.shape[1], w_attn_out.shape[1]), rows, vectors
    )
    meet(normed_low, c3)
    c3.far()
    c3.cross(0, 1, 2)
    hidden, slope, full_in = feed_in(
        place, after(normed_low, c3.held[1]), Window(c2, 0, w_in.shape[1]), bias_in
    )
    meet(hidden, c3)
    c3.landed()
    c3.cross(3)
    layer_out, second_grad, out_low, second_sums, pre_low, bias_in_grad = feed_out(
        place, hidden, Window(c3, 0, w_out.shape[1]), normed, cotangent[0], keep, vectors, slope
    )

    r_out = Reduction(place, weight_grad(place, hidden, out_low, False, "out"))
    r_in = Reduction(place, weight_grad(place, after(normed_low, r_out.made), pre_low, True, "in"))
    meet(r_in.made, r_out)
    step = r_out.near()
    first_grad, attn_low, context_grad, first_sums = feed_in_back(
        after(pre_low, r_in.made, step), full_in, second_grad, normed, scale_one, vectors, full_attn
    )
    meet(attn_low, r_in)
    step = r_in.near()
    half, quarter = pairs // 2, pairs // 4

    def back(wait, start, count, at, before=None):
        return attention_backward(
            mixed,
            contexts,
            after(context_grad, *wait),
            probs,
            probs_scale,
            start,
            count,
            at,
            half,
            before,
        )

    low_a, late_a = back((step,), 0, half, 0)
    meet(late_a, r_out, r_in)
    steps = (r_out.middle(), r_in.middle())
    r_a = Reduction(
        place, attention_grads(place, after(turned, *steps), low_a, (contexts, attn_low), "a")
    )
    meet(r_a.made, r_out)
    step = r_out.along()
    part = back((r_a.made, step), half, quarter, 0)
    meet(part[1], r_out, r_in, r_a)
    steps = (r_out.along_far(), r_in.along(), r_a.near())
    low_b, late_b = back(steps, half + quarter, quarter, quarter, part)
    meet(late_b, r_out, r_in, r_a)
    sums = (late_a, late_b, first_sums, second_sums, bias_in_grad)
    share_out = r_out.share()
    steps = (r_in.along_far(), r_a.middle(), share_out)
    r_b = Reduction(place, attention_grads(place, after(turned, *steps), low_b, sums, "b"))
    meet(r_b.made, r_in, r_a)
    share_in = r_in.share()
    inner = share_in.shape[1] // groups
    joined = jnp.concatenate(
        [share_out] + [share_in[:, n * inner : (n + 1) * inner] for n in range(groups)]
    )
    all_ffn = Replication(place, joined)
    grads = (low_a, after(low_b, r_b.made, joined, r_a.along()))
    tiles = length // TILE // 2
    input_grad = project_qkv_back(grads, full_qkv, first_grad, 0, tiles)
    meet(input_grad, r_b, r_a, all_ffn)
    steps = (r_b.near(), r_a.along_far())
    input_grad = project_qkv_back(
        grads, full_qkv, after(first_grad, *steps), tiles, tiles, input_grad
    )
    meet(input_grad, r_b, r_a)
    middle = r_b.middle()
    r_a.flying = after(r_a.flying, middle)
    all_a = Replication(place, r_a.share())
    meet(all_a.blocks[0], r_b, all_a)
    along = r_b.along_direct()
    all_a.flying = after(all_a.flying, along)
    all_ffn.flying = after(all_ffn.flying, along)
    pairs_made = (all_a.far(), all_ffn.far())
    meet(pairs_made, r_b)
    share_b = r_b.share_direct()
    all_b = Replication(place, share_b, direct=True)
    meet(share_b, all_ffn)
    w_out_grad, w_in_grad = order_feed_forward(place, all_ffn.landed(), share_in.shape[0])
    all_a.flying = after(all_a.flying, w_out_grad)
    w_attn_grad, w_qkv_grad, small = order_attention(
        place, all_a.landed(), all_b.landed(), w_attn_out.shape[0]
    )
    small = [small[8 * (n // 3) + n % 3] for n in range(12)]
    return (
        layer_out[None],
        input_grad[None],
        w_qkv_grad,
        small[B_QUERY],
        small[B_VALUE],
        w_attn_grad,
        small[B_ATTN],
        small[GAIN_ONE],
        small[SHIFT_ONE],
        w_in_grad,
        jnp.concatenate(small[B_IN:]),
        w_out_grad,
        small[B_OUT],
        small[GAIN_TWO],
        small[SHIFT_TWO],
    )


def solution(mesh):
    groups, shards = mesh.shape["grp"], mesh.shape["shard"]
    if groups == 4 and shards == 8:
        body = functools.partial(on_device_permutes, groups=groups, shards=shards)
    else:
        body = on_device
    return jax.shard_map(
        body,
        mesh=mesh,
        in_specs=(
            P(("grp", "shard"), None, None),
            P(("grp", "shard"), None),
            P(("grp", "shard"), None),
            P(("grp", "shard"), None, None),
            P("shard", "grp"),
            P("shard"),
            P("shard"),
            P("shard", "grp"),
            P("shard"),
            P("shard"),
            P("shard"),
            P("shard", "grp"),
            P("shard"),
            P("shard", "grp"),
            P("shard"),
            P("shard"),
            P("shard"),
        ),
        out_specs=(
            P(("grp", "shard"), None, None),
            P(("grp", "shard"), None, None),
            P("shard", None),
            P("shard"),
            P("shard"),
            P("shard", None),
            P("shard"),
            P("shard"),
            P("shard"),
            P("shard", None),
            P("shard"),
            P("shard", None),
            P("shard"),
            P("shard"),
            P("shard"),
        ),
        check_vma=False,
    )
```

```python
import functools
import math

import jax
import jax.numpy as jnp
from jax import lax
from jax.experimental import pallas as pl
from jax.experimental.pallas import tpu as pltpu
from jax.sharding import PartitionSpec as P

H = 16
HD = 64


masked_score = -1e30
epsilon = 1e-05


def norm_layer(rows, gain_row, shift_row):
    row_mean = jnp.mean(rows, -1, keepdims=True)
    centered = rows - row_mean
    row_var = jnp.mean(centered * centered, -1, keepdims=True)
    return centered * lax.rsqrt(row_var + epsilon) * gain_row + shift_row


def gelu_exact(values):
    return 0.5 * values * (1.0 + lax.erf(values * (1.0 / math.sqrt(2.0))))


def contract_rows(left, right):
    return lax.dot_general(
        left, right, (((0,), (0,)), ((), ())), preferred_element_type=jnp.float32
    )


def contract_cols(left, right):
    return lax.dot_general(
        left, right, (((1,), (1,)), ((), ())), preferred_element_type=jnp.float32
    )


def attend_forward(queries, key_rows, value_rows, segment_row, block_rows):
    length, model_width = queries.shape
    scaling = 1.0 / math.sqrt(HD)
    key_heads = key_rows.reshape(length, H, HD)
    value_heads = value_rows.reshape(length, H, HD)
    query_blocks = queries.reshape(length // block_rows, block_rows, H, HD)
    segment_blocks = segment_row.reshape(length // block_rows, block_rows)

    def one_block(pieces):
        query_part, segment_part = pieces
        scores = (
            jnp.einsum("qhd,khd->hqk", query_part, key_heads, preferred_element_type=jnp.float32)
            * scaling
        )
        allowed = segment_part[:, None] == segment_row[None, :]
        scores = jnp.where(allowed[None], scores, masked_score)
        row_max = jnp.max(scores, -1, keepdims=True)
        powers = jnp.exp(scores - row_max)
        totals = jnp.sum(powers, -1, keepdims=True)
        attn_probs = (powers / totals).astype(jnp.bfloat16)
        context = jnp.einsum(
            "hqk,khd->qhd", attn_probs, value_heads, preferred_element_type=jnp.float32
        )
        return (
            context.reshape(block_rows, model_width).astype(jnp.bfloat16),
            (row_max + jnp.log(totals))[:, :, 0],
        )

    contexts, log_sums = lax.map(one_block, (query_blocks, segment_blocks))
    return (contexts.reshape(length, model_width), log_sums)


def attend_backward(queries, key_rows, value_rows, segment_row, log_sums, context_grad, block_rows):
    length, model_width = queries.shape
    scaling = 1.0 / math.sqrt(HD)
    key_heads = key_rows.reshape(length, H, HD)
    value_heads = value_rows.reshape(length, H, HD)
    query_blocks = queries.reshape(length // block_rows, block_rows, H, HD)
    segment_blocks = segment_row.reshape(length // block_rows, block_rows)
    grad_blocks = context_grad.reshape(length // block_rows, block_rows, H, HD)

    def one_block(running, pieces):
        key_acc, value_acc = running
        query_part, segment_part, lse_part, grad_part = pieces
        scores = (
            jnp.einsum("qhd,khd->hqk", query_part, key_heads, preferred_element_type=jnp.float32)
            * scaling
        )
        allowed = segment_part[:, None] == segment_row[None, :]
        scores = jnp.where(allowed[None], scores, masked_score)
        probs = jnp.exp(scores - lse_part[:, :, None])
        prob_low = probs.astype(jnp.bfloat16)
        prob_grad = jnp.einsum(
            "qhd,khd->hqk", grad_part, value_heads, preferred_element_type=jnp.float32
        )
        row_dot = jnp.sum(prob_grad * probs, -1, keepdims=True)
        score_grad = (probs * (prob_grad - row_dot)).astype(jnp.bfloat16)
        query_grad = (
            jnp.einsum("hqk,khd->qhd", score_grad, key_heads, preferred_element_type=jnp.float32)
            * scaling
        )
        key_acc = (
            key_acc
            + jnp.einsum("hqk,qhd->khd", score_grad, query_part, preferred_element_type=jnp.float32)
            * scaling
        )
        value_acc = value_acc + jnp.einsum(
            "hqk,qhd->khd", prob_low, grad_part, preferred_element_type=jnp.float32
        )
        return ((key_acc, value_acc), query_grad.reshape(block_rows, model_width))

    empty_acc = jnp.zeros((length, H, HD), jnp.float32)
    (key_grad, value_grad), query_grads = lax.scan(
        one_block, (empty_acc, empty_acc), (query_blocks, segment_blocks, log_sums, grad_blocks)
    )
    return (
        query_grads.reshape(length, model_width),
        key_grad.reshape(length, model_width),
        value_grad.reshape(length, model_width),
    )


def on_device(
    tokens,
    segment_ids,
    keep_flag,
    cotangent,
    w_qkv,
    b_query,
    b_value,
    w_attn_out,
    b_attn_out,
    norm1_gain,
    norm1_bias,
    w_in,
    b_in,
    w_out,
    b_out,
    norm2_gain,
    norm2_bias,
):
    seq_count, length, model_width = tokens.shape
    block_rows = min(512, length)
    within = (
        lax.all_gather(w_qkv, "shard", axis=0, tiled=True),
        lax.all_gather(w_attn_out, "shard", axis=0, tiled=True),
        lax.all_gather(w_in, "shard", axis=0, tiled=True),
        lax.all_gather(w_out, "shard", axis=0, tiled=True),
        lax.all_gather(b_query, "shard", axis=0, tiled=True),
        lax.all_gather(b_value, "shard", axis=0, tiled=True),
        lax.all_gather(b_attn_out, "shard", axis=0, tiled=True),
        lax.all_gather(norm1_gain, "shard", axis=0, tiled=True),
        lax.all_gather(norm1_bias, "shard", axis=0, tiled=True),
        lax.all_gather(b_in, "shard", axis=0, tiled=True),
        lax.all_gather(b_out, "shard", axis=0, tiled=True),
        lax.all_gather(norm2_gain, "shard", axis=0, tiled=True),
        lax.all_gather(norm2_bias, "shard", axis=0, tiled=True),
    )
    full_qkv, full_attn, full_in, full_out = (
        lax.all_gather(within[0], "grp", axis=1, tiled=True),
        lax.all_gather(within[1], "grp", axis=1, tiled=True),
        lax.all_gather(within[2], "grp", axis=1, tiled=True),
        lax.all_gather(within[3], "grp", axis=1, tiled=True),
    )
    (
        bias_query,
        bias_value,
        bias_attn,
        gain_one,
        shift_one,
        bias_in,
        bias_out,
        gain_two,
        shift_two,
    ) = [piece.astype(jnp.float32) for piece in within[4:]]
    flat_rows = tokens.reshape(seq_count * length, model_width)
    mixed_qkv = jnp.dot(flat_rows, full_qkv, preferred_element_type=jnp.float32)
    queries = (mixed_qkv[:, :model_width] + bias_query).astype(jnp.bfloat16)
    key_rows = mixed_qkv[:, model_width : 2 * model_width].astype(jnp.bfloat16)
    value_rows = (mixed_qkv[:, 2 * model_width :] + bias_value).astype(jnp.bfloat16)
    query_seqs = queries.reshape(seq_count, length, model_width)
    key_seqs = key_rows.reshape(seq_count, length, model_width)
    value_seqs = value_rows.reshape(seq_count, length, model_width)

    def forward_sequence(pieces):
        return attend_forward(pieces[0], pieces[1], pieces[2], pieces[3], block_rows)

    contexts, log_sums = lax.map(forward_sequence, (query_seqs, key_seqs, value_seqs, segment_ids))
    contexts = contexts.reshape(seq_count * length, model_width)
    attended = jnp.dot(contexts, full_attn, preferred_element_type=jnp.float32) + bias_attn
    first_sum = flat_rows.astype(jnp.float32) + attended
    normed_one, norm_one_back = jax.vjp(norm_layer, first_sum, gain_one, shift_one)
    normed_low = normed_one.astype(jnp.bfloat16)
    hidden_pre = jnp.dot(normed_low, full_in, preferred_element_type=jnp.float32) + bias_in
    hidden, gelu_back = jax.vjp(gelu_exact, hidden_pre)
    hidden_low = hidden.astype(jnp.bfloat16)
    second_sum = normed_one + (
        jnp.dot(hidden_low, full_out, preferred_element_type=jnp.float32) + bias_out
    )
    result, norm_two_back = jax.vjp(norm_layer, second_sum, gain_two, shift_two)
    layer_out = result.astype(jnp.bfloat16).reshape(seq_count, length, model_width)
    again = (
        lax.all_gather(w_qkv, "shard", axis=0, tiled=True),
        lax.all_gather(w_attn_out, "shard", axis=0, tiled=True),
        lax.all_gather(w_in, "shard", axis=0, tiled=True),
        lax.all_gather(w_out, "shard", axis=0, tiled=True),
    )
    back_qkv, back_attn, back_in, back_out = (
        lax.all_gather(again[0], "grp", axis=1, tiled=True),
        lax.all_gather(again[1], "grp", axis=1, tiled=True),
        lax.all_gather(again[2], "grp", axis=1, tiled=True),
        lax.all_gather(again[3], "grp", axis=1, tiled=True),
    )
    masked_cot = cotangent.astype(jnp.float32).reshape(
        seq_count * length, model_width
    ) * keep_flag.reshape(seq_count * length, 1).astype(jnp.float32)
    second_grad, gain_two_grad, shift_two_grad = norm_two_back(masked_cot)
    bias_out_grad = jnp.sum(second_grad, 0)
    out_low = second_grad.astype(jnp.bfloat16)
    w_out_grad = contract_rows(hidden_low, out_low)
    hidden_grad = contract_cols(out_low, back_out)
    (pre_grad,) = gelu_back(hidden_grad)
    bias_in_grad = jnp.sum(pre_grad, 0)
    pre_low = pre_grad.astype(jnp.bfloat16)
    w_in_grad = contract_rows(normed_low, pre_low)
    normed_grad = second_grad + contract_cols(pre_low, back_in)
    first_grad, gain_one_grad, shift_one_grad = norm_one_back(normed_grad)
    bias_attn_grad = jnp.sum(first_grad, 0)
    attn_low = first_grad.astype(jnp.bfloat16)
    w_attn_grad = contract_rows(contexts, attn_low)
    context_grad = contract_cols(attn_low, back_attn).astype(jnp.bfloat16)

    def backward_sequence(pieces):
        return attend_backward(
            pieces[0], pieces[1], pieces[2], pieces[3], pieces[4], pieces[5], block_rows
        )

    query_grad, key_grad, value_grad = lax.map(
        backward_sequence,
        (
            query_seqs,
            key_seqs,
            value_seqs,
            segment_ids,
            log_sums,
            context_grad.reshape(seq_count, length, model_width),
        ),
    )
    query_grad = query_grad.reshape(seq_count * length, model_width)
    key_grad = key_grad.reshape(seq_count * length, model_width)
    value_grad = value_grad.reshape(seq_count * length, model_width)
    bias_query_grad = jnp.sum(query_grad, 0)
    bias_value_grad = jnp.sum(value_grad, 0)
    qkv_low = jnp.concatenate([query_grad, key_grad, value_grad], 1).astype(jnp.bfloat16)
    w_qkv_grad = contract_rows(flat_rows, qkv_low)
    input_grad = first_grad + contract_cols(qkv_low, back_qkv)
    reduced = (
        lax.psum_scatter(
            w_qkv_grad.astype(jnp.bfloat16), "shard", scatter_dimension=0, tiled=True
        ).astype(jnp.float32),
        lax.psum_scatter(
            bias_query_grad.astype(jnp.bfloat16), "shard", scatter_dimension=0, tiled=True
        ).astype(jnp.float32),
        lax.psum_scatter(
            bias_value_grad.astype(jnp.bfloat16), "shard", scatter_dimension=0, tiled=True
        ).astype(jnp.float32),
        lax.psum_scatter(
            w_attn_grad.astype(jnp.bfloat16), "shard", scatter_dimension=0, tiled=True
        ).astype(jnp.float32),
        lax.psum_scatter(
            bias_attn_grad.astype(jnp.bfloat16), "shard", scatter_dimension=0, tiled=True
        ).astype(jnp.float32),
        lax.psum_scatter(
            gain_one_grad.astype(jnp.bfloat16), "shard", scatter_dimension=0, tiled=True
        ).astype(jnp.float32),
        lax.psum_scatter(
            shift_one_grad.astype(jnp.bfloat16), "shard", scatter_dimension=0, tiled=True
        ).astype(jnp.float32),
        lax.psum_scatter(
            w_in_grad.astype(jnp.bfloat16), "shard", scatter_dimension=0, tiled=True
        ).astype(jnp.float32),
        lax.psum_scatter(
            bias_in_grad.astype(jnp.bfloat16), "shard", scatter_dimension=0, tiled=True
        ).astype(jnp.float32),
        lax.psum_scatter(
            w_out_grad.astype(jnp.bfloat16), "shard", scatter_dimension=0, tiled=True
        ).astype(jnp.float32),
        lax.psum_scatter(
            bias_out_grad.astype(jnp.bfloat16), "shard", scatter_dimension=0, tiled=True
        ).astype(jnp.float32),
        lax.psum_scatter(
            gain_two_grad.astype(jnp.bfloat16), "shard", scatter_dimension=0, tiled=True
        ).astype(jnp.float32),
        lax.psum_scatter(
            shift_two_grad.astype(jnp.bfloat16), "shard", scatter_dimension=0, tiled=True
        ).astype(jnp.float32),
    )
    summed = (
        lax.psum(reduced[0].astype(jnp.bfloat16), "grp").astype(jnp.float32),
        lax.psum(reduced[1].astype(jnp.bfloat16), "grp").astype(jnp.float32),
        lax.psum(reduced[2].astype(jnp.bfloat16), "grp").astype(jnp.float32),
        lax.psum(reduced[3].astype(jnp.bfloat16), "grp").astype(jnp.float32),
        lax.psum(reduced[4].astype(jnp.bfloat16), "grp").astype(jnp.float32),
        lax.psum(reduced[5].astype(jnp.bfloat16), "grp").astype(jnp.float32),
        lax.psum(reduced[6].astype(jnp.bfloat16), "grp").astype(jnp.float32),
        lax.psum(reduced[7].astype(jnp.bfloat16), "grp").astype(jnp.float32),
        lax.psum(reduced[8].astype(jnp.bfloat16), "grp").astype(jnp.float32),
        lax.psum(reduced[9].astype(jnp.bfloat16), "grp").astype(jnp.float32),
        lax.psum(reduced[10].astype(jnp.bfloat16), "grp").astype(jnp.float32),
        lax.psum(reduced[11].astype(jnp.bfloat16), "grp").astype(jnp.float32),
        lax.psum(reduced[12].astype(jnp.bfloat16), "grp").astype(jnp.float32),
    )
    return (
        layer_out,
        input_grad.reshape(seq_count, length, model_width),
        summed[0],
        summed[1],
        summed[2],
        summed[3],
        summed[4],
        summed[5],
        summed[6],
        summed[7],
        summed[8],
        summed[9],
        summed[10],
        summed[11],
        summed[12],
    )


NT = (((1,), (1,)), ((), ()))
NN = (((1,), (0,)), ((), ()))
TN = (((0,), (0,)), ((), ()))
LANES = 128
AXES = ("grp", "shard")


def mxu(left, right, dims):
    return lax.dot_general(left, right, dims, preferred_element_type=jnp.float32)


def cost(flops):
    return pl.CostEstimate(flops=2 * flops, bytes_accessed=0, transcendentals=0)


def params(megabytes=60):
    return pltpu.CompilerParams(vmem_limit_bytes=megabytes << 20)


def attention_forward_kernel(q_ref, k_ref, v_ref, seg_col, seg_row, out_ref, probs_ref, scale_ref, *, rows):
    length = q_ref.shape[0]
    first = lax.broadcasted_iota(jnp.int32, (1, LANES), 1) < HD
    keys = k_ref[...]
    values = v_ref[...]
    zero = jnp.zeros_like(keys)
    head_keys = (jnp.where(first, keys, zero), jnp.where(first, zero, keys))
    key_segments = seg_col[...]
    for block in range(length // rows):
        here = pl.ds(block * rows, rows)
        q = q_ref[here, :]
        allowed = key_segments == seg_row[:, here]
        outs, scales = [], []
        for head in range(2):
            scores = mxu(head_keys[head], q, NT)
            scores = jnp.where(allowed, scores, masked_score)
            powers = jnp.exp(scores - jnp.max(scores, 0, keepdims=True))
            scale = 1.0 / jnp.sum(powers, 0, keepdims=True)
            scales.append(jnp.broadcast_to(scale, (HD, rows)))
            powers = powers.astype(jnp.bfloat16)
            probs_ref[head, :, here] = powers
            outs.append(mxu(powers, values, TN))
        scale = jnp.transpose(jnp.concatenate(scales))
        scale_ref[here, :] = scale
        out_ref[here, :] = (jnp.where(first, outs[0], outs[1]) * scale).astype(jnp.bfloat16)


def attention_forward(qkv, seg_col, seg_row, start, pairs, before=None):
    length, width = qkv.shape[0], qkv.shape[1] // 3
    total = width // LANES
    rows = min(512, length)
    more = () if before is None else before

    def pair(part):
        return pl.BlockSpec((length, LANES), lambda j: (0, part * total + start + j))

    def body(q_ref, k_ref, v_ref, seg_c, seg_r, *refs):
        attention_forward_kernel(q_ref, k_ref, v_ref, seg_c, seg_r, *refs[-3:], rows=rows)

    return pl.pallas_call(
        body,
        grid=(pairs,),
        in_specs=[
            pair(0),
            pair(1),
            pair(2),
            pl.BlockSpec((length, 1), lambda j: (0, 0)),
            pl.BlockSpec((1, length), lambda j: (0, 0)),
        ]
        + [pl.BlockSpec(memory_space=pl.ANY)] * len(more),
        out_specs=[
            pl.BlockSpec((length, LANES), lambda j: (0, start + j)),
            pl.BlockSpec((2, length, length), lambda j: (start + j, 0, 0)),
            pl.BlockSpec((length, LANES), lambda j: (0, start + j)),
        ],
        out_shape=[
            jax.ShapeDtypeStruct((length, width), jnp.bfloat16),
            jax.ShapeDtypeStruct((2 * total, length, length), jnp.bfloat16),
            jax.ShapeDtypeStruct((length, width), jnp.float32),
        ],
        input_output_aliases={} if before is None else {5: 0, 6: 1, 7: 2},
        compiler_params=params(60),
        cost_estimate=cost(16 * length * length * pairs * LANES),
        name="attn_fwd",
    )(qkv, qkv, qkv, seg_col, seg_row, *more)


def attention_backward_kernel(
    q_ref, k_ref, v_ref, o_ref, do_ref, probs_ref, scale_ref, grad_ref, sum_ref
):
    first = lax.broadcasted_iota(jnp.int32, (1, LANES), 1) < HD
    pick = (
        lax.broadcasted_iota(jnp.int32, (8, LANES), 0)
        == lax.broadcasted_iota(jnp.int32, (8, LANES), 1) // HD
    ).astype(jnp.bfloat16)
    q = q_ref[...]
    scaled = do_ref[...].astype(jnp.float32) * scale_ref[...]
    do = scaled.astype(jnp.bfloat16)
    keys = k_ref[...]
    values = v_ref[...]
    zero = jnp.zeros_like(values)
    head_values = (jnp.where(first, values, zero), jnp.where(first, zero, values))
    products = scaled * o_ref[...].astype(jnp.float32)
    high = products.astype(jnp.bfloat16)
    low = (products - high.astype(jnp.float32)).astype(jnp.bfloat16)
    dots = mxu(pick, high, NT) + mxu(pick, low, NT)
    query_parts, key_parts, value_parts = [], [], []
    for head in range(2):
        probs = probs_ref[head]
        prob_grad = mxu(head_values[head], do, NT)
        score_grad = probs.astype(jnp.float32) * (prob_grad - dots[head : head + 1, :])
        score_grad = score_grad.astype(jnp.bfloat16)
        value_parts.append(mxu(probs, do, NN))
        key_parts.append(mxu(score_grad, q, NN))
        query_parts.append(mxu(score_grad, keys, TN))
    query_grad = jnp.where(first, *query_parts) * (1.0 / math.sqrt(HD))
    value_grad = jnp.where(first, *value_parts)
    grad_ref[0] = query_grad.astype(jnp.bfloat16)
    grad_ref[1] = jnp.where(first, *key_parts).astype(jnp.bfloat16)
    grad_ref[2] = value_grad.astype(jnp.bfloat16)
    sum_ref[0:1, :] = jnp.sum(query_grad, 0, keepdims=True)
    sum_ref[1:2, :] = jnp.sum(value_grad, 0, keepdims=True)


def attention_backward(qkv, out, out_grad, probs, scale, start, pairs, at, size, before=None):
    length, width = out.shape
    total = width // LANES
    more = () if before is None else before

    def pair(part):
        return pl.BlockSpec((length, LANES), lambda j: (0, part * total + start + j))

    def body(*refs):
        attention_backward_kernel(*refs[:7], *refs[-2:])

    return pl.pallas_call(
        body,
        grid=(pairs,),
        in_specs=[
            pair(0),
            pair(1),
            pair(2),
            pair(0),
            pair(0),
            pl.BlockSpec((2, length, length), lambda j: (start + j, 0, 0)),
            pair(0),
        ]
        + [pl.BlockSpec(memory_space=pl.ANY)] * len(more),
        out_specs=[
            pl.BlockSpec((3, length, LANES), lambda j: (0, 0, j + at)),
            pl.BlockSpec((2, LANES), lambda j: (0, j + at)),
        ],
        out_shape=[
            jax.ShapeDtypeStruct((3, length, size * LANES), jnp.bfloat16),
            jax.ShapeDtypeStruct((2, size * LANES), jnp.float32),
        ],
        input_output_aliases={} if before is None else {7: 0, 8: 1},
        compiler_params=params(60),
        cost_estimate=cost(32 * length * length * pairs * LANES),
        name="attn_bwd",
    )(qkv, qkv, qkv, out, out_grad, probs, scale, *more)


class Place:
    def __init__(self, groups, shards):
        self.groups = groups
        self.shards = shards
        self.chips = shards // 2
        self.grp = lax.axis_index("grp")
        self.shard = lax.axis_index("shard")
        self.core = self.shard % 2
        self.chip = self.shard // 2
        self.scalars = jnp.stack([self.core, self.chip, self.grp]).astype(jnp.int32)

    def permute(self, array, mask_of_core):
        pairs = [(i, i ^ mask_of_core[i % 2]) for i in range(self.groups * self.shards)]
        return lax.ppermute(array, AXES, pairs)

    def swap_core(self, array):
        return self.permute(array, (1, 1))

    def swap_grp(self, array, step):
        masks = (self.shards, 2 * self.shards)
        return self.permute(array, masks if step == 0 else masks[::-1])

    def swap_chip(self, array, step):
        masks = (2, 4)
        return self.permute(array, masks if step == 0 else masks[::-1])

    def slot_chip(self, slot):
        return self.chip ^ turn(slot, self.core)

    def slot_grp(self, slot):
        return self.grp ^ turn(slot, self.core)


def turn(slot, core):
    if isinstance(slot, int):
        return slot if slot in (0, 3) else jnp.where(core == 0, slot, 3 - slot)
    return jnp.where((core == 0) | (slot == 0) | (slot == 3), slot, 3 - slot)


def after(value, *others):
    return lax.optimization_barrier((value, *others))[0]


def meet(anchor, *flights):
    arrays = [f.flying for f in flights]
    _, *arrays = lax.optimization_barrier((anchor, *arrays))
    for f, array in zip(flights, arrays):
        f.flying = array


class Gather:
    def __init__(self, place, piece):
        self.place = place
        self.piece = piece
        self.held = [None] * 4
        self.crossed = [None] * 4

    def chips_near(self, *wait):
        self.piece = after(self.piece, *wait)
        self.flying = self.place.swap_chip(self.piece, 0)

    def chips_far(self):
        self.pair = jnp.stack([self.piece, self.flying])
        self.flying = self.place.swap_chip(self.pair, 1)
        return self.pair

    def join(self):
        self.held[0] = jnp.concatenate([self.pair, self.flying])
        return self.held[0]

    def near(self, *wait):
        self.held[0] = after(self.held[0], *wait)
        self.flying = (self.place.swap_grp(self.held[0], 0), self.place.swap_grp(self.held[0], 1))
        return self.held[0]

    def far(self, *wait):
        self.held[1:3] = self.flying
        first = after(self.held[1], *wait)
        self.flying = self.place.swap_grp(first, 1)

    def landed(self):
        self.held[3] = self.flying

    def cross(self, *which, wait=()):
        for n in which:
            self.crossed[n] = self.place.swap_core(after(self.held[n], *wait))

    def pieces(self):
        return self.held + self.crossed


class Window:
    def __init__(self, gather, start, cols):
        self.arrays = gather.pieces()
        self.start, self.cols = start, cols
        chips, rows, _ = self.arrays[0].shape
        self.chips, self.rows = chips, rows


def fetch(where, window, refs, whole, sem, by):
    rows, cols, chips = window.rows, window.cols, window.chips
    for slot in range(4):
        for side in range(2):
            core = where[0] ^ side
            ref = refs[4 * side + slot]
            distance = turn(slot, core)
            col = pl.multiple_of((where[2] ^ distance) * cols, LANES)
            for k in range(chips):
                row = ((where[1] ^ turn(k, core)) * 2 + core) * rows
                pltpu.make_async_copy(
                    ref.at[k, :, pl.ds(window.start, cols)],
                    whole.at[pl.ds(pl.multiple_of(row, rows), rows), pl.ds(col, cols)],
                    sem.at[distance if by == "grp" else 0],
                ).start()


def weight_call(place, kernel, window, inputs, in_specs, outs, out_specs, steps, by, name, flops, write=True):
    cols, groups = window.cols, place.groups
    pieces = window.arrays
    shape = (window.chips * 2 * window.rows, groups * cols)
    slots = {"grp": groups, "all": 1}[by]
    anywhere = pl.BlockSpec(memory_space=pl.ANY)

    def body(where, *refs):
        taken, refs = refs[: len(pieces)], refs[len(pieces) :]
        *refs, weight, sem, out_sem = refs
        if write:
            *refs, written = refs
        step = pl.program_id(0)

        @pl.when(step == 0)
        def _():
            fetch(where, window, taken, weight, sem, by)

        def ready():
            if by == "all":

                @pl.when(step == 0)
                def _():
                    pltpu.make_async_copy(weight, weight, sem.at[0]).wait()
                    if write:
                        pltpu.make_async_copy(weight, written, out_sem.at[0]).start()

            else:
                at = pl.ds(pl.multiple_of((where[2] ^ step) * cols, LANES), cols)
                view = weight.at[:, at]
                pltpu.make_async_copy(view, view, sem.at[step]).wait()
                pltpu.make_async_copy(view, written.at[:, at], out_sem.at[step]).start()

        kernel(where, ready, weight, *refs)

        @pl.when(step == (steps - 1 if write else -1))
        def _():
            for slot in range(slots if write else 0):
                width = shape[1] // slots
                view = weight.at[:, pl.ds(slot * width, width)]
                pltpu.make_async_copy(view, view, out_sem.at[slot]).wait()

    total = sum(math.prod(x.shape) * x.dtype.itemsize for x in list(inputs) + list(outs))
    return pl.pallas_call(
        body,
        grid_spec=pltpu.PrefetchScalarGridSpec(
            num_scalar_prefetch=1,
            grid=(steps,),
            in_specs=[anywhere] * len(pieces) + in_specs,
            out_specs=out_specs + [anywhere] * write,
            scratch_shapes=[
                pltpu.VMEM(shape, jnp.bfloat16),
                pltpu.SemaphoreType.DMA((slots,)),
                pltpu.SemaphoreType.DMA((slots,)),
            ],
        ),
        out_shape=outs + [shaped(shape, jnp.bfloat16)] * write,
        compiler_params=params(60),
        cost_estimate=cost(flops),
        name=name,
    )(place.scalars, *pieces, *inputs)


def plain_call(kernel, inputs, in_specs, outs, out_specs, steps, name, flops):
    total = sum(math.prod(x.shape) * x.dtype.itemsize for x in list(inputs) + list(outs))
    return pl.pallas_call(
        kernel,
        grid=(steps,),
        in_specs=in_specs,
        out_specs=out_specs,
        out_shape=outs,
        compiler_params=params(60),
        cost_estimate=cost(flops),
        name=name,
    )(*inputs)


TILE = 256


def row_tiles(width):
    return pl.BlockSpec((TILE, width), lambda i, *s: (i, 0))


def fixed(*shape):
    return pl.BlockSpec(shape, lambda i, *s: (0,) * len(shape))


def whole_once(shape):
    return pl.BlockSpec(shape, lambda i: (0,) * len(shape), pipeline_mode=pl.Buffered(1))


def shaped(shape, dtype):
    return jax.ShapeDtypeStruct(shape, dtype)


B_QUERY, B_VALUE, B_ATTN, GAIN_ONE, SHIFT_ONE, B_OUT, GAIN_TWO, SHIFT_TWO, B_IN = range(9)


def row(ref, n):
    return ref[n : n + 1, :]


class Vectors:
    def __init__(self, place, vectors):
        lines = [v.reshape(-1, LANES) for v in vectors]
        blank = jnp.zeros((-sum(x.shape[0] for x in lines) % 16, LANES), jnp.bfloat16)
        self.own = jnp.concatenate([*lines, blank])
        self.place = place
        self.flying = place.swap_core(self.own)

    def chips_near(self):
        self.own = jnp.stack([self.own, self.flying])
        self.flying = self.place.swap_chip(self.own, 0)

    def chips_far(self):
        self.own = jnp.stack([self.own, self.flying])
        self.flying = self.place.swap_chip(self.own, 1)

    def landed(self):
        self.slots = jnp.concatenate([self.own, self.flying])

    def unpack(self, seg_row, keep_row):
        place = self.place
        length = seg_row.shape[1]
        slots, sides, rows, lanes = self.slots.shape
        shards = place.shards

        def kernel(where, in_ref, seg_ref, keep_ref, *outs):
            rows_ref, inner_ref, qkv_ref, seg_col_ref, keep_col_ref = outs
            for line_ref, col_ref in ((seg_ref, seg_col_ref), (keep_ref, keep_col_ref)):
                line = jnp.broadcast_to(line_ref[...].astype(jnp.float32), (8, length))
                col_ref[...] = line.T[:, 0:1].astype(col_ref.dtype)
            width = shards * lanes
            qkv_ref[...] = jnp.zeros_like(qkv_ref)
            for slot in range(slots):
                for side in range(sides):
                    core = where[0] ^ side
                    shard = (where[1] ^ turn(slot, where[0])) * 2 + core
                    part = in_ref[slot, side].astype(jnp.float32)
                    at = pl.multiple_of(shard * lanes, lanes)
                    rows_ref[:, pl.ds(at, lanes)] = part
                    qkv_ref[:, pl.ds(at, lanes)] = part[B_QUERY : B_QUERY + 1]
                    qkv_ref[:, pl.ds(2 * width + at, lanes)] = part[B_VALUE : B_VALUE + 1]
                    for n in range(4):
                        start = pl.multiple_of((shard * 4 + n) * lanes, lanes)
                        inner_ref[:, pl.ds(start, lanes)] = part[B_IN + n : B_IN + n + 1]

        in_vmem = pl.BlockSpec(memory_space=pltpu.VMEM)
        return pl.pallas_call(
            kernel,
            in_specs=[pl.BlockSpec(memory_space=pltpu.SMEM)] + [in_vmem] * 3,
            out_specs=[in_vmem] * 5,
            out_shape=[
                shaped((rows, shards * lanes), jnp.float32),
                shaped((1, 4 * shards * lanes), jnp.float32),
                shaped((1, 3 * shards * lanes), jnp.float32),
                shaped((length, 1), jnp.int32),
                shaped((length, 1), jnp.float32),
            ],
            name="vectors",
        )(place.scalars, self.slots, seg_row, keep_row)


def project_qkv(place, rows, window, bias, scale):
    length, width = rows.shape
    cols = window.cols

    def kernel(where, ready, weight, x_ref, bias_ref, scale_ref, out_ref):
        ready()
        at = pl.ds(pl.multiple_of((where[2] ^ pl.program_id(0)) * cols, LANES), cols)
        size = min(512, length)
        for tile in range(length // size):
            here = pl.ds(tile * size, size)
            mixed = mxu(x_ref[here, :], weight[:, at], NN) + bias_ref[:, at]
            mixed = mixed.astype(jnp.bfloat16).astype(jnp.float32) * scale_ref[:, at]
            out_ref[here, :] = mixed.astype(jnp.bfloat16)

    total = cols * place.groups
    return weight_call(
        place,
        kernel,
        window,
        (rows, bias, scale),
        [fixed(length, width), fixed(1, total), fixed(1, total)],
        [shaped((length, total), jnp.bfloat16)],
        [pl.BlockSpec((length, cols), lambda i, s: (0, i ^ s[2]))],
        place.groups,
        "grp",
        "qkv",
        2 * length * width * total,
    )


def norm_parts(rows):
    centered = rows - jnp.mean(rows, -1, keepdims=True)
    scale = lax.rsqrt(jnp.mean(centered * centered, -1, keepdims=True) + epsilon)
    return centered * scale, scale


def norm_back(grad, normed, scale):
    return scale * (
        grad
        - jnp.mean(grad, -1, keepdims=True)
        - normed * jnp.mean(grad * normed, -1, keepdims=True)
    )


def add_rows(sum_ref, *terms):
    @pl.when(pl.program_id(0) == 0)
    def _():
        sum_ref[...] = jnp.zeros_like(sum_ref)

    for n, term in enumerate(terms):
        sum_ref[n : n + 1, :] += jnp.sum(term, 0, keepdims=True)


def project_out(place, contexts, window, rows, vectors):
    length, width = rows.shape

    def kernel(where, ready, weight, c_ref, x_ref, v_ref, n_ref, r_ref, low_ref):
        ready()
        first_sum = mxu(c_ref[...], weight[...], NN) + row(v_ref, B_ATTN)
        first_sum = first_sum + x_ref[...].astype(jnp.float32)
        normed, scale = norm_parts(first_sum)
        n_ref[...] = normed
        r_ref[...] = jnp.broadcast_to(scale, r_ref.shape)
        low_ref[...] = (normed * row(v_ref, GAIN_ONE) + row(v_ref, SHIFT_ONE)).astype(jnp.bfloat16)

    return weight_call(
        place,
        kernel,
        window,
        (contexts, rows, vectors),
        [row_tiles(width), row_tiles(width), fixed(*vectors.shape)],
        [
            shaped((length, width), jnp.float32),
            shaped((length, LANES), jnp.float32),
            shaped((length, width), jnp.bfloat16),
        ],
        [row_tiles(width), row_tiles(LANES), row_tiles(width)],
        length // TILE,
        "all",
        "attn_out",
        2 * length * width * width,
    )


def feed_in(place, normed_low, window, bias):
    length, width = normed_low.shape
    cols = window.cols

    def kernel(where, ready, weight, x_ref, bias_ref, hid_ref, slope_ref):
        ready()
        at = pl.ds(pl.multiple_of((where[2] ^ pl.program_id(0)) * cols, LANES), cols)
        size = min(512, length)
        for tile in range(length // size):
            here = pl.ds(tile * size, size)
            pre = mxu(x_ref[here, :], weight[:, at], NN) + bias_ref[:, at]
            share = 0.5 + 0.5 * lax.erf(pre * (1.0 / math.sqrt(2.0)))
            bell = jnp.exp(-0.5 * pre * pre) * (1.0 / math.sqrt(2.0 * math.pi))
            hid_ref[here, :] = (pre * share).astype(jnp.bfloat16)
            slope_ref[here, :] = (share + pre * bell).astype(jnp.bfloat16)

    total = cols * place.groups
    block = pl.BlockSpec((length, cols), lambda i, s: (0, i ^ s[2]))
    return weight_call(
        place,
        kernel,
        window,
        (normed_low, bias),
        [fixed(length, width), fixed(1, total)],
        [shaped((length, total), jnp.bfloat16)] * 2,
        [block, block],
        place.groups,
        "grp",
        "feed_in",
        2 * length * width * total,
    )


def feed_out(place, hidden, window, normed, cot, keep, vectors, slope):
    length, inner = hidden.shape
    width = normed.shape[1]

    def kernel(where, ready, weight, h_ref, n_ref, cot_ref, keep_ref, v_ref, slope_ref, *outs):
        out_ref, grad_ref, low_ref, sum_ref, pre_ref, inner_ref = outs
        ready()
        fed = mxu(h_ref[...], weight[...], NN)
        normed_one = n_ref[...] * row(v_ref, GAIN_ONE) + row(v_ref, SHIFT_ONE)
        second_sum = normed_one + (fed + row(v_ref, B_OUT))
        second, scale = norm_parts(second_sum)
        out_ref[...] = (second * row(v_ref, GAIN_TWO) + row(v_ref, SHIFT_TWO)).astype(jnp.bfloat16)
        masked = cot_ref[...].astype(jnp.float32) * keep_ref[...]
        grad = norm_back(masked * row(v_ref, GAIN_TWO), second, scale)
        grad_ref[...] = grad
        low = grad.astype(jnp.bfloat16)
        low_ref[...] = low
        add_rows(sum_ref, masked * second, masked, grad)

        @pl.when(pl.program_id(0) == 0)
        def _():
            inner_ref[...] = jnp.zeros_like(inner_ref)

        size = min(1024, inner)
        for n in range(inner // size):
            at = slice(n * size, (n + 1) * size)
            pre = mxu(low, weight[at, :], NT) * slope_ref[:, at].astype(jnp.float32)
            pre_ref[:, at] = pre.astype(jnp.bfloat16)
            inner_ref[:, at] += jnp.sum(pre, 0, keepdims=True)

    return weight_call(
        place,
        kernel,
        window,
        (hidden, normed, cot, keep, vectors, slope),
        [
            row_tiles(inner),
            row_tiles(width),
            row_tiles(width),
            row_tiles(1),
            fixed(*vectors.shape),
            row_tiles(inner),
        ],
        [
            shaped((length, width), jnp.bfloat16),
            shaped((length, width), jnp.float32),
            shaped((length, width), jnp.bfloat16),
            shaped((8, width), jnp.float32),
            shaped((length, inner), jnp.bfloat16),
            shaped((1, inner), jnp.float32),
        ],
        [
            row_tiles(width),
            row_tiles(width),
            row_tiles(width),
            fixed(8, width),
            row_tiles(inner),
            fixed(1, inner),
        ],
        length // TILE,
        "all",
        "feed_out",
        4 * length * width * inner,
        write=False,
    )


def feed_in_back(pre_low, weight, second_grad, normed, scale, vectors, attn_weight):
    length, inner = pre_low.shape
    width = normed.shape[1]

    def kernel(p_ref, w_ref, g_ref, n_ref, r_ref, v_ref, a_ref, first_ref, low_ref, ctx_ref, sum_ref):
        grad = g_ref[...] + mxu(p_ref[...], w_ref[...], NT)
        first = norm_back(grad * row(v_ref, GAIN_ONE), n_ref[...], r_ref[:, :1])
        low = first.astype(jnp.bfloat16)
        first_ref[...] = first
        low_ref[...] = low
        ctx_ref[...] = mxu(low, a_ref[...], NT).astype(jnp.bfloat16)
        add_rows(sum_ref, grad * n_ref[...], grad, first)

    return plain_call(
        kernel,
        (pre_low, weight, second_grad, normed, scale, vectors, attn_weight),
        [
            row_tiles(inner),
            whole_once(weight.shape),
            row_tiles(width),
            row_tiles(width),
            row_tiles(LANES),
            fixed(*vectors.shape),
            whole_once(attn_weight.shape),
        ],
        [
            shaped((length, width), jnp.float32),
            shaped((length, width), jnp.bfloat16),
            shaped((length, width), jnp.bfloat16),
            shaped((8, width), jnp.float32),
        ],
        [row_tiles(width), row_tiles(width), row_tiles(width), fixed(8, width)],
        length // TILE,
        "feed_in_back",
        2 * length * width * (inner + width),
    )


def project_qkv_back(grads, weight, first_grad, start, tiles, before=None):
    length, width = first_grad.shape
    part = width // len(grads)

    def kernel(w_ref, *refs):
        grad_refs, first_ref, out_ref = refs[: len(grads)], refs[len(grads)], refs[-1]
        total = first_ref[...]
        for n in range(3):
            for m, grad_ref in enumerate(grad_refs):
                at = n * width + m * part
                total = total + mxu(grad_ref[n], w_ref[:, at : at + part], NT)
        out_ref[...] = total

    tile = pl.BlockSpec((TILE, width), lambda i: (start + i, 0))
    more = () if before is None else (before,)
    return pl.pallas_call(
        kernel,
        grid=(tiles,),
        in_specs=[whole_once(weight.shape)]
        + [pl.BlockSpec((3, TILE, part), lambda i: (0, start + i, 0))] * len(grads)
        + [tile]
        + [pl.BlockSpec(memory_space=pl.ANY)] * len(more),
        out_specs=tile,
        out_shape=shaped((length, width), jnp.float32),
        input_output_aliases={} if before is None else {len(grads) + 2: 0},
        compiler_params=params(60),
        cost_estimate=cost(6 * tiles * TILE * width * width),
        name="qkv_back",
    )(weight, *grads, first_grad, *more)


ORDER = (1, 3, 0, 2)


def ordered_slot(j):
    return jnp.where(j < 2, 2 * j + 1, 2 * j - 4)


def weight_grad_kernel(where, left_ref, right_ref, own, sent, kept, *, rows, groups, split):
    core = where[0]
    chips = left_ref.shape[1] // (2 * rows)

    @pl.when(pl.program_id(1) == 0)
    def _():
        keep_rows(core, left_ref, rows, kept)

    if split:
        size = min(512, right_ref.shape[1])
        for ref, side in ((sent, 1), (own, 0)):
            for n in range(right_ref.shape[1] // size):
                at = slice(n * size, (n + 1) * size)
                part = mxu(kept[side], right_ref[:, at], NN).astype(jnp.bfloat16)
                ref[0, :, :, at] = part.reshape(chips, rows, size)
    else:
        cols = right_ref.shape[1] // groups
        for ref, side in ((sent, 1), (own, 0)):
            for pos, slot in enumerate(ORDER):
                start = pl.multiple_of((where[2] ^ turn(slot, core ^ side)) * cols, LANES)
                part = mxu(kept[side], right_ref[:, pl.ds(start, cols)], NN)
                ref[pos] = part.astype(jnp.bfloat16).reshape(chips, rows, cols)


def keep_rows(core, left_ref, rows, kept):
    chips = left_ref.shape[1] // (2 * rows)
    for side in range(2):
        chosen = []
        for k in range(chips):
            even = left_ref[:, 2 * k * rows : (2 * k + 1) * rows]
            odd = left_ref[:, (2 * k + 1) * rows : (2 * k + 2) * rows]
            chosen.append(jnp.where(core == side, even, odd))
        left = chosen[0] if chips == 1 else jnp.concatenate(chosen, 1)
        kept[side] = left.T


def turned_rows(place, left):
    tokens, height = left.shape

    def kernel(where, left_ref, out_ref):
        keep_rows(where[0], left_ref, height // place.shards, out_ref)

    in_vmem = pl.BlockSpec(memory_space=pltpu.VMEM)
    return pl.pallas_call(
        kernel,
        in_specs=[pl.BlockSpec(memory_space=pltpu.SMEM), in_vmem],
        out_specs=in_vmem,
        out_shape=shaped((2, height // 2, tokens), jnp.bfloat16),
        compiler_params=params(40),
        name="turned_rows",
    )(place.scalars, left)


def attention_grads_kernel(where, *refs, rows, groups, extra):
    turned, right_ref, *refs = refs
    *more, own, sent, kept = refs
    core, grp = where[0], where[2]
    chips = turned.shape[1] // rows
    step = pl.program_id(0)

    def scatter(lefts, right, at, cols):
        for ref, side in ((sent, 1), (own, 0)):
            part = mxu(lefts[side], right, NN).astype(jnp.bfloat16)
            for g in range(groups):
                pos = position(grp ^ g, core ^ side)
                block = part[:, g * cols : (g + 1) * cols].reshape(chips, rows, cols)
                ref[pos, :, 0:rows, pl.ds(at, cols)] = block

    skip = 0
    if not extra:
        other_left, other_right = more
        skip = other_right.shape[1] // groups

        @pl.when(step == 0)
        def _():
            keep_rows(core, other_left, rows, kept)
            scatter(kept, other_right[...], 0, skip)

    cols = right_ref.shape[2] // groups
    scatter(turned, right_ref[0], pl.multiple_of(skip + step * cols, LANES), cols)

    if extra:

        @pl.when(step == 2)
        def _():
            blank = jnp.zeros((extra, own.shape[3]), jnp.bfloat16)
            for ref, side in ((sent, 1), (own, 0)):
                for k in range(chips):
                    lines = vector_sums(2 * k + (core ^ side), *more)
                    for g in range(groups):
                        pos = position(grp ^ g, core ^ side)
                        ref[pos, k, rows : rows + extra, :] = blank
                        for n in range(3):
                            ref[pos, k, rows : rows + 1, n * LANES : (n + 1) * LANES] = lines[
                                3 * g + n
                            ].astype(jnp.bfloat16)


def vector_sums(shard, a_ref, b_ref, one_ref, two_ref, inner_ref):
    half = a_ref.shape[1]
    start = shard * LANES

    def part(ref, start):
        return ref[:, pl.ds(pl.multiple_of(start, LANES), LANES)]

    late = jnp.where(
        start < half,
        part(a_ref, jnp.minimum(start, half - LANES)),
        part(b_ref, jnp.maximum(start - half, 0)),
    )
    one, two = part(one_ref, start), part(two_ref, start)
    lines = [None] * 12
    lines[B_QUERY], lines[B_VALUE] = late[0:1], late[1:2]
    lines[GAIN_ONE], lines[SHIFT_ONE], lines[B_ATTN] = one[0:1], one[1:2], one[2:3]
    lines[GAIN_TWO], lines[SHIFT_TWO], lines[B_OUT] = two[0:1], two[1:2], two[2:3]
    for n in range(4):
        lines[B_IN + n] = part(inner_ref, (4 * shard + n) * LANES)
    return lines


def position(distance, core):
    slot = turn(distance, core)
    return jnp.where(slot == 0, 2, jnp.where(slot == 1, 0, jnp.where(slot == 3, 1, 3)))


def attention_grads(place, turned, right, more, name):
    height, tokens = 2 * turned.shape[1], turned.shape[2]
    groups, chips = place.groups, place.chips
    rows = height // place.shards
    extra = 16 if len(more) > 2 else 0
    size = right.shape[2]
    cols = 3 * size // groups + (0 if extra else more[1].shape[1] // groups)
    shape = (groups, chips, rows + extra, cols)
    once = [
        pl.BlockSpec(x.shape, lambda i, s: (0, 0), pipeline_mode=pl.Buffered(1)) for x in more
    ]
    return pl.pallas_call(
        functools.partial(attention_grads_kernel, rows=rows, groups=groups, extra=extra),
        grid_spec=pltpu.PrefetchScalarGridSpec(
            num_scalar_prefetch=1,
            grid=(3,),
            in_specs=[
                pl.BlockSpec(turned.shape, lambda i, s: (0, 0, 0), pipeline_mode=pl.Buffered(1)),
                pl.BlockSpec((1, tokens, size), lambda i, s: (i, 0, 0)),
            ]
            + once,
            out_specs=[pl.BlockSpec(shape, lambda i, s: (0, 0, 0, 0))] * 2,
            scratch_shapes=[pltpu.VMEM((8, LANES) if extra else turned.shape, jnp.bfloat16)],
        ),
        out_shape=[shaped(shape, jnp.bfloat16)] * 2,
        compiler_params=params(60),
        cost_estimate=cost(2 * tokens * height * cols * groups),
        name="wgrad_" + name,
    )(place.scalars, turned, right, *more)


def weight_grad(place, left, right, split, name):
    tokens, height = left.shape
    groups, chips = place.groups, place.chips
    rows = height // place.shards
    step_chips = chips if split else max(1, 1024 // (2 * rows))
    cols = right.shape[1] // groups
    if split:
        grid = (1, groups)
        block = lambda i, j, s: (0, s[2] ^ turn(ordered_slot(j), s[0]))
        right_spec = pl.BlockSpec((tokens, cols), block)
        one = (1, chips, rows, cols)
        other = lambda j: jnp.where(j == 0, 3, jnp.where(j == 3, 0, j))
        out_specs = [
            pl.BlockSpec(one, lambda i, j, s: (j, 0, 0, 0)),
            pl.BlockSpec(one, lambda i, j, s: (other(j), 0, 0, 0)),
        ]
    else:
        grid = (chips // step_chips, 1)
        right_spec = pl.BlockSpec(right.shape, lambda i, j, s: (0, 0))
        out_specs = [
            pl.BlockSpec((groups, step_chips, rows, cols), lambda i, j, s: (0, i, 0, 0))
        ] * 2
    return pl.pallas_call(
        functools.partial(weight_grad_kernel, rows=rows, groups=groups, split=split),
        grid_spec=pltpu.PrefetchScalarGridSpec(
            num_scalar_prefetch=1,
            grid=grid,
            in_specs=[
                pl.BlockSpec((tokens, step_chips * 2 * rows), lambda i, j, s: (0, i)),
                right_spec,
            ],
            out_specs=out_specs,
            scratch_shapes=[pltpu.VMEM((2, step_chips * rows, tokens), jnp.bfloat16)],
        ),
        out_shape=[shaped((groups, chips, rows, cols), jnp.bfloat16)] * 2,
        compiler_params=params(60),
        cost_estimate=cost(2 * tokens * height * cols * groups),
        name="wgrad_" + name,
    )(place.scalars, left, right)


def add(*terms):
    total = terms[0].astype(jnp.float32)
    for term in terms[1:]:
        total = total + term.astype(jnp.float32)
    return total.astype(jnp.bfloat16)


class Reduction:
    def __init__(self, place, made):
        self.place = place
        self.made, sent = made
        self.flying = place.swap_core(sent)

    def near(self):
        self.core = self.flying
        leave = add(self.made[:2], self.core[:2])
        self.flying = self.place.swap_grp(leave, 0)
        return leave

    def middle(self):
        self.first = self.flying
        second = add(self.made[3], self.core[3], self.first[1])
        self.flying = self.place.swap_grp(second, 1)
        return second

    def column(self):
        mine = add(self.made[2], self.core[2], self.first[0], self.flying)
        return mine, lambda chip: lax.dynamic_index_in_dim(mine, chip, 0, False)

    def along(self):
        place = self.place
        mine, at = self.column()
        self.mine = [at(place.slot_chip(slot)) for slot in range(4)]
        both = jnp.stack([self.mine[1], self.mine[3]])
        self.flying = place.swap_chip(both, 0)
        return both

    def along_far(self):
        self.first = self.flying
        second = add(self.mine[2], self.first[1])
        self.flying = self.place.swap_chip(second, 1)
        return second

    def share(self):
        return add(self.mine[0], self.first[0], self.flying)

    def along_direct(self):
        place = self.place
        mine, at = self.column()
        self.mine = at(place.chip)
        self.flying = tuple(
            place.permute(at(place.chip ^ k), (2 * k, 2 * k)) for k in range(place.chips - 1, 0, -1)
        )
        return mine

    def share_direct(self):
        return add(self.mine, *self.flying)


class Replication:
    def __init__(self, place, share, direct=False):
        self.place = place
        self.blocks = [share] + [None] * 3
        if direct:
            size = place.shards
            for mask in (3, 1, 2):
                self.blocks[mask] = place.permute(share, (mask * size, mask * size))
        else:
            self.flying = place.swap_grp(share, 0)

    def far(self):
        pair = jnp.stack([self.blocks[0], self.flying])
        self.blocks[1] = self.flying
        self.flying = self.place.swap_grp(pair, 1)
        return pair

    def landed(self):
        if self.blocks[2] is None:
            self.blocks[2:] = [self.flying[0], self.flying[1]]
        return self.blocks


def order_feed_forward(place, blocks, rows_in):
    groups = place.groups
    height, cols = blocks[0].shape
    rows_out = height - groups * rows_in

    def kernel(where, *refs):
        *blocks, out_ref, in_ref = refs
        for slot, ref in enumerate(blocks):
            g = where[2] ^ turn(slot, where[0])
            at = pl.multiple_of(g * cols, LANES)
            out_ref[:, pl.ds(at, cols)] = ref[0:rows_out, :].astype(jnp.float32)
            for n in range(groups):
                at = pl.multiple_of((g * groups + n) * cols, LANES)
                part = ref[rows_out + n * rows_in : rows_out + (n + 1) * rows_in, :]
                in_ref[:, pl.ds(at, cols)] = part.astype(jnp.float32)

    in_vmem = pl.BlockSpec(memory_space=pltpu.VMEM)
    return pl.pallas_call(
        kernel,
        in_specs=[pl.BlockSpec(memory_space=pltpu.SMEM)] + [in_vmem] * groups,
        out_specs=[in_vmem] * 2,
        out_shape=[
            shaped((rows_out, groups * cols), jnp.float32),
            shaped((rows_in, groups * groups * cols), jnp.float32),
        ],
        compiler_params=params(40),
        cost_estimate=cost(height * cols * 1024),
        name="order_feed_forward",
    )(place.scalars, *blocks)


def order_attention(place, blocks_a, blocks_b, rows):
    groups = place.groups
    size = blocks_b[0].shape[1] // 3
    skip = blocks_a[0].shape[1] - 3 * size
    width = groups * skip

    def kernel(where, *refs):
        *blocks, attn_ref, qkv_ref, small_ref = refs
        for n in range(groups):
            ref = blocks[n]
            g = where[2] ^ turn(n, where[0])
            attn_ref[:, pl.ds(pl.multiple_of(g * skip, LANES), skip)] = ref[:, 0:skip].astype(
                jnp.float32
            )
            for part in range(3):
                at = pl.multiple_of(part * width + g * size, LANES)
                block = ref[:, skip + part * size : skip + (part + 1) * size]
                qkv_ref[:, pl.ds(at, size)] = block.astype(jnp.float32)
        for n in range(groups):
            ref = blocks[groups + n]
            g = where[2] ^ n
            lines = []
            for part in range(3):
                at = pl.multiple_of(part * width + width // 2 + g * size, LANES)
                here = slice(part * size, (part + 1) * size)
                qkv_ref[:, pl.ds(at, size)] = ref[0:rows, here].astype(jnp.float32)
                lines.append(ref[rows : rows + 16, here].astype(jnp.float32)[0:1])
            lines.append(jnp.zeros((5, size), jnp.float32))
            small_ref[pl.ds(pl.multiple_of(g * 8, 8), 8), :] = jnp.concatenate(lines)

    in_vmem = pl.BlockSpec(memory_space=pltpu.VMEM)
    return pl.pallas_call(
        kernel,
        in_specs=[pl.BlockSpec(memory_space=pltpu.SMEM)] + [in_vmem] * (2 * groups),
        out_specs=[in_vmem] * 3,
        out_shape=[
            shaped((rows, width), jnp.float32),
            shaped((rows, 3 * width), jnp.float32),
            shaped((8 * groups, size), jnp.float32),
        ],
        compiler_params=params(40),
        name="order_attention",
    )(place.scalars, *blocks_a, *blocks_b)


def on_device_permutes(
    tokens,
    segment_ids,
    keep_flag,
    cotangent,
    w_qkv,
    b_query,
    b_value,
    w_attn_out,
    b_attn_out,
    norm1_gain,
    norm1_bias,
    w_in,
    b_in,
    w_out,
    b_out,
    norm2_gain,
    norm2_bias,
    *,
    groups,
    shards,
):
    place = Place(groups, shards)
    _, length, width = tokens.shape
    rows = tokens[0]
    seg_row = segment_ids.reshape(1, length)
    pairs = width // LANES

    c1 = Gather(place, w_qkv)
    c2 = Gather(place, jnp.concatenate([w_in, w_attn_out], 1))
    c3 = Gather(place, w_out)
    c1.chips_near()
    small = Vectors(
        place,
        (b_query, b_value, b_attn_out, norm1_gain, norm1_bias, b_out, norm2_gain, norm2_bias, b_in),
    )
    meet(rows, c1, small)
    pair = c1.chips_far()
    small.chips_near()
    meet(pair, c1, small)
    joined = c1.join()
    c1.near()
    small.chips_far()
    c2.chips_near(joined)
    meet(joined, c2, small)
    small.landed()
    pair = c2.chips_far()
    vectors, bias_in, qkv_bias, seg_col, keep = small.unpack(
        seg_row, keep_flag.reshape(1, length)
    )
    c1.flying = lax.optimization_barrier(c1.flying)
    turned = turned_rows(place, after(rows, vectors))
    c1.far(pair, vectors)
    c1.cross(0, 1, 2)
    joined = c2.join()
    meet((joined, turned), c1)
    c1.landed()
    c2.near(c1.held[3])
    c1.cross(3)
    c3.chips_near(c1.held[3])
    blank = jnp.ones((1, width), jnp.float32)
    qkv_scale = jnp.concatenate([blank / math.sqrt(HD), blank, blank], 1)

    mixed, full_qkv = project_qkv(place, rows, Window(c1, 0, w_qkv.shape[1]), qkv_bias, qkv_scale)
    meet(mixed, c3)
    pair = c3.chips_far()
    c2.cross(0, wait=(mixed,))
    first, second = pairs * 3 // 8, pairs * 3 // 4
    forward = attention_forward(after(mixed, pair), seg_col, seg_row, 0, first)
    meet(forward[0], c2, c3)
    c2.far()
    joined = c3.join()
    c3.near()
    c2.cross(1, 2)
    forward = attention_forward(
        after(mixed, joined), seg_col, seg_row, first, second - first, forward
    )
    meet(forward[0], c2)
    c2.landed()
    c2.cross(3)
    contexts, probs, probs_scale = attention_forward(
        after(mixed, c2.held[3]), seg_col, seg_row, second, pairs - second, forward
    )
    normed, scale_one, normed_low, full_attn = project_out(
        place, contexts, Window(c2, w_in.shape[1], w_attn_out.shape[1]), rows, vectors
    )
    meet(normed_low, c3)
    c3.far()
    c3.cross(0, 1, 2)
    hidden, slope, full_in = feed_in(
        place, after(normed_low, c3.held[1]), Window(c2, 0, w_in.shape[1]), bias_in
    )
    meet(hidden, c3)
    c3.landed()
    c3.cross(3)
    layer_out, second_grad, out_low, second_sums, pre_low, bias_in_grad = feed_out(
        place, hidden, Window(c3, 0, w_out.shape[1]), normed, cotangent[0], keep, vectors, slope
    )

    r_out = Reduction(place, weight_grad(place, hidden, out_low, False, "out"))
    r_in = Reduction(place, weight_grad(place, after(normed_low, r_out.made), pre_low, True, "in"))
    meet(r_in.made, r_out)
    step = r_out.near()
    first_grad, attn_low, context_grad, first_sums = feed_in_back(
        after(pre_low, r_in.made, step), full_in, second_grad, normed, scale_one, vectors, full_attn
    )
    meet(attn_low, r_in)
    step = r_in.near()
    half, quarter = pairs // 2, pairs // 4

    def back(wait, start, count, at, before=None):
        return attention_backward(
            mixed,
            contexts,
            after(context_grad, *wait),
            probs,
            probs_scale,
            start,
            count,
            at,
            half,
            before,
        )

    low_a, late_a = back((step,), 0, half, 0)
    meet(late_a, r_out, r_in)
    steps = (r_out.middle(), r_in.middle())
    r_a = Reduction(
        place, attention_grads(place, after(turned, *steps), low_a, (contexts, attn_low), "a")
    )
    meet(r_a.made, r_out)
    step = r_out.along()
    part = back((r_a.made, step), half, quarter, 0)
    meet(part[1], r_out, r_in, r_a)
    steps = (r_out.along_far(), r_in.along(), r_a.near())
    low_b, late_b = back(steps, half + quarter, quarter, quarter, part)
    meet(late_b, r_out, r_in, r_a)
    sums = (late_a, late_b, first_sums, second_sums, bias_in_grad)
    share_out = r_out.share()
    steps = (r_in.along_far(), r_a.middle(), share_out)
    r_b = Reduction(place, attention_grads(place, after(turned, *steps), low_b, sums, "b"))
    meet(r_b.made, r_in, r_a)
    share_in = r_in.share()
    inner = share_in.shape[1] // groups
    joined = jnp.concatenate(
        [share_out] + [share_in[:, n * inner : (n + 1) * inner] for n in range(groups)]
    )
    all_ffn = Replication(place, joined)
    grads = (low_a, after(low_b, r_b.made, joined, r_a.along()))
    tiles = length // TILE // 2
    input_grad = project_qkv_back(grads, full_qkv, first_grad, 0, tiles)
    meet(input_grad, r_b, r_a, all_ffn)
    steps = (r_b.near(), r_a.along_far())
    input_grad = project_qkv_back(
        grads, full_qkv, after(first_grad, *steps), tiles, tiles, input_grad
    )
    meet(input_grad, r_b, r_a)
    middle = r_b.middle()
    r_a.flying = after(r_a.flying, middle)
    all_a = Replication(place, r_a.share())
    meet(all_a.blocks[0], r_b, all_a)
    along = r_b.along_direct()
    all_a.flying = after(all_a.flying, along)
    all_ffn.flying = after(all_ffn.flying, along)
    pairs_made = (all_a.far(), all_ffn.far())
    meet(pairs_made, r_b)
    share_b = r_b.share_direct()
    all_b = Replication(place, share_b, direct=True)
    meet(share_b, all_ffn)
    w_out_grad, w_in_grad = order_feed_forward(place, all_ffn.landed(), share_in.shape[0])
    all_a.flying = after(all_a.flying, w_out_grad)
    w_attn_grad, w_qkv_grad, small = order_attention(
        place, all_a.landed(), all_b.landed(), w_attn_out.shape[0]
    )
    small = [small[8 * (n // 3) + n % 3] for n in range(12)]
    return (
        layer_out[None],
        input_grad[None],
        w_qkv_grad,
        small[B_QUERY],
        small[B_VALUE],
        w_attn_grad,
        small[B_ATTN],
        small[GAIN_ONE],
        small[SHIFT_ONE],
        w_in_grad,
        jnp.concatenate(small[B_IN:]),
        w_out_grad,
        small[B_OUT],
        small[GAIN_TWO],
        small[SHIFT_TWO],
    )


def solution(mesh):
    groups, shards = mesh.shape["grp"], mesh.shape["shard"]
    if groups == 4 and shards == 8:
        body = functools.partial(on_device_permutes, groups=groups, shards=shards)
    else:
        body = on_device
    return jax.shard_map(
        body,
        mesh=mesh,
        in_specs=(
            P(("grp", "shard"), None, None),
            P(("grp", "shard"), None),
            P(("grp", "shard"), None),
            P(("grp", "shard"), None, None),
            P("shard", "grp"),
            P("shard"),
            P("shard"),
            P("shard", "grp"),
            P("shard"),
            P("shard"),
            P("shard"),
            P("shard", "grp"),
            P("shard"),
            P("shard", "grp"),
            P("shard"),
            P("shard"),
            P("shard"),
        ),
        out_specs=(
            P(("grp", "shard"), None, None),
            P(("grp", "shard"), None, None),
            P("shard", None),
            P("shard"),
            P("shard"),
            P("shard", None),
            P("shard"),
            P("shard"),
            P("shard"),
            P("shard", None),
            P("shard"),
            P("shard", None),
            P("shard"),
            P("shard"),
            P("shard"),
        ),
        check_vma=False,
    )
```

```python
import functools
import math

import jax
import jax.numpy as jnp
from jax import lax
from jax.experimental import pallas as pl
from jax.experimental.pallas import tpu as pltpu
from jax.sharding import PartitionSpec as P

H = 16
HD = 64


masked_score = -1e30
epsilon = 1e-05


def norm_layer(rows, gain_row, shift_row):
    row_mean = jnp.mean(rows, -1, keepdims=True)
    centered = rows - row_mean
    row_var = jnp.mean(centered * centered, -1, keepdims=True)
    return centered * lax.rsqrt(row_var + epsilon) * gain_row + shift_row


def gelu_exact(values):
    return 0.5 * values * (1.0 + lax.erf(values * (1.0 / math.sqrt(2.0))))


def contract_rows(left, right):
    return lax.dot_general(
        left, right, (((0,), (0,)), ((), ())), preferred_element_type=jnp.float32
    )


def contract_cols(left, right):
    return lax.dot_general(
        left, right, (((1,), (1,)), ((), ())), preferred_element_type=jnp.float32
    )


def attend_forward(queries, key_rows, value_rows, segment_row, block_rows):
    length, model_width = queries.shape
    scaling = 1.0 / math.sqrt(HD)
    key_heads = key_rows.reshape(length, H, HD)
    value_heads = value_rows.reshape(length, H, HD)
    query_blocks = queries.reshape(length // block_rows, block_rows, H, HD)
    segment_blocks = segment_row.reshape(length // block_rows, block_rows)

    def one_block(pieces):
        query_part, segment_part = pieces
        scores = (
            jnp.einsum("qhd,khd->hqk", query_part, key_heads, preferred_element_type=jnp.float32)
            * scaling
        )
        allowed = segment_part[:, None] == segment_row[None, :]
        scores = jnp.where(allowed[None], scores, masked_score)
        row_max = jnp.max(scores, -1, keepdims=True)
        powers = jnp.exp(scores - row_max)
        totals = jnp.sum(powers, -1, keepdims=True)
        attn_probs = (powers / totals).astype(jnp.bfloat16)
        context = jnp.einsum(
            "hqk,khd->qhd", attn_probs, value_heads, preferred_element_type=jnp.float32
        )
        return (
            context.reshape(block_rows, model_width).astype(jnp.bfloat16),
            (row_max + jnp.log(totals))[:, :, 0],
        )

    contexts, log_sums = lax.map(one_block, (query_blocks, segment_blocks))
    return (contexts.reshape(length, model_width), log_sums)


def attend_backward(queries, key_rows, value_rows, segment_row, log_sums, context_grad, block_rows):
    length, model_width = queries.shape
    scaling = 1.0 / math.sqrt(HD)
    key_heads = key_rows.reshape(length, H, HD)
    value_heads = value_rows.reshape(length, H, HD)
    query_blocks = queries.reshape(length // block_rows, block_rows, H, HD)
    segment_blocks = segment_row.reshape(length // block_rows, block_rows)
    grad_blocks = context_grad.reshape(length // block_rows, block_rows, H, HD)

    def one_block(running, pieces):
        key_acc, value_acc = running
        query_part, segment_part, lse_part, grad_part = pieces
        scores = (
            jnp.einsum("qhd,khd->hqk", query_part, key_heads, preferred_element_type=jnp.float32)
            * scaling
        )
        allowed = segment_part[:, None] == segment_row[None, :]
        scores = jnp.where(allowed[None], scores, masked_score)
        probs = jnp.exp(scores - lse_part[:, :, None])
        prob_low = probs.astype(jnp.bfloat16)
        prob_grad = jnp.einsum(
            "qhd,khd->hqk", grad_part, value_heads, preferred_element_type=jnp.float32
        )
        row_dot = jnp.sum(prob_grad * probs, -1, keepdims=True)
        score_grad = (probs * (prob_grad - row_dot)).astype(jnp.bfloat16)
        query_grad = (
            jnp.einsum("hqk,khd->qhd", score_grad, key_heads, preferred_element_type=jnp.float32)
            * scaling
        )
        key_acc = (
            key_acc
            + jnp.einsum("hqk,qhd->khd", score_grad, query_part, preferred_element_type=jnp.float32)
            * scaling
        )
        value_acc = value_acc + jnp.einsum(
            "hqk,qhd->khd", prob_low, grad_part, preferred_element_type=jnp.float32
        )
        return ((key_acc, value_acc), query_grad.reshape(block_rows, model_width))

    empty_acc = jnp.zeros((length, H, HD), jnp.float32)
    (key_grad, value_grad), query_grads = lax.scan(
        one_block, (empty_acc, empty_acc), (query_blocks, segment_blocks, log_sums, grad_blocks)
    )
    return (
        query_grads.reshape(length, model_width),
        key_grad.reshape(length, model_width),
        value_grad.reshape(length, model_width),
    )


def on_device(
    tokens,
    segment_ids,
    keep_flag,
    cotangent,
    w_qkv,
    b_query,
    b_value,
    w_attn_out,
    b_attn_out,
    norm1_gain,
    norm1_bias,
    w_in,
    b_in,
    w_out,
    b_out,
    norm2_gain,
    norm2_bias,
):
    seq_count, length, model_width = tokens.shape
    block_rows = min(512, length)
    within = (
        lax.all_gather(w_qkv, "shard", axis=0, tiled=True),
        lax.all_gather(w_attn_out, "shard", axis=0, tiled=True),
        lax.all_gather(w_in, "shard", axis=0, tiled=True),
        lax.all_gather(w_out, "shard", axis=0, tiled=True),
        lax.all_gather(b_query, "shard", axis=0, tiled=True),
        lax.all_gather(b_value, "shard", axis=0, tiled=True),
        lax.all_gather(b_attn_out, "shard", axis=0, tiled=True),
        lax.all_gather(norm1_gain, "shard", axis=0, tiled=True),
        lax.all_gather(norm1_bias, "shard", axis=0, tiled=True),
        lax.all_gather(b_in, "shard", axis=0, tiled=True),
        lax.all_gather(b_out, "shard", axis=0, tiled=True),
        lax.all_gather(norm2_gain, "shard", axis=0, tiled=True),
        lax.all_gather(norm2_bias, "shard", axis=0, tiled=True),
    )
    full_qkv, full_attn, full_in, full_out = (
        lax.all_gather(within[0], "grp", axis=1, tiled=True),
        lax.all_gather(within[1], "grp", axis=1, tiled=True),
        lax.all_gather(within[2], "grp", axis=1, tiled=True),
        lax.all_gather(within[3], "grp", axis=1, tiled=True),
    )
    (
        bias_query,
        bias_value,
        bias_attn,
        gain_one,
        shift_one,
        bias_in,
        bias_out,
        gain_two,
        shift_two,
    ) = [piece.astype(jnp.float32) for piece in within[4:]]
    flat_rows = tokens.reshape(seq_count * length, model_width)
    mixed_qkv = jnp.dot(flat_rows, full_qkv, preferred_element_type=jnp.float32)
    queries = (mixed_qkv[:, :model_width] + bias_query).astype(jnp.bfloat16)
    key_rows = mixed_qkv[:, model_width : 2 * model_width].astype(jnp.bfloat16)
    value_rows = (mixed_qkv[:, 2 * model_width :] + bias_value).astype(jnp.bfloat16)
    query_seqs = queries.reshape(seq_count, length, model_width)
    key_seqs = key_rows.reshape(seq_count, length, model_width)
    value_seqs = value_rows.reshape(seq_count, length, model_width)

    def forward_sequence(pieces):
        return attend_forward(pieces[0], pieces[1], pieces[2], pieces[3], block_rows)

    contexts, log_sums = lax.map(forward_sequence, (query_seqs, key_seqs, value_seqs, segment_ids))
    contexts = contexts.reshape(seq_count * length, model_width)
    attended = jnp.dot(contexts, full_attn, preferred_element_type=jnp.float32) + bias_attn
    first_sum = flat_rows.astype(jnp.float32) + attended
    normed_one, norm_one_back = jax.vjp(norm_layer, first_sum, gain_one, shift_one)
    normed_low = normed_one.astype(jnp.bfloat16)
    hidden_pre = jnp.dot(normed_low, full_in, preferred_element_type=jnp.float32) + bias_in
    hidden, gelu_back = jax.vjp(gelu_exact, hidden_pre)
    hidden_low = hidden.astype(jnp.bfloat16)
    second_sum = normed_one + (
        jnp.dot(hidden_low, full_out, preferred_element_type=jnp.float32) + bias_out
    )
    result, norm_two_back = jax.vjp(norm_layer, second_sum, gain_two, shift_two)
    layer_out = result.astype(jnp.bfloat16).reshape(seq_count, length, model_width)
    again = (
        lax.all_gather(w_qkv, "shard", axis=0, tiled=True),
        lax.all_gather(w_attn_out, "shard", axis=0, tiled=True),
        lax.all_gather(w_in, "shard", axis=0, tiled=True),
        lax.all_gather(w_out, "shard", axis=0, tiled=True),
    )
    back_qkv, back_attn, back_in, back_out = (
        lax.all_gather(again[0], "grp", axis=1, tiled=True),
        lax.all_gather(again[1], "grp", axis=1, tiled=True),
        lax.all_gather(again[2], "grp", axis=1, tiled=True),
        lax.all_gather(again[3], "grp", axis=1, tiled=True),
    )
    masked_cot = cotangent.astype(jnp.float32).reshape(
        seq_count * length, model_width
    ) * keep_flag.reshape(seq_count * length, 1).astype(jnp.float32)
    second_grad, gain_two_grad, shift_two_grad = norm_two_back(masked_cot)
    bias_out_grad = jnp.sum(second_grad, 0)
    out_low = second_grad.astype(jnp.bfloat16)
    w_out_grad = contract_rows(hidden_low, out_low)
    hidden_grad = contract_cols(out_low, back_out)
    (pre_grad,) = gelu_back(hidden_grad)
    bias_in_grad = jnp.sum(pre_grad, 0)
    pre_low = pre_grad.astype(jnp.bfloat16)
    w_in_grad = contract_rows(normed_low, pre_low)
    normed_grad = second_grad + contract_cols(pre_low, back_in)
    first_grad, gain_one_grad, shift_one_grad = norm_one_back(normed_grad)
    bias_attn_grad = jnp.sum(first_grad, 0)
    attn_low = first_grad.astype(jnp.bfloat16)
    w_attn_grad = contract_rows(contexts, attn_low)
    context_grad = contract_cols(attn_low, back_attn).astype(jnp.bfloat16)

    def backward_sequence(pieces):
        return attend_backward(
            pieces[0], pieces[1], pieces[2], pieces[3], pieces[4], pieces[5], block_rows
        )

    query_grad, key_grad, value_grad = lax.map(
        backward_sequence,
        (
            query_seqs,
            key_seqs,
            value_seqs,
            segment_ids,
            log_sums,
            context_grad.reshape(seq_count, length, model_width),
        ),
    )
    query_grad = query_grad.reshape(seq_count * length, model_width)
    key_grad = key_grad.reshape(seq_count * length, model_width)
    value_grad = value_grad.reshape(seq_count * length, model_width)
    bias_query_grad = jnp.sum(query_grad, 0)
    bias_value_grad = jnp.sum(value_grad, 0)
    qkv_low = jnp.concatenate([query_grad, key_grad, value_grad], 1).astype(jnp.bfloat16)
    w_qkv_grad = contract_rows(flat_rows, qkv_low)
    input_grad = first_grad + contract_cols(qkv_low, back_qkv)
    reduced = (
        lax.psum_scatter(
            w_qkv_grad.astype(jnp.bfloat16), "shard", scatter_dimension=0, tiled=True
        ).astype(jnp.float32),
        lax.psum_scatter(
            bias_query_grad.astype(jnp.bfloat16), "shard", scatter_dimension=0, tiled=True
        ).astype(jnp.float32),
        lax.psum_scatter(
            bias_value_grad.astype(jnp.bfloat16), "shard", scatter_dimension=0, tiled=True
        ).astype(jnp.float32),
        lax.psum_scatter(
            w_attn_grad.astype(jnp.bfloat16), "shard", scatter_dimension=0, tiled=True
        ).astype(jnp.float32),
        lax.psum_scatter(
            bias_attn_grad.astype(jnp.bfloat16), "shard", scatter_dimension=0, tiled=True
        ).astype(jnp.float32),
        lax.psum_scatter(
            gain_one_grad.astype(jnp.bfloat16), "shard", scatter_dimension=0, tiled=True
        ).astype(jnp.float32),
        lax.psum_scatter(
            shift_one_grad.astype(jnp.bfloat16), "shard", scatter_dimension=0, tiled=True
        ).astype(jnp.float32),
        lax.psum_scatter(
            w_in_grad.astype(jnp.bfloat16), "shard", scatter_dimension=0, tiled=True
        ).astype(jnp.float32),
        lax.psum_scatter(
            bias_in_grad.astype(jnp.bfloat16), "shard", scatter_dimension=0, tiled=True
        ).astype(jnp.float32),
        lax.psum_scatter(
            w_out_grad.astype(jnp.bfloat16), "shard", scatter_dimension=0, tiled=True
        ).astype(jnp.float32),
        lax.psum_scatter(
            bias_out_grad.astype(jnp.bfloat16), "shard", scatter_dimension=0, tiled=True
        ).astype(jnp.float32),
        lax.psum_scatter(
            gain_two_grad.astype(jnp.bfloat16), "shard", scatter_dimension=0, tiled=True
        ).astype(jnp.float32),
        lax.psum_scatter(
            shift_two_grad.astype(jnp.bfloat16), "shard", scatter_dimension=0, tiled=True
        ).astype(jnp.float32),
    )
    summed = (
        lax.psum(reduced[0].astype(jnp.bfloat16), "grp").astype(jnp.float32),
        lax.psum(reduced[1].astype(jnp.bfloat16), "grp").astype(jnp.float32),
        lax.psum(reduced[2].astype(jnp.bfloat16), "grp").astype(jnp.float32),
        lax.psum(reduced[3].astype(jnp.bfloat16), "grp").astype(jnp.float32),
        lax.psum(reduced[4].astype(jnp.bfloat16), "grp").astype(jnp.float32),
        lax.psum(reduced[5].astype(jnp.bfloat16), "grp").astype(jnp.float32),
        lax.psum(reduced[6].astype(jnp.bfloat16), "grp").astype(jnp.float32),
        lax.psum(reduced[7].astype(jnp.bfloat16), "grp").astype(jnp.float32),
        lax.psum(reduced[8].astype(jnp.bfloat16), "grp").astype(jnp.float32),
        lax.psum(reduced[9].astype(jnp.bfloat16), "grp").astype(jnp.float32),
        lax.psum(reduced[10].astype(jnp.bfloat16), "grp").astype(jnp.float32),
        lax.psum(reduced[11].astype(jnp.bfloat16), "grp").astype(jnp.float32),
        lax.psum(reduced[12].astype(jnp.bfloat16), "grp").astype(jnp.float32),
    )
    return (
        layer_out,
        input_grad.reshape(seq_count, length, model_width),
        summed[0],
        summed[1],
        summed[2],
        summed[3],
        summed[4],
        summed[5],
        summed[6],
        summed[7],
        summed[8],
        summed[9],
        summed[10],
        summed[11],
        summed[12],
    )


NT = (((1,), (1,)), ((), ()))
NN = (((1,), (0,)), ((), ()))
TN = (((0,), (0,)), ((), ()))
LANES = 128
AXES = ("grp", "shard")


def mxu(left, right, dims):
    return lax.dot_general(left, right, dims, preferred_element_type=jnp.float32)


def cost(flops):
    return pl.CostEstimate(flops=2 * flops, bytes_accessed=0, transcendentals=0)


def params(megabytes=60):
    return pltpu.CompilerParams(vmem_limit_bytes=megabytes << 20)


def attention_forward_kernel(q_ref, k_ref, v_ref, seg_col, seg_row, out_ref, probs_ref, scale_ref, *, rows):
    length = q_ref.shape[0]
    first = lax.broadcasted_iota(jnp.int32, (1, LANES), 1) < HD
    keys = k_ref[...]
    values = v_ref[...]
    zero = jnp.zeros_like(keys)
    head_keys = (jnp.where(first, keys, zero), jnp.where(first, zero, keys))
    key_segments = seg_col[...]
    for block in range(length // rows):
        here = pl.ds(block * rows, rows)
        q = q_ref[here, :]
        allowed = key_segments == seg_row[:, here]
        outs, scales = [], []
        for head in range(2):
            scores = mxu(head_keys[head], q, NT)
            scores = jnp.where(allowed, scores, masked_score)
            powers = jnp.exp(scores - jnp.max(scores, 0, keepdims=True))
            scale = 1.0 / jnp.sum(powers, 0, keepdims=True)
            scales.append(jnp.broadcast_to(scale, (HD, rows)))
            powers = powers.astype(jnp.bfloat16)
            probs_ref[head, :, here] = powers
            outs.append(mxu(powers, values, TN))
        scale = jnp.transpose(jnp.concatenate(scales))
        scale_ref[here, :] = scale
        out_ref[here, :] = (jnp.where(first, outs[0], outs[1]) * scale).astype(jnp.bfloat16)


def attention_forward(qkv, seg_col, seg_row, start, pairs, before=None):
    length, width = qkv.shape[0], qkv.shape[1] // 3
    total = width // LANES
    rows = min(512, length)
    more = () if before is None else before

    def pair(part):
        return pl.BlockSpec((length, LANES), lambda j: (0, part * total + start + j))

    def body(q_ref, k_ref, v_ref, seg_c, seg_r, *refs):
        attention_forward_kernel(q_ref, k_ref, v_ref, seg_c, seg_r, *refs[-3:], rows=rows)

    return pl.pallas_call(
        body,
        grid=(pairs,),
        in_specs=[
            pair(0),
            pair(1),
            pair(2),
            pl.BlockSpec((length, 1), lambda j: (0, 0)),
            pl.BlockSpec((1, length), lambda j: (0, 0)),
        ]
        + [pl.BlockSpec(memory_space=pl.ANY)] * len(more),
        out_specs=[
            pl.BlockSpec((length, LANES), lambda j: (0, start + j)),
            pl.BlockSpec((2, length, length), lambda j: (start + j, 0, 0)),
            pl.BlockSpec((length, LANES), lambda j: (0, start + j)),
        ],
        out_shape=[
            jax.ShapeDtypeStruct((length, width), jnp.bfloat16),
            jax.ShapeDtypeStruct((2 * total, length, length), jnp.bfloat16),
            jax.ShapeDtypeStruct((length, width), jnp.float32),
        ],
        input_output_aliases={} if before is None else {5: 0, 6: 1, 7: 2},
        compiler_params=params(60),
        cost_estimate=cost(16 * length * length * pairs * LANES),
        name="attn_fwd",
    )(qkv, qkv, qkv, seg_col, seg_row, *more)


def attention_backward_kernel(
    q_ref, k_ref, v_ref, o_ref, do_ref, probs_ref, scale_ref, grad_ref, sum_ref
):
    first = lax.broadcasted_iota(jnp.int32, (1, LANES), 1) < HD
    pick = (
        lax.broadcasted_iota(jnp.int32, (8, LANES), 0)
        == lax.broadcasted_iota(jnp.int32, (8, LANES), 1) // HD
    ).astype(jnp.bfloat16)
    q = q_ref[...]
    scaled = do_ref[...].astype(jnp.float32) * scale_ref[...]
    do = scaled.astype(jnp.bfloat16)
    keys = k_ref[...]
    values = v_ref[...]
    zero = jnp.zeros_like(values)
    head_values = (jnp.where(first, values, zero), jnp.where(first, zero, values))
    products = scaled * o_ref[...].astype(jnp.float32)
    high = products.astype(jnp.bfloat16)
    low = (products - high.astype(jnp.float32)).astype(jnp.bfloat16)
    dots = mxu(pick, high, NT) + mxu(pick, low, NT)
    query_parts, key_parts, value_parts = [], [], []
    for head in range(2):
        probs = probs_ref[head]
        prob_grad = mxu(head_values[head], do, NT)
        score_grad = probs.astype(jnp.float32) * (prob_grad - dots[head : head + 1, :])
        score_grad = score_grad.astype(jnp.bfloat16)
        value_parts.append(mxu(probs, do, NN))
        key_parts.append(mxu(score_grad, q, NN))
        query_parts.append(mxu(score_grad, keys, TN))
    query_grad = jnp.where(first, *query_parts) * (1.0 / math.sqrt(HD))
    value_grad = jnp.where(first, *value_parts)
    grad_ref[0] = query_grad.astype(jnp.bfloat16)
    grad_ref[1] = jnp.where(first, *key_parts).astype(jnp.bfloat16)
    grad_ref[2] = value_grad.astype(jnp.bfloat16)
    sum_ref[0:1, :] = jnp.sum(query_grad, 0, keepdims=True)
    sum_ref[1:2, :] = jnp.sum(value_grad, 0, keepdims=True)


def attention_backward(qkv, out, out_grad, probs, scale, start, pairs, at, size, before=None):
    length, width = out.shape
    total = width // LANES
    more = () if before is None else before

    def pair(part):
        return pl.BlockSpec((length, LANES), lambda j: (0, part * total + start + j))

    def body(*refs):
        attention_backward_kernel(*refs[:7], *refs[-2:])

    return pl.pallas_call(
        body,
        grid=(pairs,),
        in_specs=[
            pair(0),
            pair(1),
            pair(2),
            pair(0),
            pair(0),
            pl.BlockSpec((2, length, length), lambda j: (start + j, 0, 0)),
            pair(0),
        ]
        + [pl.BlockSpec(memory_space=pl.ANY)] * len(more),
        out_specs=[
            pl.BlockSpec((3, length, LANES), lambda j: (0, 0, j + at)),
            pl.BlockSpec((2, LANES), lambda j: (0, j + at)),
        ],
        out_shape=[
            jax.ShapeDtypeStruct((3, length, size * LANES), jnp.bfloat16),
            jax.ShapeDtypeStruct((2, size * LANES), jnp.float32),
        ],
        input_output_aliases={} if before is None else {7: 0, 8: 1},
        compiler_params=params(60),
        cost_estimate=cost(32 * length * length * pairs * LANES),
        name="attn_bwd",
    )(qkv, qkv, qkv, out, out_grad, probs, scale, *more)


class Place:
    def __init__(self, groups, shards):
        self.groups = groups
        self.shards = shards
        self.chips = shards // 2
        self.grp = lax.axis_index("grp")
        self.shard = lax.axis_index("shard")
        self.core = self.shard % 2
        self.chip = self.shard // 2
        self.scalars = jnp.stack([self.core, self.chip, self.grp]).astype(jnp.int32)

    def permute(self, array, mask_of_core):
        pairs = [(i, i ^ mask_of_core[i % 2]) for i in range(self.groups * self.shards)]
        return lax.ppermute(array, AXES, pairs)

    def swap_core(self, array):
        return self.permute(array, (1, 1))

    def swap_grp(self, array, step):
        masks = (self.shards, 2 * self.shards)
        return self.permute(array, masks if step == 0 else masks[::-1])

    def swap_chip(self, array, step):
        masks = (2, 4)
        return self.permute(array, masks if step == 0 else masks[::-1])

    def slot_chip(self, slot):
        return self.chip ^ turn(slot, self.core)

    def slot_grp(self, slot):
        return self.grp ^ turn(slot, self.core)


def turn(slot, core):
    if isinstance(slot, int):
        return slot if slot in (0, 3) else jnp.where(core == 0, slot, 3 - slot)
    return jnp.where((core == 0) | (slot == 0) | (slot == 3), slot, 3 - slot)


def after(value, *others):
    return lax.optimization_barrier((value, *others))[0]


def meet(anchor, *flights):
    arrays = [f.flying for f in flights]
    _, *arrays = lax.optimization_barrier((anchor, *arrays))
    for f, array in zip(flights, arrays):
        f.flying = array


class Gather:
    def __init__(self, place, piece):
        self.place = place
        self.piece = piece
        self.held = [None] * 4
        self.crossed = [None] * 4

    def chips_near(self, *wait):
        self.piece = after(self.piece, *wait)
        self.flying = self.place.swap_chip(self.piece, 0)

    def chips_far(self):
        self.pair = jnp.stack([self.piece, self.flying])
        self.flying = self.place.swap_chip(self.pair, 1)
        return self.pair

    def join(self):
        self.held[0] = jnp.concatenate([self.pair, self.flying])
        return self.held[0]

    def near(self, *wait):
        self.held[0] = after(self.held[0], *wait)
        self.flying = (self.place.swap_grp(self.held[0], 0), self.place.swap_grp(self.held[0], 1))
        return self.held[0]

    def far(self, *wait):
        self.held[1:3] = self.flying
        first = after(self.held[1], *wait)
        self.flying = self.place.swap_grp(first, 1)

    def landed(self):
        self.held[3] = self.flying

    def cross(self, *which, wait=()):
        for n in which:
            self.crossed[n] = self.place.swap_core(after(self.held[n], *wait))

    def pieces(self):
        return self.held + self.crossed


class Window:
    def __init__(self, gather, start, cols):
        self.arrays = gather.pieces()
        self.start, self.cols = start, cols
        chips, rows, _ = self.arrays[0].shape
        self.chips, self.rows = chips, rows


def fetch(where, window, refs, whole, sem, by):
    rows, cols, chips = window.rows, window.cols, window.chips
    for slot in range(4):
        for side in range(2):
            core = where[0] ^ side
            ref = refs[4 * side + slot]
            distance = turn(slot, core)
            col = pl.multiple_of((where[2] ^ distance) * cols, LANES)
            for k in range(chips):
                row = ((where[1] ^ turn(k, core)) * 2 + core) * rows
                pltpu.make_async_copy(
                    ref.at[k, :, pl.ds(window.start, cols)],
                    whole.at[pl.ds(pl.multiple_of(row, rows), rows), pl.ds(col, cols)],
                    sem.at[distance if by == "grp" else 0],
                ).start()


def weight_call(place, kernel, window, inputs, in_specs, outs, out_specs, steps, by, name, flops, write=True):
    cols, groups = window.cols, place.groups
    pieces = window.arrays
    shape = (window.chips * 2 * window.rows, groups * cols)
    slots = {"grp": groups, "all": 1}[by]
    anywhere = pl.BlockSpec(memory_space=pl.ANY)

    def body(where, *refs):
        taken, refs = refs[: len(pieces)], refs[len(pieces) :]
        *refs, weight, sem, out_sem = refs
        if write:
            *refs, written = refs
        step = pl.program_id(0)

        @pl.when(step == 0)
        def _():
            fetch(where, window, taken, weight, sem, by)

        def ready():
            if by == "all":

                @pl.when(step == 0)
                def _():
                    pltpu.make_async_copy(weight, weight, sem.at[0]).wait()
                    if write:
                        pltpu.make_async_copy(weight, written, out_sem.at[0]).start()

            else:
                at = pl.ds(pl.multiple_of((where[2] ^ step) * cols, LANES), cols)
                view = weight.at[:, at]
                pltpu.make_async_copy(view, view, sem.at[step]).wait()
                pltpu.make_async_copy(view, written.at[:, at], out_sem.at[step]).start()

        kernel(where, ready, weight, *refs)

        @pl.when(step == (steps - 1 if write else -1))
        def _():
            for slot in range(slots if write else 0):
                width = shape[1] // slots
                view = weight.at[:, pl.ds(slot * width, width)]
                pltpu.make_async_copy(view, view, out_sem.at[slot]).wait()

    total = sum(math.prod(x.shape) * x.dtype.itemsize for x in list(inputs) + list(outs))
    return pl.pallas_call(
        body,
        grid_spec=pltpu.PrefetchScalarGridSpec(
            num_scalar_prefetch=1,
            grid=(steps,),
            in_specs=[anywhere] * len(pieces) + in_specs,
            out_specs=out_specs + [anywhere] * write,
            scratch_shapes=[
                pltpu.VMEM(shape, jnp.bfloat16),
                pltpu.SemaphoreType.DMA((slots,)),
                pltpu.SemaphoreType.DMA((slots,)),
            ],
        ),
        out_shape=outs + [shaped(shape, jnp.bfloat16)] * write,
        compiler_params=params(60),
        cost_estimate=cost(flops),
        name=name,
    )(place.scalars, *pieces, *inputs)


def plain_call(kernel, inputs, in_specs, outs, out_specs, steps, name, flops):
    total = sum(math.prod(x.shape) * x.dtype.itemsize for x in list(inputs) + list(outs))
    return pl.pallas_call(
        kernel,
        grid=(steps,),
        in_specs=in_specs,
        out_specs=out_specs,
        out_shape=outs,
        compiler_params=params(60),
        cost_estimate=cost(flops),
        name=name,
    )(*inputs)


TILE = 256


def row_tiles(width):
    return pl.BlockSpec((TILE, width), lambda i, *s: (i, 0))


def fixed(*shape):
    return pl.BlockSpec(shape, lambda i, *s: (0,) * len(shape))


def whole_once(shape):
    return pl.BlockSpec(shape, lambda i: (0,) * len(shape), pipeline_mode=pl.Buffered(1))


def shaped(shape, dtype):
    return jax.ShapeDtypeStruct(shape, dtype)


B_QUERY, B_VALUE, B_ATTN, GAIN_ONE, SHIFT_ONE, B_OUT, GAIN_TWO, SHIFT_TWO, B_IN = range(9)


def row(ref, n):
    return ref[n : n + 1, :]


class Vectors:
    def __init__(self, place, vectors):
        lines = [v.reshape(-1, LANES) for v in vectors]
        blank = jnp.zeros((-sum(x.shape[0] for x in lines) % 16, LANES), jnp.bfloat16)
        self.own = jnp.concatenate([*lines, blank])
        self.place = place
        self.flying = place.swap_core(self.own)

    def chips_near(self):
        self.own = jnp.stack([self.own, self.flying])
        self.flying = self.place.swap_chip(self.own, 0)

    def chips_far(self):
        self.own = jnp.stack([self.own, self.flying])
        self.flying = self.place.swap_chip(self.own, 1)

    def landed(self):
        self.slots = jnp.concatenate([self.own, self.flying])

    def unpack(self, seg_row, keep_row):
        place = self.place
        length = seg_row.shape[1]
        slots, sides, rows, lanes = self.slots.shape
        shards = place.shards

        def kernel(where, in_ref, seg_ref, keep_ref, *outs):
            rows_ref, inner_ref, qkv_ref, seg_col_ref, keep_col_ref = outs
            for line_ref, col_ref in ((seg_ref, seg_col_ref), (keep_ref, keep_col_ref)):
                line = jnp.broadcast_to(line_ref[...].astype(jnp.float32), (8, length))
                col_ref[...] = line.T[:, 0:1].astype(col_ref.dtype)
            width = shards * lanes
            qkv_ref[...] = jnp.zeros_like(qkv_ref)
            for slot in range(slots):
                for side in range(sides):
                    core = where[0] ^ side
                    shard = (where[1] ^ turn(slot, where[0])) * 2 + core
                    part = in_ref[slot, side].astype(jnp.float32)
                    at = pl.multiple_of(shard * lanes, lanes)
                    rows_ref[:, pl.ds(at, lanes)] = part
                    qkv_ref[:, pl.ds(at, lanes)] = part[B_QUERY : B_QUERY + 1]
                    qkv_ref[:, pl.ds(2 * width + at, lanes)] = part[B_VALUE : B_VALUE + 1]
                    for n in range(4):
                        start = pl.multiple_of((shard * 4 + n) * lanes, lanes)
                        inner_ref[:, pl.ds(start, lanes)] = part[B_IN + n : B_IN + n + 1]

        in_vmem = pl.BlockSpec(memory_space=pltpu.VMEM)
        return pl.pallas_call(
            kernel,
            in_specs=[pl.BlockSpec(memory_space=pltpu.SMEM)] + [in_vmem] * 3,
            out_specs=[in_vmem] * 5,
            out_shape=[
                shaped((rows, shards * lanes), jnp.float32),
                shaped((1, 4 * shards * lanes), jnp.float32),
                shaped((1, 3 * shards * lanes), jnp.float32),
                shaped((length, 1), jnp.int32),
                shaped((length, 1), jnp.float32),
            ],
            name="vectors",
        )(place.scalars, self.slots, seg_row, keep_row)


def project_qkv(place, rows, window, bias, scale):
    length, width = rows.shape
    cols = window.cols

    def kernel(where, ready, weight, x_ref, bias_ref, scale_ref, out_ref):
        ready()
        at = pl.ds(pl.multiple_of((where[2] ^ pl.program_id(0)) * cols, LANES), cols)
        size = min(512, length)
        for tile in range(length // size):
            here = pl.ds(tile * size, size)
            mixed = mxu(x_ref[here, :], weight[:, at], NN) + bias_ref[:, at]
            mixed = mixed.astype(jnp.bfloat16).astype(jnp.float32) * scale_ref[:, at]
            out_ref[here, :] = mixed.astype(jnp.bfloat16)

    total = cols * place.groups
    return weight_call(
        place,
        kernel,
        window,
        (rows, bias, scale),
        [fixed(length, width), fixed(1, total), fixed(1, total)],
        [shaped((length, total), jnp.bfloat16)],
        [pl.BlockSpec((length, cols), lambda i, s: (0, i ^ s[2]))],
        place.groups,
        "grp",
        "qkv",
        2 * length * width * total,
    )


def norm_parts(rows):
    centered = rows - jnp.mean(rows, -1, keepdims=True)
    scale = lax.rsqrt(jnp.mean(centered * centered, -1, keepdims=True) + epsilon)
    return centered * scale, scale


def norm_back(grad, normed, scale):
    return scale * (
        grad
        - jnp.mean(grad, -1, keepdims=True)
        - normed * jnp.mean(grad * normed, -1, keepdims=True)
    )


def add_rows(sum_ref, *terms):
    @pl.when(pl.program_id(0) == 0)
    def _():
        sum_ref[...] = jnp.zeros_like(sum_ref)

    for n, term in enumerate(terms):
        sum_ref[n : n + 1, :] += jnp.sum(term, 0, keepdims=True)


def project_out(place, contexts, window, rows, vectors):
    length, width = rows.shape

    def kernel(where, ready, weight, c_ref, x_ref, v_ref, n_ref, r_ref, low_ref):
        ready()
        first_sum = mxu(c_ref[...], weight[...], NN) + row(v_ref, B_ATTN)
        first_sum = first_sum + x_ref[...].astype(jnp.float32)
        normed, scale = norm_parts(first_sum)
        n_ref[...] = normed
        r_ref[...] = jnp.broadcast_to(scale, r_ref.shape)
        low_ref[...] = (normed * row(v_ref, GAIN_ONE) + row(v_ref, SHIFT_ONE)).astype(jnp.bfloat16)

    return weight_call(
        place,
        kernel,
        window,
        (contexts, rows, vectors),
        [row_tiles(width), row_tiles(width), fixed(*vectors.shape)],
        [
            shaped((length, width), jnp.float32),
            shaped((length, LANES), jnp.float32),
            shaped((length, width), jnp.bfloat16),
        ],
        [row_tiles(width), row_tiles(LANES), row_tiles(width)],
        length // TILE,
        "all",
        "attn_out",
        2 * length * width * width,
    )


def feed_in(place, normed_low, window, bias):
    length, width = normed_low.shape
    cols = window.cols

    def kernel(where, ready, weight, x_ref, bias_ref, hid_ref, slope_ref):
        ready()
        at = pl.ds(pl.multiple_of((where[2] ^ pl.program_id(0)) * cols, LANES), cols)
        size = min(512, length)
        for tile in range(length // size):
            here = pl.ds(tile * size, size)
            pre = mxu(x_ref[here, :], weight[:, at], NN) + bias_ref[:, at]
            share = 0.5 + 0.5 * lax.erf(pre * (1.0 / math.sqrt(2.0)))
            bell = jnp.exp(-0.5 * pre * pre) * (1.0 / math.sqrt(2.0 * math.pi))
            hid_ref[here, :] = (pre * share).astype(jnp.bfloat16)
            slope_ref[here, :] = (share + pre * bell).astype(jnp.bfloat16)

    total = cols * place.groups
    block = pl.BlockSpec((length, cols), lambda i, s: (0, i ^ s[2]))
    return weight_call(
        place,
        kernel,
        window,
        (normed_low, bias),
        [fixed(length, width), fixed(1, total)],
        [shaped((length, total), jnp.bfloat16)] * 2,
        [block, block],
        place.groups,
        "grp",
        "feed_in",
        2 * length * width * total,
    )


def feed_out(place, hidden, window, normed, cot, keep, vectors, slope):
    length, inner = hidden.shape
    width = normed.shape[1]

    def kernel(where, ready, weight, h_ref, n_ref, cot_ref, keep_ref, v_ref, slope_ref, *outs):
        out_ref, grad_ref, low_ref, sum_ref, pre_ref, inner_ref = outs
        ready()
        fed = mxu(h_ref[...], weight[...], NN)
        normed_one = n_ref[...] * row(v_ref, GAIN_ONE) + row(v_ref, SHIFT_ONE)
        second_sum = normed_one + (fed + row(v_ref, B_OUT))
        second, scale = norm_parts(second_sum)
        out_ref[...] = (second * row(v_ref, GAIN_TWO) + row(v_ref, SHIFT_TWO)).astype(jnp.bfloat16)
        masked = cot_ref[...].astype(jnp.float32) * keep_ref[...]
        grad = norm_back(masked * row(v_ref, GAIN_TWO), second, scale)
        grad_ref[...] = grad
        low = grad.astype(jnp.bfloat16)
        low_ref[...] = low
        add_rows(sum_ref, masked * second, masked, grad)

        @pl.when(pl.program_id(0) == 0)
        def _():
            inner_ref[...] = jnp.zeros_like(inner_ref)

        size = min(1024, inner)
        for n in range(inner // size):
            at = slice(n * size, (n + 1) * size)
            pre = mxu(low, weight[at, :], NT) * slope_ref[:, at].astype(jnp.float32)
            pre_ref[:, at] = pre.astype(jnp.bfloat16)
            inner_ref[:, at] += jnp.sum(pre, 0, keepdims=True)

    return weight_call(
        place,
        kernel,
        window,
        (hidden, normed, cot, keep, vectors, slope),
        [
            row_tiles(inner),
            row_tiles(width),
            row_tiles(width),
            row_tiles(1),
            fixed(*vectors.shape),
            row_tiles(inner),
        ],
        [
            shaped((length, width), jnp.bfloat16),
            shaped((length, width), jnp.float32),
            shaped((length, width), jnp.bfloat16),
            shaped((8, width), jnp.float32),
            shaped((length, inner), jnp.bfloat16),
            shaped((1, inner), jnp.float32),
        ],
        [
            row_tiles(width),
            row_tiles(width),
            row_tiles(width),
            fixed(8, width),
            row_tiles(inner),
            fixed(1, inner),
        ],
        length // TILE,
        "all",
        "feed_out",
        4 * length * width * inner,
        write=False,
    )


def feed_in_back(pre_low, weight, second_grad, normed, scale, vectors, attn_weight):
    length, inner = pre_low.shape
    width = normed.shape[1]

    def kernel(p_ref, w_ref, g_ref, n_ref, r_ref, v_ref, a_ref, first_ref, low_ref, ctx_ref, sum_ref):
        grad = g_ref[...] + mxu(p_ref[...], w_ref[...], NT)
        first = norm_back(grad * row(v_ref, GAIN_ONE), n_ref[...], r_ref[:, :1])
        low = first.astype(jnp.bfloat16)
        first_ref[...] = first
        low_ref[...] = low
        ctx_ref[...] = mxu(low, a_ref[...], NT).astype(jnp.bfloat16)
        add_rows(sum_ref, grad * n_ref[...], grad, first)

    return plain_call(
        kernel,
        (pre_low, weight, second_grad, normed, scale, vectors, attn_weight),
        [
            row_tiles(inner),
            whole_once(weight.shape),
            row_tiles(width),
            row_tiles(width),
            row_tiles(LANES),
            fixed(*vectors.shape),
            whole_once(attn_weight.shape),
        ],
        [
            shaped((length, width), jnp.float32),
            shaped((length, width), jnp.bfloat16),
            shaped((length, width), jnp.bfloat16),
            shaped((8, width), jnp.float32),
        ],
        [row_tiles(width), row_tiles(width), row_tiles(width), fixed(8, width)],
        length // TILE,
        "feed_in_back",
        2 * length * width * (inner + width),
    )


def project_qkv_back(grads, weight, first_grad, start, tiles, before=None):
    length, width = first_grad.shape
    part = width // len(grads)

    def kernel(w_ref, *refs):
        grad_refs, first_ref, out_ref = refs[: len(grads)], refs[len(grads)], refs[-1]
        total = first_ref[...]
        for n in range(3):
            for m, grad_ref in enumerate(grad_refs):
                at = n * width + m * part
                total = total + mxu(grad_ref[n], w_ref[:, at : at + part], NT)
        out_ref[...] = total

    tile = pl.BlockSpec((TILE, width), lambda i: (start + i, 0))
    more = () if before is None else (before,)
    return pl.pallas_call(
        kernel,
        grid=(tiles,),
        in_specs=[whole_once(weight.shape)]
        + [pl.BlockSpec((3, TILE, part), lambda i: (0, start + i, 0))] * len(grads)
        + [tile]
        + [pl.BlockSpec(memory_space=pl.ANY)] * len(more),
        out_specs=tile,
        out_shape=shaped((length, width), jnp.float32),
        input_output_aliases={} if before is None else {len(grads) + 2: 0},
        compiler_params=params(60),
        cost_estimate=cost(6 * tiles * TILE * width * width),
        name="qkv_back",
    )(weight, *grads, first_grad, *more)


ORDER = (1, 3, 0, 2)


def ordered_slot(j):
    return jnp.where(j < 2, 2 * j + 1, 2 * j - 4)


def weight_grad_kernel(where, left_ref, right_ref, own, sent, kept, *, rows, groups, split):
    core = where[0]
    chips = left_ref.shape[1] // (2 * rows)

    @pl.when(pl.program_id(1) == 0)
    def _():
        keep_rows(core, left_ref, rows, kept)

    if split:
        size = min(512, right_ref.shape[1])
        for ref, side in ((sent, 1), (own, 0)):
            for n in range(right_ref.shape[1] // size):
                at = slice(n * size, (n + 1) * size)
                part = mxu(kept[side], right_ref[:, at], NN).astype(jnp.bfloat16)
                ref[0, :, :, at] = part.reshape(chips, rows, size)
    else:
        cols = right_ref.shape[1] // groups
        for ref, side in ((sent, 1), (own, 0)):
            for pos, slot in enumerate(ORDER):
                start = pl.multiple_of((where[2] ^ turn(slot, core ^ side)) * cols, LANES)
                part = mxu(kept[side], right_ref[:, pl.ds(start, cols)], NN)
                ref[pos] = part.astype(jnp.bfloat16).reshape(chips, rows, cols)


def keep_rows(core, left_ref, rows, kept):
    chips = left_ref.shape[1] // (2 * rows)
    for side in range(2):
        chosen = []
        for k in range(chips):
            even = left_ref[:, 2 * k * rows : (2 * k + 1) * rows]
            odd = left_ref[:, (2 * k + 1) * rows : (2 * k + 2) * rows]
            chosen.append(jnp.where(core == side, even, odd))
        left = chosen[0] if chips == 1 else jnp.concatenate(chosen, 1)
        kept[side] = left.T


def turned_rows(place, left):
    tokens, height = left.shape

    def kernel(where, left_ref, out_ref):
        keep_rows(where[0], left_ref, height // place.shards, out_ref)

    in_vmem = pl.BlockSpec(memory_space=pltpu.VMEM)
    return pl.pallas_call(
        kernel,
        in_specs=[pl.BlockSpec(memory_space=pltpu.SMEM), in_vmem],
        out_specs=in_vmem,
        out_shape=shaped((2, height // 2, tokens), jnp.bfloat16),
        compiler_params=params(40),
        name="turned_rows",
    )(place.scalars, left)


def attention_grads_kernel(where, *refs, rows, groups, extra):
    turned, right_ref, *refs = refs
    *more, own, sent, kept = refs
    core, grp = where[0], where[2]
    chips = turned.shape[1] // rows
    step = pl.program_id(0)

    def scatter(lefts, right, at, cols):
        for ref, side in ((sent, 1), (own, 0)):
            part = mxu(lefts[side], right, NN).astype(jnp.bfloat16)
            for g in range(groups):
                pos = position(grp ^ g, core ^ side)
                block = part[:, g * cols : (g + 1) * cols].reshape(chips, rows, cols)
                ref[pos, :, 0:rows, pl.ds(at, cols)] = block

    skip = 0
    if not extra:
        other_left, other_right = more
        skip = other_right.shape[1] // groups

        @pl.when(step == 0)
        def _():
            keep_rows(core, other_left, rows, kept)
            scatter(kept, other_right[...], 0, skip)

    cols = right_ref.shape[2] // groups
    scatter(turned, right_ref[0], pl.multiple_of(skip + step * cols, LANES), cols)

    if extra:

        @pl.when(step == 2)
        def _():
            blank = jnp.zeros((extra, own.shape[3]), jnp.bfloat16)
            for ref, side in ((sent, 1), (own, 0)):
                for k in range(chips):
                    lines = vector_sums(2 * k + (core ^ side), *more)
                    for g in range(groups):
                        pos = position(grp ^ g, core ^ side)
                        ref[pos, k, rows : rows + extra, :] = blank
                        for n in range(3):
                            ref[pos, k, rows : rows + 1, n * LANES : (n + 1) * LANES] = lines[
                                3 * g + n
                            ].astype(jnp.bfloat16)


def vector_sums(shard, a_ref, b_ref, one_ref, two_ref, inner_ref):
    half = a_ref.shape[1]
    start = shard * LANES

    def part(ref, start):
        return ref[:, pl.ds(pl.multiple_of(start, LANES), LANES)]

    late = jnp.where(
        start < half,
        part(a_ref, jnp.minimum(start, half - LANES)),
        part(b_ref, jnp.maximum(start - half, 0)),
    )
    one, two = part(one_ref, start), part(two_ref, start)
    lines = [None] * 12
    lines[B_QUERY], lines[B_VALUE] = late[0:1], late[1:2]
    lines[GAIN_ONE], lines[SHIFT_ONE], lines[B_ATTN] = one[0:1], one[1:2], one[2:3]
    lines[GAIN_TWO], lines[SHIFT_TWO], lines[B_OUT] = two[0:1], two[1:2], two[2:3]
    for n in range(4):
        lines[B_IN + n] = part(inner_ref, (4 * shard + n) * LANES)
    return lines


def position(distance, core):
    slot = turn(distance, core)
    return jnp.where(slot == 0, 2, jnp.where(slot == 1, 0, jnp.where(slot == 3, 1, 3)))


def attention_grads(place, turned, right, more, name):
    height, tokens = 2 * turned.shape[1], turned.shape[2]
    groups, chips = place.groups, place.chips
    rows = height // place.shards
    extra = 16 if len(more) > 2 else 0
    size = right.shape[2]
    cols = 3 * size // groups + (0 if extra else more[1].shape[1] // groups)
    shape = (groups, chips, rows + extra, cols)
    once = [
        pl.BlockSpec(x.shape, lambda i, s: (0, 0), pipeline_mode=pl.Buffered(1)) for x in more
    ]
    return pl.pallas_call(
        functools.partial(attention_grads_kernel, rows=rows, groups=groups, extra=extra),
        grid_spec=pltpu.PrefetchScalarGridSpec(
            num_scalar_prefetch=1,
            grid=(3,),
            in_specs=[
                pl.BlockSpec(turned.shape, lambda i, s: (0, 0, 0), pipeline_mode=pl.Buffered(1)),
                pl.BlockSpec((1, tokens, size), lambda i, s: (i, 0, 0)),
            ]
            + once,
            out_specs=[pl.BlockSpec(shape, lambda i, s: (0, 0, 0, 0))] * 2,
            scratch_shapes=[pltpu.VMEM((8, LANES) if extra else turned.shape, jnp.bfloat16)],
        ),
        out_shape=[shaped(shape, jnp.bfloat16)] * 2,
        compiler_params=params(60),
        cost_estimate=cost(2 * tokens * height * cols * groups),
        name="wgrad_" + name,
    )(place.scalars, turned, right, *more)


def weight_grad(place, left, right, split, name):
    tokens, height = left.shape
    groups, chips = place.groups, place.chips
    rows = height // place.shards
    step_chips = chips if split else max(1, 1024 // (2 * rows))
    cols = right.shape[1] // groups
    if split:
        grid = (1, groups)
        block = lambda i, j, s: (0, s[2] ^ turn(ordered_slot(j), s[0]))
        right_spec = pl.BlockSpec((tokens, cols), block)
        one = (1, chips, rows, cols)
        other = lambda j: jnp.where(j == 0, 3, jnp.where(j == 3, 0, j))
        out_specs = [
            pl.BlockSpec(one, lambda i, j, s: (j, 0, 0, 0)),
            pl.BlockSpec(one, lambda i, j, s: (other(j), 0, 0, 0)),
        ]
    else:
        grid = (chips // step_chips, 1)
        right_spec = pl.BlockSpec(right.shape, lambda i, j, s: (0, 0))
        out_specs = [
            pl.BlockSpec((groups, step_chips, rows, cols), lambda i, j, s: (0, i, 0, 0))
        ] * 2
    return pl.pallas_call(
        functools.partial(weight_grad_kernel, rows=rows, groups=groups, split=split),
        grid_spec=pltpu.PrefetchScalarGridSpec(
            num_scalar_prefetch=1,
            grid=grid,
            in_specs=[
                pl.BlockSpec((tokens, step_chips * 2 * rows), lambda i, j, s: (0, i)),
                right_spec,
            ],
            out_specs=out_specs,
            scratch_shapes=[pltpu.VMEM((2, step_chips * rows, tokens), jnp.bfloat16)],
        ),
        out_shape=[shaped((groups, chips, rows, cols), jnp.bfloat16)] * 2,
        compiler_params=params(60),
        cost_estimate=cost(2 * tokens * height * cols * groups),
        name="wgrad_" + name,
    )(place.scalars, left, right)


def add(*terms):
    total = terms[0].astype(jnp.float32)
    for term in terms[1:]:
        total = total + term.astype(jnp.float32)
    return total.astype(jnp.bfloat16)


class Reduction:
    def __init__(self, place, made):
        self.place = place
        self.made, sent = made
        self.flying = place.swap_core(sent)

    def near(self):
        self.core = self.flying
        leave = add(self.made[:2], self.core[:2])
        self.flying = self.place.swap_grp(leave, 0)
        return leave

    def middle(self):
        self.first = self.flying
        second = add(self.made[3], self.core[3], self.first[1])
        self.flying = self.place.swap_grp(second, 1)
        return second

    def column(self):
        mine = add(self.made[2], self.core[2], self.first[0], self.flying)
        return mine, lambda chip: lax.dynamic_index_in_dim(mine, chip, 0, False)

    def along(self):
        place = self.place
        mine, at = self.column()
        self.mine = [at(place.slot_chip(slot)) for slot in range(4)]
        both = jnp.stack([self.mine[1], self.mine[3]])
        self.flying = place.swap_chip(both, 0)
        return both

    def along_far(self):
        self.first = self.flying
        second = add(self.mine[2], self.first[1])
        self.flying = self.place.swap_chip(second, 1)
        return second

    def share(self):
        return add(self.mine[0], self.first[0], self.flying)

    def along_direct(self):
        place = self.place
        mine, at = self.column()
        self.mine = at(place.chip)
        self.flying = tuple(
            place.permute(at(place.chip ^ k), (2 * k, 2 * k)) for k in range(place.chips - 1, 0, -1)
        )
        return mine

    def share_direct(self):
        return add(self.mine, *self.flying)


class Replication:
    def __init__(self, place, share, direct=False):
        self.place = place
        self.blocks = [share] + [None] * 3
        if direct:
            size = place.shards
            for mask in (3, 1, 2):
                self.blocks[mask] = place.permute(share, (mask * size, mask * size))
        else:
            self.flying = place.swap_grp(share, 0)

    def far(self):
        pair = jnp.stack([self.blocks[0], self.flying])
        self.blocks[1] = self.flying
        self.flying = self.place.swap_grp(pair, 1)
        return pair

    def landed(self):
        if self.blocks[2] is None:
            self.blocks[2:] = [self.flying[0], self.flying[1]]
        return self.blocks


def order_feed_forward(place, blocks, rows_in):
    groups = place.groups
    height, cols = blocks[0].shape
    rows_out = height - groups * rows_in

    def kernel(where, *refs):
        *blocks, out_ref, in_ref = refs
        for slot, ref in enumerate(blocks):
            g = where[2] ^ turn(slot, where[0])
            at = pl.multiple_of(g * cols, LANES)
            out_ref[:, pl.ds(at, cols)] = ref[0:rows_out, :].astype(jnp.float32)
            for n in range(groups):
                at = pl.multiple_of((g * groups + n) * cols, LANES)
                part = ref[rows_out + n * rows_in : rows_out + (n + 1) * rows_in, :]
                in_ref[:, pl.ds(at, cols)] = part.astype(jnp.float32)

    in_vmem = pl.BlockSpec(memory_space=pltpu.VMEM)
    return pl.pallas_call(
        kernel,
        in_specs=[pl.BlockSpec(memory_space=pltpu.SMEM)] + [in_vmem] * groups,
        out_specs=[in_vmem] * 2,
        out_shape=[
            shaped((rows_out, groups * cols), jnp.float32),
            shaped((rows_in, groups * groups * cols), jnp.float32),
        ],
        compiler_params=params(40),
        cost_estimate=cost(height * cols * 1024),
        name="order_feed_forward",
    )(place.scalars, *blocks)


def order_attention(place, blocks_a, blocks_b, rows):
    groups = place.groups
    size = blocks_b[0].shape[1] // 3
    skip = blocks_a[0].shape[1] - 3 * size
    width = groups * skip

    def kernel(where, *refs):
        *blocks, attn_ref, qkv_ref, small_ref = refs
        for n in range(groups):
            ref = blocks[n]
            g = where[2] ^ turn(n, where[0])
            attn_ref[:, pl.ds(pl.multiple_of(g * skip, LANES), skip)] = ref[:, 0:skip].astype(
                jnp.float32
            )
            for part in range(3):
                at = pl.multiple_of(part * width + g * size, LANES)
                block = ref[:, skip + part * size : skip + (part + 1) * size]
                qkv_ref[:, pl.ds(at, size)] = block.astype(jnp.float32)
        for n in range(groups):
            ref = blocks[groups + n]
            g = where[2] ^ n
            lines = []
            for part in range(3):
                at = pl.multiple_of(part * width + width // 2 + g * size, LANES)
                here = slice(part * size, (part + 1) * size)
                qkv_ref[:, pl.ds(at, size)] = ref[0:rows, here].astype(jnp.float32)
                lines.append(ref[rows : rows + 16, here].astype(jnp.float32)[0:1])
            lines.append(jnp.zeros((5, size), jnp.float32))
            small_ref[pl.ds(pl.multiple_of(g * 8, 8), 8), :] = jnp.concatenate(lines)

    in_vmem = pl.BlockSpec(memory_space=pltpu.VMEM)
    return pl.pallas_call(
        kernel,
        in_specs=[pl.BlockSpec(memory_space=pltpu.SMEM)] + [in_vmem] * (2 * groups),
        out_specs=[in_vmem] * 3,
        out_shape=[
            shaped((rows, width), jnp.float32),
            shaped((rows, 3 * width), jnp.float32),
            shaped((8 * groups, size), jnp.float32),
        ],
        compiler_params=params(40),
        name="order_attention",
    )(place.scalars, *blocks_a, *blocks_b)


def on_device_permutes(
    tokens,
    segment_ids,
    keep_flag,
    cotangent,
    w_qkv,
    b_query,
    b_value,
    w_attn_out,
    b_attn_out,
    norm1_gain,
    norm1_bias,
    w_in,
    b_in,
    w_out,
    b_out,
    norm2_gain,
    norm2_bias,
    *,
    groups,
    shards,
):
    place = Place(groups, shards)
    _, length, width = tokens.shape
    rows = tokens[0]
    seg_row = segment_ids.reshape(1, length)
    pairs = width // LANES

    c1 = Gather(place, w_qkv)
    c2 = Gather(place, jnp.concatenate([w_in, w_attn_out], 1))
    c3 = Gather(place, w_out)
    c1.chips_near()
    small = Vectors(
        place,
        (b_query, b_value, b_attn_out, norm1_gain, norm1_bias, b_out, norm2_gain, norm2_bias, b_in),
    )
    meet(rows, c1, small)
    pair = c1.chips_far()
    small.chips_near()
    meet(pair, c1, small)
    joined = c1.join()
    c1.near()
    small.chips_far()
    c2.chips_near(joined)
    meet(joined, c2, small)
    small.landed()
    pair = c2.chips_far()
    vectors, bias_in, qkv_bias, seg_col, keep = small.unpack(
        seg_row, keep_flag.reshape(1, length)
    )
    c1.flying = lax.optimization_barrier(c1.flying)
    turned = turned_rows(place, after(rows, vectors))
    c1.far(pair, vectors)
    c1.cross(0, 1, 2)
    joined = c2.join()
    meet((joined, turned), c1)
    c1.landed()
    c2.near(c1.held[3])
    c1.cross(3)
    c3.chips_near(c1.held[3])
    blank = jnp.ones((1, width), jnp.float32)
    qkv_scale = jnp.concatenate([blank / math.sqrt(HD), blank, blank], 1)

    mixed, full_qkv = project_qkv(place, rows, Window(c1, 0, w_qkv.shape[1]), qkv_bias, qkv_scale)
    meet(mixed, c3)
    pair = c3.chips_far()
    c2.cross(0, wait=(mixed,))
    first, second = pairs * 3 // 8, pairs * 3 // 4
    forward = attention_forward(after(mixed, pair), seg_col, seg_row, 0, first)
    meet(forward[0], c2, c3)
    c2.far()
    joined = c3.join()
    c3.near()
    c2.cross(1, 2)
    forward = attention_forward(
        after(mixed, joined), seg_col, seg_row, first, second - first, forward
    )
    meet(forward[0], c2)
    c2.landed()
    c2.cross(3)
    contexts, probs, probs_scale = attention_forward(
        after(mixed, c2.held[3]), seg_col, seg_row, second, pairs - second, forward
    )
    normed, scale_one, normed_low, full_attn = project_out(
        place, contexts, Window(c2, w_in.shape[1], w_attn_out.shape[1]), rows, vectors
    )
    meet(normed_low, c3)
    c3.far()
    c3.cross(0, 1, 2)
    hidden, slope, full_in = feed_in(
        place, after(normed_low, c3.held[1]), Window(c2, 0, w_in.shape[1]), bias_in
    )
    meet(hidden, c3)
    c3.landed()
    c3.cross(3)
    layer_out, second_grad, out_low, second_sums, pre_low, bias_in_grad = feed_out(
        place, hidden, Window(c3, 0, w_out.shape[1]), normed, cotangent[0], keep, vectors, slope
    )

    r_out = Reduction(place, weight_grad(place, hidden, out_low, False, "out"))
    r_in = Reduction(place, weight_grad(place, after(normed_low, r_out.made), pre_low, True, "in"))
    meet(r_in.made, r_out)
    step = r_out.near()
    first_grad, attn_low, context_grad, first_sums = feed_in_back(
        after(pre_low, r_in.made, step), full_in, second_grad, normed, scale_one, vectors, full_attn
    )
    meet(attn_low, r_in)
    step = r_in.near()
    half, quarter = pairs // 2, pairs // 4

    def back(wait, start, count, at, before=None):
        return attention_backward(
            mixed,
            contexts,
            after(context_grad, *wait),
            probs,
            probs_scale,
            start,
            count,
            at,
            half,
            before,
        )

    low_a, late_a = back((step,), 0, half, 0)
    meet(late_a, r_out, r_in)
    steps = (r_out.middle(), r_in.middle())
    r_a = Reduction(
        place, attention_grads(place, after(turned, *steps), low_a, (contexts, attn_low), "a")
    )
    meet(r_a.made, r_out)
    step = r_out.along()
    part = back((r_a.made, step), half, quarter, 0)
    meet(part[1], r_in, r_a)
    steps = (r_in.along(), r_a.near())
    low_b, late_b = back(steps, half + quarter, quarter, quarter, part)
    meet(late_b, r_out, r_in, r_a)
    sums = (late_a, late_b, first_sums, second_sums, bias_in_grad)
    steps = (r_out.along_far(), r_in.along_far(), r_a.middle())
    r_b = Reduction(place, attention_grads(place, after(turned, *steps), low_b, sums, "b"))
    meet(r_b.made, r_out, r_in, r_a)
    share_out, share_in = r_out.share(), r_in.share()
    inner = share_in.shape[1] // groups
    joined = jnp.concatenate(
        [share_out] + [share_in[:, n * inner : (n + 1) * inner] for n in range(groups)]
    )
    all_ffn = Replication(place, joined)
    grads = (low_a, after(low_b, r_b.made, joined, r_a.along()))
    tiles = length // TILE // 2
    input_grad = project_qkv_back(grads, full_qkv, first_grad, 0, tiles)
    meet(input_grad, r_b, r_a, all_ffn)
    steps = (r_b.near(), r_a.along_far())
    input_grad = project_qkv_back(
        grads, full_qkv, after(first_grad, *steps), tiles, tiles, input_grad
    )
    meet(input_grad, r_b, r_a)
    middle = r_b.middle()
    r_a.flying = after(r_a.flying, middle)
    all_a = Replication(place, r_a.share())
    meet(all_a.blocks[0], r_b, all_a)
    along = r_b.along_direct()
    all_a.flying = after(all_a.flying, along)
    all_ffn.flying = after(all_ffn.flying, along)
    pairs_made = (all_a.far(), all_ffn.far())
    meet(pairs_made, r_b)
    share_b = r_b.share_direct()
    all_b = Replication(place, share_b, direct=True)
    meet(share_b, all_ffn)
    w_out_grad, w_in_grad = order_feed_forward(place, all_ffn.landed(), share_in.shape[0])
    all_a.flying = after(all_a.flying, w_out_grad)
    w_attn_grad, w_qkv_grad, small = order_attention(
        place, all_a.landed(), all_b.landed(), w_attn_out.shape[0]
    )
    small = [small[8 * (n // 3) + n % 3] for n in range(12)]
    return (
        layer_out[None],
        input_grad[None],
        w_qkv_grad,
        small[B_QUERY],
        small[B_VALUE],
        w_attn_grad,
        small[B_ATTN],
        small[GAIN_ONE],
        small[SHIFT_ONE],
        w_in_grad,
        jnp.concatenate(small[B_IN:]),
        w_out_grad,
        small[B_OUT],
        small[GAIN_TWO],
        small[SHIFT_TWO],
    )


def solution(mesh):
    groups, shards = mesh.shape["grp"], mesh.shape["shard"]
    if groups == 4 and shards == 8:
        body = functools.partial(on_device_permutes, groups=groups, shards=shards)
    else:
        body = on_device
    return jax.shard_map(
        body,
        mesh=mesh,
        in_specs=(
            P(("grp", "shard"), None, None),
            P(("grp", "shard"), None),
            P(("grp", "shard"), None),
            P(("grp", "shard"), None, None),
            P("shard", "grp"),
            P("shard"),
            P("shard"),
            P("shard", "grp"),
            P("shard"),
            P("shard"),
            P("shard"),
            P("shard", "grp"),
            P("shard"),
            P("shard", "grp"),
            P("shard"),
            P("shard"),
            P("shard"),
        ),
        out_specs=(
            P(("grp", "shard"), None, None),
            P(("grp", "shard"), None, None),
            P("shard", None),
            P("shard"),
            P("shard"),
            P("shard", None),
            P("shard"),
            P("shard"),
            P("shard"),
            P("shard", None),
            P("shard"),
            P("shard", None),
            P("shard"),
            P("shard"),
            P("shard"),
        ),
        check_vma=False,
    )
```

```python
import functools
import math

import jax
import jax.numpy as jnp
from jax import lax
from jax.experimental import pallas as pl
from jax.experimental.pallas import tpu as pltpu
from jax.sharding import PartitionSpec as P

H = 16
HD = 64


masked_score = -1e30
epsilon = 1e-05


def norm_layer(rows, gain_row, shift_row):
    row_mean = jnp.mean(rows, -1, keepdims=True)
    centered = rows - row_mean
    row_var = jnp.mean(centered * centered, -1, keepdims=True)
    return centered * lax.rsqrt(row_var + epsilon) * gain_row + shift_row


def gelu_exact(values):
    return 0.5 * values * (1.0 + lax.erf(values * (1.0 / math.sqrt(2.0))))


def contract_rows(left, right):
    return lax.dot_general(
        left, right, (((0,), (0,)), ((), ())), preferred_element_type=jnp.float32
    )


def contract_cols(left, right):
    return lax.dot_general(
        left, right, (((1,), (1,)), ((), ())), preferred_element_type=jnp.float32
    )


def attend_forward(queries, key_rows, value_rows, segment_row, block_rows):
    length, model_width = queries.shape
    scaling = 1.0 / math.sqrt(HD)
    key_heads = key_rows.reshape(length, H, HD)
    value_heads = value_rows.reshape(length, H, HD)
    query_blocks = queries.reshape(length // block_rows, block_rows, H, HD)
    segment_blocks = segment_row.reshape(length // block_rows, block_rows)

    def one_block(pieces):
        query_part, segment_part = pieces
        scores = (
            jnp.einsum("qhd,khd->hqk", query_part, key_heads, preferred_element_type=jnp.float32)
            * scaling
        )
        allowed = segment_part[:, None] == segment_row[None, :]
        scores = jnp.where(allowed[None], scores, masked_score)
        row_max = jnp.max(scores, -1, keepdims=True)
        powers = jnp.exp(scores - row_max)
        totals = jnp.sum(powers, -1, keepdims=True)
        attn_probs = (powers / totals).astype(jnp.bfloat16)
        context = jnp.einsum(
            "hqk,khd->qhd", attn_probs, value_heads, preferred_element_type=jnp.float32
        )
        return (
            context.reshape(block_rows, model_width).astype(jnp.bfloat16),
            (row_max + jnp.log(totals))[:, :, 0],
        )

    contexts, log_sums = lax.map(one_block, (query_blocks, segment_blocks))
    return (contexts.reshape(length, model_width), log_sums)


def attend_backward(queries, key_rows, value_rows, segment_row, log_sums, context_grad, block_rows):
    length, model_width = queries.shape
    scaling = 1.0 / math.sqrt(HD)
    key_heads = key_rows.reshape(length, H, HD)
    value_heads = value_rows.reshape(length, H, HD)
    query_blocks = queries.reshape(length // block_rows, block_rows, H, HD)
    segment_blocks = segment_row.reshape(length // block_rows, block_rows)
    grad_blocks = context_grad.reshape(length // block_rows, block_rows, H, HD)

    def one_block(running, pieces):
        key_acc, value_acc = running
        query_part, segment_part, lse_part, grad_part = pieces
        scores = (
            jnp.einsum("qhd,khd->hqk", query_part, key_heads, preferred_element_type=jnp.float32)
            * scaling
        )
        allowed = segment_part[:, None] == segment_row[None, :]
        scores = jnp.where(allowed[None], scores, masked_score)
        probs = jnp.exp(scores - lse_part[:, :, None])
        prob_low = probs.astype(jnp.bfloat16)
        prob_grad = jnp.einsum(
            "qhd,khd->hqk", grad_part, value_heads, preferred_element_type=jnp.float32
        )
        row_dot = jnp.sum(prob_grad * probs, -1, keepdims=True)
        score_grad = (probs * (prob_grad - row_dot)).astype(jnp.bfloat16)
        query_grad = (
            jnp.einsum("hqk,khd->qhd", score_grad, key_heads, preferred_element_type=jnp.float32)
            * scaling
        )
        key_acc = (
            key_acc
            + jnp.einsum("hqk,qhd->khd", score_grad, query_part, preferred_element_type=jnp.float32)
            * scaling
        )
        value_acc = value_acc + jnp.einsum(
            "hqk,qhd->khd", prob_low, grad_part, preferred_element_type=jnp.float32
        )
        return ((key_acc, value_acc), query_grad.reshape(block_rows, model_width))

    empty_acc = jnp.zeros((length, H, HD), jnp.float32)
    (key_grad, value_grad), query_grads = lax.scan(
        one_block, (empty_acc, empty_acc), (query_blocks, segment_blocks, log_sums, grad_blocks)
    )
    return (
        query_grads.reshape(length, model_width),
        key_grad.reshape(length, model_width),
        value_grad.reshape(length, model_width),
    )


def on_device(
    tokens,
    segment_ids,
    keep_flag,
    cotangent,
    w_qkv,
    b_query,
    b_value,
    w_attn_out,
    b_attn_out,
    norm1_gain,
    norm1_bias,
    w_in,
    b_in,
    w_out,
    b_out,
    norm2_gain,
    norm2_bias,
):
    seq_count, length, model_width = tokens.shape
    block_rows = min(512, length)
    within = (
        lax.all_gather(w_qkv, "shard", axis=0, tiled=True),
        lax.all_gather(w_attn_out, "shard", axis=0, tiled=True),
        lax.all_gather(w_in, "shard", axis=0, tiled=True),
        lax.all_gather(w_out, "shard", axis=0, tiled=True),
        lax.all_gather(b_query, "shard", axis=0, tiled=True),
        lax.all_gather(b_value, "shard", axis=0, tiled=True),
        lax.all_gather(b_attn_out, "shard", axis=0, tiled=True),
        lax.all_gather(norm1_gain, "shard", axis=0, tiled=True),
        lax.all_gather(norm1_bias, "shard", axis=0, tiled=True),
        lax.all_gather(b_in, "shard", axis=0, tiled=True),
        lax.all_gather(b_out, "shard", axis=0, tiled=True),
        lax.all_gather(norm2_gain, "shard", axis=0, tiled=True),
        lax.all_gather(norm2_bias, "shard", axis=0, tiled=True),
    )
    full_qkv, full_attn, full_in, full_out = (
        lax.all_gather(within[0], "grp", axis=1, tiled=True),
        lax.all_gather(within[1], "grp", axis=1, tiled=True),
        lax.all_gather(within[2], "grp", axis=1, tiled=True),
        lax.all_gather(within[3], "grp", axis=1, tiled=True),
    )
    (
        bias_query,
        bias_value,
        bias_attn,
        gain_one,
        shift_one,
        bias_in,
        bias_out,
        gain_two,
        shift_two,
    ) = [piece.astype(jnp.float32) for piece in within[4:]]
    flat_rows = tokens.reshape(seq_count * length, model_width)
    mixed_qkv = jnp.dot(flat_rows, full_qkv, preferred_element_type=jnp.float32)
    queries = (mixed_qkv[:, :model_width] + bias_query).astype(jnp.bfloat16)
    key_rows = mixed_qkv[:, model_width : 2 * model_width].astype(jnp.bfloat16)
    value_rows = (mixed_qkv[:, 2 * model_width :] + bias_value).astype(jnp.bfloat16)
    query_seqs = queries.reshape(seq_count, length, model_width)
    key_seqs = key_rows.reshape(seq_count, length, model_width)
    value_seqs = value_rows.reshape(seq_count, length, model_width)

    def forward_sequence(pieces):
        return attend_forward(pieces[0], pieces[1], pieces[2], pieces[3], block_rows)

    contexts, log_sums = lax.map(forward_sequence, (query_seqs, key_seqs, value_seqs, segment_ids))
    contexts = contexts.reshape(seq_count * length, model_width)
    attended = jnp.dot(contexts, full_attn, preferred_element_type=jnp.float32) + bias_attn
    first_sum = flat_rows.astype(jnp.float32) + attended
    normed_one, norm_one_back = jax.vjp(norm_layer, first_sum, gain_one, shift_one)
    normed_low = normed_one.astype(jnp.bfloat16)
    hidden_pre = jnp.dot(normed_low, full_in, preferred_element_type=jnp.float32) + bias_in
    hidden, gelu_back = jax.vjp(gelu_exact, hidden_pre)
    hidden_low = hidden.astype(jnp.bfloat16)
    second_sum = normed_one + (
        jnp.dot(hidden_low, full_out, preferred_element_type=jnp.float32) + bias_out
    )
    result, norm_two_back = jax.vjp(norm_layer, second_sum, gain_two, shift_two)
    layer_out = result.astype(jnp.bfloat16).reshape(seq_count, length, model_width)
    again = (
        lax.all_gather(w_qkv, "shard", axis=0, tiled=True),
        lax.all_gather(w_attn_out, "shard", axis=0, tiled=True),
        lax.all_gather(w_in, "shard", axis=0, tiled=True),
        lax.all_gather(w_out, "shard", axis=0, tiled=True),
    )
    back_qkv, back_attn, back_in, back_out = (
        lax.all_gather(again[0], "grp", axis=1, tiled=True),
        lax.all_gather(again[1], "grp", axis=1, tiled=True),
        lax.all_gather(again[2], "grp", axis=1, tiled=True),
        lax.all_gather(again[3], "grp", axis=1, tiled=True),
    )
    masked_cot = cotangent.astype(jnp.float32).reshape(
        seq_count * length, model_width
    ) * keep_flag.reshape(seq_count * length, 1).astype(jnp.float32)
    second_grad, gain_two_grad, shift_two_grad = norm_two_back(masked_cot)
    bias_out_grad = jnp.sum(second_grad, 0)
    out_low = second_grad.astype(jnp.bfloat16)
    w_out_grad = contract_rows(hidden_low, out_low)
    hidden_grad = contract_cols(out_low, back_out)
    (pre_grad,) = gelu_back(hidden_grad)
    bias_in_grad = jnp.sum(pre_grad, 0)
    pre_low = pre_grad.astype(jnp.bfloat16)
    w_in_grad = contract_rows(normed_low, pre_low)
    normed_grad = second_grad + contract_cols(pre_low, back_in)
    first_grad, gain_one_grad, shift_one_grad = norm_one_back(normed_grad)
    bias_attn_grad = jnp.sum(first_grad, 0)
    attn_low = first_grad.astype(jnp.bfloat16)
    w_attn_grad = contract_rows(contexts, attn_low)
    context_grad = contract_cols(attn_low, back_attn).astype(jnp.bfloat16)

    def backward_sequence(pieces):
        return attend_backward(
            pieces[0], pieces[1], pieces[2], pieces[3], pieces[4], pieces[5], block_rows
        )

    query_grad, key_grad, value_grad = lax.map(
        backward_sequence,
        (
            query_seqs,
            key_seqs,
            value_seqs,
            segment_ids,
            log_sums,
            context_grad.reshape(seq_count, length, model_width),
        ),
    )
    query_grad = query_grad.reshape(seq_count * length, model_width)
    key_grad = key_grad.reshape(seq_count * length, model_width)
    value_grad = value_grad.reshape(seq_count * length, model_width)
    bias_query_grad = jnp.sum(query_grad, 0)
    bias_value_grad = jnp.sum(value_grad, 0)
    qkv_low = jnp.concatenate([query_grad, key_grad, value_grad], 1).astype(jnp.bfloat16)
    w_qkv_grad = contract_rows(flat_rows, qkv_low)
    input_grad = first_grad + contract_cols(qkv_low, back_qkv)
    reduced = (
        lax.psum_scatter(
            w_qkv_grad.astype(jnp.bfloat16), "shard", scatter_dimension=0, tiled=True
        ).astype(jnp.float32),
        lax.psum_scatter(
            bias_query_grad.astype(jnp.bfloat16), "shard", scatter_dimension=0, tiled=True
        ).astype(jnp.float32),
        lax.psum_scatter(
            bias_value_grad.astype(jnp.bfloat16), "shard", scatter_dimension=0, tiled=True
        ).astype(jnp.float32),
        lax.psum_scatter(
            w_attn_grad.astype(jnp.bfloat16), "shard", scatter_dimension=0, tiled=True
        ).astype(jnp.float32),
        lax.psum_scatter(
            bias_attn_grad.astype(jnp.bfloat16), "shard", scatter_dimension=0, tiled=True
        ).astype(jnp.float32),
        lax.psum_scatter(
            gain_one_grad.astype(jnp.bfloat16), "shard", scatter_dimension=0, tiled=True
        ).astype(jnp.float32),
        lax.psum_scatter(
            shift_one_grad.astype(jnp.bfloat16), "shard", scatter_dimension=0, tiled=True
        ).astype(jnp.float32),
        lax.psum_scatter(
            w_in_grad.astype(jnp.bfloat16), "shard", scatter_dimension=0, tiled=True
        ).astype(jnp.float32),
        lax.psum_scatter(
            bias_in_grad.astype(jnp.bfloat16), "shard", scatter_dimension=0, tiled=True
        ).astype(jnp.float32),
        lax.psum_scatter(
            w_out_grad.astype(jnp.bfloat16), "shard", scatter_dimension=0, tiled=True
        ).astype(jnp.float32),
        lax.psum_scatter(
            bias_out_grad.astype(jnp.bfloat16), "shard", scatter_dimension=0, tiled=True
        ).astype(jnp.float32),
        lax.psum_scatter(
            gain_two_grad.astype(jnp.bfloat16), "shard", scatter_dimension=0, tiled=True
        ).astype(jnp.float32),
        lax.psum_scatter(
            shift_two_grad.astype(jnp.bfloat16), "shard", scatter_dimension=0, tiled=True
        ).astype(jnp.float32),
    )
    summed = (
        lax.psum(reduced[0].astype(jnp.bfloat16), "grp").astype(jnp.float32),
        lax.psum(reduced[1].astype(jnp.bfloat16), "grp").astype(jnp.float32),
        lax.psum(reduced[2].astype(jnp.bfloat16), "grp").astype(jnp.float32),
        lax.psum(reduced[3].astype(jnp.bfloat16), "grp").astype(jnp.float32),
        lax.psum(reduced[4].astype(jnp.bfloat16), "grp").astype(jnp.float32),
        lax.psum(reduced[5].astype(jnp.bfloat16), "grp").astype(jnp.float32),
        lax.psum(reduced[6].astype(jnp.bfloat16), "grp").astype(jnp.float32),
        lax.psum(reduced[7].astype(jnp.bfloat16), "grp").astype(jnp.float32),
        lax.psum(reduced[8].astype(jnp.bfloat16), "grp").astype(jnp.float32),
        lax.psum(reduced[9].astype(jnp.bfloat16), "grp").astype(jnp.float32),
        lax.psum(reduced[10].astype(jnp.bfloat16), "grp").astype(jnp.float32),
        lax.psum(reduced[11].astype(jnp.bfloat16), "grp").astype(jnp.float32),
        lax.psum(reduced[12].astype(jnp.bfloat16), "grp").astype(jnp.float32),
    )
    return (
        layer_out,
        input_grad.reshape(seq_count, length, model_width),
        summed[0],
        summed[1],
        summed[2],
        summed[3],
        summed[4],
        summed[5],
        summed[6],
        summed[7],
        summed[8],
        summed[9],
        summed[10],
        summed[11],
        summed[12],
    )


NT = (((1,), (1,)), ((), ()))
NN = (((1,), (0,)), ((), ()))
TN = (((0,), (0,)), ((), ()))
LANES = 128
AXES = ("grp", "shard")


def mxu(left, right, dims):
    return lax.dot_general(left, right, dims, preferred_element_type=jnp.float32)


def cost(flops):
    return pl.CostEstimate(flops=2 * flops, bytes_accessed=0, transcendentals=0)


def params(megabytes=60):
    return pltpu.CompilerParams(vmem_limit_bytes=megabytes << 20)


def attention_forward_kernel(q_ref, k_ref, v_ref, seg_col, seg_row, out_ref, probs_ref, scale_ref, *, rows):
    length = q_ref.shape[0]
    first = lax.broadcasted_iota(jnp.int32, (1, LANES), 1) < HD
    keys = k_ref[...]
    values = v_ref[...]
    zero = jnp.zeros_like(keys)
    head_keys = (jnp.where(first, keys, zero), jnp.where(first, zero, keys))
    key_segments = seg_col[...]
    for block in range(length // rows):
        here = pl.ds(block * rows, rows)
        q = q_ref[here, :]
        allowed = key_segments == seg_row[:, here]
        outs, scales = [], []
        for head in range(2):
            scores = mxu(head_keys[head], q, NT)
            scores = jnp.where(allowed, scores, masked_score)
            powers = jnp.exp(scores - jnp.max(scores, 0, keepdims=True))
            scale = 1.0 / jnp.sum(powers, 0, keepdims=True)
            scales.append(jnp.broadcast_to(scale, (HD, rows)))
            powers = powers.astype(jnp.bfloat16)
            probs_ref[head, :, here] = powers
            outs.append(mxu(powers, values, TN))
        scale = jnp.transpose(jnp.concatenate(scales))
        scale_ref[here, :] = scale
        out_ref[here, :] = (jnp.where(first, outs[0], outs[1]) * scale).astype(jnp.bfloat16)


def attention_forward(qkv, seg_col, seg_row, start, pairs, before=None):
    length, width = qkv.shape[0], qkv.shape[1] // 3
    total = width // LANES
    rows = min(512, length)
    more = () if before is None else before

    def pair(part):
        return pl.BlockSpec((length, LANES), lambda j: (0, part * total + start + j))

    def body(q_ref, k_ref, v_ref, seg_c, seg_r, *refs):
        attention_forward_kernel(q_ref, k_ref, v_ref, seg_c, seg_r, *refs[-3:], rows=rows)

    return pl.pallas_call(
        body,
        grid=(pairs,),
        in_specs=[
            pair(0),
            pair(1),
            pair(2),
            pl.BlockSpec((length, 1), lambda j: (0, 0)),
            pl.BlockSpec((1, length), lambda j: (0, 0)),
        ]
        + [pl.BlockSpec(memory_space=pl.ANY)] * len(more),
        out_specs=[
            pl.BlockSpec((length, LANES), lambda j: (0, start + j)),
            pl.BlockSpec((2, length, length), lambda j: (start + j, 0, 0)),
            pl.BlockSpec((length, LANES), lambda j: (0, start + j)),
        ],
        out_shape=[
            jax.ShapeDtypeStruct((length, width), jnp.bfloat16),
            jax.ShapeDtypeStruct((2 * total, length, length), jnp.bfloat16),
            jax.ShapeDtypeStruct((length, width), jnp.float32),
        ],
        input_output_aliases={} if before is None else {5: 0, 6: 1, 7: 2},
        compiler_params=params(60),
        cost_estimate=cost(16 * length * length * pairs * LANES),
        name="attn_fwd",
    )(qkv, qkv, qkv, seg_col, seg_row, *more)


def attention_backward_kernel(
    q_ref, k_ref, v_ref, o_ref, do_ref, probs_ref, scale_ref, grad_ref, sum_ref
):
    first = lax.broadcasted_iota(jnp.int32, (1, LANES), 1) < HD
    pick = (
        lax.broadcasted_iota(jnp.int32, (8, LANES), 0)
        == lax.broadcasted_iota(jnp.int32, (8, LANES), 1) // HD
    ).astype(jnp.bfloat16)
    q = q_ref[...]
    scaled = do_ref[...].astype(jnp.float32) * scale_ref[...]
    do = scaled.astype(jnp.bfloat16)
    keys = k_ref[...]
    values = v_ref[...]
    zero = jnp.zeros_like(values)
    head_values = (jnp.where(first, values, zero), jnp.where(first, zero, values))
    products = scaled * o_ref[...].astype(jnp.float32)
    high = products.astype(jnp.bfloat16)
    low = (products - high.astype(jnp.float32)).astype(jnp.bfloat16)
    dots = mxu(pick, high, NT) + mxu(pick, low, NT)
    query_parts, key_parts, value_parts = [], [], []
    for head in range(2):
        probs = probs_ref[head]
        prob_grad = mxu(head_values[head], do, NT)
        score_grad = probs.astype(jnp.float32) * (prob_grad - dots[head : head + 1, :])
        score_grad = score_grad.astype(jnp.bfloat16)
        value_parts.append(mxu(probs, do, NN))
        key_parts.append(mxu(score_grad, q, NN))
        query_parts.append(mxu(score_grad, keys, TN))
    query_grad = jnp.where(first, *query_parts) * (1.0 / math.sqrt(HD))
    value_grad = jnp.where(first, *value_parts)
    grad_ref[0] = query_grad.astype(jnp.bfloat16)
    grad_ref[1] = jnp.where(first, *key_parts).astype(jnp.bfloat16)
    grad_ref[2] = value_grad.astype(jnp.bfloat16)
    sum_ref[0:1, :] = jnp.sum(query_grad, 0, keepdims=True)
    sum_ref[1:2, :] = jnp.sum(value_grad, 0, keepdims=True)


def attention_backward(qkv, out, out_grad, probs, scale, start, pairs, at, size, before=None):
    length, width = out.shape
    total = width // LANES
    more = () if before is None else before

    def pair(part):
        return pl.BlockSpec((length, LANES), lambda j: (0, part * total + start + j))

    def body(*refs):
        attention_backward_kernel(*refs[:7], *refs[-2:])

    return pl.pallas_call(
        body,
        grid=(pairs,),
        in_specs=[
            pair(0),
            pair(1),
            pair(2),
            pair(0),
            pair(0),
            pl.BlockSpec((2, length, length), lambda j: (start + j, 0, 0)),
            pair(0),
        ]
        + [pl.BlockSpec(memory_space=pl.ANY)] * len(more),
        out_specs=[
            pl.BlockSpec((3, length, LANES), lambda j: (0, 0, j + at)),
            pl.BlockSpec((2, LANES), lambda j: (0, j + at)),
        ],
        out_shape=[
            jax.ShapeDtypeStruct((3, length, size * LANES), jnp.bfloat16),
            jax.ShapeDtypeStruct((2, size * LANES), jnp.float32),
        ],
        input_output_aliases={} if before is None else {7: 0, 8: 1},
        compiler_params=params(60),
        cost_estimate=cost(32 * length * length * pairs * LANES),
        name="attn_bwd",
    )(qkv, qkv, qkv, out, out_grad, probs, scale, *more)


class Place:
    def __init__(self, groups, shards):
        self.groups = groups
        self.shards = shards
        self.chips = shards // 2
        self.grp = lax.axis_index("grp")
        self.shard = lax.axis_index("shard")
        self.core = self.shard % 2
        self.chip = self.shard // 2
        self.scalars = jnp.stack([self.core, self.chip, self.grp]).astype(jnp.int32)

    def permute(self, array, mask_of_core):
        pairs = [(i, i ^ mask_of_core[i % 2]) for i in range(self.groups * self.shards)]
        return lax.ppermute(array, AXES, pairs)

    def swap_core(self, array):
        return self.permute(array, (1, 1))

    def swap_grp(self, array, step):
        masks = (self.shards, 2 * self.shards)
        return self.permute(array, masks if step == 0 else masks[::-1])

    def swap_chip(self, array, step):
        masks = (2, 4)
        return self.permute(array, masks if step == 0 else masks[::-1])

    def slot_chip(self, slot):
        return self.chip ^ turn(slot, self.core)

    def slot_grp(self, slot):
        return self.grp ^ turn(slot, self.core)


def turn(slot, core):
    if isinstance(slot, int):
        return slot if slot in (0, 3) else jnp.where(core == 0, slot, 3 - slot)
    return jnp.where((core == 0) | (slot == 0) | (slot == 3), slot, 3 - slot)


def after(value, *others):
    return lax.optimization_barrier((value, *others))[0]


def meet(anchor, *flights):
    arrays = [f.flying for f in flights]
    _, *arrays = lax.optimization_barrier((anchor, *arrays))
    for f, array in zip(flights, arrays):
        f.flying = array


class Gather:
    def __init__(self, place, piece):
        self.place = place
        self.piece = piece
        self.held = [None] * 4
        self.crossed = [None] * 4

    def chips_near(self, *wait):
        self.piece = after(self.piece, *wait)
        self.flying = self.place.swap_chip(self.piece, 0)

    def chips_far(self):
        self.pair = jnp.stack([self.piece, self.flying])
        self.flying = self.place.swap_chip(self.pair, 1)
        return self.pair

    def join(self):
        self.held[0] = jnp.concatenate([self.pair, self.flying])
        return self.held[0]

    def near(self, *wait):
        self.held[0] = after(self.held[0], *wait)
        self.flying = (self.place.swap_grp(self.held[0], 0), self.place.swap_grp(self.held[0], 1))
        return self.held[0]

    def far(self, *wait):
        self.held[1:3] = self.flying
        first = after(self.held[1], *wait)
        self.flying = self.place.swap_grp(first, 1)

    def landed(self):
        self.held[3] = self.flying

    def cross(self, *which, wait=()):
        for n in which:
            self.crossed[n] = self.place.swap_core(after(self.held[n], *wait))

    def pieces(self):
        return self.held + self.crossed


class Window:
    def __init__(self, gather, start, cols):
        self.arrays = gather.pieces()
        self.start, self.cols = start, cols
        chips, rows, _ = self.arrays[0].shape
        self.chips, self.rows = chips, rows


def fetch(where, window, refs, whole, sem, by):
    rows, cols, chips = window.rows, window.cols, window.chips
    for slot in range(4):
        for side in range(2):
            core = where[0] ^ side
            ref = refs[4 * side + slot]
            distance = turn(slot, core)
            col = pl.multiple_of((where[2] ^ distance) * cols, LANES)
            for k in range(chips):
                row = ((where[1] ^ turn(k, core)) * 2 + core) * rows
                pltpu.make_async_copy(
                    ref.at[k, :, pl.ds(window.start, cols)],
                    whole.at[pl.ds(pl.multiple_of(row, rows), rows), pl.ds(col, cols)],
                    sem.at[distance if by == "grp" else 0],
                ).start()


def weight_call(place, kernel, window, inputs, in_specs, outs, out_specs, steps, by, name, flops, write=True):
    cols, groups = window.cols, place.groups
    pieces = window.arrays
    shape = (window.chips * 2 * window.rows, groups * cols)
    slots = {"grp": groups, "all": 1}[by]
    anywhere = pl.BlockSpec(memory_space=pl.ANY)

    def body(where, *refs):
        taken, refs = refs[: len(pieces)], refs[len(pieces) :]
        *refs, weight, sem, out_sem = refs
        if write:
            *refs, written = refs
        step = pl.program_id(0)

        @pl.when(step == 0)
        def _():
            fetch(where, window, taken, weight, sem, by)

        def ready():
            if by == "all":

                @pl.when(step == 0)
                def _():
                    pltpu.make_async_copy(weight, weight, sem.at[0]).wait()
                    if write:
                        pltpu.make_async_copy(weight, written, out_sem.at[0]).start()

            else:
                at = pl.ds(pl.multiple_of((where[2] ^ step) * cols, LANES), cols)
                view = weight.at[:, at]
                pltpu.make_async_copy(view, view, sem.at[step]).wait()
                pltpu.make_async_copy(view, written.at[:, at], out_sem.at[step]).start()

        kernel(where, ready, weight, *refs)

        @pl.when(step == (steps - 1 if write else -1))
        def _():
            for slot in range(slots if write else 0):
                width = shape[1] // slots
                view = weight.at[:, pl.ds(slot * width, width)]
                pltpu.make_async_copy(view, view, out_sem.at[slot]).wait()

    total = sum(math.prod(x.shape) * x.dtype.itemsize for x in list(inputs) + list(outs))
    return pl.pallas_call(
        body,
        grid_spec=pltpu.PrefetchScalarGridSpec(
            num_scalar_prefetch=1,
            grid=(steps,),
            in_specs=[anywhere] * len(pieces) + in_specs,
            out_specs=out_specs + [anywhere] * write,
            scratch_shapes=[
                pltpu.VMEM(shape, jnp.bfloat16),
                pltpu.SemaphoreType.DMA((slots,)),
                pltpu.SemaphoreType.DMA((slots,)),
            ],
        ),
        out_shape=outs + [shaped(shape, jnp.bfloat16)] * write,
        compiler_params=params(60),
        cost_estimate=cost(flops),
        name=name,
    )(place.scalars, *pieces, *inputs)


def plain_call(kernel, inputs, in_specs, outs, out_specs, steps, name, flops):
    total = sum(math.prod(x.shape) * x.dtype.itemsize for x in list(inputs) + list(outs))
    return pl.pallas_call(
        kernel,
        grid=(steps,),
        in_specs=in_specs,
        out_specs=out_specs,
        out_shape=outs,
        compiler_params=params(60),
        cost_estimate=cost(flops),
        name=name,
    )(*inputs)


TILE = 256


def row_tiles(width):
    return pl.BlockSpec((TILE, width), lambda i, *s: (i, 0))


def fixed(*shape):
    return pl.BlockSpec(shape, lambda i, *s: (0,) * len(shape))


def whole_once(shape):
    return pl.BlockSpec(shape, lambda i: (0,) * len(shape), pipeline_mode=pl.Buffered(1))


def shaped(shape, dtype):
    return jax.ShapeDtypeStruct(shape, dtype)


B_QUERY, B_VALUE, B_ATTN, GAIN_ONE, SHIFT_ONE, B_OUT, GAIN_TWO, SHIFT_TWO, B_IN = range(9)


def row(ref, n):
    return ref[n : n + 1, :]


class Vectors:
    def __init__(self, place, vectors):
        lines = [v.reshape(-1, LANES) for v in vectors]
        blank = jnp.zeros((-sum(x.shape[0] for x in lines) % 16, LANES), jnp.bfloat16)
        self.own = jnp.concatenate([*lines, blank])
        self.place = place
        self.flying = place.swap_core(self.own)

    def chips_near(self):
        self.own = jnp.stack([self.own, self.flying])
        self.flying = self.place.swap_chip(self.own, 0)

    def chips_far(self):
        self.own = jnp.stack([self.own, self.flying])
        self.flying = self.place.swap_chip(self.own, 1)

    def landed(self):
        self.slots = jnp.concatenate([self.own, self.flying])

    def unpack(self, seg_row, keep_row):
        place = self.place
        length = seg_row.shape[1]
        slots, sides, rows, lanes = self.slots.shape
        shards = place.shards

        def kernel(where, in_ref, seg_ref, keep_ref, *outs):
            rows_ref, inner_ref, qkv_ref, seg_col_ref, keep_col_ref = outs
            for line_ref, col_ref in ((seg_ref, seg_col_ref), (keep_ref, keep_col_ref)):
                line = jnp.broadcast_to(line_ref[...].astype(jnp.float32), (8, length))
                col_ref[...] = line.T[:, 0:1].astype(col_ref.dtype)
            width = shards * lanes
            qkv_ref[...] = jnp.zeros_like(qkv_ref)
            for slot in range(slots):
                for side in range(sides):
                    core = where[0] ^ side
                    shard = (where[1] ^ turn(slot, where[0])) * 2 + core
                    part = in_ref[slot, side].astype(jnp.float32)
                    at = pl.multiple_of(shard * lanes, lanes)
                    rows_ref[:, pl.ds(at, lanes)] = part
                    qkv_ref[:, pl.ds(at, lanes)] = part[B_QUERY : B_QUERY + 1]
                    qkv_ref[:, pl.ds(2 * width + at, lanes)] = part[B_VALUE : B_VALUE + 1]
                    for n in range(4):
                        start = pl.multiple_of((shard * 4 + n) * lanes, lanes)
                        inner_ref[:, pl.ds(start, lanes)] = part[B_IN + n : B_IN + n + 1]

        in_vmem = pl.BlockSpec(memory_space=pltpu.VMEM)
        return pl.pallas_call(
            kernel,
            in_specs=[pl.BlockSpec(memory_space=pltpu.SMEM)] + [in_vmem] * 3,
            out_specs=[in_vmem] * 5,
            out_shape=[
                shaped((rows, shards * lanes), jnp.float32),
                shaped((1, 4 * shards * lanes), jnp.float32),
                shaped((1, 3 * shards * lanes), jnp.float32),
                shaped((length, 1), jnp.int32),
                shaped((length, 1), jnp.float32),
            ],
            name="vectors",
        )(place.scalars, self.slots, seg_row, keep_row)


def project_qkv(place, rows, window, bias, scale):
    length, width = rows.shape
    cols = window.cols

    def kernel(where, ready, weight, x_ref, bias_ref, scale_ref, out_ref):
        ready()
        at = pl.ds(pl.multiple_of((where[2] ^ pl.program_id(0)) * cols, LANES), cols)
        size = min(512, length)
        for tile in range(length // size):
            here = pl.ds(tile * size, size)
            mixed = mxu(x_ref[here, :], weight[:, at], NN) + bias_ref[:, at]
            mixed = mixed.astype(jnp.bfloat16).astype(jnp.float32) * scale_ref[:, at]
            out_ref[here, :] = mixed.astype(jnp.bfloat16)

    total = cols * place.groups
    return weight_call(
        place,
        kernel,
        window,
        (rows, bias, scale),
        [fixed(length, width), fixed(1, total), fixed(1, total)],
        [shaped((length, total), jnp.bfloat16)],
        [pl.BlockSpec((length, cols), lambda i, s: (0, i ^ s[2]))],
        place.groups,
        "grp",
        "qkv",
        2 * length * width * total,
    )


def norm_parts(rows):
    centered = rows - jnp.mean(rows, -1, keepdims=True)
    scale = lax.rsqrt(jnp.mean(centered * centered, -1, keepdims=True) + epsilon)
    return centered * scale, scale


def norm_back(grad, normed, scale):
    return scale * (
        grad
        - jnp.mean(grad, -1, keepdims=True)
        - normed * jnp.mean(grad * normed, -1, keepdims=True)
    )


def add_rows(sum_ref, *terms):
    @pl.when(pl.program_id(0) == 0)
    def _():
        sum_ref[...] = jnp.zeros_like(sum_ref)

    for n, term in enumerate(terms):
        sum_ref[n : n + 1, :] += jnp.sum(term, 0, keepdims=True)


def project_out(place, contexts, window, rows, vectors):
    length, width = rows.shape

    def kernel(where, ready, weight, c_ref, x_ref, v_ref, n_ref, r_ref, low_ref):
        ready()
        first_sum = mxu(c_ref[...], weight[...], NN) + row(v_ref, B_ATTN)
        first_sum = first_sum + x_ref[...].astype(jnp.float32)
        normed, scale = norm_parts(first_sum)
        n_ref[...] = normed
        r_ref[...] = jnp.broadcast_to(scale, r_ref.shape)
        low_ref[...] = (normed * row(v_ref, GAIN_ONE) + row(v_ref, SHIFT_ONE)).astype(jnp.bfloat16)

    return weight_call(
        place,
        kernel,
        window,
        (contexts, rows, vectors),
        [row_tiles(width), row_tiles(width), fixed(*vectors.shape)],
        [
            shaped((length, width), jnp.float32),
            shaped((length, LANES), jnp.float32),
            shaped((length, width), jnp.bfloat16),
        ],
        [row_tiles(width), row_tiles(LANES), row_tiles(width)],
        length // TILE,
        "all",
        "attn_out",
        2 * length * width * width,
    )


def feed_in(place, normed_low, window, bias):
    length, width = normed_low.shape
    cols = window.cols

    def kernel(where, ready, weight, x_ref, bias_ref, hid_ref, slope_ref):
        ready()
        at = pl.ds(pl.multiple_of((where[2] ^ pl.program_id(0)) * cols, LANES), cols)
        size = min(512, length)
        for tile in range(length // size):
            here = pl.ds(tile * size, size)
            pre = mxu(x_ref[here, :], weight[:, at], NN) + bias_ref[:, at]
            share = 0.5 + 0.5 * lax.erf(pre * (1.0 / math.sqrt(2.0)))
            bell = jnp.exp(-0.5 * pre * pre) * (1.0 / math.sqrt(2.0 * math.pi))
            hid_ref[here, :] = (pre * share).astype(jnp.bfloat16)
            slope_ref[here, :] = (share + pre * bell).astype(jnp.bfloat16)

    total = cols * place.groups
    block = pl.BlockSpec((length, cols), lambda i, s: (0, i ^ s[2]))
    return weight_call(
        place,
        kernel,
        window,
        (normed_low, bias),
        [fixed(length, width), fixed(1, total)],
        [shaped((length, total), jnp.bfloat16)] * 2,
        [block, block],
        place.groups,
        "grp",
        "feed_in",
        2 * length * width * total,
    )


def feed_out(place, hidden, window, normed, cot, keep, vectors, slope):
    length, inner = hidden.shape
    width = normed.shape[1]

    def kernel(where, ready, weight, h_ref, n_ref, cot_ref, keep_ref, v_ref, slope_ref, *outs):
        out_ref, grad_ref, low_ref, sum_ref, pre_ref, inner_ref = outs
        ready()
        fed = mxu(h_ref[...], weight[...], NN)
        normed_one = n_ref[...] * row(v_ref, GAIN_ONE) + row(v_ref, SHIFT_ONE)
        second_sum = normed_one + (fed + row(v_ref, B_OUT))
        second, scale = norm_parts(second_sum)
        out_ref[...] = (second * row(v_ref, GAIN_TWO) + row(v_ref, SHIFT_TWO)).astype(jnp.bfloat16)
        masked = cot_ref[...].astype(jnp.float32) * keep_ref[...]
        grad = norm_back(masked * row(v_ref, GAIN_TWO), second, scale)
        grad_ref[...] = grad
        low = grad.astype(jnp.bfloat16)
        low_ref[...] = low
        add_rows(sum_ref, masked * second, masked, grad)

        @pl.when(pl.program_id(0) == 0)
        def _():
            inner_ref[...] = jnp.zeros_like(inner_ref)

        size = min(1024, inner)
        for n in range(inner // size):
            at = slice(n * size, (n + 1) * size)
            pre = mxu(low, weight[at, :], NT) * slope_ref[:, at].astype(jnp.float32)
            pre_ref[:, at] = pre.astype(jnp.bfloat16)
            inner_ref[:, at] += jnp.sum(pre, 0, keepdims=True)

    return weight_call(
        place,
        kernel,
        window,
        (hidden, normed, cot, keep, vectors, slope),
        [
            row_tiles(inner),
            row_tiles(width),
            row_tiles(width),
            row_tiles(1),
            fixed(*vectors.shape),
            row_tiles(inner),
        ],
        [
            shaped((length, width), jnp.bfloat16),
            shaped((length, width), jnp.float32),
            shaped((length, width), jnp.bfloat16),
            shaped((8, width), jnp.float32),
            shaped((length, inner), jnp.bfloat16),
            shaped((1, inner), jnp.float32),
        ],
        [
            row_tiles(width),
            row_tiles(width),
            row_tiles(width),
            fixed(8, width),
            row_tiles(inner),
            fixed(1, inner),
        ],
        length // TILE,
        "all",
        "feed_out",
        4 * length * width * inner,
        write=False,
    )


def feed_in_back(pre_low, weight, second_grad, normed, scale, vectors, attn_weight):
    length, inner = pre_low.shape
    width = normed.shape[1]

    def kernel(p_ref, w_ref, g_ref, n_ref, r_ref, v_ref, a_ref, first_ref, low_ref, ctx_ref, sum_ref):
        grad = g_ref[...] + mxu(p_ref[...], w_ref[...], NT)
        first = norm_back(grad * row(v_ref, GAIN_ONE), n_ref[...], r_ref[:, :1])
        low = first.astype(jnp.bfloat16)
        first_ref[...] = first
        low_ref[...] = low
        ctx_ref[...] = mxu(low, a_ref[...], NT).astype(jnp.bfloat16)
        add_rows(sum_ref, grad * n_ref[...], grad, first)

    return plain_call(
        kernel,
        (pre_low, weight, second_grad, normed, scale, vectors, attn_weight),
        [
            row_tiles(inner),
            whole_once(weight.shape),
            row_tiles(width),
            row_tiles(width),
            row_tiles(LANES),
            fixed(*vectors.shape),
            whole_once(attn_weight.shape),
        ],
        [
            shaped((length, width), jnp.float32),
            shaped((length, width), jnp.bfloat16),
            shaped((length, width), jnp.bfloat16),
            shaped((8, width), jnp.float32),
        ],
        [row_tiles(width), row_tiles(width), row_tiles(width), fixed(8, width)],
        length // TILE,
        "feed_in_back",
        2 * length * width * (inner + width),
    )


def project_qkv_back(grads, weight, first_grad, start, tiles, before=None):
    length, width = first_grad.shape
    part = width // len(grads)

    def kernel(w_ref, *refs):
        grad_refs, first_ref, out_ref = refs[: len(grads)], refs[len(grads)], refs[-1]
        total = first_ref[...]
        for n in range(3):
            for m, grad_ref in enumerate(grad_refs):
                at = n * width + m * part
                total = total + mxu(grad_ref[n], w_ref[:, at : at + part], NT)
        out_ref[...] = total

    tile = pl.BlockSpec((TILE, width), lambda i: (start + i, 0))
    more = () if before is None else (before,)
    return pl.pallas_call(
        kernel,
        grid=(tiles,),
        in_specs=[whole_once(weight.shape)]
        + [pl.BlockSpec((3, TILE, part), lambda i: (0, start + i, 0))] * len(grads)
        + [tile]
        + [pl.BlockSpec(memory_space=pl.ANY)] * len(more),
        out_specs=tile,
        out_shape=shaped((length, width), jnp.float32),
        input_output_aliases={} if before is None else {len(grads) + 2: 0},
        compiler_params=params(60),
        cost_estimate=cost(6 * tiles * TILE * width * width),
        name="qkv_back",
    )(weight, *grads, first_grad, *more)


ORDER = (1, 3, 0, 2)


def ordered_slot(j):
    return jnp.where(j < 2, 2 * j + 1, 2 * j - 4)


def weight_grad_kernel(where, left_ref, right_ref, own, sent, kept, *, rows, groups, split):
    core = where[0]
    chips = left_ref.shape[1] // (2 * rows)

    @pl.when(pl.program_id(1) == 0)
    def _():
        keep_rows(core, left_ref, rows, kept)

    if split:
        size = min(512, right_ref.shape[1])
        for ref, side in ((sent, 1), (own, 0)):
            for n in range(right_ref.shape[1] // size):
                at = slice(n * size, (n + 1) * size)
                part = mxu(kept[side], right_ref[:, at], NN).astype(jnp.bfloat16)
                ref[0, :, :, at] = part.reshape(chips, rows, size)
    else:
        cols = right_ref.shape[1] // groups
        for ref, side in ((sent, 1), (own, 0)):
            for pos, slot in enumerate(ORDER):
                start = pl.multiple_of((where[2] ^ turn(slot, core ^ side)) * cols, LANES)
                part = mxu(kept[side], right_ref[:, pl.ds(start, cols)], NN)
                ref[pos] = part.astype(jnp.bfloat16).reshape(chips, rows, cols)


def keep_rows(core, left_ref, rows, kept):
    chips = left_ref.shape[1] // (2 * rows)
    for side in range(2):
        chosen = []
        for k in range(chips):
            even = left_ref[:, 2 * k * rows : (2 * k + 1) * rows]
            odd = left_ref[:, (2 * k + 1) * rows : (2 * k + 2) * rows]
            chosen.append(jnp.where(core == side, even, odd))
        left = chosen[0] if chips == 1 else jnp.concatenate(chosen, 1)
        kept[side] = left.T


def turned_rows(place, left):
    tokens, height = left.shape

    def kernel(where, left_ref, out_ref):
        keep_rows(where[0], left_ref, height // place.shards, out_ref)

    in_vmem = pl.BlockSpec(memory_space=pltpu.VMEM)
    return pl.pallas_call(
        kernel,
        in_specs=[pl.BlockSpec(memory_space=pltpu.SMEM), in_vmem],
        out_specs=in_vmem,
        out_shape=shaped((2, height // 2, tokens), jnp.bfloat16),
        compiler_params=params(40),
        name="turned_rows",
    )(place.scalars, left)


def attention_grads_kernel(where, *refs, rows, groups, extra):
    turned, right_ref, *refs = refs
    *more, own, sent, kept = refs
    core, grp = where[0], where[2]
    chips = turned.shape[1] // rows
    step = pl.program_id(0)

    def scatter(lefts, right, at, cols):
        for ref, side in ((sent, 1), (own, 0)):
            part = mxu(lefts[side], right, NN).astype(jnp.bfloat16)
            for g in range(groups):
                pos = position(grp ^ g, core ^ side)
                block = part[:, g * cols : (g + 1) * cols].reshape(chips, rows, cols)
                ref[pos, :, 0:rows, pl.ds(at, cols)] = block

    skip = 0
    if not extra:
        other_left, other_right = more
        skip = other_right.shape[1] // groups

        @pl.when(step == 0)
        def _():
            keep_rows(core, other_left, rows, kept)
            scatter(kept, other_right[...], 0, skip)

    cols = right_ref.shape[2] // groups
    scatter(turned, right_ref[0], pl.multiple_of(skip + step * cols, LANES), cols)

    if extra:

        @pl.when(step == 2)
        def _():
            blank = jnp.zeros((extra, own.shape[3]), jnp.bfloat16)
            for ref, side in ((sent, 1), (own, 0)):
                for k in range(chips):
                    lines = vector_sums(2 * k + (core ^ side), *more)
                    for g in range(groups):
                        pos = position(grp ^ g, core ^ side)
                        ref[pos, k, rows : rows + extra, :] = blank
                        for n in range(3):
                            ref[pos, k, rows : rows + 1, n * LANES : (n + 1) * LANES] = lines[
                                3 * g + n
                            ].astype(jnp.bfloat16)


def vector_sums(shard, a_ref, b_ref, one_ref, two_ref, inner_ref):
    half = a_ref.shape[1]
    start = shard * LANES

    def part(ref, start):
        return ref[:, pl.ds(pl.multiple_of(start, LANES), LANES)]

    late = jnp.where(
        start < half,
        part(a_ref, jnp.minimum(start, half - LANES)),
        part(b_ref, jnp.maximum(start - half, 0)),
    )
    one, two = part(one_ref, start), part(two_ref, start)
    lines = [None] * 12
    lines[B_QUERY], lines[B_VALUE] = late[0:1], late[1:2]
    lines[GAIN_ONE], lines[SHIFT_ONE], lines[B_ATTN] = one[0:1], one[1:2], one[2:3]
    lines[GAIN_TWO], lines[SHIFT_TWO], lines[B_OUT] = two[0:1], two[1:2], two[2:3]
    for n in range(4):
        lines[B_IN + n] = part(inner_ref, (4 * shard + n) * LANES)
    return lines


def position(distance, core):
    slot = turn(distance, core)
    return jnp.where(slot == 0, 2, jnp.where(slot == 1, 0, jnp.where(slot == 3, 1, 3)))


def attention_grads(place, turned, right, more, name):
    height, tokens = 2 * turned.shape[1], turned.shape[2]
    groups, chips = place.groups, place.chips
    rows = height // place.shards
    extra = 16 if len(more) > 2 else 0
    size = right.shape[2]
    cols = 3 * size // groups + (0 if extra else more[1].shape[1] // groups)
    shape = (groups, chips, rows + extra, cols)
    once = [
        pl.BlockSpec(x.shape, lambda i, s: (0, 0), pipeline_mode=pl.Buffered(1)) for x in more
    ]
    return pl.pallas_call(
        functools.partial(attention_grads_kernel, rows=rows, groups=groups, extra=extra),
        grid_spec=pltpu.PrefetchScalarGridSpec(
            num_scalar_prefetch=1,
            grid=(3,),
            in_specs=[
                pl.BlockSpec(turned.shape, lambda i, s: (0, 0, 0), pipeline_mode=pl.Buffered(1)),
                pl.BlockSpec((1, tokens, size), lambda i, s: (i, 0, 0)),
            ]
            + once,
            out_specs=[pl.BlockSpec(shape, lambda i, s: (0, 0, 0, 0))] * 2,
            scratch_shapes=[pltpu.VMEM((8, LANES) if extra else turned.shape, jnp.bfloat16)],
        ),
        out_shape=[shaped(shape, jnp.bfloat16)] * 2,
        compiler_params=params(60),
        cost_estimate=cost(2 * tokens * height * cols * groups),
        name="wgrad_" + name,
    )(place.scalars, turned, right, *more)


def weight_grad(place, left, right, split, name):
    tokens, height = left.shape
    groups, chips = place.groups, place.chips
    rows = height // place.shards
    step_chips = chips if split else max(1, 1024 // (2 * rows))
    cols = right.shape[1] // groups
    if split:
        grid = (1, groups)
        block = lambda i, j, s: (0, s[2] ^ turn(ordered_slot(j), s[0]))
        right_spec = pl.BlockSpec((tokens, cols), block)
        one = (1, chips, rows, cols)
        other = lambda j: jnp.where(j == 0, 3, jnp.where(j == 3, 0, j))
        out_specs = [
            pl.BlockSpec(one, lambda i, j, s: (j, 0, 0, 0)),
            pl.BlockSpec(one, lambda i, j, s: (other(j), 0, 0, 0)),
        ]
    else:
        grid = (chips // step_chips, 1)
        right_spec = pl.BlockSpec(right.shape, lambda i, j, s: (0, 0))
        out_specs = [
            pl.BlockSpec((groups, step_chips, rows, cols), lambda i, j, s: (0, i, 0, 0))
        ] * 2
    return pl.pallas_call(
        functools.partial(weight_grad_kernel, rows=rows, groups=groups, split=split),
        grid_spec=pltpu.PrefetchScalarGridSpec(
            num_scalar_prefetch=1,
            grid=grid,
            in_specs=[
                pl.BlockSpec((tokens, step_chips * 2 * rows), lambda i, j, s: (0, i)),
                right_spec,
            ],
            out_specs=out_specs,
            scratch_shapes=[pltpu.VMEM((2, step_chips * rows, tokens), jnp.bfloat16)],
        ),
        out_shape=[shaped((groups, chips, rows, cols), jnp.bfloat16)] * 2,
        compiler_params=params(60),
        cost_estimate=cost(2 * tokens * height * cols * groups),
        name="wgrad_" + name,
    )(place.scalars, left, right)


def add(*terms):
    total = terms[0].astype(jnp.float32)
    for term in terms[1:]:
        total = total + term.astype(jnp.float32)
    return total.astype(jnp.bfloat16)


class Reduction:
    def __init__(self, place, made):
        self.place = place
        self.made, sent = made
        self.flying = place.swap_core(sent)

    def near(self):
        self.core = self.flying
        leave = add(self.made[:2], self.core[:2])
        self.flying = self.place.swap_grp(leave, 0)
        return leave

    def middle(self):
        self.first = self.flying
        second = add(self.made[3], self.core[3], self.first[1])
        self.flying = self.place.swap_grp(second, 1)
        return second

    def column(self):
        mine = add(self.made[2], self.core[2], self.first[0], self.flying)
        return mine, lambda chip: lax.dynamic_index_in_dim(mine, chip, 0, False)

    def along(self):
        place = self.place
        mine, at = self.column()
        self.mine = [at(place.slot_chip(slot)) for slot in range(4)]
        both = jnp.stack([self.mine[1], self.mine[3]])
        self.flying = place.swap_chip(both, 0)
        return both

    def along_far(self):
        self.first = self.flying
        second = add(self.mine[2], self.first[1])
        self.flying = self.place.swap_chip(second, 1)
        return second

    def share(self):
        return add(self.mine[0], self.first[0], self.flying)

    def along_direct(self):
        place = self.place
        mine, at = self.column()
        self.mine = at(place.chip)
        self.flying = tuple(
            place.permute(at(place.chip ^ k), (2 * k, 2 * k)) for k in range(place.chips - 1, 0, -1)
        )
        return mine

    def share_direct(self):
        return add(self.mine, *self.flying)


class Replication:
    def __init__(self, place, share, direct=False):
        self.place = place
        self.blocks = [share] + [None] * 3
        if direct:
            size = place.shards
            for mask in (3, 1, 2):
                self.blocks[mask] = place.permute(share, (mask * size, mask * size))
        else:
            self.flying = place.swap_grp(share, 0)

    def far(self):
        pair = jnp.stack([self.blocks[0], self.flying])
        self.blocks[1] = self.flying
        self.flying = self.place.swap_grp(pair, 1)
        return pair

    def landed(self):
        if self.blocks[2] is None:
            self.blocks[2:] = [self.flying[0], self.flying[1]]
        return self.blocks


def order_feed_forward(place, blocks, rows_in):
    groups = place.groups
    height, cols = blocks[0].shape
    rows_out = height - groups * rows_in

    def kernel(where, *refs):
        *blocks, out_ref, in_ref = refs
        for slot, ref in enumerate(blocks):
            g = where[2] ^ turn(slot, where[0])
            at = pl.multiple_of(g * cols, LANES)
            out_ref[:, pl.ds(at, cols)] = ref[0:rows_out, :].astype(jnp.float32)
            for n in range(groups):
                at = pl.multiple_of((g * groups + n) * cols, LANES)
                part = ref[rows_out + n * rows_in : rows_out + (n + 1) * rows_in, :]
                in_ref[:, pl.ds(at, cols)] = part.astype(jnp.float32)

    in_vmem = pl.BlockSpec(memory_space=pltpu.VMEM)
    return pl.pallas_call(
        kernel,
        in_specs=[pl.BlockSpec(memory_space=pltpu.SMEM)] + [in_vmem] * groups,
        out_specs=[in_vmem] * 2,
        out_shape=[
            shaped((rows_out, groups * cols), jnp.float32),
            shaped((rows_in, groups * groups * cols), jnp.float32),
        ],
        compiler_params=params(40),
        cost_estimate=cost(height * cols * 1024),
        name="order_feed_forward",
    )(place.scalars, *blocks)


def order_attention(place, blocks_a, blocks_b, rows):
    groups = place.groups
    size = blocks_b[0].shape[1] // 3
    skip = blocks_a[0].shape[1] - 3 * size
    width = groups * skip

    def kernel(where, *refs):
        *blocks, attn_ref, qkv_ref, small_ref = refs
        for n in range(groups):
            ref = blocks[n]
            g = where[2] ^ turn(n, where[0])
            attn_ref[:, pl.ds(pl.multiple_of(g * skip, LANES), skip)] = ref[:, 0:skip].astype(
                jnp.float32
            )
            for part in range(3):
                at = pl.multiple_of(part * width + g * size, LANES)
                block = ref[:, skip + part * size : skip + (part + 1) * size]
                qkv_ref[:, pl.ds(at, size)] = block.astype(jnp.float32)
        for n in range(groups):
            ref = blocks[groups + n]
            g = where[2] ^ n
            lines = []
            for part in range(3):
                at = pl.multiple_of(part * width + width // 2 + g * size, LANES)
                here = slice(part * size, (part + 1) * size)
                qkv_ref[:, pl.ds(at, size)] = ref[0:rows, here].astype(jnp.float32)
                lines.append(ref[rows : rows + 16, here].astype(jnp.float32)[0:1])
            lines.append(jnp.zeros((5, size), jnp.float32))
            small_ref[pl.ds(pl.multiple_of(g * 8, 8), 8), :] = jnp.concatenate(lines)

    in_vmem = pl.BlockSpec(memory_space=pltpu.VMEM)
    return pl.pallas_call(
        kernel,
        in_specs=[pl.BlockSpec(memory_space=pltpu.SMEM)] + [in_vmem] * (2 * groups),
        out_specs=[in_vmem] * 3,
        out_shape=[
            shaped((rows, width), jnp.float32),
            shaped((rows, 3 * width), jnp.float32),
            shaped((8 * groups, size), jnp.float32),
        ],
        compiler_params=params(40),
        name="order_attention",
    )(place.scalars, *blocks_a, *blocks_b)


def on_device_permutes(
    tokens,
    segment_ids,
    keep_flag,
    cotangent,
    w_qkv,
    b_query,
    b_value,
    w_attn_out,
    b_attn_out,
    norm1_gain,
    norm1_bias,
    w_in,
    b_in,
    w_out,
    b_out,
    norm2_gain,
    norm2_bias,
    *,
    groups,
    shards,
):
    place = Place(groups, shards)
    _, length, width = tokens.shape
    rows = tokens[0]
    seg_row = segment_ids.reshape(1, length)
    pairs = width // LANES

    c1 = Gather(place, w_qkv)
    c2 = Gather(place, jnp.concatenate([w_in, w_attn_out], 1))
    c3 = Gather(place, w_out)
    c1.chips_near()
    small = Vectors(
        place,
        (b_query, b_value, b_attn_out, norm1_gain, norm1_bias, b_out, norm2_gain, norm2_bias, b_in),
    )
    meet(rows, c1, small)
    pair = c1.chips_far()
    small.chips_near()
    meet(pair, c1, small)
    joined = c1.join()
    c1.near()
    small.chips_far()
    c2.chips_near(joined)
    meet(joined, c2, small)
    small.landed()
    pair = c2.chips_far()
    vectors, bias_in, qkv_bias, seg_col, keep = small.unpack(
        seg_row, keep_flag.reshape(1, length)
    )
    c1.flying = lax.optimization_barrier(c1.flying)
    turned = turned_rows(place, after(rows, vectors))
    c1.far(pair, vectors)
    c1.cross(0, 1, 2)
    joined = c2.join()
    meet((joined, turned), c1)
    c1.landed()
    c2.near(c1.held[3])
    c1.cross(3)
    c3.chips_near(c1.held[3])
    blank = jnp.ones((1, width), jnp.float32)
    qkv_scale = jnp.concatenate([blank / math.sqrt(HD), blank, blank], 1)

    mixed, full_qkv = project_qkv(place, rows, Window(c1, 0, w_qkv.shape[1]), qkv_bias, qkv_scale)
    meet(mixed, c3)
    pair = c3.chips_far()
    c2.cross(0, wait=(mixed,))
    first, second = pairs * 3 // 8, pairs * 3 // 4
    forward = attention_forward(after(mixed, pair), seg_col, seg_row, 0, first)
    meet(forward[0], c2, c3)
    c2.far()
    joined = c3.join()
    c3.near()
    c2.cross(1, 2)
    forward = attention_forward(
        after(mixed, joined), seg_col, seg_row, first, second - first, forward
    )
    meet(forward[0], c2)
    c2.landed()
    c2.cross(3)
    contexts, probs, probs_scale = attention_forward(
        after(mixed, c2.held[3]), seg_col, seg_row, second, pairs - second, forward
    )
    normed, scale_one, normed_low, full_attn = project_out(
        place, contexts, Window(c2, w_in.shape[1], w_attn_out.shape[1]), rows, vectors
    )
    meet(normed_low, c3)
    c3.far()
    c3.cross(0, 1, 2)
    hidden, slope, full_in = feed_in(
        place, after(normed_low, c3.held[1]), Window(c2, 0, w_in.shape[1]), bias_in
    )
    meet(hidden, c3)
    c3.landed()
    c3.cross(3)
    layer_out, second_grad, out_low, second_sums, pre_low, bias_in_grad = feed_out(
        place, hidden, Window(c3, 0, w_out.shape[1]), normed, cotangent[0], keep, vectors, slope
    )

    r_out = Reduction(place, weight_grad(place, hidden, out_low, False, "out"))
    r_in = Reduction(place, weight_grad(place, after(normed_low, r_out.made), pre_low, True, "in"))
    meet(r_in.made, r_out)
    step = r_out.near()
    first_grad, attn_low, context_grad, first_sums = feed_in_back(
        after(pre_low, r_in.made, step), full_in, second_grad, normed, scale_one, vectors, full_attn
    )
    meet(attn_low, r_in)
    step = r_in.near()
    half, quarter = pairs // 2, pairs // 4

    def back(wait, start, count, at, before=None):
        return attention_backward(
            mixed,
            contexts,
            after(context_grad, *wait),
            probs,
            probs_scale,
            start,
            count,
            at,
            half,
            before,
        )

    low_a, late_a = back((step,), 0, half, 0)
    meet(late_a, r_out)
    step = r_out.middle()
    meet(step, r_in)
    steps = (step, r_in.middle())
    r_a = Reduction(
        place, attention_grads(place, after(turned, *steps), low_a, (contexts, attn_low), "a")
    )
    meet(r_a.made, r_out)
    step = r_out.along()
    part = back((r_a.made, step), half, quarter, 0)
    meet(part[1], r_out, r_in, r_a)
    steps = (r_out.along_far(), r_in.along(), r_a.near())
    low_b, late_b = back(steps, half + quarter, quarter, quarter, part)
    meet(late_b, r_out, r_in, r_a)
    sums = (late_a, late_b, first_sums, second_sums, bias_in_grad)
    share_out = r_out.share()
    steps = (r_in.along_far(), r_a.middle(), share_out)
    r_b = Reduction(place, attention_grads(place, after(turned, *steps), low_b, sums, "b"))
    meet(r_b.made, r_in, r_a)
    share_in = r_in.share()
    inner = share_in.shape[1] // groups
    joined = jnp.concatenate(
        [share_out] + [share_in[:, n * inner : (n + 1) * inner] for n in range(groups)]
    )
    all_ffn = Replication(place, joined)
    grads = (low_a, after(low_b, r_b.made, joined, r_a.along()))
    tiles = length // TILE // 2
    input_grad = project_qkv_back(grads, full_qkv, first_grad, 0, tiles)
    meet(input_grad, r_b, r_a, all_ffn)
    steps = (r_b.near(), r_a.along_far())
    input_grad = project_qkv_back(
        grads, full_qkv, after(first_grad, *steps), tiles, tiles, input_grad
    )
    meet(input_grad, r_b, r_a)
    middle = r_b.middle()
    r_a.flying = after(r_a.flying, middle)
    all_a = Replication(place, r_a.share())
    meet(all_a.blocks[0], r_b, all_a)
    along = r_b.along_direct()
    all_a.flying = after(all_a.flying, along)
    all_ffn.flying = after(all_ffn.flying, along)
    pairs_made = (all_a.far(), all_ffn.far())
    meet(pairs_made, r_b)
    share_b = r_b.share_direct()
    all_b = Replication(place, share_b, direct=True)
    meet(share_b, all_ffn)
    w_out_grad, w_in_grad = order_feed_forward(place, all_ffn.landed(), share_in.shape[0])
    all_a.flying = after(all_a.flying, w_out_grad)
    w_attn_grad, w_qkv_grad, small = order_attention(
        place, all_a.landed(), all_b.landed(), w_attn_out.shape[0]
    )
    small = [small[8 * (n // 3) + n % 3] for n in range(12)]
    return (
        layer_out[None],
        input_grad[None],
        w_qkv_grad,
        small[B_QUERY],
        small[B_VALUE],
        w_attn_grad,
        small[B_ATTN],
        small[GAIN_ONE],
        small[SHIFT_ONE],
        w_in_grad,
        jnp.concatenate(small[B_IN:]),
        w_out_grad,
        small[B_OUT],
        small[GAIN_TWO],
        small[SHIFT_TWO],
    )


def solution(mesh):
    groups, shards = mesh.shape["grp"], mesh.shape["shard"]
    if groups == 4 and shards == 8:
        body = functools.partial(on_device_permutes, groups=groups, shards=shards)
    else:
        body = on_device
    return jax.shard_map(
        body,
        mesh=mesh,
        in_specs=(
            P(("grp", "shard"), None, None),
            P(("grp", "shard"), None),
            P(("grp", "shard"), None),
            P(("grp", "shard"), None, None),
            P("shard", "grp"),
            P("shard"),
            P("shard"),
            P("shard", "grp"),
            P("shard"),
            P("shard"),
            P("shard"),
            P("shard", "grp"),
            P("shard"),
            P("shard", "grp"),
            P("shard"),
            P("shard"),
            P("shard"),
        ),
        out_specs=(
            P(("grp", "shard"), None, None),
            P(("grp", "shard"), None, None),
            P("shard", None),
            P("shard"),
            P("shard"),
            P("shard", None),
            P("shard"),
            P("shard"),
            P("shard"),
            P("shard", None),
            P("shard"),
            P("shard", None),
            P("shard"),
            P("shard"),
            P("shard"),
        ),
        check_vma=False,
    )
```

```python
import functools
import math

import jax
import jax.numpy as jnp
from jax import lax
from jax.experimental import pallas as pl
from jax.experimental.pallas import tpu as pltpu
from jax.sharding import PartitionSpec as P

H = 16
HD = 64


masked_score = -1e30
epsilon = 1e-05


def norm_layer(rows, gain_row, shift_row):
    row_mean = jnp.mean(rows, -1, keepdims=True)
    centered = rows - row_mean
    row_var = jnp.mean(centered * centered, -1, keepdims=True)
    return centered * lax.rsqrt(row_var + epsilon) * gain_row + shift_row


def gelu_exact(values):
    return 0.5 * values * (1.0 + lax.erf(values * (1.0 / math.sqrt(2.0))))


def contract_rows(left, right):
    return lax.dot_general(
        left, right, (((0,), (0,)), ((), ())), preferred_element_type=jnp.float32
    )


def contract_cols(left, right):
    return lax.dot_general(
        left, right, (((1,), (1,)), ((), ())), preferred_element_type=jnp.float32
    )


def attend_forward(queries, key_rows, value_rows, segment_row, block_rows):
    length, model_width = queries.shape
    scaling = 1.0 / math.sqrt(HD)
    key_heads = key_rows.reshape(length, H, HD)
    value_heads = value_rows.reshape(length, H, HD)
    query_blocks = queries.reshape(length // block_rows, block_rows, H, HD)
    segment_blocks = segment_row.reshape(length // block_rows, block_rows)

    def one_block(pieces):
        query_part, segment_part = pieces
        scores = (
            jnp.einsum("qhd,khd->hqk", query_part, key_heads, preferred_element_type=jnp.float32)
            * scaling
        )
        allowed = segment_part[:, None] == segment_row[None, :]
        scores = jnp.where(allowed[None], scores, masked_score)
        row_max = jnp.max(scores, -1, keepdims=True)
        powers = jnp.exp(scores - row_max)
        totals = jnp.sum(powers, -1, keepdims=True)
        attn_probs = (powers / totals).astype(jnp.bfloat16)
        context = jnp.einsum(
            "hqk,khd->qhd", attn_probs, value_heads, preferred_element_type=jnp.float32
        )
        return (
            context.reshape(block_rows, model_width).astype(jnp.bfloat16),
            (row_max + jnp.log(totals))[:, :, 0],
        )

    contexts, log_sums = lax.map(one_block, (query_blocks, segment_blocks))
    return (contexts.reshape(length, model_width), log_sums)


def attend_backward(queries, key_rows, value_rows, segment_row, log_sums, context_grad, block_rows):
    length, model_width = queries.shape
    scaling = 1.0 / math.sqrt(HD)
    key_heads = key_rows.reshape(length, H, HD)
    value_heads = value_rows.reshape(length, H, HD)
    query_blocks = queries.reshape(length // block_rows, block_rows, H, HD)
    segment_blocks = segment_row.reshape(length // block_rows, block_rows)
    grad_blocks = context_grad.reshape(length // block_rows, block_rows, H, HD)

    def one_block(running, pieces):
        key_acc, value_acc = running
        query_part, segment_part, lse_part, grad_part = pieces
        scores = (
            jnp.einsum("qhd,khd->hqk", query_part, key_heads, preferred_element_type=jnp.float32)
            * scaling
        )
        allowed = segment_part[:, None] == segment_row[None, :]
        scores = jnp.where(allowed[None], scores, masked_score)
        probs = jnp.exp(scores - lse_part[:, :, None])
        prob_low = probs.astype(jnp.bfloat16)
        prob_grad = jnp.einsum(
            "qhd,khd->hqk", grad_part, value_heads, preferred_element_type=jnp.float32
        )
        row_dot = jnp.sum(prob_grad * probs, -1, keepdims=True)
        score_grad = (probs * (prob_grad - row_dot)).astype(jnp.bfloat16)
        query_grad = (
            jnp.einsum("hqk,khd->qhd", score_grad, key_heads, preferred_element_type=jnp.float32)
            * scaling
        )
        key_acc = (
            key_acc
            + jnp.einsum("hqk,qhd->khd", score_grad, query_part, preferred_element_type=jnp.float32)
            * scaling
        )
        value_acc = value_acc + jnp.einsum(
            "hqk,qhd->khd", prob_low, grad_part, preferred_element_type=jnp.float32
        )
        return ((key_acc, value_acc), query_grad.reshape(block_rows, model_width))

    empty_acc = jnp.zeros((length, H, HD), jnp.float32)
    (key_grad, value_grad), query_grads = lax.scan(
        one_block, (empty_acc, empty_acc), (query_blocks, segment_blocks, log_sums, grad_blocks)
    )
    return (
        query_grads.reshape(length, model_width),
        key_grad.reshape(length, model_width),
        value_grad.reshape(length, model_width),
    )


def on_device(
    tokens,
    segment_ids,
    keep_flag,
    cotangent,
    w_qkv,
    b_query,
    b_value,
    w_attn_out,
    b_attn_out,
    norm1_gain,
    norm1_bias,
    w_in,
    b_in,
    w_out,
    b_out,
    norm2_gain,
    norm2_bias,
):
    seq_count, length, model_width = tokens.shape
    block_rows = min(512, length)
    within = (
        lax.all_gather(w_qkv, "shard", axis=0, tiled=True),
        lax.all_gather(w_attn_out, "shard", axis=0, tiled=True),
        lax.all_gather(w_in, "shard", axis=0, tiled=True),
        lax.all_gather(w_out, "shard", axis=0, tiled=True),
        lax.all_gather(b_query, "shard", axis=0, tiled=True),
        lax.all_gather(b_value, "shard", axis=0, tiled=True),
        lax.all_gather(b_attn_out, "shard", axis=0, tiled=True),
        lax.all_gather(norm1_gain, "shard", axis=0, tiled=True),
        lax.all_gather(norm1_bias, "shard", axis=0, tiled=True),
        lax.all_gather(b_in, "shard", axis=0, tiled=True),
        lax.all_gather(b_out, "shard", axis=0, tiled=True),
        lax.all_gather(norm2_gain, "shard", axis=0, tiled=True),
        lax.all_gather(norm2_bias, "shard", axis=0, tiled=True),
    )
    full_qkv, full_attn, full_in, full_out = (
        lax.all_gather(within[0], "grp", axis=1, tiled=True),
        lax.all_gather(within[1], "grp", axis=1, tiled=True),
        lax.all_gather(within[2], "grp", axis=1, tiled=True),
        lax.all_gather(within[3], "grp", axis=1, tiled=True),
    )
    (
        bias_query,
        bias_value,
        bias_attn,
        gain_one,
        shift_one,
        bias_in,
        bias_out,
        gain_two,
        shift_two,
    ) = [piece.astype(jnp.float32) for piece in within[4:]]
    flat_rows = tokens.reshape(seq_count * length, model_width)
    mixed_qkv = jnp.dot(flat_rows, full_qkv, preferred_element_type=jnp.float32)
    queries = (mixed_qkv[:, :model_width] + bias_query).astype(jnp.bfloat16)
    key_rows = mixed_qkv[:, model_width : 2 * model_width].astype(jnp.bfloat16)
    value_rows = (mixed_qkv[:, 2 * model_width :] + bias_value).astype(jnp.bfloat16)
    query_seqs = queries.reshape(seq_count, length, model_width)
    key_seqs = key_rows.reshape(seq_count, length, model_width)
    value_seqs = value_rows.reshape(seq_count, length, model_width)

    def forward_sequence(pieces):
        return attend_forward(pieces[0], pieces[1], pieces[2], pieces[3], block_rows)

    contexts, log_sums = lax.map(forward_sequence, (query_seqs, key_seqs, value_seqs, segment_ids))
    contexts = contexts.reshape(seq_count * length, model_width)
    attended = jnp.dot(contexts, full_attn, preferred_element_type=jnp.float32) + bias_attn
    first_sum = flat_rows.astype(jnp.float32) + attended
    normed_one, norm_one_back = jax.vjp(norm_layer, first_sum, gain_one, shift_one)
    normed_low = normed_one.astype(jnp.bfloat16)
    hidden_pre = jnp.dot(normed_low, full_in, preferred_element_type=jnp.float32) + bias_in
    hidden, gelu_back = jax.vjp(gelu_exact, hidden_pre)
    hidden_low = hidden.astype(jnp.bfloat16)
    second_sum = normed_one + (
        jnp.dot(hidden_low, full_out, preferred_element_type=jnp.float32) + bias_out
    )
    result, norm_two_back = jax.vjp(norm_layer, second_sum, gain_two, shift_two)
    layer_out = result.astype(jnp.bfloat16).reshape(seq_count, length, model_width)
    again = (
        lax.all_gather(w_qkv, "shard", axis=0, tiled=True),
        lax.all_gather(w_attn_out, "shard", axis=0, tiled=True),
        lax.all_gather(w_in, "shard", axis=0, tiled=True),
        lax.all_gather(w_out, "shard", axis=0, tiled=True),
    )
    back_qkv, back_attn, back_in, back_out = (
        lax.all_gather(again[0], "grp", axis=1, tiled=True),
        lax.all_gather(again[1], "grp", axis=1, tiled=True),
        lax.all_gather(again[2], "grp", axis=1, tiled=True),
        lax.all_gather(again[3], "grp", axis=1, tiled=True),
    )
    masked_cot = cotangent.astype(jnp.float32).reshape(
        seq_count * length, model_width
    ) * keep_flag.reshape(seq_count * length, 1).astype(jnp.float32)
    second_grad, gain_two_grad, shift_two_grad = norm_two_back(masked_cot)
    bias_out_grad = jnp.sum(second_grad, 0)
    out_low = second_grad.astype(jnp.bfloat16)
    w_out_grad = contract_rows(hidden_low, out_low)
    hidden_grad = contract_cols(out_low, back_out)
    (pre_grad,) = gelu_back(hidden_grad)
    bias_in_grad = jnp.sum(pre_grad, 0)
    pre_low = pre_grad.astype(jnp.bfloat16)
    w_in_grad = contract_rows(normed_low, pre_low)
    normed_grad = second_grad + contract_cols(pre_low, back_in)
    first_grad, gain_one_grad, shift_one_grad = norm_one_back(normed_grad)
    bias_attn_grad = jnp.sum(first_grad, 0)
    attn_low = first_grad.astype(jnp.bfloat16)
    w_attn_grad = contract_rows(contexts, attn_low)
    context_grad = contract_cols(attn_low, back_attn).astype(jnp.bfloat16)

    def backward_sequence(pieces):
        return attend_backward(
            pieces[0], pieces[1], pieces[2], pieces[3], pieces[4], pieces[5], block_rows
        )

    query_grad, key_grad, value_grad = lax.map(
        backward_sequence,
        (
            query_seqs,
            key_seqs,
            value_seqs,
            segment_ids,
            log_sums,
            context_grad.reshape(seq_count, length, model_width),
        ),
    )
    query_grad = query_grad.reshape(seq_count * length, model_width)
    key_grad = key_grad.reshape(seq_count * length, model_width)
    value_grad = value_grad.reshape(seq_count * length, model_width)
    bias_query_grad = jnp.sum(query_grad, 0)
    bias_value_grad = jnp.sum(value_grad, 0)
    qkv_low = jnp.concatenate([query_grad, key_grad, value_grad], 1).astype(jnp.bfloat16)
    w_qkv_grad = contract_rows(flat_rows, qkv_low)
    input_grad = first_grad + contract_cols(qkv_low, back_qkv)
    reduced = (
        lax.psum_scatter(
            w_qkv_grad.astype(jnp.bfloat16), "shard", scatter_dimension=0, tiled=True
        ).astype(jnp.float32),
        lax.psum_scatter(
            bias_query_grad.astype(jnp.bfloat16), "shard", scatter_dimension=0, tiled=True
        ).astype(jnp.float32),
        lax.psum_scatter(
            bias_value_grad.astype(jnp.bfloat16), "shard", scatter_dimension=0, tiled=True
        ).astype(jnp.float32),
        lax.psum_scatter(
            w_attn_grad.astype(jnp.bfloat16), "shard", scatter_dimension=0, tiled=True
        ).astype(jnp.float32),
        lax.psum_scatter(
            bias_attn_grad.astype(jnp.bfloat16), "shard", scatter_dimension=0, tiled=True
        ).astype(jnp.float32),
        lax.psum_scatter(
            gain_one_grad.astype(jnp.bfloat16), "shard", scatter_dimension=0, tiled=True
        ).astype(jnp.float32),
        lax.psum_scatter(
            shift_one_grad.astype(jnp.bfloat16), "shard", scatter_dimension=0, tiled=True
        ).astype(jnp.float32),
        lax.psum_scatter(
            w_in_grad.astype(jnp.bfloat16), "shard", scatter_dimension=0, tiled=True
        ).astype(jnp.float32),
        lax.psum_scatter(
            bias_in_grad.astype(jnp.bfloat16), "shard", scatter_dimension=0, tiled=True
        ).astype(jnp.float32),
        lax.psum_scatter(
            w_out_grad.astype(jnp.bfloat16), "shard", scatter_dimension=0, tiled=True
        ).astype(jnp.float32),
        lax.psum_scatter(
            bias_out_grad.astype(jnp.bfloat16), "shard", scatter_dimension=0, tiled=True
        ).astype(jnp.float32),
        lax.psum_scatter(
            gain_two_grad.astype(jnp.bfloat16), "shard", scatter_dimension=0, tiled=True
        ).astype(jnp.float32),
        lax.psum_scatter(
            shift_two_grad.astype(jnp.bfloat16), "shard", scatter_dimension=0, tiled=True
        ).astype(jnp.float32),
    )
    summed = (
        lax.psum(reduced[0].astype(jnp.bfloat16), "grp").astype(jnp.float32),
        lax.psum(reduced[1].astype(jnp.bfloat16), "grp").astype(jnp.float32),
        lax.psum(reduced[2].astype(jnp.bfloat16), "grp").astype(jnp.float32),
        lax.psum(reduced[3].astype(jnp.bfloat16), "grp").astype(jnp.float32),
        lax.psum(reduced[4].astype(jnp.bfloat16), "grp").astype(jnp.float32),
        lax.psum(reduced[5].astype(jnp.bfloat16), "grp").astype(jnp.float32),
        lax.psum(reduced[6].astype(jnp.bfloat16), "grp").astype(jnp.float32),
        lax.psum(reduced[7].astype(jnp.bfloat16), "grp").astype(jnp.float32),
        lax.psum(reduced[8].astype(jnp.bfloat16), "grp").astype(jnp.float32),
        lax.psum(reduced[9].astype(jnp.bfloat16), "grp").astype(jnp.float32),
        lax.psum(reduced[10].astype(jnp.bfloat16), "grp").astype(jnp.float32),
        lax.psum(reduced[11].astype(jnp.bfloat16), "grp").astype(jnp.float32),
        lax.psum(reduced[12].astype(jnp.bfloat16), "grp").astype(jnp.float32),
    )
    return (
        layer_out,
        input_grad.reshape(seq_count, length, model_width),
        summed[0],
        summed[1],
        summed[2],
        summed[3],
        summed[4],
        summed[5],
        summed[6],
        summed[7],
        summed[8],
        summed[9],
        summed[10],
        summed[11],
        summed[12],
    )


NT = (((1,), (1,)), ((), ()))
NN = (((1,), (0,)), ((), ()))
TN = (((0,), (0,)), ((), ()))
LANES = 128
AXES = ("grp", "shard")


def mxu(left, right, dims):
    return lax.dot_general(left, right, dims, preferred_element_type=jnp.float32)


def cost(flops):
    return pl.CostEstimate(flops=2 * flops, bytes_accessed=0, transcendentals=0)


def params(megabytes=60):
    return pltpu.CompilerParams(vmem_limit_bytes=megabytes << 20)


def attention_forward_kernel(q_ref, k_ref, v_ref, seg_col, seg_row, out_ref, probs_ref, scale_ref, *, rows):
    length = q_ref.shape[0]
    first = lax.broadcasted_iota(jnp.int32, (1, LANES), 1) < HD
    keys = k_ref[...]
    values = v_ref[...]
    zero = jnp.zeros_like(keys)
    head_keys = (jnp.where(first, keys, zero), jnp.where(first, zero, keys))
    key_segments = seg_col[...]
    for block in range(length // rows):
        here = pl.ds(block * rows, rows)
        q = q_ref[here, :]
        allowed = key_segments == seg_row[:, here]
        outs, scales = [], []
        for head in range(2):
            scores = mxu(head_keys[head], q, NT)
            scores = jnp.where(allowed, scores, masked_score)
            powers = jnp.exp(scores - jnp.max(scores, 0, keepdims=True))
            scale = 1.0 / jnp.sum(powers, 0, keepdims=True)
            scales.append(jnp.broadcast_to(scale, (HD, rows)))
            powers = powers.astype(jnp.bfloat16)
            probs_ref[head, :, here] = powers
            outs.append(mxu(powers, values, TN))
        scale = jnp.transpose(jnp.concatenate(scales))
        scale_ref[here, :] = scale
        out_ref[here, :] = (jnp.where(first, outs[0], outs[1]) * scale).astype(jnp.bfloat16)


def attention_forward(qkv, seg_col, seg_row, start, pairs, before=None):
    length, width = qkv.shape[0], qkv.shape[1] // 3
    total = width // LANES
    rows = min(512, length)
    more = () if before is None else before

    def pair(part):
        return pl.BlockSpec((length, LANES), lambda j: (0, part * total + start + j))

    def body(q_ref, k_ref, v_ref, seg_c, seg_r, *refs):
        attention_forward_kernel(q_ref, k_ref, v_ref, seg_c, seg_r, *refs[-3:], rows=rows)

    return pl.pallas_call(
        body,
        grid=(pairs,),
        in_specs=[
            pair(0),
            pair(1),
            pair(2),
            pl.BlockSpec((length, 1), lambda j: (0, 0)),
            pl.BlockSpec((1, length), lambda j: (0, 0)),
        ]
        + [pl.BlockSpec(memory_space=pl.ANY)] * len(more),
        out_specs=[
            pl.BlockSpec((length, LANES), lambda j: (0, start + j)),
            pl.BlockSpec((2, length, length), lambda j: (start + j, 0, 0)),
            pl.BlockSpec((length, LANES), lambda j: (0, start + j)),
        ],
        out_shape=[
            jax.ShapeDtypeStruct((length, width), jnp.bfloat16),
            jax.ShapeDtypeStruct((2 * total, length, length), jnp.bfloat16),
            jax.ShapeDtypeStruct((length, width), jnp.float32),
        ],
        input_output_aliases={} if before is None else {5: 0, 6: 1, 7: 2},
        compiler_params=params(60),
        cost_estimate=cost(16 * length * length * pairs * LANES),
        name="attn_fwd",
    )(qkv, qkv, qkv, seg_col, seg_row, *more)


def attention_backward_kernel(
    q_ref, k_ref, v_ref, o_ref, do_ref, probs_ref, scale_ref, grad_ref, sum_ref
):
    first = lax.broadcasted_iota(jnp.int32, (1, LANES), 1) < HD
    pick = (
        lax.broadcasted_iota(jnp.int32, (8, LANES), 0)
        == lax.broadcasted_iota(jnp.int32, (8, LANES), 1) // HD
    ).astype(jnp.bfloat16)
    q = q_ref[...]
    scaled = do_ref[...].astype(jnp.float32) * scale_ref[...]
    do = scaled.astype(jnp.bfloat16)
    keys = k_ref[...]
    values = v_ref[...]
    zero = jnp.zeros_like(values)
    head_values = (jnp.where(first, values, zero), jnp.where(first, zero, values))
    products = scaled * o_ref[...].astype(jnp.float32)
    high = products.astype(jnp.bfloat16)
    low = (products - high.astype(jnp.float32)).astype(jnp.bfloat16)
    dots = mxu(pick, high, NT) + mxu(pick, low, NT)
    query_parts, key_parts, value_parts = [], [], []
    for head in range(2):
        probs = probs_ref[head]
        prob_grad = mxu(head_values[head], do, NT)
        score_grad = probs.astype(jnp.float32) * (prob_grad - dots[head : head + 1, :])
        score_grad = score_grad.astype(jnp.bfloat16)
        value_parts.append(mxu(probs, do, NN))
        key_parts.append(mxu(score_grad, q, NN))
        query_parts.append(mxu(score_grad, keys, TN))
    query_grad = jnp.where(first, *query_parts) * (1.0 / math.sqrt(HD))
    value_grad = jnp.where(first, *value_parts)
    grad_ref[0] = query_grad.astype(jnp.bfloat16)
    grad_ref[1] = jnp.where(first, *key_parts).astype(jnp.bfloat16)
    grad_ref[2] = value_grad.astype(jnp.bfloat16)
    sum_ref[0:1, :] = jnp.sum(query_grad, 0, keepdims=True)
    sum_ref[1:2, :] = jnp.sum(value_grad, 0, keepdims=True)


def attention_backward(qkv, out, out_grad, probs, scale, start, pairs, at, size, before=None):
    length, width = out.shape
    total = width // LANES
    more = () if before is None else before

    def pair(part):
        return pl.BlockSpec((length, LANES), lambda j: (0, part * total + start + j))

    def body(*refs):
        attention_backward_kernel(*refs[:7], *refs[-2:])

    return pl.pallas_call(
        body,
        grid=(pairs,),
        in_specs=[
            pair(0),
            pair(1),
            pair(2),
            pair(0),
            pair(0),
            pl.BlockSpec((2, length, length), lambda j: (start + j, 0, 0)),
            pair(0),
        ]
        + [pl.BlockSpec(memory_space=pl.ANY)] * len(more),
        out_specs=[
            pl.BlockSpec((3, length, LANES), lambda j: (0, 0, j + at)),
            pl.BlockSpec((2, LANES), lambda j: (0, j + at)),
        ],
        out_shape=[
            jax.ShapeDtypeStruct((3, length, size * LANES), jnp.bfloat16),
            jax.ShapeDtypeStruct((2, size * LANES), jnp.float32),
        ],
        input_output_aliases={} if before is None else {7: 0, 8: 1},
        compiler_params=params(60),
        cost_estimate=cost(32 * length * length * pairs * LANES),
        name="attn_bwd",
    )(qkv, qkv, qkv, out, out_grad, probs, scale, *more)


class Place:
    def __init__(self, groups, shards):
        self.groups = groups
        self.shards = shards
        self.chips = shards // 2
        self.grp = lax.axis_index("grp")
        self.shard = lax.axis_index("shard")
        self.core = self.shard % 2
        self.chip = self.shard // 2
        self.scalars = jnp.stack([self.core, self.chip, self.grp]).astype(jnp.int32)

    def permute(self, array, mask_of_core):
        pairs = [(i, i ^ mask_of_core[i % 2]) for i in range(self.groups * self.shards)]
        return lax.ppermute(array, AXES, pairs)

    def swap_core(self, array):
        return self.permute(array, (1, 1))

    def swap_grp(self, array, step):
        masks = (self.shards, 2 * self.shards)
        return self.permute(array, masks if step == 0 else masks[::-1])

    def swap_chip(self, array, step):
        masks = (2, 4)
        return self.permute(array, masks if step == 0 else masks[::-1])

    def slot_chip(self, slot):
        return self.chip ^ turn(slot, self.core)

    def slot_grp(self, slot):
        return self.grp ^ turn(slot, self.core)


def turn(slot, core):
    if isinstance(slot, int):
        return slot if slot in (0, 3) else jnp.where(core == 0, slot, 3 - slot)
    return jnp.where((core == 0) | (slot == 0) | (slot == 3), slot, 3 - slot)


def after(value, *others):
    return lax.optimization_barrier((value, *others))[0]


def meet(anchor, *flights):
    arrays = [f.flying for f in flights]
    _, *arrays = lax.optimization_barrier((anchor, *arrays))
    for f, array in zip(flights, arrays):
        f.flying = array


class Gather:
    def __init__(self, place, piece):
        self.place = place
        self.piece = piece
        self.held = [None] * 4
        self.crossed = [None] * 4

    def chips_near(self, *wait):
        self.piece = after(self.piece, *wait)
        self.flying = self.place.swap_chip(self.piece, 0)

    def chips_far(self):
        self.pair = jnp.stack([self.piece, self.flying])
        self.flying = self.place.swap_chip(self.pair, 1)
        return self.pair

    def join(self):
        self.held[0] = jnp.concatenate([self.pair, self.flying])
        return self.held[0]

    def near(self, *wait):
        self.held[0] = after(self.held[0], *wait)
        self.flying = (self.place.swap_grp(self.held[0], 0), self.place.swap_grp(self.held[0], 1))
        return self.held[0]

    def far(self, *wait):
        self.held[1:3] = self.flying
        first = after(self.held[1], *wait)
        self.flying = self.place.swap_grp(first, 1)

    def landed(self):
        self.held[3] = self.flying

    def cross(self, *which, wait=()):
        for n in which:
            self.crossed[n] = self.place.swap_core(after(self.held[n], *wait))

    def pieces(self):
        return self.held + self.crossed


class Window:
    def __init__(self, gather, start, cols):
        self.arrays = gather.pieces()
        self.start, self.cols = start, cols
        chips, rows, _ = self.arrays[0].shape
        self.chips, self.rows = chips, rows


def fetch(where, window, refs, whole, sem, by):
    rows, cols, chips = window.rows, window.cols, window.chips
    for slot in range(4):
        for side in range(2):
            core = where[0] ^ side
            ref = refs[4 * side + slot]
            distance = turn(slot, core)
            col = pl.multiple_of((where[2] ^ distance) * cols, LANES)
            for k in range(chips):
                row = ((where[1] ^ turn(k, core)) * 2 + core) * rows
                pltpu.make_async_copy(
                    ref.at[k, :, pl.ds(window.start, cols)],
                    whole.at[pl.ds(pl.multiple_of(row, rows), rows), pl.ds(col, cols)],
                    sem.at[distance if by == "grp" else 0],
                ).start()


def weight_call(place, kernel, window, inputs, in_specs, outs, out_specs, steps, by, name, flops, write=True):
    cols, groups = window.cols, place.groups
    pieces = window.arrays
    shape = (window.chips * 2 * window.rows, groups * cols)
    slots = {"grp": groups, "all": 1}[by]
    anywhere = pl.BlockSpec(memory_space=pl.ANY)

    def body(where, *refs):
        taken, refs = refs[: len(pieces)], refs[len(pieces) :]
        *refs, weight, sem, out_sem = refs
        if write:
            *refs, written = refs
        step = pl.program_id(0)

        @pl.when(step == 0)
        def _():
            fetch(where, window, taken, weight, sem, by)

        def ready():
            if by == "all":

                @pl.when(step == 0)
                def _():
                    pltpu.make_async_copy(weight, weight, sem.at[0]).wait()
                    if write:
                        pltpu.make_async_copy(weight, written, out_sem.at[0]).start()

            else:
                at = pl.ds(pl.multiple_of((where[2] ^ step) * cols, LANES), cols)
                view = weight.at[:, at]
                pltpu.make_async_copy(view, view, sem.at[step]).wait()
                pltpu.make_async_copy(view, written.at[:, at], out_sem.at[step]).start()

        kernel(where, ready, weight, *refs)

        @pl.when(step == (steps - 1 if write else -1))
        def _():
            for slot in range(slots if write else 0):
                width = shape[1] // slots
                view = weight.at[:, pl.ds(slot * width, width)]
                pltpu.make_async_copy(view, view, out_sem.at[slot]).wait()

    total = sum(math.prod(x.shape) * x.dtype.itemsize for x in list(inputs) + list(outs))
    return pl.pallas_call(
        body,
        grid_spec=pltpu.PrefetchScalarGridSpec(
            num_scalar_prefetch=1,
            grid=(steps,),
            in_specs=[anywhere] * len(pieces) + in_specs,
            out_specs=out_specs + [anywhere] * write,
            scratch_shapes=[
                pltpu.VMEM(shape, jnp.bfloat16),
                pltpu.SemaphoreType.DMA((slots,)),
                pltpu.SemaphoreType.DMA((slots,)),
            ],
        ),
        out_shape=outs + [shaped(shape, jnp.bfloat16)] * write,
        compiler_params=params(60),
        cost_estimate=cost(flops),
        name=name,
    )(place.scalars, *pieces, *inputs)


def plain_call(kernel, inputs, in_specs, outs, out_specs, steps, name, flops):
    total = sum(math.prod(x.shape) * x.dtype.itemsize for x in list(inputs) + list(outs))
    return pl.pallas_call(
        kernel,
        grid=(steps,),
        in_specs=in_specs,
        out_specs=out_specs,
        out_shape=outs,
        compiler_params=params(60),
        cost_estimate=cost(flops),
        name=name,
    )(*inputs)


TILE = 256


def row_tiles(width):
    return pl.BlockSpec((TILE, width), lambda i, *s: (i, 0))


def fixed(*shape):
    return pl.BlockSpec(shape, lambda i, *s: (0,) * len(shape))


def whole_once(shape):
    return pl.BlockSpec(shape, lambda i: (0,) * len(shape), pipeline_mode=pl.Buffered(1))


def shaped(shape, dtype):
    return jax.ShapeDtypeStruct(shape, dtype)


B_QUERY, B_VALUE, B_ATTN, GAIN_ONE, SHIFT_ONE, B_OUT, GAIN_TWO, SHIFT_TWO, B_IN = range(9)


def row(ref, n):
    return ref[n : n + 1, :]


class Vectors:
    def __init__(self, place, vectors):
        lines = [v.reshape(-1, LANES) for v in vectors]
        blank = jnp.zeros((-sum(x.shape[0] for x in lines) % 16, LANES), jnp.bfloat16)
        self.own = jnp.concatenate([*lines, blank])
        self.place = place
        self.flying = place.swap_core(self.own)

    def chips_near(self):
        self.own = jnp.stack([self.own, self.flying])
        self.flying = self.place.swap_chip(self.own, 0)

    def chips_far(self):
        self.own = jnp.stack([self.own, self.flying])
        self.flying = self.place.swap_chip(self.own, 1)

    def landed(self):
        self.slots = jnp.concatenate([self.own, self.flying])

    def unpack(self, seg_row, keep_row):
        place = self.place
        length = seg_row.shape[1]
        slots, sides, rows, lanes = self.slots.shape
        shards = place.shards

        def kernel(where, in_ref, seg_ref, keep_ref, *outs):
            rows_ref, inner_ref, qkv_ref, seg_col_ref, keep_col_ref = outs
            for line_ref, col_ref in ((seg_ref, seg_col_ref), (keep_ref, keep_col_ref)):
                line = jnp.broadcast_to(line_ref[...].astype(jnp.float32), (8, length))
                col_ref[...] = line.T[:, 0:1].astype(col_ref.dtype)
            width = shards * lanes
            qkv_ref[...] = jnp.zeros_like(qkv_ref)
            for slot in range(slots):
                for side in range(sides):
                    core = where[0] ^ side
                    shard = (where[1] ^ turn(slot, where[0])) * 2 + core
                    part = in_ref[slot, side].astype(jnp.float32)
                    at = pl.multiple_of(shard * lanes, lanes)
                    rows_ref[:, pl.ds(at, lanes)] = part
                    qkv_ref[:, pl.ds(at, lanes)] = part[B_QUERY : B_QUERY + 1]
                    qkv_ref[:, pl.ds(2 * width + at, lanes)] = part[B_VALUE : B_VALUE + 1]
                    for n in range(4):
                        start = pl.multiple_of((shard * 4 + n) * lanes, lanes)
                        inner_ref[:, pl.ds(start, lanes)] = part[B_IN + n : B_IN + n + 1]

        in_vmem = pl.BlockSpec(memory_space=pltpu.VMEM)
        return pl.pallas_call(
            kernel,
            in_specs=[pl.BlockSpec(memory_space=pltpu.SMEM)] + [in_vmem] * 3,
            out_specs=[in_vmem] * 5,
            out_shape=[
                shaped((rows, shards * lanes), jnp.float32),
                shaped((1, 4 * shards * lanes), jnp.float32),
                shaped((1, 3 * shards * lanes), jnp.float32),
                shaped((length, 1), jnp.int32),
                shaped((length, 1), jnp.float32),
            ],
            name="vectors",
        )(place.scalars, self.slots, seg_row, keep_row)


def project_qkv(place, rows, window, bias, scale):
    length, width = rows.shape
    cols = window.cols

    def kernel(where, ready, weight, x_ref, bias_ref, scale_ref, out_ref):
        ready()
        at = pl.ds(pl.multiple_of((where[2] ^ pl.program_id(0)) * cols, LANES), cols)
        size = min(512, length)
        for tile in range(length // size):
            here = pl.ds(tile * size, size)
            mixed = mxu(x_ref[here, :], weight[:, at], NN) + bias_ref[:, at]
            mixed = mixed.astype(jnp.bfloat16).astype(jnp.float32) * scale_ref[:, at]
            out_ref[here, :] = mixed.astype(jnp.bfloat16)

    total = cols * place.groups
    return weight_call(
        place,
        kernel,
        window,
        (rows, bias, scale),
        [fixed(length, width), fixed(1, total), fixed(1, total)],
        [shaped((length, total), jnp.bfloat16)],
        [pl.BlockSpec((length, cols), lambda i, s: (0, i ^ s[2]))],
        place.groups,
        "grp",
        "qkv",
        2 * length * width * total,
    )


def norm_parts(rows):
    centered = rows - jnp.mean(rows, -1, keepdims=True)
    scale = lax.rsqrt(jnp.mean(centered * centered, -1, keepdims=True) + epsilon)
    return centered * scale, scale


def norm_back(grad, normed, scale):
    return scale * (
        grad
        - jnp.mean(grad, -1, keepdims=True)
        - normed * jnp.mean(grad * normed, -1, keepdims=True)
    )


def add_rows(sum_ref, *terms):
    @pl.when(pl.program_id(0) == 0)
    def _():
        sum_ref[...] = jnp.zeros_like(sum_ref)

    for n, term in enumerate(terms):
        sum_ref[n : n + 1, :] += jnp.sum(term, 0, keepdims=True)


def project_out(place, contexts, window, rows, vectors):
    length, width = rows.shape

    def kernel(where, ready, weight, c_ref, x_ref, v_ref, n_ref, r_ref, low_ref):
        ready()
        first_sum = mxu(c_ref[...], weight[...], NN) + row(v_ref, B_ATTN)
        first_sum = first_sum + x_ref[...].astype(jnp.float32)
        normed, scale = norm_parts(first_sum)
        n_ref[...] = normed
        r_ref[...] = jnp.broadcast_to(scale, r_ref.shape)
        low_ref[...] = (normed * row(v_ref, GAIN_ONE) + row(v_ref, SHIFT_ONE)).astype(jnp.bfloat16)

    return weight_call(
        place,
        kernel,
        window,
        (contexts, rows, vectors),
        [row_tiles(width), row_tiles(width), fixed(*vectors.shape)],
        [
            shaped((length, width), jnp.float32),
            shaped((length, LANES), jnp.float32),
            shaped((length, width), jnp.bfloat16),
        ],
        [row_tiles(width), row_tiles(LANES), row_tiles(width)],
        length // TILE,
        "all",
        "attn_out",
        2 * length * width * width,
    )


def feed_in(place, normed_low, window, bias):
    length, width = normed_low.shape
    cols = window.cols

    def kernel(where, ready, weight, x_ref, bias_ref, hid_ref, slope_ref):
        ready()
        at = pl.ds(pl.multiple_of((where[2] ^ pl.program_id(0)) * cols, LANES), cols)
        size = min(512, length)
        for tile in range(length // size):
            here = pl.ds(tile * size, size)
            pre = mxu(x_ref[here, :], weight[:, at], NN) + bias_ref[:, at]
            share = 0.5 + 0.5 * lax.erf(pre * (1.0 / math.sqrt(2.0)))
            bell = jnp.exp(-0.5 * pre * pre) * (1.0 / math.sqrt(2.0 * math.pi))
            hid_ref[here, :] = (pre * share).astype(jnp.bfloat16)
            slope_ref[here, :] = (share + pre * bell).astype(jnp.bfloat16)

    total = cols * place.groups
    block = pl.BlockSpec((length, cols), lambda i, s: (0, i ^ s[2]))
    return weight_call(
        place,
        kernel,
        window,
        (normed_low, bias),
        [fixed(length, width), fixed(1, total)],
        [shaped((length, total), jnp.bfloat16)] * 2,
        [block, block],
        place.groups,
        "grp",
        "feed_in",
        2 * length * width * total,
    )


def feed_out(place, hidden, window, normed, cot, keep, vectors, slope):
    length, inner = hidden.shape
    width = normed.shape[1]

    def kernel(where, ready, weight, h_ref, n_ref, cot_ref, keep_ref, v_ref, slope_ref, *outs):
        out_ref, grad_ref, low_ref, sum_ref, pre_ref, inner_ref = outs
        ready()
        fed = mxu(h_ref[...], weight[...], NN)
        normed_one = n_ref[...] * row(v_ref, GAIN_ONE) + row(v_ref, SHIFT_ONE)
        second_sum = normed_one + (fed + row(v_ref, B_OUT))
        second, scale = norm_parts(second_sum)
        out_ref[...] = (second * row(v_ref, GAIN_TWO) + row(v_ref, SHIFT_TWO)).astype(jnp.bfloat16)
        masked = cot_ref[...].astype(jnp.float32) * keep_ref[...]
        grad = norm_back(masked * row(v_ref, GAIN_TWO), second, scale)
        grad_ref[...] = grad
        low = grad.astype(jnp.bfloat16)
        low_ref[...] = low
        add_rows(sum_ref, masked * second, masked, grad)

        @pl.when(pl.program_id(0) == 0)
        def _():
            inner_ref[...] = jnp.zeros_like(inner_ref)

        size = min(1024, inner)
        for n in range(inner // size):
            at = slice(n * size, (n + 1) * size)
            pre = mxu(low, weight[at, :], NT) * slope_ref[:, at].astype(jnp.float32)
            pre_ref[:, at] = pre.astype(jnp.bfloat16)
            inner_ref[:, at] += jnp.sum(pre, 0, keepdims=True)

    return weight_call(
        place,
        kernel,
        window,
        (hidden, normed, cot, keep, vectors, slope),
        [
            row_tiles(inner),
            row_tiles(width),
            row_tiles(width),
            row_tiles(1),
            fixed(*vectors.shape),
            row_tiles(inner),
        ],
        [
            shaped((length, width), jnp.bfloat16),
            shaped((length, width), jnp.float32),
            shaped((length, width), jnp.bfloat16),
            shaped((8, width), jnp.float32),
            shaped((length, inner), jnp.bfloat16),
            shaped((1, inner), jnp.float32),
        ],
        [
            row_tiles(width),
            row_tiles(width),
            row_tiles(width),
            fixed(8, width),
            row_tiles(inner),
            fixed(1, inner),
        ],
        length // TILE,
        "all",
        "feed_out",
        4 * length * width * inner,
        write=False,
    )


def feed_in_back(pre_low, weight, second_grad, normed, scale, vectors, attn_weight):
    length, inner = pre_low.shape
    width = normed.shape[1]

    def kernel(p_ref, w_ref, g_ref, n_ref, r_ref, v_ref, a_ref, first_ref, low_ref, ctx_ref, sum_ref):
        grad = g_ref[...] + mxu(p_ref[...], w_ref[...], NT)
        first = norm_back(grad * row(v_ref, GAIN_ONE), n_ref[...], r_ref[:, :1])
        low = first.astype(jnp.bfloat16)
        first_ref[...] = first
        low_ref[...] = low
        ctx_ref[...] = mxu(low, a_ref[...], NT).astype(jnp.bfloat16)
        add_rows(sum_ref, grad * n_ref[...], grad, first)

    return plain_call(
        kernel,
        (pre_low, weight, second_grad, normed, scale, vectors, attn_weight),
        [
            row_tiles(inner),
            whole_once(weight.shape),
            row_tiles(width),
            row_tiles(width),
            row_tiles(LANES),
            fixed(*vectors.shape),
            whole_once(attn_weight.shape),
        ],
        [
            shaped((length, width), jnp.float32),
            shaped((length, width), jnp.bfloat16),
            shaped((length, width), jnp.bfloat16),
            shaped((8, width), jnp.float32),
        ],
        [row_tiles(width), row_tiles(width), row_tiles(width), fixed(8, width)],
        length // TILE,
        "feed_in_back",
        2 * length * width * (inner + width),
    )


def project_qkv_back(grads, weight, first_grad, start, tiles, before=None):
    length, width = first_grad.shape
    part = width // len(grads)

    def kernel(w_ref, *refs):
        grad_refs, first_ref, out_ref = refs[: len(grads)], refs[len(grads)], refs[-1]
        total = first_ref[...]
        for n in range(3):
            for m, grad_ref in enumerate(grad_refs):
                at = n * width + m * part
                total = total + mxu(grad_ref[n], w_ref[:, at : at + part], NT)
        out_ref[...] = total

    tile = pl.BlockSpec((TILE, width), lambda i: (start + i, 0))
    more = () if before is None else (before,)
    return pl.pallas_call(
        kernel,
        grid=(tiles,),
        in_specs=[whole_once(weight.shape)]
        + [pl.BlockSpec((3, TILE, part), lambda i: (0, start + i, 0))] * len(grads)
        + [tile]
        + [pl.BlockSpec(memory_space=pl.ANY)] * len(more),
        out_specs=tile,
        out_shape=shaped((length, width), jnp.float32),
        input_output_aliases={} if before is None else {len(grads) + 2: 0},
        compiler_params=params(60),
        cost_estimate=cost(6 * tiles * TILE * width * width),
        name="qkv_back",
    )(weight, *grads, first_grad, *more)


ORDER = (1, 3, 0, 2)


def ordered_slot(j):
    return jnp.where(j < 2, 2 * j + 1, 2 * j - 4)


def weight_grad_kernel(where, left_ref, right_ref, own, sent, kept, *, rows, groups, split):
    core = where[0]
    chips = left_ref.shape[1] // (2 * rows)

    @pl.when(pl.program_id(1) == 0)
    def _():
        keep_rows(core, left_ref, rows, kept)

    if split:
        size = min(512, right_ref.shape[1])
        for ref, side in ((sent, 1), (own, 0)):
            for n in range(right_ref.shape[1] // size):
                at = slice(n * size, (n + 1) * size)
                part = mxu(kept[side], right_ref[:, at], NN).astype(jnp.bfloat16)
                ref[0, :, :, at] = part.reshape(chips, rows, size)
    else:
        cols = right_ref.shape[1] // groups
        for ref, side in ((sent, 1), (own, 0)):
            for pos, slot in enumerate(ORDER):
                start = pl.multiple_of((where[2] ^ turn(slot, core ^ side)) * cols, LANES)
                part = mxu(kept[side], right_ref[:, pl.ds(start, cols)], NN)
                ref[pos] = part.astype(jnp.bfloat16).reshape(chips, rows, cols)


def keep_rows(core, left_ref, rows, kept):
    chips = left_ref.shape[1] // (2 * rows)
    for side in range(2):
        chosen = []
        for k in range(chips):
            even = left_ref[:, 2 * k * rows : (2 * k + 1) * rows]
            odd = left_ref[:, (2 * k + 1) * rows : (2 * k + 2) * rows]
            chosen.append(jnp.where(core == side, even, odd))
        left = chosen[0] if chips == 1 else jnp.concatenate(chosen, 1)
        kept[side] = left.T


def turned_rows(place, left):
    tokens, height = left.shape

    def kernel(where, left_ref, out_ref):
        keep_rows(where[0], left_ref, height // place.shards, out_ref)

    in_vmem = pl.BlockSpec(memory_space=pltpu.VMEM)
    return pl.pallas_call(
        kernel,
        in_specs=[pl.BlockSpec(memory_space=pltpu.SMEM), in_vmem],
        out_specs=in_vmem,
        out_shape=shaped((2, height // 2, tokens), jnp.bfloat16),
        compiler_params=params(40),
        name="turned_rows",
    )(place.scalars, left)


def attention_grads_kernel(where, *refs, rows, groups, extra):
    turned, right_ref, *refs = refs
    *more, own, sent, kept = refs
    core, grp = where[0], where[2]
    chips = turned.shape[1] // rows
    step = pl.program_id(0)

    def scatter(lefts, right, at, cols):
        for ref, side in ((sent, 1), (own, 0)):
            part = mxu(lefts[side], right, NN).astype(jnp.bfloat16)
            for g in range(groups):
                pos = position(grp ^ g, core ^ side)
                block = part[:, g * cols : (g + 1) * cols].reshape(chips, rows, cols)
                ref[pos, :, 0:rows, pl.ds(at, cols)] = block

    skip = 0
    if not extra:
        other_left, other_right = more
        skip = other_right.shape[1] // groups

        @pl.when(step == 0)
        def _():
            keep_rows(core, other_left, rows, kept)
            scatter(kept, other_right[...], 0, skip)

    cols = right_ref.shape[2] // groups
    scatter(turned, right_ref[0], pl.multiple_of(skip + step * cols, LANES), cols)

    if extra:

        @pl.when(step == 2)
        def _():
            blank = jnp.zeros((extra, own.shape[3]), jnp.bfloat16)
            for ref, side in ((sent, 1), (own, 0)):
                for k in range(chips):
                    lines = vector_sums(2 * k + (core ^ side), *more)
                    for g in range(groups):
                        pos = position(grp ^ g, core ^ side)
                        ref[pos, k, rows : rows + extra, :] = blank
                        for n in range(3):
                            ref[pos, k, rows : rows + 1, n * LANES : (n + 1) * LANES] = lines[
                                3 * g + n
                            ].astype(jnp.bfloat16)


def vector_sums(shard, a_ref, b_ref, one_ref, two_ref, inner_ref):
    half = a_ref.shape[1]
    start = shard * LANES

    def part(ref, start):
        return ref[:, pl.ds(pl.multiple_of(start, LANES), LANES)]

    late = jnp.where(
        start < half,
        part(a_ref, jnp.minimum(start, half - LANES)),
        part(b_ref, jnp.maximum(start - half, 0)),
    )
    one, two = part(one_ref, start), part(two_ref, start)
    lines = [None] * 12
    lines[B_QUERY], lines[B_VALUE] = late[0:1], late[1:2]
    lines[GAIN_ONE], lines[SHIFT_ONE], lines[B_ATTN] = one[0:1], one[1:2], one[2:3]
    lines[GAIN_TWO], lines[SHIFT_TWO], lines[B_OUT] = two[0:1], two[1:2], two[2:3]
    for n in range(4):
        lines[B_IN + n] = part(inner_ref, (4 * shard + n) * LANES)
    return lines


def position(distance, core):
    slot = turn(distance, core)
    return jnp.where(slot == 0, 2, jnp.where(slot == 1, 0, jnp.where(slot == 3, 1, 3)))


def attention_grads(place, turned, right, more, name):
    height, tokens = 2 * turned.shape[1], turned.shape[2]
    groups, chips = place.groups, place.chips
    rows = height // place.shards
    extra = 16 if len(more) > 2 else 0
    size = right.shape[2]
    cols = 3 * size // groups + (0 if extra else more[1].shape[1] // groups)
    shape = (groups, chips, rows + extra, cols)
    once = [
        pl.BlockSpec(x.shape, lambda i, s: (0, 0), pipeline_mode=pl.Buffered(1)) for x in more
    ]
    return pl.pallas_call(
        functools.partial(attention_grads_kernel, rows=rows, groups=groups, extra=extra),
        grid_spec=pltpu.PrefetchScalarGridSpec(
            num_scalar_prefetch=1,
            grid=(3,),
            in_specs=[
                pl.BlockSpec(turned.shape, lambda i, s: (0, 0, 0), pipeline_mode=pl.Buffered(1)),
                pl.BlockSpec((1, tokens, size), lambda i, s: (i, 0, 0)),
            ]
            + once,
            out_specs=[pl.BlockSpec(shape, lambda i, s: (0, 0, 0, 0))] * 2,
            scratch_shapes=[pltpu.VMEM((8, LANES) if extra else turned.shape, jnp.bfloat16)],
        ),
        out_shape=[shaped(shape, jnp.bfloat16)] * 2,
        compiler_params=params(60),
        cost_estimate=cost(2 * tokens * height * cols * groups),
        name="wgrad_" + name,
    )(place.scalars, turned, right, *more)


def weight_grad(place, left, right, split, name):
    tokens, height = left.shape
    groups, chips = place.groups, place.chips
    rows = height // place.shards
    step_chips = chips if split else max(1, 1024 // (2 * rows))
    cols = right.shape[1] // groups
    if split:
        grid = (1, groups)
        block = lambda i, j, s: (0, s[2] ^ turn(ordered_slot(j), s[0]))
        right_spec = pl.BlockSpec((tokens, cols), block)
        one = (1, chips, rows, cols)
        other = lambda j: jnp.where(j == 0, 3, jnp.where(j == 3, 0, j))
        out_specs = [
            pl.BlockSpec(one, lambda i, j, s: (j, 0, 0, 0)),
            pl.BlockSpec(one, lambda i, j, s: (other(j), 0, 0, 0)),
        ]
    else:
        grid = (chips // step_chips, 1)
        right_spec = pl.BlockSpec(right.shape, lambda i, j, s: (0, 0))
        out_specs = [
            pl.BlockSpec((groups, step_chips, rows, cols), lambda i, j, s: (0, i, 0, 0))
        ] * 2
    return pl.pallas_call(
        functools.partial(weight_grad_kernel, rows=rows, groups=groups, split=split),
        grid_spec=pltpu.PrefetchScalarGridSpec(
            num_scalar_prefetch=1,
            grid=grid,
            in_specs=[
                pl.BlockSpec((tokens, step_chips * 2 * rows), lambda i, j, s: (0, i)),
                right_spec,
            ],
            out_specs=out_specs,
            scratch_shapes=[pltpu.VMEM((2, step_chips * rows, tokens), jnp.bfloat16)],
        ),
        out_shape=[shaped((groups, chips, rows, cols), jnp.bfloat16)] * 2,
        compiler_params=params(60),
        cost_estimate=cost(2 * tokens * height * cols * groups),
        name="wgrad_" + name,
    )(place.scalars, left, right)


def add(*terms):
    total = terms[0].astype(jnp.float32)
    for term in terms[1:]:
        total = total + term.astype(jnp.float32)
    return total.astype(jnp.bfloat16)


class Reduction:
    def __init__(self, place, made):
        self.place = place
        self.made, sent = made
        self.flying = place.swap_core(sent)

    def near(self):
        self.core = self.flying
        leave = add(self.made[:2], self.core[:2])
        self.flying = self.place.swap_grp(leave, 0)
        return leave

    def middle(self):
        self.first = self.flying
        second = add(self.made[3], self.core[3], self.first[1])
        self.flying = self.place.swap_grp(second, 1)
        return second

    def column(self):
        mine = add(self.made[2], self.core[2], self.first[0], self.flying)
        return mine, lambda chip: lax.dynamic_index_in_dim(mine, chip, 0, False)

    def along(self):
        place = self.place
        mine, at = self.column()
        self.mine = [at(place.slot_chip(slot)) for slot in range(4)]
        both = jnp.stack([self.mine[1], self.mine[3]])
        self.flying = place.swap_chip(both, 0)
        return both

    def along_far(self):
        self.first = self.flying
        second = add(self.mine[2], self.first[1])
        self.flying = self.place.swap_chip(second, 1)
        return second

    def share(self):
        return add(self.mine[0], self.first[0], self.flying)

    def along_direct(self):
        place = self.place
        mine, at = self.column()
        self.mine = at(place.chip)
        self.flying = tuple(
            place.permute(at(place.chip ^ k), (2 * k, 2 * k)) for k in range(place.chips - 1, 0, -1)
        )
        return mine

    def share_direct(self):
        return add(self.mine, *self.flying)


class Replication:
    def __init__(self, place, share, direct=False):
        self.place = place
        self.blocks = [share] + [None] * 3
        if direct:
            size = place.shards
            for mask in (3, 1, 2):
                self.blocks[mask] = place.permute(share, (mask * size, mask * size))
        else:
            self.flying = place.swap_grp(share, 0)

    def far(self):
        pair = jnp.stack([self.blocks[0], self.flying])
        self.blocks[1] = self.flying
        self.flying = self.place.swap_grp(pair, 1)
        return pair

    def landed(self):
        if self.blocks[2] is None:
            self.blocks[2:] = [self.flying[0], self.flying[1]]
        return self.blocks


def order_feed_forward(place, blocks, rows_in):
    groups = place.groups
    height, cols = blocks[0].shape
    rows_out = height - groups * rows_in

    def kernel(where, *refs):
        *blocks, out_ref, in_ref = refs
        for slot, ref in enumerate(blocks):
            g = where[2] ^ turn(slot, where[0])
            at = pl.multiple_of(g * cols, LANES)
            out_ref[:, pl.ds(at, cols)] = ref[0:rows_out, :].astype(jnp.float32)
            for n in range(groups):
                at = pl.multiple_of((g * groups + n) * cols, LANES)
                part = ref[rows_out + n * rows_in : rows_out + (n + 1) * rows_in, :]
                in_ref[:, pl.ds(at, cols)] = part.astype(jnp.float32)

    in_vmem = pl.BlockSpec(memory_space=pltpu.VMEM)
    return pl.pallas_call(
        kernel,
        in_specs=[pl.BlockSpec(memory_space=pltpu.SMEM)] + [in_vmem] * groups,
        out_specs=[in_vmem] * 2,
        out_shape=[
            shaped((rows_out, groups * cols), jnp.float32),
            shaped((rows_in, groups * groups * cols), jnp.float32),
        ],
        compiler_params=params(40),
        cost_estimate=cost(height * cols * 1024),
        name="order_feed_forward",
    )(place.scalars, *blocks)


def order_attention(place, blocks_a, blocks_b, rows):
    groups = place.groups
    size = blocks_b[0].shape[1] // 3
    skip = blocks_a[0].shape[1] - 3 * size
    width = groups * skip

    def kernel(where, *refs):
        *blocks, attn_ref, qkv_ref, small_ref = refs
        for n in range(groups):
            ref = blocks[n]
            g = where[2] ^ turn(n, where[0])
            attn_ref[:, pl.ds(pl.multiple_of(g * skip, LANES), skip)] = ref[:, 0:skip].astype(
                jnp.float32
            )
            for part in range(3):
                at = pl.multiple_of(part * width + g * size, LANES)
                block = ref[:, skip + part * size : skip + (part + 1) * size]
                qkv_ref[:, pl.ds(at, size)] = block.astype(jnp.float32)
        for n in range(groups):
            ref = blocks[groups + n]
            g = where[2] ^ n
            lines = []
            for part in range(3):
                at = pl.multiple_of(part * width + width // 2 + g * size, LANES)
                here = slice(part * size, (part + 1) * size)
                qkv_ref[:, pl.ds(at, size)] = ref[0:rows, here].astype(jnp.float32)
                lines.append(ref[rows : rows + 16, here].astype(jnp.float32)[0:1])
            lines.append(jnp.zeros((5, size), jnp.float32))
            small_ref[pl.ds(pl.multiple_of(g * 8, 8), 8), :] = jnp.concatenate(lines)

    in_vmem = pl.BlockSpec(memory_space=pltpu.VMEM)
    return pl.pallas_call(
        kernel,
        in_specs=[pl.BlockSpec(memory_space=pltpu.SMEM)] + [in_vmem] * (2 * groups),
        out_specs=[in_vmem] * 3,
        out_shape=[
            shaped((rows, width), jnp.float32),
            shaped((rows, 3 * width), jnp.float32),
            shaped((8 * groups, size), jnp.float32),
        ],
        compiler_params=params(40),
        name="order_attention",
    )(place.scalars, *blocks_a, *blocks_b)


def on_device_permutes(
    tokens,
    segment_ids,
    keep_flag,
    cotangent,
    w_qkv,
    b_query,
    b_value,
    w_attn_out,
    b_attn_out,
    norm1_gain,
    norm1_bias,
    w_in,
    b_in,
    w_out,
    b_out,
    norm2_gain,
    norm2_bias,
    *,
    groups,
    shards,
):
    place = Place(groups, shards)
    _, length, width = tokens.shape
    rows = tokens[0]
    seg_row = segment_ids.reshape(1, length)
    pairs = width // LANES

    c1 = Gather(place, w_qkv)
    c2 = Gather(place, jnp.concatenate([w_in, w_attn_out], 1))
    c3 = Gather(place, w_out)
    c1.chips_near()
    small = Vectors(
        place,
        (b_query, b_value, b_attn_out, norm1_gain, norm1_bias, b_out, norm2_gain, norm2_bias, b_in),
    )
    meet(rows, c1, small)
    pair = c1.chips_far()
    small.chips_near()
    meet(pair, c1, small)
    joined = c1.join()
    c1.near()
    small.chips_far()
    c2.chips_near(joined)
    meet(joined, c2, small)
    small.landed()
    pair = c2.chips_far()
    vectors, bias_in, qkv_bias, seg_col, keep = small.unpack(
        seg_row, keep_flag.reshape(1, length)
    )
    c1.flying = lax.optimization_barrier(c1.flying)
    turned = turned_rows(place, after(rows, vectors))
    c1.far(pair, vectors)
    c1.cross(0, 1, 2)
    joined = c2.join()
    meet((joined, turned), c1)
    c1.landed()
    c2.near(c1.held[3])
    c1.cross(3)
    c3.chips_near(c1.held[3])
    blank = jnp.ones((1, width), jnp.float32)
    qkv_scale = jnp.concatenate([blank / math.sqrt(HD), blank, blank], 1)

    mixed, full_qkv = project_qkv(place, rows, Window(c1, 0, w_qkv.shape[1]), qkv_bias, qkv_scale)
    meet(mixed, c3)
    pair = c3.chips_far()
    c2.cross(0, wait=(mixed,))
    first, second = pairs * 3 // 8, pairs * 3 // 4
    forward = attention_forward(after(mixed, pair), seg_col, seg_row, 0, first)
    meet(forward[0], c2, c3)
    c2.far()
    joined = c3.join()
    c3.near()
    c2.cross(1, 2)
    forward = attention_forward(
        after(mixed, joined), seg_col, seg_row, first, second - first, forward
    )
    meet(forward[0], c2)
    c2.landed()
    c2.cross(3)
    contexts, probs, probs_scale = attention_forward(
        after(mixed, c2.held[3]), seg_col, seg_row, second, pairs - second, forward
    )
    normed, scale_one, normed_low, full_attn = project_out(
        place, contexts, Window(c2, w_in.shape[1], w_attn_out.shape[1]), rows, vectors
    )
    meet(normed_low, c3)
    c3.far()
    c3.cross(0, 1, 2)
    hidden, slope, full_in = feed_in(
        place, after(normed_low, c3.held[1]), Window(c2, 0, w_in.shape[1]), bias_in
    )
    meet(hidden, c3)
    c3.landed()
    c3.cross(3)
    layer_out, second_grad, out_low, second_sums, pre_low, bias_in_grad = feed_out(
        place, hidden, Window(c3, 0, w_out.shape[1]), normed, cotangent[0], keep, vectors, slope
    )

    r_out = Reduction(place, weight_grad(place, hidden, out_low, False, "out"))
    r_in = Reduction(place, weight_grad(place, after(normed_low, r_out.made), pre_low, True, "in"))
    meet(r_in.made, r_out)
    step = r_out.near()
    first_grad, attn_low, context_grad, first_sums = feed_in_back(
        after(pre_low, r_in.made, step), full_in, second_grad, normed, scale_one, vectors, full_attn
    )
    meet(attn_low, r_in)
    step = r_in.near()
    half, quarter = pairs // 2, pairs // 4

    def back(wait, start, count, at, before=None):
        return attention_backward(
            mixed,
            contexts,
            after(context_grad, *wait),
            probs,
            probs_scale,
            start,
            count,
            at,
            half,
            before,
        )

    low_a, late_a = back((step,), 0, half, 0)
    meet(late_a, r_out)
    step = r_out.middle()
    meet(step, r_in)
    steps = (step, r_in.middle())
    r_a = Reduction(
        place, attention_grads(place, after(turned, *steps), low_a, (contexts, attn_low), "a")
    )
    meet(r_a.made, r_out)
    step = r_out.along()
    part = back((r_a.made, step), half, quarter, 0)
    meet(part[1], r_out, r_in, r_a)
    steps = (r_out.along_far(), r_in.along(), r_a.near())
    low_b, late_b = back(steps, half + quarter, quarter, quarter, part)
    meet(late_b, r_a)
    middle = r_a.middle()
    meet(middle, r_out, r_in)
    sums = (late_a, late_b, first_sums, second_sums, bias_in_grad)
    share_out = r_out.share()
    steps = (r_in.along_far(), middle, share_out)
    r_b = Reduction(place, attention_grads(place, after(turned, *steps), low_b, sums, "b"))
    meet(r_b.made, r_in, r_a)
    share_in = r_in.share()
    inner = share_in.shape[1] // groups
    joined = jnp.concatenate(
        [share_out] + [share_in[:, n * inner : (n + 1) * inner] for n in range(groups)]
    )
    all_ffn = Replication(place, joined)
    grads = (low_a, after(low_b, r_b.made, joined, r_a.along()))
    tiles = length // TILE // 2
    input_grad = project_qkv_back(grads, full_qkv, first_grad, 0, tiles)
    meet(input_grad, r_b, r_a, all_ffn)
    steps = (r_b.near(), r_a.along_far())
    input_grad = project_qkv_back(
        grads, full_qkv, after(first_grad, *steps), tiles, tiles, input_grad
    )
    meet(input_grad, r_b, r_a)
    middle = r_b.middle()
    r_a.flying = after(r_a.flying, middle)
    all_a = Replication(place, r_a.share())
    meet(all_a.blocks[0], r_b, all_a)
    along = r_b.along_direct()
    all_a.flying = after(all_a.flying, along)
    all_ffn.flying = after(all_ffn.flying, along)
    pairs_made = (all_a.far(), all_ffn.far())
    meet(pairs_made, r_b)
    share_b = r_b.share_direct()
    all_b = Replication(place, share_b, direct=True)
    meet(share_b, all_ffn)
    w_out_grad, w_in_grad = order_feed_forward(place, all_ffn.landed(), share_in.shape[0])
    all_a.flying = after(all_a.flying, w_out_grad)
    w_attn_grad, w_qkv_grad, small = order_attention(
        place, all_a.landed(), all_b.landed(), w_attn_out.shape[0]
    )
    small = [small[8 * (n // 3) + n % 3] for n in range(12)]
    return (
        layer_out[None],
        input_grad[None],
        w_qkv_grad,
        small[B_QUERY],
        small[B_VALUE],
        w_attn_grad,
        small[B_ATTN],
        small[GAIN_ONE],
        small[SHIFT_ONE],
        w_in_grad,
        jnp.concatenate(small[B_IN:]),
        w_out_grad,
        small[B_OUT],
        small[GAIN_TWO],
        small[SHIFT_TWO],
    )


def solution(mesh):
    groups, shards = mesh.shape["grp"], mesh.shape["shard"]
    if groups == 4 and shards == 8:
        body = functools.partial(on_device_permutes, groups=groups, shards=shards)
    else:
        body = on_device
    return jax.shard_map(
        body,
        mesh=mesh,
        in_specs=(
            P(("grp", "shard"), None, None),
            P(("grp", "shard"), None),
            P(("grp", "shard"), None),
            P(("grp", "shard"), None, None),
            P("shard", "grp"),
            P("shard"),
            P("shard"),
            P("shard", "grp"),
            P("shard"),
            P("shard"),
            P("shard"),
            P("shard", "grp"),
            P("shard"),
            P("shard", "grp"),
            P("shard"),
            P("shard"),
            P("shard"),
        ),
        out_specs=(
            P(("grp", "shard"), None, None),
            P(("grp", "shard"), None, None),
            P("shard", None),
            P("shard"),
            P("shard"),
            P("shard", None),
            P("shard"),
            P("shard"),
            P("shard"),
            P("shard", None),
            P("shard"),
            P("shard", None),
            P("shard"),
            P("shard"),
            P("shard"),
        ),
        check_vma=False,
    )
```
